32 devices in a mesh: dp: 8 (over y, x, core), ctx: 4 (over z).
Axes of the slice: x: 2, y: 2, z: 4, core: 2. Of those that a mesh axis runs over, the one named last changes fastest.
Arguments:
- inputs: bfloat16 [16, 1024, 1536], P('dp', 'ctx'), may hold values from -6 to 6
- gain_in: bfloat16 [1536], P(('dp', 'ctx')), may hold values from 0.5 to 1.5
- in_weight: bfloat16 [1536, 6448], P(('dp', 'ctx')), may hold values from -0.15625 to 0.15625
- conv_weight: bfloat16 [4, 3328], P(None, ('dp', 'ctx')), may hold values from -3 to 3
- conv_bias: bfloat16 [3328], P(('dp', 'ctx')), may hold values from -2 to 2
- step_bias: float32 [48], replicated, may hold values from -4 to -2
- decay_log: float32 [48], replicated, may hold values from -8 to -0.5
- skip_gain: float32 [48], replicated, may hold values from 0.5 to 2
- gain_out: bfloat16 [3072], P(('dp', 'ctx')), may hold values from 0.5 to 1.5
- out_weight: bfloat16 [3072, 1536], P(('dp', 'ctx')), may hold values from -0.109375 to 0.109375
- cotangent: bfloat16 [16, 1024, 1536], P('dp', 'ctx'), may hold values from -6 to 6
Outputs:
- output: bfloat16 [16, 1024, 1536], P('dp', 'ctx')
- grad_input: float32 [16, 1024, 1536], P('dp', 'ctx')
- grad_gain_in: float32 [1536], P(('dp', 'ctx'))
- grad_in_weight: float32 [1536, 6448], P(('dp', 'ctx'))
- grad_conv_weight: float32 [4, 3328], P(None, ('dp', 'ctx'))
- grad_conv_bias: float32 [3328], P(('dp', 'ctx'))
- grad_step_bias: float32 [48], replicated
- grad_decay_log: float32 [48], replicated
- grad_skip_gain: float32 [48], replicated
- grad_gain_out: float32 [3072], P(('dp', 'ctx'))
- grad_out_weight: float32 [3072, 1536], P(('dp', 'ctx'))
The draws below stay inside these ranges and needn't reach their ends.
All inputs are finite; a program needn't handle non-finite values.
Results may differ from the reference program's by a relative error of at most 0.006.
Values may be sent and summed in bfloat16 or wider, within the bound.
A program may use at most 256 MiB of HBM per device.

```python
import math
import jax
import jax.numpy as jnp
from jax import lax

D = 1536
INNER = 3072
STATE = 128
HEAD_DIM = 64
KERNEL = 4
SEG = 256
HEADS = 48
CONV_CH = 3328
PROJ = 6448
LENGTH = 1024
BATCH = 16
N_CTX = 4


def draw_decay_log(key, part):
    key = jax.random.fold_in(key, 7)
    low_end = max(math.log(3.0 / LENGTH), -8.0)
    high_end = math.log(0.5)
    return jax.random.uniform(key, (HEADS,), jnp.float32, low_end, high_end)


def block_levels(rng, dims, split, low, top_value):
    level, own = 1.0, jax.random.fold_in(rng, 6)
    for dim, blocks in split:
        heights = jnp.exp(jax.random.uniform(jax.random.fold_in(own, dim), (blocks,), jnp.float32, low / len(split), top_value / len(split)))
        level = level * jnp.repeat(heights, dims[dim] // blocks).reshape([-1 if axis == dim else 1 for axis in range(len(dims))])
    return level


def noise(own_key, shape, deviation, limit, cuts=(), dtype=jnp.bfloat16):
    level = block_levels(own_key, shape, cuts, -0.22, 0.18) if cuts else 1.0
    values = jax.random.normal(own_key, shape, jnp.float32) * deviation * level
    return jnp.minimum(jnp.maximum(values, -limit), limit).astype(dtype)


def setup_inputs(seed: int = 0) -> dict:
    arg_keys = jax.random.split(jax.random.key(seed), 12)
    inputs = noise(arg_keys[0], (BATCH, LENGTH, D), 1.0, 6.0, ((0, 8), (1, 4)))
    gain_in = jnp.clip(1.0 + 0.1 * jax.random.normal(arg_keys[1], (D,), jnp.float32), 0.5, 1.5).astype(jnp.bfloat16)
    in_weight = noise(arg_keys[2], (D, PROJ), D ** -0.5, 0.15625, ((0, 32),))
    conv_weight = noise(arg_keys[3], (KERNEL, CONV_CH), 0.5, 3.0, ((1, 32),))
    conv_bias = noise(arg_keys[4], (CONV_CH,), 0.3, 2.0, ((0, 32),))
    step_bias = jnp.clip(jax.random.uniform(arg_keys[5], (HEADS,), jnp.float32, -4.0, -2.0), -4.0, -2.0)
    decay_log = draw_decay_log(jax.random.fold_in(arg_keys[11], 71), 0)
    skip_gain = jnp.clip(jax.random.uniform(arg_keys[7], (HEADS,), jnp.float32, 0.5, 2.0), 0.5, 2.0)
    gain_out = jnp.clip(1.0 + 0.1 * jax.random.normal(arg_keys[8], (INNER,), jnp.float32), 0.5, 1.5).astype(jnp.bfloat16)
    out_weight = noise(arg_keys[9], (INNER, D), INNER ** -0.5, 0.109375, ((0, 32),))
    cotangent = noise(arg_keys[10], (BATCH, LENGTH, D), 1.0, 6.0, ((0, 8), (1, 4)))
    return dict(inputs=inputs, gain_in=gain_in, in_weight=in_weight, conv_weight=conv_weight, conv_bias=conv_bias, step_bias=step_bias, decay_log=decay_log, skip_gain=skip_gain, gain_out=gain_out, out_weight=out_weight, cotangent=cotangent)


EPS = 1e-05
HIGH = lax.Precision.HIGHEST

@jax.custom_vjp
def low(v):
    return lax.optimization_barrier(v.astype(jnp.bfloat16)).astype(jnp.float32)

@jax.custom_vjp
def low_back(v):
    return v

def low_keep(v):
    return (low(v), None)

def low_pass(kept, grad):
    return (grad,)

def back_keep(v):
    return (v, None)

def back_low(kept, grad):
    return (low(grad),)
low.defvjp(low_keep, low_pass)
low_back.defvjp(back_keep, back_low)

def rms_scale(values, gain):
    return values * lax.rsqrt(lax.optimization_barrier(jnp.mean(values * values, axis=-1, keepdims=True)) + EPS) * gain

def convolve(padded, kernel, bias_c):
    taps_count = kernel.shape[0]
    length = padded.shape[0] - taps_count + 1
    total = bias_c + kernel[0] * padded[0:length]
    for offset in range(1, taps_count):
        total = total + kernel[offset] * padded[offset:offset + length]
    return jax.nn.silu(total)

def group_math(x_heads, b_proj, c_proj, log_decay, step_size, carried):
    cumulative = jnp.cumsum(log_decay, axis=0)
    length = log_decay.shape[0]
    row_ids = lax.broadcasted_iota(jnp.int32, (length, length), 0)
    col_ids = lax.broadcasted_iota(jnp.int32, (length, length), 1)
    causal = (col_ids <= row_ids)[:, :, None]
    differ = jnp.where(causal, cumulative[:, None, :] - cumulative[None, :, :], -jnp.inf)
    decays = jnp.exp(differ)
    intersection = jnp.dot(c_proj, b_proj.T, precision=HIGH)
    mixing = intersection[:, :, None] * decays * step_size[None, :, :]
    result = jnp.einsum('tsh,shp->thp', mixing, x_heads, precision=HIGH)
    result = result + jnp.exp(cumulative)[:, :, None] * jnp.einsum('tn,hnp->thp', c_proj, carried, precision=HIGH)
    weights_end = jnp.exp(cumulative[-1][None, :] - cumulative) * step_size
    local_state = jnp.einsum('sn,shp->hnp', b_proj, x_heads * weights_end[:, :, None], precision=HIGH)
    ending = jnp.exp(cumulative[-1])[:, None, None] * carried + local_state
    return (result, ending)

def branch(seq_in, gain_in, in_weight, conv_weight, conv_bias, step_bias, decay_log, skip_gain, gain_out, out_weight):
    normed = low(rms_scale(seq_in, gain_in))
    project = low_back(jnp.dot(normed, in_weight, precision=HIGH))
    gate_z = project[:, :INNER]
    conv_in = project[:, INNER:INNER + CONV_CH]
    step_raw = project[:, INNER + CONV_CH:]
    padded = jnp.pad(conv_in, ((KERNEL - 1, 0), (0, 0)))
    acts = convolve(padded, conv_weight, conv_bias)
    x_heads = acts[:, :INNER].reshape(LENGTH, HEADS, HEAD_DIM)
    b_proj = acts[:, INNER:INNER + STATE]
    c_proj = acts[:, INNER + STATE:]
    step_size = jax.nn.softplus(step_raw + step_bias)
    log_decay = step_size * -jnp.exp(decay_log)

    def group_step(carried, pieces):
        part_x, part_b, part_c, part_log, part_step = pieces
        result, ending = group_math(part_x, part_b, part_c, part_log, part_step, carried)
        return (ending, result)
    pieces = (x_heads.reshape(N_CTX, SEG, HEADS, HEAD_DIM), b_proj.reshape(N_CTX, SEG, STATE), c_proj.reshape(N_CTX, SEG, STATE), log_decay.reshape(N_CTX, SEG, HEADS), step_size.reshape(N_CTX, SEG, HEADS))
    start = jnp.zeros((HEADS, STATE, HEAD_DIM), jnp.float32)
    unused, scan_out = lax.scan(jax.checkpoint(group_step), start, pieces)
    mixed = scan_out.reshape(LENGTH, HEADS, HEAD_DIM) + skip_gain[None, :, None] * x_heads
    gated = mixed.reshape(LENGTH, INNER) * jax.nn.silu(gate_z)
    normed_out = low(rms_scale(gated, gain_out))
    return jnp.dot(normed_out, out_weight, precision=HIGH)

def reference(inputs, gain_in, in_weight, conv_weight, conv_bias, step_bias, decay_log, skip_gain, gain_out, out_weight, cotangent):
    params = (gain_in.astype(jnp.float32), in_weight.astype(jnp.float32), conv_weight.astype(jnp.float32), conv_bias.astype(jnp.float32), step_bias.astype(jnp.float32), decay_log.astype(jnp.float32), skip_gain.astype(jnp.float32), gain_out.astype(jnp.float32), out_weight.astype(jnp.float32))

    def one_seq(totals, pair):
        seq_in, seq_cot = pair
        branch_out, pullback = jax.vjp(branch, seq_in, *params)
        grads = pullback(seq_cot)
        totals = jax.tree.map(lambda acc, add: acc + add, totals, tuple(grads[1:]))
        return (totals, ((seq_in + branch_out).astype(jnp.bfloat16), grads[0] + seq_cot))
    zeros = jax.tree.map(jnp.zeros_like, params)
    totals, outs_seq = lax.scan(one_seq, zeros, (inputs.astype(jnp.float32), cotangent.astype(jnp.float32)))
    output, grad_input = outs_seq
    return (output, grad_input, totals[0], totals[1], totals[2], totals[3], totals[4], totals[5], totals[6], totals[7], totals[8])
```

```python
import functools

import jax
import jax.numpy as jnp
from jax import lax
from jax.experimental import pallas as pl
from jax.experimental.pallas import tpu as pltpu
from jax.sharding import PartitionSpec as P

EPS = 1e-05
LOG2E = 1.4426950408889634
HIGH = lax.Precision.HIGHEST
F32 = jnp.float32
BF16 = jnp.bfloat16
CHUNK = 128
GROUP = 256
EDGE = 8
LANES = 128
VMEM_LIMIT = 56 * 1024 * 1024


def dot(a, b, dims=((1,), (0,))):
    return lax.dot_general(a, b, (dims, ((), ())), preferred_element_type=F32)


def nt(a, b):
    return dot(a, b, ((1,), (1,)))


def params():
    return pltpu.CompilerParams(
        dimension_semantics=("arbitrary",), vmem_limit_bytes=VMEM_LIMIT
    )


def whole(shape):
    return pl.BlockSpec(shape, lambda i: (0,) * len(shape))


def sigmoid(v):
    return 1.0 / (1.0 + jnp.exp(-v))


def softplus(v):
    return jnp.maximum(v, 0.0) + jnp.log1p(jnp.exp(-jnp.abs(v)))


def causal_conv(ext, w, b, seg):
    taps = w.shape[0]
    total = b
    for k in range(taps):
        at = EDGE - (taps - 1) + k
        total = total + w[k : k + 1] * ext[at : at + seg]
    return total


def lane_shift(value, lanes):
    return pltpu.roll(value, lax.rem(LANES - lanes, LANES), 1)


def head_rows(ref, first):
    base = pl.multiple_of(first // 8 * 8, 8)
    return pltpu.roll(ref[pl.ds(base, 8), :], lax.rem(8 - lax.rem(first, 8), 8), 0)


def spread(cols, at, head_dim):
    rows = cols.shape[0]
    lane = lax.broadcasted_iota(jnp.int32, (rows, LANES), 1)
    first = jnp.broadcast_to(cols[:, at : at + 1], (rows, LANES))
    second = jnp.broadcast_to(cols[:, at + 1 : at + 2], (rows, LANES))
    return jnp.where(lane < head_dim, first, second)


def spread_all(cols, heads, head_dim):
    return jnp.concatenate([spread(cols, j, head_dim) for j in range(0, heads, 2)], axis=1)


def block_diagonal(pair, head_dim):
    lane = lax.broadcasted_iota(jnp.int32, pair.shape, 1)
    zero = jnp.zeros_like(pair)
    return jnp.concatenate(
        [jnp.where(lane < head_dim, pair, zero), jnp.where(lane < head_dim, zero, pair)], axis=0
    )


def fwd_a_kernel(
    head_dim, pc_ref, w_ref, b_ref, raw_ref, sb_ref, dl_ref,
    x_ref, bc_ref, dt_ref, cum_ref, cumt_ref, loc0_ref, seg_ref, tot_ref, bt_ref,
):
    step = pl.program_id(0)
    seqs = pc_ref.shape[0]
    seg = pc_ref.shape[1] - EDGE
    chunks = seg // CHUNK
    w, b = w_ref[...], b_ref[...]

    def acts_of(s):
        pre = causal_conv(pc_ref[s], w, b, seg)
        return pre * sigmoid(pre)

    @pl.when(step == 0)
    def _():
        row = lax.broadcasted_iota(jnp.int32, (CHUNK, CHUNK), 0)
        col = lax.broadcasted_iota(jnp.int32, (CHUNK, CHUNK), 1)
        tri = (col <= row).astype(F32)
        rate = -jnp.exp(dl_ref[...])
        for s in range(seqs):
            acts = acts_of(s)
            bc_ref[s * seg : (s + 1) * seg] = acts
            for c in range(chunks):
                q = s * chunks + c
                rows = slice(q * CHUNK, (q + 1) * CHUNK)
                bt_ref[q] = acts[c * CHUNK : (c + 1) * CHUNK, :LANES].T.astype(BF16)
                dt = softplus(raw_ref[s, EDGE + c * CHUNK : EDGE + (c + 1) * CHUNK] + sb_ref[...])
                cum = LOG2E * jnp.dot(tri, dt * rate, precision=HIGH, preferred_element_type=F32)
                dt_ref[rows] = dt
                cum_ref[rows] = cum
                cumt_ref[:, rows] = cum.T

    @pl.when(step > 0)
    def _():
        heads = GROUP // head_dim
        first = (step - 1) * heads
        cumg = lane_shift(cum_ref[...], first)
        dtg = lane_shift(dt_ref[...], first)
        for s in range(seqs):
            x = acts_of(s)
            x_ref[s * seg : (s + 1) * seg] = x
            state, total = None, None
            for c in range(chunks):
                q = s * chunks + c
                rows = slice(q * CHUNK, (q + 1) * CHUNK)
                ce = spread_all(cumg[rows], heads, head_dim)
                de = spread_all(dtg[rows], heads, head_dim)
                end = ce[CHUNK - 1 : CHUNK]
                uw = x[c * CHUNK : (c + 1) * CHUNK] * de * jnp.exp2(end - ce)
                loc = dot(bt_ref[q], uw.astype(BF16))
                tot = jnp.exp2(end)
                tot_ref[q : q + 1] = tot
                if c == 0:
                    loc0_ref[s] = loc
                    state, total = loc, tot
                else:
                    state, total = tot * state + loc, tot * total
            seg_ref[s] = state.astype(BF16)
            tot_ref[seqs * chunks + s : seqs * chunks + s + 1] = total


def fwd_a(pc, w, b, sb, dl, inner, head_dim):
    seqs, rows, cols = pc.shape
    seg = rows - EDGE
    tokens = seqs * seg
    groups = inner // GROUP
    state = LANES
    chunks = tokens // CHUNK
    at = lambda i: (i + groups) % (groups + 1)
    back = lambda i: jnp.maximum(i - 1, 0)
    return pl.pallas_call(
        functools.partial(fwd_a_kernel, head_dim),
        grid=(groups + 1,),
        in_specs=[
            pl.BlockSpec((seqs, rows, GROUP), lambda i: (0, 0, at(i))),
            pl.BlockSpec((w.shape[0], GROUP), lambda i: (0, at(i))),
            pl.BlockSpec((1, GROUP), lambda i: (0, at(i))),
            pl.BlockSpec((seqs, rows, LANES), lambda i: (0, 0, cols // LANES - 1)),
            whole((1, LANES)),
            whole((1, LANES)),
        ],
        out_specs=[
            pl.BlockSpec((tokens, GROUP), lambda i: (0, back(i))),
            whole((tokens, GROUP)),
            whole((tokens, LANES)),
            whole((tokens, LANES)),
            whole((LANES, tokens)),
            pl.BlockSpec((seqs, state, GROUP), lambda i: (0, 0, back(i))),
            pl.BlockSpec((seqs, state, GROUP), lambda i: (0, 0, back(i))),
            pl.BlockSpec((8, GROUP), lambda i: (0, back(i))),
        ],
        out_shape=[
            jax.ShapeDtypeStruct((tokens, inner), F32),
            jax.ShapeDtypeStruct((tokens, GROUP), F32),
            jax.ShapeDtypeStruct((tokens, LANES), F32),
            jax.ShapeDtypeStruct((tokens, LANES), F32),
            jax.ShapeDtypeStruct((LANES, tokens), F32),
            jax.ShapeDtypeStruct((seqs, state, inner), F32),
            jax.ShapeDtypeStruct((seqs, state, inner), BF16),
            jax.ShapeDtypeStruct((8, inner), F32),
        ],
        scratch_shapes=[pltpu.VMEM((chunks, LANES, CHUNK), BF16)],
        compiler_params=params(),
        name="conv_states",
    )(pc, w, b, pc, sb, dl)


def fwd_b_kernel(
    head_dim, x_ref, bc_ref, dt_ref, cum_ref, cumt_ref, s0_ref, loc0_ref, tot_ref, skip_ref,
    mixed_ref, s1_ref, cb_ref,
):
    step = pl.program_id(0)
    seqs = s0_ref.shape[0]
    chunks = x_ref.shape[0] // CHUNK // seqs
    heads = GROUP // head_dim

    @pl.when(step == 0)
    def _():
        for q in range(seqs * chunks):
            rows = slice(q * CHUNK, (q + 1) * CHUNK)
            cb_ref[q] = nt(bc_ref[rows, LANES:].astype(BF16), bc_ref[rows, :LANES].astype(BF16))

    first = step * heads
    cumg = lane_shift(cum_ref[...], first)
    dtg = lane_shift(dt_ref[...], first)
    cumr = head_rows(cumt_ref, first)
    row = lax.broadcasted_iota(jnp.int32, (CHUNK, CHUNK), 0)
    col = lax.broadcasted_iota(jnp.int32, (CHUNK, CHUNK), 1)
    causal = col <= row
    skip = skip_ref[...]
    for s in range(seqs):
        start = s0_ref[s]
        for c in range(chunks):
            q = s * chunks + c
            rows = slice(q * CHUNK, (q + 1) * CHUNK)
            x = x_ref[rows]
            ce = spread_all(cumg[rows], heads, head_dim)
            de = spread_all(dtg[rows], heads, head_dim)
            ub = (x * de).astype(BF16)
            cb = cb_ref[q]
            parts = []
            for j in range(0, heads, 2):
                mats = []
                for h in (j, j + 1):
                    there = jnp.broadcast_to(cumg[rows, h : h + 1], (CHUNK, CHUNK))
                    here = cumr[h : h + 1, rows]
                    decay = jnp.exp2(jnp.where(causal, there - here, -jnp.inf))
                    mats.append((decay * cb).astype(BF16))
                pair = ub[:, j * head_dim : (j + 2) * head_dim]
                parts.append(dot(jnp.concatenate(mats, axis=1), block_diagonal(pair, head_dim)))
            y = jnp.concatenate(parts, axis=1)
            y = y + jnp.exp2(ce) * dot(bc_ref[rows, LANES:].astype(BF16), start)
            mixed_ref[rows] = y + skip * x
            if c == 0:
                start = (tot_ref[q : q + 1] * start.astype(F32) + loc0_ref[s]).astype(BF16)
                s1_ref[s] = start


def fwd_b(x, bc, dt, cum, cumt, s0, loc0, tot, skip, head_dim):
    tokens, inner = x.shape
    seqs, state, _ = s0.shape
    groups = inner // GROUP
    wide = pl.BlockSpec((tokens, GROUP), lambda i: (0, i))
    states = pl.BlockSpec((seqs, state, GROUP), lambda i: (0, 0, i))
    return pl.pallas_call(
        functools.partial(fwd_b_kernel, head_dim),
        grid=(groups,),
        in_specs=[
            wide, whole(bc.shape), whole(dt.shape), whole(cum.shape), whole(cumt.shape),
            states, states,
            pl.BlockSpec((8, GROUP), lambda i: (0, i)),
            pl.BlockSpec((1, GROUP), lambda i: (0, i)),
        ],
        out_specs=[wide, states],
        out_shape=[
            jax.ShapeDtypeStruct((tokens, inner), F32),
            jax.ShapeDtypeStruct((seqs, state, inner), BF16),
        ],
        scratch_shapes=[pltpu.VMEM((tokens // CHUNK, CHUNK, CHUNK), F32)],
        compiler_params=params(),
        name="scan_outputs",
    )(x, bc, dt, cum, cumt, s0, loc0, tot, skip)


def mid_kernel(
    normed_ref, wg_ref, mixed_ref, wo_ref, gain_ref, in_ref, cot_ref,
    no_ref, out_ref, dm_ref, dz_ref, gg_ref, z_ref, dno_ref, acc_ref,
):
    step = pl.program_id(0)
    inner = mixed_ref.shape[1]
    tile = 512
    tiles = inner // tile

    @pl.when(step == 0)
    def _():
        gg_ref[...] = jnp.zeros_like(gg_ref)

    def lanes_of(i):
        return pl.ds(pl.multiple_of(i * tile, tile), tile)

    def fold(v):
        total = v[:, :LANES]
        for k in range(LANES, tile, LANES):
            total = total + v[:, k : k + LANES]
        return total

    normed = normed_ref[...]
    cot = cot_ref[...]

    def one(i, sums):
        sq, hg = sums
        at = lanes_of(i)
        z = dot(normed, wg_ref[:, at])
        z_ref[:, at] = z
        g = mixed_ref[:, at] * z * sigmoid(z)
        dno = nt(cot, wo_ref[at, :])
        dno_ref[:, at] = dno
        return sq + fold(g * g), hg + fold(dno * gain_ref[:, at] * g)

    zero = jnp.zeros((normed.shape[0], LANES), F32)
    sq, hg = lax.fori_loop(0, tiles, one, (zero, zero))
    scale = lax.rsqrt(jnp.sum(sq, axis=1, keepdims=True) / inner + EPS)
    pull = scale * scale * scale * (jnp.sum(hg, axis=1, keepdims=True) / inner)
    acc_ref[...] = in_ref[...].astype(F32)

    def two(i, carry):
        at = lanes_of(i)
        z, mixed, dno, gain = z_ref[:, at], mixed_ref[:, at], dno_ref[:, at], gain_ref[:, at]
        sig = sigmoid(z)
        act = z * sig
        g = mixed * act
        gs = g * scale
        no = (gs * gain).astype(BF16)
        no_ref[:, at] = no
        acc_ref[...] += dot(no, wo_ref[at, :])
        gg_ref[:, at] += jnp.sum(dno * gs, axis=0, keepdims=True)
        dg = scale * (dno * gain) - g * pull
        dm_ref[:, at] = dg * act
        dz_ref[:, at] = (dg * mixed * (sig * (1.0 + z * (1.0 - sig)))).astype(BF16)
        return carry

    lax.fori_loop(0, tiles, two, 0)
    out_ref[...] = acc_ref[...].astype(BF16)


def mid(normed, wg, mixed, wo, gain, inputs, cot):
    tokens, inner = mixed.shape
    width = inputs.shape[1]
    narrow = pl.BlockSpec((CHUNK, width), lambda i: (i, 0))
    wide = pl.BlockSpec((CHUNK, inner), lambda i: (i, 0))
    once = lambda shape: pl.BlockSpec(shape, lambda i: (0, 0), pipeline_mode=pl.Buffered(1))
    return pl.pallas_call(
        mid_kernel,
        grid=(tokens // CHUNK,),
        in_specs=[narrow, once(wg.shape), wide, once(wo.shape), whole((1, inner)), narrow, narrow],
        out_specs=[wide, narrow, wide, wide, whole((1, inner))],
        out_shape=[
            jax.ShapeDtypeStruct((tokens, inner), BF16),
            jax.ShapeDtypeStruct((tokens, width), BF16),
            jax.ShapeDtypeStruct((tokens, inner), F32),
            jax.ShapeDtypeStruct((tokens, inner), BF16),
            jax.ShapeDtypeStruct((1, inner), F32),
        ],
        scratch_shapes=[
            pltpu.VMEM((CHUNK, inner), F32),
            pltpu.VMEM((CHUNK, inner), F32),
            pltpu.VMEM((CHUNK, width), F32),
        ],
        compiler_params=params(),
        name="gate_norm_project",
    )(normed, wg, mixed, wo, gain, inputs, cot)


def bwd_a_kernel(head_dim, seqs, dm_ref, bc_ref, cum_ref, tot_ref, seg_ref, ct_ref):
    step = pl.program_id(0)
    chunks = dm_ref.shape[0] // CHUNK // seqs
    heads = GROUP // head_dim

    @pl.when(step == 0)
    def _():
        for q in range(seqs * chunks):
            ct_ref[q] = bc_ref[q * CHUNK : (q + 1) * CHUNK, LANES:].T.astype(BF16)

    cumg = lane_shift(cum_ref[...], step * heads)
    for s in range(seqs):
        state = None
        for c in range(chunks - 1, -1, -1):
            q = s * chunks + c
            rows = slice(q * CHUNK, (q + 1) * CHUNK)
            ey = jnp.exp2(spread_all(cumg[rows], heads, head_dim)) * dm_ref[rows]
            loc = dot(ct_ref[q], ey.astype(BF16))
            state = loc if state is None else tot_ref[q : q + 1] * state + loc
        seg_ref[s] = state.astype(BF16)


def bwd_a(dm, bc, cum, tot, seqs, head_dim):
    tokens, inner = dm.shape
    return pl.pallas_call(
        functools.partial(bwd_a_kernel, head_dim, seqs),
        grid=(inner // GROUP,),
        in_specs=[
            pl.BlockSpec((tokens, GROUP), lambda i: (0, i)), whole(bc.shape), whole(cum.shape),
            pl.BlockSpec((8, GROUP), lambda i: (0, i)),
        ],
        out_specs=pl.BlockSpec((seqs, LANES, GROUP), lambda i: (0, 0, i)),
        out_shape=jax.ShapeDtypeStruct((seqs, LANES, inner), BF16),
        scratch_shapes=[pltpu.VMEM((tokens // CHUNK, LANES, CHUNK), BF16)],
        compiler_params=params(),
        name="adjoint_states",
    )(dm, bc, cum, tot)


def bwd_b_kernel(
    head_dim, groups, pc_ref, w_ref, b_ref, raw_ref, sb_ref, dl_ref, bc_ref, dt_ref, cum_ref, cumt_ref,
    dm_ref, mixed_ref, s0_ref, s1_ref, s2_ref, g_ref, tot_ref, skip_ref,
    dc_ref, tail_ref, edge_ref, gw_ref, gb_ref, gskip_ref, draw_ref, hsum_ref,
    cbt_ref, dcbt_ref, db_acc, dc_acc, r1_ref, r2_ref, dtot_ref,
):
    step = pl.program_id(0)
    seqs = pc_ref.shape[0]
    seg = pc_ref.shape[1] - EDGE
    chunks = seg // CHUNK
    heads = GROUP // head_dim
    w, b = w_ref[...], b_ref[...]
    taps = w.shape[0]

    @pl.when(step == 0)
    def _():
        for q in range(seqs * chunks):
            rows = slice(q * CHUNK, (q + 1) * CHUNK)
            cbt_ref[q] = nt(bc_ref[rows, :LANES].astype(BF16), bc_ref[rows, LANES:].astype(BF16))
        dcbt_ref[...] = jnp.zeros_like(dcbt_ref)
        db_acc[...] = jnp.zeros_like(db_acc)
        dc_acc[...] = jnp.zeros_like(dc_acc)
        r1_ref[...] = jnp.zeros_like(r1_ref)
        r2_ref[...] = jnp.zeros_like(r2_ref)
        dtot_ref[...] = jnp.zeros_like(dtot_ref)

    def conv_back(s, ext, pre, sig, d_act):
        d_pre = d_act * (sig * (1.0 + pre * (1.0 - sig)))
        zero = jnp.zeros((EDGE, d_pre.shape[1]), F32)
        padded = jnp.concatenate([zero, d_pre, zero], axis=0)
        total = None
        for k in range(taps):
            at = taps - 1 - k
            term = w[k : k + 1] * padded[at : at + seg + EDGE]
            total = term if total is None else total + term
        edge_ref[s] = total[:EDGE]
        dc_ref[s * seg : (s + 1) * seg] = total[EDGE:].astype(BF16)
        tail_ref[s] = total[seg:]
        for k in range(taps):
            at = EDGE - (taps - 1) + k
            grad = jnp.sum(ext[at : at + seg] * d_pre, axis=0, keepdims=True)
            gw_ref[k : k + 1] = grad if s == 0 else gw_ref[k : k + 1] + grad
        grad = jnp.sum(d_pre, axis=0, keepdims=True)
        gb_ref[...] = grad if s == 0 else gb_ref[...] + grad

    def by_head(value, pick):
        high = value.astype(BF16)
        return dot(high, pick) + dot((value - high.astype(F32)).astype(BF16), pick)

    @pl.when(step < groups)
    def _():
        first = step * heads
        cumg = lane_shift(cum_ref[...], first)
        dtg = lane_shift(dt_ref[...], first)
        cumr = head_rows(cumt_ref, first)
        row = lax.broadcasted_iota(jnp.int32, (CHUNK, CHUNK), 0)
        col = lax.broadcasted_iota(jnp.int32, (CHUNK, CHUNK), 1)
        causal = row <= col
        lane = lax.broadcasted_iota(jnp.int32, (GROUP, LANES), 0)
        head = lax.broadcasted_iota(jnp.int32, (GROUP, LANES), 1)
        pick = (head == first + lane // head_dim).astype(BF16)
        skip = skip_ref[...]
        grad_skip = None
        for s in range(seqs):
            ext = pc_ref[s]
            pre = causal_conv(ext, w, b, seg)
            sig = sigmoid(pre)
            acts = pre * sig
            adj = g_ref[s].astype(F32)
            d_acts = [None] * chunks
            for c in range(chunks - 1, -1, -1):
                q = s * chunks + c
                rows = slice(q * CHUNK, (q + 1) * CHUNK)
                x = acts[c * CHUNK : (c + 1) * CHUNK]
                dy = dm_ref[rows]
                ce = spread_all(cumg[rows], heads, head_dim)
                de = spread_all(dtg[rows], heads, head_dim)
                weight = jnp.exp2(ce[CHUNK - 1 : CHUNK] - ce)
                u = x * de
                ub = u.astype(BF16)
                dyb = dy.astype(BF16)
                cbt = cbt_ref[q]
                parts = []
                dcbt = dcbt_ref[q]
                for j in range(0, heads, 2):
                    lanes = slice(j * head_dim, (j + 2) * head_dim)
                    dy_block = block_diagonal(dyb[:, lanes], head_dim)
                    dm = nt(ub[:, lanes], dy_block)
                    mats = []
                    for k, h in enumerate((j, j + 1)):
                        here = jnp.broadcast_to(cumg[rows, h : h + 1], (CHUNK, CHUNK))
                        there = cumr[h : h + 1, rows]
                        decay = jnp.exp2(jnp.where(causal, there - here, -jnp.inf))
                        mats.append((decay * cbt).astype(BF16))
                        dcbt = dcbt + decay * dm[:, k * CHUNK : (k + 1) * CHUNK]
                    parts.append(dot(jnp.concatenate(mats, axis=1), dy_block))
                dcbt_ref[q] = dcbt
                start = s0_ref[s] if c == 0 else s1_ref[s]
                end = s2_ref[s] if c == chunks - 1 else s1_ref[s]
                adj_b = adj.astype(BF16)
                bb = bc_ref[rows, :LANES].astype(BF16)
                cb = bc_ref[rows, LANES:].astype(BF16)
                ey = (jnp.exp2(ce) * dy).astype(BF16)
                du = jnp.concatenate(parts, axis=1) + weight * dot(bb, adj_b)
                db_acc[rows] += nt((u * weight).astype(BF16), adj_b)
                dc_acc[rows] += nt(ey, start)
                r1_ref[rows] += by_head(dyb.astype(F32) * (mixed_ref[rows] - skip * x), pick)
                r2_ref[rows] += by_head(x * du, pick)
                dtot_ref[q : q + 1] += by_head(
                    jnp.sum(adj * end.astype(F32), axis=0, keepdims=True), pick
                )
                grad = jnp.sum(dy * x, axis=0, keepdims=True)
                grad_skip = grad if grad_skip is None else grad_skip + grad
                d_acts[c] = du * de + skip * dy
                if c > 0:
                    adj = tot_ref[q : q + 1] * adj + dot(cb, ey, ((0,), (0,)))
            conv_back(s, ext, pre, sig, jnp.concatenate(d_acts, axis=0))
        gskip_ref[...] = grad_skip

    @pl.when(step == groups)
    def _():
        row = lax.broadcasted_iota(jnp.int32, (CHUNK, CHUNK), 0)
        col = lax.broadcasted_iota(jnp.int32, (CHUNK, CHUNK), 1)
        later = (row <= col).astype(F32)
        rate = -jnp.exp(dl_ref[...])
        sum_raw = jnp.zeros((1, LANES), F32)
        sum_log = jnp.zeros((1, LANES), F32)
        for s in range(seqs):
            ext = pc_ref[s]
            pre = causal_conv(ext, w, b, seg)
            sig = sigmoid(pre)
            parts = []
            for c in range(chunks):
                q = s * chunks + c
                rows = slice(q * CHUNK, (q + 1) * CHUNK)
                dcbt = dcbt_ref[q]
                bb = bc_ref[rows, :LANES].astype(BF16)
                cb = bc_ref[rows, LANES:].astype(BF16)
                d_b = db_acc[rows] + dot(dcbt.astype(BF16), cb)
                d_c = dc_acc[rows] + dot(dcbt.T.astype(BF16), bb)
                parts.append(jnp.concatenate([d_b, d_c], axis=1))
                dt = dt_ref[rows]
                r2 = r2_ref[rows]
                d_log = jnp.dot(
                    later, r1_ref[rows] - dt * r2, precision=HIGH, preferred_element_type=F32
                )
                d_log = d_log + dtot_ref[q : q + 1]
                raw = raw_ref[s, EDGE + c * CHUNK : EDGE + (c + 1) * CHUNK] + sb_ref[...]
                d_raw = (r2 + rate * d_log) * sigmoid(raw)
                draw_ref[rows] = d_raw
                sum_raw = sum_raw + jnp.sum(d_raw, axis=0, keepdims=True)
                sum_log = sum_log + jnp.sum(d_log * dt, axis=0, keepdims=True) * rate
            conv_back(s, ext, pre, sig, jnp.concatenate(parts, axis=0))
        hsum_ref[0:1] = sum_raw
        hsum_ref[1:2] = sum_log


def bwd_b(pc, w, b, sb, dl, bc, dt, cum, cumt, dm, mixed, s0, s1, s2, g, tot, skip, head_dim):
    seqs, rows, cols = pc.shape
    tokens, inner = dm.shape
    groups = inner // GROUP
    taps, channels = w.shape
    wide = pl.BlockSpec((tokens, GROUP), lambda i: (0, jnp.minimum(i, groups - 1)))
    states = pl.BlockSpec((seqs, LANES, GROUP), lambda i: (0, 0, jnp.minimum(i, groups - 1)))
    line = lambda n: pl.BlockSpec((n, GROUP), lambda i: (0, jnp.minimum(i, groups - 1)))
    conv = lambda n: pl.BlockSpec((n, GROUP), lambda i: (0, i))
    ends = pl.BlockSpec((seqs, EDGE, GROUP), lambda i: (0, 0, i))
    chunks = tokens // CHUNK
    shape = jax.ShapeDtypeStruct
    return pl.pallas_call(
        functools.partial(bwd_b_kernel, head_dim, groups),
        grid=(groups + 1,),
        in_specs=[
            pl.BlockSpec((seqs, rows, GROUP), lambda i: (0, 0, i)),
            conv(taps),
            conv(1),
            pl.BlockSpec((seqs, rows, LANES), lambda i: (0, 0, cols // LANES - 1)),
            whole((1, LANES)), whole((1, LANES)),
            whole(bc.shape), whole(dt.shape), whole(cum.shape), whole(cumt.shape),
            wide, wide, states, states, states, states, line(8), line(1),
        ],
        out_specs=[
            conv(tokens), ends, ends, conv(taps), conv(1), line(1),
            whole((tokens, LANES)), whole((2, LANES)),
        ],
        out_shape=[
            shape((tokens, channels), BF16),
            shape((seqs, EDGE, channels), F32),
            shape((seqs, EDGE, channels), F32),
            shape((taps, channels), F32),
            shape((1, channels), F32),
            shape((1, inner), F32),
            shape((tokens, LANES), F32),
            shape((2, LANES), F32),
        ],
        scratch_shapes=[
            pltpu.VMEM((chunks, CHUNK, CHUNK), F32),
            pltpu.VMEM((chunks, CHUNK, CHUNK), F32),
            pltpu.VMEM((tokens, LANES), F32),
            pltpu.VMEM((tokens, LANES), F32),
            pltpu.VMEM((tokens, LANES), F32),
            pltpu.VMEM((tokens, LANES), F32),
            pltpu.VMEM((8, LANES), F32),
        ],
        compiler_params=params(),
        name="scan_backward",
    )(pc, w, b, pc, sb, dl, bc, dt, cum, cumt, dm, mixed, s0, s1, s2, g, tot, skip)


def passed_along(value, axis, steps):
    count = lax.axis_size(axis)
    initial, last = (max(0, -steps), min(count, count - steps))
    return lax.ppermute(value, axis, [(source, source + steps) for source in range(initial, last)])


def prefix(total, local, axis, backward):
    count, here = lax.axis_size(axis), lax.axis_index(axis)
    totals = lax.all_gather(total.astype(BF16), axis)
    locals_ = lax.all_gather(local, axis)
    state = jnp.zeros(local.shape, F32)
    order = range(count - 1, 0, -1) if backward else range(count - 1)
    for lap in order:
        new = totals[lap].astype(F32) * state + locals_[lap].astype(F32)
        reached = lap > here if backward else lap < here
        state = jnp.where(reached, new, state)
    leaves = total * state + local.astype(F32)
    return state.astype(BF16), leaves.astype(BF16)


AXES = ("dp", "ctx")


def body(
    inputs, gain_in, in_weight, conv_weight, conv_bias, step_bias, decay_log, skip_gain, gain_out,
    out_weight, cotangent,
):
    seqs, seg, width = inputs.shape
    tokens = seqs * seg
    count = lax.axis_size(AXES)
    inner = out_weight.shape[0] * count
    taps, channels = conv_weight.shape[0], conv_weight.shape[1] * count
    num_heads = step_bias.shape[0]
    head_dim = inner // num_heads

    w_gate = in_weight[:, :inner]
    w_conv = in_weight[:, inner:]
    spare = -w_conv.shape[1] % LANES
    w_conv = jnp.pad(w_conv, ((0, 0), (0, spare)))
    small = jnp.concatenate([gain_in, gain_out, conv_bias, conv_weight.reshape(-1)])
    small = lax.all_gather(small, AXES)
    w_conv = lax.all_gather(w_conv, AXES, axis=0, tiled=True)
    w_gate = lax.all_gather(w_gate, AXES, axis=0, tiled=True)
    w_out = lax.all_gather(out_weight, AXES, axis=0, tiled=True)

    a, b, c = gain_in.shape[0], gain_out.shape[0], conv_bias.shape[0]
    g_in = small[:, :a].reshape(1, width).astype(F32)
    g_out = small[:, a : a + b].reshape(1, inner).astype(F32)
    bias = small[:, a + b : a + b + c].reshape(1, channels).astype(F32)
    kernel = small[:, a + b + c :].reshape(count, taps, c).transpose(1, 0, 2)
    kernel = kernel.reshape(taps, channels).astype(F32)
    pad_head = lambda v: jnp.pad(v, (0, LANES - num_heads)).reshape(1, LANES)
    sb, dl = pad_head(step_bias), pad_head(decay_log)
    skip = jnp.repeat(skip_gain, head_dim).reshape(1, inner)

    before = passed_along(inputs[:, seg - (taps - 1) :], "ctx", 1)
    ext = jnp.concatenate(
        [jnp.zeros((seqs, EDGE - (taps - 1), width), inputs.dtype), before, inputs], axis=1
    ).astype(F32)
    scale_ext = lax.rsqrt(jnp.mean(ext * ext, axis=-1, keepdims=True) + EPS)
    normed_ext = (ext * scale_ext * g_in).astype(BF16)
    normed = normed_ext[:, EDGE:].reshape(tokens, width)
    pc = dot(normed_ext.reshape(seqs * (seg + EDGE), width), w_conv).reshape(seqs, seg + EDGE, -1)

    x, bc, dt, cum, cumt, loc0, local, tot = fwd_a(pc, kernel, bias, sb, dl, inner, head_dim)
    per_seq = tot[tokens // CHUNK : tokens // CHUNK + seqs][:, None, :]
    s0, s2 = prefix(per_seq, local, "ctx", False)
    mixed, s1 = fwd_b(x, bc, dt, cum, cumt, s0, loc0, tot, skip, head_dim)

    flat = inputs.reshape(tokens, width)
    cot = cotangent.reshape(tokens, width)
    normed_out, output, d_mixed, d_gate, grad_gain_out = mid(
        normed, w_gate, mixed, w_out, g_out, flat, cot
    )
    scatter = lambda v: lax.psum_scatter(v, AXES, scatter_dimension=0, tiled=True).astype(F32)
    grad_out_weight = scatter(dot(normed_out, cot, ((0,), (0,))).astype(BF16))
    grad_gate_weight = scatter(dot(normed, d_gate, ((0,), (0,))).astype(BF16))

    adjoint = bwd_a(d_mixed, bc, cum, tot, seqs, head_dim)
    g, _ = prefix(per_seq, adjoint, "ctx", True)
    d_conv, tail, edge, grad_kernel, grad_bias, grad_skip, d_raw, head_sums = bwd_b(
        pc, kernel, bias, sb, dl, bc, dt, cum, cumt, d_mixed, mixed, s0, s1, s2, g, tot, skip, head_dim
    )
    after = passed_along(edge[:, EDGE - (taps - 1) :].astype(BF16), "ctx", -1).astype(F32)
    tail = tail[:, EDGE - (taps - 1) :] + after
    d_conv = d_conv.reshape(seqs, seg, channels).at[:, seg - (taps - 1) :].set(tail.astype(BF16))
    d_conv = jnp.concatenate([d_conv.reshape(tokens, channels), d_raw.astype(BF16)], axis=1)

    real = d_conv.shape[1] - spare
    grad_conv_cols = scatter(dot(normed, d_conv[:, :real], ((0,), (0,))).astype(BF16))
    d_normed = nt(d_gate, w_gate) + nt(d_conv, w_conv)
    values = flat.astype(F32)
    scale = scale_ext[:, EDGE:].reshape(tokens, 1)
    hat = values * scale
    grad_gain_in = jnp.sum(d_normed * hat, axis=0)
    weighted = d_normed * g_in
    pull = jnp.mean(weighted * hat, axis=-1, keepdims=True)
    grad_input = scale * (weighted - hat * pull) + cot.astype(F32)

    grad_in_weight = jnp.concatenate(
        [grad_gate_weight, grad_conv_cols], axis=1
    )
    by_owner = jnp.concatenate(
        [
            grad_gain_in.reshape(count, a),
            grad_gain_out.reshape(count, b),
            grad_bias.reshape(count, c),
            grad_kernel.reshape(taps, count, c).transpose(1, 0, 2).reshape(count, taps * c),
        ],
        axis=1,
    )
    grad_skip = jnp.sum(grad_skip.reshape(num_heads, head_dim), axis=1)
    heads_sum = jnp.concatenate(
        [head_sums[0, :num_heads], head_sums[1, :num_heads], grad_skip]
    )
    everyone = lax.psum(jnp.concatenate([by_owner.reshape(-1), heads_sum]), AXES)
    mine = lax.dynamic_slice_in_dim(
        everyone[: by_owner.size].reshape(count, -1), lax.axis_index(AXES), 1, 0
    )[0]
    head_totals = everyone[by_owner.size :].reshape(3, num_heads)
    return (
        output.reshape(seqs, seg, width),
        grad_input.reshape(seqs, seg, width),
        mine[:a],
        grad_in_weight,
        mine[a + b + c :].reshape(taps, c),
        mine[a + b : a + b + c],
        head_totals[0],
        head_totals[1],
        head_totals[2],
        mine[a : a + b],
        grad_out_weight,
    )


def solution(mesh):
    rows, cols, both = P("dp", "ctx", None), P(AXES, None), P(AXES)
    return jax.shard_map(
        body,
        mesh=mesh,
        in_specs=(rows, both, cols, P(None, AXES), both, P(), P(), P(), both, cols, rows),
        out_specs=(rows, rows, both, cols, P(None, AXES), both, P(), P(), P(), both, cols),
        check_vma=False,
    )
```

```python
import functools

import jax
import jax.numpy as jnp
from jax import lax
from jax.experimental import pallas as pl
from jax.experimental.pallas import tpu as pltpu
from jax.sharding import PartitionSpec as P

EPS = 1e-05
LOG2E = 1.4426950408889634
HIGH = lax.Precision.HIGHEST
F32 = jnp.float32
BF16 = jnp.bfloat16
CHUNK = 128
GROUP = 256
EDGE = 8
LANES = 128
VMEM_LIMIT = 56 * 1024 * 1024


def dot(a, b, dims=((1,), (0,))):
    return lax.dot_general(a, b, (dims, ((), ())), preferred_element_type=F32)


def nt(a, b):
    return dot(a, b, ((1,), (1,)))


def params():
    return pltpu.CompilerParams(
        dimension_semantics=("arbitrary",), vmem_limit_bytes=VMEM_LIMIT
    )


def whole(shape):
    return pl.BlockSpec(shape, lambda i: (0,) * len(shape))


def sigmoid(v):
    return 1.0 / (1.0 + jnp.exp(-v))


def softplus(v):
    return jnp.maximum(v, 0.0) + jnp.log1p(jnp.exp(-jnp.abs(v)))


def causal_conv(ext, w, b, seg):
    taps = w.shape[0]
    total = b
    for k in range(taps):
        at = EDGE - (taps - 1) + k
        total = total + w[k : k + 1] * ext[at : at + seg]
    return total


def lane_shift(value, lanes):
    return pltpu.roll(value, lax.rem(LANES - lanes, LANES), 1)


def head_rows(ref, first):
    base = pl.multiple_of(first // 8 * 8, 8)
    return pltpu.roll(ref[pl.ds(base, 8), :], lax.rem(8 - lax.rem(first, 8), 8), 0)


def spread(cols, at, head_dim):
    rows = cols.shape[0]
    lane = lax.broadcasted_iota(jnp.int32, (rows, LANES), 1)
    first = jnp.broadcast_to(cols[:, at : at + 1], (rows, LANES))
    second = jnp.broadcast_to(cols[:, at + 1 : at + 2], (rows, LANES))
    return jnp.where(lane < head_dim, first, second)


def spread_all(cols, heads, head_dim):
    return jnp.concatenate([spread(cols, j, head_dim) for j in range(0, heads, 2)], axis=1)


def block_diagonal(pair, head_dim):
    lane = lax.broadcasted_iota(jnp.int32, pair.shape, 1)
    zero = jnp.zeros_like(pair)
    return jnp.concatenate(
        [jnp.where(lane < head_dim, pair, zero), jnp.where(lane < head_dim, zero, pair)], axis=0
    )


MESH = pl.DeviceIdType.MESH


class Place:
    def __init__(self, depth):
        dp, z = lax.axis_index("dp"), lax.axis_index("ctx")
        self.depth, self.z = depth, z
        self.own = {"y": lax.div(dp, 4), "x": lax.rem(lax.div(dp, 2), 2), "c": lax.rem(dp, 2)}
        self.to = {
            name: {"dp": dp + step * (1 - 2 * self.own[name])}
            for name, step in (("y", 4), ("x", 2), ("c", 1))
        }
        self.has_left, self.has_right = z > 0, z < depth - 1
        self.left, self.right = {"ctx": z - 1}, {"ctx": z + 1}

    def flipped(self, *names):
        return {n: 1 - v if n in names else v for n, v in self.own.items()}

    def near(self, k):
        z, last = self.z, self.depth - 1
        reach = jnp.minimum(z, last - z)
        pair = jnp.where(k % 2 == 1, z - (k + 1) // 2, z + k // 2)
        alone = jnp.where(z > last - z, last - k, k)
        return z if k == 0 else jnp.where(k <= 2 * reach, pair, alone)

    def meet(self):
        barrier = pltpu.get_barrier_semaphore()
        signal = functools.partial(pl.semaphore_signal, barrier, inc=1, device_id_type=MESH)
        for name in ("y", "x", "c"):
            signal(device_id=self.to[name])
        pl.when(self.has_left)(lambda: signal(device_id=self.left))
        pl.when(self.has_right)(lambda: signal(device_id=self.right))
        ends = self.has_left.astype(jnp.int32) + self.has_right.astype(jnp.int32)
        pl.semaphore_wait(barrier, 3 + ends)


class Gather:
    SENDS, RECEIVES = 9, 8

    def __init__(self, place, src, slot, first, second, send, recv):
        self.place, self.src, self.slot_of = place, src, slot
        self.first, self.second, self.send, self.recv = first, second, send, recv

    @staticmethod
    def sems(depth):
        return 9 * depth, 8 * depth

    def slot(self, k, *flips):
        return self.slot_of(self.place.near(k), **self.place.flipped(*flips))

    def copy(self, k, kind, where, to, recv):
        src = self.src if k == 0 and where == () else self.slot(k, *where)
        return pltpu.make_async_remote_copy(
            src_ref=src,
            dst_ref=self.slot(k, *where),
            send_sem=self.send.at[kind * self.place.depth + k],
            recv_sem=self.recv.at[recv],
            device_id=to,
            device_id_type=MESH,
        )

    def along(self, k, right):
        p = self.place
        return self.copy(k, int(right), (), p.right if right else p.left, p.near(k))

    def goes(self, k, right):
        p, at = self.place, self.place.near(k)
        if right:
            return p.has_right if k == 0 else p.has_right & (at < p.z)
        return p.has_left if k == 0 else p.has_left & (at > p.z)

    def to_axis(self, k, stage):
        p, depth = self.place, self.place.depth
        f, s = self.first, self.second
        where = ((), (), (f,), (), (f,), (s,), (f, s))[stage]
        to = p.to[(f, s, s, "c", "c", "c", "c")[stage]]
        return self.copy(k, 2 + stage, where, to, (1 + stage) * depth + k)

    def arrived(self, k, stage):
        p, depth = self.place, self.place.depth
        f, s = self.first, self.second
        where = ((f,), (s,), (s, f), ("c",), ("c", f), ("c", s), ("c", f, s))[stage]
        self.copy(k, 2 + stage, where, p.to["c"], (1 + stage) * depth + k).wait_recv()

    def wave_line(self, k):
        if k:
            self.along(k, True).wait_recv()
        for right in (True, False):
            pl.when(self.goes(k, right))(lambda: self.along(k, right).start())
        for stage in (0, 1, 3):
            self.to_axis(k, stage).start()

    def wave_first(self, k):
        self.arrived(k, 0)
        self.to_axis(k, 2).start()
        self.to_axis(k, 4).start()

    def wave_second(self, k):
        self.arrived(k, 1)
        self.to_axis(k, 5).start()
        self.arrived(k, 2)
        self.to_axis(k, 6).start()

    def wave_core(self, k):
        for stage in range(3, 7):
            self.arrived(k, stage)

    def finish(self):
        for k in range(self.place.depth):
            for right in (True, False):
                pl.when(self.goes(k, right))(lambda: self.along(k, right).wait_send())
            for stage in range(7):
                self.to_axis(k, stage).wait_send()


def gather_kernel(
    depth, half, xr_ref, small_src, wc_src, wg_src, wo_src,
    pc_ref, normed_ref, small_ref, wc_ref, wg_ref, wo_ref,
    buf_ref, load_sem, own_sem, send, recv,
):
    place = Place(depth)
    place.meet()
    width = wc_src.shape[1]
    lo, hi = pl.ds(0, half), pl.ds(half, width - half)
    lanes = [
        Gather(place, small_src, lambda z, y, x, c: small_ref.at[z, y, x, c], "y", "x",
               send.at[0], recv.at[0]),
        Gather(place, wc_src.at[:, lo], lambda z, y, x, c: wc_ref.at[z, y, x, c, :, lo], "y", "x",
               send.at[1], recv.at[1]),
        Gather(place, wc_src.at[:, hi], lambda z, y, x, c: wc_ref.at[z, y, x, c, :, hi], "x", "y",
               send.at[2], recv.at[2]),
    ]
    late = [
        Gather(place, wg_src, lambda z, y, x, c: wg_ref.at[z, y, x, c], "y", "x",
               send.at[3], recv.at[3]),
        Gather(place, wo_src, lambda z, y, x, c: wo_ref.at[y, x, c, z], "x", "y",
               send.at[4], recv.at[4]),
    ]
    own = place.own
    copies = [
        pltpu.make_async_copy(small_src, small_ref.at[place.z, own["y"], own["x"], own["c"]], own_sem.at[0]),
        pltpu.make_async_copy(wc_src, wc_ref.at[place.z, own["y"], own["x"], own["c"]], own_sem.at[1]),
        pltpu.make_async_copy(wg_src, wg_ref.at[place.z, own["y"], own["x"], own["c"]], own_sem.at[2]),
        pltpu.make_async_copy(wo_src, wo_ref.at[own["y"], own["x"], own["c"], place.z], own_sem.at[3]),
    ]

    def each(group, step, k):
        for lane in group:
            getattr(lane, step)(k)

    def load(k):
        return pltpu.make_async_copy(wc_ref.at[place.near(k)], buf_ref.at[k % 2], load_sem.at[k % 2])

    rows = wc_src.shape[0]
    count = 8 * rows
    tile = 3 * LANES
    gain_rows = count // LANES

    def multiply(k):
        at = place.near(k)
        gain = sum(
            small_ref[at, y, x, c, :gain_rows] for y in (0, 1) for x in (0, 1) for c in (0, 1)
        )
        gain = jnp.concatenate([gain[i : i + 1] for i in range(gain_rows)], axis=1)
        normed_ref[at] = (xr_ref[at] * gain).astype(BF16)
        load(k).wait()
        normed = normed_ref[at]

        def one(i, carry):
            cols = pl.ds(pl.multiple_of(i * tile, tile), tile)
            block = jnp.concatenate(
                [buf_ref[k % 2, y, x, c, :, cols] for y in (0, 1) for x in (0, 1) for c in (0, 1)],
                axis=0,
            )
            part = dot(normed, block)
            if k == 0:
                pc_ref[:, cols] = part
            else:
                pc_ref[:, cols] += part
            return carry

        lax.fori_loop(0, width // tile, one, 0)

    def reached(k):
        each(lanes, "wave_core", k)
        load(k).start()

    for k in range(depth):
        each(lanes, "wave_line", k)
        if k == 0:
            for copy in copies:
                copy.start()
            for copy in copies:
                copy.wait()
        else:
            each(lanes, "wave_second", k - 1)
        each(lanes, "wave_first", k)
        if k >= 2:
            reached(k - 2)
            multiply(k - 2)
    each(late, "wave_line", 0)
    each(lanes, "wave_second", depth - 1)
    reached(depth - 2)
    multiply(depth - 2)
    each(late, "wave_first", 0)
    reached(depth - 1)
    multiply(depth - 1)
    for k in range(1, depth):
        each(late, "wave_line", k)
        each(late, "wave_second", k - 1)
        each(late, "wave_first", k)
        each(late, "wave_core", k - 1)
    each(late, "wave_second", depth - 1)
    each(late, "wave_core", depth - 1)
    for lane in lanes + late:
        lane.finish()


def gather_project(xr, small, wc, wg, wo, depth):
    shape = jax.ShapeDtypeStruct
    slots = (depth, 2, 2, 2)
    sends, receives = Gather.sems(depth)
    width = wc.shape[1]
    half = width // 2 // LANES * LANES
    anywhere, vmem = pl.BlockSpec(memory_space=pl.ANY), pl.BlockSpec(memory_space=pltpu.VMEM)
    return pl.pallas_call(
        functools.partial(gather_kernel, depth, half),
        in_specs=[vmem, vmem, anywhere, anywhere, anywhere],
        out_specs=[vmem, vmem, vmem, anywhere, anywhere, anywhere],
        out_shape=[
            shape((xr.shape[1], width), F32),
            shape(xr.shape, BF16),
            shape(slots + small.shape, F32),
            shape(slots + wc.shape, BF16),
            shape(slots + wg.shape, BF16),
            shape((2, 2, 2, depth) + wo.shape, BF16),
        ],
        scratch_shapes=[
            pltpu.VMEM((2, 2, 2, 2) + wc.shape, BF16),
            pltpu.SemaphoreType.DMA((2,)),
            pltpu.SemaphoreType.DMA((4,)),
            pltpu.SemaphoreType.DMA((5, sends)),
            pltpu.SemaphoreType.DMA((5, receives)),
        ],
        compiler_params=pltpu.CompilerParams(
            collective_id=0, has_side_effects=True, vmem_limit_bytes=VMEM_LIMIT
        ),
        name="gather_project",
    )(xr, small, wc, wg, wo)


def fwd_a_kernel(
    head_dim, pc_ref, w_ref, b_ref, raw_ref, sb_ref, dl_ref,
    x_ref, bc_ref, dt_ref, cum_ref, cumt_ref, loc0_ref, seg_ref, tot_ref, bt_ref,
):
    step = pl.program_id(0)
    seqs = pc_ref.shape[0]
    seg = pc_ref.shape[1] - EDGE
    chunks = seg // CHUNK
    w, b = w_ref[...], b_ref[...]

    def acts_of(s):
        pre = causal_conv(pc_ref[s], w, b, seg)
        return pre * sigmoid(pre)

    @pl.when(step == 0)
    def _():
        row = lax.broadcasted_iota(jnp.int32, (CHUNK, CHUNK), 0)
        col = lax.broadcasted_iota(jnp.int32, (CHUNK, CHUNK), 1)
        tri = (col <= row).astype(F32)
        rate = -jnp.exp(dl_ref[...])
        for s in range(seqs):
            acts = acts_of(s)
            bc_ref[s * seg : (s + 1) * seg] = acts
            for c in range(chunks):
                q = s * chunks + c
                rows = slice(q * CHUNK, (q + 1) * CHUNK)
                bt_ref[q] = acts[c * CHUNK : (c + 1) * CHUNK, :LANES].T.astype(BF16)
                dt = softplus(raw_ref[s, EDGE + c * CHUNK : EDGE + (c + 1) * CHUNK] + sb_ref[...])
                cum = LOG2E * jnp.dot(tri, dt * rate, precision=HIGH, preferred_element_type=F32)
                dt_ref[rows] = dt
                cum_ref[rows] = cum
                cumt_ref[:, rows] = cum.T

    @pl.when(step > 0)
    def _():
        heads = GROUP // head_dim
        first = (step - 1) * heads
        cumg = lane_shift(cum_ref[...], first)
        dtg = lane_shift(dt_ref[...], first)
        for s in range(seqs):
            x = acts_of(s)
            x_ref[s * seg : (s + 1) * seg] = x
            state, total = None, None
            for c in range(chunks):
                q = s * chunks + c
                rows = slice(q * CHUNK, (q + 1) * CHUNK)
                ce = spread_all(cumg[rows], heads, head_dim)
                de = spread_all(dtg[rows], heads, head_dim)
                end = ce[CHUNK - 1 : CHUNK]
                uw = x[c * CHUNK : (c + 1) * CHUNK] * de * jnp.exp2(end - ce)
                loc = dot(bt_ref[q], uw.astype(BF16))
                tot = jnp.exp2(end)
                tot_ref[q : q + 1] = tot
                if c == 0:
                    loc0_ref[s] = loc
                    state, total = loc, tot
                else:
                    state, total = tot * state + loc, tot * total
            seg_ref[s] = state.astype(BF16)
            tot_ref[seqs * chunks + s : seqs * chunks + s + 1] = total


def fwd_a(pc, w, b, sb, dl, inner, head_dim):
    seqs, rows, cols = pc.shape
    seg = rows - EDGE
    tokens = seqs * seg
    groups = inner // GROUP
    state = LANES
    chunks = tokens // CHUNK
    at = lambda i: (i + groups) % (groups + 1)
    back = lambda i: jnp.maximum(i - 1, 0)
    return pl.pallas_call(
        functools.partial(fwd_a_kernel, head_dim),
        grid=(groups + 1,),
        in_specs=[
            pl.BlockSpec((seqs, rows, GROUP), lambda i: (0, 0, at(i))),
            pl.BlockSpec((w.shape[0], GROUP), lambda i: (0, at(i))),
            pl.BlockSpec((1, GROUP), lambda i: (0, at(i))),
            pl.BlockSpec((seqs, rows, LANES), lambda i: (0, 0, cols // LANES - 1)),
            whole((1, LANES)),
            whole((1, LANES)),
        ],
        out_specs=[
            pl.BlockSpec((tokens, GROUP), lambda i: (0, back(i))),
            whole((tokens, GROUP)),
            whole((tokens, LANES)),
            whole((tokens, LANES)),
            whole((LANES, tokens)),
            pl.BlockSpec((seqs, state, GROUP), lambda i: (0, 0, back(i))),
            pl.BlockSpec((seqs, state, GROUP), lambda i: (0, 0, back(i))),
            pl.BlockSpec((8, GROUP), lambda i: (0, back(i))),
        ],
        out_shape=[
            jax.ShapeDtypeStruct((tokens, inner), F32),
            jax.ShapeDtypeStruct((tokens, GROUP), F32),
            jax.ShapeDtypeStruct((tokens, LANES), F32),
            jax.ShapeDtypeStruct((tokens, LANES), F32),
            jax.ShapeDtypeStruct((LANES, tokens), F32),
            jax.ShapeDtypeStruct((seqs, state, inner), F32),
            jax.ShapeDtypeStruct((seqs, state, inner), BF16),
            jax.ShapeDtypeStruct((8, inner), F32),
        ],
        scratch_shapes=[pltpu.VMEM((chunks, LANES, CHUNK), BF16)],
        compiler_params=params(),
        name="conv_states",
    )(pc, w, b, pc, sb, dl)


def fwd_b_kernel(
    head_dim, x_ref, bc_ref, dt_ref, cum_ref, cumt_ref, s0_ref, loc0_ref, tot_ref, skip_ref,
    mixed_ref, s1_ref, cb_ref,
):
    step = pl.program_id(0)
    seqs = s0_ref.shape[0]
    chunks = x_ref.shape[0] // CHUNK // seqs
    heads = GROUP // head_dim

    @pl.when(step == 0)
    def _():
        for q in range(seqs * chunks):
            rows = slice(q * CHUNK, (q + 1) * CHUNK)
            cb_ref[q] = nt(bc_ref[rows, LANES:].astype(BF16), bc_ref[rows, :LANES].astype(BF16))

    first = step * heads
    cumg = lane_shift(cum_ref[...], first)
    dtg = lane_shift(dt_ref[...], first)
    cumr = head_rows(cumt_ref, first)
    row = lax.broadcasted_iota(jnp.int32, (CHUNK, CHUNK), 0)
    col = lax.broadcasted_iota(jnp.int32, (CHUNK, CHUNK), 1)
    causal = col <= row
    skip = skip_ref[...]
    for s in range(seqs):
        start = s0_ref[s]
        for c in range(chunks):
            q = s * chunks + c
            rows = slice(q * CHUNK, (q + 1) * CHUNK)
            x = x_ref[rows]
            ce = spread_all(cumg[rows], heads, head_dim)
            de = spread_all(dtg[rows], heads, head_dim)
            ub = (x * de).astype(BF16)
            cb = cb_ref[q]
            parts = []
            for j in range(0, heads, 2):
                mats = []
                for h in (j, j + 1):
                    there = jnp.broadcast_to(cumg[rows, h : h + 1], (CHUNK, CHUNK))
                    here = cumr[h : h + 1, rows]
                    decay = jnp.exp2(jnp.where(causal, there - here, -jnp.inf))
                    mats.append((decay * cb).astype(BF16))
                pair = ub[:, j * head_dim : (j + 2) * head_dim]
                parts.append(dot(jnp.concatenate(mats, axis=1), block_diagonal(pair, head_dim)))
            y = jnp.concatenate(parts, axis=1)
            y = y + jnp.exp2(ce) * dot(bc_ref[rows, LANES:].astype(BF16), start)
            mixed_ref[rows] = y + skip * x
            if c == 0:
                start = (tot_ref[q : q + 1] * start.astype(F32) + loc0_ref[s]).astype(BF16)
                s1_ref[s] = start


def fwd_b(x, bc, dt, cum, cumt, s0, loc0, tot, skip, head_dim):
    tokens, inner = x.shape
    seqs, state, _ = s0.shape
    groups = inner // GROUP
    wide = pl.BlockSpec((tokens, GROUP), lambda i: (0, i))
    states = pl.BlockSpec((seqs, state, GROUP), lambda i: (0, 0, i))
    return pl.pallas_call(
        functools.partial(fwd_b_kernel, head_dim),
        grid=(groups,),
        in_specs=[
            wide, whole(bc.shape), whole(dt.shape), whole(cum.shape), whole(cumt.shape),
            states, states,
            pl.BlockSpec((8, GROUP), lambda i: (0, i)),
            pl.BlockSpec((1, GROUP), lambda i: (0, i)),
        ],
        out_specs=[wide, states],
        out_shape=[
            jax.ShapeDtypeStruct((tokens, inner), F32),
            jax.ShapeDtypeStruct((seqs, state, inner), BF16),
        ],
        scratch_shapes=[pltpu.VMEM((tokens // CHUNK, CHUNK, CHUNK), F32)],
        compiler_params=params(),
        name="scan_outputs",
    )(x, bc, dt, cum, cumt, s0, loc0, tot, skip)


def mid_kernel(
    normed_ref, wg_ref, mixed_ref, wo_ref, gain_ref, in_ref, cot_ref,
    no_ref, out_ref, dm_ref, dz_ref, gg_ref, z_ref, dno_ref, acc_ref,
):
    step = pl.program_id(0)
    inner = mixed_ref.shape[1]
    tile = 512
    tiles = inner // tile

    @pl.when(step == 0)
    def _():
        gg_ref[...] = jnp.zeros_like(gg_ref)

    def lanes_of(i):
        return pl.ds(pl.multiple_of(i * tile, tile), tile)

    def fold(v):
        total = v[:, :LANES]
        for k in range(LANES, tile, LANES):
            total = total + v[:, k : k + LANES]
        return total

    normed = normed_ref[...]
    cot = cot_ref[...]

    def one(i, sums):
        sq, hg = sums
        at = lanes_of(i)
        z = dot(normed, wg_ref[:, at])
        z_ref[:, at] = z
        g = mixed_ref[:, at] * z * sigmoid(z)
        dno = nt(cot, wo_ref[at, :])
        dno_ref[:, at] = dno
        return sq + fold(g * g), hg + fold(dno * gain_ref[:, at] * g)

    zero = jnp.zeros((normed.shape[0], LANES), F32)
    sq, hg = lax.fori_loop(0, tiles, one, (zero, zero))
    scale = lax.rsqrt(jnp.sum(sq, axis=1, keepdims=True) / inner + EPS)
    pull = scale * scale * scale * (jnp.sum(hg, axis=1, keepdims=True) / inner)
    acc_ref[...] = in_ref[...].astype(F32)

    def two(i, carry):
        at = lanes_of(i)
        z, mixed, dno, gain = z_ref[:, at], mixed_ref[:, at], dno_ref[:, at], gain_ref[:, at]
        sig = sigmoid(z)
        act = z * sig
        g = mixed * act
        gs = g * scale
        no = (gs * gain).astype(BF16)
        no_ref[:, at] = no
        acc_ref[...] += dot(no, wo_ref[at, :])
        gg_ref[:, at] += jnp.sum(dno * gs, axis=0, keepdims=True)
        dg = scale * (dno * gain) - g * pull
        dm_ref[:, at] = dg * act
        dz_ref[:, at] = (dg * mixed * (sig * (1.0 + z * (1.0 - sig)))).astype(BF16)
        return carry

    lax.fori_loop(0, tiles, two, 0)
    out_ref[...] = acc_ref[...].astype(BF16)


def mid(normed, wg, mixed, wo, gain, inputs, cot):
    tokens, inner = mixed.shape
    width = inputs.shape[1]
    narrow = pl.BlockSpec((CHUNK, width), lambda i: (i, 0))
    wide = pl.BlockSpec((CHUNK, inner), lambda i: (i, 0))
    once = lambda shape: pl.BlockSpec(shape, lambda i: (0, 0), pipeline_mode=pl.Buffered(1))
    return pl.pallas_call(
        mid_kernel,
        grid=(tokens // CHUNK,),
        in_specs=[narrow, once(wg.shape), wide, once(wo.shape), whole((1, inner)), narrow, narrow],
        out_specs=[wide, narrow, wide, wide, whole((1, inner))],
        out_shape=[
            jax.ShapeDtypeStruct((tokens, inner), BF16),
            jax.ShapeDtypeStruct((tokens, width), BF16),
            jax.ShapeDtypeStruct((tokens, inner), F32),
            jax.ShapeDtypeStruct((tokens, inner), BF16),
            jax.ShapeDtypeStruct((1, inner), F32),
        ],
        scratch_shapes=[
            pltpu.VMEM((CHUNK, inner), F32),
            pltpu.VMEM((CHUNK, inner), F32),
            pltpu.VMEM((CHUNK, width), F32),
        ],
        compiler_params=params(),
        name="gate_norm_project",
    )(normed, wg, mixed, wo, gain, inputs, cot)


def bwd_a_kernel(head_dim, seqs, dm_ref, bc_ref, cum_ref, tot_ref, seg_ref, ct_ref):
    step = pl.program_id(0)
    chunks = dm_ref.shape[0] // CHUNK // seqs
    heads = GROUP // head_dim

    @pl.when(step == 0)
    def _():
        for q in range(seqs * chunks):
            ct_ref[q] = bc_ref[q * CHUNK : (q + 1) * CHUNK, LANES:].T.astype(BF16)

    cumg = lane_shift(cum_ref[...], step * heads)
    for s in range(seqs):
        state = None
        for c in range(chunks - 1, -1, -1):
            q = s * chunks + c
            rows = slice(q * CHUNK, (q + 1) * CHUNK)
            ey = jnp.exp2(spread_all(cumg[rows], heads, head_dim)) * dm_ref[rows]
            loc = dot(ct_ref[q], ey.astype(BF16))
            state = loc if state is None else tot_ref[q : q + 1] * state + loc
        seg_ref[s] = state.astype(BF16)


def bwd_a(dm, bc, cum, tot, seqs, head_dim):
    tokens, inner = dm.shape
    return pl.pallas_call(
        functools.partial(bwd_a_kernel, head_dim, seqs),
        grid=(inner // GROUP,),
        in_specs=[
            pl.BlockSpec((tokens, GROUP), lambda i: (0, i)), whole(bc.shape), whole(cum.shape),
            pl.BlockSpec((8, GROUP), lambda i: (0, i)),
        ],
        out_specs=pl.BlockSpec((seqs, LANES, GROUP), lambda i: (0, 0, i)),
        out_shape=jax.ShapeDtypeStruct((seqs, LANES, inner), BF16),
        scratch_shapes=[pltpu.VMEM((tokens // CHUNK, LANES, CHUNK), BF16)],
        compiler_params=params(),
        name="adjoint_states",
    )(dm, bc, cum, tot)


def bwd_b_kernel(
    head_dim, groups, pc_ref, w_ref, b_ref, raw_ref, sb_ref, dl_ref, bc_ref, dt_ref, cum_ref, cumt_ref,
    dm_ref, mixed_ref, s0_ref, s1_ref, s2_ref, g_ref, tot_ref, skip_ref,
    dc_ref, tail_ref, edge_ref, gw_ref, gb_ref, gskip_ref, draw_ref, hsum_ref,
    cbt_ref, dcbt_ref, db_acc, dc_acc, r1_ref, r2_ref, dtot_ref,
):
    step = pl.program_id(0)
    seqs = pc_ref.shape[0]
    seg = pc_ref.shape[1] - EDGE
    chunks = seg // CHUNK
    heads = GROUP // head_dim
    w, b = w_ref[...], b_ref[...]
    taps = w.shape[0]

    @pl.when(step == 0)
    def _():
        for q in range(seqs * chunks):
            rows = slice(q * CHUNK, (q + 1) * CHUNK)
            cbt_ref[q] = nt(bc_ref[rows, :LANES].astype(BF16), bc_ref[rows, LANES:].astype(BF16))
        dcbt_ref[...] = jnp.zeros_like(dcbt_ref)
        db_acc[...] = jnp.zeros_like(db_acc)
        dc_acc[...] = jnp.zeros_like(dc_acc)
        r1_ref[...] = jnp.zeros_like(r1_ref)
        r2_ref[...] = jnp.zeros_like(r2_ref)
        dtot_ref[...] = jnp.zeros_like(dtot_ref)

    def conv_back(s, ext, pre, sig, d_act):
        d_pre = d_act * (sig * (1.0 + pre * (1.0 - sig)))
        zero = jnp.zeros((EDGE, d_pre.shape[1]), F32)
        padded = jnp.concatenate([zero, d_pre, zero], axis=0)
        total = None
        for k in range(taps):
            at = taps - 1 - k
            term = w[k : k + 1] * padded[at : at + seg + EDGE]
            total = term if total is None else total + term
        edge_ref[s] = total[:EDGE]
        dc_ref[s * seg : (s + 1) * seg] = total[EDGE:].astype(BF16)
        tail_ref[s] = total[seg:]
        for k in range(taps):
            at = EDGE - (taps - 1) + k
            grad = jnp.sum(ext[at : at + seg] * d_pre, axis=0, keepdims=True)
            gw_ref[k : k + 1] = grad if s == 0 else gw_ref[k : k + 1] + grad
        grad = jnp.sum(d_pre, axis=0, keepdims=True)
        gb_ref[...] = grad if s == 0 else gb_ref[...] + grad

    def by_head(value, pick):
        high = value.astype(BF16)
        return dot(high, pick) + dot((value - high.astype(F32)).astype(BF16), pick)

    @pl.when(step < groups)
    def _():
        first = step * heads
        cumg = lane_shift(cum_ref[...], first)
        dtg = lane_shift(dt_ref[...], first)
        cumr = head_rows(cumt_ref, first)
        row = lax.broadcasted_iota(jnp.int32, (CHUNK, CHUNK), 0)
        col = lax.broadcasted_iota(jnp.int32, (CHUNK, CHUNK), 1)
        causal = row <= col
        lane = lax.broadcasted_iota(jnp.int32, (GROUP, LANES), 0)
        head = lax.broadcasted_iota(jnp.int32, (GROUP, LANES), 1)
        pick = (head == first + lane // head_dim).astype(BF16)
        skip = skip_ref[...]
        grad_skip = None
        for s in range(seqs):
            ext = pc_ref[s]
            pre = causal_conv(ext, w, b, seg)
            sig = sigmoid(pre)
            acts = pre * sig
            adj = g_ref[s].astype(F32)
            d_acts = [None] * chunks
            for c in range(chunks - 1, -1, -1):
                q = s * chunks + c
                rows = slice(q * CHUNK, (q + 1) * CHUNK)
                x = acts[c * CHUNK : (c + 1) * CHUNK]
                dy = dm_ref[rows]
                ce = spread_all(cumg[rows], heads, head_dim)
                de = spread_all(dtg[rows], heads, head_dim)
                weight = jnp.exp2(ce[CHUNK - 1 : CHUNK] - ce)
                u = x * de
                ub = u.astype(BF16)
                dyb = dy.astype(BF16)
                cbt = cbt_ref[q]
                parts = []
                dcbt = dcbt_ref[q]
                for j in range(0, heads, 2):
                    lanes = slice(j * head_dim, (j + 2) * head_dim)
                    dy_block = block_diagonal(dyb[:, lanes], head_dim)
                    dm = nt(ub[:, lanes], dy_block)
                    mats = []
                    for k, h in enumerate((j, j + 1)):
                        here = jnp.broadcast_to(cumg[rows, h : h + 1], (CHUNK, CHUNK))
                        there = cumr[h : h + 1, rows]
                        decay = jnp.exp2(jnp.where(causal, there - here, -jnp.inf))
                        mats.append((decay * cbt).astype(BF16))
                        dcbt = dcbt + decay * dm[:, k * CHUNK : (k + 1) * CHUNK]
                    parts.append(dot(jnp.concatenate(mats, axis=1), dy_block))
                dcbt_ref[q] = dcbt
                start = s0_ref[s] if c == 0 else s1_ref[s]
                end = s2_ref[s] if c == chunks - 1 else s1_ref[s]
                adj_b = adj.astype(BF16)
                bb = bc_ref[rows, :LANES].astype(BF16)
                cb = bc_ref[rows, LANES:].astype(BF16)
                ey = (jnp.exp2(ce) * dy).astype(BF16)
                du = jnp.concatenate(parts, axis=1) + weight * dot(bb, adj_b)
                db_acc[rows] += nt((u * weight).astype(BF16), adj_b)
                dc_acc[rows] += nt(ey, start)
                r1_ref[rows] += by_head(dyb.astype(F32) * (mixed_ref[rows] - skip * x), pick)
                r2_ref[rows] += by_head(x * du, pick)
                dtot_ref[q : q + 1] += by_head(
                    jnp.sum(adj * end.astype(F32), axis=0, keepdims=True), pick
                )
                grad = jnp.sum(dy * x, axis=0, keepdims=True)
                grad_skip = grad if grad_skip is None else grad_skip + grad
                d_acts[c] = du * de + skip * dy
                if c > 0:
                    adj = tot_ref[q : q + 1] * adj + dot(cb, ey, ((0,), (0,)))
            conv_back(s, ext, pre, sig, jnp.concatenate(d_acts, axis=0))
        gskip_ref[...] = grad_skip

    @pl.when(step == groups)
    def _():
        row = lax.broadcasted_iota(jnp.int32, (CHUNK, CHUNK), 0)
        col = lax.broadcasted_iota(jnp.int32, (CHUNK, CHUNK), 1)
        later = (row <= col).astype(F32)
        rate = -jnp.exp(dl_ref[...])
        sum_raw = jnp.zeros((1, LANES), F32)
        sum_log = jnp.zeros((1, LANES), F32)
        for s in range(seqs):
            ext = pc_ref[s]
            pre = causal_conv(ext, w, b, seg)
            sig = sigmoid(pre)
            parts = []
            for c in range(chunks):
                q = s * chunks + c
                rows = slice(q * CHUNK, (q + 1) * CHUNK)
                dcbt = dcbt_ref[q]
                bb = bc_ref[rows, :LANES].astype(BF16)
                cb = bc_ref[rows, LANES:].astype(BF16)
                d_b = db_acc[rows] + dot(dcbt.astype(BF16), cb)
                d_c = dc_acc[rows] + dot(dcbt.T.astype(BF16), bb)
                parts.append(jnp.concatenate([d_b, d_c], axis=1))
                dt = dt_ref[rows]
                r2 = r2_ref[rows]
                d_log = jnp.dot(
                    later, r1_ref[rows] - dt * r2, precision=HIGH, preferred_element_type=F32
                )
                d_log = d_log + dtot_ref[q : q + 1]
                raw = raw_ref[s, EDGE + c * CHUNK : EDGE + (c + 1) * CHUNK] + sb_ref[...]
                d_raw = (r2 + rate * d_log) * sigmoid(raw)
                draw_ref[rows] = d_raw
                sum_raw = sum_raw + jnp.sum(d_raw, axis=0, keepdims=True)
                sum_log = sum_log + jnp.sum(d_log * dt, axis=0, keepdims=True) * rate
            conv_back(s, ext, pre, sig, jnp.concatenate(parts, axis=0))
        hsum_ref[0:1] = sum_raw
        hsum_ref[1:2] = sum_log


def bwd_b(pc, w, b, sb, dl, bc, dt, cum, cumt, dm, mixed, s0, s1, s2, g, tot, skip, head_dim):
    seqs, rows, cols = pc.shape
    tokens, inner = dm.shape
    groups = inner // GROUP
    taps, channels = w.shape
    wide = pl.BlockSpec((tokens, GROUP), lambda i: (0, jnp.minimum(i, groups - 1)))
    states = pl.BlockSpec((seqs, LANES, GROUP), lambda i: (0, 0, jnp.minimum(i, groups - 1)))
    line = lambda n: pl.BlockSpec((n, GROUP), lambda i: (0, jnp.minimum(i, groups - 1)))
    conv = lambda n: pl.BlockSpec((n, GROUP), lambda i: (0, i))
    ends = pl.BlockSpec((seqs, EDGE, GROUP), lambda i: (0, 0, i))
    chunks = tokens // CHUNK
    shape = jax.ShapeDtypeStruct
    return pl.pallas_call(
        functools.partial(bwd_b_kernel, head_dim, groups),
        grid=(groups + 1,),
        in_specs=[
            pl.BlockSpec((seqs, rows, GROUP), lambda i: (0, 0, i)),
            conv(taps),
            conv(1),
            pl.BlockSpec((seqs, rows, LANES), lambda i: (0, 0, cols // LANES - 1)),
            whole((1, LANES)), whole((1, LANES)),
            whole(bc.shape), whole(dt.shape), whole(cum.shape), whole(cumt.shape),
            wide, wide, states, states, states, states, line(8), line(1),
        ],
        out_specs=[
            conv(tokens), ends, ends, conv(taps), conv(1), line(1),
            whole((tokens, LANES)), whole((2, LANES)),
        ],
        out_shape=[
            shape((tokens, channels), BF16),
            shape((seqs, EDGE, channels), F32),
            shape((seqs, EDGE, channels), F32),
            shape((taps, channels), F32),
            shape((1, channels), F32),
            shape((1, inner), F32),
            shape((tokens, LANES), F32),
            shape((2, LANES), F32),
        ],
        scratch_shapes=[
            pltpu.VMEM((chunks, CHUNK, CHUNK), F32),
            pltpu.VMEM((chunks, CHUNK, CHUNK), F32),
            pltpu.VMEM((tokens, LANES), F32),
            pltpu.VMEM((tokens, LANES), F32),
            pltpu.VMEM((tokens, LANES), F32),
            pltpu.VMEM((tokens, LANES), F32),
            pltpu.VMEM((8, LANES), F32),
        ],
        compiler_params=params(),
        name="scan_backward",
    )(pc, w, b, pc, sb, dl, bc, dt, cum, cumt, dm, mixed, s0, s1, s2, g, tot, skip)


def passed_along(value, axis, steps):
    count = lax.axis_size(axis)
    initial, last = (max(0, -steps), min(count, count - steps))
    return lax.ppermute(value, axis, [(source, source + steps) for source in range(initial, last)])


def prefix(total, local, axis, backward):
    count, here = lax.axis_size(axis), lax.axis_index(axis)
    totals = lax.all_gather(total.astype(BF16), axis)
    locals_ = lax.all_gather(local, axis)
    state = jnp.zeros(local.shape, F32)
    order = range(count - 1, 0, -1) if backward else range(count - 1)
    for lap in order:
        new = totals[lap].astype(F32) * state + locals_[lap].astype(F32)
        reached = lap > here if backward else lap < here
        state = jnp.where(reached, new, state)
    leaves = total * state + local.astype(F32)
    return state.astype(BF16), leaves.astype(BF16)


AXES = ("dp", "ctx")


def body(
    inputs, gain_in, in_weight, conv_weight, conv_bias, step_bias, decay_log, skip_gain, gain_out,
    out_weight, cotangent,
):
    seqs, seg, width = inputs.shape
    tokens = seqs * seg
    count = lax.axis_size(AXES)
    inner = out_weight.shape[0] * count
    taps, channels = conv_weight.shape[0], conv_weight.shape[1] * count
    num_heads = step_bias.shape[0]
    head_dim = inner // num_heads

    w_gate = in_weight[:, :inner]
    w_conv = in_weight[:, inner:]
    spare = -w_conv.shape[1] % LANES
    w_conv = jnp.pad(w_conv, ((0, 0), (0, spare)))
    a, b, c = gain_in.shape[0], gain_out.shape[0], conv_bias.shape[0]
    dp, depth = lax.axis_size("dp"), lax.axis_size("ctx")
    fast = dp == 8
    rest = jnp.concatenate([gain_out, conv_bias, conv_weight.reshape(-1)])

    before = passed_along(inputs[:, seg - (taps - 1) :], "ctx", 1)
    ext = jnp.concatenate(
        [jnp.zeros((seqs, EDGE - (taps - 1), width), inputs.dtype), before, inputs], axis=1
    ).astype(F32)
    scale_ext = lax.rsqrt(jnp.mean(ext * ext, axis=-1, keepdims=True) + EPS)
    flat_rows = seqs * (seg + EDGE)
    hat_ext = (ext * scale_ext).reshape(flat_rows, width)

    if fast:
        head = jnp.zeros((dp * a,), F32)
        head = lax.dynamic_update_slice(head, gain_in.astype(F32), (lax.axis_index("dp") * a,))
        small = jnp.concatenate([head, rest.astype(F32)])
        small = jnp.pad(small, (0, 8 * LANES - small.size)).reshape(8, LANES)
        hat_z = hat_ext.reshape(flat_rows, dp, depth, a).transpose(2, 0, 1, 3)
        hat_z = hat_z.reshape(depth, flat_rows, dp * a)
        pc, normed, small, w_conv, w_gate, w_out = gather_project(
            hat_z, small, w_conv, w_gate, out_weight, depth
        )
        w_conv = w_conv.reshape(width, -1)
        w_gate = w_gate.reshape(width, inner)
        w_out = w_out.reshape(inner, width)
        normed = normed.reshape(depth, seqs, seg + EDGE, dp * a)[:, :, EDGE:]
        normed = normed.transpose(1, 2, 0, 3).reshape(tokens, width)
        small = small.reshape(depth, dp, 8 * LANES)
        g_in = small[:, :, : dp * a].sum(axis=1).reshape(depth, dp, a)
        g_in = g_in.transpose(1, 0, 2).reshape(1, width)
        rest = small.transpose(1, 0, 2).reshape(count, 8 * LANES)[:, dp * a :]
        plain = lambda v: v.reshape(-1, depth, dp, a).transpose(0, 2, 1, 3).reshape(-1, width)
    else:
        small = lax.all_gather(jnp.concatenate([gain_in, rest]), AXES).astype(F32)
        w_conv = lax.all_gather(w_conv, AXES, axis=0, tiled=True)
        w_gate = lax.all_gather(w_gate, AXES, axis=0, tiled=True)
        w_out = lax.all_gather(out_weight, AXES, axis=0, tiled=True)
        g_in, rest = small[:, :a].reshape(1, width), small[:, a:]
        normed_ext = (hat_ext * g_in).astype(BF16)
        pc = dot(normed_ext, w_conv)
        normed = normed_ext.reshape(seqs, seg + EDGE, width)[:, EDGE:].reshape(tokens, width)
        plain = lambda v: v
    pc = pc.reshape(seqs, seg + EDGE, -1)
    g_out = rest[:, :b].reshape(1, inner)
    bias = rest[:, b : b + c].reshape(1, channels)
    kernel = rest[:, b + c : b + c + taps * c].reshape(count, taps, c).transpose(1, 0, 2)
    kernel = kernel.reshape(taps, channels)
    pad_head = lambda v: jnp.pad(v, (0, LANES - num_heads)).reshape(1, LANES)
    sb, dl = pad_head(step_bias), pad_head(decay_log)
    skip = jnp.repeat(skip_gain, head_dim).reshape(1, inner)

    x, bc, dt, cum, cumt, loc0, local, tot = fwd_a(pc, kernel, bias, sb, dl, inner, head_dim)
    per_seq = tot[tokens // CHUNK : tokens // CHUNK + seqs][:, None, :]
    s0, s2 = prefix(per_seq, local, "ctx", False)
    mixed, s1 = fwd_b(x, bc, dt, cum, cumt, s0, loc0, tot, skip, head_dim)

    flat = inputs.reshape(tokens, width)
    cot = cotangent.reshape(tokens, width)
    normed_out, output, d_mixed, d_gate, grad_gain_out = mid(
        normed, w_gate, mixed, w_out, g_out, flat, cot
    )
    scatter = lambda v: lax.psum_scatter(v, AXES, scatter_dimension=0, tiled=True).astype(F32)
    grad_out_weight = scatter(dot(normed_out, cot, ((0,), (0,))).astype(BF16))
    normed_plain = plain(normed)
    grad_gate_weight = scatter(dot(normed_plain, d_gate, ((0,), (0,))).astype(BF16))

    adjoint = bwd_a(d_mixed, bc, cum, tot, seqs, head_dim)
    g, _ = prefix(per_seq, adjoint, "ctx", True)
    d_conv, tail, edge, grad_kernel, grad_bias, grad_skip, d_raw, head_sums = bwd_b(
        pc, kernel, bias, sb, dl, bc, dt, cum, cumt, d_mixed, mixed, s0, s1, s2, g, tot, skip, head_dim
    )
    after = passed_along(edge[:, EDGE - (taps - 1) :].astype(BF16), "ctx", -1).astype(F32)
    tail = tail[:, EDGE - (taps - 1) :] + after
    d_conv = d_conv.reshape(seqs, seg, channels).at[:, seg - (taps - 1) :].set(tail.astype(BF16))
    d_conv = jnp.concatenate([d_conv.reshape(tokens, channels), d_raw.astype(BF16)], axis=1)

    real = d_conv.shape[1] - spare
    grad_conv_cols = scatter(dot(normed_plain, d_conv[:, :real], ((0,), (0,))).astype(BF16))
    d_normed = plain(nt(d_gate, w_gate) + nt(d_conv, w_conv))
    values = flat.astype(F32)
    scale = scale_ext[:, EDGE:].reshape(tokens, 1)
    hat = values * scale
    grad_gain_in = jnp.sum(d_normed * hat, axis=0)
    weighted = d_normed * g_in
    pull = jnp.mean(weighted * hat, axis=-1, keepdims=True)
    grad_input = scale * (weighted - hat * pull) + cot.astype(F32)

    grad_in_weight = jnp.concatenate(
        [grad_gate_weight, grad_conv_cols], axis=1
    )
    by_owner = jnp.concatenate(
        [
            grad_gain_in.reshape(count, a),
            grad_gain_out.reshape(count, b),
            grad_bias.reshape(count, c),
            grad_kernel.reshape(taps, count, c).transpose(1, 0, 2).reshape(count, taps * c),
        ],
        axis=1,
    )
    grad_skip = jnp.sum(grad_skip.reshape(num_heads, head_dim), axis=1)
    heads_sum = jnp.concatenate(
        [head_sums[0, :num_heads], head_sums[1, :num_heads], grad_skip]
    )
    everyone = lax.psum(jnp.concatenate([by_owner.reshape(-1), heads_sum]), AXES)
    mine = lax.dynamic_slice_in_dim(
        everyone[: by_owner.size].reshape(count, -1), lax.axis_index(AXES), 1, 0
    )[0]
    head_totals = everyone[by_owner.size :].reshape(3, num_heads)
    return (
        output.reshape(seqs, seg, width),
        grad_input.reshape(seqs, seg, width),
        mine[:a],
        grad_in_weight,
        mine[a + b + c :].reshape(taps, c),
        mine[a + b : a + b + c],
        head_totals[0],
        head_totals[1],
        head_totals[2],
        mine[a : a + b],
        grad_out_weight,
    )


def solution(mesh):
    rows, cols, both = P("dp", "ctx", None), P(AXES, None), P(AXES)
    return jax.shard_map(
        body,
        mesh=mesh,
        in_specs=(rows, both, cols, P(None, AXES), both, P(), P(), P(), both, cols, rows),
        out_specs=(rows, rows, both, cols, P(None, AXES), both, P(), P(), P(), both, cols),
        check_vma=False,
    )
```

```python
import functools

import jax
import jax.numpy as jnp
from jax import lax
from jax.experimental import pallas as pl
from jax.experimental.pallas import tpu as pltpu
from jax.sharding import PartitionSpec as P

EPS = 1e-05
LOG2E = 1.4426950408889634
HIGH = lax.Precision.HIGHEST
F32 = jnp.float32
BF16 = jnp.bfloat16
CHUNK = 128
GROUP = 256
EDGE = 16
LANES = 128
VMEM_LIMIT = 56 * 1024 * 1024


def dot(a, b, dims=((1,), (0,))):
    return lax.dot_general(a, b, (dims, ((), ())), preferred_element_type=F32)


def nt(a, b):
    return dot(a, b, ((1,), (1,)))


def params():
    return pltpu.CompilerParams(
        dimension_semantics=("arbitrary",), vmem_limit_bytes=VMEM_LIMIT
    )


def whole(shape):
    return pl.BlockSpec(shape, lambda i: (0,) * len(shape))


def sigmoid(v):
    return 1.0 / (1.0 + jnp.exp(-v))


def softplus(v):
    return jnp.maximum(v, 0.0) + jnp.log1p(jnp.exp(-jnp.abs(v)))


def causal_conv(ext, w, b, seg):
    taps = w.shape[0]
    total = b
    for k in range(taps):
        at = EDGE - (taps - 1) + k
        total = total + w[k : k + 1] * ext[at : at + seg]
    return total


def lane_shift(value, lanes):
    return pltpu.roll(value, lax.rem(LANES - lanes, LANES), 1)


def head_rows(ref, first):
    base = pl.multiple_of(first // 8 * 8, 8)
    return pltpu.roll(ref[pl.ds(base, 8), :], lax.rem(8 - lax.rem(first, 8), 8), 0)


def spread(cols, at, head_dim):
    rows = cols.shape[0]
    lane = lax.broadcasted_iota(jnp.int32, (rows, LANES), 1)
    first = jnp.broadcast_to(cols[:, at : at + 1], (rows, LANES))
    second = jnp.broadcast_to(cols[:, at + 1 : at + 2], (rows, LANES))
    return jnp.where(lane < head_dim, first, second)


def spread_all(cols, heads, head_dim):
    return jnp.concatenate([spread(cols, j, head_dim) for j in range(0, heads, 2)], axis=1)


def block_diagonal(pair, head_dim):
    lane = lax.broadcasted_iota(jnp.int32, pair.shape, 1)
    zero = jnp.zeros_like(pair)
    return jnp.concatenate(
        [jnp.where(lane < head_dim, pair, zero), jnp.where(lane < head_dim, zero, pair)], axis=0
    )


MESH = pl.DeviceIdType.MESH


class Place:
    def __init__(self, depth):
        dp, z = lax.axis_index("dp"), lax.axis_index("ctx")
        self.depth, self.z = depth, z
        self.own = {"y": lax.div(dp, 4), "x": lax.rem(lax.div(dp, 2), 2), "c": lax.rem(dp, 2)}
        self.to = {
            name: {"dp": dp + step * (1 - 2 * self.own[name])}
            for name, step in (("y", 4), ("x", 2), ("c", 1))
        }
        self.has_left, self.has_right = z > 0, z < depth - 1
        self.left, self.right = {"ctx": z - 1}, {"ctx": z + 1}

    def flipped(self, *names):
        return {n: 1 - v if n in names else v for n, v in self.own.items()}

    def near(self, k):
        z, last = self.z, self.depth - 1
        reach = jnp.minimum(z, last - z)
        pair = jnp.where(k % 2 == 1, z - (k + 1) // 2, z + k // 2)
        alone = jnp.where(z > last - z, last - k, k)
        return z if k == 0 else jnp.where(k <= 2 * reach, pair, alone)

    def meet(self):
        barrier = pltpu.get_barrier_semaphore()
        signal = functools.partial(pl.semaphore_signal, barrier, inc=1, device_id_type=MESH)
        for name in ("y", "x", "c"):
            signal(device_id=self.to[name])
        pl.when(self.has_left)(lambda: signal(device_id=self.left))
        pl.when(self.has_right)(lambda: signal(device_id=self.right))
        ends = self.has_left.astype(jnp.int32) + self.has_right.astype(jnp.int32)
        pl.semaphore_wait(barrier, 3 + ends)


def remote(src, dst, send, recv, to):
    return pltpu.make_async_remote_copy(
        src_ref=src, dst_ref=dst, send_sem=send, recv_sem=recv, device_id=to, device_id_type=MESH
    )


class Gather:
    def __init__(self, place, src, slot, first, second, send, recv):
        self.place, self.src, self.slot_of = place, src, slot
        self.first, self.second, self.send, self.recv = first, second, send, recv

    @staticmethod
    def sems(depth):
        return 9 * depth, 8 * depth

    def slot(self, k, *flips):
        return self.slot_of(self.place.near(k), **self.place.flipped(*flips))

    def copy(self, k, kind, where, to, recv):
        src = self.src if k == 0 and where == () else self.slot(k, *where)
        send = self.send.at[kind * self.place.depth + k]
        return remote(src, self.slot(k, *where), send, self.recv.at[recv], to)

    def along(self, k, right):
        p = self.place
        return self.copy(k, int(right), (), p.right if right else p.left, p.near(k))

    def goes(self, k, right):
        p, at = self.place, self.place.near(k)
        if right:
            return p.has_right if k == 0 else p.has_right & (at < p.z)
        return p.has_left if k == 0 else p.has_left & (at > p.z)

    def to_axis(self, k, stage):
        p, depth = self.place, self.place.depth
        f, s = self.first, self.second
        where = ((), (), (f,), (), (f,), (s,), (f, s))[stage]
        to = p.to[(f, s, s, "c", "c", "c", "c")[stage]]
        return self.copy(k, 2 + stage, where, to, (1 + stage) * depth + k)

    def arrived(self, k, stage):
        p, depth = self.place, self.place.depth
        f, s = self.first, self.second
        where = ((f,), (s,), (s, f), ("c",), ("c", f), ("c", s), ("c", f, s))[stage]
        self.copy(k, 2 + stage, where, p.to["c"], (1 + stage) * depth + k).wait_recv()

    def line(self, k):
        if k:
            self.along(k, True).wait_recv()
        for right in (True, False):
            pl.when(self.goes(k, right))(lambda: self.along(k, right).start())
        for stage in (0, 1, 3):
            self.to_axis(k, stage).start()

    def from_first(self, k):
        self.arrived(k, 0)
        self.to_axis(k, 2).start()
        self.to_axis(k, 4).start()

    def from_second(self, k):
        self.arrived(k, 1)
        self.to_axis(k, 5).start()

    def from_both(self, k):
        self.arrived(k, 2)
        self.to_axis(k, 6).start()

    def finish(self):
        for k in range(self.place.depth):
            for right in (True, False):
                pl.when(self.goes(k, right))(lambda: self.along(k, right).wait_send())
            for stage in range(7):
                self.to_axis(k, stage).wait_send()


class Line:
    def __init__(self, place, keep, sent, came, send, recv):
        self.place, self.keep, self.sent, self.came = place, keep, sent, came
        self.send, self.recv = send, recv

    def copy(self, k, to, at):
        zk = self.place.near(k)
        return remote(self.sent.at[zk], self.came.at[at], self.send.at[k], self.recv.at[at], to)

    def take(self, at):
        self.copy(1, self.place.left, at).wait_recv()
        zk = jnp.where(at == self.place.depth, self.place.z, at)
        self.keep[zk] = self.keep[zk] + self.came[at].astype(F32)

    def moves(self, k):
        p, zk = self.place, self.place.near(k)
        return (
            (zk < p.z, p.left, zk),
            (zk > p.z, p.right, jnp.where(zk == p.z + 1, p.depth, zk)),
        )

    def step(self, k):
        p, zk = self.place, self.place.near(k)
        if k == 0:
            pl.when(p.has_right)(lambda: self.take(p.z))
            pl.when(p.has_left)(lambda: self.take(p.depth))
            return
        farther = ((zk < p.z) & p.has_right) | ((zk > p.z) & p.has_left)
        pl.when(farther)(lambda: self.take(zk))
        self.sent[zk] = self.keep[zk].astype(self.sent.dtype)
        for goes, to, at in self.moves(k):
            pl.when(goes)(lambda: self.copy(k, to, at).start())

    def finish(self):
        for k in range(1, self.place.depth):
            for goes, to, at in self.moves(k):
                pl.when(goes)(lambda: self.copy(k, to, at).wait_send())


class Scatter:
    def __init__(self, place, lhs, lhs_pair, rhs, rhs_pair, first, second, bufs, send, recv):
        self.place, self.lhs, self.lhs_pair, self.rhs, self.rhs_pair = place, lhs, lhs_pair, rhs, rhs_pair
        self.first, self.second, self.send, self.recv = first, second, send, recv
        self.s_sent, self.s_came, self.f_sent, self.f_came, self.keep, z_sent, z_came = bufs
        depth = place.depth
        self.sums = Line(place, self.keep, z_sent, z_came, send.at[pl.ds(3 * depth, depth)],
                         recv.at[pl.ds(3 * depth, depth + 1)])

    @staticmethod
    def sems(depth):
        return 4 * depth, 4 * depth + 1

    @staticmethod
    def scratch(depth, rows, cols):
        block = lambda *lead: pltpu.VMEM(lead + (rows, cols), BF16)
        return [
            block(2, depth), block(2, depth), block(depth), block(depth),
            pltpu.VMEM((depth, rows, cols), F32), block(depth), block(depth + 1),
        ]

    def product(self, flips, store):
        at = self.place.flipped(*flips)
        pair = 2 * at["y"] + at["x"]
        one = 2 * pair + at["c"]
        rows, cols = self.keep.shape[1:]
        tile = 512

        def block(start, size):
            lanes = pl.ds(start, size)
            part = dot(self.lhs[one], self.rhs[:, lanes]) + dot(self.lhs_pair[pair], self.rhs_pair[:, lanes])
            for z in range(self.place.depth):
                store(z, lanes, part[z * rows : (z + 1) * rows])

        def loop(i, carry):
            block(pl.multiple_of(i * tile, tile), tile)
            return carry

        lax.fori_loop(0, cols // tile, loop, 0)
        if cols % tile:
            block(cols // tile * tile, cols % tile)

    def to_second(self, j, k):
        zk, n = self.place.near(k), j * self.place.depth + k
        return remote(self.s_sent.at[j, zk], self.s_came.at[j, zk], self.send.at[n], self.recv.at[n],
                      self.place.to[self.second])

    def to_first(self, k):
        zk, n = self.place.near(k), 2 * self.place.depth + k
        return remote(self.f_sent.at[zk], self.f_came.at[zk], self.send.at[n], self.recv.at[n],
                      self.place.to[self.first])

    def waves(self):
        return range(self.place.depth - 1, -1, -1)

    def send_second(self, j):
        def store(z, lanes, part):
            self.s_sent[j, z, :, lanes] = part.astype(BF16)

        self.product((self.second, self.first) if j == 0 else (self.second,), store)
        for k in self.waves():
            self.to_second(j, k).start()

    def send_first(self):
        for k in self.waves():
            self.to_second(0, k).wait_recv()

        def store(z, lanes, part):
            self.f_sent[z, :, lanes] = (part + self.s_came[0, z, :, lanes].astype(F32)).astype(BF16)

        self.product((self.first,), store)
        for k in self.waves():
            self.to_first(k).start()

    def hold(self):
        for k in self.waves():
            self.to_second(1, k).wait_recv()

        def store(z, lanes, part):
            self.keep[z, :, lanes] = part + self.s_came[1, z, :, lanes].astype(F32)

        self.product((), store)

    def step(self, k):
        self.to_first(k).wait_recv()
        zk = self.place.near(k)
        self.keep[zk] = self.keep[zk] + self.f_came[zk].astype(F32)
        self.sums.step(k)

    def finish(self):
        for k in self.waves():
            self.to_second(0, k).wait_send()
            self.to_second(1, k).wait_send()
            self.to_first(k).wait_send()
        self.sums.finish()


class SmallScatter:
    def __init__(self, place, src, c_came, half, x_came, keep, y_came, z_sent, z_came, send, recv):
        self.place, self.src, self.c_came, self.half = place, src, c_came, half
        self.x_came, self.keep, self.y_came = x_came, keep, y_came
        self.send, self.recv = send, recv
        depth = place.depth
        self.sums = Line(place, keep, z_sent, z_came, send.at[pl.ds(7, depth)],
                         recv.at[pl.ds(7, depth + 1)])

    @staticmethod
    def sems(depth):
        return 7 + depth, 8 + depth

    @staticmethod
    def scratch(depth, shape):
        block = lambda *lead: pltpu.VMEM(lead + shape, F32)
        return [
            block(2, 2, depth), block(2, 2, depth), block(2, depth), block(depth), block(depth),
            block(depth), block(depth + 1),
        ]

    def copy(self, n):
        p, own = self.place, self.place.own
        if n < 4:
            y, x = n // 2, n % 2
            src, dst, to = self.src.at[y, x, 1 - own["c"]], self.c_came.at[y, x], "c"
        elif n < 6:
            src, dst, to = self.half.at[n - 4, 1 - own["x"]], self.x_came.at[n - 4], "x"
        else:
            src, dst, to = self.half.at[1 - own["y"], own["x"]], self.y_came, "y"
        return remote(src, dst, self.send.at[n], self.recv.at[n], p.to[to])

    def stage(self, n):
        own = self.place.own
        if n == 0:
            for i in range(4):
                self.copy(i).start()
        elif n == 1:
            for i in range(4):
                self.copy(i).wait_recv()
            for y in (0, 1):
                for x in (0, 1):
                    self.half[y, x] = self.src[y, x, own["c"]] + self.c_came[y, x]
            for i in (4, 5):
                self.copy(i).start()
        elif n == 2:
            for i in (4, 5):
                self.copy(i).wait_recv()
            for y in (0, 1):
                self.half[y, own["x"]] = self.half[y, own["x"]] + self.x_came[y]
            self.copy(6).start()
        else:
            self.copy(6).wait_recv()
            self.keep[...] = self.half[own["y"], own["x"]] + self.y_came[...]

    def finish(self):
        for n in range(7):
            self.copy(n).wait_send()
        self.sums.finish()


def gather_kernel(
    depth, half, x_ref, small_src, wc_src, pc_ref, normed_ref, normt_ref, small_ref, wc_ref,
    hat_ref, edge_ref, buf_ref, edge_sem, load_sem, own_sem, send, recv,
):
    place = Place(depth)
    place.meet()
    seqs, seg, features = x_ref.shape
    width = wc_src.shape[1]
    lo, hi = pl.ds(0, half), pl.ds(half, width - half)
    lanes = [
        Gather(place, small_src, lambda z, y, x, c: small_ref.at[y, x, c, z], "y", "x",
               send.at[0], recv.at[0]),
        Gather(place, wc_src.at[:, lo], lambda z, y, x, c: wc_ref.at[y, x, c, z, :, lo], "y", "x",
               send.at[1], recv.at[1]),
        Gather(place, wc_src.at[:, hi], lambda z, y, x, c: wc_ref.at[y, x, c, z, :, hi], "x", "y",
               send.at[2], recv.at[2]),
    ]
    own = place.own
    mine = (own["y"], own["x"], own["c"], place.z)
    copies = [
        pltpu.make_async_copy(src, dst.at[mine], own_sem.at[n])
        for n, (src, dst) in enumerate(((small_src, small_ref), (wc_src, wc_ref)))
    ]
    edge = remote(x_ref.at[:, pl.ds(seg - EDGE, EDGE)], edge_ref, edge_sem.at[0], edge_sem.at[1], place.right)

    def each(group, *steps):
        for name, k in steps:
            for lane in group:
                getattr(lane, name)(k)

    def core(group, stage):
        for k in range(depth):
            for lane in group:
                lane.arrived(k, stage)

    def load(n, at):
        return pltpu.make_async_copy(wc_ref.at[at["y"], at["x"]], buf_ref.at[n % 2], load_sem.at[n % 2])

    rows = wc_src.shape[0]
    count = 2 * depth * rows
    tile = 3 * LANES

    def multiply(n, at):
        group = 2 * at["y"] + at["x"]
        here = pl.ds(pl.multiple_of(group * count, LANES), count)
        gain = sum(
            small_ref[at["y"], at["x"], c, z, : count // LANES] for c in (0, 1) for z in range(depth)
        )
        gain = jnp.concatenate([gain[i : i + 1] for i in range(count // LANES)], axis=1)
        for s in range(seqs):
            normed = (hat_ref[s, :, here] * gain).astype(BF16)
            normed_ref[s, :, here] = normed
            turned = normed[EDGE:].astype(F32).T.astype(BF16)
            for c in (0, 1):
                normt_ref[2 * group + c, :, s * seg : (s + 1) * seg] = turned[c * depth * rows : (c + 1) * depth * rows]
        load(n, at).wait()

        def one(i, carry):
            cols = pl.ds(pl.multiple_of(i * tile, tile), tile)
            block = jnp.concatenate(
                [buf_ref[n % 2, c, z, :, cols] for c in (0, 1) for z in range(depth)], axis=0
            )
            for s in range(seqs):
                part = dot(normed_ref[s, :, here], block)
                if n == 0:
                    pc_ref[s, :, cols] = part
                else:
                    pc_ref[s, :, cols] += part
            return carry

        lax.fori_loop(0, width // tile, one, 0)

    each(lanes, ("line", 0))
    pl.when(place.has_right)(edge.start)
    for copy in copies:
        copy.start()
    pl.when(place.has_left)(edge.wait_recv)

    @pl.when(jnp.logical_not(place.has_left))
    def _():
        edge_ref[...] = jnp.zeros_like(edge_ref)

    for s in range(seqs):
        for start, rows_in in ((0, edge_ref), (EDGE, x_ref)):
            size = rows_in.shape[1]
            step = min(size, 64)
            for r in range(0, size, step):
                values = rows_in[s, r : r + step].astype(F32)
                mean = jnp.mean(values * values, axis=1, keepdims=True)
                hat_ref[s, start + r : start + r + step] = values * lax.rsqrt(mean + EPS)
    for copy in copies:
        copy.wait()
    for k in range(1, depth):
        each(lanes, ("line", k), ("from_first", k - 1))
        if k >= 2:
            each(lanes, ("from_second", k - 2), ("from_both", k - 2))
    last = depth - 1
    each(lanes, ("from_first", last), ("from_second", last - 1), ("from_both", last - 1))
    each(lanes, ("from_second", last))
    groups = [place.flipped(*f) for f in ((), ("y",), ("x",), ("y", "x"))]
    core(lanes, 3)
    load(0, groups[0]).start()
    multiply(0, groups[0])
    core(lanes, 4)
    core(lanes, 5)
    load(1, groups[1]).start()
    load(2, groups[2]).start()
    multiply(1, groups[1])
    each(lanes, ("from_both", last))
    multiply(2, groups[2])
    core(lanes, 6)
    load(3, groups[3]).start()
    multiply(3, groups[3])
    for lane in lanes:
        lane.finish()
    pl.when(place.has_right)(edge.wait_send)


def gather_project(x, small, wc, depth):
    shape = jax.ShapeDtypeStruct
    seqs, seg, features = x.shape
    slots = (2, 2, 2, depth)
    sends, receives = Gather.sems(depth)
    width = wc.shape[1]
    half = width // 2 // LANES * LANES
    anywhere, vmem = pl.BlockSpec(memory_space=pl.ANY), pl.BlockSpec(memory_space=pltpu.VMEM)
    dma = pltpu.SemaphoreType.DMA
    return pl.pallas_call(
        functools.partial(gather_kernel, depth, half),
        in_specs=[vmem, vmem, anywhere],
        out_specs=[vmem, vmem, vmem, vmem, anywhere],
        out_shape=[
            shape((seqs, seg + EDGE, width), F32),
            shape((seqs, seg + EDGE, features), BF16),
            shape((8, depth * wc.shape[0], seqs * seg), BF16),
            shape(slots + small.shape, F32),
            shape(slots + wc.shape, BF16),
        ],
        scratch_shapes=[
            pltpu.VMEM((seqs, seg + EDGE, features), F32),
            pltpu.VMEM((seqs, EDGE, features), BF16),
            pltpu.VMEM((2, 2, depth) + wc.shape, BF16),
            dma((2,)), dma((2,)), dma((2,)), dma((3, sends)), dma((3, receives)),
        ],
        compiler_params=pltpu.CompilerParams(
            collective_id=0, has_side_effects=True, vmem_limit_bytes=VMEM_LIMIT
        ),
        name="gather_project",
    )(x, small, wc)


def pair_copies(place, pairs, send, recv):
    found = []
    other = 1 - place.own["c"]
    for lhs, lhs_pair, rhs, rhs_pair in pairs:
        parts = [(rhs, rhs_pair)]
        if lhs is not None:
            parts = [(lhs.at[2 * g + other], lhs_pair.at[g]) for g in range(4)] + parts
        for src, dst in parts:
            n = len(found)
            found.append(remote(src, dst, send.at[n], recv.at[n], place.to["c"]))
    return found


def run_scatters(scatters, small=None):
    for lane in scatters:
        lane.send_second(0)
    if small:
        small.stage(0)
    for lane in scatters:
        lane.send_second(1)
    if small:
        small.stage(1)
    for lane in scatters:
        lane.send_first()
    if small:
        small.stage(2)
    for lane in scatters:
        lane.hold()
    if small:
        small.stage(3)
    for k in scatters[0].waves():
        if small:
            small.sums.step(k)
        for lane in scatters:
            lane.step(k)


def scatter_two_kernel(depth, a_lhs, a_rhs, b_lhs, b_rhs, a_out, b_out, *refs):
    place = Place(depth)
    place.meet()
    a_lp, a_rp, b_lp, b_rp, pair_send, pair_recv, send, recv = refs[:8]
    copies = pair_copies(place, ((a_lhs, a_lp, a_rhs, a_rp), (b_lhs, b_lp, b_rhs, b_rp)), pair_send, pair_recv)
    for copy in copies:
        copy.start()
    a = Scatter(place, a_lhs, a_lp, a_rhs, a_rp, "y", "x", refs[8:15], send.at[0], recv.at[0])
    b = Scatter(place, b_lhs, b_lp, b_rhs, b_rp, "x", "y", refs[15:22], send.at[1], recv.at[1])
    for copy in copies:
        copy.wait_recv()
    run_scatters((a, b))
    for lane, out in ((a, a_out), (b, b_out)):
        out[...] = lane.keep[place.z]
        lane.finish()
    for copy in copies:
        copy.wait_send()


def scatter_two(a_lhs, a_rhs, b_lhs, b_rhs, depth):
    shape = jax.ShapeDtypeStruct
    vmem, dma = pl.BlockSpec(memory_space=pltpu.VMEM), pltpu.SemaphoreType.DMA
    sends, receives = Scatter.sems(depth)
    a_rows, b_rows = a_lhs.shape[1] // depth, b_lhs.shape[1] // depth
    half = lambda v: pltpu.VMEM((4,) + v.shape[1:], v.dtype)
    like = lambda v: pltpu.VMEM(v.shape, v.dtype)
    return pl.pallas_call(
        functools.partial(scatter_two_kernel, depth),
        in_specs=[vmem] * 4,
        out_specs=[vmem] * 2,
        out_shape=[shape((a_rows, a_rhs.shape[1]), F32), shape((b_rows, b_rhs.shape[1]), F32)],
        scratch_shapes=[
            half(a_lhs), like(a_rhs), half(b_lhs), like(b_rhs), dma((10,)), dma((10,)),
            dma((2, sends)), dma((2, receives)),
            *Scatter.scratch(depth, a_rows, a_rhs.shape[1]),
            *Scatter.scratch(depth, b_rows, b_rhs.shape[1]),
        ],
        compiler_params=pltpu.CompilerParams(
            collective_id=1, has_side_effects=True, vmem_limit_bytes=VMEM_LIMIT
        ),
        name="scatter_two",
    )(a_lhs, a_rhs, b_lhs, b_rhs)


def scatter_last_kernel(depth, half, lhs, rhs, small_src, out, small_out, *refs):
    place = Place(depth)
    place.meet()
    lp, rp_lo, rp_hi, pair_send, pair_recv, send, recv, small_send, small_recv = refs[:9]
    width = rhs.shape[1]
    lo, hi = rhs.at[:, pl.ds(0, half)], rhs.at[:, pl.ds(half, width - half)]
    copies = pair_copies(place, ((lhs, lp, lo, rp_lo), (None, None, hi, rp_hi)), pair_send, pair_recv)
    for copy in copies:
        copy.start()
    a = Scatter(place, lhs, lp, lo, rp_lo, "y", "x", refs[9:16], send.at[0], recv.at[0])
    b = Scatter(place, lhs, lp, hi, rp_hi, "x", "y", refs[16:23], send.at[1], recv.at[1])
    small = SmallScatter(place, small_src, *refs[23:30], small_send, small_recv)
    for copy in copies:
        copy.wait_recv()
    run_scatters((a, b), small)
    out[:, :half] = a.keep[place.z]
    out[:, half:] = b.keep[place.z]
    small_out[...] = small.keep[place.z]
    for lane in (a, b, small):
        lane.finish()
    for copy in copies:
        copy.wait_send()


def scatter_last(lhs, rhs, small, depth):
    shape = jax.ShapeDtypeStruct
    vmem, dma = pl.BlockSpec(memory_space=pltpu.VMEM), pltpu.SemaphoreType.DMA
    sends, receives = Scatter.sems(depth)
    rows, (tokens, width) = lhs.shape[1] // depth, rhs.shape
    half = width // 2 // LANES * LANES
    small_shape = small.shape[4:]
    small_sends, small_receives = SmallScatter.sems(depth)
    return pl.pallas_call(
        functools.partial(scatter_last_kernel, depth, half),
        in_specs=[vmem] * 3,
        out_specs=[vmem] * 2,
        out_shape=[shape((rows, width), F32), shape(small_shape, F32)],
        scratch_shapes=[
            pltpu.VMEM((4,) + lhs.shape[1:], lhs.dtype),
            pltpu.VMEM((tokens, half), rhs.dtype),
            pltpu.VMEM((tokens, width - half), rhs.dtype),
            dma((6,)), dma((6,)), dma((2, sends)), dma((2, receives)),
            dma((small_sends,)), dma((small_receives,)),
            *Scatter.scratch(depth, rows, half),
            *Scatter.scratch(depth, rows, width - half),
            *SmallScatter.scratch(depth, small_shape),
        ],
        compiler_params=pltpu.CompilerParams(
            collective_id=2, has_side_effects=True, vmem_limit_bytes=VMEM_LIMIT
        ),
        name="scatter_last",
    )(lhs, rhs, small)


def fwd_a_kernel(
    head_dim, pc_ref, w_ref, b_ref, raw_ref, sb_ref, dl_ref,
    x_ref, bc_ref, dt_ref, cum_ref, cumt_ref, loc0_ref, seg_ref, tot_ref, bt_ref,
):
    step = pl.program_id(0)
    seqs = pc_ref.shape[0]
    seg = pc_ref.shape[1] - EDGE
    chunks = seg // CHUNK
    w, b = w_ref[...], b_ref[...]

    def acts_of(s):
        pre = causal_conv(pc_ref[s], w, b, seg)
        return pre * sigmoid(pre)

    @pl.when(step == 0)
    def _():
        row = lax.broadcasted_iota(jnp.int32, (CHUNK, CHUNK), 0)
        col = lax.broadcasted_iota(jnp.int32, (CHUNK, CHUNK), 1)
        tri = (col <= row).astype(F32)
        rate = -jnp.exp(dl_ref[...])
        for s in range(seqs):
            acts = acts_of(s)
            bc_ref[s * seg : (s + 1) * seg] = acts
            for c in range(chunks):
                q = s * chunks + c
                rows = slice(q * CHUNK, (q + 1) * CHUNK)
                bt_ref[q] = acts[c * CHUNK : (c + 1) * CHUNK, :LANES].T.astype(BF16)
                dt = softplus(raw_ref[s, EDGE + c * CHUNK : EDGE + (c + 1) * CHUNK] + sb_ref[...])
                cum = LOG2E * jnp.dot(tri, dt * rate, precision=HIGH, preferred_element_type=F32)
                dt_ref[rows] = dt
                cum_ref[rows] = cum
                cumt_ref[:, rows] = cum.T

    @pl.when(step > 0)
    def _():
        heads = GROUP // head_dim
        first = (step - 1) * heads
        cumg = lane_shift(cum_ref[...], first)
        dtg = lane_shift(dt_ref[...], first)
        for s in range(seqs):
            x = acts_of(s)
            x_ref[s * seg : (s + 1) * seg] = x
            state, total = None, None
            for c in range(chunks):
                q = s * chunks + c
                rows = slice(q * CHUNK, (q + 1) * CHUNK)
                ce = spread_all(cumg[rows], heads, head_dim)
                de = spread_all(dtg[rows], heads, head_dim)
                end = ce[CHUNK - 1 : CHUNK]
                uw = x[c * CHUNK : (c + 1) * CHUNK] * de * jnp.exp2(end - ce)
                loc = dot(bt_ref[q], uw.astype(BF16))
                tot = jnp.exp2(end)
                tot_ref[q : q + 1] = tot
                if c == 0:
                    loc0_ref[s] = loc
                    state, total = loc, tot
                else:
                    state, total = tot * state + loc, tot * total
            seg_ref[s] = state.astype(BF16)
            tot_ref[seqs * chunks + s : seqs * chunks + s + 1] = total


def fwd_a(pc, w, b, sb, dl, inner, head_dim):
    seqs, rows, cols = pc.shape
    seg = rows - EDGE
    tokens = seqs * seg
    groups = inner // GROUP
    state = LANES
    chunks = tokens // CHUNK
    at = lambda i: (i + groups) % (groups + 1)
    back = lambda i: jnp.maximum(i - 1, 0)
    return pl.pallas_call(
        functools.partial(fwd_a_kernel, head_dim),
        grid=(groups + 1,),
        in_specs=[
            pl.BlockSpec((seqs, rows, GROUP), lambda i: (0, 0, at(i))),
            pl.BlockSpec((w.shape[0], GROUP), lambda i: (0, at(i))),
            pl.BlockSpec((1, GROUP), lambda i: (0, at(i))),
            pl.BlockSpec((seqs, rows, LANES), lambda i: (0, 0, cols // LANES - 1)),
            whole((1, LANES)),
            whole((1, LANES)),
        ],
        out_specs=[
            pl.BlockSpec((tokens, GROUP), lambda i: (0, back(i))),
            whole((tokens, GROUP)),
            whole((tokens, LANES)),
            whole((tokens, LANES)),
            whole((LANES, tokens)),
            pl.BlockSpec((seqs, state, GROUP), lambda i: (0, 0, back(i))),
            pl.BlockSpec((seqs, state, GROUP), lambda i: (0, 0, back(i))),
            pl.BlockSpec((8, GROUP), lambda i: (0, back(i))),
        ],
        out_shape=[
            jax.ShapeDtypeStruct((tokens, inner), F32),
            jax.ShapeDtypeStruct((tokens, GROUP), F32),
            jax.ShapeDtypeStruct((tokens, LANES), F32),
            jax.ShapeDtypeStruct((tokens, LANES), F32),
            jax.ShapeDtypeStruct((LANES, tokens), F32),
            jax.ShapeDtypeStruct((seqs, state, inner), F32),
            jax.ShapeDtypeStruct((seqs, state, inner), BF16),
            jax.ShapeDtypeStruct((8, inner), F32),
        ],
        scratch_shapes=[pltpu.VMEM((chunks, LANES, CHUNK), BF16)],
        compiler_params=params(),
        name="conv_states",
    )(pc, w, b, pc, sb, dl)


def fwd_b_kernel(
    head_dim, x_ref, bc_ref, dt_ref, cum_ref, cumt_ref, s0_ref, loc0_ref, tot_ref, skip_ref,
    mixed_ref, s1_ref, cb_ref,
):
    step = pl.program_id(0)
    seqs = s0_ref.shape[0]
    chunks = x_ref.shape[0] // CHUNK // seqs
    heads = GROUP // head_dim

    @pl.when(step == 0)
    def _():
        for q in range(seqs * chunks):
            rows = slice(q * CHUNK, (q + 1) * CHUNK)
            cb_ref[q] = nt(bc_ref[rows, LANES:].astype(BF16), bc_ref[rows, :LANES].astype(BF16))

    first = step * heads
    cumg = lane_shift(cum_ref[...], first)
    dtg = lane_shift(dt_ref[...], first)
    cumr = head_rows(cumt_ref, first)
    row = lax.broadcasted_iota(jnp.int32, (CHUNK, CHUNK), 0)
    col = lax.broadcasted_iota(jnp.int32, (CHUNK, CHUNK), 1)
    causal = col <= row
    skip = skip_ref[...]
    for s in range(seqs):
        start = s0_ref[s]
        for c in range(chunks):
            q = s * chunks + c
            rows = slice(q * CHUNK, (q + 1) * CHUNK)
            x = x_ref[rows]
            ce = spread_all(cumg[rows], heads, head_dim)
            de = spread_all(dtg[rows], heads, head_dim)
            ub = (x * de).astype(BF16)
            cb = cb_ref[q]
            parts = []
            for j in range(0, heads, 2):
                mats = []
                for h in (j, j + 1):
                    there = jnp.broadcast_to(cumg[rows, h : h + 1], (CHUNK, CHUNK))
                    here = cumr[h : h + 1, rows]
                    decay = jnp.exp2(jnp.where(causal, there - here, -jnp.inf))
                    mats.append((decay * cb).astype(BF16))
                pair = ub[:, j * head_dim : (j + 2) * head_dim]
                parts.append(dot(jnp.concatenate(mats, axis=1), block_diagonal(pair, head_dim)))
            y = jnp.concatenate(parts, axis=1)
            y = y + jnp.exp2(ce) * dot(bc_ref[rows, LANES:].astype(BF16), start)
            mixed_ref[rows] = y + skip * x
            if c == 0:
                start = (tot_ref[q : q + 1] * start.astype(F32) + loc0_ref[s]).astype(BF16)
                s1_ref[s] = start


def fwd_b(x, bc, dt, cum, cumt, s0, loc0, tot, skip, head_dim):
    tokens, inner = x.shape
    seqs, state, _ = s0.shape
    groups = inner // GROUP
    wide = pl.BlockSpec((tokens, GROUP), lambda i: (0, i))
    states = pl.BlockSpec((seqs, state, GROUP), lambda i: (0, 0, i))
    return pl.pallas_call(
        functools.partial(fwd_b_kernel, head_dim),
        grid=(groups,),
        in_specs=[
            wide, whole(bc.shape), whole(dt.shape), whole(cum.shape), whole(cumt.shape),
            states, states,
            pl.BlockSpec((8, GROUP), lambda i: (0, i)),
            pl.BlockSpec((1, GROUP), lambda i: (0, i)),
        ],
        out_specs=[wide, states],
        out_shape=[
            jax.ShapeDtypeStruct((tokens, inner), F32),
            jax.ShapeDtypeStruct((seqs, state, inner), BF16),
        ],
        scratch_shapes=[pltpu.VMEM((tokens // CHUNK, CHUNK, CHUNK), F32)],
        compiler_params=params(),
        name="scan_outputs",
    )(x, bc, dt, cum, cumt, s0, loc0, tot, skip)


class Chain:
    def __init__(self, place, came, sent, send, recv, backward):
        self.came, self.sent, self.send, self.recv = came, sent, send, recv
        self.gets, self.gives = place.has_left, place.has_right
        self.to = place.left if backward else place.right
        if backward:
            self.gets, self.gives = self.gives, self.gets
        self.behind = place.depth - 1 - place.z if backward else place.z

    def copy(self, g):
        return remote(self.sent.at[g], self.came.at[g], self.send.at[g], self.recv.at[g], self.to)

    def step(self, g, total, own):
        pl.when(self.gets)(lambda: self.copy(g).wait_recv())

        @pl.when(jnp.logical_not(self.gets))
        def _():
            self.came[g] = jnp.zeros(self.came.shape[1:], self.came.dtype)

        self.sent[g] = (total * self.came[g].astype(F32) + own).astype(BF16)
        pl.when(self.gives)(lambda: self.copy(g).start())

    def finish(self):
        groups = self.came.shape[0]

        def one(g, carry):
            self.copy(g).wait_send()
            return carry

        @pl.when(self.gives)
        def _():
            lax.fori_loop(0, groups, one, 0)


def scan_forward_kernel(
    depth, head_dim, groups,
    pc_ref, w_ref, b_ref, raw_ref, sb_ref, dl_ref, skip_ref, wg_src, wo_src,
    bc_ref, dt_ref, cum_ref, cumt_ref, mixed_ref, s0_ref, s1_ref, s2_ref, tot_ref, wg_ref, wo_ref,
    bt_ref, cb_ref, x_ring, loc_ring, seg_ring, tot_ring, came, sent,
    chain_send, chain_recv, own_sem, send, recv,
):
    step = pl.program_id(0)
    lag = depth - 1
    seqs = pc_ref.shape[0]
    seg = pc_ref.shape[1] - EDGE
    chunks = seg // CHUNK
    heads = GROUP // head_dim
    w, b = w_ref[...], b_ref[...]
    place = Place(depth)
    chain = Chain(place, came, sent, chain_send, chain_recv, False)
    lanes = [
        Gather(place, wg_src, lambda z, y, x, c: wg_ref.at[y, x, c, z], "y", "x", send.at[0], recv.at[0]),
        Gather(place, wo_src, lambda z, y, x, c: wo_ref.at[y, x, c, z], "x", "y", send.at[1], recv.at[1]),
    ]
    mine = (place.own["y"], place.own["x"], place.own["c"], place.z)
    copies = [
        pltpu.make_async_copy(wg_src, wg_ref.at[mine], own_sem.at[0]),
        pltpu.make_async_copy(wo_src, wo_ref.at[mine], own_sem.at[1]),
    ]

    def waves(*steps):
        for name, k in steps:
            for lane in lanes:
                getattr(lane, name)(k)

    def acts_of(s):
        pre = causal_conv(pc_ref[s], w, b, seg)
        return pre * sigmoid(pre)

    @pl.when(step == 0)
    def _():
        place.meet()
        waves(("line", 0))
        for copy in copies:
            copy.start()
        row = lax.broadcasted_iota(jnp.int32, (CHUNK, CHUNK), 0)
        col = lax.broadcasted_iota(jnp.int32, (CHUNK, CHUNK), 1)
        tri = (col <= row).astype(F32)
        rate = -jnp.exp(dl_ref[...])
        for s in range(seqs):
            acts = acts_of(s)
            bc_ref[s * seg : (s + 1) * seg] = acts
            for c in range(chunks):
                q = s * chunks + c
                rows = slice(q * CHUNK, (q + 1) * CHUNK)
                b_proj = acts[c * CHUNK : (c + 1) * CHUNK, :LANES]
                c_proj = acts[c * CHUNK : (c + 1) * CHUNK, LANES:]
                bt_ref[q] = b_proj.T.astype(BF16)
                cb_ref[q] = nt(c_proj.astype(BF16), b_proj.astype(BF16))
                dt = softplus(raw_ref[s, EDGE + c * CHUNK : EDGE + (c + 1) * CHUNK] + sb_ref[...])
                cum = LOG2E * jnp.dot(tri, dt * rate, precision=HIGH, preferred_element_type=F32)
                dt_ref[rows] = dt
                cum_ref[rows] = cum
                cumt_ref[:, rows] = cum.T

    @pl.when((step > 0) & (step <= groups))
    def _():
        g = step - 1
        at = lax.rem(g, lag + 1)
        first = g * heads
        cumg = lane_shift(cum_ref[...], first)
        dtg = lane_shift(dt_ref[...], first)
        for s in range(seqs):
            x = acts_of(s)
            x_ring[at, s * seg : (s + 1) * seg] = x
            state, total = None, None
            for c in range(chunks):
                q = s * chunks + c
                rows = slice(q * CHUNK, (q + 1) * CHUNK)
                ce = spread_all(cumg[rows], heads, head_dim)
                de = spread_all(dtg[rows], heads, head_dim)
                end = ce[CHUNK - 1 : CHUNK]
                uw = x[c * CHUNK : (c + 1) * CHUNK] * de * jnp.exp2(end - ce)
                loc = dot(bt_ref[q], uw.astype(BF16))
                tot = jnp.exp2(end)
                tot_ring[at, q : q + 1] = tot
                if c == 0:
                    loc_ring[at, s] = loc
                    state, total = loc, tot
                else:
                    state, total = tot * state + loc, tot * total
            seg_ring[at, s] = state
            tot_ring[at, seqs * chunks + s : seqs * chunks + s + 1] = total

    handed = step - 1 - chain.behind

    @pl.when((handed >= 0) & (handed < groups))
    def _():
        at = lax.rem(handed, lag + 1)
        totals = tot_ring[at, seqs * chunks : seqs * chunks + seqs]
        chain.step(handed, totals[:, None, :], seg_ring[at])

    @pl.when(step > lag)
    def _():
        g = step - 1 - lag
        at = lax.rem(g, lag + 1)
        first = g * heads
        cumg = lane_shift(cum_ref[...], first)
        dtg = lane_shift(dt_ref[...], first)
        cumr = head_rows(cumt_ref, first)
        row = lax.broadcasted_iota(jnp.int32, (CHUNK, CHUNK), 0)
        col = lax.broadcasted_iota(jnp.int32, (CHUNK, CHUNK), 1)
        causal = col <= row
        skip = skip_ref[...]
        s0_ref[...] = came[g]
        s2_ref[...] = sent[g]
        tot_ref[...] = tot_ring[at]
        for s in range(seqs):
            start = came[g, s]
            for c in range(chunks):
                q = s * chunks + c
                rows = slice(q * CHUNK, (q + 1) * CHUNK)
                x = x_ring[at, rows]
                ce = spread_all(cumg[rows], heads, head_dim)
                de = spread_all(dtg[rows], heads, head_dim)
                ub = (x * de).astype(BF16)
                cb = cb_ref[q]
                parts = []
                for j in range(0, heads, 2):
                    mats = []
                    for h in (j, j + 1):
                        there = jnp.broadcast_to(cumg[rows, h : h + 1], (CHUNK, CHUNK))
                        here = cumr[h : h + 1, rows]
                        decay = jnp.exp2(jnp.where(causal, there - here, -jnp.inf))
                        mats.append((decay * cb).astype(BF16))
                    pair = ub[:, j * head_dim : (j + 2) * head_dim]
                    parts.append(dot(jnp.concatenate(mats, axis=1), block_diagonal(pair, head_dim)))
                y = jnp.concatenate(parts, axis=1)
                y = y + jnp.exp2(ce) * dot(bc_ref[rows, LANES:].astype(BF16), start)
                mixed_ref[rows] = y + skip * x
                if c == 0:
                    start = (tot_ring[at, q : q + 1] * start.astype(F32) + loc_ring[at, s]).astype(BF16)
                    s1_ref[s] = start

    last = depth - 1
    order = [("from_first", 0), ("line", 1), ("from_second", 0), ("from_both", 0)]
    for k in range(1, depth):
        order.append(("from_first", k))
        if k < last:
            order.append(("line", k + 1))
        order += [("from_second", k), ("from_both", k)]
    early = (4, 6, 8, 9, 11, 13)
    for at, item in zip(early, order):
        pl.when(step == at)(lambda: waves(item))

    @pl.when(step == groups + lag)
    def _():
        waves(*order[len(early) :])
        for copy in copies:
            copy.wait()
        for stage in range(3, 7):
            for k in range(depth):
                for lane in lanes:
                    lane.arrived(k, stage)
        for lane in lanes:
            lane.finish()
        chain.finish()


def scan_forward(pc, w, b, sb, dl, skip, wg, wo, inner, head_dim, depth):
    seqs, rows, cols = pc.shape
    tokens = seqs * (rows - EDGE)
    groups = inner // GROUP
    lag = depth - 1
    chunks = tokens // CHUNK
    shape, dma = jax.ShapeDtypeStruct, pltpu.SemaphoreType.DMA
    into = lambda i: jnp.where(i == 0, groups, jnp.minimum(i - 1, groups - 1))
    out = lambda i: jnp.maximum(i - 1 - lag, 0)
    states = pl.BlockSpec((seqs, LANES, GROUP), lambda i: (0, 0, out(i)))
    anywhere = pl.BlockSpec(memory_space=pl.ANY)
    sends, receives = Gather.sems(depth)
    slots = (2, 2, 2, depth)
    ring = lambda *dims: pltpu.VMEM((lag + 1,) + dims, F32)
    link = pltpu.VMEM((groups, seqs, LANES, GROUP), BF16)
    return pl.pallas_call(
        functools.partial(scan_forward_kernel, depth, head_dim, groups),
        grid=(groups + 1 + lag,),
        in_specs=[
            pl.BlockSpec((seqs, rows, GROUP), lambda i: (0, 0, into(i))),
            pl.BlockSpec((w.shape[0], GROUP), lambda i: (0, into(i))),
            pl.BlockSpec((1, GROUP), lambda i: (0, into(i))),
            pl.BlockSpec((seqs, rows, LANES), lambda i: (0, 0, cols // LANES - 1)),
            whole((1, LANES)),
            whole((1, LANES)),
            pl.BlockSpec((1, GROUP), lambda i: (0, out(i))),
            anywhere,
            anywhere,
        ],
        out_specs=[
            whole((tokens, GROUP)),
            whole((tokens, LANES)),
            whole((tokens, LANES)),
            whole((LANES, tokens)),
            pl.BlockSpec((tokens, GROUP), lambda i: (0, out(i))),
            states, states, states,
            pl.BlockSpec((8, GROUP), lambda i: (0, out(i))),
            anywhere,
            anywhere,
        ],
        out_shape=[
            shape((tokens, GROUP), F32),
            shape((tokens, LANES), F32),
            shape((tokens, LANES), F32),
            shape((LANES, tokens), F32),
            shape((tokens, inner), F32),
            shape((seqs, LANES, inner), BF16),
            shape((seqs, LANES, inner), BF16),
            shape((seqs, LANES, inner), BF16),
            shape((8, inner), F32),
            shape(slots + wg.shape, BF16),
            shape(slots + wo.shape, BF16),
        ],
        scratch_shapes=[
            pltpu.VMEM((chunks, LANES, CHUNK), BF16),
            pltpu.VMEM((chunks, CHUNK, CHUNK), F32),
            ring(tokens, GROUP), ring(seqs, LANES, GROUP), ring(seqs, LANES, GROUP), ring(8, GROUP),
            link, link,
            dma((groups,)), dma((groups,)), dma((2,)), dma((2, sends)), dma((2, receives)),
        ],
        compiler_params=pltpu.CompilerParams(
            dimension_semantics=("arbitrary",), collective_id=3, has_side_effects=True,
            vmem_limit_bytes=VMEM_LIMIT,
        ),
        name="scan_forward",
    )(pc, w, b, pc, sb, dl, skip, wg, wo)


def mid_kernel(
    normed_ref, wg_ref, mixed_ref, wo_ref, gain_ref, in_ref, cot_ref,
    not_ref, out_ref, dm_ref, dz_ref, gg_ref, z_ref, dno_ref, acc_ref,
):
    step = pl.program_id(0)
    inner = mixed_ref.shape[1]
    tiles, tile = not_ref.shape[0], not_ref.shape[1]
    per_seq = (normed_ref.shape[1] - EDGE) // CHUNK

    @pl.when(step == 0)
    def _():
        gg_ref[...] = jnp.zeros_like(gg_ref)

    def lanes_of(i):
        return pl.ds(pl.multiple_of(i * tile, tile), tile)

    def fold(v):
        total = v[:, :LANES]
        for k in range(LANES, tile, LANES):
            total = total + v[:, k : k + LANES]
        return total

    start = pl.multiple_of(EDGE + lax.rem(step, per_seq) * CHUNK, EDGE)
    normed = normed_ref[lax.div(step, per_seq), pl.ds(start, CHUNK), :]
    cot = cot_ref[...]

    def one(i, sums):
        sq, hg = sums
        at = lanes_of(i)
        z = dot(normed, wg_ref[:, at])
        z_ref[:, at] = z
        g = mixed_ref[:, at] * z * sigmoid(z)
        dno = nt(cot, wo_ref[at, :])
        dno_ref[:, at] = dno
        return sq + fold(g * g), hg + fold(dno * gain_ref[:, at] * g)

    zero = jnp.zeros((normed.shape[0], LANES), F32)
    sq, hg = lax.fori_loop(0, tiles, one, (zero, zero))
    scale = lax.rsqrt(jnp.sum(sq, axis=1, keepdims=True) / inner + EPS)
    pull = scale * scale * scale * (jnp.sum(hg, axis=1, keepdims=True) / inner)
    acc_ref[...] = in_ref[...].astype(F32)

    def two(i, carry):
        at = lanes_of(i)
        z, mixed, dno, gain = z_ref[:, at], mixed_ref[:, at], dno_ref[:, at], gain_ref[:, at]
        sig = sigmoid(z)
        act = z * sig
        g = mixed * act
        gs = g * scale
        no = gs * gain
        not_ref[i] = no.T.astype(BF16)
        acc_ref[...] += dot(no.astype(BF16), wo_ref[at, :])
        gg_ref[:, at] += jnp.sum(dno * gs, axis=0, keepdims=True)
        dg = scale * (dno * gain) - g * pull
        dm_ref[:, at] = dg * act
        dz_ref[:, at] = (dg * mixed * (sig * (1.0 + z * (1.0 - sig)))).astype(BF16)
        return carry

    lax.fori_loop(0, tiles, two, 0)
    out_ref[...] = acc_ref[...].astype(BF16)


def mid(normed, wg, mixed, wo, gain, inputs, cot, tiles):
    tokens, inner = mixed.shape
    width = inputs.shape[1]
    tile = inner // tiles
    narrow = pl.BlockSpec((CHUNK, width), lambda i: (i, 0))
    wide = pl.BlockSpec((CHUNK, inner), lambda i: (i, 0))
    once = lambda v: pl.BlockSpec(v.shape, lambda i: (0,) * v.ndim, pipeline_mode=pl.Buffered(1))
    return pl.pallas_call(
        mid_kernel,
        grid=(tokens // CHUNK,),
        in_specs=[once(normed), once(wg), wide, once(wo), whole((1, inner)), narrow, narrow],
        out_specs=[
            pl.BlockSpec((tiles, tile, CHUNK), lambda i: (0, 0, i)), narrow, wide, wide,
            whole((1, inner)),
        ],
        out_shape=[
            jax.ShapeDtypeStruct((tiles, tile, tokens), BF16),
            jax.ShapeDtypeStruct((tokens, width), BF16),
            jax.ShapeDtypeStruct((tokens, inner), F32),
            jax.ShapeDtypeStruct((tokens, inner), BF16),
            jax.ShapeDtypeStruct((1, inner), F32),
        ],
        scratch_shapes=[
            pltpu.VMEM((CHUNK, inner), F32),
            pltpu.VMEM((CHUNK, inner), F32),
            pltpu.VMEM((CHUNK, width), F32),
        ],
        compiler_params=params(),
        name="gate_norm_project",
    )(normed, wg, mixed, wo, gain, inputs, cot)


def bwd_a_kernel(head_dim, seqs, dm_ref, bc_ref, cum_ref, tot_ref, seg_ref, ct_ref):
    step = pl.program_id(0)
    chunks = dm_ref.shape[0] // CHUNK // seqs
    heads = GROUP // head_dim

    @pl.when(step == 0)
    def _():
        for q in range(seqs * chunks):
            ct_ref[q] = bc_ref[q * CHUNK : (q + 1) * CHUNK, LANES:].T.astype(BF16)

    cumg = lane_shift(cum_ref[...], step * heads)
    for s in range(seqs):
        state = None
        for c in range(chunks - 1, -1, -1):
            q = s * chunks + c
            rows = slice(q * CHUNK, (q + 1) * CHUNK)
            ey = jnp.exp2(spread_all(cumg[rows], heads, head_dim)) * dm_ref[rows]
            loc = dot(ct_ref[q], ey.astype(BF16))
            state = loc if state is None else tot_ref[q : q + 1] * state + loc
        seg_ref[s] = state.astype(BF16)


def bwd_a(dm, bc, cum, tot, seqs, head_dim):
    tokens, inner = dm.shape
    return pl.pallas_call(
        functools.partial(bwd_a_kernel, head_dim, seqs),
        grid=(inner // GROUP,),
        in_specs=[
            pl.BlockSpec((tokens, GROUP), lambda i: (0, i)), whole(bc.shape), whole(cum.shape),
            pl.BlockSpec((8, GROUP), lambda i: (0, i)),
        ],
        out_specs=pl.BlockSpec((seqs, LANES, GROUP), lambda i: (0, 0, i)),
        out_shape=jax.ShapeDtypeStruct((seqs, LANES, inner), BF16),
        scratch_shapes=[pltpu.VMEM((tokens // CHUNK, LANES, CHUNK), BF16)],
        compiler_params=params(),
        name="adjoint_states",
    )(dm, bc, cum, tot)


def bwd_b_kernel(
    head_dim, groups, pc_ref, w_ref, b_ref, raw_ref, sb_ref, dl_ref, bc_ref, dt_ref, cum_ref, cumt_ref,
    dm_ref, mixed_ref, s0_ref, s1_ref, s2_ref, g_ref, tot_ref, skip_ref,
    dc_ref, tail_ref, edge_ref, gw_ref, gb_ref, gskip_ref, draw_ref, hsum_ref,
    cbt_ref, dcbt_ref, db_acc, dc_acc, r1_ref, r2_ref, dtot_ref,
):
    step = pl.program_id(0)
    seqs = pc_ref.shape[0]
    seg = pc_ref.shape[1] - EDGE
    chunks = seg // CHUNK
    heads = GROUP // head_dim
    w, b = w_ref[...], b_ref[...]
    taps = w.shape[0]

    @pl.when(step == 0)
    def _():
        for q in range(seqs * chunks):
            rows = slice(q * CHUNK, (q + 1) * CHUNK)
            cbt_ref[q] = nt(bc_ref[rows, :LANES].astype(BF16), bc_ref[rows, LANES:].astype(BF16))
        dcbt_ref[...] = jnp.zeros_like(dcbt_ref)
        db_acc[...] = jnp.zeros_like(db_acc)
        dc_acc[...] = jnp.zeros_like(dc_acc)
        r1_ref[...] = jnp.zeros_like(r1_ref)
        r2_ref[...] = jnp.zeros_like(r2_ref)
        dtot_ref[...] = jnp.zeros_like(dtot_ref)

    def conv_back(s, ext, pre, sig, d_act):
        d_pre = d_act * (sig * (1.0 + pre * (1.0 - sig)))
        zero = jnp.zeros((EDGE, d_pre.shape[1]), F32)
        padded = jnp.concatenate([zero, d_pre, zero], axis=0)
        total = None
        for k in range(taps):
            at = taps - 1 - k
            term = w[k : k + 1] * padded[at : at + seg + EDGE]
            total = term if total is None else total + term
        edge_ref[s] = total[:EDGE]
        dc_ref[s * seg : (s + 1) * seg] = total[EDGE:].astype(BF16)
        tail_ref[s] = total[seg:]
        for k in range(taps):
            at = EDGE - (taps - 1) + k
            grad = jnp.sum(ext[at : at + seg] * d_pre, axis=0, keepdims=True)
            gw_ref[k : k + 1] = grad if s == 0 else gw_ref[k : k + 1] + grad
        grad = jnp.sum(d_pre, axis=0, keepdims=True)
        gb_ref[...] = grad if s == 0 else gb_ref[...] + grad

    def by_head(value, pick):
        high = value.astype(BF16)
        return dot(high, pick) + dot((value - high.astype(F32)).astype(BF16), pick)

    @pl.when(step < groups)
    def _():
        first = step * heads
        cumg = lane_shift(cum_ref[...], first)
        dtg = lane_shift(dt_ref[...], first)
        cumr = head_rows(cumt_ref, first)
        row = lax.broadcasted_iota(jnp.int32, (CHUNK, CHUNK), 0)
        col = lax.broadcasted_iota(jnp.int32, (CHUNK, CHUNK), 1)
        causal = row <= col
        lane = lax.broadcasted_iota(jnp.int32, (GROUP, LANES), 0)
        head = lax.broadcasted_iota(jnp.int32, (GROUP, LANES), 1)
        pick = (head == first + lane // head_dim).astype(BF16)
        skip = skip_ref[...]
        grad_skip = None
        for s in range(seqs):
            ext = pc_ref[s]
            pre = causal_conv(ext, w, b, seg)
            sig = sigmoid(pre)
            acts = pre * sig
            adj = g_ref[s].astype(F32)
            d_acts = [None] * chunks
            for c in range(chunks - 1, -1, -1):
                q = s * chunks + c
                rows = slice(q * CHUNK, (q + 1) * CHUNK)
                x = acts[c * CHUNK : (c + 1) * CHUNK]
                dy = dm_ref[rows]
                ce = spread_all(cumg[rows], heads, head_dim)
                de = spread_all(dtg[rows], heads, head_dim)
                weight = jnp.exp2(ce[CHUNK - 1 : CHUNK] - ce)
                u = x * de
                ub = u.astype(BF16)
                dyb = dy.astype(BF16)
                cbt = cbt_ref[q]
                parts = []
                dcbt = dcbt_ref[q]
                for j in range(0, heads, 2):
                    lanes = slice(j * head_dim, (j + 2) * head_dim)
                    dy_block = block_diagonal(dyb[:, lanes], head_dim)
                    dm = nt(ub[:, lanes], dy_block)
                    mats = []
                    for k, h in enumerate((j, j + 1)):
                        here = jnp.broadcast_to(cumg[rows, h : h + 1], (CHUNK, CHUNK))
                        there = cumr[h : h + 1, rows]
                        decay = jnp.exp2(jnp.where(causal, there - here, -jnp.inf))
                        mats.append((decay * cbt).astype(BF16))
                        dcbt = dcbt + decay * dm[:, k * CHUNK : (k + 1) * CHUNK]
                    parts.append(dot(jnp.concatenate(mats, axis=1), dy_block))
                dcbt_ref[q] = dcbt
                start = s0_ref[s] if c == 0 else s1_ref[s]
                end = s2_ref[s] if c == chunks - 1 else s1_ref[s]
                adj_b = adj.astype(BF16)
                bb = bc_ref[rows, :LANES].astype(BF16)
                cb = bc_ref[rows, LANES:].astype(BF16)
                ey = (jnp.exp2(ce) * dy).astype(BF16)
                du = jnp.concatenate(parts, axis=1) + weight * dot(bb, adj_b)
                db_acc[rows] += nt((u * weight).astype(BF16), adj_b)
                dc_acc[rows] += nt(ey, start)
                r1_ref[rows] += by_head(dyb.astype(F32) * (mixed_ref[rows] - skip * x), pick)
                r2_ref[rows] += by_head(x * du, pick)
                dtot_ref[q : q + 1] += by_head(
                    jnp.sum(adj * end.astype(F32), axis=0, keepdims=True), pick
                )
                grad = jnp.sum(dy * x, axis=0, keepdims=True)
                grad_skip = grad if grad_skip is None else grad_skip + grad
                d_acts[c] = du * de + skip * dy
                if c > 0:
                    adj = tot_ref[q : q + 1] * adj + dot(cb, ey, ((0,), (0,)))
            conv_back(s, ext, pre, sig, jnp.concatenate(d_acts, axis=0))
        gskip_ref[...] = grad_skip

    @pl.when(step == groups)
    def _():
        row = lax.broadcasted_iota(jnp.int32, (CHUNK, CHUNK), 0)
        col = lax.broadcasted_iota(jnp.int32, (CHUNK, CHUNK), 1)
        later = (row <= col).astype(F32)
        rate = -jnp.exp(dl_ref[...])
        sum_raw = jnp.zeros((1, LANES), F32)
        sum_log = jnp.zeros((1, LANES), F32)
        for s in range(seqs):
            ext = pc_ref[s]
            pre = causal_conv(ext, w, b, seg)
            sig = sigmoid(pre)
            parts = []
            for c in range(chunks):
                q = s * chunks + c
                rows = slice(q * CHUNK, (q + 1) * CHUNK)
                dcbt = dcbt_ref[q]
                bb = bc_ref[rows, :LANES].astype(BF16)
                cb = bc_ref[rows, LANES:].astype(BF16)
                d_b = db_acc[rows] + dot(dcbt.astype(BF16), cb)
                d_c = dc_acc[rows] + dot(dcbt.T.astype(BF16), bb)
                parts.append(jnp.concatenate([d_b, d_c], axis=1))
                dt = dt_ref[rows]
                r2 = r2_ref[rows]
                d_log = jnp.dot(
                    later, r1_ref[rows] - dt * r2, precision=HIGH, preferred_element_type=F32
                )
                d_log = d_log + dtot_ref[q : q + 1]
                raw = raw_ref[s, EDGE + c * CHUNK : EDGE + (c + 1) * CHUNK] + sb_ref[...]
                d_raw = (r2 + rate * d_log) * sigmoid(raw)
                draw_ref[rows] = d_raw
                sum_raw = sum_raw + jnp.sum(d_raw, axis=0, keepdims=True)
                sum_log = sum_log + jnp.sum(d_log * dt, axis=0, keepdims=True) * rate
            conv_back(s, ext, pre, sig, jnp.concatenate(parts, axis=0))
        hsum_ref[0:1] = sum_raw
        hsum_ref[1:2] = sum_log


def bwd_b(pc, w, b, sb, dl, bc, dt, cum, cumt, dm, mixed, s0, s1, s2, g, tot, skip, head_dim):
    seqs, rows, cols = pc.shape
    tokens, inner = dm.shape
    groups = inner // GROUP
    taps, channels = w.shape
    wide = pl.BlockSpec((tokens, GROUP), lambda i: (0, jnp.minimum(i, groups - 1)))
    states = pl.BlockSpec((seqs, LANES, GROUP), lambda i: (0, 0, jnp.minimum(i, groups - 1)))
    line = lambda n: pl.BlockSpec((n, GROUP), lambda i: (0, jnp.minimum(i, groups - 1)))
    conv = lambda n: pl.BlockSpec((n, GROUP), lambda i: (0, i))
    ends = pl.BlockSpec((seqs, EDGE, GROUP), lambda i: (0, 0, i))
    chunks = tokens // CHUNK
    shape = jax.ShapeDtypeStruct
    return pl.pallas_call(
        functools.partial(bwd_b_kernel, head_dim, groups),
        grid=(groups + 1,),
        in_specs=[
            pl.BlockSpec((seqs, rows, GROUP), lambda i: (0, 0, i)),
            conv(taps),
            conv(1),
            pl.BlockSpec((seqs, rows, LANES), lambda i: (0, 0, cols // LANES - 1)),
            whole((1, LANES)), whole((1, LANES)),
            whole(bc.shape), whole(dt.shape), whole(cum.shape), whole(cumt.shape),
            wide, wide, states, states, states, states, line(8), line(1),
        ],
        out_specs=[
            conv(tokens), ends, ends, conv(taps), conv(1), line(1),
            whole((tokens, LANES)), whole((2, LANES)),
        ],
        out_shape=[
            shape((tokens, channels), BF16),
            shape((seqs, EDGE, channels), F32),
            shape((seqs, EDGE, channels), F32),
            shape((taps, channels), F32),
            shape((1, channels), F32),
            shape((1, inner), F32),
            shape((tokens, LANES), F32),
            shape((2, LANES), F32),
        ],
        scratch_shapes=[
            pltpu.VMEM((chunks, CHUNK, CHUNK), F32),
            pltpu.VMEM((chunks, CHUNK, CHUNK), F32),
            pltpu.VMEM((tokens, LANES), F32),
            pltpu.VMEM((tokens, LANES), F32),
            pltpu.VMEM((tokens, LANES), F32),
            pltpu.VMEM((tokens, LANES), F32),
            pltpu.VMEM((8, LANES), F32),
        ],
        compiler_params=params(),
        name="scan_backward",
    )(pc, w, b, pc, sb, dl, bc, dt, cum, cumt, dm, mixed, s0, s1, s2, g, tot, skip)


def passed_along(value, axis, steps):
    count = lax.axis_size(axis)
    initial, last = (max(0, -steps), min(count, count - steps))
    return lax.ppermute(value, axis, [(source, source + steps) for source in range(initial, last)])


def prefix(total, local, axis, backward):
    count, here = lax.axis_size(axis), lax.axis_index(axis)
    totals = lax.all_gather(total.astype(BF16), axis)
    locals_ = lax.all_gather(local, axis)
    state = jnp.zeros(local.shape, F32)
    order = range(count - 1, 0, -1) if backward else range(count - 1)
    for lap in order:
        new = totals[lap].astype(F32) * state + locals_[lap].astype(F32)
        reached = lap > here if backward else lap < here
        state = jnp.where(reached, new, state)
    leaves = total * state + local.astype(F32)
    return state.astype(BF16), leaves.astype(BF16)


AXES = ("dp", "ctx")


def body(
    inputs, gain_in, in_weight, conv_weight, conv_bias, step_bias, decay_log, skip_gain, gain_out,
    out_weight, cotangent,
):
    seqs, seg, width = inputs.shape
    tokens = seqs * seg
    count = lax.axis_size(AXES)
    dp, depth = lax.axis_size("dp"), lax.axis_size("ctx")
    own_links = dp == 8
    inner = out_weight.shape[0] * count
    taps, channels = conv_weight.shape[0], conv_weight.shape[1] * count
    num_heads = step_bias.shape[0]
    head_dim = inner // num_heads
    a, b, c = gain_in.shape[0], gain_out.shape[0], conv_bias.shape[0]

    w_gate = in_weight[:, :inner]
    w_conv = in_weight[:, inner:]
    spare = -w_conv.shape[1] % LANES
    w_conv = jnp.pad(w_conv, ((0, 0), (0, spare)))
    rest = jnp.concatenate([gain_out, conv_bias, conv_weight.reshape(-1)])
    ends = taps - 1
    flat = inputs.reshape(tokens, width)
    cot = cotangent.reshape(tokens, width)

    if own_links:
        group = 2 * depth * a
        at = lax.rem(lax.axis_index("dp"), 2) * depth + lax.axis_index("ctx")
        head = lax.dynamic_update_slice(jnp.zeros((group,), F32), gain_in.astype(F32), (at * a,))
        small = jnp.concatenate([head, rest.astype(F32)])
        small = jnp.pad(small, (0, 8 * LANES - small.size)).reshape(8, LANES)
        pc, normed_ext, normed_t, small, w_conv = gather_project(inputs, small, w_conv, depth)
        w_conv = w_conv.reshape(width, -1)
        small = small.reshape(4, 2 * depth, 8 * LANES)
        g_in = small[:, :, :group].sum(axis=1).reshape(1, width)
        rest = small[:, :, group:].reshape(count, -1)
    else:
        before = passed_along(inputs[:, seg - EDGE :], "ctx", 1)
        ext = jnp.concatenate([before, inputs], axis=1).astype(F32)
        scale_ext = lax.rsqrt(jnp.mean(ext * ext, axis=-1, keepdims=True) + EPS)
        small = lax.all_gather(jnp.concatenate([gain_in, rest]), AXES).astype(F32)
        w_conv = lax.all_gather(w_conv, AXES, axis=0, tiled=True)
        w_gate = lax.all_gather(w_gate, AXES, axis=0, tiled=True)
        w_out = lax.all_gather(out_weight, AXES, axis=0, tiled=True)
        g_in, rest = small[:, :a].reshape(1, width), small[:, a:]
        normed_ext = (ext * scale_ext * g_in).astype(BF16)
        pc = dot(normed_ext.reshape(-1, width), w_conv).reshape(seqs, seg + EDGE, -1)
    g_out = rest[:, :b].reshape(1, inner)
    bias = rest[:, b : b + c].reshape(1, channels)
    kernel = rest[:, b + c : b + c + taps * c].reshape(count, taps, c).transpose(1, 0, 2)
    kernel = kernel.reshape(taps, channels)
    pad_head = lambda v: jnp.pad(v, (0, LANES - num_heads)).reshape(1, LANES)
    sb, dl = pad_head(step_bias), pad_head(decay_log)
    skip = jnp.repeat(skip_gain, head_dim).reshape(1, inner)

    if own_links:
        bc, dt, cum, cumt, mixed, s0, s1, s2, tot, w_gate, w_out = scan_forward(
            pc, kernel, bias, sb, dl, skip, w_gate, out_weight, inner, head_dim, depth
        )
        w_gate = w_gate.reshape(width, inner)
        w_out = w_out.reshape(inner, width)
        per_seq = tot[tokens // CHUNK : tokens // CHUNK + seqs][:, None, :]
    else:
        x, bc, dt, cum, cumt, loc0, local, tot = fwd_a(pc, kernel, bias, sb, dl, inner, head_dim)
        per_seq = tot[tokens // CHUNK : tokens // CHUNK + seqs][:, None, :]
        s0, s2 = prefix(per_seq, local, "ctx", False)
        mixed, s1 = fwd_b(x, bc, dt, cum, cumt, s0, loc0, tot, skip, head_dim)

    turned, output, d_mixed, d_gate, grad_gain_out = mid(
        normed_ext, w_gate, mixed, w_out, g_out, flat, cot, 8
    )
    if own_links:
        grad_gate_weight, grad_out_weight = scatter_two(normed_t, d_gate, turned, cot, depth)
    else:
        scatter = lambda v: lax.psum_scatter(v.astype(BF16), AXES, scatter_dimension=0, tiled=True).astype(F32)
        normed = normed_ext[:, EDGE:].reshape(tokens, width)
        grad_out_weight = scatter(dot(turned.reshape(inner, tokens), cot))
        grad_gate_weight = scatter(dot(normed, d_gate, ((0,), (0,))))

    adjoint = bwd_a(d_mixed, bc, cum, tot, seqs, head_dim)
    g, _ = prefix(per_seq, adjoint, "ctx", True)
    d_conv, tail, edge, grad_kernel, grad_bias, grad_skip, d_raw, head_sums = bwd_b(
        pc, kernel, bias, sb, dl, bc, dt, cum, cumt, d_mixed, mixed, s0, s1, s2, g, tot, skip, head_dim
    )
    after = passed_along(edge[:, EDGE - ends :].astype(BF16), "ctx", -1).astype(F32)
    tail = tail[:, EDGE - ends :] + after
    d_conv = d_conv.reshape(seqs, seg, channels).at[:, seg - ends :].set(tail.astype(BF16))
    d_conv = jnp.concatenate([d_conv.reshape(tokens, channels), d_raw.astype(BF16)], axis=1)

    d_normed = nt(d_gate, w_gate) + nt(d_conv, w_conv)
    values = flat.astype(F32)
    scale = lax.rsqrt(jnp.mean(values * values, axis=-1, keepdims=True) + EPS)
    hat = values * scale
    grad_gain_in = jnp.sum(d_normed * hat, axis=0)
    weighted = d_normed * g_in
    pull = jnp.mean(weighted * hat, axis=-1, keepdims=True)
    grad_input = scale * (weighted - hat * pull) + cot.astype(F32)

    grad_skip = jnp.sum(grad_skip.reshape(num_heads, head_dim), axis=1)
    heads_sum = jnp.concatenate([head_sums[0, :num_heads], head_sums[1, :num_heads], grad_skip])
    by_owner = jnp.concatenate(
        [
            grad_gain_in.reshape(count, a),
            grad_gain_out.reshape(count, b),
            grad_bias.reshape(count, c),
            grad_kernel.reshape(taps, count, c).transpose(1, 0, 2).reshape(count, taps * c),
            jnp.broadcast_to(heads_sum, (count, 3 * num_heads)),
        ],
        axis=1,
    )
    real = d_conv.shape[1] - spare
    if own_links:
        by_owner = jnp.pad(by_owner, ((0, 0), (0, 8 * LANES - by_owner.shape[1])))
        grad_conv_cols, mine = scatter_last(
            normed_t, d_conv, by_owner.reshape(2, 2, 2, depth, 8, LANES), depth
        )
        grad_conv_cols, mine = grad_conv_cols[:, :real], mine.reshape(-1)
    else:
        grad_conv_cols = scatter(dot(normed, d_conv[:, :real], ((0,), (0,))))
        mine = lax.dynamic_index_in_dim(lax.psum(by_owner, AXES), lax.axis_index(AXES), 0, False)
    at = a + b + c + taps * c
    head_totals = mine[at : at + 3 * num_heads].reshape(3, num_heads)
    return (
        output.reshape(seqs, seg, width),
        grad_input.reshape(seqs, seg, width),
        mine[:a],
        jnp.concatenate([grad_gate_weight, grad_conv_cols], axis=1),
        mine[a + b + c : at].reshape(taps, c),
        mine[a + b : a + b + c],
        head_totals[0],
        head_totals[1],
        head_totals[2],
        mine[a : a + b],
        grad_out_weight,
    )


def solution(mesh):
    rows, cols, both = P("dp", "ctx", None), P(AXES, None), P(AXES)
    return jax.shard_map(
        body,
        mesh=mesh,
        in_specs=(rows, both, cols, P(None, AXES), both, P(), P(), P(), both, cols, rows),
        out_specs=(rows, rows, both, cols, P(None, AXES), both, P(), P(), P(), both, cols),
        check_vma=False,
    )
```

```python
import functools

import jax
import jax.numpy as jnp
from jax import lax
from jax.experimental import pallas as pl
from jax.experimental.pallas import tpu as pltpu
from jax.sharding import PartitionSpec as P

EPS = 1e-05
LOG2E = 1.4426950408889634
HIGH = lax.Precision.HIGHEST
F32 = jnp.float32
BF16 = jnp.bfloat16
CHUNK = 128
GROUP = 256
EDGE = 16
LANES = 128
VMEM_LIMIT = 56 * 1024 * 1024


def dot(a, b, dims=((1,), (0,))):
    return lax.dot_general(a, b, (dims, ((), ())), preferred_element_type=F32)


def nt(a, b):
    return dot(a, b, ((1,), (1,)))


def params():
    return pltpu.CompilerParams(
        dimension_semantics=("arbitrary",), vmem_limit_bytes=VMEM_LIMIT
    )


def whole(shape):
    return pl.BlockSpec(shape, lambda i: (0,) * len(shape))


def sigmoid(v):
    return 1.0 / (1.0 + jnp.exp(-v))


def softplus(v):
    return jnp.maximum(v, 0.0) + jnp.log1p(jnp.exp(-jnp.abs(v)))


def causal_conv(ext, w, b, seg):
    taps = w.shape[0]
    total = b
    for k in range(taps):
        at = EDGE - (taps - 1) + k
        total = total + w[k : k + 1] * ext[at : at + seg]
    return total


def lane_shift(value, lanes):
    return pltpu.roll(value, lax.rem(LANES - lanes, LANES), 1)


def head_rows(ref, first):
    base = pl.multiple_of(first // 8 * 8, 8)
    return pltpu.roll(ref[pl.ds(base, 8), :], lax.rem(8 - lax.rem(first, 8), 8), 0)


def spread(cols, at, head_dim):
    rows = cols.shape[0]
    lane = lax.broadcasted_iota(jnp.int32, (rows, LANES), 1)
    first = jnp.broadcast_to(cols[:, at : at + 1], (rows, LANES))
    second = jnp.broadcast_to(cols[:, at + 1 : at + 2], (rows, LANES))
    return jnp.where(lane < head_dim, first, second)


def spread_all(cols, heads, head_dim):
    return jnp.concatenate([spread(cols, j, head_dim) for j in range(0, heads, 2)], axis=1)


def block_diagonal(pair, head_dim):
    lane = lax.broadcasted_iota(jnp.int32, pair.shape, 1)
    zero = jnp.zeros_like(pair)
    return jnp.concatenate(
        [jnp.where(lane < head_dim, pair, zero), jnp.where(lane < head_dim, zero, pair)], axis=0
    )


MESH = pl.DeviceIdType.MESH


class Place:
    def __init__(self, depth):
        dp, z = lax.axis_index("dp"), lax.axis_index("ctx")
        self.depth, self.z = depth, z
        self.own = {"y": lax.div(dp, 4), "x": lax.rem(lax.div(dp, 2), 2), "c": lax.rem(dp, 2)}
        self.to = {
            name: {"dp": dp + step * (1 - 2 * self.own[name])}
            for name, step in (("y", 4), ("x", 2), ("c", 1))
        }
        self.has_left, self.has_right = z > 0, z < depth - 1
        self.left, self.right = {"ctx": z - 1}, {"ctx": z + 1}

    def flipped(self, *names):
        return {n: 1 - v if n in names else v for n, v in self.own.items()}

    def near(self, k):
        z, last = self.z, self.depth - 1
        reach = jnp.minimum(z, last - z)
        pair = jnp.where(k % 2 == 1, z - (k + 1) // 2, z + k // 2)
        alone = jnp.where(z > last - z, last - k, k)
        return z if k == 0 else jnp.where(k <= 2 * reach, pair, alone)

    def meet(self):
        barrier = pltpu.get_barrier_semaphore()
        signal = functools.partial(pl.semaphore_signal, barrier, inc=1, device_id_type=MESH)
        for name in ("y", "x", "c"):
            signal(device_id=self.to[name])
        pl.when(self.has_left)(lambda: signal(device_id=self.left))
        pl.when(self.has_right)(lambda: signal(device_id=self.right))
        ends = self.has_left.astype(jnp.int32) + self.has_right.astype(jnp.int32)
        pl.semaphore_wait(barrier, 3 + ends)


def remote(src, dst, send, recv, to):
    return pltpu.make_async_remote_copy(
        src_ref=src, dst_ref=dst, send_sem=send, recv_sem=recv, device_id=to, device_id_type=MESH
    )


class Gather:
    def __init__(self, place, src, slot, first, second, send, recv):
        self.place, self.src, self.slot_of = place, src, slot
        self.first, self.second, self.send, self.recv = first, second, send, recv

    @staticmethod
    def sems(depth):
        return 9 * depth, 8 * depth

    def slot(self, k, *flips):
        return self.slot_of(self.place.near(k), **self.place.flipped(*flips))

    def copy(self, k, kind, where, to, recv):
        src = self.src if k == 0 and where == () else self.slot(k, *where)
        send = self.send.at[kind * self.place.depth + k]
        return remote(src, self.slot(k, *where), send, self.recv.at[recv], to)

    def along(self, k, right):
        p = self.place
        return self.copy(k, int(right), (), p.right if right else p.left, p.near(k))

    def goes(self, k, right):
        p, at = self.place, self.place.near(k)
        if right:
            return p.has_right if k == 0 else p.has_right & (at < p.z)
        return p.has_left if k == 0 else p.has_left & (at > p.z)

    def to_axis(self, k, stage):
        p, depth = self.place, self.place.depth
        f, s = self.first, self.second
        where = ((), (), (f,), (), (f,), (s,), (f, s))[stage]
        to = p.to[(f, s, s, "c", "c", "c", "c")[stage]]
        return self.copy(k, 2 + stage, where, to, (1 + stage) * depth + k)

    def arrived(self, k, stage):
        p, depth = self.place, self.place.depth
        f, s = self.first, self.second
        where = ((f,), (s,), (s, f), ("c",), ("c", f), ("c", s), ("c", f, s))[stage]
        self.copy(k, 2 + stage, where, p.to["c"], (1 + stage) * depth + k).wait_recv()

    def line(self, k):
        if k:
            self.along(k, True).wait_recv()
        for right in (True, False):
            pl.when(self.goes(k, right))(lambda: self.along(k, right).start())
        for stage in (0, 1, 3):
            self.to_axis(k, stage).start()

    def from_first(self, k):
        self.arrived(k, 0)
        self.to_axis(k, 2).start()
        self.to_axis(k, 4).start()

    def from_second(self, k):
        self.arrived(k, 1)
        self.to_axis(k, 5).start()

    def from_both(self, k):
        self.arrived(k, 2)
        self.to_axis(k, 6).start()

    def finish(self):
        for k in range(self.place.depth):
            for right in (True, False):
                pl.when(self.goes(k, right))(lambda: self.along(k, right).wait_send())
            for stage in range(7):
                self.to_axis(k, stage).wait_send()


class Line:
    def __init__(self, place, keep, sent, came, send, recv):
        self.place, self.keep, self.sent, self.came = place, keep, sent, came
        self.send, self.recv = send, recv

    def copy(self, k, to, at):
        zk = self.place.near(k)
        return remote(self.sent.at[zk], self.came.at[at], self.send.at[k], self.recv.at[at], to)

    def take(self, at):
        self.copy(1, self.place.left, at).wait_recv()
        zk = jnp.where(at == self.place.depth, self.place.z, at)
        self.keep[zk] = self.keep[zk] + self.came[at].astype(F32)

    def moves(self, k):
        p, zk = self.place, self.place.near(k)
        return (
            (zk < p.z, p.left, zk),
            (zk > p.z, p.right, jnp.where(zk == p.z + 1, p.depth, zk)),
        )

    def step(self, k):
        p, zk = self.place, self.place.near(k)
        if k == 0:
            pl.when(p.has_right)(lambda: self.take(p.z))
            pl.when(p.has_left)(lambda: self.take(p.depth))
            return
        farther = ((zk < p.z) & p.has_right) | ((zk > p.z) & p.has_left)
        pl.when(farther)(lambda: self.take(zk))
        self.sent[zk] = self.keep[zk].astype(self.sent.dtype)
        for goes, to, at in self.moves(k):
            pl.when(goes)(lambda: self.copy(k, to, at).start())

    def finish(self):
        for k in range(1, self.place.depth):
            for goes, to, at in self.moves(k):
                pl.when(goes)(lambda: self.copy(k, to, at).wait_send())


class Scatter:
    def __init__(self, place, lhs, lhs_pair, rhs, rhs_pair, first, second, bufs, send, recv):
        self.place, self.lhs, self.lhs_pair, self.rhs, self.rhs_pair = place, lhs, lhs_pair, rhs, rhs_pair
        self.first, self.second, self.send, self.recv = first, second, send, recv
        self.s_sent, self.s_came, self.f_sent, self.f_came, self.keep, z_sent, z_came = bufs
        depth = place.depth
        self.sums = Line(place, self.keep, z_sent, z_came, send.at[pl.ds(3 * depth, depth)],
                         recv.at[pl.ds(3 * depth, depth + 1)])

    @staticmethod
    def sems(depth):
        return 4 * depth, 4 * depth + 1

    @staticmethod
    def scratch(depth, rows, cols):
        block = lambda *lead: pltpu.VMEM(lead + (rows, cols), BF16)
        return [
            block(2, depth), block(2, depth), block(depth), block(depth),
            pltpu.VMEM((depth, rows, cols), F32), block(depth), block(depth + 1),
        ]

    def product(self, flips, store):
        at = self.place.flipped(*flips)
        pair = 2 * at["y"] + at["x"]
        one = 2 * pair + at["c"]
        rows, cols = self.keep.shape[1:]
        tile = 512

        def block(start, size):
            lanes = pl.ds(start, size)
            part = dot(self.lhs[one], self.rhs[:, lanes]) + dot(self.lhs_pair[pair], self.rhs_pair[:, lanes])
            for z in range(self.place.depth):
                store(z, lanes, part[z * rows : (z + 1) * rows])

        def loop(i, carry):
            block(pl.multiple_of(i * tile, tile), tile)
            return carry

        lax.fori_loop(0, cols // tile, loop, 0)
        if cols % tile:
            block(cols // tile * tile, cols % tile)

    def to_second(self, j, k):
        zk, n = self.place.near(k), j * self.place.depth + k
        return remote(self.s_sent.at[j, zk], self.s_came.at[j, zk], self.send.at[n], self.recv.at[n],
                      self.place.to[self.second])

    def to_first(self, k):
        zk, n = self.place.near(k), 2 * self.place.depth + k
        return remote(self.f_sent.at[zk], self.f_came.at[zk], self.send.at[n], self.recv.at[n],
                      self.place.to[self.first])

    def waves(self):
        return range(self.place.depth - 1, -1, -1)

    def send_second(self, j):
        def store(z, lanes, part):
            self.s_sent[j, z, :, lanes] = part.astype(BF16)

        self.product((self.second, self.first) if j == 0 else (self.second,), store)
        for k in self.waves():
            self.to_second(j, k).start()

    def send_first(self):
        for k in self.waves():
            self.to_second(0, k).wait_recv()

        def store(z, lanes, part):
            self.f_sent[z, :, lanes] = (part + self.s_came[0, z, :, lanes].astype(F32)).astype(BF16)

        self.product((self.first,), store)
        for k in self.waves():
            self.to_first(k).start()

    def hold(self):
        for k in self.waves():
            self.to_second(1, k).wait_recv()

        def store(z, lanes, part):
            self.keep[z, :, lanes] = part + self.s_came[1, z, :, lanes].astype(F32)

        self.product((), store)

    def step(self, k):
        self.to_first(k).wait_recv()
        zk = self.place.near(k)
        self.keep[zk] = self.keep[zk] + self.f_came[zk].astype(F32)
        self.sums.step(k)

    def finish(self):
        for k in self.waves():
            self.to_second(0, k).wait_send()
            self.to_second(1, k).wait_send()
            self.to_first(k).wait_send()
        self.sums.finish()


class SmallScatter:
    def __init__(self, place, src, c_came, half, x_came, keep, y_came, z_sent, z_came, send, recv):
        self.place, self.src, self.c_came, self.half = place, src, c_came, half
        self.x_came, self.keep, self.y_came = x_came, keep, y_came
        self.send, self.recv = send, recv
        depth = place.depth
        self.sums = Line(place, keep, z_sent, z_came, send.at[pl.ds(7, depth)],
                         recv.at[pl.ds(7, depth + 1)])

    @staticmethod
    def sems(depth):
        return 7 + depth, 8 + depth

    @staticmethod
    def scratch(depth, shape):
        block = lambda *lead: pltpu.VMEM(lead + shape, F32)
        return [
            block(2, 2, depth), block(2, 2, depth), block(2, depth), block(depth), block(depth),
            block(depth), block(depth + 1),
        ]

    def copy(self, n):
        p, own = self.place, self.place.own
        if n < 4:
            y, x = n // 2, n % 2
            src, dst, to = self.src.at[y, x, 1 - own["c"]], self.c_came.at[y, x], "c"
        elif n < 6:
            src, dst, to = self.half.at[n - 4, 1 - own["x"]], self.x_came.at[n - 4], "x"
        else:
            src, dst, to = self.half.at[1 - own["y"], own["x"]], self.y_came, "y"
        return remote(src, dst, self.send.at[n], self.recv.at[n], p.to[to])

    def stage(self, n):
        own = self.place.own
        if n == 0:
            for i in range(4):
                self.copy(i).start()
        elif n == 1:
            for i in range(4):
                self.copy(i).wait_recv()
            for y in (0, 1):
                for x in (0, 1):
                    self.half[y, x] = self.src[y, x, own["c"]] + self.c_came[y, x]
            for i in (4, 5):
                self.copy(i).start()
        elif n == 2:
            for i in (4, 5):
                self.copy(i).wait_recv()
            for y in (0, 1):
                self.half[y, own["x"]] = self.half[y, own["x"]] + self.x_came[y]
            self.copy(6).start()
        else:
            self.copy(6).wait_recv()
            self.keep[...] = self.half[own["y"], own["x"]] + self.y_came[...]

    def finish(self):
        for n in range(7):
            self.copy(n).wait_send()
        self.sums.finish()


def gather_kernel(
    depth, half, x_ref, small_src, wc_src, pc_ref, normed_ref, normt_ref, small_ref, wc_ref,
    hat_ref, edge_ref, buf_ref, edge_sem, load_sem, own_sem, send, recv,
):
    place = Place(depth)
    place.meet()
    seqs, seg, features = x_ref.shape
    width = wc_src.shape[1]
    lo, hi = pl.ds(0, half), pl.ds(half, width - half)
    lanes = [
        Gather(place, small_src, lambda z, y, x, c: small_ref.at[y, x, c, z], "y", "x",
               send.at[0], recv.at[0]),
        Gather(place, wc_src.at[:, lo], lambda z, y, x, c: wc_ref.at[y, x, c, z, :, lo], "y", "x",
               send.at[1], recv.at[1]),
        Gather(place, wc_src.at[:, hi], lambda z, y, x, c: wc_ref.at[y, x, c, z, :, hi], "x", "y",
               send.at[2], recv.at[2]),
    ]
    own = place.own
    mine = (own["y"], own["x"], own["c"], place.z)
    copies = [
        pltpu.make_async_copy(src, dst.at[mine], own_sem.at[n])
        for n, (src, dst) in enumerate(((small_src, small_ref), (wc_src, wc_ref)))
    ]
    edge = remote(x_ref.at[:, pl.ds(seg - EDGE, EDGE)], edge_ref, edge_sem.at[0], edge_sem.at[1], place.right)

    def each(group, *steps):
        for name, k in steps:
            for lane in group:
                getattr(lane, name)(k)

    def core(group, stage):
        for k in range(depth):
            for lane in group:
                lane.arrived(k, stage)

    def load(n, at):
        return pltpu.make_async_copy(wc_ref.at[at["y"], at["x"]], buf_ref.at[n % 2], load_sem.at[n % 2])

    rows = wc_src.shape[0]
    count = 2 * depth * rows
    tile = 3 * LANES

    def multiply(n, at):
        group = 2 * at["y"] + at["x"]
        here = pl.ds(pl.multiple_of(group * count, LANES), count)
        gain = sum(
            small_ref[at["y"], at["x"], c, z, : count // LANES] for c in (0, 1) for z in range(depth)
        )
        gain = jnp.concatenate([gain[i : i + 1] for i in range(count // LANES)], axis=1)
        for s in range(seqs):
            normed = (hat_ref[s, :, here] * gain).astype(BF16)
            normed_ref[s, :, here] = normed
            turned = normed[EDGE:].astype(F32).T.astype(BF16)
            for c in (0, 1):
                normt_ref[2 * group + c, :, s * seg : (s + 1) * seg] = turned[c * depth * rows : (c + 1) * depth * rows]
        load(n, at).wait()

        def one(i, carry):
            cols = pl.ds(pl.multiple_of(i * tile, tile), tile)
            block = jnp.concatenate(
                [buf_ref[n % 2, c, z, :, cols] for c in (0, 1) for z in range(depth)], axis=0
            )
            for s in range(seqs):
                part = dot(normed_ref[s, :, here], block)
                if n == 0:
                    pc_ref[s, :, cols] = part
                else:
                    pc_ref[s, :, cols] += part
            return carry

        lax.fori_loop(0, width // tile, one, 0)

    each(lanes, ("line", 0))
    pl.when(place.has_right)(edge.start)
    for copy in copies:
        copy.start()
    pl.when(place.has_left)(edge.wait_recv)

    @pl.when(jnp.logical_not(place.has_left))
    def _():
        edge_ref[...] = jnp.zeros_like(edge_ref)

    for s in range(seqs):
        for start, rows_in in ((0, edge_ref), (EDGE, x_ref)):
            size = rows_in.shape[1]
            step = min(size, 64)
            for r in range(0, size, step):
                values = rows_in[s, r : r + step].astype(F32)
                mean = jnp.mean(values * values, axis=1, keepdims=True)
                hat_ref[s, start + r : start + r + step] = values * lax.rsqrt(mean + EPS)
    for copy in copies:
        copy.wait()
    for k in range(1, depth):
        each(lanes, ("line", k), ("from_first", k - 1))
        if k >= 2:
            each(lanes, ("from_second", k - 2), ("from_both", k - 2))
    last = depth - 1
    each(lanes, ("from_first", last), ("from_second", last - 1), ("from_both", last - 1))
    each(lanes, ("from_second", last))
    groups = [place.flipped(*f) for f in ((), ("y",), ("x",), ("y", "x"))]
    core(lanes, 3)
    load(0, groups[0]).start()
    multiply(0, groups[0])
    core(lanes, 4)
    core(lanes, 5)
    load(1, groups[1]).start()
    load(2, groups[2]).start()
    multiply(1, groups[1])
    each(lanes, ("from_both", last))
    multiply(2, groups[2])
    core(lanes, 6)
    load(3, groups[3]).start()
    multiply(3, groups[3])
    for lane in lanes:
        lane.finish()
    pl.when(place.has_right)(edge.wait_send)


def gather_project(x, small, wc, depth):
    shape = jax.ShapeDtypeStruct
    seqs, seg, features = x.shape
    slots = (2, 2, 2, depth)
    sends, receives = Gather.sems(depth)
    width = wc.shape[1]
    half = width // 2 // LANES * LANES
    anywhere, vmem = pl.BlockSpec(memory_space=pl.ANY), pl.BlockSpec(memory_space=pltpu.VMEM)
    dma = pltpu.SemaphoreType.DMA
    return pl.pallas_call(
        functools.partial(gather_kernel, depth, half),
        in_specs=[vmem, vmem, anywhere],
        out_specs=[vmem, vmem, vmem, vmem, anywhere],
        out_shape=[
            shape((seqs, seg + EDGE, width), F32),
            shape((seqs, seg + EDGE, features), BF16),
            shape((8, depth * wc.shape[0], seqs * seg), BF16),
            shape(slots + small.shape, F32),
            shape(slots + wc.shape, BF16),
        ],
        scratch_shapes=[
            pltpu.VMEM((seqs, seg + EDGE, features), F32),
            pltpu.VMEM((seqs, EDGE, features), BF16),
            pltpu.VMEM((2, 2, depth) + wc.shape, BF16),
            dma((2,)), dma((2,)), dma((2,)), dma((3, sends)), dma((3, receives)),
        ],
        compiler_params=pltpu.CompilerParams(
            collective_id=0, has_side_effects=True, vmem_limit_bytes=VMEM_LIMIT
        ),
        name="gather_project",
    )(x, small, wc)


def fwd_a_kernel(
    head_dim, pc_ref, w_ref, b_ref, raw_ref, sb_ref, dl_ref,
    x_ref, bc_ref, dt_ref, cum_ref, cumt_ref, loc0_ref, seg_ref, tot_ref, bt_ref,
):
    step = pl.program_id(0)
    seqs = pc_ref.shape[0]
    seg = pc_ref.shape[1] - EDGE
    chunks = seg // CHUNK
    w, b = w_ref[...], b_ref[...]

    def acts_of(s):
        pre = causal_conv(pc_ref[s], w, b, seg)
        return pre * sigmoid(pre)

    @pl.when(step == 0)
    def _():
        row = lax.broadcasted_iota(jnp.int32, (CHUNK, CHUNK), 0)
        col = lax.broadcasted_iota(jnp.int32, (CHUNK, CHUNK), 1)
        tri = (col <= row).astype(F32)
        rate = -jnp.exp(dl_ref[...])
        for s in range(seqs):
            acts = acts_of(s)
            bc_ref[s * seg : (s + 1) * seg] = acts
            for c in range(chunks):
                q = s * chunks + c
                rows = slice(q * CHUNK, (q + 1) * CHUNK)
                bt_ref[q] = acts[c * CHUNK : (c + 1) * CHUNK, :LANES].T.astype(BF16)
                dt = softplus(raw_ref[s, EDGE + c * CHUNK : EDGE + (c + 1) * CHUNK] + sb_ref[...])
                cum = LOG2E * jnp.dot(tri, dt * rate, precision=HIGH, preferred_element_type=F32)
                dt_ref[rows] = dt
                cum_ref[rows] = cum
                cumt_ref[:, rows] = cum.T

    @pl.when(step > 0)
    def _():
        heads = GROUP // head_dim
        first = (step - 1) * heads
        cumg = lane_shift(cum_ref[...], first)
        dtg = lane_shift(dt_ref[...], first)
        for s in range(seqs):
            x = acts_of(s)
            x_ref[s * seg : (s + 1) * seg] = x
            state, total = None, None
            for c in range(chunks):
                q = s * chunks + c
                rows = slice(q * CHUNK, (q + 1) * CHUNK)
                ce = spread_all(cumg[rows], heads, head_dim)
                de = spread_all(dtg[rows], heads, head_dim)
                end = ce[CHUNK - 1 : CHUNK]
                uw = x[c * CHUNK : (c + 1) * CHUNK] * de * jnp.exp2(end - ce)
                loc = dot(bt_ref[q], uw.astype(BF16))
                tot = jnp.exp2(end)
                tot_ref[q : q + 1] = tot
                if c == 0:
                    loc0_ref[s] = loc
                    state, total = loc, tot
                else:
                    state, total = tot * state + loc, tot * total
            seg_ref[s] = state.astype(BF16)
            tot_ref[seqs * chunks + s : seqs * chunks + s + 1] = total


def fwd_a(pc, w, b, sb, dl, inner, head_dim):
    seqs, rows, cols = pc.shape
    seg = rows - EDGE
    tokens = seqs * seg
    groups = inner // GROUP
    state = LANES
    chunks = tokens // CHUNK
    at = lambda i: (i + groups) % (groups + 1)
    back = lambda i: jnp.maximum(i - 1, 0)
    return pl.pallas_call(
        functools.partial(fwd_a_kernel, head_dim),
        grid=(groups + 1,),
        in_specs=[
            pl.BlockSpec((seqs, rows, GROUP), lambda i: (0, 0, at(i))),
            pl.BlockSpec((w.shape[0], GROUP), lambda i: (0, at(i))),
            pl.BlockSpec((1, GROUP), lambda i: (0, at(i))),
            pl.BlockSpec((seqs, rows, LANES), lambda i: (0, 0, cols // LANES - 1)),
            whole((1, LANES)),
            whole((1, LANES)),
        ],
        out_specs=[
            pl.BlockSpec((tokens, GROUP), lambda i: (0, back(i))),
            whole((tokens, GROUP)),
            whole((tokens, LANES)),
            whole((tokens, LANES)),
            whole((LANES, tokens)),
            pl.BlockSpec((seqs, state, GROUP), lambda i: (0, 0, back(i))),
            pl.BlockSpec((seqs, state, GROUP), lambda i: (0, 0, back(i))),
            pl.BlockSpec((8, GROUP), lambda i: (0, back(i))),
        ],
        out_shape=[
            jax.ShapeDtypeStruct((tokens, inner), F32),
            jax.ShapeDtypeStruct((tokens, GROUP), F32),
            jax.ShapeDtypeStruct((tokens, LANES), F32),
            jax.ShapeDtypeStruct((tokens, LANES), F32),
            jax.ShapeDtypeStruct((LANES, tokens), F32),
            jax.ShapeDtypeStruct((seqs, state, inner), F32),
            jax.ShapeDtypeStruct((seqs, state, inner), BF16),
            jax.ShapeDtypeStruct((8, inner), F32),
        ],
        scratch_shapes=[pltpu.VMEM((chunks, LANES, CHUNK), BF16)],
        compiler_params=params(),
        name="conv_states",
    )(pc, w, b, pc, sb, dl)


def fwd_b_kernel(
    head_dim, x_ref, bc_ref, dt_ref, cum_ref, cumt_ref, s0_ref, loc0_ref, tot_ref, skip_ref,
    mixed_ref, s1_ref, cb_ref,
):
    step = pl.program_id(0)
    seqs = s0_ref.shape[0]
    chunks = x_ref.shape[0] // CHUNK // seqs
    heads = GROUP // head_dim

    @pl.when(step == 0)
    def _():
        for q in range(seqs * chunks):
            rows = slice(q * CHUNK, (q + 1) * CHUNK)
            cb_ref[q] = nt(bc_ref[rows, LANES:].astype(BF16), bc_ref[rows, :LANES].astype(BF16))

    first = step * heads
    cumg = lane_shift(cum_ref[...], first)
    dtg = lane_shift(dt_ref[...], first)
    cumr = head_rows(cumt_ref, first)
    row = lax.broadcasted_iota(jnp.int32, (CHUNK, CHUNK), 0)
    col = lax.broadcasted_iota(jnp.int32, (CHUNK, CHUNK), 1)
    causal = col <= row
    skip = skip_ref[...]
    for s in range(seqs):
        start = s0_ref[s]
        for c in range(chunks):
            q = s * chunks + c
            rows = slice(q * CHUNK, (q + 1) * CHUNK)
            x = x_ref[rows]
            ce = spread_all(cumg[rows], heads, head_dim)
            de = spread_all(dtg[rows], heads, head_dim)
            ub = (x * de).astype(BF16)
            cb = cb_ref[q]
            parts = []
            for j in range(0, heads, 2):
                mats = []
                for h in (j, j + 1):
                    there = jnp.broadcast_to(cumg[rows, h : h + 1], (CHUNK, CHUNK))
                    here = cumr[h : h + 1, rows]
                    decay = jnp.exp2(jnp.where(causal, there - here, -jnp.inf))
                    mats.append((decay * cb).astype(BF16))
                pair = ub[:, j * head_dim : (j + 2) * head_dim]
                parts.append(dot(jnp.concatenate(mats, axis=1), block_diagonal(pair, head_dim)))
            y = jnp.concatenate(parts, axis=1)
            y = y + jnp.exp2(ce) * dot(bc_ref[rows, LANES:].astype(BF16), start)
            mixed_ref[rows] = y + skip * x
            if c == 0:
                start = (tot_ref[q : q + 1] * start.astype(F32) + loc0_ref[s]).astype(BF16)
                s1_ref[s] = start


def fwd_b(x, bc, dt, cum, cumt, s0, loc0, tot, skip, head_dim):
    tokens, inner = x.shape
    seqs, state, _ = s0.shape
    groups = inner // GROUP
    wide = pl.BlockSpec((tokens, GROUP), lambda i: (0, i))
    states = pl.BlockSpec((seqs, state, GROUP), lambda i: (0, 0, i))
    return pl.pallas_call(
        functools.partial(fwd_b_kernel, head_dim),
        grid=(groups,),
        in_specs=[
            wide, whole(bc.shape), whole(dt.shape), whole(cum.shape), whole(cumt.shape),
            states, states,
            pl.BlockSpec((8, GROUP), lambda i: (0, i)),
            pl.BlockSpec((1, GROUP), lambda i: (0, i)),
        ],
        out_specs=[wide, states],
        out_shape=[
            jax.ShapeDtypeStruct((tokens, inner), F32),
            jax.ShapeDtypeStruct((seqs, state, inner), BF16),
        ],
        scratch_shapes=[pltpu.VMEM((tokens // CHUNK, CHUNK, CHUNK), F32)],
        compiler_params=params(),
        name="scan_outputs",
    )(x, bc, dt, cum, cumt, s0, loc0, tot, skip)


def halves(v):
    high = v.astype(BF16)
    return high, (v - high.astype(F32)).astype(BF16)


def dot_pairs(a, b, dims=((1,), (0,))):
    (ah, al), (bh, bl) = halves(a), halves(b)
    return dot(ah, bh, dims) + (dot(al, bh, dims) + dot(ah, bl, dims))


def dot_pair(a, b, dims=((1,), (0,))):
    high, low = halves(a)
    return dot(high, b, dims) + dot(low, b, dims)


def nt_exact(a, b):
    return lax.dot_general(a, b, (((1,), (1,)), ((), ())), precision=HIGH, preferred_element_type=F32)


class Chain:
    def __init__(self, place, came, sent, send, recv, backward):
        self.came, self.sent, self.send, self.recv = came, sent, send, recv
        self.gets, self.gives = place.has_left, place.has_right
        self.to = place.left if backward else place.right
        if backward:
            self.gets, self.gives = self.gives, self.gets
        self.behind = place.depth - 1 - place.z if backward else place.z

    def copy(self, g):
        return remote(self.sent.at[g], self.came.at[g], self.send.at[g], self.recv.at[g], self.to)

    def step(self, g, total, own):
        pl.when(self.gets)(lambda: self.copy(g).wait_recv())

        @pl.when(jnp.logical_not(self.gets))
        def _():
            self.came[g] = jnp.zeros(self.came.shape[1:], self.came.dtype)

        self.sent[g] = (total * self.came[g].astype(F32) + own).astype(BF16)
        pl.when(self.gives)(lambda: self.copy(g).start())

    def finish(self):
        groups = self.came.shape[0]

        def one(g, carry):
            self.copy(g).wait_send()
            return carry

        @pl.when(self.gives)
        def _():
            lax.fori_loop(0, groups, one, 0)


def scan_forward_kernel(
    depth, head_dim, groups,
    pc_ref, w_ref, b_ref, raw_ref, sb_ref, dl_ref, skip_ref, wg_src, wo_src,
    bc_ref, dt_ref, cum_ref, cumt_ref, mixed_ref, s0_ref, s1_ref, s2_ref, tot_ref, wg_ref, wo_ref,
    bt_ref, cb_ref, x_ring, loc_ring, seg_ring, tot_ring, came, sent,
    chain_send, chain_recv, own_sem, send, recv,
):
    step = pl.program_id(0)
    lag = depth - 1
    seqs = pc_ref.shape[0]
    seg = pc_ref.shape[1] - EDGE
    chunks = seg // CHUNK
    heads = GROUP // head_dim
    w, b = w_ref[...], b_ref[...]
    place = Place(depth)
    chain = Chain(place, came, sent, chain_send, chain_recv, False)
    lanes = [
        Gather(place, wg_src, lambda z, y, x, c: wg_ref.at[y, x, c, z], "y", "x", send.at[0], recv.at[0]),
        Gather(place, wo_src, lambda z, y, x, c: wo_ref.at[y, x, c, z], "x", "y", send.at[1], recv.at[1]),
    ]
    mine = (place.own["y"], place.own["x"], place.own["c"], place.z)
    copies = [
        pltpu.make_async_copy(wg_src, wg_ref.at[mine], own_sem.at[0]),
        pltpu.make_async_copy(wo_src, wo_ref.at[mine], own_sem.at[1]),
    ]

    def waves(*steps):
        for name, k in steps:
            for lane in lanes:
                getattr(lane, name)(k)

    def acts_of(s):
        pre = causal_conv(pc_ref[s], w, b, seg)
        return pre * sigmoid(pre)

    @pl.when(step == 0)
    def _():
        place.meet()
        waves(("line", 0))
        for copy in copies:
            copy.start()
        row = lax.broadcasted_iota(jnp.int32, (CHUNK, CHUNK), 0)
        col = lax.broadcasted_iota(jnp.int32, (CHUNK, CHUNK), 1)
        tri = (col <= row).astype(F32)
        rate = -jnp.exp(dl_ref[...])
        for s in range(seqs):
            acts = acts_of(s)
            bc_ref[s * seg : (s + 1) * seg] = acts
            for c in range(chunks):
                q = s * chunks + c
                rows = slice(q * CHUNK, (q + 1) * CHUNK)
                b_proj = acts[c * CHUNK : (c + 1) * CHUNK, :LANES]
                c_proj = acts[c * CHUNK : (c + 1) * CHUNK, LANES:]
                bt_ref[q] = b_proj.T
                cb_ref[q] = nt_exact(c_proj, b_proj)
                dt = softplus(raw_ref[s, EDGE + c * CHUNK : EDGE + (c + 1) * CHUNK] + sb_ref[...])
                cum = LOG2E * jnp.dot(tri, dt * rate, precision=HIGH, preferred_element_type=F32)
                dt_ref[rows] = dt
                cum_ref[rows] = cum
                cumt_ref[:, rows] = cum.T

    @pl.when((step > 0) & (step <= groups))
    def _():
        g = step - 1
        at = lax.rem(g, lag + 1)
        first = g * heads
        cumg = lane_shift(cum_ref[...], first)
        dtg = lane_shift(dt_ref[...], first)
        for s in range(seqs):
            x = acts_of(s)
            x_ring[at, s * seg : (s + 1) * seg] = x
            state, total = None, None
            for c in range(chunks):
                q = s * chunks + c
                rows = slice(q * CHUNK, (q + 1) * CHUNK)
                ce = spread_all(cumg[rows], heads, head_dim)
                de = spread_all(dtg[rows], heads, head_dim)
                end = ce[CHUNK - 1 : CHUNK]
                uw = x[c * CHUNK : (c + 1) * CHUNK] * de * jnp.exp2(end - ce)
                loc = dot_pairs(bt_ref[q], uw)
                tot = jnp.exp2(end)
                tot_ring[at, q : q + 1] = tot
                if c == 0:
                    loc_ring[at, s] = loc
                    state, total = loc, tot
                else:
                    state, total = tot * state + loc, tot * total
            seg_ring[at, s] = state
            tot_ring[at, seqs * chunks + s : seqs * chunks + s + 1] = total

    handed = step - 1 - chain.behind

    @pl.when((handed >= 0) & (handed < groups))
    def _():
        at = lax.rem(handed, lag + 1)
        totals = tot_ring[at, seqs * chunks : seqs * chunks + seqs]
        chain.step(handed, totals[:, None, :], seg_ring[at])

    @pl.when(step > lag)
    def _():
        g = step - 1 - lag
        at = lax.rem(g, lag + 1)
        first = g * heads
        cumg = lane_shift(cum_ref[...], first)
        dtg = lane_shift(dt_ref[...], first)
        cumr = head_rows(cumt_ref, first)
        row = lax.broadcasted_iota(jnp.int32, (CHUNK, CHUNK), 0)
        col = lax.broadcasted_iota(jnp.int32, (CHUNK, CHUNK), 1)
        causal = col <= row
        skip = skip_ref[...]
        s0_ref[...] = came[g]
        s2_ref[...] = sent[g]
        tot_ref[...] = tot_ring[at]
        for s in range(seqs):
            start = came[g, s]
            for c in range(chunks):
                q = s * chunks + c
                rows = slice(q * CHUNK, (q + 1) * CHUNK)
                x = x_ring[at, rows]
                ce = spread_all(cumg[rows], heads, head_dim)
                de = spread_all(dtg[rows], heads, head_dim)
                ub = (x * de).astype(BF16)
                cb = cb_ref[q]
                parts = []
                for j in range(0, heads, 2):
                    mats = []
                    for h in (j, j + 1):
                        there = jnp.broadcast_to(cumg[rows, h : h + 1], (CHUNK, CHUNK))
                        here = cumr[h : h + 1, rows]
                        decay = jnp.exp2(jnp.where(causal, there - here, -jnp.inf))
                        mats.append((decay * cb).astype(BF16))
                    pair = ub[:, j * head_dim : (j + 2) * head_dim]
                    parts.append(dot(jnp.concatenate(mats, axis=1), block_diagonal(pair, head_dim)))
                y = jnp.concatenate(parts, axis=1)
                y = y + jnp.exp2(ce) * dot(bc_ref[rows, LANES:].astype(BF16), start)
                mixed_ref[rows] = y + skip * x
                if c == 0:
                    later = tot_ring[at, q : q + 1] * start.astype(F32) + loc_ring[at, s]
                    s1_ref[s] = later
                    start = later.astype(BF16)

    last = depth - 1
    order = [("from_first", 0), ("line", 1), ("from_second", 0), ("from_both", 0)]
    for k in range(1, depth):
        order.append(("from_first", k))
        if k < last:
            order.append(("line", k + 1))
        order += [("from_second", k), ("from_both", k)]
    early = (4, 6, 8, 9, 11, 13)
    for at, item in zip(early, order):
        pl.when(step == at)(lambda: waves(item))

    @pl.when(step == groups + lag)
    def _():
        waves(*order[len(early) :])
        for copy in copies:
            copy.wait()
        for stage in range(3, 7):
            for k in range(depth):
                for lane in lanes:
                    lane.arrived(k, stage)
        for lane in lanes:
            lane.finish()
        chain.finish()


def scan_forward(pc, w, b, sb, dl, skip, wg, wo, inner, head_dim, depth):
    seqs, rows, cols = pc.shape
    tokens = seqs * (rows - EDGE)
    groups = inner // GROUP
    lag = depth - 1
    chunks = tokens // CHUNK
    shape, dma = jax.ShapeDtypeStruct, pltpu.SemaphoreType.DMA
    into = lambda i: jnp.where(i == 0, groups, jnp.minimum(i - 1, groups - 1))
    out = lambda i: jnp.maximum(i - 1 - lag, 0)
    states = pl.BlockSpec((seqs, LANES, GROUP), lambda i: (0, 0, out(i)))
    anywhere = pl.BlockSpec(memory_space=pl.ANY)
    sends, receives = Gather.sems(depth)
    slots = (2, 2, 2, depth)
    ring = lambda *dims: pltpu.VMEM((lag + 1,) + dims, F32)
    link = pltpu.VMEM((groups, seqs, LANES, GROUP), BF16)
    return pl.pallas_call(
        functools.partial(scan_forward_kernel, depth, head_dim, groups),
        grid=(groups + 1 + lag,),
        in_specs=[
            pl.BlockSpec((seqs, rows, GROUP), lambda i: (0, 0, into(i))),
            pl.BlockSpec((w.shape[0], GROUP), lambda i: (0, into(i))),
            pl.BlockSpec((1, GROUP), lambda i: (0, into(i))),
            pl.BlockSpec((seqs, rows, LANES), lambda i: (0, 0, cols // LANES - 1)),
            whole((1, LANES)),
            whole((1, LANES)),
            pl.BlockSpec((1, GROUP), lambda i: (0, out(i))),
            anywhere,
            anywhere,
        ],
        out_specs=[
            whole((tokens, GROUP)),
            whole((tokens, LANES)),
            whole((tokens, LANES)),
            whole((LANES, tokens)),
            pl.BlockSpec((tokens, GROUP), lambda i: (0, out(i))),
            states, states, states,
            pl.BlockSpec((8, GROUP), lambda i: (0, out(i))),
            anywhere,
            anywhere,
        ],
        out_shape=[
            shape((tokens, GROUP), F32),
            shape((tokens, LANES), F32),
            shape((tokens, LANES), F32),
            shape((LANES, tokens), F32),
            shape((tokens, inner), F32),
            shape((seqs, LANES, inner), BF16),
            shape((seqs, LANES, inner), F32),
            shape((seqs, LANES, inner), BF16),
            shape((8, inner), F32),
            shape(slots + wg.shape, BF16),
            shape(slots + wo.shape, BF16),
        ],
        scratch_shapes=[
            pltpu.VMEM((chunks, LANES, CHUNK), F32),
            pltpu.VMEM((chunks, CHUNK, CHUNK), F32),
            ring(tokens, GROUP), ring(seqs, LANES, GROUP), ring(seqs, LANES, GROUP), ring(8, GROUP),
            link, link,
            dma((groups,)), dma((groups,)), dma((2,)), dma((2, sends)), dma((2, receives)),
        ],
        compiler_params=pltpu.CompilerParams(
            dimension_semantics=("arbitrary",), collective_id=3, has_side_effects=True,
            vmem_limit_bytes=VMEM_LIMIT,
        ),
        name="scan_forward",
    )(pc, w, b, pc, sb, dl, skip, wg, wo)


def mid_kernel(
    normed_ref, wg_ref, mixed_ref, wo_ref, gain_ref, in_ref, cot_ref,
    not_ref, out_ref, dm_ref, dz_ref, gg_ref, z_ref, dno_ref, acc_ref,
):
    step = pl.program_id(0)
    inner = mixed_ref.shape[1]
    tiles, tile = not_ref.shape[0], not_ref.shape[1]
    per_seq = (normed_ref.shape[1] - EDGE) // CHUNK

    @pl.when(step == 0)
    def _():
        gg_ref[...] = jnp.zeros_like(gg_ref)

    def lanes_of(i):
        return pl.ds(pl.multiple_of(i * tile, tile), tile)

    def fold(v):
        total = v[:, :LANES]
        for k in range(LANES, tile, LANES):
            total = total + v[:, k : k + LANES]
        return total

    start = pl.multiple_of(EDGE + lax.rem(step, per_seq) * CHUNK, EDGE)
    normed = normed_ref[lax.div(step, per_seq), pl.ds(start, CHUNK), :]
    cot = cot_ref[...]

    def one(i, sums):
        sq, hg = sums
        at = lanes_of(i)
        z = dot(normed, wg_ref[:, at])
        z_ref[:, at] = z
        g = mixed_ref[:, at] * z * sigmoid(z)
        dno = nt(cot, wo_ref[at, :])
        dno_ref[:, at] = dno
        return sq + fold(g * g), hg + fold(dno * gain_ref[:, at] * g)

    zero = jnp.zeros((normed.shape[0], LANES), F32)
    sq, hg = lax.fori_loop(0, tiles, one, (zero, zero))
    scale = lax.rsqrt(jnp.sum(sq, axis=1, keepdims=True) / inner + EPS)
    pull = scale * scale * scale * (jnp.sum(hg, axis=1, keepdims=True) / inner)
    acc_ref[...] = in_ref[...].astype(F32)

    def two(i, carry):
        at = lanes_of(i)
        z, mixed, dno, gain = z_ref[:, at], mixed_ref[:, at], dno_ref[:, at], gain_ref[:, at]
        sig = sigmoid(z)
        act = z * sig
        g = mixed * act
        gs = g * scale
        no = gs * gain
        not_ref[i] = no.T.astype(BF16)
        acc_ref[...] += dot(no.astype(BF16), wo_ref[at, :])
        gg_ref[:, at] += jnp.sum(dno * gs, axis=0, keepdims=True)
        dg = scale * (dno * gain) - g * pull
        dm_ref[:, at] = dg * act
        dz_ref[:, at] = (dg * mixed * (sig * (1.0 + z * (1.0 - sig)))).astype(BF16)
        return carry

    lax.fori_loop(0, tiles, two, 0)
    out_ref[...] = acc_ref[...].astype(BF16)


def mid(normed, wg, mixed, wo, gain, inputs, cot, tiles):
    tokens, inner = mixed.shape
    width = inputs.shape[1]
    tile = inner // tiles
    narrow = pl.BlockSpec((CHUNK, width), lambda i: (i, 0))
    wide = pl.BlockSpec((CHUNK, inner), lambda i: (i, 0))
    once = lambda v: pl.BlockSpec(v.shape, lambda i: (0,) * v.ndim, pipeline_mode=pl.Buffered(1))
    return pl.pallas_call(
        mid_kernel,
        grid=(tokens // CHUNK,),
        in_specs=[once(normed), once(wg), wide, once(wo), whole((1, inner)), narrow, narrow],
        out_specs=[
            pl.BlockSpec((tiles, tile, CHUNK), lambda i: (0, 0, i)), narrow, wide, wide,
            whole((1, inner)),
        ],
        out_shape=[
            jax.ShapeDtypeStruct((tiles, tile, tokens), BF16),
            jax.ShapeDtypeStruct((tokens, width), BF16),
            jax.ShapeDtypeStruct((tokens, inner), F32),
            jax.ShapeDtypeStruct((tokens, inner), BF16),
            jax.ShapeDtypeStruct((1, inner), F32),
        ],
        scratch_shapes=[
            pltpu.VMEM((CHUNK, inner), F32),
            pltpu.VMEM((CHUNK, inner), F32),
            pltpu.VMEM((CHUNK, width), F32),
        ],
        compiler_params=params(),
        name="gate_norm_project",
    )(normed, wg, mixed, wo, gain, inputs, cot)


def bwd_a_kernel(head_dim, seqs, dm_ref, bc_ref, cum_ref, tot_ref, seg_ref, ct_ref):
    step = pl.program_id(0)
    chunks = dm_ref.shape[0] // CHUNK // seqs
    heads = GROUP // head_dim

    @pl.when(step == 0)
    def _():
        for q in range(seqs * chunks):
            ct_ref[q] = bc_ref[q * CHUNK : (q + 1) * CHUNK, LANES:].T.astype(BF16)

    cumg = lane_shift(cum_ref[...], step * heads)
    for s in range(seqs):
        state = None
        for c in range(chunks - 1, -1, -1):
            q = s * chunks + c
            rows = slice(q * CHUNK, (q + 1) * CHUNK)
            ey = jnp.exp2(spread_all(cumg[rows], heads, head_dim)) * dm_ref[rows]
            loc = dot(ct_ref[q], ey.astype(BF16))
            state = loc if state is None else tot_ref[q : q + 1] * state + loc
        seg_ref[s] = state.astype(BF16)


def bwd_a(dm, bc, cum, tot, seqs, head_dim):
    tokens, inner = dm.shape
    return pl.pallas_call(
        functools.partial(bwd_a_kernel, head_dim, seqs),
        grid=(inner // GROUP,),
        in_specs=[
            pl.BlockSpec((tokens, GROUP), lambda i: (0, i)), whole(bc.shape), whole(cum.shape),
            pl.BlockSpec((8, GROUP), lambda i: (0, i)),
        ],
        out_specs=pl.BlockSpec((seqs, LANES, GROUP), lambda i: (0, 0, i)),
        out_shape=jax.ShapeDtypeStruct((seqs, LANES, inner), BF16),
        scratch_shapes=[pltpu.VMEM((tokens // CHUNK, LANES, CHUNK), BF16)],
        compiler_params=params(),
        name="adjoint_states",
    )(dm, bc, cum, tot)


def bwd_b_kernel(
    head_dim, groups, pc_ref, w_ref, b_ref, raw_ref, sb_ref, dl_ref, bc_ref, dt_ref, cum_ref, cumt_ref,
    dm_ref, mixed_ref, s0_ref, s1_ref, s2_ref, g_ref, tot_ref, skip_ref,
    dc_ref, tail_ref, edge_ref, gw_ref, gb_ref, gskip_ref, draw_ref, hsum_ref,
    cbt_ref, dcbt_ref, db_acc, dc_acc, r1_ref, r2_ref, dtot_ref,
):
    step = pl.program_id(0)
    seqs = pc_ref.shape[0]
    seg = pc_ref.shape[1] - EDGE
    chunks = seg // CHUNK
    heads = GROUP // head_dim
    w, b = w_ref[...], b_ref[...]
    taps = w.shape[0]

    @pl.when(step == 0)
    def _():
        for q in range(seqs * chunks):
            rows = slice(q * CHUNK, (q + 1) * CHUNK)
            cbt_ref[q] = nt(bc_ref[rows, :LANES].astype(BF16), bc_ref[rows, LANES:].astype(BF16))
        dcbt_ref[...] = jnp.zeros_like(dcbt_ref)
        db_acc[...] = jnp.zeros_like(db_acc)
        dc_acc[...] = jnp.zeros_like(dc_acc)
        r1_ref[...] = jnp.zeros_like(r1_ref)
        r2_ref[...] = jnp.zeros_like(r2_ref)
        dtot_ref[...] = jnp.zeros_like(dtot_ref)

    def conv_back(s, ext, pre, sig, d_act):
        d_pre = d_act * (sig * (1.0 + pre * (1.0 - sig)))
        zero = jnp.zeros((EDGE, d_pre.shape[1]), F32)
        padded = jnp.concatenate([zero, d_pre, zero], axis=0)
        total = None
        for k in range(taps):
            at = taps - 1 - k
            term = w[k : k + 1] * padded[at : at + seg + EDGE]
            total = term if total is None else total + term
        edge_ref[s] = total[:EDGE]
        dc_ref[s * seg : (s + 1) * seg] = total[EDGE:].astype(BF16)
        tail_ref[s] = total[seg:]
        for k in range(taps):
            at = EDGE - (taps - 1) + k
            grad = jnp.sum(ext[at : at + seg] * d_pre, axis=0, keepdims=True)
            gw_ref[k : k + 1] = grad if s == 0 else gw_ref[k : k + 1] + grad
        grad = jnp.sum(d_pre, axis=0, keepdims=True)
        gb_ref[...] = grad if s == 0 else gb_ref[...] + grad

    def by_head(value, pick):
        high = value.astype(BF16)
        return dot(high, pick) + dot((value - high.astype(F32)).astype(BF16), pick)

    @pl.when(step < groups)
    def _():
        first = step * heads
        cumg = lane_shift(cum_ref[...], first)
        dtg = lane_shift(dt_ref[...], first)
        cumr = head_rows(cumt_ref, first)
        row = lax.broadcasted_iota(jnp.int32, (CHUNK, CHUNK), 0)
        col = lax.broadcasted_iota(jnp.int32, (CHUNK, CHUNK), 1)
        causal = row <= col
        lane = lax.broadcasted_iota(jnp.int32, (GROUP, LANES), 0)
        head = lax.broadcasted_iota(jnp.int32, (GROUP, LANES), 1)
        pick = (head == first + lane // head_dim).astype(BF16)
        skip = skip_ref[...]
        grad_skip = None
        for s in range(seqs):
            ext = pc_ref[s]
            pre = causal_conv(ext, w, b, seg)
            sig = sigmoid(pre)
            acts = pre * sig
            adj = g_ref[s].astype(F32)
            d_acts = [None] * chunks
            for c in range(chunks - 1, -1, -1):
                q = s * chunks + c
                rows = slice(q * CHUNK, (q + 1) * CHUNK)
                x = acts[c * CHUNK : (c + 1) * CHUNK]
                dy = dm_ref[rows]
                ce = spread_all(cumg[rows], heads, head_dim)
                de = spread_all(dtg[rows], heads, head_dim)
                weight = jnp.exp2(ce[CHUNK - 1 : CHUNK] - ce)
                u = x * de
                ub = u.astype(BF16)
                dyb = dy.astype(BF16)
                cbt = cbt_ref[q]
                parts = []
                dcbt = dcbt_ref[q]
                for j in range(0, heads, 2):
                    lanes = slice(j * head_dim, (j + 2) * head_dim)
                    dy_block = block_diagonal(dyb[:, lanes], head_dim)
                    dm = nt(ub[:, lanes], dy_block)
                    mats = []
                    for k, h in enumerate((j, j + 1)):
                        here = jnp.broadcast_to(cumg[rows, h : h + 1], (CHUNK, CHUNK))
                        there = cumr[h : h + 1, rows]
                        decay = jnp.exp2(jnp.where(causal, there - here, -jnp.inf))
                        mats.append((decay * cbt).astype(BF16))
                        dcbt = dcbt + decay * dm[:, k * CHUNK : (k + 1) * CHUNK]
                    parts.append(dot(jnp.concatenate(mats, axis=1), dy_block))
                dcbt_ref[q] = dcbt
                start = s0_ref[s] if c == 0 else s1_ref[s]
                end = s2_ref[s] if c == chunks - 1 else s1_ref[s]
                adj_b = adj.astype(BF16)
                bb = bc_ref[rows, :LANES].astype(BF16)
                cb = bc_ref[rows, LANES:].astype(BF16)
                ey = (jnp.exp2(ce) * dy).astype(BF16)
                du = jnp.concatenate(parts, axis=1) + weight * dot(bb, adj_b)
                db_acc[rows] += nt((u * weight).astype(BF16), adj_b)
                dc_acc[rows] += nt(ey, start)
                r1_ref[rows] += by_head(dyb.astype(F32) * (mixed_ref[rows] - skip * x), pick)
                r2_ref[rows] += by_head(x * du, pick)
                dtot_ref[q : q + 1] += by_head(
                    jnp.sum(adj * end.astype(F32), axis=0, keepdims=True), pick
                )
                grad = jnp.sum(dy * x, axis=0, keepdims=True)
                grad_skip = grad if grad_skip is None else grad_skip + grad
                d_acts[c] = du * de + skip * dy
                if c > 0:
                    adj = tot_ref[q : q + 1] * adj + dot(cb, ey, ((0,), (0,)))
            conv_back(s, ext, pre, sig, jnp.concatenate(d_acts, axis=0))
        gskip_ref[...] = grad_skip

    @pl.when(step == groups)
    def _():
        row = lax.broadcasted_iota(jnp.int32, (CHUNK, CHUNK), 0)
        col = lax.broadcasted_iota(jnp.int32, (CHUNK, CHUNK), 1)
        later = (row <= col).astype(F32)
        rate = -jnp.exp(dl_ref[...])
        sum_raw = jnp.zeros((1, LANES), F32)
        sum_log = jnp.zeros((1, LANES), F32)
        for s in range(seqs):
            ext = pc_ref[s]
            pre = causal_conv(ext, w, b, seg)
            sig = sigmoid(pre)
            parts = []
            for c in range(chunks):
                q = s * chunks + c
                rows = slice(q * CHUNK, (q + 1) * CHUNK)
                dcbt = dcbt_ref[q]
                bb = bc_ref[rows, :LANES].astype(BF16)
                cb = bc_ref[rows, LANES:].astype(BF16)
                d_b = db_acc[rows] + dot(dcbt.astype(BF16), cb)
                d_c = dc_acc[rows] + dot(dcbt.T.astype(BF16), bb)
                parts.append(jnp.concatenate([d_b, d_c], axis=1))
                dt = dt_ref[rows]
                r2 = r2_ref[rows]
                d_log = jnp.dot(
                    later, r1_ref[rows] - dt * r2, precision=HIGH, preferred_element_type=F32
                )
                d_log = d_log + dtot_ref[q : q + 1]
                raw = raw_ref[s, EDGE + c * CHUNK : EDGE + (c + 1) * CHUNK] + sb_ref[...]
                d_raw = (r2 + rate * d_log) * sigmoid(raw)
                draw_ref[rows] = d_raw
                sum_raw = sum_raw + jnp.sum(d_raw, axis=0, keepdims=True)
                sum_log = sum_log + jnp.sum(d_log * dt, axis=0, keepdims=True) * rate
            conv_back(s, ext, pre, sig, jnp.concatenate(parts, axis=0))
        hsum_ref[0:1] = sum_raw
        hsum_ref[1:2] = sum_log


def bwd_b(pc, w, b, sb, dl, bc, dt, cum, cumt, dm, mixed, s0, s1, s2, g, tot, skip, head_dim):
    seqs, rows, cols = pc.shape
    tokens, inner = dm.shape
    groups = inner // GROUP
    taps, channels = w.shape
    wide = pl.BlockSpec((tokens, GROUP), lambda i: (0, jnp.minimum(i, groups - 1)))
    states = pl.BlockSpec((seqs, LANES, GROUP), lambda i: (0, 0, jnp.minimum(i, groups - 1)))
    line = lambda n: pl.BlockSpec((n, GROUP), lambda i: (0, jnp.minimum(i, groups - 1)))
    conv = lambda n: pl.BlockSpec((n, GROUP), lambda i: (0, i))
    ends = pl.BlockSpec((seqs, EDGE, GROUP), lambda i: (0, 0, i))
    chunks = tokens // CHUNK
    shape = jax.ShapeDtypeStruct
    return pl.pallas_call(
        functools.partial(bwd_b_kernel, head_dim, groups),
        grid=(groups + 1,),
        in_specs=[
            pl.BlockSpec((seqs, rows, GROUP), lambda i: (0, 0, i)),
            conv(taps),
            conv(1),
            pl.BlockSpec((seqs, rows, LANES), lambda i: (0, 0, cols // LANES - 1)),
            whole((1, LANES)), whole((1, LANES)),
            whole(bc.shape), whole(dt.shape), whole(cum.shape), whole(cumt.shape),
            wide, wide, states, states, states, states, line(8), line(1),
        ],
        out_specs=[
            conv(tokens), ends, ends, conv(taps), conv(1), line(1),
            whole((tokens, LANES)), whole((2, LANES)),
        ],
        out_shape=[
            shape((tokens, channels), BF16),
            shape((seqs, EDGE, channels), F32),
            shape((seqs, EDGE, channels), F32),
            shape((taps, channels), F32),
            shape((1, channels), F32),
            shape((1, inner), F32),
            shape((tokens, LANES), F32),
            shape((2, LANES), F32),
        ],
        scratch_shapes=[
            pltpu.VMEM((chunks, CHUNK, CHUNK), F32),
            pltpu.VMEM((chunks, CHUNK, CHUNK), F32),
            pltpu.VMEM((tokens, LANES), F32),
            pltpu.VMEM((tokens, LANES), F32),
            pltpu.VMEM((tokens, LANES), F32),
            pltpu.VMEM((tokens, LANES), F32),
            pltpu.VMEM((8, LANES), F32),
        ],
        compiler_params=params(),
        name="scan_backward",
    )(pc, w, b, pc, sb, dl, bc, dt, cum, cumt, dm, mixed, s0, s1, s2, g, tot, skip)


def pair_copies(place, lhs, rhs, send, recv):
    other = 1 - place.own["c"]
    parts = [(src.at[2 * g + other], dst.at[g]) for src, dst in lhs for g in range(4)] + list(rhs)
    return [
        remote(src, dst, send.at[n], recv.at[n], place.to["c"]) for n, (src, dst) in enumerate(parts)
    ]


def scan_backward_kernel(
    depth, head_dim, groups,
    pc_ref, w_ref, b_ref, raw_ref, sb_ref, dl_ref, bc_ref, dt_ref, cum_ref, cumt_ref,
    dma_ref, dm_ref, mixed_ref, s0_ref, s1_ref, s2_ref, tot_ref, skip_ref,
    nt_src, dz_src, no_src, cot_src,
    dc_out, gw_ref, gb_ref, gskip_ref, hsum_ref, a_out, b_out, nt_out, dz_out, no_out, cot_out,
    cbt_ref, ct_ref, dcbt_ref, db_acc, dc_acc, r1_ref, r2_ref, dtot_ref,
    dc_ref, tail_ref, edge_ref, edge_came, seg_ring, tot_ring, came, sent,
    nt_pair, dz_pair, no_pair, cot_pair,
    chain_send, chain_recv, edge_send, edge_recv, pair_send, pair_recv, out_sem, send, recv, *bufs,
):
    step = pl.program_id(0)
    lag = depth - 1
    seqs = pc_ref.shape[0]
    seg = pc_ref.shape[1] - EDGE
    chunks = seg // CHUNK
    heads = GROUP // head_dim
    w, b = w_ref[...], b_ref[...]
    taps = w.shape[0]
    channels = tail_ref.shape[2]
    place = Place(depth)
    chain = Chain(place, came, sent, chain_send, chain_recv, True)
    pairs = pair_copies(
        place, ((nt_src, nt_pair), (no_src, no_pair)), ((dz_src, dz_pair), (cot_src, cot_pair)),
        pair_send, pair_recv,
    )
    half = lambda ref: ref.at[:, pl.ds(0, ref.shape[1] // 2)]
    lanes = [
        Scatter(place, nt_src, nt_pair, half(dz_src), half(dz_pair), "y", "x", bufs[:7], send.at[0], recv.at[0]),
        Scatter(place, no_src, no_pair, half(cot_src), half(cot_pair), "x", "y", bufs[7:], send.at[1], recv.at[1]),
    ]
    edges = [
        remote(edge_ref.at[:, :, cols], edge_came.at[:, :, cols], edge_send.at[n], edge_recv.at[n], place.left)
        for n, cols in enumerate((pl.ds(0, channels - GROUP), pl.ds(channels - GROUP, GROUP)))
    ]
    outs = [
        pltpu.make_async_copy(src, dst, out_sem.at[n])
        for n, (src, dst) in enumerate(
            ((nt_pair, nt_out), (no_pair, no_out), (dz_pair, dz_out), (cot_pair, cot_out), (dc_ref, dc_out))
        )
    ]

    def at_step(n, *names):
        def run():
            for name, *rest in names:
                for lane in lanes:
                    getattr(lane, name)(*rest)

        pl.when(step == n)(run)

    @pl.when(step == 0)
    def _():
        place.meet()
        for copy in pairs:
            copy.start()
        for q in range(seqs * chunks):
            rows = slice(q * CHUNK, (q + 1) * CHUNK)
            b_proj, c_proj = bc_ref[rows, :LANES], bc_ref[rows, LANES:]
            cbt_ref[q] = nt_exact(b_proj, c_proj)
            ct_ref[q] = c_proj.T
        dcbt_ref[...] = jnp.zeros_like(dcbt_ref)
        db_acc[...] = jnp.zeros_like(db_acc)
        dc_acc[...] = jnp.zeros_like(dc_acc)
        r1_ref[...] = jnp.zeros_like(r1_ref)
        r2_ref[...] = jnp.zeros_like(r2_ref)
        dtot_ref[...] = jnp.zeros_like(dtot_ref)

    @pl.when(step < groups)
    def _():
        at = lax.rem(step, lag + 1)
        cumg = lane_shift(cum_ref[...], step * heads)
        tot_ring[at] = tot_ref[...]
        for s in range(seqs):
            state = None
            for c in range(chunks - 1, -1, -1):
                q = s * chunks + c
                rows = slice(q * CHUNK, (q + 1) * CHUNK)
                ey = jnp.exp2(spread_all(cumg[rows], heads, head_dim)) * dma_ref[rows]
                loc = dot_pairs(ct_ref[q], ey)
                state = loc if state is None else tot_ref[q : q + 1] * state + loc
            seg_ring[at, s] = state

    handed = step - chain.behind

    @pl.when((handed >= 0) & (handed < groups))
    def _():
        at = lax.rem(handed, lag + 1)
        totals = tot_ring[at, seqs * chunks : seqs * chunks + seqs]
        chain.step(handed, totals[:, None, :], seg_ring[at])

    @pl.when(step == lag)
    def _():
        for copy in pairs:
            copy.wait_recv()
        for copy in outs[:4]:
            copy.start()

    at_step(lag, ("send_second", 0))
    at_step(lag + 1, ("send_second", 1))

    def conv_back(s, ext, pre, sig, d_act, at):
        lanes_at = pl.ds(pl.multiple_of(at * GROUP, GROUP), GROUP)
        d_pre = d_act * (sig * (1.0 + pre * (1.0 - sig)))
        zero = jnp.zeros((EDGE, d_pre.shape[1]), F32)
        padded = jnp.concatenate([zero, d_pre, zero], axis=0)
        total = None
        for k in range(taps):
            start = taps - 1 - k
            term = w[k : k + 1] * padded[start : start + seg + EDGE]
            total = term if total is None else total + term
        edge_ref[s, :, lanes_at] = total[:EDGE].astype(BF16)
        dc_ref[s * seg : (s + 1) * seg, lanes_at] = total[EDGE:].astype(BF16)
        tail_ref[s, :, lanes_at] = total[seg:]
        for k in range(taps):
            start = EDGE - (taps - 1) + k
            grad = jnp.sum(ext[start : start + seg] * d_pre, axis=0, keepdims=True)
            gw_ref[k : k + 1] = grad if s == 0 else gw_ref[k : k + 1] + grad
        grad = jnp.sum(d_pre, axis=0, keepdims=True)
        gb_ref[...] = grad if s == 0 else gb_ref[...] + grad

    def by_head(value, pick):
        high = value.astype(BF16)
        return dot(high, pick) + dot((value - high.astype(F32)).astype(BF16), pick)

    @pl.when((step >= lag) & (step < lag + groups))
    def _():
        g = step - lag
        at = lax.rem(g, lag + 1)
        first = g * heads
        cumg = lane_shift(cum_ref[...], first)
        dtg = lane_shift(dt_ref[...], first)
        cumr = head_rows(cumt_ref, first)
        row = lax.broadcasted_iota(jnp.int32, (CHUNK, CHUNK), 0)
        col = lax.broadcasted_iota(jnp.int32, (CHUNK, CHUNK), 1)
        causal = row <= col
        lane = lax.broadcasted_iota(jnp.int32, (GROUP, LANES), 0)
        head = lax.broadcasted_iota(jnp.int32, (GROUP, LANES), 1)
        pick = (head == first + lane // head_dim).astype(BF16)
        skip = skip_ref[...]
        grad_skip = None
        for s in range(seqs):
            ext = pc_ref[s]
            pre = causal_conv(ext, w, b, seg)
            sig = sigmoid(pre)
            acts = pre * sig
            adj = came[g, s].astype(F32)
            d_acts = [None] * chunks
            for c in range(chunks - 1, -1, -1):
                q = s * chunks + c
                rows = slice(q * CHUNK, (q + 1) * CHUNK)
                x = acts[c * CHUNK : (c + 1) * CHUNK]
                dy = dm_ref[rows]
                ce = spread_all(cumg[rows], heads, head_dim)
                de = spread_all(dtg[rows], heads, head_dim)
                weight = jnp.exp2(ce[CHUNK - 1 : CHUNK] - ce)
                u = x * de
                ub = u.astype(BF16)
                dyb = dy.astype(BF16)
                cbt = cbt_ref[q]
                parts = []
                dcbt = dcbt_ref[q]
                for j in range(0, heads, 2):
                    two = slice(j * head_dim, (j + 2) * head_dim)
                    dy_block = block_diagonal(dyb[:, two], head_dim)
                    dm = nt(ub[:, two], dy_block)
                    mats = []
                    for k, h in enumerate((j, j + 1)):
                        here = jnp.broadcast_to(cumg[rows, h : h + 1], (CHUNK, CHUNK))
                        there = cumr[h : h + 1, rows]
                        decay = jnp.exp2(jnp.where(causal, there - here, -jnp.inf))
                        mats.append((decay * cbt).astype(BF16))
                        dcbt = dcbt + decay * dm[:, k * CHUNK : (k + 1) * CHUNK]
                    parts.append(dot(jnp.concatenate(mats, axis=1), dy_block))
                dcbt_ref[q] = dcbt
                start = s0_ref[s] if c == 0 else s1_ref[s]
                end = s2_ref[s] if c == chunks - 1 else s1_ref[s]
                adj_b = adj.astype(BF16)
                bb = bc_ref[rows, :LANES].astype(BF16)
                ey = jnp.exp2(ce) * dy
                du = jnp.concatenate(parts, axis=1) + weight * dot(bb, adj_b)
                uw = u * weight
                across = ((1,), (1,))
                db_acc[rows] += dot_pair(uw, adj_b, across) if c == chunks - 1 else dot_pairs(uw, adj, across)
                dc_acc[rows] += dot_pair(ey, start, across) if c == 0 else dot_pairs(ey, start, across)
                r1_ref[rows] += by_head(dyb.astype(F32) * (mixed_ref[rows] - skip * x), pick)
                r2_ref[rows] += by_head(x * du, pick)
                dtot_ref[q : q + 1] += by_head(
                    jnp.sum(adj * end.astype(F32), axis=0, keepdims=True), pick
                )
                grad = jnp.sum(dy * x, axis=0, keepdims=True)
                grad_skip = grad if grad_skip is None else grad_skip + grad
                d_acts[c] = du * de + skip * dy
                if c > 0:
                    adj = tot_ring[at, q : q + 1] * adj + dot_pairs(ct_ref[q], ey)
            conv_back(s, ext, pre, sig, jnp.concatenate(d_acts, axis=0), g)
        gskip_ref[...] = grad_skip

    at_step(lag + 5, ("send_first",))
    at_step(lag + 9, ("hold",))

    @pl.when(step == lag + groups)
    def _():
        pl.when(place.has_left)(edges[0].start)
        row = lax.broadcasted_iota(jnp.int32, (CHUNK, CHUNK), 0)
        col = lax.broadcasted_iota(jnp.int32, (CHUNK, CHUNK), 1)
        later = (row <= col).astype(F32)
        rate = -jnp.exp(dl_ref[...])
        sum_raw = jnp.zeros((1, LANES), F32)
        sum_log = jnp.zeros((1, LANES), F32)
        for s in range(seqs):
            ext = pc_ref[s]
            pre = causal_conv(ext, w, b, seg)
            sig = sigmoid(pre)
            parts = []
            for c in range(chunks):
                q = s * chunks + c
                rows = slice(q * CHUNK, (q + 1) * CHUNK)
                dcbt = dcbt_ref[q]
                d_b = db_acc[rows] + dot_pairs(dcbt, bc_ref[rows, LANES:])
                d_c = dc_acc[rows] + dot_pairs(dcbt.T, bc_ref[rows, :LANES])
                parts.append(jnp.concatenate([d_b, d_c], axis=1))
                dt = dt_ref[rows]
                r2 = r2_ref[rows]
                d_log = jnp.dot(
                    later, r1_ref[rows] - dt * r2, precision=HIGH, preferred_element_type=F32
                )
                d_log = d_log + dtot_ref[q : q + 1]
                raw = raw_ref[s, EDGE + c * CHUNK : EDGE + (c + 1) * CHUNK] + sb_ref[...]
                d_raw = (r2 + rate * d_log) * sigmoid(raw)
                dc_ref[rows, channels:] = d_raw.astype(BF16)
                sum_raw = sum_raw + jnp.sum(d_raw, axis=0, keepdims=True)
                sum_log = sum_log + jnp.sum(d_log * dt, axis=0, keepdims=True) * rate
            conv_back(s, ext, pre, sig, jnp.concatenate(parts, axis=0), groups)
        hsum_ref[0:1] = sum_raw
        hsum_ref[1:2] = sum_log
        pl.when(place.has_left)(edges[1].start)

        @pl.when(place.has_right)
        def _():
            for copy in edges:
                copy.wait_recv()
            for s in range(seqs):
                fixed = tail_ref[s] + edge_came[s].astype(F32)
                dc_ref[(s + 1) * seg - EDGE : (s + 1) * seg, :channels] = fixed.astype(BF16)

        outs[4].start()
        for k in lanes[0].waves():
            for lane in lanes:
                lane.step(k)
        a_out[...] = lanes[0].keep[place.z]
        b_out[...] = lanes[1].keep[place.z]
        for lane in lanes:
            lane.finish()
        chain.finish()

        @pl.when(place.has_left)
        def _():
            for copy in edges:
                copy.wait_send()

        for copy in pairs:
            copy.wait_send()
        for copy in outs:
            copy.wait()


def scan_backward(
    pc, w, b, sb, dl, bc, dt, cum, cumt, dm, mixed, s0, s1, s2, tot, skip, normed_t, dz, turned, cot,
    head_dim, depth,
):
    seqs, rows, cols = pc.shape
    tokens, inner = dm.shape
    groups = inner // GROUP
    lag = depth - 1
    taps, channels = w.shape
    out = lambda i: jnp.maximum(i - lag, 0)
    inside = lambda i: jnp.minimum(out(i), groups - 1)
    wide = pl.BlockSpec((tokens, GROUP), lambda i: (0, inside(i)))
    states = pl.BlockSpec((seqs, LANES, GROUP), lambda i: (0, 0, inside(i)))
    line = lambda n: pl.BlockSpec((n, GROUP), lambda i: (0, inside(i)))
    conv = lambda n: pl.BlockSpec((n, GROUP), lambda i: (0, out(i)))
    ahead = lambda n: pl.BlockSpec((n, GROUP), lambda i: (0, jnp.minimum(i, groups - 1)))
    once = lambda v: pl.BlockSpec(v.shape, lambda i: (0,) * v.ndim, pipeline_mode=pl.Buffered(1))
    anywhere = pl.BlockSpec(memory_space=pl.ANY)
    chunks = tokens // CHUNK
    shape, dma = jax.ShapeDtypeStruct, pltpu.SemaphoreType.DMA
    a_rows, b_rows = normed_t.shape[1] // depth, turned.shape[1] // depth
    a_cols, b_cols = dz.shape[1] // 2, cot.shape[1] // 2
    half = lambda v: (4,) + v.shape[1:]
    sends, receives = Scatter.sems(depth)
    ring = lambda *dims: pltpu.VMEM((lag + 1,) + dims, F32)
    link = pltpu.VMEM((groups, seqs, LANES, GROUP), BF16)
    square = pltpu.VMEM((chunks, CHUNK, CHUNK), F32)
    column = pltpu.VMEM((tokens, LANES), F32)
    return pl.pallas_call(
        functools.partial(scan_backward_kernel, depth, head_dim, groups),
        grid=(groups + 1 + lag,),
        in_specs=[
            pl.BlockSpec((seqs, rows, GROUP), lambda i: (0, 0, out(i))),
            conv(taps),
            conv(1),
            pl.BlockSpec((seqs, rows, LANES), lambda i: (0, 0, cols // LANES - 1)),
            whole((1, LANES)), whole((1, LANES)),
            whole(bc.shape), whole(dt.shape), whole(cum.shape), whole(cumt.shape),
            ahead(tokens), wide, wide, states, states, states, ahead(8), line(1),
            once(normed_t), once(dz), once(turned), once(cot),
        ],
        out_specs=[
            anywhere, conv(taps), conv(1), line(1), whole((2, LANES)),
            whole((a_rows, a_cols)), whole((b_rows, b_cols)),
            anywhere, anywhere, anywhere, anywhere,
        ],
        out_shape=[
            shape((tokens, cols), BF16),
            shape((taps, channels), F32),
            shape((1, channels), F32),
            shape((1, inner), F32),
            shape((2, LANES), F32),
            shape((a_rows, a_cols), F32),
            shape((b_rows, b_cols), F32),
            shape(half(normed_t), BF16),
            shape(dz.shape, BF16),
            shape(half(turned), BF16),
            shape(cot.shape, BF16),
        ],
        scratch_shapes=[
            square, pltpu.VMEM((chunks, LANES, CHUNK), F32), square, column, column, column, column,
            pltpu.VMEM((8, LANES), F32),
            pltpu.VMEM((tokens, cols), BF16),
            pltpu.VMEM((seqs, EDGE, channels), F32),
            pltpu.VMEM((seqs, EDGE, channels), BF16),
            pltpu.VMEM((seqs, EDGE, channels), BF16),
            ring(seqs, LANES, GROUP), ring(8, GROUP), link, link,
            pltpu.VMEM(half(normed_t), BF16), pltpu.VMEM(dz.shape, BF16),
            pltpu.VMEM(half(turned), BF16), pltpu.VMEM(cot.shape, BF16),
            dma((groups,)), dma((groups,)), dma((2,)), dma((2,)), dma((10,)), dma((10,)), dma((5,)),
            dma((2, sends)), dma((2, receives)),
            *Scatter.scratch(depth, a_rows, a_cols),
            *Scatter.scratch(depth, b_rows, b_cols),
        ],
        compiler_params=pltpu.CompilerParams(
            dimension_semantics=("arbitrary",), collective_id=1, has_side_effects=True,
            vmem_limit_bytes=VMEM_LIMIT,
        ),
        name="scan_backward_sums",
    )(
        pc, w, b, pc, sb, dl, bc, dt, cum, cumt, dm, dm, mixed, s0, s1, s2, tot, skip,
        normed_t, dz, turned, cot,
    )


def scatter_last_kernel(
    depth, splits, nt_ref, nt_pair, dz_ref, dz_pair, no_ref, no_pair, cot_ref, cot_pair, dc_ref, small_src,
    a_out, b_out, c_out, small_out, *refs,
):
    place = Place(depth)
    place.meet()
    pieces = len(splits) - 1
    dc_pairs, refs = refs[:pieces], refs[pieces:]
    pair_send, pair_recv, send, recv, small_send, small_recv = refs[:6]
    refs = refs[6:]
    cuts = [dc_ref.at[:, pl.ds(lo, hi - lo)] for lo, hi in zip(splits, splits[1:])]
    copies = pair_copies(place, (), tuple(zip(cuts, dc_pairs)), pair_send, pair_recv)
    for copy in copies:
        copy.start()
    terms = [
        (nt_ref, nt_pair, dz_ref, dz_pair),
        (no_ref, no_pair, cot_ref, cot_pair),
        *((nt_ref, nt_pair, cut, pair) for cut, pair in zip(cuts, dc_pairs)),
    ]
    lanes = [
        Scatter(place, *term, *(("y", "x") if n % 2 == 0 else ("x", "y")), refs[7 * n : 7 * n + 7],
                send.at[n], recv.at[n])
        for n, term in enumerate(terms)
    ]
    small = SmallScatter(place, small_src, *refs[7 * len(lanes) :], small_send, small_recv)

    def run(*steps):
        for first, name, *rest in steps:
            for lane in lanes[first : first + 2]:
                getattr(lane, name)(*rest)

    def waves(first):
        for k in lanes[0].waves():
            run((first, "step", k))

    run((0, "send_second", 0), (0, "send_second", 1))
    small.stage(0)
    for copy in copies[:2]:
        copy.wait_recv()
    run((2, "send_second", 0), (2, "send_second", 1))
    small.stage(1)
    run((0, "send_first"))
    for copy in copies[2:]:
        copy.wait_recv()
    run((4, "send_second", 0), (4, "send_second", 1))
    small.stage(2)
    run((0, "hold"), (2, "send_first"))
    small.stage(3)
    waves(0)
    run((2, "hold"), (4, "send_first"))
    for k in lanes[0].waves():
        small.sums.step(k)
    waves(2)
    run((4, "hold"))
    waves(4)
    for lane, out in zip(lanes, (a_out, b_out)):
        out[...] = lane.keep[place.z]
    for lane, lo, hi in zip(lanes[2:], splits, splits[1:]):
        c_out[:, lo:hi] = lane.keep[place.z]
    small_out[...] = small.keep[place.z]
    for lane in lanes:
        lane.finish()
    small.finish()
    for copy in copies:
        copy.wait_send()


def scatter_last(normed_t, nt_pair, dz, dz_pair, turned, no_pair, cot, cot_pair, dc, small, depth):
    shape = jax.ShapeDtypeStruct
    vmem, dma = pl.BlockSpec(memory_space=pltpu.VMEM), pltpu.SemaphoreType.DMA
    right = lambda v: pl.BlockSpec((v.shape[0], v.shape[1] // 2), lambda i: (0, 1))
    sends, receives = Scatter.sems(depth)
    a_rows, b_rows = normed_t.shape[1] // depth, turned.shape[1] // depth
    a_cols, b_cols = dz.shape[1] // 2, cot.shape[1] // 2
    tokens, width = dc.shape
    blocks = width // LANES
    splits = tuple(LANES * (-(-blocks * n // 4)) for n in range(5))
    small_shape = small.shape[4:]
    small_sends, small_receives = SmallScatter.sems(depth)
    sizes = [hi - lo for lo, hi in zip(splits, splits[1:])]
    scratch = [*Scatter.scratch(depth, a_rows, a_cols), *Scatter.scratch(depth, b_rows, b_cols)]
    for size in sizes:
        scratch += Scatter.scratch(depth, a_rows, size)
    return pl.pallas_call(
        functools.partial(scatter_last_kernel, depth, splits),
        grid=(1,),
        in_specs=[vmem, vmem, right(dz), right(dz_pair), vmem, vmem, right(cot), right(cot_pair), vmem, vmem],
        out_specs=[vmem] * 4,
        out_shape=[
            shape((a_rows, a_cols), F32),
            shape((b_rows, b_cols), F32),
            shape((a_rows, width), F32),
            shape(small_shape, F32),
        ],
        scratch_shapes=[
            *(pltpu.VMEM((tokens, size), BF16) for size in sizes),
            dma((4,)), dma((4,)), dma((6, sends)), dma((6, receives)),
            dma((small_sends,)), dma((small_receives,)),
            *scratch,
            *SmallScatter.scratch(depth, small_shape),
        ],
        compiler_params=pltpu.CompilerParams(
            collective_id=2, has_side_effects=True, vmem_limit_bytes=VMEM_LIMIT
        ),
        name="scatter_last",
    )(normed_t, nt_pair, dz, dz_pair, turned, no_pair, cot, cot_pair, dc, small)


def passed_along(value, axis, steps):
    count = lax.axis_size(axis)
    initial, last = (max(0, -steps), min(count, count - steps))
    return lax.ppermute(value, axis, [(source, source + steps) for source in range(initial, last)])


def prefix(total, local, axis, backward):
    count, here = lax.axis_size(axis), lax.axis_index(axis)
    totals = lax.all_gather(total.astype(BF16), axis)
    locals_ = lax.all_gather(local, axis)
    state = jnp.zeros(local.shape, F32)
    order = range(count - 1, 0, -1) if backward else range(count - 1)
    for lap in order:
        new = totals[lap].astype(F32) * state + locals_[lap].astype(F32)
        reached = lap > here if backward else lap < here
        state = jnp.where(reached, new, state)
    leaves = total * state + local.astype(F32)
    return state.astype(BF16), leaves.astype(BF16)


AXES = ("dp", "ctx")


def body(
    inputs, gain_in, in_weight, conv_weight, conv_bias, step_bias, decay_log, skip_gain, gain_out,
    out_weight, cotangent,
):
    seqs, seg, width = inputs.shape
    tokens = seqs * seg
    count = lax.axis_size(AXES)
    dp, depth = lax.axis_size("dp"), lax.axis_size("ctx")
    own_links = dp == 8
    inner = out_weight.shape[0] * count
    taps, channels = conv_weight.shape[0], conv_weight.shape[1] * count
    num_heads = step_bias.shape[0]
    head_dim = inner // num_heads
    a, b, c = gain_in.shape[0], gain_out.shape[0], conv_bias.shape[0]

    w_gate = in_weight[:, :inner]
    w_conv = in_weight[:, inner:]
    spare = -w_conv.shape[1] % LANES
    w_conv = jnp.pad(w_conv, ((0, 0), (0, spare)))
    rest = jnp.concatenate([gain_out, conv_bias, conv_weight.reshape(-1)])
    ends = taps - 1
    flat = inputs.reshape(tokens, width)
    cot = cotangent.reshape(tokens, width)

    if own_links:
        group = 2 * depth * a
        at = lax.rem(lax.axis_index("dp"), 2) * depth + lax.axis_index("ctx")
        head = lax.dynamic_update_slice(jnp.zeros((group,), F32), gain_in.astype(F32), (at * a,))
        small = jnp.concatenate([head, rest.astype(F32)])
        small = jnp.pad(small, (0, 8 * LANES - small.size)).reshape(8, LANES)
        pc, normed_ext, normed_t, small, w_conv = gather_project(inputs, small, w_conv, depth)
        w_conv = w_conv.reshape(width, -1)
        small = small.reshape(4, 2 * depth, 8 * LANES)
        g_in = small[:, :, :group].sum(axis=1).reshape(1, width)
        rest = small[:, :, group:].reshape(count, -1)
    else:
        before = passed_along(inputs[:, seg - EDGE :], "ctx", 1)
        ext = jnp.concatenate([before, inputs], axis=1).astype(F32)
        scale_ext = lax.rsqrt(jnp.mean(ext * ext, axis=-1, keepdims=True) + EPS)
        small = lax.all_gather(jnp.concatenate([gain_in, rest]), AXES).astype(F32)
        w_conv = lax.all_gather(w_conv, AXES, axis=0, tiled=True)
        w_gate = lax.all_gather(w_gate, AXES, axis=0, tiled=True)
        w_out = lax.all_gather(out_weight, AXES, axis=0, tiled=True)
        g_in, rest = small[:, :a].reshape(1, width), small[:, a:]
        normed_ext = (ext * scale_ext * g_in).astype(BF16)
        pc = dot(normed_ext.reshape(-1, width), w_conv).reshape(seqs, seg + EDGE, -1)
    g_out = rest[:, :b].reshape(1, inner)
    bias = rest[:, b : b + c].reshape(1, channels)
    kernel = rest[:, b + c : b + c + taps * c].reshape(count, taps, c).transpose(1, 0, 2)
    kernel = kernel.reshape(taps, channels)
    pad_head = lambda v: jnp.pad(v, (0, LANES - num_heads)).reshape(1, LANES)
    sb, dl = pad_head(step_bias), pad_head(decay_log)
    skip = jnp.repeat(skip_gain, head_dim).reshape(1, inner)

    if own_links:
        bc, dt, cum, cumt, mixed, s0, s1, s2, tot, w_gate, w_out = scan_forward(
            pc, kernel, bias, sb, dl, skip, w_gate, out_weight, inner, head_dim, depth
        )
        w_gate = w_gate.reshape(width, inner)
        w_out = w_out.reshape(inner, width)
        per_seq = tot[tokens // CHUNK : tokens // CHUNK + seqs][:, None, :]
    else:
        x, bc, dt, cum, cumt, loc0, local, tot = fwd_a(pc, kernel, bias, sb, dl, inner, head_dim)
        per_seq = tot[tokens // CHUNK : tokens // CHUNK + seqs][:, None, :]
        s0, s2 = prefix(per_seq, local, "ctx", False)
        mixed, s1 = fwd_b(x, bc, dt, cum, cumt, s0, loc0, tot, skip, head_dim)

    turned, output, d_mixed, d_gate, grad_gain_out = mid(
        normed_ext, w_gate, mixed, w_out, g_out, flat, cot, 8
    )
    if own_links:
        d_conv, grad_kernel, grad_bias, grad_skip, head_sums, gate_left, out_left, *pairs = scan_backward(
            pc, kernel, bias, sb, dl, bc, dt, cum, cumt, d_mixed, mixed, s0, s1, s2, tot, skip,
            normed_t, d_gate, turned, cot, head_dim, depth,
        )
    else:
        scatter = lambda v: lax.psum_scatter(v.astype(BF16), AXES, scatter_dimension=0, tiled=True).astype(F32)
        normed = normed_ext[:, EDGE:].reshape(tokens, width)
        grad_out_weight = scatter(dot(turned.reshape(inner, tokens), cot))
        grad_gate_weight = scatter(dot(normed, d_gate, ((0,), (0,))))
        adjoint = bwd_a(d_mixed, bc, cum, tot, seqs, head_dim)
        g, _ = prefix(per_seq, adjoint, "ctx", True)
        d_conv, tail, edge, grad_kernel, grad_bias, grad_skip, d_raw, head_sums = bwd_b(
            pc, kernel, bias, sb, dl, bc, dt, cum, cumt, d_mixed, mixed, s0, s1, s2, g, tot, skip, head_dim
        )
        after = passed_along(edge[:, EDGE - ends :].astype(BF16), "ctx", -1).astype(F32)
        tail = tail[:, EDGE - ends :] + after
        d_conv = d_conv.reshape(seqs, seg, channels).at[:, seg - ends :].set(tail.astype(BF16))
        d_conv = jnp.concatenate([d_conv.reshape(tokens, channels), d_raw.astype(BF16)], axis=1)

    d_normed = nt(d_gate, w_gate) + nt(d_conv, w_conv)
    values = flat.astype(F32)
    scale = lax.rsqrt(jnp.mean(values * values, axis=-1, keepdims=True) + EPS)
    hat = values * scale
    grad_gain_in = jnp.sum(d_normed * hat, axis=0)
    weighted = d_normed * g_in
    pull = jnp.mean(weighted * hat, axis=-1, keepdims=True)
    grad_input = scale * (weighted - hat * pull) + cot.astype(F32)

    grad_skip = jnp.sum(grad_skip.reshape(num_heads, head_dim), axis=1)
    heads_sum = jnp.concatenate([head_sums[0, :num_heads], head_sums[1, :num_heads], grad_skip])
    by_owner = jnp.concatenate(
        [
            grad_gain_in.reshape(count, a),
            grad_gain_out.reshape(count, b),
            grad_bias.reshape(count, c),
            grad_kernel.reshape(taps, count, c).transpose(1, 0, 2).reshape(count, taps * c),
            jnp.broadcast_to(heads_sum, (count, 3 * num_heads)),
        ],
        axis=1,
    )
    real = d_conv.shape[1] - spare
    if own_links:
        by_owner = jnp.pad(by_owner, ((0, 0), (0, 8 * LANES - by_owner.shape[1])))
        nt_pair, dz_pair, no_pair, cot_pair = pairs
        gate_right, out_right, grad_conv_cols, mine = scatter_last(
            normed_t, nt_pair, d_gate, dz_pair, turned, no_pair, cot, cot_pair, d_conv,
            by_owner.reshape(2, 2, 2, depth, 8, LANES), depth,
        )
        grad_gate_weight = jnp.concatenate([gate_left, gate_right], axis=1)
        grad_out_weight = jnp.concatenate([out_left, out_right], axis=1)
        grad_conv_cols, mine = grad_conv_cols[:, :real], mine.reshape(-1)
    else:
        grad_conv_cols = scatter(dot(normed, d_conv[:, :real], ((0,), (0,))))
        mine = lax.dynamic_index_in_dim(lax.psum(by_owner, AXES), lax.axis_index(AXES), 0, False)
    at = a + b + c + taps * c
    head_totals = mine[at : at + 3 * num_heads].reshape(3, num_heads)
    return (
        output.reshape(seqs, seg, width),
        grad_input.reshape(seqs, seg, width),
        mine[:a],
        jnp.concatenate([grad_gate_weight, grad_conv_cols], axis=1),
        mine[a + b + c : at].reshape(taps, c),
        mine[a + b : a + b + c],
        head_totals[0],
        head_totals[1],
        head_totals[2],
        mine[a : a + b],
        grad_out_weight,
    )


def solution(mesh):
    rows, cols, both = P("dp", "ctx", None), P(AXES, None), P(AXES)
    return jax.shard_map(
        body,
        mesh=mesh,
        in_specs=(rows, both, cols, P(None, AXES), both, P(), P(), P(), both, cols, rows),
        out_specs=(rows, rows, both, cols, P(None, AXES), both, P(), P(), P(), both, cols),
        check_vma=False,
    )
```

```python
import functools

import jax
import jax.numpy as jnp
from jax import lax
from jax.experimental import pallas as pl
from jax.experimental.pallas import tpu as pltpu
from jax.sharding import PartitionSpec as P

EPS = 1e-05
LOG2E = 1.4426950408889634
HIGH = lax.Precision.HIGHEST
F32 = jnp.float32
BF16 = jnp.bfloat16
CHUNK = 128
GROUP = 256
EDGE = 16
LANES = 128
VMEM_LIMIT = 60 * 1024 * 1024


def dot(a, b, dims=((1,), (0,))):
    return lax.dot_general(a, b, (dims, ((), ())), preferred_element_type=F32)


def nt(a, b):
    return dot(a, b, ((1,), (1,)))


def params():
    return pltpu.CompilerParams(
        dimension_semantics=("arbitrary",), vmem_limit_bytes=VMEM_LIMIT
    )


def whole(shape):
    return pl.BlockSpec(shape, lambda i: (0,) * len(shape))


def sigmoid(v):
    return 1.0 / (1.0 + jnp.exp(-v))


def softplus(v):
    return jnp.maximum(v, 0.0) + jnp.log1p(jnp.exp(-jnp.abs(v)))


def causal_conv(ext, w, b, seg):
    taps = w.shape[0]
    total = b
    for k in range(taps):
        at = EDGE - (taps - 1) + k
        total = total + w[k : k + 1] * ext[at : at + seg]
    return total


def lane_shift(value, lanes):
    return pltpu.roll(value, lax.rem(LANES - lanes, LANES), 1)


def head_rows(ref, first):
    base = pl.multiple_of(first // 8 * 8, 8)
    return pltpu.roll(ref[pl.ds(base, 8), :], lax.rem(8 - lax.rem(first, 8), 8), 0)


def spread(cols, at, head_dim):
    rows = cols.shape[0]
    lane = lax.broadcasted_iota(jnp.int32, (rows, LANES), 1)
    first = jnp.broadcast_to(cols[:, at : at + 1], (rows, LANES))
    second = jnp.broadcast_to(cols[:, at + 1 : at + 2], (rows, LANES))
    return jnp.where(lane < head_dim, first, second)


def spread_all(cols, heads, head_dim):
    return jnp.concatenate([spread(cols, j, head_dim) for j in range(0, heads, 2)], axis=1)


def block_diagonal(pair, head_dim):
    lane = lax.broadcasted_iota(jnp.int32, pair.shape, 1)
    zero = jnp.zeros_like(pair)
    return jnp.concatenate(
        [jnp.where(lane < head_dim, pair, zero), jnp.where(lane < head_dim, zero, pair)], axis=0
    )


MESH = pl.DeviceIdType.MESH


class Place:
    def __init__(self, depth):
        dp, z = lax.axis_index("dp"), lax.axis_index("ctx")
        self.depth, self.z = depth, z
        self.own = {"y": lax.div(dp, 4), "x": lax.rem(lax.div(dp, 2), 2), "c": lax.rem(dp, 2)}
        self.to = {
            name: {"dp": dp + step * (1 - 2 * self.own[name])}
            for name, step in (("y", 4), ("x", 2), ("c", 1))
        }
        self.has_left, self.has_right = z > 0, z < depth - 1
        self.left, self.right = {"ctx": z - 1}, {"ctx": z + 1}

    def flipped(self, *names):
        return {n: 1 - v if n in names else v for n, v in self.own.items()}

    def near(self, k):
        z, last = self.z, self.depth - 1
        reach = jnp.minimum(z, last - z)
        pair = jnp.where(k % 2 == 1, z - (k + 1) // 2, z + k // 2)
        alone = jnp.where(z > last - z, last - k, k)
        return z if k == 0 else jnp.where(k <= 2 * reach, pair, alone)

    def meet(self):
        barrier = pltpu.get_barrier_semaphore()
        signal = functools.partial(pl.semaphore_signal, barrier, inc=1, device_id_type=MESH)
        for name in ("y", "x", "c"):
            signal(device_id=self.to[name])
        pl.when(self.has_left)(lambda: signal(device_id=self.left))
        pl.when(self.has_right)(lambda: signal(device_id=self.right))
        ends = self.has_left.astype(jnp.int32) + self.has_right.astype(jnp.int32)
        pl.semaphore_wait(barrier, 3 + ends)


def remote(src, dst, send, recv, to):
    return pltpu.make_async_remote_copy(
        src_ref=src, dst_ref=dst, send_sem=send, recv_sem=recv, device_id=to, device_id_type=MESH
    )


class Gather:
    def __init__(self, place, src, slot, first, second, send, recv):
        self.place, self.src, self.slot_of = place, src, slot
        self.first, self.second, self.send, self.recv = first, second, send, recv

    @staticmethod
    def sems(depth):
        return 9 * depth, 8 * depth

    def slot(self, k, *flips):
        return self.slot_of(self.place.near(k), **self.place.flipped(*flips))

    def copy(self, k, kind, where, to, recv):
        src = self.src if k == 0 and where == () else self.slot(k, *where)
        send = self.send.at[kind * self.place.depth + k]
        return remote(src, self.slot(k, *where), send, self.recv.at[recv], to)

    def along(self, k, right):
        p = self.place
        return self.copy(k, int(right), (), p.right if right else p.left, p.near(k))

    def goes(self, k, right):
        p, at = self.place, self.place.near(k)
        if right:
            return p.has_right if k == 0 else p.has_right & (at < p.z)
        return p.has_left if k == 0 else p.has_left & (at > p.z)

    def to_axis(self, k, stage):
        p, depth = self.place, self.place.depth
        f, s = self.first, self.second
        where = ((), (), (f,), (), (f,), (s,), (f, s))[stage]
        to = p.to[(f, s, s, "c", "c", "c", "c")[stage]]
        return self.copy(k, 2 + stage, where, to, (1 + stage) * depth + k)

    def arrived(self, k, stage):
        p, depth = self.place, self.place.depth
        f, s = self.first, self.second
        where = ((f,), (s,), (s, f), ("c",), ("c", f), ("c", s), ("c", f, s))[stage]
        self.copy(k, 2 + stage, where, p.to["c"], (1 + stage) * depth + k).wait_recv()

    def line(self, k):
        if k:
            self.along(k, True).wait_recv()
        for right in (True, False):
            pl.when(self.goes(k, right))(lambda: self.along(k, right).start())
        for stage in (0, 1, 3):
            self.to_axis(k, stage).start()

    def from_first(self, k):
        self.arrived(k, 0)
        self.to_axis(k, 2).start()
        self.to_axis(k, 4).start()

    def from_second(self, k):
        self.arrived(k, 1)
        self.to_axis(k, 5).start()

    def from_both(self, k):
        self.arrived(k, 2)
        self.to_axis(k, 6).start()

    def finish(self):
        for k in range(self.place.depth):
            for right in (True, False):
                pl.when(self.goes(k, right))(lambda: self.along(k, right).wait_send())
            for stage in range(7):
                self.to_axis(k, stage).wait_send()


class Line:
    def __init__(self, place, keep, sent, came, send, recv):
        self.place, self.keep, self.sent, self.came = place, keep, sent, came
        self.send, self.recv = send, recv

    def copy(self, k, to, at):
        zk = self.place.near(k)
        return remote(self.sent.at[zk], self.came.at[at], self.send.at[k], self.recv.at[at], to)

    def take(self, at):
        self.copy(1, self.place.left, at).wait_recv()
        zk = jnp.where(at == self.place.depth, self.place.z, at)
        self.keep[zk] = self.keep[zk] + self.came[at].astype(F32)

    def moves(self, k):
        p, zk = self.place, self.place.near(k)
        return (
            (zk < p.z, p.left, zk),
            (zk > p.z, p.right, jnp.where(zk == p.z + 1, p.depth, zk)),
        )

    def step(self, k):
        p, zk = self.place, self.place.near(k)
        if k == 0:
            pl.when(p.has_right)(lambda: self.take(p.z))
            pl.when(p.has_left)(lambda: self.take(p.depth))
            return
        farther = ((zk < p.z) & p.has_right) | ((zk > p.z) & p.has_left)
        pl.when(farther)(lambda: self.take(zk))
        self.sent[zk] = self.keep[zk].astype(self.sent.dtype)
        for goes, to, at in self.moves(k):
            pl.when(goes)(lambda: self.copy(k, to, at).start())

    def finish(self):
        for k in range(1, self.place.depth):
            for goes, to, at in self.moves(k):
                pl.when(goes)(lambda: self.copy(k, to, at).wait_send())


class Scatter:
    def __init__(self, place, lhs, lhs_pair, rhs, rhs_pair, first, second, bufs, send, recv):
        self.place, self.lhs, self.lhs_pair, self.rhs, self.rhs_pair = place, lhs, lhs_pair, rhs, rhs_pair
        self.first, self.second, self.send, self.recv = first, second, send, recv
        self.s_sent, self.s_came, self.f_sent, self.f_came, self.keep, z_sent, z_came = bufs
        depth = place.depth
        self.sums = Line(place, self.keep, z_sent, z_came, send.at[pl.ds(3 * depth, depth)],
                         recv.at[pl.ds(3 * depth, depth + 1)])

    @staticmethod
    def sems(depth):
        return 4 * depth, 4 * depth + 1

    @staticmethod
    def scratch(depth, rows, cols):
        block = lambda *lead: pltpu.VMEM(lead + (rows, cols), BF16)
        return [
            block(2, depth), block(2, depth), block(depth), block(depth),
            pltpu.VMEM((depth, rows, cols), F32), block(depth), block(depth + 1),
        ]

    def product(self, flips, store):
        at = self.place.flipped(*flips)
        pair = 2 * at["y"] + at["x"]
        one = 2 * pair + at["c"]
        rows, cols = self.keep.shape[1:]
        tile = 512

        def block(start, size):
            lanes = pl.ds(start, size)
            part = dot(self.lhs[one], self.rhs[:, lanes]) + dot(self.lhs_pair[pair], self.rhs_pair[:, lanes])
            for z in range(self.place.depth):
                store(z, lanes, part[z * rows : (z + 1) * rows])

        def loop(i, carry):
            block(pl.multiple_of(i * tile, tile), tile)
            return carry

        lax.fori_loop(0, cols // tile, loop, 0)
        if cols % tile:
            block(cols // tile * tile, cols % tile)

    def to_second(self, j, k):
        zk, n = self.place.near(k), j * self.place.depth + k
        return remote(self.s_sent.at[j, zk], self.s_came.at[j, zk], self.send.at[n], self.recv.at[n],
                      self.place.to[self.second])

    def to_first(self, k):
        zk, n = self.place.near(k), 2 * self.place.depth + k
        return remote(self.f_sent.at[zk], self.f_came.at[zk], self.send.at[n], self.recv.at[n],
                      self.place.to[self.first])

    def waves(self):
        return range(self.place.depth - 1, -1, -1)

    def send_second(self, j):
        def store(z, lanes, part):
            self.s_sent[j, z, :, lanes] = part.astype(BF16)

        self.product((self.second, self.first) if j == 0 else (self.second,), store)
        for k in self.waves():
            self.to_second(j, k).start()

    def send_first(self):
        for k in self.waves():
            self.to_second(0, k).wait_recv()

        def store(z, lanes, part):
            self.f_sent[z, :, lanes] = (part + self.s_came[0, z, :, lanes].astype(F32)).astype(BF16)

        self.product((self.first,), store)
        for k in self.waves():
            self.to_first(k).start()

    def hold(self):
        for k in self.waves():
            self.to_second(1, k).wait_recv()

        def store(z, lanes, part):
            self.keep[z, :, lanes] = part + self.s_came[1, z, :, lanes].astype(F32)

        self.product((), store)

    def step(self, k):
        self.to_first(k).wait_recv()
        zk = self.place.near(k)
        self.keep[zk] = self.keep[zk] + self.f_came[zk].astype(F32)
        self.sums.step(k)

    def finish(self):
        for k in self.waves():
            self.to_second(0, k).wait_send()
            self.to_second(1, k).wait_send()
            self.to_first(k).wait_send()
        self.sums.finish()


class SmallScatter:
    def __init__(self, place, src, c_came, half, x_came, keep, y_came, z_sent, z_came, send, recv):
        self.place, self.src, self.c_came, self.half = place, src, c_came, half
        self.x_came, self.keep, self.y_came = x_came, keep, y_came
        self.send, self.recv = send, recv
        depth = place.depth
        self.sums = Line(place, keep, z_sent, z_came, send.at[pl.ds(7, depth)],
                         recv.at[pl.ds(7, depth + 1)])

    @staticmethod
    def sems(depth):
        return 7 + depth, 8 + depth

    @staticmethod
    def scratch(depth, shape):
        block = lambda *lead: pltpu.VMEM(lead + shape, F32)
        return [
            block(2, 2, depth), block(2, 2, depth), block(2, depth), block(depth), block(depth),
            block(depth), block(depth + 1),
        ]

    def copy(self, n):
        p, own = self.place, self.place.own
        if n < 4:
            y, x = n // 2, n % 2
            src, dst, to = self.src.at[y, x, 1 - own["c"]], self.c_came.at[y, x], "c"
        elif n < 6:
            src, dst, to = self.half.at[n - 4, 1 - own["x"]], self.x_came.at[n - 4], "x"
        else:
            src, dst, to = self.half.at[1 - own["y"], own["x"]], self.y_came, "y"
        return remote(src, dst, self.send.at[n], self.recv.at[n], p.to[to])

    def stage(self, n):
        own = self.place.own
        if n == 0:
            for i in range(4):
                self.copy(i).start()
        elif n == 1:
            for i in range(4):
                self.copy(i).wait_recv()
            for y in (0, 1):
                for x in (0, 1):
                    self.half[y, x] = self.src[y, x, own["c"]] + self.c_came[y, x]
            for i in (4, 5):
                self.copy(i).start()
        elif n == 2:
            for i in (4, 5):
                self.copy(i).wait_recv()
            for y in (0, 1):
                self.half[y, own["x"]] = self.half[y, own["x"]] + self.x_came[y]
            self.copy(6).start()
        else:
            self.copy(6).wait_recv()
            self.keep[...] = self.half[own["y"], own["x"]] + self.y_came[...]

    def finish(self):
        for n in range(7):
            self.copy(n).wait_send()
        self.sums.finish()


def gather_kernel(
    depth, half, x_ref, small_src, wc_src, pc_ref, normed_ref, normt_ref, small_ref, wc_ref,
    hat_ref, edge_ref, buf_ref, edge_sem, load_sem, own_sem, send, recv,
):
    place = Place(depth)
    place.meet()
    seqs, seg, features = x_ref.shape
    width = wc_src.shape[1]
    lo, hi = pl.ds(0, half), pl.ds(half, width - half)
    lanes = [
        Gather(place, small_src, lambda z, y, x, c: small_ref.at[y, x, c, z], "y", "x",
               send.at[0], recv.at[0]),
        Gather(place, wc_src.at[:, lo], lambda z, y, x, c: wc_ref.at[y, x, c, z, :, lo], "y", "x",
               send.at[1], recv.at[1]),
        Gather(place, wc_src.at[:, hi], lambda z, y, x, c: wc_ref.at[y, x, c, z, :, hi], "x", "y",
               send.at[2], recv.at[2]),
    ]
    own = place.own
    mine = (own["y"], own["x"], own["c"], place.z)
    copies = [
        pltpu.make_async_copy(src, dst.at[mine], own_sem.at[n])
        for n, (src, dst) in enumerate(((small_src, small_ref), (wc_src, wc_ref)))
    ]
    edge = remote(x_ref.at[:, pl.ds(seg - EDGE, EDGE)], edge_ref, edge_sem.at[0], edge_sem.at[1], place.right)

    def each(group, *steps):
        for name, k in steps:
            for lane in group:
                getattr(lane, name)(k)

    def core(group, stage):
        for k in range(depth):
            for lane in group:
                lane.arrived(k, stage)

    def load(n, at):
        return pltpu.make_async_copy(wc_ref.at[at["y"], at["x"]], buf_ref.at[n % 2], load_sem.at[n % 2])

    rows = wc_src.shape[0]
    count = 2 * depth * rows
    tile = 3 * LANES

    def multiply(n, at):
        group = 2 * at["y"] + at["x"]
        here = pl.ds(pl.multiple_of(group * count, LANES), count)
        gain = sum(
            small_ref[at["y"], at["x"], c, z, : count // LANES] for c in (0, 1) for z in range(depth)
        )
        gain = jnp.concatenate([gain[i : i + 1] for i in range(count // LANES)], axis=1)
        for s in range(seqs):
            normed = (hat_ref[s, :, here] * gain).astype(BF16)
            normed_ref[s, :, here] = normed
            turned = normed[EDGE:].astype(F32).T.astype(BF16)
            for c in (0, 1):
                normt_ref[2 * group + c, :, s * seg : (s + 1) * seg] = turned[c * depth * rows : (c + 1) * depth * rows]
        load(n, at).wait()

        def one(i, carry):
            cols = pl.ds(pl.multiple_of(i * tile, tile), tile)
            block = jnp.concatenate(
                [buf_ref[n % 2, c, z, :, cols] for c in (0, 1) for z in range(depth)], axis=0
            )
            for s in range(seqs):
                part = dot(normed_ref[s, :, here], block)
                if n == 0:
                    pc_ref[s, :, cols] = part
                else:
                    pc_ref[s, :, cols] += part
            return carry

        lax.fori_loop(0, width // tile, one, 0)

    each(lanes, ("line", 0))
    pl.when(place.has_right)(edge.start)
    for copy in copies:
        copy.start()
    pl.when(place.has_left)(edge.wait_recv)

    @pl.when(jnp.logical_not(place.has_left))
    def _():
        edge_ref[...] = jnp.zeros_like(edge_ref)

    for s in range(seqs):
        for start, rows_in in ((0, edge_ref), (EDGE, x_ref)):
            size = rows_in.shape[1]
            step = min(size, 64)
            for r in range(0, size, step):
                values = rows_in[s, r : r + step].astype(F32)
                mean = jnp.mean(values * values, axis=1, keepdims=True)
                hat_ref[s, start + r : start + r + step] = values * lax.rsqrt(mean + EPS)
    for copy in copies:
        copy.wait()
    for k in range(1, depth):
        each(lanes, ("line", k), ("from_first", k - 1))
        if k >= 2:
            each(lanes, ("from_second", k - 2), ("from_both", k - 2))
    last = depth - 1
    each(lanes, ("from_first", last), ("from_second", last - 1), ("from_both", last - 1))
    each(lanes, ("from_second", last))
    groups = [place.flipped(*f) for f in ((), ("y",), ("x",), ("y", "x"))]
    core(lanes, 3)
    load(0, groups[0]).start()
    multiply(0, groups[0])
    core(lanes, 4)
    core(lanes, 5)
    load(1, groups[1]).start()
    load(2, groups[2]).start()
    multiply(1, groups[1])
    each(lanes, ("from_both", last))
    multiply(2, groups[2])
    core(lanes, 6)
    load(3, groups[3]).start()
    multiply(3, groups[3])
    for lane in lanes:
        lane.finish()
    pl.when(place.has_right)(edge.wait_send)


def gather_project(x, small, wc, depth):
    shape = jax.ShapeDtypeStruct
    seqs, seg, features = x.shape
    slots = (2, 2, 2, depth)
    sends, receives = Gather.sems(depth)
    width = wc.shape[1]
    half = width // 2 // LANES * LANES
    anywhere, vmem = pl.BlockSpec(memory_space=pl.ANY), pl.BlockSpec(memory_space=pltpu.VMEM)
    dma = pltpu.SemaphoreType.DMA
    return pl.pallas_call(
        functools.partial(gather_kernel, depth, half),
        in_specs=[vmem, vmem, anywhere],
        out_specs=[vmem, vmem, vmem, vmem, anywhere],
        out_shape=[
            shape((seqs, seg + EDGE, width), F32),
            shape((seqs, seg + EDGE, features), BF16),
            shape((8, depth * wc.shape[0], seqs * seg), BF16),
            shape(slots + small.shape, F32),
            shape(slots + wc.shape, BF16),
        ],
        scratch_shapes=[
            pltpu.VMEM((seqs, seg + EDGE, features), F32),
            pltpu.VMEM((seqs, EDGE, features), BF16),
            pltpu.VMEM((2, 2, depth) + wc.shape, BF16),
            dma((2,)), dma((2,)), dma((2,)), dma((3, sends)), dma((3, receives)),
        ],
        compiler_params=pltpu.CompilerParams(
            collective_id=0, has_side_effects=True, vmem_limit_bytes=VMEM_LIMIT
        ),
        name="gather_project",
    )(x, small, wc)


def fwd_a_kernel(
    head_dim, pc_ref, w_ref, b_ref, raw_ref, sb_ref, dl_ref,
    x_ref, bc_ref, dt_ref, cum_ref, cumt_ref, loc0_ref, seg_ref, tot_ref, bt_ref,
):
    step = pl.program_id(0)
    seqs = pc_ref.shape[0]
    seg = pc_ref.shape[1] - EDGE
    chunks = seg // CHUNK
    w, b = w_ref[...], b_ref[...]

    def acts_of(s):
        pre = causal_conv(pc_ref[s], w, b, seg)
        return pre * sigmoid(pre)

    @pl.when(step == 0)
    def _():
        row = lax.broadcasted_iota(jnp.int32, (CHUNK, CHUNK), 0)
        col = lax.broadcasted_iota(jnp.int32, (CHUNK, CHUNK), 1)
        tri = (col <= row).astype(F32)
        rate = -jnp.exp(dl_ref[...])
        for s in range(seqs):
            acts = acts_of(s)
            bc_ref[s * seg : (s + 1) * seg] = acts
            for c in range(chunks):
                q = s * chunks + c
                rows = slice(q * CHUNK, (q + 1) * CHUNK)
                bt_ref[q] = acts[c * CHUNK : (c + 1) * CHUNK, :LANES].T.astype(BF16)
                dt = softplus(raw_ref[s, EDGE + c * CHUNK : EDGE + (c + 1) * CHUNK] + sb_ref[...])
                cum = LOG2E * jnp.dot(tri, dt * rate, precision=HIGH, preferred_element_type=F32)
                dt_ref[rows] = dt
                cum_ref[rows] = cum
                cumt_ref[:, rows] = cum.T

    @pl.when(step > 0)
    def _():
        heads = GROUP // head_dim
        first = (step - 1) * heads
        cumg = lane_shift(cum_ref[...], first)
        dtg = lane_shift(dt_ref[...], first)
        for s in range(seqs):
            x = acts_of(s)
            x_ref[s * seg : (s + 1) * seg] = x
            state, total = None, None
            for c in range(chunks):
                q = s * chunks + c
                rows = slice(q * CHUNK, (q + 1) * CHUNK)
                ce = spread_all(cumg[rows], heads, head_dim)
                de = spread_all(dtg[rows], heads, head_dim)
                end = ce[CHUNK - 1 : CHUNK]
                uw = x[c * CHUNK : (c + 1) * CHUNK] * de * jnp.exp2(end - ce)
                loc = dot(bt_ref[q], uw.astype(BF16))
                tot = jnp.exp2(end)
                tot_ref[q : q + 1] = tot
                if c == 0:
                    loc0_ref[s] = loc
                    state, total = loc, tot
                else:
                    state, total = tot * state + loc, tot * total
            seg_ref[s] = state.astype(BF16)
            tot_ref[seqs * chunks + s : seqs * chunks + s + 1] = total


def fwd_a(pc, w, b, sb, dl, inner, head_dim):
    seqs, rows, cols = pc.shape
    seg = rows - EDGE
    tokens = seqs * seg
    groups = inner // GROUP
    state = LANES
    chunks = tokens // CHUNK
    at = lambda i: (i + groups) % (groups + 1)
    back = lambda i: jnp.maximum(i - 1, 0)
    return pl.pallas_call(
        functools.partial(fwd_a_kernel, head_dim),
        grid=(groups + 1,),
        in_specs=[
            pl.BlockSpec((seqs, rows, GROUP), lambda i: (0, 0, at(i))),
            pl.BlockSpec((w.shape[0], GROUP), lambda i: (0, at(i))),
            pl.BlockSpec((1, GROUP), lambda i: (0, at(i))),
            pl.BlockSpec((seqs, rows, LANES), lambda i: (0, 0, cols // LANES - 1)),
            whole((1, LANES)),
            whole((1, LANES)),
        ],
        out_specs=[
            pl.BlockSpec((tokens, GROUP), lambda i: (0, back(i))),
            whole((tokens, GROUP)),
            whole((tokens, LANES)),
            whole((tokens, LANES)),
            whole((LANES, tokens)),
            pl.BlockSpec((seqs, state, GROUP), lambda i: (0, 0, back(i))),
            pl.BlockSpec((seqs, state, GROUP), lambda i: (0, 0, back(i))),
            pl.BlockSpec((8, GROUP), lambda i: (0, back(i))),
        ],
        out_shape=[
            jax.ShapeDtypeStruct((tokens, inner), F32),
            jax.ShapeDtypeStruct((tokens, GROUP), F32),
            jax.ShapeDtypeStruct((tokens, LANES), F32),
            jax.ShapeDtypeStruct((tokens, LANES), F32),
            jax.ShapeDtypeStruct((LANES, tokens), F32),
            jax.ShapeDtypeStruct((seqs, state, inner), F32),
            jax.ShapeDtypeStruct((seqs, state, inner), BF16),
            jax.ShapeDtypeStruct((8, inner), F32),
        ],
        scratch_shapes=[pltpu.VMEM((chunks, LANES, CHUNK), BF16)],
        compiler_params=params(),
        name="conv_states",
    )(pc, w, b, pc, sb, dl)


def fwd_b_kernel(
    head_dim, x_ref, bc_ref, dt_ref, cum_ref, cumt_ref, s0_ref, loc0_ref, tot_ref, skip_ref,
    mixed_ref, s1_ref, cb_ref,
):
    step = pl.program_id(0)
    seqs = s0_ref.shape[0]
    chunks = x_ref.shape[0] // CHUNK // seqs
    heads = GROUP // head_dim

    @pl.when(step == 0)
    def _():
        for q in range(seqs * chunks):
            rows = slice(q * CHUNK, (q + 1) * CHUNK)
            cb_ref[q] = nt(bc_ref[rows, LANES:].astype(BF16), bc_ref[rows, :LANES].astype(BF16))

    first = step * heads
    cumg = lane_shift(cum_ref[...], first)
    dtg = lane_shift(dt_ref[...], first)
    cumr = head_rows(cumt_ref, first)
    row = lax.broadcasted_iota(jnp.int32, (CHUNK, CHUNK), 0)
    col = lax.broadcasted_iota(jnp.int32, (CHUNK, CHUNK), 1)
    causal = col <= row
    skip = skip_ref[...]
    for s in range(seqs):
        start = s0_ref[s]
        for c in range(chunks):
            q = s * chunks + c
            rows = slice(q * CHUNK, (q + 1) * CHUNK)
            x = x_ref[rows]
            ce = spread_all(cumg[rows], heads, head_dim)
            de = spread_all(dtg[rows], heads, head_dim)
            ub = (x * de).astype(BF16)
            cb = cb_ref[q]
            parts = []
            for j in range(0, heads, 2):
                mats = []
                for h in (j, j + 1):
                    there = jnp.broadcast_to(cumg[rows, h : h + 1], (CHUNK, CHUNK))
                    here = cumr[h : h + 1, rows]
                    decay = jnp.exp2(jnp.where(causal, there - here, -jnp.inf))
                    mats.append((decay * cb).astype(BF16))
                pair = ub[:, j * head_dim : (j + 2) * head_dim]
                parts.append(dot(jnp.concatenate(mats, axis=1), block_diagonal(pair, head_dim)))
            y = jnp.concatenate(parts, axis=1)
            y = y + jnp.exp2(ce) * dot(bc_ref[rows, LANES:].astype(BF16), start)
            mixed_ref[rows] = y + skip * x
            if c == 0:
                start = (tot_ref[q : q + 1] * start.astype(F32) + loc0_ref[s]).astype(BF16)
                s1_ref[s] = start


def fwd_b(x, bc, dt, cum, cumt, s0, loc0, tot, skip, head_dim):
    tokens, inner = x.shape
    seqs, state, _ = s0.shape
    groups = inner // GROUP
    wide = pl.BlockSpec((tokens, GROUP), lambda i: (0, i))
    states = pl.BlockSpec((seqs, state, GROUP), lambda i: (0, 0, i))
    return pl.pallas_call(
        functools.partial(fwd_b_kernel, head_dim),
        grid=(groups,),
        in_specs=[
            wide, whole(bc.shape), whole(dt.shape), whole(cum.shape), whole(cumt.shape),
            states, states,
            pl.BlockSpec((8, GROUP), lambda i: (0, i)),
            pl.BlockSpec((1, GROUP), lambda i: (0, i)),
        ],
        out_specs=[wide, states],
        out_shape=[
            jax.ShapeDtypeStruct((tokens, inner), F32),
            jax.ShapeDtypeStruct((seqs, state, inner), BF16),
        ],
        scratch_shapes=[pltpu.VMEM((tokens // CHUNK, CHUNK, CHUNK), F32)],
        compiler_params=params(),
        name="scan_outputs",
    )(x, bc, dt, cum, cumt, s0, loc0, tot, skip)


def halves(v):
    high = v.astype(BF16)
    return high, (v - high.astype(F32)).astype(BF16)


def dot_pairs(a, b, dims=((1,), (0,))):
    (ah, al), (bh, bl) = halves(a), halves(b)
    return dot(ah, bh, dims) + (dot(al, bh, dims) + dot(ah, bl, dims))


def dot_pair(a, b, dims=((1,), (0,))):
    high, low = halves(a)
    return dot(high, b, dims) + dot(low, b, dims)


def nt_exact(a, b):
    return lax.dot_general(a, b, (((1,), (1,)), ((), ())), precision=HIGH, preferred_element_type=F32)


class Chain:
    def __init__(self, place, came, sent, send, recv, backward):
        self.came, self.sent, self.send, self.recv = came, sent, send, recv
        self.gets, self.gives = place.has_left, place.has_right
        self.to = place.left if backward else place.right
        if backward:
            self.gets, self.gives = self.gives, self.gets
        self.behind = place.depth - 1 - place.z if backward else place.z

    def copy(self, g):
        return remote(self.sent.at[g], self.came.at[g], self.send.at[g], self.recv.at[g], self.to)

    def step(self, g, total, own):
        pl.when(self.gets)(lambda: self.copy(g).wait_recv())

        @pl.when(jnp.logical_not(self.gets))
        def _():
            self.came[g] = jnp.zeros(self.came.shape[1:], self.came.dtype)

        self.sent[g] = (total * self.came[g].astype(F32) + own).astype(BF16)
        pl.when(self.gives)(lambda: self.copy(g).start())

    def finish(self):
        groups = self.came.shape[0]

        def one(g, carry):
            self.copy(g).wait_send()
            return carry

        @pl.when(self.gives)
        def _():
            lax.fori_loop(0, groups, one, 0)


def scan_forward_kernel(
    depth, head_dim, groups,
    pc_ref, w_ref, b_ref, raw_ref, sb_ref, dl_ref, skip_ref, normed_ref, cot_ref, wi_src, wo_src,
    bc_ref, dt_ref, cum_ref, cumt_ref, mixed_ref, s0_ref, s1_ref, s2_ref, tot_ref, z_out, dno_out, wg_ref, wo_ref,
    bt_ref, cb_ref, x_ring, loc_ring, seg_ring, tot_ring, came, sent,
    z_ref, dno_ref, wg_buf, wo_buf, chain_send, chain_recv, own_sem, load_sem, out_sem, send, recv,
):
    step = pl.program_id(0)
    lag = depth - 1
    seqs = pc_ref.shape[0]
    seg = pc_ref.shape[1] - EDGE
    chunks = seg // CHUNK
    heads = GROUP // head_dim
    w, b = w_ref[...], b_ref[...]
    place = Place(depth)
    chain = Chain(place, came, sent, chain_send, chain_recv, False)
    wg_src = wi_src.at[:, pl.ds(0, z_ref.shape[1])]
    lanes = [
        Gather(place, wg_src, lambda z, y, x, c: wg_ref.at[y, x, c, z], "y", "x", send.at[0], recv.at[0]),
        Gather(place, wo_src, lambda z, y, x, c: wo_ref.at[y, x, c, z], "x", "y", send.at[1], recv.at[1]),
    ]
    mine = (place.own["y"], place.own["x"], place.own["c"], place.z)
    copies = [
        pltpu.make_async_copy(wg_src, wg_ref.at[mine], own_sem.at[0]),
        pltpu.make_async_copy(wo_src, wo_ref.at[mine], own_sem.at[1]),
    ]

    def waves(*steps):
        for name, k in steps:
            for lane in lanes:
                getattr(lane, name)(k)

    def acts_of(s):
        pre = causal_conv(pc_ref[s], w, b, seg)
        return pre * sigmoid(pre)

    @pl.when(step == 0)
    def _():
        place.meet()
        waves(("line", 0))
        for copy in copies:
            copy.start()
        row = lax.broadcasted_iota(jnp.int32, (CHUNK, CHUNK), 0)
        col = lax.broadcasted_iota(jnp.int32, (CHUNK, CHUNK), 1)
        tri = (col <= row).astype(F32)
        rate = -jnp.exp(dl_ref[...])
        for s in range(seqs):
            acts = acts_of(s)
            bc_ref[s * seg : (s + 1) * seg] = acts
            for c in range(chunks):
                q = s * chunks + c
                rows = slice(q * CHUNK, (q + 1) * CHUNK)
                b_proj = acts[c * CHUNK : (c + 1) * CHUNK, :LANES]
                c_proj = acts[c * CHUNK : (c + 1) * CHUNK, LANES:]
                bt_ref[q] = b_proj.T
                cb_ref[q] = nt_exact(c_proj, b_proj)
                dt = softplus(raw_ref[s, EDGE + c * CHUNK : EDGE + (c + 1) * CHUNK] + sb_ref[...])
                cum = LOG2E * jnp.dot(tri, dt * rate, precision=HIGH, preferred_element_type=F32)
                dt_ref[rows] = dt
                cum_ref[rows] = cum
                cumt_ref[:, rows] = cum.T

    @pl.when((step > 0) & (step <= groups))
    def _():
        g = step - 1
        at = lax.rem(g, lag + 1)
        first = g * heads
        cumg = lane_shift(cum_ref[...], first)
        dtg = lane_shift(dt_ref[...], first)
        for s in range(seqs):
            x = acts_of(s)
            x_ring[at, s * seg : (s + 1) * seg] = x
            state, total = None, None
            for c in range(chunks):
                q = s * chunks + c
                rows = slice(q * CHUNK, (q + 1) * CHUNK)
                ce = spread_all(cumg[rows], heads, head_dim)
                de = spread_all(dtg[rows], heads, head_dim)
                end = ce[CHUNK - 1 : CHUNK]
                uw = x[c * CHUNK : (c + 1) * CHUNK] * de * jnp.exp2(end - ce)
                loc = dot_pairs(bt_ref[q], uw)
                tot = jnp.exp2(end)
                tot_ring[at, q : q + 1] = tot
                if c == 0:
                    loc_ring[at, s] = loc
                    state, total = loc, tot
                else:
                    state, total = tot * state + loc, tot * total
            seg_ring[at, s] = state
            tot_ring[at, seqs * chunks + s : seqs * chunks + s + 1] = total

    handed = step - 1 - chain.behind

    @pl.when((handed >= 0) & (handed < groups))
    def _():
        at = lax.rem(handed, lag + 1)
        totals = tot_ring[at, seqs * chunks : seqs * chunks + seqs]
        chain.step(handed, totals[:, None, :], seg_ring[at])

    @pl.when(step > lag)
    def _():
        g = step - 1 - lag
        at = lax.rem(g, lag + 1)
        first = g * heads
        cumg = lane_shift(cum_ref[...], first)
        dtg = lane_shift(dt_ref[...], first)
        cumr = head_rows(cumt_ref, first)
        row = lax.broadcasted_iota(jnp.int32, (CHUNK, CHUNK), 0)
        col = lax.broadcasted_iota(jnp.int32, (CHUNK, CHUNK), 1)
        causal = col <= row
        skip = skip_ref[...]
        s0_ref[...] = came[g]
        s2_ref[...] = sent[g]
        tot_ref[...] = tot_ring[at]
        for s in range(seqs):
            start = came[g, s]
            for c in range(chunks):
                q = s * chunks + c
                rows = slice(q * CHUNK, (q + 1) * CHUNK)
                x = x_ring[at, rows]
                ce = spread_all(cumg[rows], heads, head_dim)
                de = spread_all(dtg[rows], heads, head_dim)
                ub = (x * de).astype(BF16)
                cb = cb_ref[q]
                parts = []
                for j in range(0, heads, 2):
                    mats = []
                    for h in (j, j + 1):
                        there = jnp.broadcast_to(cumg[rows, h : h + 1], (CHUNK, CHUNK))
                        here = cumr[h : h + 1, rows]
                        decay = jnp.exp2(jnp.where(causal, there - here, -jnp.inf))
                        mats.append((decay * cb).astype(BF16))
                    pair = ub[:, j * head_dim : (j + 2) * head_dim]
                    parts.append(dot(jnp.concatenate(mats, axis=1), block_diagonal(pair, head_dim)))
                y = jnp.concatenate(parts, axis=1)
                y = y + jnp.exp2(ce) * dot(bc_ref[rows, LANES:].astype(BF16), start)
                mixed_ref[rows] = y + skip * x
                if c == 0:
                    later = tot_ring[at, q : q + 1] * start.astype(F32) + loc_ring[at, s]
                    s1_ref[s] = later
                    start = later.astype(BF16)

    last = depth - 1
    order = [("from_first", 0), ("line", 1), ("from_second", 0), ("from_both", 0)]
    for k in range(1, depth):
        order.append(("from_first", k))
        if k < last:
            order.append(("line", k + 1))
        order += [("from_second", k), ("from_both", k)]
    early = (4, 6, 8, 9, 11, 13)
    for at, item in zip(early, order):
        pl.when(step == at)(lambda: waves(item))

    @pl.when(step == groups + lag)
    def _():
        waves(*(item for item in order[len(early) :] if item != ("from_both", last)))
        for copy in copies:
            copy.wait()
        groups_at = [place.flipped(*f) for f in ((), ("y",), ("x",), ("y", "x"))]

        def load(at):
            return [
                pltpu.make_async_copy(src.at[at["y"], at["x"]], buf, load_sem.at[n])
                for n, (src, buf) in enumerate(((wg_ref, wg_buf), (wo_ref, wo_buf)))
            ]

        def dno_copy(at):
            size = dno_ref.shape[1] // 4
            lanes_at = pl.ds(pl.multiple_of((2 * at["y"] + at["x"]) * size, LANES), size)
            return pltpu.make_async_copy(dno_ref.at[:, lanes_at], dno_out.at[:, lanes_at], out_sem.at[0])

        def core(stage):
            for k in range(depth):
                for lane in lanes:
                    lane.arrived(k, stage)

        def multiply(n, at):
            group = 2 * at["y"] + at["x"]
            rows = 2 * depth * wi_src.shape[0]
            here = pl.ds(pl.multiple_of(group * rows, LANES), rows)
            tile = 4 * LANES
            for copy in load(at):
                copy.wait()

            def one(i, carry):
                cols = pl.ds(pl.multiple_of(i * tile, tile), tile)
                block = jnp.concatenate(
                    [wg_buf[c, z, :, cols] for c in (0, 1) for z in range(depth)], axis=0
                )
                for s in range(seqs):
                    part = dot(normed_ref[s, EDGE:, here], block)
                    at_rows = slice(s * seg, (s + 1) * seg)
                    if n == 0:
                        z_ref[at_rows, cols] = part
                    else:
                        z_ref[at_rows, cols] += part
                return carry

            lax.fori_loop(0, z_ref.shape[1] // tile, one, 0)
            size = dno_ref.shape[1] // 8
            for c in (0, 1):
                block = jnp.concatenate([wo_buf[c, z] for z in range(depth)], axis=0)
                cols = pl.ds(pl.multiple_of((2 * group + c) * size, LANES), size)
                dno_ref[:, cols] = nt(cot_ref[...], block)

        def fetch(at):
            for copy in load(at):
                copy.start()

        core(3)
        fetch(groups_at[0])
        multiply(0, groups_at[0])
        core(4)
        core(5)
        fetch(groups_at[1])
        multiply(1, groups_at[1])
        fetch(groups_at[2])
        waves(("from_both", last))
        multiply(2, groups_at[2])
        for n in range(3):
            dno_copy(groups_at[n]).start()
            dno_copy(groups_at[n]).wait()
        core(6)
        fetch(groups_at[3])
        multiply(3, groups_at[3])
        z_copy = pltpu.make_async_copy(z_ref, z_out, out_sem.at[1])
        z_copy.start()
        dno_copy(groups_at[3]).start()
        for lane in lanes:
            lane.finish()
        chain.finish()
        dno_copy(groups_at[3]).wait()
        z_copy.wait()


def scan_forward(pc, w, b, sb, dl, skip, normed, cot, w_in, wo, inner, head_dim, depth):
    seqs, rows, cols = pc.shape
    tokens = seqs * (rows - EDGE)
    groups = inner // GROUP
    lag = depth - 1
    chunks = tokens // CHUNK
    shape, dma = jax.ShapeDtypeStruct, pltpu.SemaphoreType.DMA
    into = lambda i: jnp.where(i == 0, groups, jnp.minimum(i - 1, groups - 1))
    out = lambda i: jnp.maximum(i - 1 - lag, 0)
    states = pl.BlockSpec((seqs, LANES, GROUP), lambda i: (0, 0, out(i)))
    anywhere = pl.BlockSpec(memory_space=pl.ANY)
    sends, receives = Gather.sems(depth)
    slots = (2, 2, 2, depth)
    ring = lambda *dims: pltpu.VMEM((lag + 1,) + dims, F32)
    link = pltpu.VMEM((groups, seqs, LANES, GROUP), BF16)
    once = lambda v: pl.BlockSpec(v.shape, lambda i: (0,) * v.ndim, pipeline_mode=pl.Buffered(1))
    return pl.pallas_call(
        functools.partial(scan_forward_kernel, depth, head_dim, groups),
        grid=(groups + 1 + lag,),
        in_specs=[
            pl.BlockSpec((seqs, rows, GROUP), lambda i: (0, 0, into(i))),
            pl.BlockSpec((w.shape[0], GROUP), lambda i: (0, into(i))),
            pl.BlockSpec((1, GROUP), lambda i: (0, into(i))),
            pl.BlockSpec((seqs, rows, LANES), lambda i: (0, 0, cols // LANES - 1)),
            whole((1, LANES)),
            whole((1, LANES)),
            pl.BlockSpec((1, GROUP), lambda i: (0, out(i))),
            once(normed),
            once(cot),
            anywhere,
            anywhere,
        ],
        out_specs=[
            whole((tokens, GROUP)),
            whole((tokens, LANES)),
            whole((tokens, LANES)),
            whole((LANES, tokens)),
            pl.BlockSpec((tokens, GROUP), lambda i: (0, out(i))),
            states, states, states,
            pl.BlockSpec((8, GROUP), lambda i: (0, out(i))),
            anywhere,
            anywhere,
            anywhere,
            anywhere,
        ],
        out_shape=[
            shape((tokens, GROUP), F32),
            shape((tokens, LANES), F32),
            shape((tokens, LANES), F32),
            shape((LANES, tokens), F32),
            shape((tokens, inner), F32),
            shape((seqs, LANES, inner), BF16),
            shape((seqs, LANES, inner), F32),
            shape((seqs, LANES, inner), BF16),
            shape((8, inner), F32),
            shape((tokens, inner), F32),
            shape((tokens, inner), F32),
            shape(slots + (w_in.shape[0], inner), BF16),
            shape(slots + wo.shape, BF16),
        ],
        scratch_shapes=[
            pltpu.VMEM((chunks, LANES, CHUNK), F32),
            pltpu.VMEM((chunks, CHUNK, CHUNK), F32),
            ring(tokens, GROUP), ring(seqs, LANES, GROUP), ring(seqs, LANES, GROUP), ring(8, GROUP),
            link, link,
            pltpu.VMEM((tokens, inner), F32), pltpu.VMEM((tokens, inner), F32),
            pltpu.VMEM((2, depth, w_in.shape[0], inner), BF16), pltpu.VMEM((2, depth) + wo.shape, BF16),
            dma((groups,)), dma((groups,)), dma((2,)), dma((2,)), dma((2,)), dma((2, sends)), dma((2, receives)),
        ],
        compiler_params=pltpu.CompilerParams(
            dimension_semantics=("arbitrary",), collective_id=3, has_side_effects=True,
            vmem_limit_bytes=VMEM_LIMIT,
        ),
        name="scan_forward",
    )(pc, w, b, pc, sb, dl, skip, normed, cot, w_in, wo)


def mid_kernel(
    z_ref, dno_ref, mixed_ref, wo_ref, gain_ref, in_ref, not_ref, out_ref, dm_ref, dz_ref, gg_ref, acc_ref,
):
    step = pl.program_id(0)
    inner = mixed_ref.shape[1]
    tiles, tile = not_ref.shape[0], not_ref.shape[1]

    @pl.when(step == 0)
    def _():
        gg_ref[...] = jnp.zeros_like(gg_ref)

    def lanes_of(i):
        return pl.ds(pl.multiple_of(i * tile, tile), tile)

    def fold(v):
        total = v[:, :LANES]
        for k in range(LANES, tile, LANES):
            total = total + v[:, k : k + LANES]
        return total

    def one(i, sums):
        sq, hg = sums
        at = lanes_of(i)
        z = z_ref[:, at]
        g = mixed_ref[:, at] * z * sigmoid(z)
        return sq + fold(g * g), hg + fold(dno_ref[:, at] * gain_ref[:, at] * g)

    zero = jnp.zeros((mixed_ref.shape[0], LANES), F32)
    sq, hg = lax.fori_loop(0, tiles, one, (zero, zero))
    scale = lax.rsqrt(jnp.sum(sq, axis=1, keepdims=True) / inner + EPS)
    pull = scale * scale * scale * (jnp.sum(hg, axis=1, keepdims=True) / inner)
    acc_ref[...] = in_ref[...].astype(F32)

    def two(i, carry):
        at = lanes_of(i)
        z, mixed, dno, gain = z_ref[:, at], mixed_ref[:, at], dno_ref[:, at], gain_ref[:, at]
        sig = sigmoid(z)
        act = z * sig
        g = mixed * act
        gs = g * scale
        no = gs * gain
        not_ref[i] = no.T.astype(BF16)
        acc_ref[...] += dot(no.astype(BF16), wo_ref[at, :])
        gg_ref[:, at] += jnp.sum(dno * gs, axis=0, keepdims=True)
        dg = scale * (dno * gain) - g * pull
        dm_ref[:, at] = dg * act
        dz_ref[:, at] = (dg * mixed * (sig * (1.0 + z * (1.0 - sig)))).astype(BF16)
        return carry

    lax.fori_loop(0, tiles, two, 0)
    out_ref[...] = acc_ref[...].astype(BF16)


def mid(z, dno, mixed, wo, gain, inputs, tiles):
    tokens, inner = mixed.shape
    width = inputs.shape[1]
    tile = inner // tiles
    narrow = pl.BlockSpec((CHUNK, width), lambda i: (i, 0))
    wide = pl.BlockSpec((CHUNK, inner), lambda i: (i, 0))
    once = lambda v: pl.BlockSpec(v.shape, lambda i: (0,) * v.ndim, pipeline_mode=pl.Buffered(1))
    return pl.pallas_call(
        mid_kernel,
        grid=(tokens // CHUNK,),
        in_specs=[wide, wide, wide, once(wo), whole((1, inner)), narrow],
        out_specs=[
            pl.BlockSpec((tiles, tile, CHUNK), lambda i: (0, 0, i)), narrow, wide, wide,
            whole((1, inner)),
        ],
        out_shape=[
            jax.ShapeDtypeStruct((tiles, tile, tokens), BF16),
            jax.ShapeDtypeStruct((tokens, width), BF16),
            jax.ShapeDtypeStruct((tokens, inner), F32),
            jax.ShapeDtypeStruct((tokens, inner), BF16),
            jax.ShapeDtypeStruct((1, inner), F32),
        ],
        scratch_shapes=[pltpu.VMEM((CHUNK, width), F32)],
        compiler_params=params(),
        name="gate_norm_project",
    )(z, dno, mixed, wo, gain, inputs)


def bwd_a_kernel(head_dim, seqs, dm_ref, bc_ref, cum_ref, tot_ref, seg_ref, ct_ref):
    step = pl.program_id(0)
    chunks = dm_ref.shape[0] // CHUNK // seqs
    heads = GROUP // head_dim

    @pl.when(step == 0)
    def _():
        for q in range(seqs * chunks):
            ct_ref[q] = bc_ref[q * CHUNK : (q + 1) * CHUNK, LANES:].T.astype(BF16)

    cumg = lane_shift(cum_ref[...], step * heads)
    for s in range(seqs):
        state = None
        for c in range(chunks - 1, -1, -1):
            q = s * chunks + c
            rows = slice(q * CHUNK, (q + 1) * CHUNK)
            ey = jnp.exp2(spread_all(cumg[rows], heads, head_dim)) * dm_ref[rows]
            loc = dot(ct_ref[q], ey.astype(BF16))
            state = loc if state is None else tot_ref[q : q + 1] * state + loc
        seg_ref[s] = state.astype(BF16)


def bwd_a(dm, bc, cum, tot, seqs, head_dim):
    tokens, inner = dm.shape
    return pl.pallas_call(
        functools.partial(bwd_a_kernel, head_dim, seqs),
        grid=(inner // GROUP,),
        in_specs=[
            pl.BlockSpec((tokens, GROUP), lambda i: (0, i)), whole(bc.shape), whole(cum.shape),
            pl.BlockSpec((8, GROUP), lambda i: (0, i)),
        ],
        out_specs=pl.BlockSpec((seqs, LANES, GROUP), lambda i: (0, 0, i)),
        out_shape=jax.ShapeDtypeStruct((seqs, LANES, inner), BF16),
        scratch_shapes=[pltpu.VMEM((tokens // CHUNK, LANES, CHUNK), BF16)],
        compiler_params=params(),
        name="adjoint_states",
    )(dm, bc, cum, tot)


def bwd_b_kernel(
    head_dim, groups, pc_ref, w_ref, b_ref, raw_ref, sb_ref, dl_ref, bc_ref, dt_ref, cum_ref, cumt_ref,
    dm_ref, mixed_ref, s0_ref, s1_ref, s2_ref, g_ref, tot_ref, skip_ref,
    dc_ref, tail_ref, edge_ref, gw_ref, gb_ref, gskip_ref, draw_ref, hsum_ref,
    cbt_ref, dcbt_ref, db_acc, dc_acc, r1_ref, r2_ref, dtot_ref,
):
    step = pl.program_id(0)
    seqs = pc_ref.shape[0]
    seg = pc_ref.shape[1] - EDGE
    chunks = seg // CHUNK
    heads = GROUP // head_dim
    w, b = w_ref[...], b_ref[...]
    taps = w.shape[0]

    @pl.when(step == 0)
    def _():
        for q in range(seqs * chunks):
            rows = slice(q * CHUNK, (q + 1) * CHUNK)
            cbt_ref[q] = nt(bc_ref[rows, :LANES].astype(BF16), bc_ref[rows, LANES:].astype(BF16))
        dcbt_ref[...] = jnp.zeros_like(dcbt_ref)
        db_acc[...] = jnp.zeros_like(db_acc)
        dc_acc[...] = jnp.zeros_like(dc_acc)
        r1_ref[...] = jnp.zeros_like(r1_ref)
        r2_ref[...] = jnp.zeros_like(r2_ref)
        dtot_ref[...] = jnp.zeros_like(dtot_ref)

    def conv_back(s, ext, pre, sig, d_act):
        d_pre = d_act * (sig * (1.0 + pre * (1.0 - sig)))
        zero = jnp.zeros((EDGE, d_pre.shape[1]), F32)
        padded = jnp.concatenate([zero, d_pre, zero], axis=0)
        total = None
        for k in range(taps):
            at = taps - 1 - k
            term = w[k : k + 1] * padded[at : at + seg + EDGE]
            total = term if total is None else total + term
        edge_ref[s] = total[:EDGE]
        dc_ref[s * seg : (s + 1) * seg] = total[EDGE:].astype(BF16)
        tail_ref[s] = total[seg:]
        for k in range(taps):
            at = EDGE - (taps - 1) + k
            grad = jnp.sum(ext[at : at + seg] * d_pre, axis=0, keepdims=True)
            gw_ref[k : k + 1] = grad if s == 0 else gw_ref[k : k + 1] + grad
        grad = jnp.sum(d_pre, axis=0, keepdims=True)
        gb_ref[...] = grad if s == 0 else gb_ref[...] + grad

    def by_head(value, pick):
        high = value.astype(BF16)
        return dot(high, pick) + dot((value - high.astype(F32)).astype(BF16), pick)

    @pl.when(step < groups)
    def _():
        first = step * heads
        cumg = lane_shift(cum_ref[...], first)
        dtg = lane_shift(dt_ref[...], first)
        cumr = head_rows(cumt_ref, first)
        row = lax.broadcasted_iota(jnp.int32, (CHUNK, CHUNK), 0)
        col = lax.broadcasted_iota(jnp.int32, (CHUNK, CHUNK), 1)
        causal = row <= col
        lane = lax.broadcasted_iota(jnp.int32, (GROUP, LANES), 0)
        head = lax.broadcasted_iota(jnp.int32, (GROUP, LANES), 1)
        pick = (head == first + lane // head_dim).astype(BF16)
        skip = skip_ref[...]
        grad_skip = None
        for s in range(seqs):
            ext = pc_ref[s]
            pre = causal_conv(ext, w, b, seg)
            sig = sigmoid(pre)
            acts = pre * sig
            adj = g_ref[s].astype(F32)
            d_acts = [None] * chunks
            for c in range(chunks - 1, -1, -1):
                q = s * chunks + c
                rows = slice(q * CHUNK, (q + 1) * CHUNK)
                x = acts[c * CHUNK : (c + 1) * CHUNK]
                dy = dm_ref[rows]
                ce = spread_all(cumg[rows], heads, head_dim)
                de = spread_all(dtg[rows], heads, head_dim)
                weight = jnp.exp2(ce[CHUNK - 1 : CHUNK] - ce)
                u = x * de
                ub = u.astype(BF16)
                dyb = dy.astype(BF16)
                cbt = cbt_ref[q]
                parts = []
                dcbt = dcbt_ref[q]
                for j in range(0, heads, 2):
                    lanes = slice(j * head_dim, (j + 2) * head_dim)
                    dy_block = block_diagonal(dyb[:, lanes], head_dim)
                    dm = nt(ub[:, lanes], dy_block)
                    mats = []
                    for k, h in enumerate((j, j + 1)):
                        here = jnp.broadcast_to(cumg[rows, h : h + 1], (CHUNK, CHUNK))
                        there = cumr[h : h + 1, rows]
                        decay = jnp.exp2(jnp.where(causal, there - here, -jnp.inf))
                        mats.append((decay * cbt).astype(BF16))
                        dcbt = dcbt + decay * dm[:, k * CHUNK : (k + 1) * CHUNK]
                    parts.append(dot(jnp.concatenate(mats, axis=1), dy_block))
                dcbt_ref[q] = dcbt
                start = s0_ref[s] if c == 0 else s1_ref[s]
                end = s2_ref[s] if c == chunks - 1 else s1_ref[s]
                adj_b = adj.astype(BF16)
                bb = bc_ref[rows, :LANES].astype(BF16)
                cb = bc_ref[rows, LANES:].astype(BF16)
                ey = (jnp.exp2(ce) * dy).astype(BF16)
                du = jnp.concatenate(parts, axis=1) + weight * dot(bb, adj_b)
                db_acc[rows] += nt((u * weight).astype(BF16), adj_b)
                dc_acc[rows] += nt(ey, start)
                r1_ref[rows] += by_head(dyb.astype(F32) * (mixed_ref[rows] - skip * x), pick)
                r2_ref[rows] += by_head(x * du, pick)
                dtot_ref[q : q + 1] += by_head(
                    jnp.sum(adj * end.astype(F32), axis=0, keepdims=True), pick
                )
                grad = jnp.sum(dy * x, axis=0, keepdims=True)
                grad_skip = grad if grad_skip is None else grad_skip + grad
                d_acts[c] = du * de + skip * dy
                if c > 0:
                    adj = tot_ref[q : q + 1] * adj + dot(cb, ey, ((0,), (0,)))
            conv_back(s, ext, pre, sig, jnp.concatenate(d_acts, axis=0))
        gskip_ref[...] = grad_skip

    @pl.when(step == groups)
    def _():
        row = lax.broadcasted_iota(jnp.int32, (CHUNK, CHUNK), 0)
        col = lax.broadcasted_iota(jnp.int32, (CHUNK, CHUNK), 1)
        later = (row <= col).astype(F32)
        rate = -jnp.exp(dl_ref[...])
        sum_raw = jnp.zeros((1, LANES), F32)
        sum_log = jnp.zeros((1, LANES), F32)
        for s in range(seqs):
            ext = pc_ref[s]
            pre = causal_conv(ext, w, b, seg)
            sig = sigmoid(pre)
            parts = []
            for c in range(chunks):
                q = s * chunks + c
                rows = slice(q * CHUNK, (q + 1) * CHUNK)
                dcbt = dcbt_ref[q]
                bb = bc_ref[rows, :LANES].astype(BF16)
                cb = bc_ref[rows, LANES:].astype(BF16)
                d_b = db_acc[rows] + dot(dcbt.astype(BF16), cb)
                d_c = dc_acc[rows] + dot(dcbt.T.astype(BF16), bb)
                parts.append(jnp.concatenate([d_b, d_c], axis=1))
                dt = dt_ref[rows]
                r2 = r2_ref[rows]
                d_log = jnp.dot(
                    later, r1_ref[rows] - dt * r2, precision=HIGH, preferred_element_type=F32
                )
                d_log = d_log + dtot_ref[q : q + 1]
                raw = raw_ref[s, EDGE + c * CHUNK : EDGE + (c + 1) * CHUNK] + sb_ref[...]
                d_raw = (r2 + rate * d_log) * sigmoid(raw)
                draw_ref[rows] = d_raw
                sum_raw = sum_raw + jnp.sum(d_raw, axis=0, keepdims=True)
                sum_log = sum_log + jnp.sum(d_log * dt, axis=0, keepdims=True) * rate
            conv_back(s, ext, pre, sig, jnp.concatenate(parts, axis=0))
        hsum_ref[0:1] = sum_raw
        hsum_ref[1:2] = sum_log


def bwd_b(pc, w, b, sb, dl, bc, dt, cum, cumt, dm, mixed, s0, s1, s2, g, tot, skip, head_dim):
    seqs, rows, cols = pc.shape
    tokens, inner = dm.shape
    groups = inner // GROUP
    taps, channels = w.shape
    wide = pl.BlockSpec((tokens, GROUP), lambda i: (0, jnp.minimum(i, groups - 1)))
    states = pl.BlockSpec((seqs, LANES, GROUP), lambda i: (0, 0, jnp.minimum(i, groups - 1)))
    line = lambda n: pl.BlockSpec((n, GROUP), lambda i: (0, jnp.minimum(i, groups - 1)))
    conv = lambda n: pl.BlockSpec((n, GROUP), lambda i: (0, i))
    ends = pl.BlockSpec((seqs, EDGE, GROUP), lambda i: (0, 0, i))
    chunks = tokens // CHUNK
    shape = jax.ShapeDtypeStruct
    return pl.pallas_call(
        functools.partial(bwd_b_kernel, head_dim, groups),
        grid=(groups + 1,),
        in_specs=[
            pl.BlockSpec((seqs, rows, GROUP), lambda i: (0, 0, i)),
            conv(taps),
            conv(1),
            pl.BlockSpec((seqs, rows, LANES), lambda i: (0, 0, cols // LANES - 1)),
            whole((1, LANES)), whole((1, LANES)),
            whole(bc.shape), whole(dt.shape), whole(cum.shape), whole(cumt.shape),
            wide, wide, states, states, states, states, line(8), line(1),
        ],
        out_specs=[
            conv(tokens), ends, ends, conv(taps), conv(1), line(1),
            whole((tokens, LANES)), whole((2, LANES)),
        ],
        out_shape=[
            shape((tokens, channels), BF16),
            shape((seqs, EDGE, channels), F32),
            shape((seqs, EDGE, channels), F32),
            shape((taps, channels), F32),
            shape((1, channels), F32),
            shape((1, inner), F32),
            shape((tokens, LANES), F32),
            shape((2, LANES), F32),
        ],
        scratch_shapes=[
            pltpu.VMEM((chunks, CHUNK, CHUNK), F32),
            pltpu.VMEM((chunks, CHUNK, CHUNK), F32),
            pltpu.VMEM((tokens, LANES), F32),
            pltpu.VMEM((tokens, LANES), F32),
            pltpu.VMEM((tokens, LANES), F32),
            pltpu.VMEM((tokens, LANES), F32),
            pltpu.VMEM((8, LANES), F32),
        ],
        compiler_params=params(),
        name="scan_backward",
    )(pc, w, b, pc, sb, dl, bc, dt, cum, cumt, dm, mixed, s0, s1, s2, g, tot, skip)


def pair_copies(place, lhs, rhs, send, recv):
    other = 1 - place.own["c"]
    parts = [(src.at[2 * g + other], dst.at[g]) for src, dst in lhs for g in range(4)] + list(rhs)
    return [
        remote(src, dst, send.at[n], recv.at[n], place.to["c"]) for n, (src, dst) in enumerate(parts)
    ]


def scan_backward_kernel(
    depth, head_dim, groups,
    pc_ref, w_ref, b_ref, raw_ref, sb_ref, dl_ref, bc_ref, dt_ref, cum_ref, cumt_ref,
    dma_ref, dm_ref, mixed_ref, s0_ref, s1_ref, s2_ref, tot_ref, skip_ref,
    nt_src, dz_src, no_src, cot_src,
    dc_out, gw_ref, gb_ref, gskip_ref, hsum_ref, a_out, b_out, nt_out,
    cbt_ref, ct_ref, dcbt_ref, db_acc, dc_acc, r1_ref, r2_ref, dtot_ref,
    dc_ref, tail_ref, edge_ref, edge_came, seg_ring, tot_ring, came, sent,
    nt_pair, dz_pair, no_pair, cot_pair,
    chain_send, chain_recv, edge_send, edge_recv, pair_send, pair_recv, out_sem, send, recv, *bufs,
):
    step = pl.program_id(0)
    lag = depth - 1
    seqs = pc_ref.shape[0]
    seg = pc_ref.shape[1] - EDGE
    chunks = seg // CHUNK
    heads = GROUP // head_dim
    w, b = w_ref[...], b_ref[...]
    taps = w.shape[0]
    channels = tail_ref.shape[2]
    place = Place(depth)
    chain = Chain(place, came, sent, chain_send, chain_recv, True)
    pairs = pair_copies(
        place, ((nt_src, nt_pair), (no_src, no_pair)), ((dz_src, dz_pair), (cot_src, cot_pair)),
        pair_send, pair_recv,
    )
    def half(ref, n):
        size = ref.shape[1] // 2
        return ref.at[:, pl.ds(n * size, size)]

    lanes = []
    for n in (0, 1):
        lanes += [
            Scatter(place, nt_src, nt_pair, half(dz_src, n), half(dz_pair, n), "y", "x",
                    bufs[14 * n : 14 * n + 7], send.at[2 * n], recv.at[2 * n]),
            Scatter(place, no_src, no_pair, half(cot_src, n), half(cot_pair, n), "x", "y",
                    bufs[14 * n + 7 : 14 * n + 14], send.at[2 * n + 1], recv.at[2 * n + 1]),
        ]
    edges = [
        remote(edge_ref.at[:, :, cols], edge_came.at[:, :, cols], edge_send.at[n], edge_recv.at[n], place.left)
        for n, cols in enumerate((pl.ds(0, channels - GROUP), pl.ds(channels - GROUP, GROUP)))
    ]
    outs = [
        pltpu.make_async_copy(src, dst, out_sem.at[n])
        for n, (src, dst) in enumerate(((nt_pair, nt_out), (dc_ref, dc_out)))
    ]

    def run(first, name, *rest):
        for lane in lanes[2 * first : 2 * first + 2]:
            getattr(lane, name)(*rest)

    def at_step(n, *what):
        pl.when(step == n)(lambda: run(*what))

    @pl.when(step == 0)
    def _():
        place.meet()
        for copy in pairs:
            copy.start()
        for q in range(seqs * chunks):
            rows = slice(q * CHUNK, (q + 1) * CHUNK)
            b_proj, c_proj = bc_ref[rows, :LANES], bc_ref[rows, LANES:]
            cbt_ref[q] = nt_exact(b_proj, c_proj)
            ct_ref[q] = c_proj.T
        dcbt_ref[...] = jnp.zeros_like(dcbt_ref)
        db_acc[...] = jnp.zeros_like(db_acc)
        dc_acc[...] = jnp.zeros_like(dc_acc)
        r1_ref[...] = jnp.zeros_like(r1_ref)
        r2_ref[...] = jnp.zeros_like(r2_ref)
        dtot_ref[...] = jnp.zeros_like(dtot_ref)

    @pl.when(step < groups)
    def _():
        at = lax.rem(step, lag + 1)
        cumg = lane_shift(cum_ref[...], step * heads)
        tot_ring[at] = tot_ref[...]
        for s in range(seqs):
            state = None
            for c in range(chunks - 1, -1, -1):
                q = s * chunks + c
                rows = slice(q * CHUNK, (q + 1) * CHUNK)
                ey = jnp.exp2(spread_all(cumg[rows], heads, head_dim)) * dma_ref[rows]
                loc = dot_pairs(ct_ref[q], ey)
                state = loc if state is None else tot_ref[q : q + 1] * state + loc
            seg_ring[at, s] = state

    handed = step - chain.behind

    @pl.when((handed >= 0) & (handed < groups))
    def _():
        at = lax.rem(handed, lag + 1)
        totals = tot_ring[at, seqs * chunks : seqs * chunks + seqs]
        chain.step(handed, totals[:, None, :], seg_ring[at])

    @pl.when(step == lag)
    def _():
        for copy in pairs:
            copy.wait_recv()
        outs[0].start()

    at_step(lag, 0, "send_second", 0)
    at_step(lag + 1, 0, "send_second", 1)
    at_step(lag + 4, 0, "send_first")
    at_step(lag + 5, 1, "send_second", 0)
    at_step(lag + 6, 1, "send_second", 1)
    at_step(lag + 7, 0, "hold")
    for n, k in enumerate(lanes[0].waves()):
        at_step(lag + 9 + n, 0, "step", k)
    at_step(lag + 11, 1, "send_first")

    def conv_back(s, ext, pre, sig, d_act, at):
        lanes_at = pl.ds(pl.multiple_of(at * GROUP, GROUP), GROUP)
        d_pre = d_act * (sig * (1.0 + pre * (1.0 - sig)))
        zero = jnp.zeros((EDGE, d_pre.shape[1]), F32)
        padded = jnp.concatenate([zero, d_pre, zero], axis=0)
        total = None
        for k in range(taps):
            start = taps - 1 - k
            term = w[k : k + 1] * padded[start : start + seg + EDGE]
            total = term if total is None else total + term
        edge_ref[s, :, lanes_at] = total[:EDGE].astype(BF16)
        dc_ref[s * seg : (s + 1) * seg, lanes_at] = total[EDGE:].astype(BF16)
        tail_ref[s, :, lanes_at] = total[seg:]
        for k in range(taps):
            start = EDGE - (taps - 1) + k
            grad = jnp.sum(ext[start : start + seg] * d_pre, axis=0, keepdims=True)
            gw_ref[k : k + 1] = grad if s == 0 else gw_ref[k : k + 1] + grad
        grad = jnp.sum(d_pre, axis=0, keepdims=True)
        gb_ref[...] = grad if s == 0 else gb_ref[...] + grad

    def by_head(value, pick):
        high = value.astype(BF16)
        return dot(high, pick) + dot((value - high.astype(F32)).astype(BF16), pick)

    @pl.when((step >= lag) & (step < lag + groups))
    def _():
        g = step - lag
        at = lax.rem(g, lag + 1)
        first = g * heads
        cumg = lane_shift(cum_ref[...], first)
        dtg = lane_shift(dt_ref[...], first)
        cumr = head_rows(cumt_ref, first)
        row = lax.broadcasted_iota(jnp.int32, (CHUNK, CHUNK), 0)
        col = lax.broadcasted_iota(jnp.int32, (CHUNK, CHUNK), 1)
        causal = row <= col
        lane = lax.broadcasted_iota(jnp.int32, (GROUP, LANES), 0)
        head = lax.broadcasted_iota(jnp.int32, (GROUP, LANES), 1)
        pick = (head == first + lane // head_dim).astype(BF16)
        skip = skip_ref[...]
        grad_skip = None
        for s in range(seqs):
            ext = pc_ref[s]
            pre = causal_conv(ext, w, b, seg)
            sig = sigmoid(pre)
            acts = pre * sig
            adj = came[g, s].astype(F32)
            d_acts = [None] * chunks
            for c in range(chunks - 1, -1, -1):
                q = s * chunks + c
                rows = slice(q * CHUNK, (q + 1) * CHUNK)
                x = acts[c * CHUNK : (c + 1) * CHUNK]
                dy = dm_ref[rows]
                ce = spread_all(cumg[rows], heads, head_dim)
                de = spread_all(dtg[rows], heads, head_dim)
                weight = jnp.exp2(ce[CHUNK - 1 : CHUNK] - ce)
                u = x * de
                ub = u.astype(BF16)
                dyb = dy.astype(BF16)
                cbt = cbt_ref[q]
                parts = []
                dcbt = dcbt_ref[q]
                for j in range(0, heads, 2):
                    two = slice(j * head_dim, (j + 2) * head_dim)
                    dy_block = block_diagonal(dyb[:, two], head_dim)
                    dm = nt(ub[:, two], dy_block)
                    mats = []
                    for k, h in enumerate((j, j + 1)):
                        here = jnp.broadcast_to(cumg[rows, h : h + 1], (CHUNK, CHUNK))
                        there = cumr[h : h + 1, rows]
                        decay = jnp.exp2(jnp.where(causal, there - here, -jnp.inf))
                        mats.append((decay * cbt).astype(BF16))
                        dcbt = dcbt + decay * dm[:, k * CHUNK : (k + 1) * CHUNK]
                    parts.append(dot(jnp.concatenate(mats, axis=1), dy_block))
                dcbt_ref[q] = dcbt
                start = s0_ref[s] if c == 0 else s1_ref[s]
                end = s2_ref[s] if c == chunks - 1 else s1_ref[s]
                adj_b = adj.astype(BF16)
                bb = bc_ref[rows, :LANES].astype(BF16)
                ey = jnp.exp2(ce) * dy
                du = jnp.concatenate(parts, axis=1) + weight * dot(bb, adj_b)
                uw = u * weight
                across = ((1,), (1,))
                db_acc[rows] += dot_pair(uw, adj_b, across) if c == chunks - 1 else dot_pairs(uw, adj, across)
                dc_acc[rows] += dot_pair(ey, start, across) if c == 0 else dot_pairs(ey, start, across)
                r1_ref[rows] += by_head(dyb.astype(F32) * (mixed_ref[rows] - skip * x), pick)
                r2_ref[rows] += by_head(x * du, pick)
                dtot_ref[q : q + 1] += by_head(
                    jnp.sum(adj * end.astype(F32), axis=0, keepdims=True), pick
                )
                grad = jnp.sum(dy * x, axis=0, keepdims=True)
                grad_skip = grad if grad_skip is None else grad_skip + grad
                d_acts[c] = du * de + skip * dy
                if c > 0:
                    adj = tot_ring[at, q : q + 1] * adj + dot_pairs(ct_ref[q], ey)
            conv_back(s, ext, pre, sig, jnp.concatenate(d_acts, axis=0), g)
        gskip_ref[...] = grad_skip

    @pl.when(step == lag + groups)
    def _():
        pl.when(place.has_left)(edges[0].start)
        row = lax.broadcasted_iota(jnp.int32, (CHUNK, CHUNK), 0)
        col = lax.broadcasted_iota(jnp.int32, (CHUNK, CHUNK), 1)
        later = (row <= col).astype(F32)
        rate = -jnp.exp(dl_ref[...])
        sum_raw = jnp.zeros((1, LANES), F32)
        sum_log = jnp.zeros((1, LANES), F32)
        for s in range(seqs):
            ext = pc_ref[s]
            pre = causal_conv(ext, w, b, seg)
            sig = sigmoid(pre)
            parts = []
            for c in range(chunks):
                q = s * chunks + c
                rows = slice(q * CHUNK, (q + 1) * CHUNK)
                dcbt = dcbt_ref[q]
                d_b = db_acc[rows] + dot_pairs(dcbt, bc_ref[rows, LANES:])
                d_c = dc_acc[rows] + dot_pairs(dcbt.T, bc_ref[rows, :LANES])
                parts.append(jnp.concatenate([d_b, d_c], axis=1))
                dt = dt_ref[rows]
                r2 = r2_ref[rows]
                d_log = jnp.dot(
                    later, r1_ref[rows] - dt * r2, precision=HIGH, preferred_element_type=F32
                )
                d_log = d_log + dtot_ref[q : q + 1]
                raw = raw_ref[s, EDGE + c * CHUNK : EDGE + (c + 1) * CHUNK] + sb_ref[...]
                d_raw = (r2 + rate * d_log) * sigmoid(raw)
                dc_ref[rows, channels:] = d_raw.astype(BF16)
                sum_raw = sum_raw + jnp.sum(d_raw, axis=0, keepdims=True)
                sum_log = sum_log + jnp.sum(d_log * dt, axis=0, keepdims=True) * rate
            conv_back(s, ext, pre, sig, jnp.concatenate(parts, axis=0), groups)
        hsum_ref[0:1] = sum_raw
        hsum_ref[1:2] = sum_log
        pl.when(place.has_left)(edges[1].start)

        @pl.when(place.has_right)
        def _():
            for copy in edges:
                copy.wait_recv()
            for s in range(seqs):
                fixed = tail_ref[s] + edge_came[s].astype(F32)
                dc_ref[(s + 1) * seg - EDGE : (s + 1) * seg, :channels] = fixed.astype(BF16)

        outs[1].start()
        run(1, "hold")
        for k in lanes[0].waves():
            run(1, "step", k)
        for n, out in enumerate((a_out, b_out)):
            size = out.shape[1] // 2
            out[:, :size] = lanes[n].keep[place.z]
            out[:, size:] = lanes[2 + n].keep[place.z]
        for lane in lanes:
            lane.finish()
        chain.finish()

        @pl.when(place.has_left)
        def _():
            for copy in edges:
                copy.wait_send()

        for copy in pairs:
            copy.wait_send()
        for copy in outs:
            copy.wait()


def scan_backward(
    pc, w, b, sb, dl, bc, dt, cum, cumt, dm, mixed, s0, s1, s2, tot, skip, normed_t, dz, turned, cot,
    head_dim, depth,
):
    seqs, rows, cols = pc.shape
    tokens, inner = dm.shape
    groups = inner // GROUP
    lag = depth - 1
    taps, channels = w.shape
    out = lambda i: jnp.maximum(i - lag, 0)
    inside = lambda i: jnp.minimum(out(i), groups - 1)
    wide = pl.BlockSpec((tokens, GROUP), lambda i: (0, inside(i)))
    states = pl.BlockSpec((seqs, LANES, GROUP), lambda i: (0, 0, inside(i)))
    line = lambda n: pl.BlockSpec((n, GROUP), lambda i: (0, inside(i)))
    conv = lambda n: pl.BlockSpec((n, GROUP), lambda i: (0, out(i)))
    ahead = lambda n: pl.BlockSpec((n, GROUP), lambda i: (0, jnp.minimum(i, groups - 1)))
    once = lambda v: pl.BlockSpec(v.shape, lambda i: (0,) * v.ndim, pipeline_mode=pl.Buffered(1))
    anywhere = pl.BlockSpec(memory_space=pl.ANY)
    chunks = tokens // CHUNK
    shape, dma = jax.ShapeDtypeStruct, pltpu.SemaphoreType.DMA
    a_rows, b_rows = normed_t.shape[1] // depth, turned.shape[1] // depth
    a_cols, b_cols = dz.shape[1] // 2, cot.shape[1] // 2
    half = lambda v: (4,) + v.shape[1:]
    sends, receives = Scatter.sems(depth)
    ring = lambda *dims: pltpu.VMEM((lag + 1,) + dims, F32)
    link = pltpu.VMEM((groups, seqs, LANES, GROUP), BF16)
    square = pltpu.VMEM((chunks, CHUNK, CHUNK), F32)
    column = pltpu.VMEM((tokens, LANES), F32)
    return pl.pallas_call(
        functools.partial(scan_backward_kernel, depth, head_dim, groups),
        grid=(groups + 1 + lag,),
        in_specs=[
            pl.BlockSpec((seqs, rows, GROUP), lambda i: (0, 0, out(i))),
            conv(taps),
            conv(1),
            pl.BlockSpec((seqs, rows, LANES), lambda i: (0, 0, cols // LANES - 1)),
            whole((1, LANES)), whole((1, LANES)),
            whole(bc.shape), whole(dt.shape), whole(cum.shape), whole(cumt.shape),
            ahead(tokens), wide, wide, states, states, states, ahead(8), line(1),
            once(normed_t), once(dz), once(turned), once(cot),
        ],
        out_specs=[
            anywhere, conv(taps), conv(1), line(1), whole((2, LANES)),
            whole((a_rows, 2 * a_cols)), whole((b_rows, 2 * b_cols)), anywhere,
        ],
        out_shape=[
            shape((tokens, cols), BF16),
            shape((taps, channels), F32),
            shape((1, channels), F32),
            shape((1, inner), F32),
            shape((2, LANES), F32),
            shape((a_rows, 2 * a_cols), F32),
            shape((b_rows, 2 * b_cols), F32),
            shape(half(normed_t), BF16),
        ],
        scratch_shapes=[
            square, pltpu.VMEM((chunks, LANES, CHUNK), F32), square, column, column, column, column,
            pltpu.VMEM((8, LANES), F32),
            pltpu.VMEM((tokens, cols), BF16),
            pltpu.VMEM((seqs, EDGE, channels), F32),
            pltpu.VMEM((seqs, EDGE, channels), BF16),
            pltpu.VMEM((seqs, EDGE, channels), BF16),
            ring(seqs, LANES, GROUP), ring(8, GROUP), link, link,
            pltpu.VMEM(half(normed_t), BF16), pltpu.VMEM(dz.shape, BF16),
            pltpu.VMEM(half(turned), BF16), pltpu.VMEM(cot.shape, BF16),
            dma((groups,)), dma((groups,)), dma((2,)), dma((2,)), dma((10,)), dma((10,)), dma((2,)),
            dma((4, sends)), dma((4, receives)),
            *(2 * (Scatter.scratch(depth, a_rows, a_cols) + Scatter.scratch(depth, b_rows, b_cols))),
        ],
        compiler_params=pltpu.CompilerParams(
            dimension_semantics=("arbitrary",), collective_id=1, has_side_effects=True,
            vmem_limit_bytes=VMEM_LIMIT,
        ),
        name="scan_backward_sums",
    )(
        pc, w, b, pc, sb, dl, bc, dt, cum, cumt, dm, dm, mixed, s0, s1, s2, tot, skip,
        normed_t, dz, turned, cot,
    )


def scatter_last_kernel(
    depth, splits, nt_ref, nt_pair, dc_ref, dz_ref, wg_src, wc_src, x_ref, cot_ref, gain_ref, small_in,
    c_out, gi_ref, small_out, *refs,
):
    place = Place(depth)
    place.meet()
    pieces = len(splits) - 1
    dc_pairs, refs = refs[:pieces], refs[pieces:]
    small_src, tiles_ref, tile_sem, pair_send, pair_recv, send, recv, small_send, small_recv = refs[:9]
    refs = refs[9:]
    cuts = [dc_ref.at[:, pl.ds(lo, hi - lo)] for lo, hi in zip(splits, splits[1:])]
    copies = pair_copies(place, (), tuple(zip(cuts, dc_pairs)), pair_send, pair_recv)
    for copy in copies:
        copy.start()
    lanes = [
        Scatter(place, nt_ref, nt_pair, cut, pair, *(("y", "x") if n % 2 == 0 else ("x", "y")),
                refs[7 * n : 7 * n + 7], send.at[n], recv.at[n])
        for n, (cut, pair) in enumerate(zip(cuts, dc_pairs))
    ]
    small = SmallScatter(place, small_src, *refs[7 * pieces :], small_send, small_recv)
    tile = tiles_ref.shape[2]
    tokens = x_ref.shape[0]

    def d_normed(src, grad_ref, first):
        count = src.shape[1] // tile

        def fetch(i, slot):
            cols = pl.ds(pl.multiple_of(i * tile, LANES), tile)
            return pltpu.make_async_copy(src.at[:, cols], tiles_ref.at[slot], tile_sem.at[slot])

        fetch(0, 0).start()

        def one(i, carry):
            slot = lax.rem(i, 2)
            pl.when(i + 1 < count)(lambda: fetch(i + 1, 1 - slot).start())
            fetch(i, slot).wait()
            cols = pl.ds(pl.multiple_of(i * tile, LANES), tile)
            for r in range(0, tokens, 2 * CHUNK):
                rows = slice(r, r + 2 * CHUNK)
                part = nt(grad_ref[rows, cols], tiles_ref[slot])
                if first:

                    @pl.when(i == 0)
                    def _():
                        gi_ref[rows] = part

                    @pl.when(i > 0)
                    def _():
                        gi_ref[rows] += part
                else:
                    gi_ref[rows] += part
            return carry

        lax.fori_loop(0, count, one, 0)

    def input_grad():
        gain = gain_ref[...]
        size = 64

        def one(i, total):
            rows = pl.ds(pl.multiple_of(i * size, size), size)
            d = gi_ref[rows, :]
            values = x_ref[rows, :].astype(F32)
            scale = lax.rsqrt(jnp.mean(values * values, axis=1, keepdims=True) + EPS)
            hat = values * scale
            weighted = d * gain
            pull = jnp.mean(weighted * hat, axis=1, keepdims=True)
            gi_ref[rows, :] = scale * (weighted - hat * pull) + cot_ref[rows, :].astype(F32)
            return total + jnp.sum(d * hat, axis=0, keepdims=True)

        grad_gain = lax.fori_loop(0, tokens // size, one, jnp.zeros(gain.shape, F32))
        small_src[...] = small_in[...]
        own = grad_gain.shape[1] // (8 * depth)
        for n in range(8 * depth):
            at = (n // depth // 4, n // depth // 2 % 2, n // depth % 2, n % depth)
            small_src[(*at, slice(0, 1), slice(0, own))] = grad_gain[:, n * own : (n + 1) * own]

    def run(first, name, *rest):
        for lane in lanes[first : first + 2]:
            getattr(lane, name)(*rest)

    d_normed(wg_src, dz_ref, True)
    for copy in copies[:2]:
        copy.wait_recv()
    run(0, "send_second", 0)
    run(0, "send_second", 1)
    for copy in copies[2:]:
        copy.wait_recv()
    run(2, "send_second", 0)
    run(0, "send_first")
    run(2, "send_second", 1)
    d_normed(wc_src, dc_ref, False)
    input_grad()
    small.stage(0)
    run(0, "hold")
    small.stage(1)
    run(2, "send_first")
    small.stage(2)
    for n, k in enumerate(lanes[0].waves()):
        run(0, "step", k)
        if n == 0:
            small.stage(3)
    run(2, "hold")
    for k in lanes[0].waves():
        small.sums.step(k)
        run(2, "step", k)
    for lane, lo, hi in zip(lanes, splits, splits[1:]):
        c_out[:, lo:hi] = lane.keep[place.z]
    small_out[...] = small.keep[place.z]
    for lane in lanes:
        lane.finish()
    small.finish()
    for copy in copies:
        copy.wait_send()


def scatter_last(normed_t, nt_pair, dc, dz, wg, wc, x, cot, gain, small, depth):
    shape = jax.ShapeDtypeStruct
    vmem, dma = pl.BlockSpec(memory_space=pltpu.VMEM), pltpu.SemaphoreType.DMA
    anywhere = pl.BlockSpec(memory_space=pl.ANY)
    sends, receives = Scatter.sems(depth)
    rows = normed_t.shape[1] // depth
    tokens, width = dc.shape
    blocks = width // LANES
    splits = tuple(LANES * (-(-blocks * n // 4)) for n in range(5))
    small_shape = small.shape[4:]
    small_sends, small_receives = SmallScatter.sems(depth)
    sizes = [hi - lo for lo, hi in zip(splits, splits[1:])]
    scratch = []
    for size in sizes:
        scratch += Scatter.scratch(depth, rows, size)
    return pl.pallas_call(
        functools.partial(scatter_last_kernel, depth, splits),
        in_specs=[vmem, vmem, vmem, vmem, anywhere, anywhere, vmem, vmem, vmem, vmem],
        out_specs=[vmem] * 3,
        out_shape=[shape((rows, width), F32), shape((tokens, x.shape[1]), F32), shape(small_shape, F32)],
        scratch_shapes=[
            *(pltpu.VMEM((tokens, size), BF16) for size in sizes),
            pltpu.VMEM(small.shape, F32),
            pltpu.VMEM((2, wg.shape[0], 3 * LANES), BF16),
            dma((2,)), dma((4,)), dma((4,)), dma((4, sends)), dma((4, receives)),
            dma((small_sends,)), dma((small_receives,)),
            *scratch,
            *SmallScatter.scratch(depth, small_shape),
        ],
        compiler_params=pltpu.CompilerParams(
            collective_id=2, has_side_effects=True, vmem_limit_bytes=VMEM_LIMIT
        ),
        name="scatter_last",
    )(normed_t, nt_pair, dc, dz, wg, wc, x, cot, gain, small)


def passed_along(value, axis, steps):
    count = lax.axis_size(axis)
    initial, last = (max(0, -steps), min(count, count - steps))
    return lax.ppermute(value, axis, [(source, source + steps) for source in range(initial, last)])


def prefix(total, local, axis, backward):
    count, here = lax.axis_size(axis), lax.axis_index(axis)
    totals = lax.all_gather(total.astype(BF16), axis)
    locals_ = lax.all_gather(local, axis)
    state = jnp.zeros(local.shape, F32)
    order = range(count - 1, 0, -1) if backward else range(count - 1)
    for lap in order:
        new = totals[lap].astype(F32) * state + locals_[lap].astype(F32)
        reached = lap > here if backward else lap < here
        state = jnp.where(reached, new, state)
    leaves = total * state + local.astype(F32)
    return state.astype(BF16), leaves.astype(BF16)


AXES = ("dp", "ctx")


def body(
    inputs, gain_in, in_weight, conv_weight, conv_bias, step_bias, decay_log, skip_gain, gain_out,
    out_weight, cotangent,
):
    seqs, seg, width = inputs.shape
    tokens = seqs * seg
    count = lax.axis_size(AXES)
    dp, depth = lax.axis_size("dp"), lax.axis_size("ctx")
    own_links = dp == 8
    inner = out_weight.shape[0] * count
    taps, channels = conv_weight.shape[0], conv_weight.shape[1] * count
    num_heads = step_bias.shape[0]
    head_dim = inner // num_heads
    a, b, c = gain_in.shape[0], gain_out.shape[0], conv_bias.shape[0]

    w_gate = in_weight[:, :inner]
    w_conv = in_weight[:, inner:]
    spare = -w_conv.shape[1] % LANES
    w_conv = jnp.pad(w_conv, ((0, 0), (0, spare)))
    rest = jnp.concatenate([gain_out, conv_bias, conv_weight.reshape(-1)])
    ends = taps - 1
    flat = inputs.reshape(tokens, width)
    cot = cotangent.reshape(tokens, width)

    if own_links:
        group = 2 * depth * a
        at = lax.rem(lax.axis_index("dp"), 2) * depth + lax.axis_index("ctx")
        head = lax.dynamic_update_slice(jnp.zeros((group,), F32), gain_in.astype(F32), (at * a,))
        small = jnp.concatenate([head, rest.astype(F32)])
        small = jnp.pad(small, (0, 8 * LANES - small.size)).reshape(8, LANES)
        pc, normed_ext, normed_t, small, w_conv = gather_project(inputs, small, w_conv, depth)
        w_conv = w_conv.reshape(width, -1)
        small = small.reshape(4, 2 * depth, 8 * LANES)
        g_in = small[:, :, :group].sum(axis=1).reshape(1, width)
        rest = small[:, :, group:].reshape(count, -1)
    else:
        before = passed_along(inputs[:, seg - EDGE :], "ctx", 1)
        ext = jnp.concatenate([before, inputs], axis=1).astype(F32)
        scale_ext = lax.rsqrt(jnp.mean(ext * ext, axis=-1, keepdims=True) + EPS)
        small = lax.all_gather(jnp.concatenate([gain_in, rest]), AXES).astype(F32)
        w_conv = lax.all_gather(w_conv, AXES, axis=0, tiled=True)
        w_gate = lax.all_gather(w_gate, AXES, axis=0, tiled=True)
        w_out = lax.all_gather(out_weight, AXES, axis=0, tiled=True)
        g_in, rest = small[:, :a].reshape(1, width), small[:, a:]
        normed_ext = (ext * scale_ext * g_in).astype(BF16)
        pc = dot(normed_ext.reshape(-1, width), w_conv).reshape(seqs, seg + EDGE, -1)
    g_out = rest[:, :b].reshape(1, inner)
    bias = rest[:, b : b + c].reshape(1, channels)
    kernel = rest[:, b + c : b + c + taps * c].reshape(count, taps, c).transpose(1, 0, 2)
    kernel = kernel.reshape(taps, channels)
    pad_head = lambda v: jnp.pad(v, (0, LANES - num_heads)).reshape(1, LANES)
    sb, dl = pad_head(step_bias), pad_head(decay_log)
    skip = jnp.repeat(skip_gain, head_dim).reshape(1, inner)

    if own_links:
        bc, dt, cum, cumt, mixed, s0, s1, s2, tot, z, dno, w_gate, w_out = scan_forward(
            pc, kernel, bias, sb, dl, skip, normed_ext, cot, in_weight, out_weight, inner, head_dim, depth
        )
        w_gate = w_gate.reshape(width, inner)
        w_out = w_out.reshape(inner, width)
        per_seq = tot[tokens // CHUNK : tokens // CHUNK + seqs][:, None, :]
    else:
        x, bc, dt, cum, cumt, loc0, local, tot = fwd_a(pc, kernel, bias, sb, dl, inner, head_dim)
        per_seq = tot[tokens // CHUNK : tokens // CHUNK + seqs][:, None, :]
        s0, s2 = prefix(per_seq, local, "ctx", False)
        mixed, s1 = fwd_b(x, bc, dt, cum, cumt, s0, loc0, tot, skip, head_dim)
        z = dot(normed_ext[:, EDGE:].reshape(tokens, width), w_gate)
        dno = nt(cot, w_out)

    turned, output, d_mixed, d_gate, grad_gain_out = mid(z, dno, mixed, w_out, g_out, flat, 8)
    if own_links:
        (
            d_conv, grad_kernel, grad_bias, grad_skip, head_sums, grad_gate_weight, grad_out_weight, nt_pair
        ) = scan_backward(
            pc, kernel, bias, sb, dl, bc, dt, cum, cumt, d_mixed, mixed, s0, s1, s2, tot, skip,
            normed_t, d_gate, turned, cot, head_dim, depth,
        )
    else:
        scatter = lambda v: lax.psum_scatter(v.astype(BF16), AXES, scatter_dimension=0, tiled=True).astype(F32)
        normed = normed_ext[:, EDGE:].reshape(tokens, width)
        grad_out_weight = scatter(dot(turned.reshape(inner, tokens), cot))
        grad_gate_weight = scatter(dot(normed, d_gate, ((0,), (0,))))
        adjoint = bwd_a(d_mixed, bc, cum, tot, seqs, head_dim)
        g, _ = prefix(per_seq, adjoint, "ctx", True)
        d_conv, tail, edge, grad_kernel, grad_bias, grad_skip, d_raw, head_sums = bwd_b(
            pc, kernel, bias, sb, dl, bc, dt, cum, cumt, d_mixed, mixed, s0, s1, s2, g, tot, skip, head_dim
        )
        after = passed_along(edge[:, EDGE - ends :].astype(BF16), "ctx", -1).astype(F32)
        tail = tail[:, EDGE - ends :] + after
        d_conv = d_conv.reshape(seqs, seg, channels).at[:, seg - ends :].set(tail.astype(BF16))
        d_conv = jnp.concatenate([d_conv.reshape(tokens, channels), d_raw.astype(BF16)], axis=1)

    grad_skip = jnp.sum(grad_skip.reshape(num_heads, head_dim), axis=1)
    heads_sum = jnp.concatenate([head_sums[0, :num_heads], head_sums[1, :num_heads], grad_skip])
    by_owner = jnp.concatenate(
        [
            grad_gain_out.reshape(count, b),
            grad_bias.reshape(count, c),
            grad_kernel.reshape(taps, count, c).transpose(1, 0, 2).reshape(count, taps * c),
            jnp.broadcast_to(heads_sum, (count, 3 * num_heads)),
        ],
        axis=1,
    )
    real = d_conv.shape[1] - spare
    if own_links:
        by_owner = jnp.pad(by_owner, ((0, 0), (LANES, 7 * LANES - by_owner.shape[1])))
        grad_conv_cols, grad_input, mine = scatter_last(
            normed_t, nt_pair, d_conv, d_gate, w_gate, w_conv, flat, cot, g_in,
            by_owner.reshape(2, 2, 2, depth, 8, LANES), depth,
        )
        grad_conv_cols, mine = grad_conv_cols[:, :real], mine.reshape(-1)
        grad_gain_in, mine = mine[:a], mine[LANES:]
    else:
        d_normed = nt(d_gate, w_gate) + nt(d_conv, w_conv)
        values = flat.astype(F32)
        scale = lax.rsqrt(jnp.mean(values * values, axis=-1, keepdims=True) + EPS)
        hat = values * scale
        weighted = d_normed * g_in
        pull = jnp.mean(weighted * hat, axis=-1, keepdims=True)
        grad_input = scale * (weighted - hat * pull) + cot.astype(F32)
        grad_conv_cols = scatter(dot(normed, d_conv[:, :real], ((0,), (0,))))
        by_owner = jnp.concatenate([jnp.sum(d_normed * hat, axis=0).reshape(count, a), by_owner], axis=1)
        mine = lax.dynamic_index_in_dim(lax.psum(by_owner, AXES), lax.axis_index(AXES), 0, False)
        grad_gain_in, mine = mine[:a], mine[a:]
    at = b + c + taps * c
    head_totals = mine[at : at + 3 * num_heads].reshape(3, num_heads)
    return (
        output.reshape(seqs, seg, width),
        grad_input.reshape(seqs, seg, width),
        grad_gain_in,
        jnp.concatenate([grad_gate_weight, grad_conv_cols], axis=1),
        mine[b + c : at].reshape(taps, c),
        mine[b : b + c],
        head_totals[0],
        head_totals[1],
        head_totals[2],
        mine[:b],
        grad_out_weight,
    )


def solution(mesh):
    rows, cols, both = P("dp", "ctx", None), P(AXES, None), P(AXES)
    return jax.shard_map(
        body,
        mesh=mesh,
        in_specs=(rows, both, cols, P(None, AXES), both, P(), P(), P(), both, cols, rows),
        out_specs=(rows, rows, both, cols, P(None, AXES), both, P(), P(), P(), both, cols),
        check_vma=False,
    )
```

```python
import functools

import jax
import jax.numpy as jnp
from jax import lax
from jax.experimental import pallas as pl
from jax.experimental.pallas import tpu as pltpu
from jax.sharding import PartitionSpec as P

EPS = 1e-05
LOG2E = 1.4426950408889634
HIGH = lax.Precision.HIGHEST
F32 = jnp.float32
BF16 = jnp.bfloat16
CHUNK = 128
GROUP = 256
EDGE = 16
LANES = 128
VMEM_LIMIT = 60 * 1024 * 1024


def dot(a, b, dims=((1,), (0,))):
    return lax.dot_general(a, b, (dims, ((), ())), preferred_element_type=F32)


def nt(a, b):
    return dot(a, b, ((1,), (1,)))


def params():
    return pltpu.CompilerParams(
        dimension_semantics=("arbitrary",), vmem_limit_bytes=VMEM_LIMIT
    )


def whole(shape):
    return pl.BlockSpec(shape, lambda i: (0,) * len(shape))


def sigmoid(v):
    return 1.0 / (1.0 + jnp.exp(-v))


def softplus(v):
    return jnp.maximum(v, 0.0) + jnp.log1p(jnp.exp(-jnp.abs(v)))


def causal_conv(ext, w, b, seg):
    taps = w.shape[0]
    total = b
    for k in range(taps):
        at = EDGE - (taps - 1) + k
        total = total + w[k : k + 1] * ext[at : at + seg]
    return total


def lane_shift(value, lanes):
    return pltpu.roll(value, lax.rem(LANES - lanes, LANES), 1)


def head_rows(ref, first):
    base = pl.multiple_of(first // 8 * 8, 8)
    return pltpu.roll(ref[pl.ds(base, 8), :], lax.rem(8 - lax.rem(first, 8), 8), 0)


def spread(cols, at, head_dim):
    rows = cols.shape[0]
    lane = lax.broadcasted_iota(jnp.int32, (rows, LANES), 1)
    first = jnp.broadcast_to(cols[:, at : at + 1], (rows, LANES))
    second = jnp.broadcast_to(cols[:, at + 1 : at + 2], (rows, LANES))
    return jnp.where(lane < head_dim, first, second)


def spread_all(cols, heads, head_dim):
    return jnp.concatenate([spread(cols, j, head_dim) for j in range(0, heads, 2)], axis=1)


def block_diagonal(pair, head_dim):
    lane = lax.broadcasted_iota(jnp.int32, pair.shape, 1)
    zero = jnp.zeros_like(pair)
    return jnp.concatenate(
        [jnp.where(lane < head_dim, pair, zero), jnp.where(lane < head_dim, zero, pair)], axis=0
    )


MESH = pl.DeviceIdType.MESH


class Place:
    def __init__(self, depth):
        dp, z = lax.axis_index("dp"), lax.axis_index("ctx")
        self.depth, self.z = depth, z
        self.own = {"y": lax.div(dp, 4), "x": lax.rem(lax.div(dp, 2), 2), "c": lax.rem(dp, 2)}
        self.to = {
            name: {"dp": dp + step * (1 - 2 * self.own[name])}
            for name, step in (("y", 4), ("x", 2), ("c", 1))
        }
        self.has_left, self.has_right = z > 0, z < depth - 1
        self.left, self.right = {"ctx": z - 1}, {"ctx": z + 1}

    def flipped(self, *names):
        return {n: 1 - v if n in names else v for n, v in self.own.items()}

    def near(self, k):
        z, last = self.z, self.depth - 1
        reach = jnp.minimum(z, last - z)
        pair = jnp.where(k % 2 == 1, z - (k + 1) // 2, z + k // 2)
        alone = jnp.where(z > last - z, last - k, k)
        return z if k == 0 else jnp.where(k <= 2 * reach, pair, alone)

    def meet(self):
        barrier = pltpu.get_barrier_semaphore()
        signal = functools.partial(pl.semaphore_signal, barrier, inc=1, device_id_type=MESH)
        for name in ("y", "x", "c"):
            signal(device_id=self.to[name])
        pl.when(self.has_left)(lambda: signal(device_id=self.left))
        pl.when(self.has_right)(lambda: signal(device_id=self.right))
        ends = self.has_left.astype(jnp.int32) + self.has_right.astype(jnp.int32)
        pl.semaphore_wait(barrier, 3 + ends)


def remote(src, dst, send, recv, to):
    return pltpu.make_async_remote_copy(
        src_ref=src, dst_ref=dst, send_sem=send, recv_sem=recv, device_id=to, device_id_type=MESH
    )


class Gather:
    def __init__(self, place, src, line, first, second, send, recv, part=()):
        self.place, self.src, self.line_of, self.part = place, src, line, part
        self.first, self.second, self.send, self.recv = first, second, send, recv

    @staticmethod
    def sems(depth):
        return 6 * depth + 3, 5 * depth + 3

    def flips(self, g):
        return ((), (self.first,), (self.second,), (self.first, self.second))[g]

    def slot(self, k, *flips):
        return self.line_of(**self.place.flipped(*flips)).at[(self.place.near(k), *self.part)]

    def copy(self, k, where, to, send, recv):
        src = self.src if k == 0 and where == () else self.slot(k, *where)
        return remote(src, self.slot(k, *where), self.send.at[send], self.recv.at[recv], to)

    def along(self, k, right):
        p = self.place
        return self.copy(k, (), p.right if right else p.left, int(right) * p.depth + k, p.near(k))

    def goes(self, k, right):
        p, at = self.place, self.place.near(k)
        if right:
            return p.has_right if k == 0 else p.has_right & (at < p.z)
        return p.has_left if k == 0 else p.has_left & (at > p.z)

    def to_axis(self, k, stage, there=False):
        p, depth = self.place, self.place.depth
        f, s = self.first, self.second
        where = ((), (), (f,), (f, s))[stage]
        axis = (f, s, s, "c")[stage]
        if there:
            where = where + (axis,)
        return self.copy(k, where, p.to[axis], (2 + stage) * depth + k, (1 + stage) * depth + k)

    def to_core(self, g, there=False):
        depth = self.place.depth
        flips = self.flips(g) + (("c",) if there else ())
        line = self.line_of(**self.place.flipped(*flips)).at[(pl.ds(0, depth), *self.part)]
        return remote(line, line, self.send.at[6 * depth + g], self.recv.at[5 * depth + g], self.place.to["c"])

    def line(self, k):
        if k:
            self.along(k, True).wait_recv()
        for right in (True, False):
            pl.when(self.goes(k, right))(lambda: self.along(k, right).start())
        for stage in (0, 1):
            self.to_axis(k, stage).start()

    def from_first(self, k):
        self.to_axis(k, 0, True).wait_recv()
        self.to_axis(k, 2).start()

    def from_second(self, k):
        self.to_axis(k, 1, True).wait_recv()

    def from_both(self, k):
        self.to_axis(k, 2, True).wait_recv()
        self.to_axis(k, 3).start()

    def core(self, g):
        self.to_core(g).start()

    def whole(self, g):
        if g < 3:
            self.to_core(g, True).wait_recv()
        else:
            for k in range(self.place.depth):
                self.to_axis(k, 3, True).wait_recv()

    def finish(self):
        for k in range(self.place.depth):
            for right in (True, False):
                pl.when(self.goes(k, right))(lambda: self.along(k, right).wait_send())
            for stage in range(4):
                self.to_axis(k, stage).wait_send()
        for g in range(3):
            self.to_core(g).wait_send()


class Line:
    def __init__(self, place, keep, sent, came, send, recv):
        self.place, self.keep, self.sent, self.came = place, keep, sent, came
        self.send, self.recv = send, recv

    def copy(self, k, to, at):
        zk = self.place.near(k)
        return remote(self.sent.at[zk], self.came.at[at], self.send.at[k], self.recv.at[at], to)

    def take(self, at):
        self.copy(1, self.place.left, at).wait_recv()
        zk = jnp.where(at == self.place.depth, self.place.z, at)
        self.keep[zk] = self.keep[zk] + self.came[at].astype(F32)

    def moves(self, k):
        p, zk = self.place, self.place.near(k)
        return (
            (zk < p.z, p.left, zk),
            (zk > p.z, p.right, jnp.where(zk == p.z + 1, p.depth, zk)),
        )

    def step(self, k):
        p, zk = self.place, self.place.near(k)
        if k == 0:
            pl.when(p.has_right)(lambda: self.take(p.z))
            pl.when(p.has_left)(lambda: self.take(p.depth))
            return
        farther = ((zk < p.z) & p.has_right) | ((zk > p.z) & p.has_left)
        pl.when(farther)(lambda: self.take(zk))
        self.sent[zk] = self.keep[zk].astype(self.sent.dtype)
        for goes, to, at in self.moves(k):
            pl.when(goes)(lambda: self.copy(k, to, at).start())

    def finish(self):
        for k in range(1, self.place.depth):
            for goes, to, at in self.moves(k):
                pl.when(goes)(lambda: self.copy(k, to, at).wait_send())


class Scatter:
    def __init__(self, place, lhs, lhs_pair, rhs, rhs_pair, first, second, bufs, send, recv):
        self.place, self.lhs, self.lhs_pair, self.rhs, self.rhs_pair = place, lhs, lhs_pair, rhs, rhs_pair
        self.first, self.second, self.send, self.recv = first, second, send, recv
        self.s_sent, self.s_came, self.f_sent, self.f_came, self.keep, z_sent, z_came = bufs
        depth = place.depth
        self.sums = Line(place, self.keep, z_sent, z_came, send.at[pl.ds(2 + depth, depth)],
                         recv.at[pl.ds(2 + depth, depth + 1)])

    @staticmethod
    def sems(depth):
        return 2 + 2 * depth, 3 + 2 * depth

    @staticmethod
    def scratch(depth, rows, cols):
        block = lambda *lead: pltpu.VMEM(lead + (rows, cols), BF16)
        return [
            block(2, depth), block(2, depth), block(depth), block(depth),
            pltpu.VMEM((depth, rows, cols), F32), block(depth), block(depth + 1),
        ]

    def product(self, flips, store):
        at = self.place.flipped(*flips)
        pair = 2 * at["y"] + at["x"]
        one = 2 * pair + at["c"]
        rows, cols = self.keep.shape[1:]
        tile = 512

        def block(start, size):
            lanes = pl.ds(start, size)
            part = dot(self.lhs[one], self.rhs[:, lanes]) + dot(self.lhs_pair[pair], self.rhs_pair[:, lanes])
            for z in range(self.place.depth):
                store(z, lanes, part[z * rows : (z + 1) * rows])

        def loop(i, carry):
            block(pl.multiple_of(i * tile, tile), tile)
            return carry

        lax.fori_loop(0, cols // tile, loop, 0)
        if cols % tile:
            block(cols // tile * tile, cols % tile)

    def to_second(self, j):
        return remote(self.s_sent.at[j], self.s_came.at[j], self.send.at[j], self.recv.at[j],
                      self.place.to[self.second])

    def to_first(self, k):
        zk, n = self.place.near(k), 2 + k
        return remote(self.f_sent.at[zk], self.f_came.at[zk], self.send.at[n], self.recv.at[n],
                      self.place.to[self.first])

    def waves(self):
        return range(self.place.depth - 1, -1, -1)

    def send_second(self, j):
        def store(z, lanes, part):
            self.s_sent[j, z, :, lanes] = part.astype(BF16)

        self.product((self.second, self.first) if j == 0 else (self.second,), store)
        self.to_second(j).start()

    def send_first(self):
        self.to_second(0).wait_recv()

        def store(z, lanes, part):
            self.f_sent[z, :, lanes] = (part + self.s_came[0, z, :, lanes].astype(F32)).astype(BF16)

        self.product((self.first,), store)
        for k in self.waves():
            self.to_first(k).start()

    def hold(self):
        self.to_second(1).wait_recv()

        def store(z, lanes, part):
            self.keep[z, :, lanes] = part + self.s_came[1, z, :, lanes].astype(F32)

        self.product((), store)

    def step(self, k):
        self.to_first(k).wait_recv()
        zk = self.place.near(k)
        self.keep[zk] = self.keep[zk] + self.f_came[zk].astype(F32)
        self.sums.step(k)

    def finish(self):
        for j in (0, 1):
            self.to_second(j).wait_send()
        for k in self.waves():
            self.to_first(k).wait_send()
        self.sums.finish()


class SmallScatter:
    def __init__(self, place, src, c_came, half, x_came, keep, y_came, z_sent, z_came, send, recv):
        self.place, self.src, self.c_came, self.half = place, src, c_came, half
        self.x_came, self.keep, self.y_came = x_came, keep, y_came
        self.send, self.recv = send, recv
        depth = place.depth
        self.sums = Line(place, keep, z_sent, z_came, send.at[pl.ds(7, depth)],
                         recv.at[pl.ds(7, depth + 1)])

    @staticmethod
    def sems(depth):
        return 7 + depth, 8 + depth

    @staticmethod
    def scratch(depth, shape):
        block = lambda *lead: pltpu.VMEM(lead + shape, F32)
        return [
            block(2, 2, depth), block(2, 2, depth), block(2, depth), block(depth), block(depth),
            block(depth), block(depth + 1),
        ]

    def copy(self, n):
        p, own = self.place, self.place.own
        if n < 4:
            y, x = n // 2, n % 2
            src, dst, to = self.src.at[y, x, 1 - own["c"]], self.c_came.at[y, x], "c"
        elif n < 6:
            src, dst, to = self.half.at[n - 4, 1 - own["x"]], self.x_came.at[n - 4], "x"
        else:
            src, dst, to = self.half.at[1 - own["y"], own["x"]], self.y_came, "y"
        return remote(src, dst, self.send.at[n], self.recv.at[n], p.to[to])

    def stage(self, n):
        own = self.place.own
        if n == 0:
            for i in range(4):
                self.copy(i).start()
        elif n == 1:
            for i in range(4):
                self.copy(i).wait_recv()
            for y in (0, 1):
                for x in (0, 1):
                    self.half[y, x] = self.src[y, x, own["c"]] + self.c_came[y, x]
            for i in (4, 5):
                self.copy(i).start()
        elif n == 2:
            for i in (4, 5):
                self.copy(i).wait_recv()
            for y in (0, 1):
                self.half[y, own["x"]] = self.half[y, own["x"]] + self.x_came[y]
            self.copy(6).start()
        else:
            self.copy(6).wait_recv()
            self.keep[...] = self.half[own["y"], own["x"]] + self.y_came[...]

    def finish(self):
        for n in range(7):
            self.copy(n).wait_send()
        self.sums.finish()


def gather_kernel(
    depth, half, x_ref, small_src, wc_src, pc_ref, normed_ref, normt_ref, small_ref, wc_ref,
    hat_ref, edge_ref, buf_ref, edge_sem, load_sem, own_sem, send, recv,
):
    place = Place(depth)
    place.meet()
    seqs, seg, features = x_ref.shape
    width = wc_src.shape[1]
    lo, hi = pl.ds(0, half), pl.ds(half, width - half)
    every = slice(None)
    weights = lambda y, x, c: wc_ref.at[y, x, c]
    lanes = [
        Gather(place, small_src, lambda y, x, c: small_ref.at[y, x, c], "y", "x", send.at[0], recv.at[0]),
        Gather(place, wc_src.at[:, lo], weights, "y", "x", send.at[1], recv.at[1], (every, lo)),
        Gather(place, wc_src.at[:, hi], weights, "x", "y", send.at[2], recv.at[2], (every, hi)),
    ]
    early, late = lanes[:2], lanes[2:]
    own = place.own
    mine = (own["y"], own["x"], own["c"], place.z)
    copies = [
        pltpu.make_async_copy(src, dst.at[mine], own_sem.at[n])
        for n, (src, dst) in enumerate(((small_src, small_ref), (wc_src, wc_ref)))
    ]
    edge = remote(x_ref.at[:, pl.ds(seg - EDGE, EDGE)], edge_ref, edge_sem.at[0], edge_sem.at[1], place.right)

    def each(group, *steps):
        for name, k in steps:
            for lane in group:
                getattr(lane, name)(k)

    def load(at, n):
        cols = (lo, hi)[n]
        return pltpu.make_async_copy(
            wc_ref.at[at["y"], at["x"], :, :, :, cols], buf_ref.at[:, :, :, cols], load_sem.at[n]
        )

    rows = wc_src.shape[0]
    count = 2 * depth * rows

    def norm(flips):
        at = place.flipped(*flips)
        group = 2 * at["y"] + at["x"]
        here = pl.ds(pl.multiple_of(group * count, LANES), count)
        gain = sum(
            small_ref[at["y"], at["x"], c, z, : count // LANES] for c in (0, 1) for z in range(depth)
        )
        gain = jnp.concatenate([gain[i : i + 1] for i in range(count // LANES)], axis=1)
        for s in range(seqs):
            normed = (hat_ref[s, :, here] * gain).astype(BF16)
            normed_ref[s, :, here] = normed
            turned = normed[EDGE:].astype(F32).T.astype(BF16)
            for c in (0, 1):
                normt_ref[2 * group + c, :, s * seg : (s + 1) * seg] = turned[c * depth * rows : (c + 1) * depth * rows]

    def multiply(flips, n):
        at = place.flipped(*flips)
        here = pl.ds(pl.multiple_of((2 * at["y"] + at["x"]) * count, LANES), count)
        load(at, n).start()
        load(at, n).wait()
        first, last = ((0, half), (half, width))[n]
        tile = 4 * LANES
        for start in range(first, last, tile):
            cols = slice(start, min(start + tile, last))
            block = jnp.concatenate(
                [buf_ref[c, z, :, cols] for c in (0, 1) for z in range(depth)], axis=0
            )
            for s in range(seqs):
                part = dot(normed_ref[s, :, here], block)
                if flips == ():
                    pc_ref[s, :, cols] = part
                else:
                    pc_ref[s, :, cols] += part

    each(early, ("line", 0))
    pl.when(place.has_right)(edge.start)
    for copy in copies:
        copy.start()
    pl.when(place.has_left)(edge.wait_recv)

    @pl.when(jnp.logical_not(place.has_left))
    def _():
        edge_ref[...] = jnp.zeros_like(edge_ref)

    def scale_rows(s, start, rows_in, r, step):
        values = rows_in[s, r : r + step].astype(F32)
        mean = jnp.mean(values * values, axis=1, keepdims=True)
        hat_ref[s, start + r : start + r + step] = values * lax.rsqrt(mean + EPS)

    pieces = []
    for s in range(seqs):
        pieces.append((s, 0, edge_ref, 0, EDGE))
        pieces += [(s, EDGE, x_ref, r, 64) for r in range(0, seg, 64)]
    share = -(-len(pieces) // depth)
    for k in range(depth):
        for piece in pieces[k * share : (k + 1) * share]:
            scale_rows(*piece)
        if k + 1 < depth:
            each(early, ("line", k + 1))
        if k == depth - 2:
            each(late, ("line", 0))
    for copy in copies:
        copy.wait()
    each(early, ("core", 0))
    for k in range(1, depth):
        each(late, ("line", k))
    each(late, ("core", 0))
    for k in range(depth):
        each(early, ("from_first", k), ("from_second", k))
    each(early, ("core", 1), ("core", 2))
    each(late, ("from_first", 0), ("from_first", 1))
    each(early, ("whole", 0))
    norm(())
    multiply((), 0)
    for k in range(2, depth):
        each(late, ("from_first", k))
    each(early, ("whole", 1))
    norm(("y",))
    multiply(("y",), 0)
    for k in range(depth):
        each(late, ("from_second", k))
    each(late, ("core", 1), ("core", 2))
    each(early, ("whole", 2))
    norm(("x",))
    multiply(("x",), 0)
    each(late, ("whole", 0))
    multiply((), 1)
    for k in range(depth - 1):
        each(lanes, ("from_both", k))
    each(late, ("whole", 1), ("whole", 2))
    multiply(("y",), 1)
    multiply(("x",), 1)
    each(lanes, ("from_both", depth - 1))
    each(early, ("whole", 3))
    norm(("y", "x"))
    multiply(("y", "x"), 0)
    each(late, ("whole", 3))
    multiply(("y", "x"), 1)
    for lane in lanes:
        lane.finish()
    pl.when(place.has_right)(edge.wait_send)


def gather_project(x, small, wc, depth):
    shape = jax.ShapeDtypeStruct
    seqs, seg, features = x.shape
    slots = (2, 2, 2, depth)
    sends, receives = Gather.sems(depth)
    width = wc.shape[1]
    half = width // 2 // LANES * LANES
    anywhere, vmem = pl.BlockSpec(memory_space=pl.ANY), pl.BlockSpec(memory_space=pltpu.VMEM)
    dma = pltpu.SemaphoreType.DMA
    return pl.pallas_call(
        functools.partial(gather_kernel, depth, half),
        in_specs=[vmem, vmem, anywhere],
        out_specs=[vmem, vmem, vmem, vmem, anywhere],
        out_shape=[
            shape((seqs, seg + EDGE, width), F32),
            shape((seqs, seg + EDGE, features), BF16),
            shape((8, depth * wc.shape[0], seqs * seg), BF16),
            shape(slots + small.shape, F32),
            shape(slots + wc.shape, BF16),
        ],
        scratch_shapes=[
            pltpu.VMEM((seqs, seg + EDGE, features), F32),
            pltpu.VMEM((seqs, EDGE, features), BF16),
            pltpu.VMEM((2, depth) + wc.shape, BF16),
            dma((2,)), dma((2,)), dma((2,)), dma((3, sends)), dma((3, receives)),
        ],
        compiler_params=pltpu.CompilerParams(
            collective_id=0, has_side_effects=True, vmem_limit_bytes=VMEM_LIMIT
        ),
        name="gather_project",
    )(x, small, wc)


def fwd_a_kernel(
    head_dim, pc_ref, w_ref, b_ref, raw_ref, sb_ref, dl_ref,
    x_ref, bc_ref, dt_ref, cum_ref, cumt_ref, loc0_ref, seg_ref, tot_ref, bt_ref,
):
    step = pl.program_id(0)
    seqs = pc_ref.shape[0]
    seg = pc_ref.shape[1] - EDGE
    chunks = seg // CHUNK
    w, b = w_ref[...], b_ref[...]

    def acts_of(s):
        pre = causal_conv(pc_ref[s], w, b, seg)
        return pre * sigmoid(pre)

    @pl.when(step == 0)
    def _():
        row = lax.broadcasted_iota(jnp.int32, (CHUNK, CHUNK), 0)
        col = lax.broadcasted_iota(jnp.int32, (CHUNK, CHUNK), 1)
        tri = (col <= row).astype(F32)
        rate = -jnp.exp(dl_ref[...])
        for s in range(seqs):
            acts = acts_of(s)
            bc_ref[s * seg : (s + 1) * seg] = acts
            for c in range(chunks):
                q = s * chunks + c
                rows = slice(q * CHUNK, (q + 1) * CHUNK)
                bt_ref[q] = acts[c * CHUNK : (c + 1) * CHUNK, :LANES].T.astype(BF16)
                dt = softplus(raw_ref[s, EDGE + c * CHUNK : EDGE + (c + 1) * CHUNK] + sb_ref[...])
                cum = LOG2E * jnp.dot(tri, dt * rate, precision=HIGH, preferred_element_type=F32)
                dt_ref[rows] = dt
                cum_ref[rows] = cum
                cumt_ref[:, rows] = cum.T

    @pl.when(step > 0)
    def _():
        heads = GROUP // head_dim
        first = (step - 1) * heads
        cumg = lane_shift(cum_ref[...], first)
        dtg = lane_shift(dt_ref[...], first)
        for s in range(seqs):
            x = acts_of(s)
            x_ref[s * seg : (s + 1) * seg] = x
            state, total = None, None
            for c in range(chunks):
                q = s * chunks + c
                rows = slice(q * CHUNK, (q + 1) * CHUNK)
                ce = spread_all(cumg[rows], heads, head_dim)
                de = spread_all(dtg[rows], heads, head_dim)
                end = ce[CHUNK - 1 : CHUNK]
                uw = x[c * CHUNK : (c + 1) * CHUNK] * de * jnp.exp2(end - ce)
                loc = dot(bt_ref[q], uw.astype(BF16))
                tot = jnp.exp2(end)
                tot_ref[q : q + 1] = tot
                if c == 0:
                    loc0_ref[s] = loc
                    state, total = loc, tot
                else:
                    state, total = tot * state + loc, tot * total
            seg_ref[s] = state.astype(BF16)
            tot_ref[seqs * chunks + s : seqs * chunks + s + 1] = total


def fwd_a(pc, w, b, sb, dl, inner, head_dim):
    seqs, rows, cols = pc.shape
    seg = rows - EDGE
    tokens = seqs * seg
    groups = inner // GROUP
    state = LANES
    chunks = tokens // CHUNK
    at = lambda i: (i + groups) % (groups + 1)
    back = lambda i: jnp.maximum(i - 1, 0)
    return pl.pallas_call(
        functools.partial(fwd_a_kernel, head_dim),
        grid=(groups + 1,),
        in_specs=[
            pl.BlockSpec((seqs, rows, GROUP), lambda i: (0, 0, at(i))),
            pl.BlockSpec((w.shape[0], GROUP), lambda i: (0, at(i))),
            pl.BlockSpec((1, GROUP), lambda i: (0, at(i))),
            pl.BlockSpec((seqs, rows, LANES), lambda i: (0, 0, cols // LANES - 1)),
            whole((1, LANES)),
            whole((1, LANES)),
        ],
        out_specs=[
            pl.BlockSpec((tokens, GROUP), lambda i: (0, back(i))),
            whole((tokens, GROUP)),
            whole((tokens, LANES)),
            whole((tokens, LANES)),
            whole((LANES, tokens)),
            pl.BlockSpec((seqs, state, GROUP), lambda i: (0, 0, back(i))),
            pl.BlockSpec((seqs, state, GROUP), lambda i: (0, 0, back(i))),
            pl.BlockSpec((8, GROUP), lambda i: (0, back(i))),
        ],
        out_shape=[
            jax.ShapeDtypeStruct((tokens, inner), F32),
            jax.ShapeDtypeStruct((tokens, GROUP), F32),
            jax.ShapeDtypeStruct((tokens, LANES), F32),
            jax.ShapeDtypeStruct((tokens, LANES), F32),
            jax.ShapeDtypeStruct((LANES, tokens), F32),
            jax.ShapeDtypeStruct((seqs, state, inner), F32),
            jax.ShapeDtypeStruct((seqs, state, inner), BF16),
            jax.ShapeDtypeStruct((8, inner), F32),
        ],
        scratch_shapes=[pltpu.VMEM((chunks, LANES, CHUNK), BF16)],
        compiler_params=params(),
        name="conv_states",
    )(pc, w, b, pc, sb, dl)


def fwd_b_kernel(
    head_dim, x_ref, bc_ref, dt_ref, cum_ref, cumt_ref, s0_ref, loc0_ref, tot_ref, skip_ref,
    mixed_ref, s1_ref, cb_ref,
):
    step = pl.program_id(0)
    seqs = s0_ref.shape[0]
    chunks = x_ref.shape[0] // CHUNK // seqs
    heads = GROUP // head_dim

    @pl.when(step == 0)
    def _():
        for q in range(seqs * chunks):
            rows = slice(q * CHUNK, (q + 1) * CHUNK)
            cb_ref[q] = nt(bc_ref[rows, LANES:].astype(BF16), bc_ref[rows, :LANES].astype(BF16))

    first = step * heads
    cumg = lane_shift(cum_ref[...], first)
    dtg = lane_shift(dt_ref[...], first)
    cumr = head_rows(cumt_ref, first)
    row = lax.broadcasted_iota(jnp.int32, (CHUNK, CHUNK), 0)
    col = lax.broadcasted_iota(jnp.int32, (CHUNK, CHUNK), 1)
    causal = col <= row
    skip = skip_ref[...]
    for s in range(seqs):
        start = s0_ref[s]
        for c in range(chunks):
            q = s * chunks + c
            rows = slice(q * CHUNK, (q + 1) * CHUNK)
            x = x_ref[rows]
            ce = spread_all(cumg[rows], heads, head_dim)
            de = spread_all(dtg[rows], heads, head_dim)
            ub = (x * de).astype(BF16)
            cb = cb_ref[q]
            parts = []
            for j in range(0, heads, 2):
                mats = []
                for h in (j, j + 1):
                    there = jnp.broadcast_to(cumg[rows, h : h + 1], (CHUNK, CHUNK))
                    here = cumr[h : h + 1, rows]
                    decay = jnp.exp2(jnp.where(causal, there - here, -jnp.inf))
                    mats.append((decay * cb).astype(BF16))
                pair = ub[:, j * head_dim : (j + 2) * head_dim]
                parts.append(dot(jnp.concatenate(mats, axis=1), block_diagonal(pair, head_dim)))
            y = jnp.concatenate(parts, axis=1)
            y = y + jnp.exp2(ce) * dot(bc_ref[rows, LANES:].astype(BF16), start)
            mixed_ref[rows] = y + skip * x
            if c == 0:
                start = (tot_ref[q : q + 1] * start.astype(F32) + loc0_ref[s]).astype(BF16)
                s1_ref[s] = start


def fwd_b(x, bc, dt, cum, cumt, s0, loc0, tot, skip, head_dim):
    tokens, inner = x.shape
    seqs, state, _ = s0.shape
    groups = inner // GROUP
    wide = pl.BlockSpec((tokens, GROUP), lambda i: (0, i))
    states = pl.BlockSpec((seqs, state, GROUP), lambda i: (0, 0, i))
    return pl.pallas_call(
        functools.partial(fwd_b_kernel, head_dim),
        grid=(groups,),
        in_specs=[
            wide, whole(bc.shape), whole(dt.shape), whole(cum.shape), whole(cumt.shape),
            states, states,
            pl.BlockSpec((8, GROUP), lambda i: (0, i)),
            pl.BlockSpec((1, GROUP), lambda i: (0, i)),
        ],
        out_specs=[wide, states],
        out_shape=[
            jax.ShapeDtypeStruct((tokens, inner), F32),
            jax.ShapeDtypeStruct((seqs, state, inner), BF16),
        ],
        scratch_shapes=[pltpu.VMEM((tokens // CHUNK, CHUNK, CHUNK), F32)],
        compiler_params=params(),
        name="scan_outputs",
    )(x, bc, dt, cum, cumt, s0, loc0, tot, skip)


def halves(v):
    high = v.astype(BF16)
    return high, (v - high.astype(F32)).astype(BF16)


def dot_pairs(a, b, dims=((1,), (0,))):
    (ah, al), (bh, bl) = halves(a), halves(b)
    return dot(ah, bh, dims) + (dot(al, bh, dims) + dot(ah, bl, dims))


def dot_pair(a, b, dims=((1,), (0,))):
    high, low = halves(a)
    return dot(high, b, dims) + dot(low, b, dims)


def nt_exact(a, b):
    return lax.dot_general(a, b, (((1,), (1,)), ((), ())), precision=HIGH, preferred_element_type=F32)


class Chain:
    def __init__(self, place, came, sent, send, recv, backward):
        self.came, self.sent, self.send, self.recv = came, sent, send, recv
        self.gets, self.gives = place.has_left, place.has_right
        self.to = place.left if backward else place.right
        if backward:
            self.gets, self.gives = self.gives, self.gets
        self.behind = place.depth - 1 - place.z if backward else place.z

    def copy(self, g):
        return remote(self.sent.at[g], self.came.at[g], self.send.at[g], self.recv.at[g], self.to)

    def step(self, g, total, own):
        pl.when(self.gets)(lambda: self.copy(g).wait_recv())

        @pl.when(jnp.logical_not(self.gets))
        def _():
            self.came[g] = jnp.zeros(self.came.shape[1:], self.came.dtype)

        self.sent[g] = (total * self.came[g].astype(F32) + own).astype(BF16)
        pl.when(self.gives)(lambda: self.copy(g).start())

    def finish(self):
        groups = self.came.shape[0]

        def one(g, carry):
            self.copy(g).wait_send()
            return carry

        @pl.when(self.gives)
        def _():
            lax.fori_loop(0, groups, one, 0)


def scan_forward_kernel(
    depth, head_dim, groups,
    pc_ref, w_ref, b_ref, raw_ref, sb_ref, dl_ref, skip_ref, normed_ref, cot_ref, wi_src, wo_src,
    bc_ref, dt_ref, cum_ref, cumt_ref, mixed_ref, s0_ref, s1_ref, s2_ref, tot_ref, z_out, dno_out, wg_ref, wo_ref,
    bt_ref, cb_ref, x_ring, loc_ring, seg_ring, tot_ring, came, sent,
    z_ref, dno_ref, wg_buf, wo_buf, chain_send, chain_recv, own_sem, load_sem, out_sem, send, recv,
):
    step = pl.program_id(0)
    lag = depth - 1
    seqs = pc_ref.shape[0]
    seg = pc_ref.shape[1] - EDGE
    chunks = seg // CHUNK
    heads = GROUP // head_dim
    w, b = w_ref[...], b_ref[...]
    place = Place(depth)
    chain = Chain(place, came, sent, chain_send, chain_recv, False)
    wg_src = wi_src.at[:, pl.ds(0, z_ref.shape[1])]
    gate = Gather(place, wg_src, lambda y, x, c: wg_ref.at[y, x, c], "y", "x", send.at[0], recv.at[0])
    out = Gather(place, wo_src, lambda y, x, c: wo_ref.at[y, x, c], "x", "y", send.at[1], recv.at[1])
    mine = (place.own["y"], place.own["x"], place.own["c"], place.z)
    copies = [
        pltpu.make_async_copy(wg_src, wg_ref.at[mine], own_sem.at[0]),
        pltpu.make_async_copy(wo_src, wo_ref.at[mine], own_sem.at[1]),
    ]

    def waves(*steps):
        for lane, name, k in steps:
            getattr(lane, name)(k)

    def acts_of(s):
        pre = causal_conv(pc_ref[s], w, b, seg)
        return pre * sigmoid(pre)

    @pl.when(step == 0)
    def _():
        place.meet()
        waves((gate, "line", 0))
        for copy in copies:
            copy.start()
        row = lax.broadcasted_iota(jnp.int32, (CHUNK, CHUNK), 0)
        col = lax.broadcasted_iota(jnp.int32, (CHUNK, CHUNK), 1)
        tri = (col <= row).astype(F32)
        rate = -jnp.exp(dl_ref[...])
        for s in range(seqs):
            acts = acts_of(s)
            bc_ref[s * seg : (s + 1) * seg] = acts
            for c in range(chunks):
                q = s * chunks + c
                rows = slice(q * CHUNK, (q + 1) * CHUNK)
                b_proj = acts[c * CHUNK : (c + 1) * CHUNK, :LANES]
                c_proj = acts[c * CHUNK : (c + 1) * CHUNK, LANES:]
                bt_ref[q] = b_proj.T
                cb_ref[q] = nt_exact(c_proj, b_proj)
                dt = softplus(raw_ref[s, EDGE + c * CHUNK : EDGE + (c + 1) * CHUNK] + sb_ref[...])
                cum = LOG2E * jnp.dot(tri, dt * rate, precision=HIGH, preferred_element_type=F32)
                dt_ref[rows] = dt
                cum_ref[rows] = cum
                cumt_ref[:, rows] = cum.T

    @pl.when((step > 0) & (step <= groups))
    def _():
        g = step - 1
        at = lax.rem(g, lag + 1)
        first = g * heads
        cumg = lane_shift(cum_ref[...], first)
        dtg = lane_shift(dt_ref[...], first)
        for s in range(seqs):
            x = acts_of(s)
            x_ring[at, s * seg : (s + 1) * seg] = x
            state, total = None, None
            for c in range(chunks):
                q = s * chunks + c
                rows = slice(q * CHUNK, (q + 1) * CHUNK)
                ce = spread_all(cumg[rows], heads, head_dim)
                de = spread_all(dtg[rows], heads, head_dim)
                end = ce[CHUNK - 1 : CHUNK]
                uw = x[c * CHUNK : (c + 1) * CHUNK] * de * jnp.exp2(end - ce)
                loc = dot_pairs(bt_ref[q], uw)
                tot = jnp.exp2(end)
                tot_ring[at, q : q + 1] = tot
                if c == 0:
                    loc_ring[at, s] = loc
                    state, total = loc, tot
                else:
                    state, total = tot * state + loc, tot * total
            seg_ring[at, s] = state
            tot_ring[at, seqs * chunks + s : seqs * chunks + s + 1] = total

    handed = step - 1 - chain.behind

    @pl.when((handed >= 0) & (handed < groups))
    def _():
        at = lax.rem(handed, lag + 1)
        totals = tot_ring[at, seqs * chunks : seqs * chunks + seqs]
        chain.step(handed, totals[:, None, :], seg_ring[at])

    @pl.when(step > lag)
    def _():
        g = step - 1 - lag
        at = lax.rem(g, lag + 1)
        first = g * heads
        cumg = lane_shift(cum_ref[...], first)
        dtg = lane_shift(dt_ref[...], first)
        cumr = head_rows(cumt_ref, first)
        row = lax.broadcasted_iota(jnp.int32, (CHUNK, CHUNK), 0)
        col = lax.broadcasted_iota(jnp.int32, (CHUNK, CHUNK), 1)
        causal = col <= row
        skip = skip_ref[...]
        s0_ref[...] = came[g]
        s2_ref[...] = sent[g]
        tot_ref[...] = tot_ring[at]
        for s in range(seqs):
            start = came[g, s]
            for c in range(chunks):
                q = s * chunks + c
                rows = slice(q * CHUNK, (q + 1) * CHUNK)
                x = x_ring[at, rows]
                ce = spread_all(cumg[rows], heads, head_dim)
                de = spread_all(dtg[rows], heads, head_dim)
                ub = (x * de).astype(BF16)
                cb = cb_ref[q]
                parts = []
                for j in range(0, heads, 2):
                    mats = []
                    for h in (j, j + 1):
                        there = jnp.broadcast_to(cumg[rows, h : h + 1], (CHUNK, CHUNK))
                        here = cumr[h : h + 1, rows]
                        decay = jnp.exp2(jnp.where(causal, there - here, -jnp.inf))
                        mats.append((decay * cb).astype(BF16))
                    pair = ub[:, j * head_dim : (j + 2) * head_dim]
                    parts.append(dot(jnp.concatenate(mats, axis=1), block_diagonal(pair, head_dim)))
                y = jnp.concatenate(parts, axis=1)
                y = y + jnp.exp2(ce) * dot(bc_ref[rows, LANES:].astype(BF16), start)
                mixed_ref[rows] = y + skip * x
                if c == 0:
                    later = tot_ring[at, q : q + 1] * start.astype(F32) + loc_ring[at, s]
                    s1_ref[s] = later
                    start = later.astype(BF16)

    beside = {
        3: [(gate, "line", 1)],
        6: [(gate, "line", 2), (out, "line", 0)],
        9: [(gate, "line", 3)],
        12: [(out, "line", 1)],
    }
    for at, steps in beside.items():
        pl.when(step == at)(lambda: waves(*steps))

    @pl.when(step == groups + lag)
    def _():
        rows = 2 * depth * wi_src.shape[0]
        tile = 4 * LANES
        size = dno_ref.shape[1] // 8

        def fetch(src, buf, flips, n):
            at = place.flipped(*flips)
            copy = pltpu.make_async_copy(src.at[at["y"], at["x"]], buf, load_sem.at[n])
            copy.start()
            copy.wait()
            return 2 * at["y"] + at["x"]

        def gate_product(flips):
            group = fetch(wg_ref, wg_buf, flips, 0)
            here = pl.ds(pl.multiple_of(group * rows, LANES), rows)

            def one(i, carry):
                cols = pl.ds(pl.multiple_of(i * tile, tile), tile)
                block = jnp.concatenate(
                    [wg_buf[c, z, :, cols] for c in (0, 1) for z in range(depth)], axis=0
                )
                for s in range(seqs):
                    part = dot(normed_ref[s, EDGE:, here], block)
                    at_rows = slice(s * seg, (s + 1) * seg)
                    if flips == ():
                        z_ref[at_rows, cols] = part
                    else:
                        z_ref[at_rows, cols] += part
                return carry

            lax.fori_loop(0, z_ref.shape[1] // tile, one, 0)

        def out_product(flips, n):
            group = fetch(wo_ref, wo_buf, flips, 1)
            for c in (0, 1):
                block = jnp.concatenate([wo_buf[c, z] for z in range(depth)], axis=0)
                cols = pl.ds(pl.multiple_of((2 * group + c) * size, LANES), size)
                dno_ref[:, cols] = nt(cot_ref[...], block)
            dno_copy(flips, n).start()

        def dno_copy(flips, n):
            at = place.flipped(*flips)
            cols = pl.ds(pl.multiple_of((2 * at["y"] + at["x"]) * 2 * size, LANES), 2 * size)
            return pltpu.make_async_copy(dno_ref.at[:, cols], dno_out.at[:, cols], out_sem.at[n])

        by_group = ((), ("y",), ("x",), ("y", "x"))
        every = range(depth)
        for copy in copies:
            copy.wait()
        waves((gate, "core", 0), *((out, "line", k) for k in range(2, depth)), (out, "core", 0))
        waves(*((gate, name, k) for k in every for name in ("from_first", "from_second")))
        waves((gate, "core", 1), (gate, "core", 2))
        waves((out, "from_first", 0), (out, "from_first", 1), (gate, "whole", 0))
        gate_product(by_group[0])
        waves(*((out, "from_first", k) for k in range(2, depth)))
        waves((gate, "whole", 1))
        gate_product(by_group[1])
        waves(*((out, "from_second", k) for k in every), (out, "core", 1), (out, "core", 2))
        waves((gate, "whole", 2))
        gate_product(by_group[2])
        waves((gate, "from_both", 0), (out, "from_both", 0), (out, "whole", 0))
        out_product(by_group[0], 0)
        waves((gate, "from_both", 1), (out, "from_both", 1), (out, "whole", 2))
        out_product(by_group[1], 1)
        waves(*((lane, "from_both", k) for k in range(2, depth - 1) for lane in (gate, out)))
        waves((out, "whole", 1))
        out_product(by_group[2], 2)
        waves((gate, "from_both", depth - 1), (out, "from_both", depth - 1), (gate, "whole", 3))
        gate_product(by_group[3])
        z_copy = pltpu.make_async_copy(z_ref, z_out, out_sem.at[4])
        z_copy.start()
        waves((out, "whole", 3))
        out_product(by_group[3], 3)
        for lane in (gate, out):
            lane.finish()
        chain.finish()
        for n, flips in enumerate(by_group):
            dno_copy(flips, n).wait()
        z_copy.wait()


def scan_forward(pc, w, b, sb, dl, skip, normed, cot, w_in, wo, inner, head_dim, depth):
    seqs, rows, cols = pc.shape
    tokens = seqs * (rows - EDGE)
    groups = inner // GROUP
    lag = depth - 1
    chunks = tokens // CHUNK
    shape, dma = jax.ShapeDtypeStruct, pltpu.SemaphoreType.DMA
    into = lambda i: jnp.where(i == 0, groups, jnp.minimum(i - 1, groups - 1))
    out = lambda i: jnp.maximum(i - 1 - lag, 0)
    states = pl.BlockSpec((seqs, LANES, GROUP), lambda i: (0, 0, out(i)))
    anywhere = pl.BlockSpec(memory_space=pl.ANY)
    sends, receives = Gather.sems(depth)
    slots = (2, 2, 2, depth)
    ring = lambda *dims: pltpu.VMEM((lag + 1,) + dims, F32)
    link = pltpu.VMEM((groups, seqs, LANES, GROUP), BF16)
    once = lambda v: pl.BlockSpec(v.shape, lambda i: (0,) * v.ndim, pipeline_mode=pl.Buffered(1))
    return pl.pallas_call(
        functools.partial(scan_forward_kernel, depth, head_dim, groups),
        grid=(groups + 1 + lag,),
        in_specs=[
            pl.BlockSpec((seqs, rows, GROUP), lambda i: (0, 0, into(i))),
            pl.BlockSpec((w.shape[0], GROUP), lambda i: (0, into(i))),
            pl.BlockSpec((1, GROUP), lambda i: (0, into(i))),
            pl.BlockSpec((seqs, rows, LANES), lambda i: (0, 0, cols // LANES - 1)),
            whole((1, LANES)),
            whole((1, LANES)),
            pl.BlockSpec((1, GROUP), lambda i: (0, out(i))),
            once(normed),
            once(cot),
            anywhere,
            anywhere,
        ],
        out_specs=[
            whole((tokens, GROUP)),
            whole((tokens, LANES)),
            whole((tokens, LANES)),
            whole((LANES, tokens)),
            pl.BlockSpec((tokens, GROUP), lambda i: (0, out(i))),
            states, states, states,
            pl.BlockSpec((8, GROUP), lambda i: (0, out(i))),
            anywhere,
            anywhere,
            anywhere,
            anywhere,
        ],
        out_shape=[
            shape((tokens, GROUP), F32),
            shape((tokens, LANES), F32),
            shape((tokens, LANES), F32),
            shape((LANES, tokens), F32),
            shape((tokens, inner), F32),
            shape((seqs, LANES, inner), BF16),
            shape((seqs, LANES, inner), F32),
            shape((seqs, LANES, inner), BF16),
            shape((8, inner), F32),
            shape((tokens, inner), F32),
            shape((tokens, inner), F32),
            shape(slots + (w_in.shape[0], inner), BF16),
            shape(slots + wo.shape, BF16),
        ],
        scratch_shapes=[
            pltpu.VMEM((chunks, LANES, CHUNK), F32),
            pltpu.VMEM((chunks, CHUNK, CHUNK), F32),
            ring(tokens, GROUP), ring(seqs, LANES, GROUP), ring(seqs, LANES, GROUP), ring(8, GROUP),
            link, link,
            pltpu.VMEM((tokens, inner), F32), pltpu.VMEM((tokens, inner), F32),
            pltpu.VMEM((2, depth, w_in.shape[0], inner), BF16), pltpu.VMEM((2, depth) + wo.shape, BF16),
            dma((groups,)), dma((groups,)), dma((2,)), dma((2,)), dma((5,)), dma((2, sends)), dma((2, receives)),
        ],
        compiler_params=pltpu.CompilerParams(
            dimension_semantics=("arbitrary",), collective_id=3, has_side_effects=True,
            vmem_limit_bytes=VMEM_LIMIT,
        ),
        name="scan_forward",
    )(pc, w, b, pc, sb, dl, skip, normed, cot, w_in, wo)


def mid_kernel(
    z_ref, dno_ref, mixed_ref, wo_ref, gain_ref, in_ref, not_ref, out_ref, dm_ref, dz_ref, gg_ref, acc_ref,
):
    step = pl.program_id(0)
    inner = mixed_ref.shape[1]
    tiles, tile = not_ref.shape[0], not_ref.shape[1]

    @pl.when(step == 0)
    def _():
        gg_ref[...] = jnp.zeros_like(gg_ref)

    def lanes_of(i):
        return pl.ds(pl.multiple_of(i * tile, tile), tile)

    def fold(v):
        total = v[:, :LANES]
        for k in range(LANES, tile, LANES):
            total = total + v[:, k : k + LANES]
        return total

    def one(i, sums):
        sq, hg = sums
        at = lanes_of(i)
        z = z_ref[:, at]
        g = mixed_ref[:, at] * z * sigmoid(z)
        return sq + fold(g * g), hg + fold(dno_ref[:, at] * gain_ref[:, at] * g)

    zero = jnp.zeros((mixed_ref.shape[0], LANES), F32)
    sq, hg = lax.fori_loop(0, tiles, one, (zero, zero))
    scale = lax.rsqrt(jnp.sum(sq, axis=1, keepdims=True) / inner + EPS)
    pull = scale * scale * scale * (jnp.sum(hg, axis=1, keepdims=True) / inner)
    acc_ref[...] = in_ref[...].astype(F32)

    def two(i, carry):
        at = lanes_of(i)
        z, mixed, dno, gain = z_ref[:, at], mixed_ref[:, at], dno_ref[:, at], gain_ref[:, at]
        sig = sigmoid(z)
        act = z * sig
        g = mixed * act
        gs = g * scale
        no = gs * gain
        not_ref[i] = no.T.astype(BF16)
        acc_ref[...] += dot(no.astype(BF16), wo_ref[at, :])
        gg_ref[:, at] += jnp.sum(dno * gs, axis=0, keepdims=True)
        dg = scale * (dno * gain) - g * pull
        dm_ref[:, at] = dg * act
        dz_ref[:, at] = (dg * mixed * (sig * (1.0 + z * (1.0 - sig)))).astype(BF16)
        return carry

    lax.fori_loop(0, tiles, two, 0)
    out_ref[...] = acc_ref[...].astype(BF16)


def mid(z, dno, mixed, wo, gain, inputs, tiles):
    tokens, inner = mixed.shape
    width = inputs.shape[1]
    tile = inner // tiles
    narrow = pl.BlockSpec((CHUNK, width), lambda i: (i, 0))
    wide = pl.BlockSpec((CHUNK, inner), lambda i: (i, 0))
    once = lambda v: pl.BlockSpec(v.shape, lambda i: (0,) * v.ndim, pipeline_mode=pl.Buffered(1))
    return pl.pallas_call(
        mid_kernel,
        grid=(tokens // CHUNK,),
        in_specs=[wide, wide, wide, once(wo), whole((1, inner)), narrow],
        out_specs=[
            pl.BlockSpec((tiles, tile, CHUNK), lambda i: (0, 0, i)), narrow, wide, wide,
            whole((1, inner)),
        ],
        out_shape=[
            jax.ShapeDtypeStruct((tiles, tile, tokens), BF16),
            jax.ShapeDtypeStruct((tokens, width), BF16),
            jax.ShapeDtypeStruct((tokens, inner), F32),
            jax.ShapeDtypeStruct((tokens, inner), BF16),
            jax.ShapeDtypeStruct((1, inner), F32),
        ],
        scratch_shapes=[pltpu.VMEM((CHUNK, width), F32)],
        compiler_params=params(),
        name="gate_norm_project",
    )(z, dno, mixed, wo, gain, inputs)


def bwd_a_kernel(head_dim, seqs, dm_ref, bc_ref, cum_ref, tot_ref, seg_ref, ct_ref):
    step = pl.program_id(0)
    chunks = dm_ref.shape[0] // CHUNK // seqs
    heads = GROUP // head_dim

    @pl.when(step == 0)
    def _():
        for q in range(seqs * chunks):
            ct_ref[q] = bc_ref[q * CHUNK : (q + 1) * CHUNK, LANES:].T.astype(BF16)

    cumg = lane_shift(cum_ref[...], step * heads)
    for s in range(seqs):
        state = None
        for c in range(chunks - 1, -1, -1):
            q = s * chunks + c
            rows = slice(q * CHUNK, (q + 1) * CHUNK)
            ey = jnp.exp2(spread_all(cumg[rows], heads, head_dim)) * dm_ref[rows]
            loc = dot(ct_ref[q], ey.astype(BF16))
            state = loc if state is None else tot_ref[q : q + 1] * state + loc
        seg_ref[s] = state.astype(BF16)


def bwd_a(dm, bc, cum, tot, seqs, head_dim):
    tokens, inner = dm.shape
    return pl.pallas_call(
        functools.partial(bwd_a_kernel, head_dim, seqs),
        grid=(inner // GROUP,),
        in_specs=[
            pl.BlockSpec((tokens, GROUP), lambda i: (0, i)), whole(bc.shape), whole(cum.shape),
            pl.BlockSpec((8, GROUP), lambda i: (0, i)),
        ],
        out_specs=pl.BlockSpec((seqs, LANES, GROUP), lambda i: (0, 0, i)),
        out_shape=jax.ShapeDtypeStruct((seqs, LANES, inner), BF16),
        scratch_shapes=[pltpu.VMEM((tokens // CHUNK, LANES, CHUNK), BF16)],
        compiler_params=params(),
        name="adjoint_states",
    )(dm, bc, cum, tot)


def bwd_b_kernel(
    head_dim, groups, pc_ref, w_ref, b_ref, raw_ref, sb_ref, dl_ref, bc_ref, dt_ref, cum_ref, cumt_ref,
    dm_ref, mixed_ref, s0_ref, s1_ref, s2_ref, g_ref, tot_ref, skip_ref,
    dc_ref, tail_ref, edge_ref, gw_ref, gb_ref, gskip_ref, draw_ref, hsum_ref,
    cbt_ref, dcbt_ref, db_acc, dc_acc, r1_ref, r2_ref, dtot_ref,
):
    step = pl.program_id(0)
    seqs = pc_ref.shape[0]
    seg = pc_ref.shape[1] - EDGE
    chunks = seg // CHUNK
    heads = GROUP // head_dim
    w, b = w_ref[...], b_ref[...]
    taps = w.shape[0]

    @pl.when(step == 0)
    def _():
        for q in range(seqs * chunks):
            rows = slice(q * CHUNK, (q + 1) * CHUNK)
            cbt_ref[q] = nt(bc_ref[rows, :LANES].astype(BF16), bc_ref[rows, LANES:].astype(BF16))
        dcbt_ref[...] = jnp.zeros_like(dcbt_ref)
        db_acc[...] = jnp.zeros_like(db_acc)
        dc_acc[...] = jnp.zeros_like(dc_acc)
        r1_ref[...] = jnp.zeros_like(r1_ref)
        r2_ref[...] = jnp.zeros_like(r2_ref)
        dtot_ref[...] = jnp.zeros_like(dtot_ref)

    def conv_back(s, ext, pre, sig, d_act):
        d_pre = d_act * (sig * (1.0 + pre * (1.0 - sig)))
        zero = jnp.zeros((EDGE, d_pre.shape[1]), F32)
        padded = jnp.concatenate([zero, d_pre, zero], axis=0)
        total = None
        for k in range(taps):
            at = taps - 1 - k
            term = w[k : k + 1] * padded[at : at + seg + EDGE]
            total = term if total is None else total + term
        edge_ref[s] = total[:EDGE]
        dc_ref[s * seg : (s + 1) * seg] = total[EDGE:].astype(BF16)
        tail_ref[s] = total[seg:]
        for k in range(taps):
            at = EDGE - (taps - 1) + k
            grad = jnp.sum(ext[at : at + seg] * d_pre, axis=0, keepdims=True)
            gw_ref[k : k + 1] = grad if s == 0 else gw_ref[k : k + 1] + grad
        grad = jnp.sum(d_pre, axis=0, keepdims=True)
        gb_ref[...] = grad if s == 0 else gb_ref[...] + grad

    def by_head(value, pick):
        high = value.astype(BF16)
        return dot(high, pick) + dot((value - high.astype(F32)).astype(BF16), pick)

    @pl.when(step < groups)
    def _():
        first = step * heads
        cumg = lane_shift(cum_ref[...], first)
        dtg = lane_shift(dt_ref[...], first)
        cumr = head_rows(cumt_ref, first)
        row = lax.broadcasted_iota(jnp.int32, (CHUNK, CHUNK), 0)
        col = lax.broadcasted_iota(jnp.int32, (CHUNK, CHUNK), 1)
        causal = row <= col
        lane = lax.broadcasted_iota(jnp.int32, (GROUP, LANES), 0)
        head = lax.broadcasted_iota(jnp.int32, (GROUP, LANES), 1)
        pick = (head == first + lane // head_dim).astype(BF16)
        skip = skip_ref[...]
        grad_skip = None
        for s in range(seqs):
            ext = pc_ref[s]
            pre = causal_conv(ext, w, b, seg)
            sig = sigmoid(pre)
            acts = pre * sig
            adj = g_ref[s].astype(F32)
            d_acts = [None] * chunks
            for c in range(chunks - 1, -1, -1):
                q = s * chunks + c
                rows = slice(q * CHUNK, (q + 1) * CHUNK)
                x = acts[c * CHUNK : (c + 1) * CHUNK]
                dy = dm_ref[rows]
                ce = spread_all(cumg[rows], heads, head_dim)
                de = spread_all(dtg[rows], heads, head_dim)
                weight = jnp.exp2(ce[CHUNK - 1 : CHUNK] - ce)
                u = x * de
                ub = u.astype(BF16)
                dyb = dy.astype(BF16)
                cbt = cbt_ref[q]
                parts = []
                dcbt = dcbt_ref[q]
                for j in range(0, heads, 2):
                    lanes = slice(j * head_dim, (j + 2) * head_dim)
                    dy_block = block_diagonal(dyb[:, lanes], head_dim)
                    dm = nt(ub[:, lanes], dy_block)
                    mats = []
                    for k, h in enumerate((j, j + 1)):
                        here = jnp.broadcast_to(cumg[rows, h : h + 1], (CHUNK, CHUNK))
                        there = cumr[h : h + 1, rows]
                        decay = jnp.exp2(jnp.where(causal, there - here, -jnp.inf))
                        mats.append((decay * cbt).astype(BF16))
                        dcbt = dcbt + decay * dm[:, k * CHUNK : (k + 1) * CHUNK]
                    parts.append(dot(jnp.concatenate(mats, axis=1), dy_block))
                dcbt_ref[q] = dcbt
                start = s0_ref[s] if c == 0 else s1_ref[s]
                end = s2_ref[s] if c == chunks - 1 else s1_ref[s]
                adj_b = adj.astype(BF16)
                bb = bc_ref[rows, :LANES].astype(BF16)
                cb = bc_ref[rows, LANES:].astype(BF16)
                ey = (jnp.exp2(ce) * dy).astype(BF16)
                du = jnp.concatenate(parts, axis=1) + weight * dot(bb, adj_b)
                db_acc[rows] += nt((u * weight).astype(BF16), adj_b)
                dc_acc[rows] += nt(ey, start)
                r1_ref[rows] += by_head(dyb.astype(F32) * (mixed_ref[rows] - skip * x), pick)
                r2_ref[rows] += by_head(x * du, pick)
                dtot_ref[q : q + 1] += by_head(
                    jnp.sum(adj * end.astype(F32), axis=0, keepdims=True), pick
                )
                grad = jnp.sum(dy * x, axis=0, keepdims=True)
                grad_skip = grad if grad_skip is None else grad_skip + grad
                d_acts[c] = du * de + skip * dy
                if c > 0:
                    adj = tot_ref[q : q + 1] * adj + dot(cb, ey, ((0,), (0,)))
            conv_back(s, ext, pre, sig, jnp.concatenate(d_acts, axis=0))
        gskip_ref[...] = grad_skip

    @pl.when(step == groups)
    def _():
        row = lax.broadcasted_iota(jnp.int32, (CHUNK, CHUNK), 0)
        col = lax.broadcasted_iota(jnp.int32, (CHUNK, CHUNK), 1)
        later = (row <= col).astype(F32)
        rate = -jnp.exp(dl_ref[...])
        sum_raw = jnp.zeros((1, LANES), F32)
        sum_log = jnp.zeros((1, LANES), F32)
        for s in range(seqs):
            ext = pc_ref[s]
            pre = causal_conv(ext, w, b, seg)
            sig = sigmoid(pre)
            parts = []
            for c in range(chunks):
                q = s * chunks + c
                rows = slice(q * CHUNK, (q + 1) * CHUNK)
                dcbt = dcbt_ref[q]
                bb = bc_ref[rows, :LANES].astype(BF16)
                cb = bc_ref[rows, LANES:].astype(BF16)
                d_b = db_acc[rows] + dot(dcbt.astype(BF16), cb)
                d_c = dc_acc[rows] + dot(dcbt.T.astype(BF16), bb)
                parts.append(jnp.concatenate([d_b, d_c], axis=1))
                dt = dt_ref[rows]
                r2 = r2_ref[rows]
                d_log = jnp.dot(
                    later, r1_ref[rows] - dt * r2, precision=HIGH, preferred_element_type=F32
                )
                d_log = d_log + dtot_ref[q : q + 1]
                raw = raw_ref[s, EDGE + c * CHUNK : EDGE + (c + 1) * CHUNK] + sb_ref[...]
                d_raw = (r2 + rate * d_log) * sigmoid(raw)
                draw_ref[rows] = d_raw
                sum_raw = sum_raw + jnp.sum(d_raw, axis=0, keepdims=True)
                sum_log = sum_log + jnp.sum(d_log * dt, axis=0, keepdims=True) * rate
            conv_back(s, ext, pre, sig, jnp.concatenate(parts, axis=0))
        hsum_ref[0:1] = sum_raw
        hsum_ref[1:2] = sum_log


def bwd_b(pc, w, b, sb, dl, bc, dt, cum, cumt, dm, mixed, s0, s1, s2, g, tot, skip, head_dim):
    seqs, rows, cols = pc.shape
    tokens, inner = dm.shape
    groups = inner // GROUP
    taps, channels = w.shape
    wide = pl.BlockSpec((tokens, GROUP), lambda i: (0, jnp.minimum(i, groups - 1)))
    states = pl.BlockSpec((seqs, LANES, GROUP), lambda i: (0, 0, jnp.minimum(i, groups - 1)))
    line = lambda n: pl.BlockSpec((n, GROUP), lambda i: (0, jnp.minimum(i, groups - 1)))
    conv = lambda n: pl.BlockSpec((n, GROUP), lambda i: (0, i))
    ends = pl.BlockSpec((seqs, EDGE, GROUP), lambda i: (0, 0, i))
    chunks = tokens // CHUNK
    shape = jax.ShapeDtypeStruct
    return pl.pallas_call(
        functools.partial(bwd_b_kernel, head_dim, groups),
        grid=(groups + 1,),
        in_specs=[
            pl.BlockSpec((seqs, rows, GROUP), lambda i: (0, 0, i)),
            conv(taps),
            conv(1),
            pl.BlockSpec((seqs, rows, LANES), lambda i: (0, 0, cols // LANES - 1)),
            whole((1, LANES)), whole((1, LANES)),
            whole(bc.shape), whole(dt.shape), whole(cum.shape), whole(cumt.shape),
            wide, wide, states, states, states, states, line(8), line(1),
        ],
        out_specs=[
            conv(tokens), ends, ends, conv(taps), conv(1), line(1),
            whole((tokens, LANES)), whole((2, LANES)),
        ],
        out_shape=[
            shape((tokens, channels), BF16),
            shape((seqs, EDGE, channels), F32),
            shape((seqs, EDGE, channels), F32),
            shape((taps, channels), F32),
            shape((1, channels), F32),
            shape((1, inner), F32),
            shape((tokens, LANES), F32),
            shape((2, LANES), F32),
        ],
        scratch_shapes=[
            pltpu.VMEM((chunks, CHUNK, CHUNK), F32),
            pltpu.VMEM((chunks, CHUNK, CHUNK), F32),
            pltpu.VMEM((tokens, LANES), F32),
            pltpu.VMEM((tokens, LANES), F32),
            pltpu.VMEM((tokens, LANES), F32),
            pltpu.VMEM((tokens, LANES), F32),
            pltpu.VMEM((8, LANES), F32),
        ],
        compiler_params=params(),
        name="scan_backward",
    )(pc, w, b, pc, sb, dl, bc, dt, cum, cumt, dm, mixed, s0, s1, s2, g, tot, skip)


PIECES = (3, 2, 1)


def piece_of(columns, n):
    unit = columns // sum(PIECES)
    return sum(PIECES[:n]) * unit, sum(PIECES[: n + 1]) * unit


def pair_copies(place, lhs, rhs, send, recv):
    other = 1 - place.own["c"]
    parts = [(src.at[2 * g + other], dst.at[g]) for src, dst in lhs for g in range(4)] + list(rhs)
    return [
        remote(src, dst, send.at[n], recv.at[n], place.to["c"]) for n, (src, dst) in enumerate(parts)
    ]


def scan_backward_kernel(
    depth, head_dim, groups,
    pc_ref, w_ref, b_ref, raw_ref, sb_ref, dl_ref, bc_ref, dt_ref, cum_ref, cumt_ref,
    dma_ref, dm_ref, mixed_ref, s0_ref, s1_ref, s2_ref, tot_ref, skip_ref,
    nt_src, dz_src, no_src, cot_src,
    dc_out, gw_ref, gb_ref, hsum_ref, a_out, b_out, nt_out,
    cbt_ref, ct_ref, dcbt_ref, db_acc, dc_acc, r1_ref, r2_ref, dtot_ref, skip_acc,
    dc_ref, tail_ref, edge_ref, edge_came, seg_ring, tot_ring, came, sent,
    nt_pair, dz_pair, no_pair, cot_pair,
    chain_send, chain_recv, edge_send, edge_recv, pair_send, pair_recv, out_sem, send, recv, *bufs,
):
    step = pl.program_id(0)
    lag = depth - 1
    seqs = pc_ref.shape[0]
    seg = pc_ref.shape[1] - EDGE
    chunks = seg // CHUNK
    heads = GROUP // head_dim
    w, b = w_ref[...], b_ref[...]
    taps = w.shape[0]
    channels = tail_ref.shape[2]
    place = Place(depth)
    chain = Chain(place, came, sent, chain_send, chain_recv, True)
    cut = lambda ref, lo, hi: ref.at[:, pl.ds(lo, hi - lo)]
    rhs = []
    for n in range(2):
        for src, dst in ((dz_src, dz_pair), (cot_src, cot_pair)):
            lo, hi = piece_of(src.shape[1], n)
            hi = hi if n == 0 else src.shape[1]
            rhs.append((cut(src, lo, hi), cut(dst, lo, hi)))
    pairs = pair_copies(place, ((nt_src, nt_pair), (no_src, no_pair)), rhs, pair_send, pair_recv)
    def piece(ref, n):
        lo, hi = piece_of(ref.shape[1], n)
        return ref.at[:, pl.ds(lo, hi - lo)]

    lanes = []
    for n in range(len(PIECES)):
        lanes += [
            Scatter(place, nt_src, nt_pair, piece(dz_src, n), piece(dz_pair, n), "y", "x",
                    bufs[14 * n : 14 * n + 7], send.at[2 * n], recv.at[2 * n]),
            Scatter(place, no_src, no_pair, piece(cot_src, n), piece(cot_pair, n), "x", "y",
                    bufs[14 * n + 7 : 14 * n + 14], send.at[2 * n + 1], recv.at[2 * n + 1]),
        ]
    edges = [
        remote(edge_ref.at[:, :, cols], edge_came.at[:, :, cols], edge_send.at[n], edge_recv.at[n], place.left)
        for n, cols in enumerate((pl.ds(0, channels - GROUP), pl.ds(channels - GROUP, GROUP)))
    ]
    outs = [
        pltpu.make_async_copy(src, dst, out_sem.at[n])
        for n, (src, dst) in enumerate(((nt_pair, nt_out), (dc_ref, dc_out)))
    ]

    def run(first, name, *rest):
        for lane in lanes[2 * first : 2 * first + 2]:
            getattr(lane, name)(*rest)

    def at_step(n, *what):
        pl.when(step == n)(lambda: run(*what))

    @pl.when(step == 0)
    def _():
        place.meet()
        for copy in pairs:
            copy.start()
        for q in range(seqs * chunks):
            rows = slice(q * CHUNK, (q + 1) * CHUNK)
            b_proj, c_proj = bc_ref[rows, :LANES], bc_ref[rows, LANES:]
            cbt_ref[q] = nt_exact(b_proj, c_proj)
            ct_ref[q] = c_proj.T
        dcbt_ref[...] = jnp.zeros_like(dcbt_ref)
        db_acc[...] = jnp.zeros_like(db_acc)
        dc_acc[...] = jnp.zeros_like(dc_acc)
        r1_ref[...] = jnp.zeros_like(r1_ref)
        r2_ref[...] = jnp.zeros_like(r2_ref)
        skip_acc[...] = jnp.zeros_like(skip_acc)
        dtot_ref[...] = jnp.zeros_like(dtot_ref)

    @pl.when(step < groups)
    def _():
        at = lax.rem(step, lag + 1)
        cumg = lane_shift(cum_ref[...], step * heads)
        tot_ring[at] = tot_ref[...]
        for s in range(seqs):
            state = None
            for c in range(chunks - 1, -1, -1):
                q = s * chunks + c
                rows = slice(q * CHUNK, (q + 1) * CHUNK)
                ey = jnp.exp2(spread_all(cumg[rows], heads, head_dim)) * dma_ref[rows]
                loc = dot_pairs(ct_ref[q], ey)
                state = loc if state is None else tot_ref[q : q + 1] * state + loc
            seg_ring[at, s] = state

    handed = step - chain.behind

    @pl.when((handed >= 0) & (handed < groups))
    def _():
        at = lax.rem(handed, lag + 1)
        totals = tot_ring[at, seqs * chunks : seqs * chunks + seqs]
        chain.step(handed, totals[:, None, :], seg_ring[at])

    @pl.when(step == lag)
    def _():
        for copy in pairs[:10]:
            copy.wait_recv()
        outs[0].start()

    @pl.when(step == lag + 4)
    def _():
        for copy in pairs[10:]:
            copy.wait_recv()

    at_step(lag, 0, "send_second", 0)
    at_step(lag + 1, 0, "send_second", 1)
    at_step(lag + 3, 0, "send_first")
    at_step(lag + 4, 1, "send_second", 0)
    at_step(lag + 5, 1, "send_second", 1)
    at_step(lag + 6, 0, "hold")
    at_step(lag + 7, 2, "send_second", 0)
    at_step(lag + 8, 2, "send_second", 1)
    for n, k in enumerate(lanes[0].waves()):
        at_step(lag + 8 + n, 0, "step", k)
    at_step(lag + 10, 1, "send_first")

    def conv_back(s, ext, pre, sig, d_act, at):
        lanes_at = pl.ds(pl.multiple_of(at * GROUP, GROUP), GROUP)
        d_pre = d_act * (sig * (1.0 + pre * (1.0 - sig)))
        zero = jnp.zeros((EDGE, d_pre.shape[1]), F32)
        padded = jnp.concatenate([zero, d_pre, zero], axis=0)
        total = None
        for k in range(taps):
            start = taps - 1 - k
            term = w[k : k + 1] * padded[start : start + seg + EDGE]
            total = term if total is None else total + term
        edge_ref[s, :, lanes_at] = total[:EDGE].astype(BF16)
        dc_ref[s * seg : (s + 1) * seg, lanes_at] = total[EDGE:].astype(BF16)
        tail_ref[s, :, lanes_at] = total[seg:]
        for k in range(taps):
            start = EDGE - (taps - 1) + k
            grad = jnp.sum(ext[start : start + seg] * d_pre, axis=0, keepdims=True)
            gw_ref[k : k + 1] = grad if s == 0 else gw_ref[k : k + 1] + grad
        grad = jnp.sum(d_pre, axis=0, keepdims=True)
        gb_ref[...] = grad if s == 0 else gb_ref[...] + grad

    def by_head(value, pick):
        high = value.astype(BF16)
        return dot(high, pick) + dot((value - high.astype(F32)).astype(BF16), pick)

    @pl.when((step >= lag) & (step < lag + groups))
    def _():
        g = step - lag
        at = lax.rem(g, lag + 1)
        first = g * heads
        cumg = lane_shift(cum_ref[...], first)
        dtg = lane_shift(dt_ref[...], first)
        cumr = head_rows(cumt_ref, first)
        row = lax.broadcasted_iota(jnp.int32, (CHUNK, CHUNK), 0)
        col = lax.broadcasted_iota(jnp.int32, (CHUNK, CHUNK), 1)
        causal = row <= col
        lane = lax.broadcasted_iota(jnp.int32, (GROUP, LANES), 0)
        head = lax.broadcasted_iota(jnp.int32, (GROUP, LANES), 1)
        pick = (head == first + lane // head_dim).astype(BF16)
        skip = skip_ref[...]
        grad_skip = None
        for s in range(seqs):
            ext = pc_ref[s]
            pre = causal_conv(ext, w, b, seg)
            sig = sigmoid(pre)
            acts = pre * sig
            adj = came[g, s].astype(F32)
            d_acts = [None] * chunks
            for c in range(chunks - 1, -1, -1):
                q = s * chunks + c
                rows = slice(q * CHUNK, (q + 1) * CHUNK)
                x = acts[c * CHUNK : (c + 1) * CHUNK]
                dy = dm_ref[rows]
                ce = spread_all(cumg[rows], heads, head_dim)
                de = spread_all(dtg[rows], heads, head_dim)
                weight = jnp.exp2(ce[CHUNK - 1 : CHUNK] - ce)
                u = x * de
                ub = u.astype(BF16)
                dyb = dy.astype(BF16)
                cbt = cbt_ref[q]
                parts = []
                dcbt = dcbt_ref[q]
                for j in range(0, heads, 2):
                    two = slice(j * head_dim, (j + 2) * head_dim)
                    dy_block = block_diagonal(dyb[:, two], head_dim)
                    dm = nt(ub[:, two], dy_block)
                    mats = []
                    for k, h in enumerate((j, j + 1)):
                        here = jnp.broadcast_to(cumg[rows, h : h + 1], (CHUNK, CHUNK))
                        there = cumr[h : h + 1, rows]
                        decay = jnp.exp2(jnp.where(causal, there - here, -jnp.inf))
                        mats.append((decay * cbt).astype(BF16))
                        dcbt = dcbt + decay * dm[:, k * CHUNK : (k + 1) * CHUNK]
                    parts.append(dot(jnp.concatenate(mats, axis=1), dy_block))
                dcbt_ref[q] = dcbt
                start = s0_ref[s] if c == 0 else s1_ref[s]
                end = s2_ref[s] if c == chunks - 1 else s1_ref[s]
                adj_b = adj.astype(BF16)
                bb = bc_ref[rows, :LANES].astype(BF16)
                ey = jnp.exp2(ce) * dy
                du = jnp.concatenate(parts, axis=1) + weight * dot(bb, adj_b)
                uw = u * weight
                across = ((1,), (1,))
                db_acc[rows] += dot_pair(uw, adj_b, across) if c == chunks - 1 else dot_pairs(uw, adj, across)
                dc_acc[rows] += dot_pair(ey, start, across) if c == 0 else dot_pairs(ey, start, across)
                r1_ref[rows] += by_head(dyb.astype(F32) * (mixed_ref[rows] - skip * x), pick)
                r2_ref[rows] += by_head(x * du, pick)
                dtot_ref[q : q + 1] += by_head(
                    jnp.sum(adj * end.astype(F32), axis=0, keepdims=True), pick
                )
                grad = jnp.sum(dy * x, axis=0, keepdims=True)
                grad_skip = grad if grad_skip is None else grad_skip + grad
                d_acts[c] = du * de + skip * dy
                if c > 0:
                    adj = tot_ring[at, q : q + 1] * adj + dot_pairs(ct_ref[q], ey)
            conv_back(s, ext, pre, sig, jnp.concatenate(d_acts, axis=0), g)
        skip_acc[0:1] += by_head(grad_skip, pick)

    @pl.when(step == lag + groups)
    def _():
        pl.when(place.has_left)(edges[0].start)
        row = lax.broadcasted_iota(jnp.int32, (CHUNK, CHUNK), 0)
        col = lax.broadcasted_iota(jnp.int32, (CHUNK, CHUNK), 1)
        later = (row <= col).astype(F32)
        rate = -jnp.exp(dl_ref[...])
        sum_raw = jnp.zeros((1, LANES), F32)
        sum_log = jnp.zeros((1, LANES), F32)
        for s in range(seqs):
            ext = pc_ref[s]
            pre = causal_conv(ext, w, b, seg)
            sig = sigmoid(pre)
            parts = []
            for c in range(chunks):
                q = s * chunks + c
                rows = slice(q * CHUNK, (q + 1) * CHUNK)
                dcbt = dcbt_ref[q]
                d_b = db_acc[rows] + dot_pairs(dcbt, bc_ref[rows, LANES:])
                d_c = dc_acc[rows] + dot_pairs(dcbt.T, bc_ref[rows, :LANES])
                parts.append(jnp.concatenate([d_b, d_c], axis=1))
                dt = dt_ref[rows]
                r2 = r2_ref[rows]
                d_log = jnp.dot(
                    later, r1_ref[rows] - dt * r2, precision=HIGH, preferred_element_type=F32
                )
                d_log = d_log + dtot_ref[q : q + 1]
                raw = raw_ref[s, EDGE + c * CHUNK : EDGE + (c + 1) * CHUNK] + sb_ref[...]
                d_raw = (r2 + rate * d_log) * sigmoid(raw)
                dc_ref[rows, channels:] = d_raw.astype(BF16)
                sum_raw = sum_raw + jnp.sum(d_raw, axis=0, keepdims=True)
                sum_log = sum_log + jnp.sum(d_log * dt, axis=0, keepdims=True) * rate
            conv_back(s, ext, pre, sig, jnp.concatenate(parts, axis=0), groups)
        hsum_ref[0:1] = sum_raw
        hsum_ref[1:2] = sum_log
        hsum_ref[2:3] = skip_acc[0:1]
        pl.when(place.has_left)(edges[1].start)

        @pl.when(place.has_right)
        def _():
            for copy in edges:
                copy.wait_recv()
            for s in range(seqs):
                fixed = tail_ref[s] + edge_came[s].astype(F32)
                dc_ref[(s + 1) * seg - EDGE : (s + 1) * seg, :channels] = fixed.astype(BF16)

        outs[1].start()
        run(1, "hold")
        run(2, "send_first")
        for k in lanes[0].waves():
            run(1, "step", k)
        run(2, "hold")
        for k in lanes[0].waves():
            run(2, "step", k)
        for n, out in enumerate((a_out, b_out)):
            for i in range(len(PIECES)):
                lo, hi = piece_of(out.shape[1], i)
                out[:, lo:hi] = lanes[2 * i + n].keep[place.z]
        for lane in lanes:
            lane.finish()
        chain.finish()

        @pl.when(place.has_left)
        def _():
            for copy in edges:
                copy.wait_send()

        for copy in pairs:
            copy.wait_send()
        for copy in outs:
            copy.wait()


def scan_backward(
    pc, w, b, sb, dl, bc, dt, cum, cumt, dm, mixed, s0, s1, s2, tot, skip, normed_t, dz, turned, cot,
    head_dim, depth,
):
    seqs, rows, cols = pc.shape
    tokens, inner = dm.shape
    groups = inner // GROUP
    lag = depth - 1
    taps, channels = w.shape
    out = lambda i: jnp.maximum(i - lag, 0)
    inside = lambda i: jnp.minimum(out(i), groups - 1)
    wide = pl.BlockSpec((tokens, GROUP), lambda i: (0, inside(i)))
    states = pl.BlockSpec((seqs, LANES, GROUP), lambda i: (0, 0, inside(i)))
    line = lambda n: pl.BlockSpec((n, GROUP), lambda i: (0, inside(i)))
    conv = lambda n: pl.BlockSpec((n, GROUP), lambda i: (0, out(i)))
    ahead = lambda n: pl.BlockSpec((n, GROUP), lambda i: (0, jnp.minimum(i, groups - 1)))
    once = lambda v: pl.BlockSpec(v.shape, lambda i: (0,) * v.ndim, pipeline_mode=pl.Buffered(1))
    anywhere = pl.BlockSpec(memory_space=pl.ANY)
    chunks = tokens // CHUNK
    shape, dma = jax.ShapeDtypeStruct, pltpu.SemaphoreType.DMA
    a_rows, b_rows = normed_t.shape[1] // depth, turned.shape[1] // depth
    a_cols, b_cols = dz.shape[1], cot.shape[1]
    half = lambda v: (4,) + v.shape[1:]
    sends, receives = Scatter.sems(depth)
    buffers = []
    for n in range(len(PIECES)):
        for rows_of, cols_of in ((a_rows, a_cols), (b_rows, b_cols)):
            lo, hi = piece_of(cols_of, n)
            buffers += Scatter.scratch(depth, rows_of, hi - lo)
    ring = lambda *dims: pltpu.VMEM((lag + 1,) + dims, F32)
    link = pltpu.VMEM((groups, seqs, LANES, GROUP), BF16)
    square = pltpu.VMEM((chunks, CHUNK, CHUNK), F32)
    column = pltpu.VMEM((tokens, LANES), F32)
    return pl.pallas_call(
        functools.partial(scan_backward_kernel, depth, head_dim, groups),
        grid=(groups + 1 + lag,),
        in_specs=[
            pl.BlockSpec((seqs, rows, GROUP), lambda i: (0, 0, out(i))),
            conv(taps),
            conv(1),
            pl.BlockSpec((seqs, rows, LANES), lambda i: (0, 0, cols // LANES - 1)),
            whole((1, LANES)), whole((1, LANES)),
            whole(bc.shape), whole(dt.shape), whole(cum.shape), whole(cumt.shape),
            ahead(tokens), wide, wide, states, states, states, ahead(8), line(1),
            once(normed_t), once(dz), once(turned), once(cot),
        ],
        out_specs=[
            anywhere, conv(taps), conv(1), whole((3, LANES)),
            whole((a_rows, a_cols)), whole((b_rows, b_cols)), anywhere,
        ],
        out_shape=[
            shape((tokens, cols), BF16),
            shape((taps, channels), F32),
            shape((1, channels), F32),
            shape((3, LANES), F32),
            shape((a_rows, a_cols), F32),
            shape((b_rows, b_cols), F32),
            shape(half(normed_t), BF16),
        ],
        scratch_shapes=[
            square, pltpu.VMEM((chunks, LANES, CHUNK), F32), square, column, column, column, column,
            pltpu.VMEM((8, LANES), F32),
            pltpu.VMEM((8, LANES), F32),
            pltpu.VMEM((tokens, cols), BF16),
            pltpu.VMEM((seqs, EDGE, channels), F32),
            pltpu.VMEM((seqs, EDGE, channels), BF16),
            pltpu.VMEM((seqs, EDGE, channels), BF16),
            ring(seqs, LANES, GROUP), ring(8, GROUP), link, link,
            pltpu.VMEM(half(normed_t), BF16), pltpu.VMEM(dz.shape, BF16),
            pltpu.VMEM(half(turned), BF16), pltpu.VMEM(cot.shape, BF16),
            dma((groups,)), dma((groups,)), dma((2,)), dma((2,)), dma((12,)), dma((12,)), dma((2,)),
            dma((2 * len(PIECES), sends)), dma((2 * len(PIECES), receives)),
            *buffers,
        ],
        compiler_params=pltpu.CompilerParams(
            dimension_semantics=("arbitrary",), collective_id=1, has_side_effects=True,
            vmem_limit_bytes=VMEM_LIMIT,
        ),
        name="scan_backward_sums",
    )(
        pc, w, b, pc, sb, dl, bc, dt, cum, cumt, dm, dm, mixed, s0, s1, s2, tot, skip,
        normed_t, dz, turned, cot,
    )


def scatter_last_kernel(
    depth, splits, nt_ref, nt_pair, dc_ref, dz_ref, wg_src, wc_src, x_ref, cot_ref, gain_ref,
    ggain_ref, gb_ref, gw_ref, hsum_ref, c_out, gi_ref, small_out, *refs,
):
    place = Place(depth)
    place.meet()
    pieces = len(splits) - 1
    dc_pairs, refs = refs[:pieces], refs[pieces:]
    small_src, tiles_ref, tile_sem, pair_send, pair_recv, send, recv, small_send, small_recv = refs[:9]
    refs = refs[9:]
    cuts = [dc_ref.at[:, pl.ds(lo, hi - lo)] for lo, hi in zip(splits, splits[1:])]
    copies = pair_copies(place, (), tuple(zip(cuts, dc_pairs)), pair_send, pair_recv)
    for copy in copies:
        copy.start()
    lanes = [
        Scatter(place, nt_ref, nt_pair, cut, pair, *(("y", "x") if n % 2 == 0 else ("x", "y")),
                refs[7 * n : 7 * n + 7], send.at[n], recv.at[n])
        for n, (cut, pair) in enumerate(zip(cuts, dc_pairs))
    ]
    small = SmallScatter(place, small_src, *refs[7 * pieces :], small_send, small_recv)
    tile = tiles_ref.shape[2]
    tokens = x_ref.shape[0]

    def d_normed(src, grad_ref, first):
        count = src.shape[1] // tile

        def fetch(i, slot):
            cols = pl.ds(pl.multiple_of(i * tile, LANES), tile)
            return pltpu.make_async_copy(src.at[:, cols], tiles_ref.at[slot], tile_sem.at[slot])

        fetch(0, 0).start()

        def one(i, carry):
            slot = lax.rem(i, 2)
            pl.when(i + 1 < count)(lambda: fetch(i + 1, 1 - slot).start())
            fetch(i, slot).wait()
            cols = pl.ds(pl.multiple_of(i * tile, LANES), tile)
            for r in range(0, tokens, 2 * CHUNK):
                rows = slice(r, r + 2 * CHUNK)
                part = nt(grad_ref[rows, cols], tiles_ref[slot])
                if first:

                    @pl.when(i == 0)
                    def _():
                        gi_ref[rows] = part

                    @pl.when(i > 0)
                    def _():
                        gi_ref[rows] += part
                else:
                    gi_ref[rows] += part
            return carry

        lax.fori_loop(0, count, one, 0)

    def input_grad():
        gain = gain_ref[...]
        size = 64

        def one(i, total):
            rows = pl.ds(pl.multiple_of(i * size, size), size)
            d = gi_ref[rows, :]
            values = x_ref[rows, :].astype(F32)
            scale = lax.rsqrt(jnp.mean(values * values, axis=1, keepdims=True) + EPS)
            hat = values * scale
            weighted = d * gain
            pull = jnp.mean(weighted * hat, axis=1, keepdims=True)
            gi_ref[rows, :] = scale * (weighted - hat * pull) + cot_ref[rows, :].astype(F32)
            return total + jnp.sum(d * hat, axis=0, keepdims=True)

        grad_gain = lax.fori_loop(0, tokens // size, one, jnp.zeros(gain.shape, F32))
        small_src[...] = jnp.zeros_like(small_src)
        taps = gw_ref.shape[0]
        shares = ((0, grad_gain), (1, ggain_ref[...]), (2, gb_ref[...]), (3, gw_ref[...]))
        heads = hsum_ref[:, : LANES // 2]
        for n in range(8 * depth):
            at = (n // depth // 4, n // depth // 2 % 2, n // depth % 2, n % depth)
            for row, value in shares:
                own = value.shape[1] // (8 * depth)
                where = (*at, slice(row, row + value.shape[0]), slice(0, own))
                small_src[where] = value[:, n * own : (n + 1) * own]
            small_src[(*at, slice(0, 1), slice(LANES // 2, LANES))] = heads[0:1]
            small_src[(*at, slice(3 + taps, 4 + taps), slice(0, LANES // 2))] = heads[1:2]
            small_src[(*at, slice(3 + taps, 4 + taps), slice(LANES // 2, LANES))] = heads[2:3]

    def run(first, name, *rest):
        for lane in lanes[first : first + 2]:
            getattr(lane, name)(*rest)

    for copy in copies[:2]:
        copy.wait_recv()
    run(0, "send_second", 0)
    run(0, "send_second", 1)
    for copy in copies[2:]:
        copy.wait_recv()
    run(2, "send_second", 0)
    run(2, "send_second", 1)
    d_normed(wg_src, dz_ref, True)
    run(0, "send_first")
    run(4, "send_second", 0)
    run(4, "send_second", 1)
    d_normed(wc_src, dc_ref, False)
    run(0, "hold")
    run(2, "send_first")
    input_grad()
    small.stage(0)
    run(2, "hold")
    small.stage(1)
    for k in lanes[0].waves():
        run(0, "step", k)
    small.stage(2)
    run(4, "send_first")
    for n, k in enumerate(lanes[0].waves()):
        run(2, "step", k)
    small.stage(3)
    run(4, "hold")
    for k in lanes[0].waves():
        small.sums.step(k)
        run(4, "step", k)
    for lane, lo, hi in zip(lanes, splits, splits[1:]):
        c_out[:, lo:hi] = lane.keep[place.z]
    small_out[...] = small.keep[place.z]
    for lane in lanes:
        lane.finish()
    small.finish()
    for copy in copies:
        copy.wait_send()


def scatter_last(normed_t, nt_pair, dc, dz, wg, wc, x, cot, gain, ggain, gb, gw, hsum, depth):
    shape = jax.ShapeDtypeStruct
    vmem, dma = pl.BlockSpec(memory_space=pltpu.VMEM), pltpu.SemaphoreType.DMA
    anywhere = pl.BlockSpec(memory_space=pl.ANY)
    sends, receives = Scatter.sems(depth)
    rows = normed_t.shape[1] // depth
    tokens, width = dc.shape
    blocks = width // LANES
    parts = [share for share in PIECES for _ in (0, 1)]
    splits = tuple(LANES * (blocks * sum(parts[:n]) // sum(parts)) for n in range(len(parts) + 1))
    small_shape = (8, LANES)
    small_sends, small_receives = SmallScatter.sems(depth)
    sizes = [hi - lo for lo, hi in zip(splits, splits[1:])]
    scratch = []
    for size in sizes:
        scratch += Scatter.scratch(depth, rows, size)
    return pl.pallas_call(
        functools.partial(scatter_last_kernel, depth, splits),
        in_specs=[vmem, vmem, vmem, vmem, anywhere, anywhere] + [vmem] * 7,
        out_specs=[vmem] * 3,
        out_shape=[shape((rows, width), F32), shape((tokens, x.shape[1]), F32), shape(small_shape, F32)],
        scratch_shapes=[
            *(pltpu.VMEM((tokens, size), BF16) for size in sizes),
            pltpu.VMEM((2, 2, 2, depth) + small_shape, F32),
            pltpu.VMEM((2, wg.shape[0], 3 * LANES), BF16),
            dma((2,)), dma((6,)), dma((6,)), dma((6, sends)), dma((6, receives)),
            dma((small_sends,)), dma((small_receives,)),
            *scratch,
            *SmallScatter.scratch(depth, small_shape),
        ],
        compiler_params=pltpu.CompilerParams(
            collective_id=2, has_side_effects=True, vmem_limit_bytes=VMEM_LIMIT
        ),
        name="scatter_last",
    )(normed_t, nt_pair, dc, dz, wg, wc, x, cot, gain, ggain, gb, gw, hsum)


def passed_along(value, axis, steps):
    count = lax.axis_size(axis)
    initial, last = (max(0, -steps), min(count, count - steps))
    return lax.ppermute(value, axis, [(source, source + steps) for source in range(initial, last)])


def prefix(total, local, axis, backward):
    count, here = lax.axis_size(axis), lax.axis_index(axis)
    totals = lax.all_gather(total.astype(BF16), axis)
    locals_ = lax.all_gather(local, axis)
    state = jnp.zeros(local.shape, F32)
    order = range(count - 1, 0, -1) if backward else range(count - 1)
    for lap in order:
        new = totals[lap].astype(F32) * state + locals_[lap].astype(F32)
        reached = lap > here if backward else lap < here
        state = jnp.where(reached, new, state)
    leaves = total * state + local.astype(F32)
    return state.astype(BF16), leaves.astype(BF16)


AXES = ("dp", "ctx")


def body(
    inputs, gain_in, in_weight, conv_weight, conv_bias, step_bias, decay_log, skip_gain, gain_out,
    out_weight, cotangent,
):
    seqs, seg, width = inputs.shape
    tokens = seqs * seg
    count = lax.axis_size(AXES)
    dp, depth = lax.axis_size("dp"), lax.axis_size("ctx")
    own_links = dp == 8 and depth == 4
    inner = out_weight.shape[0] * count
    taps, channels = conv_weight.shape[0], conv_weight.shape[1] * count
    num_heads = step_bias.shape[0]
    head_dim = inner // num_heads
    a, b, c = gain_in.shape[0], gain_out.shape[0], conv_bias.shape[0]

    w_gate = in_weight[:, :inner]
    w_conv = in_weight[:, inner:]
    spare = -w_conv.shape[1] % LANES
    w_conv = jnp.pad(w_conv, ((0, 0), (0, spare)))
    rest = jnp.concatenate([gain_out, conv_bias, conv_weight.reshape(-1)])
    ends = taps - 1
    flat = inputs.reshape(tokens, width)
    cot = cotangent.reshape(tokens, width)

    if own_links:
        group = 2 * depth * a
        at = lax.rem(lax.axis_index("dp"), 2) * depth + lax.axis_index("ctx")
        head = lax.dynamic_update_slice(jnp.zeros((group,), F32), gain_in.astype(F32), (at * a,))
        small = jnp.concatenate([head, rest.astype(F32)])
        small = jnp.pad(small, (0, 8 * LANES - small.size)).reshape(8, LANES)
        pc, normed_ext, normed_t, small, w_conv = gather_project(inputs, small, w_conv, depth)
        w_conv = w_conv.reshape(width, -1)
        small = small.reshape(4, 2 * depth, 8 * LANES)
        g_in = small[:, :, :group].sum(axis=1).reshape(1, width)
        rest = small[:, :, group:].reshape(count, -1)
    else:
        before = passed_along(inputs[:, seg - EDGE :], "ctx", 1)
        ext = jnp.concatenate([before, inputs], axis=1).astype(F32)
        scale_ext = lax.rsqrt(jnp.mean(ext * ext, axis=-1, keepdims=True) + EPS)
        small = lax.all_gather(jnp.concatenate([gain_in, rest]), AXES).astype(F32)
        w_conv = lax.all_gather(w_conv, AXES, axis=0, tiled=True)
        w_gate = lax.all_gather(w_gate, AXES, axis=0, tiled=True)
        w_out = lax.all_gather(out_weight, AXES, axis=0, tiled=True)
        g_in, rest = small[:, :a].reshape(1, width), small[:, a:]
        normed_ext = (ext * scale_ext * g_in).astype(BF16)
        pc = dot(normed_ext.reshape(-1, width), w_conv).reshape(seqs, seg + EDGE, -1)
    g_out = rest[:, :b].reshape(1, inner)
    bias = rest[:, b : b + c].reshape(1, channels)
    kernel = rest[:, b + c : b + c + taps * c].reshape(count, taps, c).transpose(1, 0, 2)
    kernel = kernel.reshape(taps, channels)
    pad_head = lambda v: jnp.pad(v, (0, LANES - num_heads)).reshape(1, LANES)
    sb, dl = pad_head(step_bias), pad_head(decay_log)
    skip = jnp.repeat(skip_gain, head_dim).reshape(1, inner)

    if own_links:
        bc, dt, cum, cumt, mixed, s0, s1, s2, tot, z, dno, w_gate, w_out = scan_forward(
            pc, kernel, bias, sb, dl, skip, normed_ext, cot, in_weight, out_weight, inner, head_dim, depth
        )
        w_gate = w_gate.reshape(width, inner)
        w_out = w_out.reshape(inner, width)
        per_seq = tot[tokens // CHUNK : tokens // CHUNK + seqs][:, None, :]
    else:
        x, bc, dt, cum, cumt, loc0, local, tot = fwd_a(pc, kernel, bias, sb, dl, inner, head_dim)
        per_seq = tot[tokens // CHUNK : tokens // CHUNK + seqs][:, None, :]
        s0, s2 = prefix(per_seq, local, "ctx", False)
        mixed, s1 = fwd_b(x, bc, dt, cum, cumt, s0, loc0, tot, skip, head_dim)
        z = dot(normed_ext[:, EDGE:].reshape(tokens, width), w_gate)
        dno = nt(cot, w_out)

    turned, output, d_mixed, d_gate, grad_gain_out = mid(z, dno, mixed, w_out, g_out, flat, 8)
    if own_links:
        (
            d_conv, grad_kernel, grad_bias, head_sums, grad_gate_weight, grad_out_weight, nt_pair
        ) = scan_backward(
            pc, kernel, bias, sb, dl, bc, dt, cum, cumt, d_mixed, mixed, s0, s1, s2, tot, skip,
            normed_t, d_gate, turned, cot, head_dim, depth,
        )
    else:
        scatter = lambda v: lax.psum_scatter(v.astype(BF16), AXES, scatter_dimension=0, tiled=True).astype(F32)
        normed = normed_ext[:, EDGE:].reshape(tokens, width)
        grad_out_weight = scatter(dot(turned.reshape(inner, tokens), cot))
        grad_gate_weight = scatter(dot(normed, d_gate, ((0,), (0,))))
        adjoint = bwd_a(d_mixed, bc, cum, tot, seqs, head_dim)
        g, _ = prefix(per_seq, adjoint, "ctx", True)
        d_conv, tail, edge, grad_kernel, grad_bias, grad_skip, d_raw, head_sums = bwd_b(
            pc, kernel, bias, sb, dl, bc, dt, cum, cumt, d_mixed, mixed, s0, s1, s2, g, tot, skip, head_dim
        )
        after = passed_along(edge[:, EDGE - ends :].astype(BF16), "ctx", -1).astype(F32)
        tail = tail[:, EDGE - ends :] + after
        d_conv = d_conv.reshape(seqs, seg, channels).at[:, seg - ends :].set(tail.astype(BF16))
        d_conv = jnp.concatenate([d_conv.reshape(tokens, channels), d_raw.astype(BF16)], axis=1)

    real = d_conv.shape[1] - spare
    if own_links:
        grad_conv_cols, grad_input, mine = scatter_last(
            normed_t, nt_pair, d_conv, d_gate, w_gate, w_conv, flat, cot, g_in,
            grad_gain_out, grad_bias, grad_kernel, head_sums, depth,
        )
        grad_conv_cols = grad_conv_cols[:, :real]
        half = LANES // 2
        grad_gain_in, grad_step = mine[0, :a], mine[0, half : half + num_heads]
        grad_gain_out, grad_bias, grad_kernel = mine[1, :b], mine[2, :c], mine[3 : 3 + taps, :c]
        grad_decay = mine[3 + taps, :num_heads]
        grad_skip = mine[3 + taps, half : half + num_heads]
    else:
        d_normed = nt(d_gate, w_gate) + nt(d_conv, w_conv)
        values = flat.astype(F32)
        scale = lax.rsqrt(jnp.mean(values * values, axis=-1, keepdims=True) + EPS)
        hat = values * scale
        weighted = d_normed * g_in
        pull = jnp.mean(weighted * hat, axis=-1, keepdims=True)
        grad_input = scale * (weighted - hat * pull) + cot.astype(F32)
        grad_conv_cols = scatter(dot(normed, d_conv[:, :real], ((0,), (0,))))
        grad_skip = jnp.sum(grad_skip.reshape(num_heads, head_dim), axis=1)
        heads_sum = jnp.concatenate([head_sums[0, :num_heads], head_sums[1, :num_heads], grad_skip])
        by_owner = jnp.concatenate(
            [
                jnp.sum(d_normed * hat, axis=0).reshape(count, a),
                grad_gain_out.reshape(count, b),
                grad_bias.reshape(count, c),
                grad_kernel.reshape(taps, count, c).transpose(1, 0, 2).reshape(count, taps * c),
                jnp.broadcast_to(heads_sum, (count, 3 * num_heads)),
            ],
            axis=1,
        )
        mine = lax.dynamic_index_in_dim(lax.psum(by_owner, AXES), lax.axis_index(AXES), 0, False)
        cuts = [0, a, a + b, a + b + c, a + b + c + taps * c]
        cuts += [cuts[-1] + n * num_heads for n in (1, 2, 3)]
        parts = [mine[lo:hi] for lo, hi in zip(cuts, cuts[1:])]
        grad_gain_in, grad_gain_out, grad_bias, grad_kernel, grad_step, grad_decay, grad_skip = parts
    return (
        output.reshape(seqs, seg, width),
        grad_input.reshape(seqs, seg, width),
        grad_gain_in,
        jnp.concatenate([grad_gate_weight, grad_conv_cols], axis=1),
        grad_kernel.reshape(taps, c),
        grad_bias,
        grad_step,
        grad_decay,
        grad_skip,
        grad_gain_out,
        grad_out_weight,
    )


def solution(mesh):
    rows, cols, both = P("dp", "ctx", None), P(AXES, None), P(AXES)
    return jax.shard_map(
        body,
        mesh=mesh,
        in_specs=(rows, both, cols, P(None, AXES), both, P(), P(), P(), both, cols, rows),
        out_specs=(rows, rows, both, cols, P(None, AXES), both, P(), P(), P(), both, cols),
        check_vma=False,
    )
```

```python
import functools

import jax
import jax.numpy as jnp
from jax import lax
from jax.experimental import pallas as pl
from jax.experimental.pallas import tpu as pltpu
from jax.sharding import PartitionSpec as P

EPS = 1e-05
LOG2E = 1.4426950408889634
HIGH = lax.Precision.HIGHEST
F32 = jnp.float32
BF16 = jnp.bfloat16
CHUNK = 128
GROUP = 256
EDGE = 16
LANES = 128
VMEM_LIMIT = 60 * 1024 * 1024


def dot(a, b, dims=((1,), (0,))):
    return lax.dot_general(a, b, (dims, ((), ())), preferred_element_type=F32)


def nt(a, b):
    return dot(a, b, ((1,), (1,)))


def params():
    return pltpu.CompilerParams(
        dimension_semantics=("arbitrary",), vmem_limit_bytes=VMEM_LIMIT
    )


def whole(shape):
    return pl.BlockSpec(shape, lambda i: (0,) * len(shape))


def sigmoid(v):
    return 1.0 / (1.0 + jnp.exp(-v))


def softplus(v):
    return jnp.maximum(v, 0.0) + jnp.log1p(jnp.exp(-jnp.abs(v)))


def causal_conv(ext, w, b, seg):
    taps = w.shape[0]
    total = b
    for k in range(taps):
        at = EDGE - (taps - 1) + k
        total = total + w[k : k + 1] * ext[at : at + seg]
    return total


def lane_shift(value, lanes):
    return pltpu.roll(value, lax.rem(LANES - lanes, LANES), 1)


def head_rows(ref, first):
    base = pl.multiple_of(first // 8 * 8, 8)
    return pltpu.roll(ref[pl.ds(base, 8), :], lax.rem(8 - lax.rem(first, 8), 8), 0)


def spread(cols, at, head_dim):
    rows = cols.shape[0]
    lane = lax.broadcasted_iota(jnp.int32, (rows, LANES), 1)
    first = jnp.broadcast_to(cols[:, at : at + 1], (rows, LANES))
    second = jnp.broadcast_to(cols[:, at + 1 : at + 2], (rows, LANES))
    return jnp.where(lane < head_dim, first, second)


def spread_all(cols, heads, head_dim):
    return jnp.concatenate([spread(cols, j, head_dim) for j in range(0, heads, 2)], axis=1)


def block_diagonal(pair, head_dim):
    lane = lax.broadcasted_iota(jnp.int32, pair.shape, 1)
    zero = jnp.zeros_like(pair)
    return jnp.concatenate(
        [jnp.where(lane < head_dim, pair, zero), jnp.where(lane < head_dim, zero, pair)], axis=0
    )


MESH = pl.DeviceIdType.MESH


class Place:
    def __init__(self, depth):
        dp, z = lax.axis_index("dp"), lax.axis_index("ctx")
        self.depth, self.z = depth, z
        self.own = {"y": lax.div(dp, 4), "x": lax.rem(lax.div(dp, 2), 2), "c": lax.rem(dp, 2)}
        self.to = {
            name: {"dp": dp + step * (1 - 2 * self.own[name])}
            for name, step in (("y", 4), ("x", 2), ("c", 1))
        }
        self.has_left, self.has_right = z > 0, z < depth - 1
        self.left, self.right = {"ctx": z - 1}, {"ctx": z + 1}

    def flipped(self, *names):
        return {n: 1 - v if n in names else v for n, v in self.own.items()}

    def near(self, k):
        z, last = self.z, self.depth - 1
        reach = jnp.minimum(z, last - z)
        pair = jnp.where(k % 2 == 1, z - (k + 1) // 2, z + k // 2)
        alone = jnp.where(z > last - z, last - k, k)
        return z if k == 0 else jnp.where(k <= 2 * reach, pair, alone)

    def meet(self):
        barrier = pltpu.get_barrier_semaphore()
        signal = functools.partial(pl.semaphore_signal, barrier, inc=1, device_id_type=MESH)
        for name in ("y", "x", "c"):
            signal(device_id=self.to[name])
        pl.when(self.has_left)(lambda: signal(device_id=self.left))
        pl.when(self.has_right)(lambda: signal(device_id=self.right))
        ends = self.has_left.astype(jnp.int32) + self.has_right.astype(jnp.int32)
        pl.semaphore_wait(barrier, 3 + ends)


def remote(src, dst, send, recv, to):
    return pltpu.make_async_remote_copy(
        src_ref=src, dst_ref=dst, send_sem=send, recv_sem=recv, device_id=to, device_id_type=MESH
    )


class Gather:
    def __init__(self, place, src, line, first, second, send, recv, part=()):
        self.place, self.src, self.line_of, self.part = place, src, line, part
        self.first, self.second, self.send, self.recv = first, second, send, recv

    @staticmethod
    def sems(depth):
        return 6 * depth + 3, 5 * depth + 3

    def flips(self, g):
        return ((), (self.first,), (self.second,), (self.first, self.second))[g]

    def slot(self, k, *flips):
        return self.line_of(**self.place.flipped(*flips)).at[(self.place.near(k), *self.part)]

    def copy(self, k, where, to, send, recv):
        src = self.src if k == 0 and where == () else self.slot(k, *where)
        return remote(src, self.slot(k, *where), self.send.at[send], self.recv.at[recv], to)

    def along(self, k, right):
        p = self.place
        return self.copy(k, (), p.right if right else p.left, int(right) * p.depth + k, p.near(k))

    def goes(self, k, right):
        p, at = self.place, self.place.near(k)
        if right:
            return p.has_right if k == 0 else p.has_right & (at < p.z)
        return p.has_left if k == 0 else p.has_left & (at > p.z)

    def to_axis(self, k, stage, there=False):
        p, depth = self.place, self.place.depth
        f, s = self.first, self.second
        where = ((), (), (f,), (f, s))[stage]
        axis = (f, s, s, "c")[stage]
        if there:
            where = where + (axis,)
        return self.copy(k, where, p.to[axis], (2 + stage) * depth + k, (1 + stage) * depth + k)

    def to_core(self, g, there=False):
        depth = self.place.depth
        flips = self.flips(g) + (("c",) if there else ())
        line = self.line_of(**self.place.flipped(*flips)).at[(pl.ds(0, depth), *self.part)]
        return remote(line, line, self.send.at[6 * depth + g], self.recv.at[5 * depth + g], self.place.to["c"])

    def line(self, k):
        if k:
            self.along(k, True).wait_recv()
        for right in (True, False):
            pl.when(self.goes(k, right))(lambda: self.along(k, right).start())
        for stage in (0, 1):
            self.to_axis(k, stage).start()

    def from_first(self, k):
        self.to_axis(k, 0, True).wait_recv()
        self.to_axis(k, 2).start()

    def from_second(self, k):
        self.to_axis(k, 1, True).wait_recv()

    def from_both(self, k):
        self.to_axis(k, 2, True).wait_recv()
        self.to_axis(k, 3).start()

    def core(self, g):
        self.to_core(g).start()

    def whole(self, g):
        if g < 3:
            self.to_core(g, True).wait_recv()
        else:
            for k in range(self.place.depth):
                self.to_axis(k, 3, True).wait_recv()

    def finish(self):
        for k in range(self.place.depth):
            for right in (True, False):
                pl.when(self.goes(k, right))(lambda: self.along(k, right).wait_send())
            for stage in range(4):
                self.to_axis(k, stage).wait_send()
        for g in range(3):
            self.to_core(g).wait_send()


class Line:
    def __init__(self, place, keep, sent, came, send, recv):
        self.place, self.keep, self.sent, self.came = place, keep, sent, came
        self.send, self.recv = send, recv

    def copy(self, k, to, at):
        zk = self.place.near(k)
        return remote(self.sent.at[zk], self.came.at[at], self.send.at[k], self.recv.at[at], to)

    def take(self, at):
        self.copy(1, self.place.left, at).wait_recv()
        zk = jnp.where(at == self.place.depth, self.place.z, at)
        self.keep[zk] = self.keep[zk] + self.came[at].astype(F32)

    def moves(self, k):
        p, zk = self.place, self.place.near(k)
        return (
            (zk < p.z, p.left, zk),
            (zk > p.z, p.right, jnp.where(zk == p.z + 1, p.depth, zk)),
        )

    def step(self, k):
        p, zk = self.place, self.place.near(k)
        if k == 0:
            pl.when(p.has_right)(lambda: self.take(p.z))
            pl.when(p.has_left)(lambda: self.take(p.depth))
            return
        farther = ((zk < p.z) & p.has_right) | ((zk > p.z) & p.has_left)
        pl.when(farther)(lambda: self.take(zk))
        self.sent[zk] = self.keep[zk].astype(self.sent.dtype)
        for goes, to, at in self.moves(k):
            pl.when(goes)(lambda: self.copy(k, to, at).start())

    def finish(self):
        for k in range(1, self.place.depth):
            for goes, to, at in self.moves(k):
                pl.when(goes)(lambda: self.copy(k, to, at).wait_send())


class Scatter:
    def __init__(self, place, lhs, lhs_pair, rhs, rhs_pair, first, second, bufs, send, recv):
        self.place, self.lhs, self.lhs_pair, self.rhs, self.rhs_pair = place, lhs, lhs_pair, rhs, rhs_pair
        self.first, self.second, self.send, self.recv = first, second, send, recv
        self.s_sent, self.s_came, self.f_sent, self.f_came, self.keep, z_sent, z_came = bufs
        depth = place.depth
        self.sums = Line(place, self.keep, z_sent, z_came, send.at[pl.ds(2 + depth, depth)],
                         recv.at[pl.ds(2 + depth, depth + 1)])

    @staticmethod
    def sems(depth):
        return 2 + 2 * depth, 3 + 2 * depth

    @staticmethod
    def scratch(depth, rows, cols):
        block = lambda *lead: pltpu.VMEM(lead + (rows, cols), BF16)
        return [
            block(2, depth), block(2, depth), block(depth), block(depth),
            pltpu.VMEM((depth, rows, cols), F32), block(depth), block(depth + 1),
        ]

    def product(self, flips, store):
        at = self.place.flipped(*flips)
        pair = 2 * at["y"] + at["x"]
        one = 2 * pair + at["c"]
        rows, cols = self.keep.shape[1:]
        tile = 512

        def block(start, size):
            lanes = pl.ds(start, size)
            part = dot(self.lhs[one], self.rhs[:, lanes]) + dot(self.lhs_pair[pair], self.rhs_pair[:, lanes])
            for z in range(self.place.depth):
                store(z, lanes, part[z * rows : (z + 1) * rows])

        def loop(i, carry):
            block(pl.multiple_of(i * tile, tile), tile)
            return carry

        lax.fori_loop(0, cols // tile, loop, 0)
        if cols % tile:
            block(cols // tile * tile, cols % tile)

    def to_second(self, j):
        return remote(self.s_sent.at[j], self.s_came.at[j], self.send.at[j], self.recv.at[j],
                      self.place.to[self.second])

    def to_first(self, k):
        zk, n = self.place.near(k), 2 + k
        return remote(self.f_sent.at[zk], self.f_came.at[zk], self.send.at[n], self.recv.at[n],
                      self.place.to[self.first])

    def waves(self):
        return range(self.place.depth - 1, -1, -1)

    def send_second(self, j):
        def store(z, lanes, part):
            self.s_sent[j, z, :, lanes] = part.astype(BF16)

        self.product((self.second, self.first) if j == 0 else (self.second,), store)
        self.to_second(j).start()

    def send_first(self):
        self.to_second(0).wait_recv()

        def store(z, lanes, part):
            self.f_sent[z, :, lanes] = (part + self.s_came[0, z, :, lanes].astype(F32)).astype(BF16)

        self.product((self.first,), store)
        for k in self.waves():
            self.to_first(k).start()

    def hold(self):
        self.to_second(1).wait_recv()

        def store(z, lanes, part):
            self.keep[z, :, lanes] = part + self.s_came[1, z, :, lanes].astype(F32)

        self.product((), store)

    def step(self, k):
        self.to_first(k).wait_recv()
        zk = self.place.near(k)
        self.keep[zk] = self.keep[zk] + self.f_came[zk].astype(F32)
        self.sums.step(k)

    def finish(self):
        for j in (0, 1):
            self.to_second(j).wait_send()
        for k in self.waves():
            self.to_first(k).wait_send()
        self.sums.finish()


class SmallScatter:
    def __init__(self, place, src, c_came, half, x_came, keep, y_came, z_sent, z_came, send, recv):
        self.place, self.src, self.c_came, self.half = place, src, c_came, half
        self.x_came, self.keep, self.y_came = x_came, keep, y_came
        self.send, self.recv = send, recv
        depth = place.depth
        self.sums = Line(place, keep, z_sent, z_came, send.at[pl.ds(7, depth)],
                         recv.at[pl.ds(7, depth + 1)])

    @staticmethod
    def sems(depth):
        return 7 + depth, 8 + depth

    @staticmethod
    def scratch(depth, shape):
        block = lambda *lead: pltpu.VMEM(lead + shape, F32)
        return [
            block(2, 2, depth), block(2, 2, depth), block(2, depth), block(depth), block(depth),
            block(depth), block(depth + 1),
        ]

    def copy(self, n):
        p, own = self.place, self.place.own
        if n < 4:
            y, x = n // 2, n % 2
            src, dst, to = self.src.at[y, x, 1 - own["c"]], self.c_came.at[y, x], "c"
        elif n < 6:
            src, dst, to = self.half.at[n - 4, 1 - own["x"]], self.x_came.at[n - 4], "x"
        else:
            src, dst, to = self.half.at[1 - own["y"], own["x"]], self.y_came, "y"
        return remote(src, dst, self.send.at[n], self.recv.at[n], p.to[to])

    def stage(self, n):
        own = self.place.own
        if n == 0:
            for i in range(4):
                self.copy(i).start()
        elif n == 1:
            for i in range(4):
                self.copy(i).wait_recv()
            for y in (0, 1):
                for x in (0, 1):
                    self.half[y, x] = self.src[y, x, own["c"]] + self.c_came[y, x]
            for i in (4, 5):
                self.copy(i).start()
        elif n == 2:
            for i in (4, 5):
                self.copy(i).wait_recv()
            for y in (0, 1):
                self.half[y, own["x"]] = self.half[y, own["x"]] + self.x_came[y]
            self.copy(6).start()
        else:
            self.copy(6).wait_recv()
            self.keep[...] = self.half[own["y"], own["x"]] + self.y_came[...]

    def finish(self):
        for n in range(7):
            self.copy(n).wait_send()
        self.sums.finish()


def gather_kernel(
    depth, half, x_ref, small_src, wc_src, pc_ref, normed_ref, normt_ref, small_ref, wc_ref,
    hat_ref, edge_ref, buf_ref, edge_sem, load_sem, own_sem, send, recv,
):
    place = Place(depth)
    place.meet()
    seqs, seg, features = x_ref.shape
    width = wc_src.shape[1]
    lo, hi = pl.ds(0, half), pl.ds(half, width - half)
    every = slice(None)
    weights = lambda y, x, c: wc_ref.at[y, x, c]
    lanes = [
        Gather(place, small_src, lambda y, x, c: small_ref.at[y, x, c], "y", "x", send.at[0], recv.at[0]),
        Gather(place, wc_src.at[:, lo], weights, "y", "x", send.at[1], recv.at[1], (every, lo)),
        Gather(place, wc_src.at[:, hi], weights, "x", "y", send.at[2], recv.at[2], (every, hi)),
    ]
    early, late = lanes[:2], lanes[2:]
    own = place.own
    mine = (own["y"], own["x"], own["c"], place.z)
    copies = [
        pltpu.make_async_copy(src, dst.at[mine], own_sem.at[n])
        for n, (src, dst) in enumerate(((small_src, small_ref), (wc_src, wc_ref)))
    ]
    edge = remote(x_ref.at[:, pl.ds(seg - EDGE, EDGE)], edge_ref, edge_sem.at[0], edge_sem.at[1], place.right)

    def each(group, *steps):
        for name, k in steps:
            for lane in group:
                getattr(lane, name)(k)

    def load(at, n):
        cols = (lo, hi)[n]
        return pltpu.make_async_copy(
            wc_ref.at[at["y"], at["x"], :, :, :, cols], buf_ref.at[:, :, :, cols], load_sem.at[n]
        )

    rows = wc_src.shape[0]
    count = 2 * depth * rows

    def norm(flips):
        at = place.flipped(*flips)
        group = 2 * at["y"] + at["x"]
        here = pl.ds(pl.multiple_of(group * count, LANES), count)
        gain = sum(
            small_ref[at["y"], at["x"], c, z, : count // LANES] for c in (0, 1) for z in range(depth)
        )
        gain = jnp.concatenate([gain[i : i + 1] for i in range(count // LANES)], axis=1)
        for s in range(seqs):
            normed = (hat_ref[s, :, here] * gain).astype(BF16)
            normed_ref[s, :, here] = normed
            turned = normed[EDGE:].astype(F32).T.astype(BF16)
            for c in (0, 1):
                normt_ref[2 * group + c, :, s * seg : (s + 1) * seg] = turned[c * depth * rows : (c + 1) * depth * rows]

    def multiply(flips, n):
        at = place.flipped(*flips)
        here = pl.ds(pl.multiple_of((2 * at["y"] + at["x"]) * count, LANES), count)
        load(at, n).start()
        load(at, n).wait()
        first, last = ((0, half), (half, width))[n]
        tile = 4 * LANES
        for start in range(first, last, tile):
            cols = slice(start, min(start + tile, last))
            block = jnp.concatenate(
                [buf_ref[c, z, :, cols] for c in (0, 1) for z in range(depth)], axis=0
            )
            for s in range(seqs):
                part = dot(normed_ref[s, :, here], block)
                if flips == ():
                    pc_ref[s, :, cols] = part
                else:
                    pc_ref[s, :, cols] += part

    each(early, ("line", 0))
    pl.when(place.has_right)(edge.start)
    for copy in copies:
        copy.start()
    pl.when(place.has_left)(edge.wait_recv)

    @pl.when(jnp.logical_not(place.has_left))
    def _():
        edge_ref[...] = jnp.zeros_like(edge_ref)

    def scale_rows(s, start, rows_in, r, step):
        values = rows_in[s, r : r + step].astype(F32)
        mean = jnp.mean(values * values, axis=1, keepdims=True)
        hat_ref[s, start + r : start + r + step] = values * lax.rsqrt(mean + EPS)

    pieces = []
    for s in range(seqs):
        pieces.append((s, 0, edge_ref, 0, EDGE))
        pieces += [(s, EDGE, x_ref, r, 64) for r in range(0, seg, 64)]
    share = -(-len(pieces) // depth)
    for k in range(depth):
        for piece in pieces[k * share : (k + 1) * share]:
            scale_rows(*piece)
        if k + 1 < depth:
            each(early, ("line", k + 1))
        if k == depth - 2:
            each(late, ("line", 0))
    for copy in copies:
        copy.wait()
    each(early, ("core", 0))
    for k in range(1, depth):
        each(late, ("line", k))
    each(late, ("core", 0))
    for k in range(depth):
        each(early, ("from_first", k), ("from_second", k))
    each(early, ("core", 1), ("core", 2))
    each(late, ("from_first", 0), ("from_first", 1))
    each(early, ("whole", 0))
    norm(())
    multiply((), 0)
    for k in range(2, depth):
        each(late, ("from_first", k))
    each(early, ("whole", 1))
    norm(("y",))
    multiply(("y",), 0)
    for k in range(depth):
        each(late, ("from_second", k))
    each(late, ("core", 1), ("core", 2))
    each(early, ("whole", 2))
    norm(("x",))
    multiply(("x",), 0)
    each(late, ("whole", 0))
    multiply((), 1)
    for k in range(depth - 1):
        each(lanes, ("from_both", k))
    each(late, ("whole", 1), ("whole", 2))
    multiply(("y",), 1)
    multiply(("x",), 1)
    each(lanes, ("from_both", depth - 1))
    each(early, ("whole", 3))
    norm(("y", "x"))
    multiply(("y", "x"), 0)
    each(late, ("whole", 3))
    multiply(("y", "x"), 1)
    for lane in lanes:
        lane.finish()
    pl.when(place.has_right)(edge.wait_send)


def gather_project(x, small, wc, depth):
    shape = jax.ShapeDtypeStruct
    seqs, seg, features = x.shape
    slots = (2, 2, 2, depth)
    sends, receives = Gather.sems(depth)
    width = wc.shape[1]
    half = width // 2 // LANES * LANES
    anywhere, vmem = pl.BlockSpec(memory_space=pl.ANY), pl.BlockSpec(memory_space=pltpu.VMEM)
    dma = pltpu.SemaphoreType.DMA
    return pl.pallas_call(
        functools.partial(gather_kernel, depth, half),
        in_specs=[vmem, vmem, anywhere],
        out_specs=[vmem, vmem, vmem, vmem, anywhere],
        out_shape=[
            shape((seqs, seg + EDGE, width), F32),
            shape((seqs, seg + EDGE, features), BF16),
            shape((8, depth * wc.shape[0], seqs * seg), BF16),
            shape(slots + small.shape, F32),
            shape(slots + wc.shape, BF16),
        ],
        scratch_shapes=[
            pltpu.VMEM((seqs, seg + EDGE, features), F32),
            pltpu.VMEM((seqs, EDGE, features), BF16),
            pltpu.VMEM((2, depth) + wc.shape, BF16),
            dma((2,)), dma((2,)), dma((2,)), dma((3, sends)), dma((3, receives)),
        ],
        compiler_params=pltpu.CompilerParams(
            collective_id=0, has_side_effects=True, vmem_limit_bytes=VMEM_LIMIT
        ),
        name="gather_project",
    )(x, small, wc)


def fwd_a_kernel(
    head_dim, pc_ref, w_ref, b_ref, raw_ref, sb_ref, dl_ref,
    x_ref, bc_ref, dt_ref, cum_ref, cumt_ref, loc0_ref, seg_ref, tot_ref, bt_ref,
):
    step = pl.program_id(0)
    seqs = pc_ref.shape[0]
    seg = pc_ref.shape[1] - EDGE
    chunks = seg // CHUNK
    w, b = w_ref[...], b_ref[...]

    def acts_of(s):
        pre = causal_conv(pc_ref[s], w, b, seg)
        return pre * sigmoid(pre)

    @pl.when(step == 0)
    def _():
        row = lax.broadcasted_iota(jnp.int32, (CHUNK, CHUNK), 0)
        col = lax.broadcasted_iota(jnp.int32, (CHUNK, CHUNK), 1)
        tri = (col <= row).astype(F32)
        rate = -jnp.exp(dl_ref[...])
        for s in range(seqs):
            acts = acts_of(s)
            bc_ref[s * seg : (s + 1) * seg] = acts
            for c in range(chunks):
                q = s * chunks + c
                rows = slice(q * CHUNK, (q + 1) * CHUNK)
                bt_ref[q] = acts[c * CHUNK : (c + 1) * CHUNK, :LANES].T.astype(BF16)
                dt = softplus(raw_ref[s, EDGE + c * CHUNK : EDGE + (c + 1) * CHUNK] + sb_ref[...])
                cum = LOG2E * jnp.dot(tri, dt * rate, precision=HIGH, preferred_element_type=F32)
                dt_ref[rows] = dt
                cum_ref[rows] = cum
                cumt_ref[:, rows] = cum.T

    @pl.when(step > 0)
    def _():
        heads = GROUP // head_dim
        first = (step - 1) * heads
        cumg = lane_shift(cum_ref[...], first)
        dtg = lane_shift(dt_ref[...], first)
        for s in range(seqs):
            x = acts_of(s)
            x_ref[s * seg : (s + 1) * seg] = x
            state, total = None, None
            for c in range(chunks):
                q = s * chunks + c
                rows = slice(q * CHUNK, (q + 1) * CHUNK)
                ce = spread_all(cumg[rows], heads, head_dim)
                de = spread_all(dtg[rows], heads, head_dim)
                end = ce[CHUNK - 1 : CHUNK]
                uw = x[c * CHUNK : (c + 1) * CHUNK] * de * jnp.exp2(end - ce)
                loc = dot(bt_ref[q], uw.astype(BF16))
                tot = jnp.exp2(end)
                tot_ref[q : q + 1] = tot
                if c == 0:
                    loc0_ref[s] = loc
                    state, total = loc, tot
                else:
                    state, total = tot * state + loc, tot * total
            seg_ref[s] = state.astype(BF16)
            tot_ref[seqs * chunks + s : seqs * chunks + s + 1] = total


def fwd_a(pc, w, b, sb, dl, inner, head_dim):
    seqs, rows, cols = pc.shape
    seg = rows - EDGE
    tokens = seqs * seg
    groups = inner // GROUP
    state = LANES
    chunks = tokens // CHUNK
    at = lambda i: (i + groups) % (groups + 1)
    back = lambda i: jnp.maximum(i - 1, 0)
    return pl.pallas_call(
        functools.partial(fwd_a_kernel, head_dim),
        grid=(groups + 1,),
        in_specs=[
            pl.BlockSpec((seqs, rows, GROUP), lambda i: (0, 0, at(i))),
            pl.BlockSpec((w.shape[0], GROUP), lambda i: (0, at(i))),
            pl.BlockSpec((1, GROUP), lambda i: (0, at(i))),
            pl.BlockSpec((seqs, rows, LANES), lambda i: (0, 0, cols // LANES - 1)),
            whole((1, LANES)),
            whole((1, LANES)),
        ],
        out_specs=[
            pl.BlockSpec((tokens, GROUP), lambda i: (0, back(i))),
            whole((tokens, GROUP)),
            whole((tokens, LANES)),
            whole((tokens, LANES)),
            whole((LANES, tokens)),
            pl.BlockSpec((seqs, state, GROUP), lambda i: (0, 0, back(i))),
            pl.BlockSpec((seqs, state, GROUP), lambda i: (0, 0, back(i))),
            pl.BlockSpec((8, GROUP), lambda i: (0, back(i))),
        ],
        out_shape=[
            jax.ShapeDtypeStruct((tokens, inner), F32),
            jax.ShapeDtypeStruct((tokens, GROUP), F32),
            jax.ShapeDtypeStruct((tokens, LANES), F32),
            jax.ShapeDtypeStruct((tokens, LANES), F32),
            jax.ShapeDtypeStruct((LANES, tokens), F32),
            jax.ShapeDtypeStruct((seqs, state, inner), F32),
            jax.ShapeDtypeStruct((seqs, state, inner), BF16),
            jax.ShapeDtypeStruct((8, inner), F32),
        ],
        scratch_shapes=[pltpu.VMEM((chunks, LANES, CHUNK), BF16)],
        compiler_params=params(),
        name="conv_states",
    )(pc, w, b, pc, sb, dl)


def fwd_b_kernel(
    head_dim, x_ref, bc_ref, dt_ref, cum_ref, cumt_ref, s0_ref, loc0_ref, tot_ref, skip_ref,
    mixed_ref, s1_ref, cb_ref,
):
    step = pl.program_id(0)
    seqs = s0_ref.shape[0]
    chunks = x_ref.shape[0] // CHUNK // seqs
    heads = GROUP // head_dim

    @pl.when(step == 0)
    def _():
        for q in range(seqs * chunks):
            rows = slice(q * CHUNK, (q + 1) * CHUNK)
            cb_ref[q] = nt(bc_ref[rows, LANES:].astype(BF16), bc_ref[rows, :LANES].astype(BF16))

    first = step * heads
    cumg = lane_shift(cum_ref[...], first)
    dtg = lane_shift(dt_ref[...], first)
    cumr = head_rows(cumt_ref, first)
    row = lax.broadcasted_iota(jnp.int32, (CHUNK, CHUNK), 0)
    col = lax.broadcasted_iota(jnp.int32, (CHUNK, CHUNK), 1)
    causal = col <= row
    skip = skip_ref[...]
    for s in range(seqs):
        start = s0_ref[s]
        for c in range(chunks):
            q = s * chunks + c
            rows = slice(q * CHUNK, (q + 1) * CHUNK)
            x = x_ref[rows]
            ce = spread_all(cumg[rows], heads, head_dim)
            de = spread_all(dtg[rows], heads, head_dim)
            ub = (x * de).astype(BF16)
            cb = cb_ref[q]
            parts = []
            for j in range(0, heads, 2):
                mats = []
                for h in (j, j + 1):
                    there = jnp.broadcast_to(cumg[rows, h : h + 1], (CHUNK, CHUNK))
                    here = cumr[h : h + 1, rows]
                    decay = jnp.exp2(jnp.where(causal, there - here, -jnp.inf))
                    mats.append((decay * cb).astype(BF16))
                pair = ub[:, j * head_dim : (j + 2) * head_dim]
                parts.append(dot(jnp.concatenate(mats, axis=1), block_diagonal(pair, head_dim)))
            y = jnp.concatenate(parts, axis=1)
            y = y + jnp.exp2(ce) * dot(bc_ref[rows, LANES:].astype(BF16), start)
            mixed_ref[rows] = y + skip * x
            if c == 0:
                start = (tot_ref[q : q + 1] * start.astype(F32) + loc0_ref[s]).astype(BF16)
                s1_ref[s] = start


def fwd_b(x, bc, dt, cum, cumt, s0, loc0, tot, skip, head_dim):
    tokens, inner = x.shape
    seqs, state, _ = s0.shape
    groups = inner // GROUP
    wide = pl.BlockSpec((tokens, GROUP), lambda i: (0, i))
    states = pl.BlockSpec((seqs, state, GROUP), lambda i: (0, 0, i))
    return pl.pallas_call(
        functools.partial(fwd_b_kernel, head_dim),
        grid=(groups,),
        in_specs=[
            wide, whole(bc.shape), whole(dt.shape), whole(cum.shape), whole(cumt.shape),
            states, states,
            pl.BlockSpec((8, GROUP), lambda i: (0, i)),
            pl.BlockSpec((1, GROUP), lambda i: (0, i)),
        ],
        out_specs=[wide, states],
        out_shape=[
            jax.ShapeDtypeStruct((tokens, inner), F32),
            jax.ShapeDtypeStruct((seqs, state, inner), BF16),
        ],
        scratch_shapes=[pltpu.VMEM((tokens // CHUNK, CHUNK, CHUNK), F32)],
        compiler_params=params(),
        name="scan_outputs",
    )(x, bc, dt, cum, cumt, s0, loc0, tot, skip)


def halves(v):
    high = v.astype(BF16)
    return high, (v - high.astype(F32)).astype(BF16)


def dot_pairs(a, b, dims=((1,), (0,))):
    (ah, al), (bh, bl) = halves(a), halves(b)
    return dot(ah, bh, dims) + (dot(al, bh, dims) + dot(ah, bl, dims))


def dot_pair(a, b, dims=((1,), (0,))):
    high, low = halves(a)
    return dot(high, b, dims) + dot(low, b, dims)


def nt_exact(a, b):
    return lax.dot_general(a, b, (((1,), (1,)), ((), ())), precision=HIGH, preferred_element_type=F32)


class Chain:
    def __init__(self, place, came, sent, send, recv, backward):
        self.came, self.sent, self.send, self.recv = came, sent, send, recv
        self.gets, self.gives = place.has_left, place.has_right
        self.to = place.left if backward else place.right
        if backward:
            self.gets, self.gives = self.gives, self.gets
        self.behind = place.depth - 1 - place.z if backward else place.z

    def copy(self, g):
        return remote(self.sent.at[g], self.came.at[g], self.send.at[g], self.recv.at[g], self.to)

    def step(self, g, total, own):
        pl.when(self.gets)(lambda: self.copy(g).wait_recv())

        @pl.when(jnp.logical_not(self.gets))
        def _():
            self.came[g] = jnp.zeros(self.came.shape[1:], self.came.dtype)

        self.sent[g] = (total * self.came[g].astype(F32) + own).astype(BF16)
        pl.when(self.gives)(lambda: self.copy(g).start())

    def finish(self):
        groups = self.came.shape[0]

        def one(g, carry):
            self.copy(g).wait_send()
            return carry

        @pl.when(self.gives)
        def _():
            lax.fori_loop(0, groups, one, 0)


def scan_forward_kernel(
    depth, head_dim, groups,
    pc_ref, w_ref, b_ref, raw_ref, sb_ref, dl_ref, skip_ref, normed_ref, cot_ref, wi_src, wo_src, nt_src,
    bc_ref, dt_ref, cum_ref, cumt_ref, mixed_ref, s0_ref, s1_ref, s2_ref, tot_ref, z_out, dno_out, wg_ref, wo_ref, nt_pair, cot_pair,
    bt_ref, cb_ref, x_ring, loc_ring, seg_ring, tot_ring, came, sent,
    z_ref, dno_ref, wg_buf, wo_buf, chain_send, chain_recv, own_sem, load_sem, out_sem, send, recv,
    pair_send, pair_recv,
):
    step = pl.program_id(0)
    lag = depth - 1
    seqs = pc_ref.shape[0]
    seg = pc_ref.shape[1] - EDGE
    chunks = seg // CHUNK
    heads = GROUP // head_dim
    w, b = w_ref[...], b_ref[...]
    place = Place(depth)
    chain = Chain(place, came, sent, chain_send, chain_recv, False)
    wg_src = wi_src.at[:, pl.ds(0, z_ref.shape[1])]
    gate = Gather(place, wg_src, lambda y, x, c: wg_ref.at[y, x, c], "y", "x", send.at[0], recv.at[0])
    out = Gather(place, wo_src, lambda y, x, c: wo_ref.at[y, x, c], "x", "y", send.at[1], recv.at[1])
    mine = (place.own["y"], place.own["x"], place.own["c"], place.z)
    copies = [
        pltpu.make_async_copy(wg_src, wg_ref.at[mine], own_sem.at[0]),
        pltpu.make_async_copy(wo_src, wo_ref.at[mine], own_sem.at[1]),
    ]
    pairs = pair_copies(place, ((nt_src, nt_pair),), ((cot_ref, cot_pair),), pair_send, pair_recv)

    def waves(*steps):
        for lane, name, k in steps:
            getattr(lane, name)(k)

    def acts_of(s):
        pre = causal_conv(pc_ref[s], w, b, seg)
        return pre * sigmoid(pre)

    @pl.when(step == 0)
    def _():
        place.meet()
        waves((gate, "line", 0))
        for copy in copies + pairs:
            copy.start()
        row = lax.broadcasted_iota(jnp.int32, (CHUNK, CHUNK), 0)
        col = lax.broadcasted_iota(jnp.int32, (CHUNK, CHUNK), 1)
        tri = (col <= row).astype(F32)
        rate = -jnp.exp(dl_ref[...])
        for s in range(seqs):
            acts = acts_of(s)
            bc_ref[s * seg : (s + 1) * seg] = acts
            for c in range(chunks):
                q = s * chunks + c
                rows = slice(q * CHUNK, (q + 1) * CHUNK)
                b_proj = acts[c * CHUNK : (c + 1) * CHUNK, :LANES]
                c_proj = acts[c * CHUNK : (c + 1) * CHUNK, LANES:]
                bt_ref[q] = b_proj.T
                cb_ref[q] = nt_exact(c_proj, b_proj)
                dt = softplus(raw_ref[s, EDGE + c * CHUNK : EDGE + (c + 1) * CHUNK] + sb_ref[...])
                cum = LOG2E * jnp.dot(tri, dt * rate, precision=HIGH, preferred_element_type=F32)
                dt_ref[rows] = dt
                cum_ref[rows] = cum
                cumt_ref[:, rows] = cum.T

    @pl.when((step > 0) & (step <= groups))
    def _():
        g = step - 1
        at = lax.rem(g, lag + 1)
        first = g * heads
        cumg = lane_shift(cum_ref[...], first)
        dtg = lane_shift(dt_ref[...], first)
        for s in range(seqs):
            x = acts_of(s)
            x_ring[at, s * seg : (s + 1) * seg] = x
            state, total = None, None
            for c in range(chunks):
                q = s * chunks + c
                rows = slice(q * CHUNK, (q + 1) * CHUNK)
                ce = spread_all(cumg[rows], heads, head_dim)
                de = spread_all(dtg[rows], heads, head_dim)
                end = ce[CHUNK - 1 : CHUNK]
                uw = x[c * CHUNK : (c + 1) * CHUNK] * de * jnp.exp2(end - ce)
                loc = dot_pairs(bt_ref[q], uw)
                tot = jnp.exp2(end)
                tot_ring[at, q : q + 1] = tot
                if c == 0:
                    loc_ring[at, s] = loc
                    state, total = loc, tot
                else:
                    state, total = tot * state + loc, tot * total
            seg_ring[at, s] = state
            tot_ring[at, seqs * chunks + s : seqs * chunks + s + 1] = total

    handed = step - 1 - chain.behind

    @pl.when((handed >= 0) & (handed < groups))
    def _():
        at = lax.rem(handed, lag + 1)
        totals = tot_ring[at, seqs * chunks : seqs * chunks + seqs]
        chain.step(handed, totals[:, None, :], seg_ring[at])

    @pl.when(step > lag)
    def _():
        g = step - 1 - lag
        at = lax.rem(g, lag + 1)
        first = g * heads
        cumg = lane_shift(cum_ref[...], first)
        dtg = lane_shift(dt_ref[...], first)
        cumr = head_rows(cumt_ref, first)
        row = lax.broadcasted_iota(jnp.int32, (CHUNK, CHUNK), 0)
        col = lax.broadcasted_iota(jnp.int32, (CHUNK, CHUNK), 1)
        causal = col <= row
        skip = skip_ref[...]
        s0_ref[...] = came[g]
        s2_ref[...] = sent[g]
        tot_ref[...] = tot_ring[at]
        for s in range(seqs):
            start = came[g, s]
            for c in range(chunks):
                q = s * chunks + c
                rows = slice(q * CHUNK, (q + 1) * CHUNK)
                x = x_ring[at, rows]
                ce = spread_all(cumg[rows], heads, head_dim)
                de = spread_all(dtg[rows], heads, head_dim)
                ub = (x * de).astype(BF16)
                cb = cb_ref[q]
                parts = []
                for j in range(0, heads, 2):
                    mats = []
                    for h in (j, j + 1):
                        there = jnp.broadcast_to(cumg[rows, h : h + 1], (CHUNK, CHUNK))
                        here = cumr[h : h + 1, rows]
                        decay = jnp.exp2(jnp.where(causal, there - here, -jnp.inf))
                        mats.append((decay * cb).astype(BF16))
                    pair = ub[:, j * head_dim : (j + 2) * head_dim]
                    parts.append(dot(jnp.concatenate(mats, axis=1), block_diagonal(pair, head_dim)))
                y = jnp.concatenate(parts, axis=1)
                y = y + jnp.exp2(ce) * dot(bc_ref[rows, LANES:].astype(BF16), start)
                mixed_ref[rows] = y + skip * x
                if c == 0:
                    later = tot_ring[at, q : q + 1] * start.astype(F32) + loc_ring[at, s]
                    s1_ref[s] = later
                    start = later.astype(BF16)

    every = range(depth)

    def both(lane, *waves_of):
        return [(lane, name, k) for k in waves_of for name in ("from_first", "from_second")]

    beside = {
        3: [(gate, "line", 1)],
        6: [(gate, "line", 2), (out, "line", 0)],
        9: [(gate, "line", 3), *both(gate, 0)],
        11: [(out, "line", 1), *both(gate, 1)],
        13: both(gate, 2),
    }
    for at, steps in beside.items():
        pl.when(step == at)(lambda: waves(*steps))

    @pl.when(step == 9)
    def _():
        for copy in copies:
            copy.wait()
        waves((gate, "core", 0))

    @pl.when(step == groups + lag)
    def _():
        rows = 2 * depth * wi_src.shape[0]
        tile = 4 * LANES
        size = dno_ref.shape[1] // 8
        by_group = ((), ("y",), ("x",), ("y", "x"))

        def load(lane, g):
            src, buf = (wg_ref, wg_buf) if lane is gate else (wo_ref, wo_buf)
            at = place.flipped(*by_group[g])
            n = g % 2
            return pltpu.make_async_copy(src.at[at["y"], at["x"]], buf.at[n], load_sem.at[int(lane is out), n])

        def ready(lane, g):
            lane.whole(g if g in (0, 3) or lane is gate else 3 - g)
            load(lane, g).start()

        def group_of(g):
            at = place.flipped(*by_group[g])
            return 2 * at["y"] + at["x"]

        def gate_product(g):
            load(gate, g).wait()
            here = pl.ds(pl.multiple_of(group_of(g) * rows, LANES), rows)
            for start in range(0, z_ref.shape[1], tile):
                cols = slice(start, start + tile)
                block = jnp.concatenate(
                    [wg_buf[g % 2, c, z, :, cols] for c in (0, 1) for z in every], axis=0
                )
                for s in range(seqs):
                    part = dot(normed_ref[s, EDGE:, here], block)
                    at_rows = slice(s * seg, (s + 1) * seg)
                    if g == 0:
                        z_ref[at_rows, cols] = part
                    else:
                        z_ref[at_rows, cols] += part

        def out_product(g):
            load(out, g).wait()
            for c in (0, 1):
                block = jnp.concatenate([wo_buf[g % 2, c, z] for z in every], axis=0)
                cols = pl.ds(pl.multiple_of((2 * group_of(g) + c) * size, LANES), size)
                dno_ref[:, cols] = nt(cot_ref[...], block)
            dno_copy(g).start()

        def dno_copy(g):
            cols = pl.ds(pl.multiple_of(group_of(g) * 2 * size, LANES), 2 * size)
            return pltpu.make_async_copy(dno_ref.at[:, cols], dno_out.at[:, cols], out_sem.at[g])

        last = depth - 1
        waves((out, "line", 2), *both(gate, 3), (gate, "core", 1), (gate, "core", 2))
        waves((out, "from_first", 0))
        ready(gate, 0)
        ready(gate, 1)
        gate_product(0)
        waves((out, "line", 3), (out, "core", 0), (out, "from_first", 1))
        ready(gate, 2)
        gate_product(1)
        waves((out, "from_first", 2), (out, "from_second", 0), (out, "from_second", 1), (gate, "from_both", 0))
        ready(out, 0)
        gate_product(2)
        waves((out, "from_first", 3), (out, "from_second", 2), (out, "from_second", 3))
        waves((out, "core", 1), (out, "core", 2), (gate, "from_both", 1))
        ready(out, 1)
        out_product(0)
        waves((gate, "from_both", 2), (out, "from_both", 0), (out, "from_both", 1))
        ready(out, 2)
        out_product(1)
        waves((out, "from_both", 2))
        out_product(2)
        waves((gate, "from_both", last), (out, "from_both", last))
        ready(gate, 3)
        ready(out, 3)
        gate_product(3)
        z_copy = pltpu.make_async_copy(z_ref, z_out, out_sem.at[4])
        z_copy.start()
        out_product(3)
        for lane in (gate, out):
            lane.finish()
        chain.finish()
        for g in range(4):
            dno_copy(g).wait()
        z_copy.wait()
        for copy in pairs:
            copy.wait()


def scan_forward(pc, w, b, sb, dl, skip, normed, cot, w_in, wo, normed_t, inner, head_dim, depth):
    seqs, rows, cols = pc.shape
    tokens = seqs * (rows - EDGE)
    groups = inner // GROUP
    lag = depth - 1
    chunks = tokens // CHUNK
    shape, dma = jax.ShapeDtypeStruct, pltpu.SemaphoreType.DMA
    into = lambda i: jnp.where(i == 0, groups, jnp.minimum(i - 1, groups - 1))
    out = lambda i: jnp.maximum(i - 1 - lag, 0)
    states = pl.BlockSpec((seqs, LANES, GROUP), lambda i: (0, 0, out(i)))
    anywhere = pl.BlockSpec(memory_space=pl.ANY)
    sends, receives = Gather.sems(depth)
    slots = (2, 2, 2, depth)
    ring = lambda *dims: pltpu.VMEM((lag + 1,) + dims, F32)
    link = pltpu.VMEM((groups, seqs, LANES, GROUP), BF16)
    once = lambda v: pl.BlockSpec(v.shape, lambda i: (0,) * v.ndim, pipeline_mode=pl.Buffered(1))
    return pl.pallas_call(
        functools.partial(scan_forward_kernel, depth, head_dim, groups),
        grid=(groups + 1 + lag,),
        in_specs=[
            pl.BlockSpec((seqs, rows, GROUP), lambda i: (0, 0, into(i))),
            pl.BlockSpec((w.shape[0], GROUP), lambda i: (0, into(i))),
            pl.BlockSpec((1, GROUP), lambda i: (0, into(i))),
            pl.BlockSpec((seqs, rows, LANES), lambda i: (0, 0, cols // LANES - 1)),
            whole((1, LANES)),
            whole((1, LANES)),
            pl.BlockSpec((1, GROUP), lambda i: (0, out(i))),
            once(normed),
            once(cot),
            anywhere,
            anywhere,
            anywhere,
        ],
        out_specs=[
            whole((tokens, GROUP)),
            whole((tokens, LANES)),
            whole((tokens, LANES)),
            whole((LANES, tokens)),
            pl.BlockSpec((tokens, GROUP), lambda i: (0, out(i))),
            states, states, states,
            pl.BlockSpec((8, GROUP), lambda i: (0, out(i))),
            anywhere,
            anywhere,
            anywhere,
            anywhere,
            anywhere,
            anywhere,
        ],
        out_shape=[
            shape((tokens, GROUP), F32),
            shape((tokens, LANES), F32),
            shape((tokens, LANES), F32),
            shape((LANES, tokens), F32),
            shape((tokens, inner), F32),
            shape((seqs, LANES, inner), BF16),
            shape((seqs, LANES, inner), F32),
            shape((seqs, LANES, inner), BF16),
            shape((8, inner), F32),
            shape((tokens, inner), F32),
            shape((tokens, inner), F32),
            shape(slots + (w_in.shape[0], inner), BF16),
            shape(slots + wo.shape, BF16),
            shape((4,) + normed_t.shape[1:], BF16),
            shape(cot.shape, BF16),
        ],
        scratch_shapes=[
            pltpu.VMEM((chunks, LANES, CHUNK), F32),
            pltpu.VMEM((chunks, CHUNK, CHUNK), F32),
            ring(tokens, GROUP), ring(seqs, LANES, GROUP), ring(seqs, LANES, GROUP), ring(8, GROUP),
            link, link,
            pltpu.VMEM((tokens, inner), F32), pltpu.VMEM((tokens, inner), F32),
            pltpu.VMEM((2, 2, depth, w_in.shape[0], inner), BF16), pltpu.VMEM((2, 2, depth) + wo.shape, BF16),
            dma((groups,)), dma((groups,)), dma((2,)), dma((2, 2)), dma((5,)), dma((2, sends)), dma((2, receives)),
            dma((5,)), dma((5,)),
        ],
        compiler_params=pltpu.CompilerParams(
            dimension_semantics=("arbitrary",), collective_id=3, has_side_effects=True,
            vmem_limit_bytes=VMEM_LIMIT,
        ),
        name="scan_forward",
    )(pc, w, b, pc, sb, dl, skip, normed, cot, w_in, wo, normed_t)


def mid_kernel(
    z_ref, dno_ref, mixed_ref, wo_ref, gain_ref, in_ref, not_ref, out_ref, dm_ref, dz_ref, gg_ref, acc_ref,
):
    step = pl.program_id(0)
    inner = mixed_ref.shape[1]
    tiles, tile = not_ref.shape[0], not_ref.shape[1]

    @pl.when(step == 0)
    def _():
        gg_ref[...] = jnp.zeros_like(gg_ref)

    def lanes_of(i):
        return pl.ds(pl.multiple_of(i * tile, tile), tile)

    def fold(v):
        total = v[:, :LANES]
        for k in range(LANES, tile, LANES):
            total = total + v[:, k : k + LANES]
        return total

    def one(i, sums):
        sq, hg = sums
        at = lanes_of(i)
        z = z_ref[:, at]
        g = mixed_ref[:, at] * z * sigmoid(z)
        return sq + fold(g * g), hg + fold(dno_ref[:, at] * gain_ref[:, at] * g)

    zero = jnp.zeros((mixed_ref.shape[0], LANES), F32)
    sq, hg = lax.fori_loop(0, tiles, one, (zero, zero))
    scale = lax.rsqrt(jnp.sum(sq, axis=1, keepdims=True) / inner + EPS)
    pull = scale * scale * scale * (jnp.sum(hg, axis=1, keepdims=True) / inner)
    acc_ref[...] = in_ref[...].astype(F32)

    def two(i, carry):
        at = lanes_of(i)
        z, mixed, dno, gain = z_ref[:, at], mixed_ref[:, at], dno_ref[:, at], gain_ref[:, at]
        sig = sigmoid(z)
        act = z * sig
        g = mixed * act
        gs = g * scale
        no = gs * gain
        not_ref[i] = no.T.astype(BF16)
        acc_ref[...] += dot(no.astype(BF16), wo_ref[at, :])
        gg_ref[:, at] += jnp.sum(dno * gs, axis=0, keepdims=True)
        dg = scale * (dno * gain) - g * pull
        dm_ref[:, at] = dg * act
        dz_ref[:, at] = (dg * mixed * (sig * (1.0 + z * (1.0 - sig)))).astype(BF16)
        return carry

    lax.fori_loop(0, tiles, two, 0)
    out_ref[...] = acc_ref[...].astype(BF16)


def mid(z, dno, mixed, wo, gain, inputs, tiles):
    tokens, inner = mixed.shape
    width = inputs.shape[1]
    tile = inner // tiles
    narrow = pl.BlockSpec((CHUNK, width), lambda i: (i, 0))
    wide = pl.BlockSpec((CHUNK, inner), lambda i: (i, 0))
    once = lambda v: pl.BlockSpec(v.shape, lambda i: (0,) * v.ndim, pipeline_mode=pl.Buffered(1))
    return pl.pallas_call(
        mid_kernel,
        grid=(tokens // CHUNK,),
        in_specs=[wide, wide, wide, once(wo), whole((1, inner)), narrow],
        out_specs=[
            pl.BlockSpec((tiles, tile, CHUNK), lambda i: (0, 0, i)), narrow, wide, wide,
            whole((1, inner)),
        ],
        out_shape=[
            jax.ShapeDtypeStruct((tiles, tile, tokens), BF16),
            jax.ShapeDtypeStruct((tokens, width), BF16),
            jax.ShapeDtypeStruct((tokens, inner), F32),
            jax.ShapeDtypeStruct((tokens, inner), BF16),
            jax.ShapeDtypeStruct((1, inner), F32),
        ],
        scratch_shapes=[pltpu.VMEM((CHUNK, width), F32)],
        compiler_params=params(),
        name="gate_norm_project",
    )(z, dno, mixed, wo, gain, inputs)


def bwd_a_kernel(head_dim, seqs, dm_ref, bc_ref, cum_ref, tot_ref, seg_ref, ct_ref):
    step = pl.program_id(0)
    chunks = dm_ref.shape[0] // CHUNK // seqs
    heads = GROUP // head_dim

    @pl.when(step == 0)
    def _():
        for q in range(seqs * chunks):
            ct_ref[q] = bc_ref[q * CHUNK : (q + 1) * CHUNK, LANES:].T.astype(BF16)

    cumg = lane_shift(cum_ref[...], step * heads)
    for s in range(seqs):
        state = None
        for c in range(chunks - 1, -1, -1):
            q = s * chunks + c
            rows = slice(q * CHUNK, (q + 1) * CHUNK)
            ey = jnp.exp2(spread_all(cumg[rows], heads, head_dim)) * dm_ref[rows]
            loc = dot(ct_ref[q], ey.astype(BF16))
            state = loc if state is None else tot_ref[q : q + 1] * state + loc
        seg_ref[s] = state.astype(BF16)


def bwd_a(dm, bc, cum, tot, seqs, head_dim):
    tokens, inner = dm.shape
    return pl.pallas_call(
        functools.partial(bwd_a_kernel, head_dim, seqs),
        grid=(inner // GROUP,),
        in_specs=[
            pl.BlockSpec((tokens, GROUP), lambda i: (0, i)), whole(bc.shape), whole(cum.shape),
            pl.BlockSpec((8, GROUP), lambda i: (0, i)),
        ],
        out_specs=pl.BlockSpec((seqs, LANES, GROUP), lambda i: (0, 0, i)),
        out_shape=jax.ShapeDtypeStruct((seqs, LANES, inner), BF16),
        scratch_shapes=[pltpu.VMEM((tokens // CHUNK, LANES, CHUNK), BF16)],
        compiler_params=params(),
        name="adjoint_states",
    )(dm, bc, cum, tot)


def bwd_b_kernel(
    head_dim, groups, pc_ref, w_ref, b_ref, raw_ref, sb_ref, dl_ref, bc_ref, dt_ref, cum_ref, cumt_ref,
    dm_ref, mixed_ref, s0_ref, s1_ref, s2_ref, g_ref, tot_ref, skip_ref,
    dc_ref, tail_ref, edge_ref, gw_ref, gb_ref, gskip_ref, draw_ref, hsum_ref,
    cbt_ref, dcbt_ref, db_acc, dc_acc, r1_ref, r2_ref, dtot_ref,
):
    step = pl.program_id(0)
    seqs = pc_ref.shape[0]
    seg = pc_ref.shape[1] - EDGE
    chunks = seg // CHUNK
    heads = GROUP // head_dim
    w, b = w_ref[...], b_ref[...]
    taps = w.shape[0]

    @pl.when(step == 0)
    def _():
        for q in range(seqs * chunks):
            rows = slice(q * CHUNK, (q + 1) * CHUNK)
            cbt_ref[q] = nt(bc_ref[rows, :LANES].astype(BF16), bc_ref[rows, LANES:].astype(BF16))
        dcbt_ref[...] = jnp.zeros_like(dcbt_ref)
        db_acc[...] = jnp.zeros_like(db_acc)
        dc_acc[...] = jnp.zeros_like(dc_acc)
        r1_ref[...] = jnp.zeros_like(r1_ref)
        r2_ref[...] = jnp.zeros_like(r2_ref)
        dtot_ref[...] = jnp.zeros_like(dtot_ref)

    def conv_back(s, ext, pre, sig, d_act):
        d_pre = d_act * (sig * (1.0 + pre * (1.0 - sig)))
        zero = jnp.zeros((EDGE, d_pre.shape[1]), F32)
        padded = jnp.concatenate([zero, d_pre, zero], axis=0)
        total = None
        for k in range(taps):
            at = taps - 1 - k
            term = w[k : k + 1] * padded[at : at + seg + EDGE]
            total = term if total is None else total + term
        edge_ref[s] = total[:EDGE]
        dc_ref[s * seg : (s + 1) * seg] = total[EDGE:].astype(BF16)
        tail_ref[s] = total[seg:]
        for k in range(taps):
            at = EDGE - (taps - 1) + k
            grad = jnp.sum(ext[at : at + seg] * d_pre, axis=0, keepdims=True)
            gw_ref[k : k + 1] = grad if s == 0 else gw_ref[k : k + 1] + grad
        grad = jnp.sum(d_pre, axis=0, keepdims=True)
        gb_ref[...] = grad if s == 0 else gb_ref[...] + grad

    def by_head(value, pick):
        high = value.astype(BF16)
        return dot(high, pick) + dot((value - high.astype(F32)).astype(BF16), pick)

    @pl.when(step < groups)
    def _():
        first = step * heads
        cumg = lane_shift(cum_ref[...], first)
        dtg = lane_shift(dt_ref[...], first)
        cumr = head_rows(cumt_ref, first)
        row = lax.broadcasted_iota(jnp.int32, (CHUNK, CHUNK), 0)
        col = lax.broadcasted_iota(jnp.int32, (CHUNK, CHUNK), 1)
        causal = row <= col
        lane = lax.broadcasted_iota(jnp.int32, (GROUP, LANES), 0)
        head = lax.broadcasted_iota(jnp.int32, (GROUP, LANES), 1)
        pick = (head == first + lane // head_dim).astype(BF16)
        skip = skip_ref[...]
        grad_skip = None
        for s in range(seqs):
            ext = pc_ref[s]
            pre = causal_conv(ext, w, b, seg)
            sig = sigmoid(pre)
            acts = pre * sig
            adj = g_ref[s].astype(F32)
            d_acts = [None] * chunks
            for c in range(chunks - 1, -1, -1):
                q = s * chunks + c
                rows = slice(q * CHUNK, (q + 1) * CHUNK)
                x = acts[c * CHUNK : (c + 1) * CHUNK]
                dy = dm_ref[rows]
                ce = spread_all(cumg[rows], heads, head_dim)
                de = spread_all(dtg[rows], heads, head_dim)
                weight = jnp.exp2(ce[CHUNK - 1 : CHUNK] - ce)
                u = x * de
                ub = u.astype(BF16)
                dyb = dy.astype(BF16)
                cbt = cbt_ref[q]
                parts = []
                dcbt = dcbt_ref[q]
                for j in range(0, heads, 2):
                    lanes = slice(j * head_dim, (j + 2) * head_dim)
                    dy_block = block_diagonal(dyb[:, lanes], head_dim)
                    dm = nt(ub[:, lanes], dy_block)
                    mats = []
                    for k, h in enumerate((j, j + 1)):
                        here = jnp.broadcast_to(cumg[rows, h : h + 1], (CHUNK, CHUNK))
                        there = cumr[h : h + 1, rows]
                        decay = jnp.exp2(jnp.where(causal, there - here, -jnp.inf))
                        mats.append((decay * cbt).astype(BF16))
                        dcbt = dcbt + decay * dm[:, k * CHUNK : (k + 1) * CHUNK]
                    parts.append(dot(jnp.concatenate(mats, axis=1), dy_block))
                dcbt_ref[q] = dcbt
                start = s0_ref[s] if c == 0 else s1_ref[s]
                end = s2_ref[s] if c == chunks - 1 else s1_ref[s]
                adj_b = adj.astype(BF16)
                bb = bc_ref[rows, :LANES].astype(BF16)
                cb = bc_ref[rows, LANES:].astype(BF16)
                ey = (jnp.exp2(ce) * dy).astype(BF16)
                du = jnp.concatenate(parts, axis=1) + weight * dot(bb, adj_b)
                db_acc[rows] += nt((u * weight).astype(BF16), adj_b)
                dc_acc[rows] += nt(ey, start)
                r1_ref[rows] += by_head(dyb.astype(F32) * (mixed_ref[rows] - skip * x), pick)
                r2_ref[rows] += by_head(x * du, pick)
                dtot_ref[q : q + 1] += by_head(
                    jnp.sum(adj * end.astype(F32), axis=0, keepdims=True), pick
                )
                grad = jnp.sum(dy * x, axis=0, keepdims=True)
                grad_skip = grad if grad_skip is None else grad_skip + grad
                d_acts[c] = du * de + skip * dy
                if c > 0:
                    adj = tot_ref[q : q + 1] * adj + dot(cb, ey, ((0,), (0,)))
            conv_back(s, ext, pre, sig, jnp.concatenate(d_acts, axis=0))
        gskip_ref[...] = grad_skip

    @pl.when(step == groups)
    def _():
        row = lax.broadcasted_iota(jnp.int32, (CHUNK, CHUNK), 0)
        col = lax.broadcasted_iota(jnp.int32, (CHUNK, CHUNK), 1)
        later = (row <= col).astype(F32)
        rate = -jnp.exp(dl_ref[...])
        sum_raw = jnp.zeros((1, LANES), F32)
        sum_log = jnp.zeros((1, LANES), F32)
        for s in range(seqs):
            ext = pc_ref[s]
            pre = causal_conv(ext, w, b, seg)
            sig = sigmoid(pre)
            parts = []
            for c in range(chunks):
                q = s * chunks + c
                rows = slice(q * CHUNK, (q + 1) * CHUNK)
                dcbt = dcbt_ref[q]
                bb = bc_ref[rows, :LANES].astype(BF16)
                cb = bc_ref[rows, LANES:].astype(BF16)
                d_b = db_acc[rows] + dot(dcbt.astype(BF16), cb)
                d_c = dc_acc[rows] + dot(dcbt.T.astype(BF16), bb)
                parts.append(jnp.concatenate([d_b, d_c], axis=1))
                dt = dt_ref[rows]
                r2 = r2_ref[rows]
                d_log = jnp.dot(
                    later, r1_ref[rows] - dt * r2, precision=HIGH, preferred_element_type=F32
                )
                d_log = d_log + dtot_ref[q : q + 1]
                raw = raw_ref[s, EDGE + c * CHUNK : EDGE + (c + 1) * CHUNK] + sb_ref[...]
                d_raw = (r2 + rate * d_log) * sigmoid(raw)
                draw_ref[rows] = d_raw
                sum_raw = sum_raw + jnp.sum(d_raw, axis=0, keepdims=True)
                sum_log = sum_log + jnp.sum(d_log * dt, axis=0, keepdims=True) * rate
            conv_back(s, ext, pre, sig, jnp.concatenate(parts, axis=0))
        hsum_ref[0:1] = sum_raw
        hsum_ref[1:2] = sum_log


def bwd_b(pc, w, b, sb, dl, bc, dt, cum, cumt, dm, mixed, s0, s1, s2, g, tot, skip, head_dim):
    seqs, rows, cols = pc.shape
    tokens, inner = dm.shape
    groups = inner // GROUP
    taps, channels = w.shape
    wide = pl.BlockSpec((tokens, GROUP), lambda i: (0, jnp.minimum(i, groups - 1)))
    states = pl.BlockSpec((seqs, LANES, GROUP), lambda i: (0, 0, jnp.minimum(i, groups - 1)))
    line = lambda n: pl.BlockSpec((n, GROUP), lambda i: (0, jnp.minimum(i, groups - 1)))
    conv = lambda n: pl.BlockSpec((n, GROUP), lambda i: (0, i))
    ends = pl.BlockSpec((seqs, EDGE, GROUP), lambda i: (0, 0, i))
    chunks = tokens // CHUNK
    shape = jax.ShapeDtypeStruct
    return pl.pallas_call(
        functools.partial(bwd_b_kernel, head_dim, groups),
        grid=(groups + 1,),
        in_specs=[
            pl.BlockSpec((seqs, rows, GROUP), lambda i: (0, 0, i)),
            conv(taps),
            conv(1),
            pl.BlockSpec((seqs, rows, LANES), lambda i: (0, 0, cols // LANES - 1)),
            whole((1, LANES)), whole((1, LANES)),
            whole(bc.shape), whole(dt.shape), whole(cum.shape), whole(cumt.shape),
            wide, wide, states, states, states, states, line(8), line(1),
        ],
        out_specs=[
            conv(tokens), ends, ends, conv(taps), conv(1), line(1),
            whole((tokens, LANES)), whole((2, LANES)),
        ],
        out_shape=[
            shape((tokens, channels), BF16),
            shape((seqs, EDGE, channels), F32),
            shape((seqs, EDGE, channels), F32),
            shape((taps, channels), F32),
            shape((1, channels), F32),
            shape((1, inner), F32),
            shape((tokens, LANES), F32),
            shape((2, LANES), F32),
        ],
        scratch_shapes=[
            pltpu.VMEM((chunks, CHUNK, CHUNK), F32),
            pltpu.VMEM((chunks, CHUNK, CHUNK), F32),
            pltpu.VMEM((tokens, LANES), F32),
            pltpu.VMEM((tokens, LANES), F32),
            pltpu.VMEM((tokens, LANES), F32),
            pltpu.VMEM((tokens, LANES), F32),
            pltpu.VMEM((8, LANES), F32),
        ],
        compiler_params=params(),
        name="scan_backward",
    )(pc, w, b, pc, sb, dl, bc, dt, cum, cumt, dm, mixed, s0, s1, s2, g, tot, skip)


PIECES = (3, 2, 1)


def piece_of(columns, n):
    unit = columns // sum(PIECES)
    return sum(PIECES[:n]) * unit, sum(PIECES[: n + 1]) * unit


def pair_copies(place, lhs, rhs, send, recv):
    other = 1 - place.own["c"]
    parts = [(src.at[2 * g + other], dst.at[g]) for src, dst in lhs for g in range(4)] + list(rhs)
    return [
        remote(src, dst, send.at[n], recv.at[n], place.to["c"]) for n, (src, dst) in enumerate(parts)
    ]


def scan_backward_kernel(
    depth, head_dim, groups,
    pc_ref, w_ref, b_ref, raw_ref, sb_ref, dl_ref, bc_ref, dt_ref, cum_ref, cumt_ref,
    dma_ref, dm_ref, mixed_ref, s0_ref, s1_ref, s2_ref, tot_ref, skip_ref,
    nt_src, dz_src, no_src, cot_src, nt_pair, cot_pair,
    dc_out, gw_ref, gb_ref, hsum_ref, a_out, b_out, dc_pair,
    cbt_ref, ct_ref, dcbt_ref, db_acc, dc_acc, r1_ref, r2_ref, dtot_ref, skip_acc,
    dc_ref, tail_ref, edge_ref, edge_came, seg_ring, tot_ring, came, sent,
    dz_pair, no_pair,
    chain_send, chain_recv, edge_send, edge_recv, pair_send, pair_recv, out_sem, send, recv, *bufs,
):
    step = pl.program_id(0)
    lag = depth - 1
    seqs = pc_ref.shape[0]
    seg = pc_ref.shape[1] - EDGE
    chunks = seg // CHUNK
    heads = GROUP // head_dim
    w, b = w_ref[...], b_ref[...]
    taps = w.shape[0]
    channels = tail_ref.shape[2]
    place = Place(depth)
    chain = Chain(place, came, sent, chain_send, chain_recv, True)
    cut = lambda ref, lo, hi: ref.at[:, pl.ds(lo, hi - lo)]
    _, hi = piece_of(dz_src.shape[1], 0)
    ranges = ((0, hi), (hi, dz_src.shape[1]))
    rhs = [(cut(dz_src, *at), cut(dz_pair, *at)) for at in ranges]
    pairs = pair_copies(place, ((no_src, no_pair),), rhs, pair_send, pair_recv)
    dc_copy = remote(dc_ref, dc_pair, pair_send.at[6], pair_recv.at[6], place.to["c"])
    def piece(ref, n):
        lo, hi = piece_of(ref.shape[1], n)
        return ref.at[:, pl.ds(lo, hi - lo)]

    lanes = []
    for n in range(len(PIECES)):
        lanes += [
            Scatter(place, nt_src, nt_pair, piece(dz_src, n), piece(dz_pair, n), "y", "x",
                    bufs[14 * n : 14 * n + 7], send.at[2 * n], recv.at[2 * n]),
            Scatter(place, no_src, no_pair, piece(cot_src, n), piece(cot_pair, n), "x", "y",
                    bufs[14 * n + 7 : 14 * n + 14], send.at[2 * n + 1], recv.at[2 * n + 1]),
        ]
    edges = [
        remote(edge_ref.at[:, :, cols], edge_came.at[:, :, cols], edge_send.at[n], edge_recv.at[n], place.left)
        for n, cols in enumerate((pl.ds(0, channels - GROUP), pl.ds(channels - GROUP, GROUP)))
    ]
    outs = [pltpu.make_async_copy(dc_ref, dc_out, out_sem.at[0])]

    def run(first, name, *rest):
        for lane in lanes[2 * first : 2 * first + 2]:
            getattr(lane, name)(*rest)

    def at_step(n, *what):
        pl.when(step == n)(lambda: run(*what))

    @pl.when(step == 0)
    def _():
        place.meet()
        for copy in pairs:
            copy.start()
        for q in range(seqs * chunks):
            rows = slice(q * CHUNK, (q + 1) * CHUNK)
            b_proj, c_proj = bc_ref[rows, :LANES], bc_ref[rows, LANES:]
            cbt_ref[q] = nt_exact(b_proj, c_proj)
            ct_ref[q] = c_proj.T
        dcbt_ref[...] = jnp.zeros_like(dcbt_ref)
        db_acc[...] = jnp.zeros_like(db_acc)
        dc_acc[...] = jnp.zeros_like(dc_acc)
        r1_ref[...] = jnp.zeros_like(r1_ref)
        r2_ref[...] = jnp.zeros_like(r2_ref)
        skip_acc[...] = jnp.zeros_like(skip_acc)
        dtot_ref[...] = jnp.zeros_like(dtot_ref)

    @pl.when(step < groups)
    def _():
        at = lax.rem(step, lag + 1)
        cumg = lane_shift(cum_ref[...], step * heads)
        tot_ring[at] = tot_ref[...]
        for s in range(seqs):
            state = None
            for c in range(chunks - 1, -1, -1):
                q = s * chunks + c
                rows = slice(q * CHUNK, (q + 1) * CHUNK)
                ey = jnp.exp2(spread_all(cumg[rows], heads, head_dim)) * dma_ref[rows]
                loc = dot_pairs(ct_ref[q], ey)
                state = loc if state is None else tot_ref[q : q + 1] * state + loc
            seg_ring[at, s] = state

    handed = step - chain.behind

    @pl.when((handed >= 0) & (handed < groups))
    def _():
        at = lax.rem(handed, lag + 1)
        totals = tot_ring[at, seqs * chunks : seqs * chunks + seqs]
        chain.step(handed, totals[:, None, :], seg_ring[at])

    @pl.when(step == lag)
    def _():
        for copy in pairs[:5]:
            copy.wait_recv()

    @pl.when(step == lag + 4)
    def _():
        for copy in pairs[5:]:
            copy.wait_recv()

    at_step(lag, 0, "send_second", 0)
    at_step(lag + 1, 0, "send_second", 1)
    at_step(lag + 3, 0, "send_first")
    at_step(lag + 4, 1, "send_second", 0)
    at_step(lag + 5, 1, "send_second", 1)
    at_step(lag + 6, 0, "hold")
    at_step(lag + 7, 2, "send_second", 0)
    at_step(lag + 8, 2, "send_second", 1)
    for n, k in enumerate(lanes[0].waves()):
        at_step(lag + 8 + n, 0, "step", k)
    at_step(lag + 10, 1, "send_first")

    def conv_back(s, ext, pre, sig, d_act, at):
        lanes_at = pl.ds(pl.multiple_of(at * GROUP, GROUP), GROUP)
        d_pre = d_act * (sig * (1.0 + pre * (1.0 - sig)))
        zero = jnp.zeros((EDGE, d_pre.shape[1]), F32)
        padded = jnp.concatenate([zero, d_pre, zero], axis=0)
        total = None
        for k in range(taps):
            start = taps - 1 - k
            term = w[k : k + 1] * padded[start : start + seg + EDGE]
            total = term if total is None else total + term
        edge_ref[s, :, lanes_at] = total[:EDGE].astype(BF16)
        dc_ref[s * seg : (s + 1) * seg, lanes_at] = total[EDGE:].astype(BF16)
        tail_ref[s, :, lanes_at] = total[seg:]
        for k in range(taps):
            start = EDGE - (taps - 1) + k
            grad = jnp.sum(ext[start : start + seg] * d_pre, axis=0, keepdims=True)
            gw_ref[k : k + 1] = grad if s == 0 else gw_ref[k : k + 1] + grad
        grad = jnp.sum(d_pre, axis=0, keepdims=True)
        gb_ref[...] = grad if s == 0 else gb_ref[...] + grad

    def by_head(value, pick):
        high = value.astype(BF16)
        return dot(high, pick) + dot((value - high.astype(F32)).astype(BF16), pick)

    @pl.when((step >= lag) & (step < lag + groups))
    def _():
        g = step - lag
        at = lax.rem(g, lag + 1)
        first = g * heads
        cumg = lane_shift(cum_ref[...], first)
        dtg = lane_shift(dt_ref[...], first)
        cumr = head_rows(cumt_ref, first)
        row = lax.broadcasted_iota(jnp.int32, (CHUNK, CHUNK), 0)
        col = lax.broadcasted_iota(jnp.int32, (CHUNK, CHUNK), 1)
        causal = row <= col
        lane = lax.broadcasted_iota(jnp.int32, (GROUP, LANES), 0)
        head = lax.broadcasted_iota(jnp.int32, (GROUP, LANES), 1)
        pick = (head == first + lane // head_dim).astype(BF16)
        skip = skip_ref[...]
        grad_skip = None
        for s in range(seqs):
            ext = pc_ref[s]
            pre = causal_conv(ext, w, b, seg)
            sig = sigmoid(pre)
            acts = pre * sig
            adj = came[g, s].astype(F32)
            d_acts = [None] * chunks
            for c in range(chunks - 1, -1, -1):
                q = s * chunks + c
                rows = slice(q * CHUNK, (q + 1) * CHUNK)
                x = acts[c * CHUNK : (c + 1) * CHUNK]
                dy = dm_ref[rows]
                ce = spread_all(cumg[rows], heads, head_dim)
                de = spread_all(dtg[rows], heads, head_dim)
                weight = jnp.exp2(ce[CHUNK - 1 : CHUNK] - ce)
                u = x * de
                ub = u.astype(BF16)
                dyb = dy.astype(BF16)
                cbt = cbt_ref[q]
                parts = []
                dcbt = dcbt_ref[q]
                for j in range(0, heads, 2):
                    two = slice(j * head_dim, (j + 2) * head_dim)
                    dy_block = block_diagonal(dyb[:, two], head_dim)
                    dm = nt(ub[:, two], dy_block)
                    mats = []
                    for k, h in enumerate((j, j + 1)):
                        here = jnp.broadcast_to(cumg[rows, h : h + 1], (CHUNK, CHUNK))
                        there = cumr[h : h + 1, rows]
                        decay = jnp.exp2(jnp.where(causal, there - here, -jnp.inf))
                        mats.append((decay * cbt).astype(BF16))
                        dcbt = dcbt + decay * dm[:, k * CHUNK : (k + 1) * CHUNK]
                    parts.append(dot(jnp.concatenate(mats, axis=1), dy_block))
                dcbt_ref[q] = dcbt
                start = s0_ref[s] if c == 0 else s1_ref[s]
                end = s2_ref[s] if c == chunks - 1 else s1_ref[s]
                adj_b = adj.astype(BF16)
                bb = bc_ref[rows, :LANES].astype(BF16)
                ey = jnp.exp2(ce) * dy
                du = jnp.concatenate(parts, axis=1) + weight * dot(bb, adj_b)
                uw = u * weight
                across = ((1,), (1,))
                db_acc[rows] += dot_pair(uw, adj_b, across) if c == chunks - 1 else dot_pairs(uw, adj, across)
                dc_acc[rows] += dot_pair(ey, start, across) if c == 0 else dot_pairs(ey, start, across)
                r1_ref[rows] += by_head(dyb.astype(F32) * (mixed_ref[rows] - skip * x), pick)
                r2_ref[rows] += by_head(x * du, pick)
                dtot_ref[q : q + 1] += by_head(
                    jnp.sum(adj * end.astype(F32), axis=0, keepdims=True), pick
                )
                grad = jnp.sum(dy * x, axis=0, keepdims=True)
                grad_skip = grad if grad_skip is None else grad_skip + grad
                d_acts[c] = du * de + skip * dy
                if c > 0:
                    adj = tot_ring[at, q : q + 1] * adj + dot_pairs(ct_ref[q], ey)
            conv_back(s, ext, pre, sig, jnp.concatenate(d_acts, axis=0), g)
        skip_acc[0:1] += by_head(grad_skip, pick)

    @pl.when(step == lag + groups)
    def _():
        pl.when(place.has_left)(edges[0].start)
        row = lax.broadcasted_iota(jnp.int32, (CHUNK, CHUNK), 0)
        col = lax.broadcasted_iota(jnp.int32, (CHUNK, CHUNK), 1)
        later = (row <= col).astype(F32)
        rate = -jnp.exp(dl_ref[...])
        sum_raw = jnp.zeros((1, LANES), F32)
        sum_log = jnp.zeros((1, LANES), F32)
        for s in range(seqs):
            ext = pc_ref[s]
            pre = causal_conv(ext, w, b, seg)
            sig = sigmoid(pre)
            parts = []
            for c in range(chunks):
                q = s * chunks + c
                rows = slice(q * CHUNK, (q + 1) * CHUNK)
                dcbt = dcbt_ref[q]
                d_b = db_acc[rows] + dot_pairs(dcbt, bc_ref[rows, LANES:])
                d_c = dc_acc[rows] + dot_pairs(dcbt.T, bc_ref[rows, :LANES])
                parts.append(jnp.concatenate([d_b, d_c], axis=1))
                dt = dt_ref[rows]
                r2 = r2_ref[rows]
                d_log = jnp.dot(
                    later, r1_ref[rows] - dt * r2, precision=HIGH, preferred_element_type=F32
                )
                d_log = d_log + dtot_ref[q : q + 1]
                raw = raw_ref[s, EDGE + c * CHUNK : EDGE + (c + 1) * CHUNK] + sb_ref[...]
                d_raw = (r2 + rate * d_log) * sigmoid(raw)
                dc_ref[rows, channels:] = d_raw.astype(BF16)
                sum_raw = sum_raw + jnp.sum(d_raw, axis=0, keepdims=True)
                sum_log = sum_log + jnp.sum(d_log * dt, axis=0, keepdims=True) * rate
            conv_back(s, ext, pre, sig, jnp.concatenate(parts, axis=0), groups)
        hsum_ref[0:1] = sum_raw
        hsum_ref[1:2] = sum_log
        hsum_ref[2:3] = skip_acc[0:1]
        pl.when(place.has_left)(edges[1].start)

        @pl.when(place.has_right)
        def _():
            for copy in edges:
                copy.wait_recv()
            for s in range(seqs):
                fixed = tail_ref[s] + edge_came[s].astype(F32)
                dc_ref[(s + 1) * seg - EDGE : (s + 1) * seg, :channels] = fixed.astype(BF16)

        outs[0].start()
        dc_copy.start()
        run(1, "hold")
        run(2, "send_first")
        for k in lanes[0].waves():
            run(1, "step", k)
        run(2, "hold")
        for k in lanes[0].waves():
            run(2, "step", k)
        for n, out in enumerate((a_out, b_out)):
            for i in range(len(PIECES)):
                lo, hi = piece_of(out.shape[1], i)
                out[:, lo:hi] = lanes[2 * i + n].keep[place.z]
        for lane in lanes:
            lane.finish()
        chain.finish()

        @pl.when(place.has_left)
        def _():
            for copy in edges:
                copy.wait_send()

        for copy in pairs:
            copy.wait_send()
        for copy in outs + [dc_copy]:
            copy.wait()


def scan_backward(
    pc, w, b, sb, dl, bc, dt, cum, cumt, dm, mixed, s0, s1, s2, tot, skip, normed_t, dz, turned, cot,
    nt_pair, cot_pair, head_dim, depth,
):
    seqs, rows, cols = pc.shape
    tokens, inner = dm.shape
    groups = inner // GROUP
    lag = depth - 1
    taps, channels = w.shape
    out = lambda i: jnp.maximum(i - lag, 0)
    inside = lambda i: jnp.minimum(out(i), groups - 1)
    wide = pl.BlockSpec((tokens, GROUP), lambda i: (0, inside(i)))
    states = pl.BlockSpec((seqs, LANES, GROUP), lambda i: (0, 0, inside(i)))
    line = lambda n: pl.BlockSpec((n, GROUP), lambda i: (0, inside(i)))
    conv = lambda n: pl.BlockSpec((n, GROUP), lambda i: (0, out(i)))
    ahead = lambda n: pl.BlockSpec((n, GROUP), lambda i: (0, jnp.minimum(i, groups - 1)))
    once = lambda v: pl.BlockSpec(v.shape, lambda i: (0,) * v.ndim, pipeline_mode=pl.Buffered(1))
    anywhere = pl.BlockSpec(memory_space=pl.ANY)
    chunks = tokens // CHUNK
    shape, dma = jax.ShapeDtypeStruct, pltpu.SemaphoreType.DMA
    a_rows, b_rows = normed_t.shape[1] // depth, turned.shape[1] // depth
    a_cols, b_cols = dz.shape[1], cot.shape[1]
    half = lambda v: (4,) + v.shape[1:]
    sends, receives = Scatter.sems(depth)
    buffers = []
    for n in range(len(PIECES)):
        for rows_of, cols_of in ((a_rows, a_cols), (b_rows, b_cols)):
            lo, hi = piece_of(cols_of, n)
            buffers += Scatter.scratch(depth, rows_of, hi - lo)
    ring = lambda *dims: pltpu.VMEM((lag + 1,) + dims, F32)
    link = pltpu.VMEM((groups, seqs, LANES, GROUP), BF16)
    square = pltpu.VMEM((chunks, CHUNK, CHUNK), F32)
    column = pltpu.VMEM((tokens, LANES), F32)
    return pl.pallas_call(
        functools.partial(scan_backward_kernel, depth, head_dim, groups),
        grid=(groups + 1 + lag,),
        in_specs=[
            pl.BlockSpec((seqs, rows, GROUP), lambda i: (0, 0, out(i))),
            conv(taps),
            conv(1),
            pl.BlockSpec((seqs, rows, LANES), lambda i: (0, 0, cols // LANES - 1)),
            whole((1, LANES)), whole((1, LANES)),
            whole(bc.shape), whole(dt.shape), whole(cum.shape), whole(cumt.shape),
            ahead(tokens), wide, wide, states, states, states, ahead(8), line(1),
            once(normed_t), once(dz), once(turned), once(cot), once(nt_pair), once(cot_pair),
        ],
        out_specs=[
            anywhere, conv(taps), conv(1), whole((3, LANES)),
            whole((a_rows, a_cols)), whole((b_rows, b_cols)), anywhere,
        ],
        out_shape=[
            shape((tokens, cols), BF16),
            shape((taps, channels), F32),
            shape((1, channels), F32),
            shape((3, LANES), F32),
            shape((a_rows, a_cols), F32),
            shape((b_rows, b_cols), F32),
            shape((tokens, cols), BF16),
        ],
        scratch_shapes=[
            square, pltpu.VMEM((chunks, LANES, CHUNK), F32), square, column, column, column, column,
            pltpu.VMEM((8, LANES), F32),
            pltpu.VMEM((8, LANES), F32),
            pltpu.VMEM((tokens, cols), BF16),
            pltpu.VMEM((seqs, EDGE, channels), F32),
            pltpu.VMEM((seqs, EDGE, channels), BF16),
            pltpu.VMEM((seqs, EDGE, channels), BF16),
            ring(seqs, LANES, GROUP), ring(8, GROUP), link, link,
            pltpu.VMEM(dz.shape, BF16), pltpu.VMEM(half(turned), BF16),
            dma((groups,)), dma((groups,)), dma((2,)), dma((2,)), dma((7,)), dma((7,)), dma((1,)),
            dma((2 * len(PIECES), sends)), dma((2 * len(PIECES), receives)),
            *buffers,
        ],
        compiler_params=pltpu.CompilerParams(
            dimension_semantics=("arbitrary",), collective_id=1, has_side_effects=True,
            vmem_limit_bytes=VMEM_LIMIT,
        ),
        name="scan_backward_sums",
    )(
        pc, w, b, pc, sb, dl, bc, dt, cum, cumt, dm, dm, mixed, s0, s1, s2, tot, skip,
        normed_t, dz, turned, cot, nt_pair, cot_pair,
    )


def scatter_last_kernel(
    depth, splits, nt_ref, nt_pair, dc_ref, dc_pair, dz_ref, wg_src, wc_src, x_ref, cot_ref, gain_ref,
    ggain_ref, gb_ref, gw_ref, hsum_ref, c_out, gi_ref, small_out, *refs,
):
    place = Place(depth)
    place.meet()
    pieces = len(splits) - 1
    small_src, tiles_ref, tile_sem, send, recv, small_send, small_recv = refs[:7]
    refs = refs[7:]
    cut = lambda ref, n: ref.at[:, pl.ds(splits[n], splits[n + 1] - splits[n])]
    lanes = [
        Scatter(place, nt_ref, nt_pair, cut(dc_ref, n), cut(dc_pair, n),
                *(("y", "x") if n % 2 == 0 else ("x", "y")), refs[7 * n : 7 * n + 7], send.at[n], recv.at[n])
        for n in range(pieces)
    ]
    small = SmallScatter(place, small_src, *refs[7 * pieces :], small_send, small_recv)
    tile = tiles_ref.shape[2]
    tokens = x_ref.shape[0]

    def d_normed(src, grad_ref, first):
        count = src.shape[1] // tile

        def fetch(i, slot):
            cols = pl.ds(pl.multiple_of(i * tile, LANES), tile)
            return pltpu.make_async_copy(src.at[:, cols], tiles_ref.at[slot], tile_sem.at[slot])

        fetch(0, 0).start()

        def one(i, carry):
            slot = lax.rem(i, 2)
            pl.when(i + 1 < count)(lambda: fetch(i + 1, 1 - slot).start())
            fetch(i, slot).wait()
            cols = pl.ds(pl.multiple_of(i * tile, LANES), tile)
            for r in range(0, tokens, 2 * CHUNK):
                rows = slice(r, r + 2 * CHUNK)
                part = nt(grad_ref[rows, cols], tiles_ref[slot])
                if first:

                    @pl.when(i == 0)
                    def _():
                        gi_ref[rows] = part

                    @pl.when(i > 0)
                    def _():
                        gi_ref[rows] += part
                else:
                    gi_ref[rows] += part
            return carry

        lax.fori_loop(0, count, one, 0)

    def input_grad():
        gain = gain_ref[...]
        size = 64

        def one(i, total):
            rows = pl.ds(pl.multiple_of(i * size, size), size)
            d = gi_ref[rows, :]
            values = x_ref[rows, :].astype(F32)
            scale = lax.rsqrt(jnp.mean(values * values, axis=1, keepdims=True) + EPS)
            hat = values * scale
            weighted = d * gain
            pull = jnp.mean(weighted * hat, axis=1, keepdims=True)
            gi_ref[rows, :] = scale * (weighted - hat * pull) + cot_ref[rows, :].astype(F32)
            return total + jnp.sum(d * hat, axis=0, keepdims=True)

        grad_gain = lax.fori_loop(0, tokens // size, one, jnp.zeros(gain.shape, F32))
        small_src[...] = jnp.zeros_like(small_src)
        taps = gw_ref.shape[0]
        shares = ((0, grad_gain), (1, ggain_ref[...]), (2, gb_ref[...]), (3, gw_ref[...]))
        heads = hsum_ref[:, : LANES // 2]
        for n in range(8 * depth):
            at = (n // depth // 4, n // depth // 2 % 2, n // depth % 2, n % depth)
            for row, value in shares:
                own = value.shape[1] // (8 * depth)
                where = (*at, slice(row, row + value.shape[0]), slice(0, own))
                small_src[where] = value[:, n * own : (n + 1) * own]
            small_src[(*at, slice(0, 1), slice(LANES // 2, LANES))] = heads[0:1]
            small_src[(*at, slice(3 + taps, 4 + taps), slice(0, LANES // 2))] = heads[1:2]
            small_src[(*at, slice(3 + taps, 4 + taps), slice(LANES // 2, LANES))] = heads[2:3]

    def run(first, name, *rest):
        for lane in lanes[first : first + 2]:
            getattr(lane, name)(*rest)

    run(0, "send_second", 0)
    run(0, "send_second", 1)
    run(2, "send_second", 0)
    run(2, "send_second", 1)
    d_normed(wg_src, dz_ref, True)
    run(0, "send_first")
    run(4, "send_second", 0)
    run(4, "send_second", 1)
    d_normed(wc_src, dc_ref, False)
    run(0, "hold")
    run(2, "send_first")
    input_grad()
    small.stage(0)
    run(2, "hold")
    small.stage(1)
    for k in lanes[0].waves():
        run(0, "step", k)
    small.stage(2)
    run(4, "send_first")
    for n, k in enumerate(lanes[0].waves()):
        run(2, "step", k)
    small.stage(3)
    run(4, "hold")
    for k in lanes[0].waves():
        small.sums.step(k)
        run(4, "step", k)
    for lane, lo, hi in zip(lanes, splits, splits[1:]):
        c_out[:, lo:hi] = lane.keep[place.z]
    small_out[...] = small.keep[place.z]
    for lane in lanes:
        lane.finish()
    small.finish()


def scatter_last(normed_t, nt_pair, dc, dc_pair, dz, wg, wc, x, cot, gain, ggain, gb, gw, hsum, depth):
    shape = jax.ShapeDtypeStruct
    vmem, dma = pl.BlockSpec(memory_space=pltpu.VMEM), pltpu.SemaphoreType.DMA
    anywhere = pl.BlockSpec(memory_space=pl.ANY)
    sends, receives = Scatter.sems(depth)
    rows = normed_t.shape[1] // depth
    tokens, width = dc.shape
    blocks = width // LANES
    parts = [share for share in PIECES for _ in (0, 1)]
    splits = tuple(LANES * (blocks * sum(parts[:n]) // sum(parts)) for n in range(len(parts) + 1))
    small_shape = (8, LANES)
    small_sends, small_receives = SmallScatter.sems(depth)
    sizes = [hi - lo for lo, hi in zip(splits, splits[1:])]
    scratch = []
    for size in sizes:
        scratch += Scatter.scratch(depth, rows, size)
    return pl.pallas_call(
        functools.partial(scatter_last_kernel, depth, splits),
        in_specs=[vmem] * 5 + [anywhere] * 2 + [vmem] * 7,
        out_specs=[vmem] * 3,
        out_shape=[shape((rows, width), F32), shape((tokens, x.shape[1]), F32), shape(small_shape, F32)],
        scratch_shapes=[
            pltpu.VMEM((2, 2, 2, depth) + small_shape, F32),
            pltpu.VMEM((2, wg.shape[0], 3 * LANES), BF16),
            dma((2,)), dma((6, sends)), dma((6, receives)),
            dma((small_sends,)), dma((small_receives,)),
            *scratch,
            *SmallScatter.scratch(depth, small_shape),
        ],
        compiler_params=pltpu.CompilerParams(
            collective_id=2, has_side_effects=True, vmem_limit_bytes=VMEM_LIMIT
        ),
        name="scatter_last",
    )(normed_t, nt_pair, dc, dc_pair, dz, wg, wc, x, cot, gain, ggain, gb, gw, hsum)


def passed_along(value, axis, steps):
    count = lax.axis_size(axis)
    initial, last = (max(0, -steps), min(count, count - steps))
    return lax.ppermute(value, axis, [(source, source + steps) for source in range(initial, last)])


def prefix(total, local, axis, backward):
    count, here = lax.axis_size(axis), lax.axis_index(axis)
    totals = lax.all_gather(total.astype(BF16), axis)
    locals_ = lax.all_gather(local, axis)
    state = jnp.zeros(local.shape, F32)
    order = range(count - 1, 0, -1) if backward else range(count - 1)
    for lap in order:
        new = totals[lap].astype(F32) * state + locals_[lap].astype(F32)
        reached = lap > here if backward else lap < here
        state = jnp.where(reached, new, state)
    leaves = total * state + local.astype(F32)
    return state.astype(BF16), leaves.astype(BF16)


AXES = ("dp", "ctx")


def body(
    inputs, gain_in, in_weight, conv_weight, conv_bias, step_bias, decay_log, skip_gain, gain_out,
    out_weight, cotangent,
):
    seqs, seg, width = inputs.shape
    tokens = seqs * seg
    count = lax.axis_size(AXES)
    dp, depth = lax.axis_size("dp"), lax.axis_size("ctx")
    own_links = dp == 8 and depth == 4
    inner = out_weight.shape[0] * count
    taps, channels = conv_weight.shape[0], conv_weight.shape[1] * count
    num_heads = step_bias.shape[0]
    head_dim = inner // num_heads
    a, b, c = gain_in.shape[0], gain_out.shape[0], conv_bias.shape[0]

    w_gate = in_weight[:, :inner]
    w_conv = in_weight[:, inner:]
    spare = -w_conv.shape[1] % LANES
    w_conv = jnp.pad(w_conv, ((0, 0), (0, spare)))
    rest = jnp.concatenate([gain_out, conv_bias, conv_weight.reshape(-1)])
    ends = taps - 1
    flat = inputs.reshape(tokens, width)
    cot = cotangent.reshape(tokens, width)

    if own_links:
        group = 2 * depth * a
        at = lax.rem(lax.axis_index("dp"), 2) * depth + lax.axis_index("ctx")
        head = lax.dynamic_update_slice(jnp.zeros((group,), F32), gain_in.astype(F32), (at * a,))
        small = jnp.concatenate([head, rest.astype(F32)])
        small = jnp.pad(small, (0, 8 * LANES - small.size)).reshape(8, LANES)
        pc, normed_ext, normed_t, small, w_conv = gather_project(inputs, small, w_conv, depth)
        w_conv = w_conv.reshape(width, -1)
        small = small.reshape(4, 2 * depth, 8 * LANES)
        g_in = small[:, :, :group].sum(axis=1).reshape(1, width)
        rest = small[:, :, group:].reshape(count, -1)
    else:
        before = passed_along(inputs[:, seg - EDGE :], "ctx", 1)
        ext = jnp.concatenate([before, inputs], axis=1).astype(F32)
        scale_ext = lax.rsqrt(jnp.mean(ext * ext, axis=-1, keepdims=True) + EPS)
        small = lax.all_gather(jnp.concatenate([gain_in, rest]), AXES).astype(F32)
        w_conv = lax.all_gather(w_conv, AXES, axis=0, tiled=True)
        w_gate = lax.all_gather(w_gate, AXES, axis=0, tiled=True)
        w_out = lax.all_gather(out_weight, AXES, axis=0, tiled=True)
        g_in, rest = small[:, :a].reshape(1, width), small[:, a:]
        normed_ext = (ext * scale_ext * g_in).astype(BF16)
        pc = dot(normed_ext.reshape(-1, width), w_conv).reshape(seqs, seg + EDGE, -1)
    g_out = rest[:, :b].reshape(1, inner)
    bias = rest[:, b : b + c].reshape(1, channels)
    kernel = rest[:, b + c : b + c + taps * c].reshape(count, taps, c).transpose(1, 0, 2)
    kernel = kernel.reshape(taps, channels)
    pad_head = lambda v: jnp.pad(v, (0, LANES - num_heads)).reshape(1, LANES)
    sb, dl = pad_head(step_bias), pad_head(decay_log)
    skip = jnp.repeat(skip_gain, head_dim).reshape(1, inner)

    if own_links:
        bc, dt, cum, cumt, mixed, s0, s1, s2, tot, z, dno, w_gate, w_out, nt_pair, cot_pair = scan_forward(
            pc, kernel, bias, sb, dl, skip, normed_ext, cot, in_weight, out_weight, normed_t, inner, head_dim, depth,
        )
        w_gate = w_gate.reshape(width, inner)
        w_out = w_out.reshape(inner, width)
        per_seq = tot[tokens // CHUNK : tokens // CHUNK + seqs][:, None, :]
    else:
        x, bc, dt, cum, cumt, loc0, local, tot = fwd_a(pc, kernel, bias, sb, dl, inner, head_dim)
        per_seq = tot[tokens // CHUNK : tokens // CHUNK + seqs][:, None, :]
        s0, s2 = prefix(per_seq, local, "ctx", False)
        mixed, s1 = fwd_b(x, bc, dt, cum, cumt, s0, loc0, tot, skip, head_dim)
        z = dot(normed_ext[:, EDGE:].reshape(tokens, width), w_gate)
        dno = nt(cot, w_out)

    turned, output, d_mixed, d_gate, grad_gain_out = mid(z, dno, mixed, w_out, g_out, flat, 8)
    if own_links:
        (
            d_conv, grad_kernel, grad_bias, head_sums, grad_gate_weight, grad_out_weight, dc_pair
        ) = scan_backward(
            pc, kernel, bias, sb, dl, bc, dt, cum, cumt, d_mixed, mixed, s0, s1, s2, tot, skip,
            normed_t, d_gate, turned, cot, nt_pair, cot_pair, head_dim, depth,
        )
    else:
        scatter = lambda v: lax.psum_scatter(v.astype(BF16), AXES, scatter_dimension=0, tiled=True).astype(F32)
        normed = normed_ext[:, EDGE:].reshape(tokens, width)
        grad_out_weight = scatter(dot(turned.reshape(inner, tokens), cot))
        grad_gate_weight = scatter(dot(normed, d_gate, ((0,), (0,))))
        adjoint = bwd_a(d_mixed, bc, cum, tot, seqs, head_dim)
        g, _ = prefix(per_seq, adjoint, "ctx", True)
        d_conv, tail, edge, grad_kernel, grad_bias, grad_skip, d_raw, head_sums = bwd_b(
            pc, kernel, bias, sb, dl, bc, dt, cum, cumt, d_mixed, mixed, s0, s1, s2, g, tot, skip, head_dim
        )
        after = passed_along(edge[:, EDGE - ends :].astype(BF16), "ctx", -1).astype(F32)
        tail = tail[:, EDGE - ends :] + after
        d_conv = d_conv.reshape(seqs, seg, channels).at[:, seg - ends :].set(tail.astype(BF16))
        d_conv = jnp.concatenate([d_conv.reshape(tokens, channels), d_raw.astype(BF16)], axis=1)

    real = d_conv.shape[1] - spare
    if own_links:
        grad_conv_cols, grad_input, mine = scatter_last(
            normed_t, nt_pair, d_conv, dc_pair, d_gate, w_gate, w_conv, flat, cot, g_in,
            grad_gain_out, grad_bias, grad_kernel, head_sums, depth,
        )
        grad_conv_cols = grad_conv_cols[:, :real]
        half = LANES // 2
        grad_gain_in, grad_step = mine[0, :a], mine[0, half : half + num_heads]
        grad_gain_out, grad_bias, grad_kernel = mine[1, :b], mine[2, :c], mine[3 : 3 + taps, :c]
        grad_decay = mine[3 + taps, :num_heads]
        grad_skip = mine[3 + taps, half : half + num_heads]
    else:
        d_normed = nt(d_gate, w_gate) + nt(d_conv, w_conv)
        values = flat.astype(F32)
        scale = lax.rsqrt(jnp.mean(values * values, axis=-1, keepdims=True) + EPS)
        hat = values * scale
        weighted = d_normed * g_in
        pull = jnp.mean(weighted * hat, axis=-1, keepdims=True)
        grad_input = scale * (weighted - hat * pull) + cot.astype(F32)
        grad_conv_cols = scatter(dot(normed, d_conv[:, :real], ((0,), (0,))))
        grad_skip = jnp.sum(grad_skip.reshape(num_heads, head_dim), axis=1)
        heads_sum = jnp.concatenate([head_sums[0, :num_heads], head_sums[1, :num_heads], grad_skip])
        by_owner = jnp.concatenate(
            [
                jnp.sum(d_normed * hat, axis=0).reshape(count, a),
                grad_gain_out.reshape(count, b),
                grad_bias.reshape(count, c),
                grad_kernel.reshape(taps, count, c).transpose(1, 0, 2).reshape(count, taps * c),
                jnp.broadcast_to(heads_sum, (count, 3 * num_heads)),
            ],
            axis=1,
        )
        mine = lax.dynamic_index_in_dim(lax.psum(by_owner, AXES), lax.axis_index(AXES), 0, False)
        cuts = [0, a, a + b, a + b + c, a + b + c + taps * c]
        cuts += [cuts[-1] + n * num_heads for n in (1, 2, 3)]
        parts = [mine[lo:hi] for lo, hi in zip(cuts, cuts[1:])]
        grad_gain_in, grad_gain_out, grad_bias, grad_kernel, grad_step, grad_decay, grad_skip = parts
    return (
        output.reshape(seqs, seg, width),
        grad_input.reshape(seqs, seg, width),
        grad_gain_in,
        jnp.concatenate([grad_gate_weight, grad_conv_cols], axis=1),
        grad_kernel.reshape(taps, c),
        grad_bias,
        grad_step,
        grad_decay,
        grad_skip,
        grad_gain_out,
        grad_out_weight,
    )


def solution(mesh):
    rows, cols, both = P("dp", "ctx", None), P(AXES, None), P(AXES)
    return jax.shard_map(
        body,
        mesh=mesh,
        in_specs=(rows, both, cols, P(None, AXES), both, P(), P(), P(), both, cols, rows),
        out_specs=(rows, rows, both, cols, P(None, AXES), both, P(), P(), P(), both, cols),
        check_vma=False,
    )
```

```python
import functools

import jax
import jax.numpy as jnp
from jax import lax
from jax.experimental import pallas as pl
from jax.experimental.pallas import tpu as pltpu
from jax.sharding import PartitionSpec as P

EPS = 1e-05
LOG2E = 1.4426950408889634
HIGH = lax.Precision.HIGHEST
F32 = jnp.float32
BF16 = jnp.bfloat16
CHUNK = 128
GROUP = 256
EDGE = 16
LANES = 128
VMEM_LIMIT = 60 * 1024 * 1024


def dot(a, b, dims=((1,), (0,))):
    return lax.dot_general(a, b, (dims, ((), ())), preferred_element_type=F32)


def nt(a, b):
    return dot(a, b, ((1,), (1,)))


def params():
    return pltpu.CompilerParams(
        dimension_semantics=("arbitrary",), vmem_limit_bytes=VMEM_LIMIT
    )


def whole(shape):
    return pl.BlockSpec(shape, lambda i: (0,) * len(shape))


def sigmoid(v):
    return 1.0 / (1.0 + jnp.exp(-v))


def softplus(v):
    return jnp.maximum(v, 0.0) + jnp.log1p(jnp.exp(-jnp.abs(v)))


def causal_conv(ext, w, b, seg):
    taps = w.shape[0]
    total = b
    for k in range(taps):
        at = EDGE - (taps - 1) + k
        total = total + w[k : k + 1] * ext[at : at + seg]
    return total


def lane_shift(value, lanes):
    return pltpu.roll(value, lax.rem(LANES - lanes, LANES), 1)


def head_rows(ref, first):
    base = pl.multiple_of(first // 8 * 8, 8)
    return pltpu.roll(ref[pl.ds(base, 8), :], lax.rem(8 - lax.rem(first, 8), 8), 0)


def spread(cols, at, head_dim):
    rows = cols.shape[0]
    lane = lax.broadcasted_iota(jnp.int32, (rows, LANES), 1)
    first = jnp.broadcast_to(cols[:, at : at + 1], (rows, LANES))
    second = jnp.broadcast_to(cols[:, at + 1 : at + 2], (rows, LANES))
    return jnp.where(lane < head_dim, first, second)


def spread_all(cols, heads, head_dim):
    return jnp.concatenate([spread(cols, j, head_dim) for j in range(0, heads, 2)], axis=1)


def block_diagonal(pair, head_dim):
    lane = lax.broadcasted_iota(jnp.int32, pair.shape, 1)
    zero = jnp.zeros_like(pair)
    return jnp.concatenate(
        [jnp.where(lane < head_dim, pair, zero), jnp.where(lane < head_dim, zero, pair)], axis=0
    )


MESH = pl.DeviceIdType.MESH


class Place:
    def __init__(self, depth):
        dp, z = lax.axis_index("dp"), lax.axis_index("ctx")
        self.depth, self.z = depth, z
        self.own = {"y": lax.div(dp, 4), "x": lax.rem(lax.div(dp, 2), 2), "c": lax.rem(dp, 2)}
        self.to = {
            name: {"dp": dp + step * (1 - 2 * self.own[name])}
            for name, step in (("y", 4), ("x", 2), ("c", 1))
        }
        self.has_left, self.has_right = z > 0, z < depth - 1
        self.left, self.right = {"ctx": z - 1}, {"ctx": z + 1}

    def flipped(self, *names):
        return {n: 1 - v if n in names else v for n, v in self.own.items()}

    def near(self, k):
        z, last = self.z, self.depth - 1
        reach = jnp.minimum(z, last - z)
        pair = jnp.where(k % 2 == 1, z - (k + 1) // 2, z + k // 2)
        alone = jnp.where(z > last - z, last - k, k)
        return z if k == 0 else jnp.where(k <= 2 * reach, pair, alone)

    def meet(self):
        barrier = pltpu.get_barrier_semaphore()
        signal = functools.partial(pl.semaphore_signal, barrier, inc=1, device_id_type=MESH)
        for name in ("y", "x", "c"):
            signal(device_id=self.to[name])
        pl.when(self.has_left)(lambda: signal(device_id=self.left))
        pl.when(self.has_right)(lambda: signal(device_id=self.right))
        ends = self.has_left.astype(jnp.int32) + self.has_right.astype(jnp.int32)
        pl.semaphore_wait(barrier, 3 + ends)


def remote(src, dst, send, recv, to):
    return pltpu.make_async_remote_copy(
        src_ref=src, dst_ref=dst, send_sem=send, recv_sem=recv, device_id=to, device_id_type=MESH
    )


class Gather:
    def __init__(self, place, src, line, first, second, send, recv, part=()):
        self.place, self.src, self.line_of, self.part = place, src, line, part
        self.first, self.second, self.send, self.recv = first, second, send, recv

    @staticmethod
    def sems(depth):
        return 6 * depth + 3, 5 * depth + 3

    def flips(self, g):
        return ((), (self.first,), (self.second,), (self.first, self.second))[g]

    def slot(self, k, *flips):
        return self.line_of(**self.place.flipped(*flips)).at[(self.place.near(k), *self.part)]

    def copy(self, k, where, to, send, recv):
        src = self.src if k == 0 and where == () else self.slot(k, *where)
        return remote(src, self.slot(k, *where), self.send.at[send], self.recv.at[recv], to)

    def along(self, k, right):
        p = self.place
        return self.copy(k, (), p.right if right else p.left, int(right) * p.depth + k, p.near(k))

    def goes(self, k, right):
        p, at = self.place, self.place.near(k)
        if right:
            return p.has_right if k == 0 else p.has_right & (at < p.z)
        return p.has_left if k == 0 else p.has_left & (at > p.z)

    def to_axis(self, k, stage, there=False):
        p, depth = self.place, self.place.depth
        f, s = self.first, self.second
        where = ((), (), (f,), (f, s))[stage]
        axis = (f, s, s, "c")[stage]
        if there:
            where = where + (axis,)
        return self.copy(k, where, p.to[axis], (2 + stage) * depth + k, (1 + stage) * depth + k)

    def to_core(self, g, there=False):
        depth = self.place.depth
        flips = self.flips(g) + (("c",) if there else ())
        line = self.line_of(**self.place.flipped(*flips)).at[(pl.ds(0, depth), *self.part)]
        return remote(line, line, self.send.at[6 * depth + g], self.recv.at[5 * depth + g], self.place.to["c"])

    def line(self, k):
        if k:
            self.along(k, True).wait_recv()
        for right in (True, False):
            pl.when(self.goes(k, right))(lambda: self.along(k, right).start())
        for stage in (0, 1):
            self.to_axis(k, stage).start()

    def from_first(self, k):
        self.to_axis(k, 0, True).wait_recv()
        self.to_axis(k, 2).start()

    def from_second(self, k):
        self.to_axis(k, 1, True).wait_recv()

    def from_both(self, k):
        self.to_axis(k, 2, True).wait_recv()
        self.to_axis(k, 3).start()

    def core(self, g):
        self.to_core(g).start()

    def whole(self, g):
        if g < 3:
            self.to_core(g, True).wait_recv()
        else:
            for k in range(self.place.depth):
                self.to_axis(k, 3, True).wait_recv()

    def finish(self):
        for k in range(self.place.depth):
            for right in (True, False):
                pl.when(self.goes(k, right))(lambda: self.along(k, right).wait_send())
            for stage in range(4):
                self.to_axis(k, stage).wait_send()
        for g in range(3):
            self.to_core(g).wait_send()


class Line:
    def __init__(self, place, keep, sent, came, send, recv):
        self.place, self.keep, self.sent, self.came = place, keep, sent, came
        self.send, self.recv = send, recv

    def copy(self, k, to, at):
        zk = self.place.near(k)
        return remote(self.sent.at[zk], self.came.at[at], self.send.at[k], self.recv.at[at], to)

    def take(self, at):
        self.copy(1, self.place.left, at).wait_recv()
        zk = jnp.where(at == self.place.depth, self.place.z, at)
        self.keep[zk] = self.keep[zk] + self.came[at].astype(F32)

    def moves(self, k):
        p, zk = self.place, self.place.near(k)
        return (
            (zk < p.z, p.left, zk),
            (zk > p.z, p.right, jnp.where(zk == p.z + 1, p.depth, zk)),
        )

    def step(self, k):
        p, zk = self.place, self.place.near(k)
        if k == 0:
            pl.when(p.has_right)(lambda: self.take(p.z))
            pl.when(p.has_left)(lambda: self.take(p.depth))
            return
        farther = ((zk < p.z) & p.has_right) | ((zk > p.z) & p.has_left)
        pl.when(farther)(lambda: self.take(zk))
        self.sent[zk] = self.keep[zk].astype(self.sent.dtype)
        for goes, to, at in self.moves(k):
            pl.when(goes)(lambda: self.copy(k, to, at).start())

    def finish(self):
        for k in range(1, self.place.depth):
            for goes, to, at in self.moves(k):
                pl.when(goes)(lambda: self.copy(k, to, at).wait_send())


class Scatter:
    def __init__(self, place, lhs, lhs_pair, rhs, rhs_pair, first, second, bufs, send, recv):
        self.place, self.lhs, self.lhs_pair, self.rhs, self.rhs_pair = place, lhs, lhs_pair, rhs, rhs_pair
        self.first, self.second, self.send, self.recv = first, second, send, recv
        self.s_sent, self.s_came, self.f_sent, self.f_came, self.keep, z_sent, z_came = bufs
        depth = place.depth
        self.sums = Line(place, self.keep, z_sent, z_came, send.at[pl.ds(2 + depth, depth)],
                         recv.at[pl.ds(2 + depth, depth + 1)])

    @staticmethod
    def sems(depth):
        return 2 + 2 * depth, 3 + 2 * depth

    @staticmethod
    def scratch(depth, rows, cols):
        block = lambda *lead: pltpu.VMEM(lead + (rows, cols), BF16)
        return [
            block(2, depth), block(2, depth), block(depth), block(depth),
            pltpu.VMEM((depth, rows, cols), F32), block(depth), block(depth + 1),
        ]

    def product(self, flips, store):
        at = self.place.flipped(*flips)
        pair = 2 * at["y"] + at["x"]
        one = 2 * pair + at["c"]
        rows, cols = self.keep.shape[1:]
        tile = 512

        def block(start, size):
            lanes = pl.ds(start, size)
            part = dot(self.lhs[one], self.rhs[:, lanes]) + dot(self.lhs_pair[pair], self.rhs_pair[:, lanes])
            for z in range(self.place.depth):
                store(z, lanes, part[z * rows : (z + 1) * rows])

        def loop(i, carry):
            block(pl.multiple_of(i * tile, tile), tile)
            return carry

        lax.fori_loop(0, cols // tile, loop, 0)
        if cols % tile:
            block(cols // tile * tile, cols % tile)

    def to_second(self, j):
        return remote(self.s_sent.at[j], self.s_came.at[j], self.send.at[j], self.recv.at[j],
                      self.place.to[self.second])

    def to_first(self, k):
        zk, n = self.place.near(k), 2 + k
        return remote(self.f_sent.at[zk], self.f_came.at[zk], self.send.at[n], self.recv.at[n],
                      self.place.to[self.first])

    def waves(self):
        return range(self.place.depth - 1, -1, -1)

    def send_second(self, j):
        def store(z, lanes, part):
            self.s_sent[j, z, :, lanes] = part.astype(BF16)

        self.product((self.second, self.first) if j == 0 else (self.second,), store)
        self.to_second(j).start()

    def send_first(self):
        self.to_second(0).wait_recv()

        def store(z, lanes, part):
            self.f_sent[z, :, lanes] = (part + self.s_came[0, z, :, lanes].astype(F32)).astype(BF16)

        self.product((self.first,), store)
        for k in self.waves():
            self.to_first(k).start()

    def hold(self):
        self.to_second(1).wait_recv()

        def store(z, lanes, part):
            self.keep[z, :, lanes] = part + self.s_came[1, z, :, lanes].astype(F32)

        self.product((), store)

    def step(self, k):
        self.to_first(k).wait_recv()
        zk = self.place.near(k)
        self.keep[zk] = self.keep[zk] + self.f_came[zk].astype(F32)
        self.sums.step(k)

    def finish(self):
        for j in (0, 1):
            self.to_second(j).wait_send()
        for k in self.waves():
            self.to_first(k).wait_send()
        self.sums.finish()


class SmallScatter:
    def __init__(self, place, src, c_came, half, x_came, keep, y_came, z_sent, z_came, send, recv):
        self.place, self.src, self.c_came, self.half = place, src, c_came, half
        self.x_came, self.keep, self.y_came = x_came, keep, y_came
        self.send, self.recv = send, recv
        depth = place.depth
        self.sums = Line(place, keep, z_sent, z_came, send.at[pl.ds(7, depth)],
                         recv.at[pl.ds(7, depth + 1)])

    @staticmethod
    def sems(depth):
        return 7 + depth, 8 + depth

    @staticmethod
    def scratch(depth, shape):
        block = lambda *lead: pltpu.VMEM(lead + shape, F32)
        return [
            block(2, 2, depth), block(2, 2, depth), block(2, depth), block(depth), block(depth),
            block(depth), block(depth + 1),
        ]

    def copy(self, n):
        p, own = self.place, self.place.own
        if n < 4:
            y, x = n // 2, n % 2
            src, dst, to = self.src.at[y, x, 1 - own["c"]], self.c_came.at[y, x], "c"
        elif n < 6:
            src, dst, to = self.half.at[n - 4, 1 - own["x"]], self.x_came.at[n - 4], "x"
        else:
            src, dst, to = self.half.at[1 - own["y"], own["x"]], self.y_came, "y"
        return remote(src, dst, self.send.at[n], self.recv.at[n], p.to[to])

    def stage(self, n):
        own = self.place.own
        if n == 0:
            for i in range(4):
                self.copy(i).start()
        elif n == 1:
            for i in range(4):
                self.copy(i).wait_recv()
            for y in (0, 1):
                for x in (0, 1):
                    self.half[y, x] = self.src[y, x, own["c"]] + self.c_came[y, x]
            for i in (4, 5):
                self.copy(i).start()
        elif n == 2:
            for i in (4, 5):
                self.copy(i).wait_recv()
            for y in (0, 1):
                self.half[y, own["x"]] = self.half[y, own["x"]] + self.x_came[y]
            self.copy(6).start()
        else:
            self.copy(6).wait_recv()
            self.keep[...] = self.half[own["y"], own["x"]] + self.y_came[...]

    def finish(self):
        for n in range(7):
            self.copy(n).wait_send()
        self.sums.finish()


def gather_kernel(
    depth, half, x_ref, small_src, wc_src, pc_ref, normed_ref, normt_ref, small_ref, wc_out,
    hat_ref, edge_ref, wc_ref, edge_sem, own_sem, out_sem, send, recv,
):
    place = Place(depth)
    place.meet()
    seqs, seg, features = x_ref.shape
    width = wc_src.shape[1]
    lo, hi = pl.ds(0, half), pl.ds(half, width - half)
    every = slice(None)
    weights = lambda y, x, c: wc_ref.at[y, x, c]
    lanes = [
        Gather(place, small_src, lambda y, x, c: small_ref.at[y, x, c], "y", "x", send.at[0], recv.at[0]),
        Gather(place, wc_src.at[:, lo], weights, "y", "x", send.at[1], recv.at[1], (every, lo)),
        Gather(place, wc_src.at[:, hi], weights, "x", "y", send.at[2], recv.at[2], (every, hi)),
    ]
    early, late = lanes[:2], lanes[2:]
    own = place.own
    mine = (own["y"], own["x"], own["c"], place.z)
    copies = [
        pltpu.make_async_copy(src, dst.at[mine], own_sem.at[n])
        for n, (src, dst) in enumerate(((small_src, small_ref), (wc_src, wc_ref)))
    ]
    edge = remote(x_ref.at[:, pl.ds(seg - EDGE, EDGE)], edge_ref, edge_sem.at[0], edge_sem.at[1], place.right)

    def each(group, *steps):
        for name, k in steps:
            for lane in group:
                getattr(lane, name)(k)

    def keep(n):
        at = place.flipped(*((), ("y",), ("x",), ("y", "x"))[n])
        return pltpu.make_async_copy(wc_ref.at[at["y"], at["x"]], wc_out.at[at["y"], at["x"]], out_sem.at[n])

    rows = wc_src.shape[0]
    count = 2 * depth * rows

    def norm(flips):
        at = place.flipped(*flips)
        group = 2 * at["y"] + at["x"]
        here = pl.ds(pl.multiple_of(group * count, LANES), count)
        gain = sum(
            small_ref[at["y"], at["x"], c, z, : count // LANES] for c in (0, 1) for z in range(depth)
        )
        gain = jnp.concatenate([gain[i : i + 1] for i in range(count // LANES)], axis=1)
        for s in range(seqs):
            normed = (hat_ref[s, :, here] * gain).astype(BF16)
            normed_ref[s, :, here] = normed
            turned = normed[EDGE:].astype(F32).T.astype(BF16)
            for c in (0, 1):
                normt_ref[2 * group + c, :, s * seg : (s + 1) * seg] = turned[c * depth * rows : (c + 1) * depth * rows]

    def multiply(flips, n):
        at = place.flipped(*flips)
        here = pl.ds(pl.multiple_of((2 * at["y"] + at["x"]) * count, LANES), count)
        first, last = ((0, half), (half, width))[n]
        tile = 4 * LANES
        for start in range(first, last, tile):
            cols = slice(start, min(start + tile, last))
            block = jnp.concatenate(
                [wc_ref[at["y"], at["x"], c, z, :, cols] for c in (0, 1) for z in range(depth)], axis=0
            )
            for s in range(seqs):
                part = dot(normed_ref[s, :, here], block)
                if flips == ():
                    pc_ref[s, :, cols] = part
                else:
                    pc_ref[s, :, cols] += part

    each(early, ("line", 0))
    pl.when(place.has_right)(edge.start)
    for copy in copies:
        copy.start()
    pl.when(place.has_left)(edge.wait_recv)

    @pl.when(jnp.logical_not(place.has_left))
    def _():
        edge_ref[...] = jnp.zeros_like(edge_ref)

    def scale_rows(s, start, rows_in, r, step):
        values = rows_in[s, r : r + step].astype(F32)
        mean = jnp.mean(values * values, axis=1, keepdims=True)
        hat_ref[s, start + r : start + r + step] = values * lax.rsqrt(mean + EPS)

    pieces = []
    for s in range(seqs):
        pieces.append((s, 0, edge_ref, 0, EDGE))
        pieces += [(s, EDGE, x_ref, r, 64) for r in range(0, seg, 64)]
    share = -(-len(pieces) // depth)
    for k in range(depth):
        for piece in pieces[k * share : (k + 1) * share]:
            scale_rows(*piece)
        if k + 1 < depth:
            each(early, ("line", k + 1))
        if k == depth - 2:
            each(late, ("line", 0))
    for copy in copies:
        copy.wait()
    each(early, ("core", 0))
    for k in range(1, depth):
        each(late, ("line", k))
    each(late, ("core", 0))
    for k in range(depth):
        each(early, ("from_first", k), ("from_second", k))
    each(early, ("core", 1), ("core", 2))
    each(late, ("from_first", 0), ("from_first", 1))
    each(early, ("whole", 0))
    norm(())
    multiply((), 0)
    for k in range(2, depth):
        each(late, ("from_first", k))
    each(early, ("whole", 1))
    norm(("y",))
    multiply(("y",), 0)
    for k in range(depth):
        each(late, ("from_second", k))
    each(late, ("core", 1), ("core", 2))
    each(early, ("whole", 2))
    norm(("x",))
    multiply(("x",), 0)
    each(late, ("whole", 0))
    keep(0).start()
    multiply((), 1)
    for k in range(depth - 1):
        each(lanes, ("from_both", k))
    each(late, ("whole", 1), ("whole", 2))
    keep(1).start()
    keep(2).start()
    multiply(("y",), 1)
    multiply(("x",), 1)
    each(lanes, ("from_both", depth - 1))
    each(early, ("whole", 3))
    norm(("y", "x"))
    multiply(("y", "x"), 0)
    each(late, ("whole", 3))
    keep(3).start()
    multiply(("y", "x"), 1)
    for lane in lanes:
        lane.finish()
    for n in range(4):
        keep(n).wait()
    pl.when(place.has_right)(edge.wait_send)


def gather_project(x, small, wc, depth):
    shape = jax.ShapeDtypeStruct
    seqs, seg, features = x.shape
    slots = (2, 2, 2, depth)
    sends, receives = Gather.sems(depth)
    width = wc.shape[1]
    half = width // 2 // LANES * LANES
    anywhere, vmem = pl.BlockSpec(memory_space=pl.ANY), pl.BlockSpec(memory_space=pltpu.VMEM)
    dma = pltpu.SemaphoreType.DMA
    return pl.pallas_call(
        functools.partial(gather_kernel, depth, half),
        in_specs=[vmem, vmem, vmem],
        out_specs=[vmem, vmem, vmem, vmem, anywhere],
        out_shape=[
            shape((seqs, seg + EDGE, width), F32),
            shape((seqs, seg + EDGE, features), BF16),
            shape((8, depth * wc.shape[0], seqs * seg), BF16),
            shape(slots + small.shape, F32),
            shape(slots + wc.shape, BF16),
        ],
        scratch_shapes=[
            pltpu.VMEM((seqs, seg + EDGE, features), F32),
            pltpu.VMEM((seqs, EDGE, features), BF16),
            pltpu.VMEM(slots + wc.shape, BF16),
            dma((2,)), dma((2,)), dma((4,)), dma((3, sends)), dma((3, receives)),
        ],
        compiler_params=pltpu.CompilerParams(
            collective_id=0, has_side_effects=True, vmem_limit_bytes=VMEM_LIMIT
        ),
        name="gather_project",
    )(x, small, wc)


def fwd_a_kernel(
    head_dim, pc_ref, w_ref, b_ref, raw_ref, sb_ref, dl_ref,
    x_ref, bc_ref, dt_ref, cum_ref, cumt_ref, loc0_ref, seg_ref, tot_ref, bt_ref,
):
    step = pl.program_id(0)
    seqs = pc_ref.shape[0]
    seg = pc_ref.shape[1] - EDGE
    chunks = seg // CHUNK
    w, b = w_ref[...], b_ref[...]

    def acts_of(s):
        pre = causal_conv(pc_ref[s], w, b, seg)
        return pre * sigmoid(pre)

    @pl.when(step == 0)
    def _():
        row = lax.broadcasted_iota(jnp.int32, (CHUNK, CHUNK), 0)
        col = lax.broadcasted_iota(jnp.int32, (CHUNK, CHUNK), 1)
        tri = (col <= row).astype(F32)
        rate = -jnp.exp(dl_ref[...])
        for s in range(seqs):
            acts = acts_of(s)
            bc_ref[s * seg : (s + 1) * seg] = acts
            for c in range(chunks):
                q = s * chunks + c
                rows = slice(q * CHUNK, (q + 1) * CHUNK)
                bt_ref[q] = acts[c * CHUNK : (c + 1) * CHUNK, :LANES].T.astype(BF16)
                dt = softplus(raw_ref[s, EDGE + c * CHUNK : EDGE + (c + 1) * CHUNK] + sb_ref[...])
                cum = LOG2E * jnp.dot(tri, dt * rate, precision=HIGH, preferred_element_type=F32)
                dt_ref[rows] = dt
                cum_ref[rows] = cum
                cumt_ref[:, rows] = cum.T

    @pl.when(step > 0)
    def _():
        heads = GROUP // head_dim
        first = (step - 1) * heads
        cumg = lane_shift(cum_ref[...], first)
        dtg = lane_shift(dt_ref[...], first)
        for s in range(seqs):
            x = acts_of(s)
            x_ref[s * seg : (s + 1) * seg] = x
            state, total = None, None
            for c in range(chunks):
                q = s * chunks + c
                rows = slice(q * CHUNK, (q + 1) * CHUNK)
                ce = spread_all(cumg[rows], heads, head_dim)
                de = spread_all(dtg[rows], heads, head_dim)
                end = ce[CHUNK - 1 : CHUNK]
                uw = x[c * CHUNK : (c + 1) * CHUNK] * de * jnp.exp2(end - ce)
                loc = dot(bt_ref[q], uw.astype(BF16))
                tot = jnp.exp2(end)
                tot_ref[q : q + 1] = tot
                if c == 0:
                    loc0_ref[s] = loc
                    state, total = loc, tot
                else:
                    state, total = tot * state + loc, tot * total
            seg_ref[s] = state.astype(BF16)
            tot_ref[seqs * chunks + s : seqs * chunks + s + 1] = total


def fwd_a(pc, w, b, sb, dl, inner, head_dim):
    seqs, rows, cols = pc.shape
    seg = rows - EDGE
    tokens = seqs * seg
    groups = inner // GROUP
    state = LANES
    chunks = tokens // CHUNK
    at = lambda i: (i + groups) % (groups + 1)
    back = lambda i: jnp.maximum(i - 1, 0)
    return pl.pallas_call(
        functools.partial(fwd_a_kernel, head_dim),
        grid=(groups + 1,),
        in_specs=[
            pl.BlockSpec((seqs, rows, GROUP), lambda i: (0, 0, at(i))),
            pl.BlockSpec((w.shape[0], GROUP), lambda i: (0, at(i))),
            pl.BlockSpec((1, GROUP), lambda i: (0, at(i))),
            pl.BlockSpec((seqs, rows, LANES), lambda i: (0, 0, cols // LANES - 1)),
            whole((1, LANES)),
            whole((1, LANES)),
        ],
        out_specs=[
            pl.BlockSpec((tokens, GROUP), lambda i: (0, back(i))),
            whole((tokens, GROUP)),
            whole((tokens, LANES)),
            whole((tokens, LANES)),
            whole((LANES, tokens)),
            pl.BlockSpec((seqs, state, GROUP), lambda i: (0, 0, back(i))),
            pl.BlockSpec((seqs, state, GROUP), lambda i: (0, 0, back(i))),
            pl.BlockSpec((8, GROUP), lambda i: (0, back(i))),
        ],
        out_shape=[
            jax.ShapeDtypeStruct((tokens, inner), F32),
            jax.ShapeDtypeStruct((tokens, GROUP), F32),
            jax.ShapeDtypeStruct((tokens, LANES), F32),
            jax.ShapeDtypeStruct((tokens, LANES), F32),
            jax.ShapeDtypeStruct((LANES, tokens), F32),
            jax.ShapeDtypeStruct((seqs, state, inner), F32),
            jax.ShapeDtypeStruct((seqs, state, inner), BF16),
            jax.ShapeDtypeStruct((8, inner), F32),
        ],
        scratch_shapes=[pltpu.VMEM((chunks, LANES, CHUNK), BF16)],
        compiler_params=params(),
        name="conv_states",
    )(pc, w, b, pc, sb, dl)


def fwd_b_kernel(
    head_dim, x_ref, bc_ref, dt_ref, cum_ref, cumt_ref, s0_ref, loc0_ref, tot_ref, skip_ref,
    mixed_ref, s1_ref, cb_ref,
):
    step = pl.program_id(0)
    seqs = s0_ref.shape[0]
    chunks = x_ref.shape[0] // CHUNK // seqs
    heads = GROUP // head_dim

    @pl.when(step == 0)
    def _():
        for q in range(seqs * chunks):
            rows = slice(q * CHUNK, (q + 1) * CHUNK)
            cb_ref[q] = nt(bc_ref[rows, LANES:].astype(BF16), bc_ref[rows, :LANES].astype(BF16))

    first = step * heads
    cumg = lane_shift(cum_ref[...], first)
    dtg = lane_shift(dt_ref[...], first)
    cumr = head_rows(cumt_ref, first)
    row = lax.broadcasted_iota(jnp.int32, (CHUNK, CHUNK), 0)
    col = lax.broadcasted_iota(jnp.int32, (CHUNK, CHUNK), 1)
    causal = col <= row
    skip = skip_ref[...]
    for s in range(seqs):
        start = s0_ref[s]
        for c in range(chunks):
            q = s * chunks + c
            rows = slice(q * CHUNK, (q + 1) * CHUNK)
            x = x_ref[rows]
            ce = spread_all(cumg[rows], heads, head_dim)
            de = spread_all(dtg[rows], heads, head_dim)
            ub = (x * de).astype(BF16)
            cb = cb_ref[q]
            parts = []
            for j in range(0, heads, 2):
                mats = []
                for h in (j, j + 1):
                    there = jnp.broadcast_to(cumg[rows, h : h + 1], (CHUNK, CHUNK))
                    here = cumr[h : h + 1, rows]
                    decay = jnp.exp2(jnp.where(causal, there - here, -jnp.inf))
                    mats.append((decay * cb).astype(BF16))
                pair = ub[:, j * head_dim : (j + 2) * head_dim]
                parts.append(dot(jnp.concatenate(mats, axis=1), block_diagonal(pair, head_dim)))
            y = jnp.concatenate(parts, axis=1)
            y = y + jnp.exp2(ce) * dot(bc_ref[rows, LANES:].astype(BF16), start)
            mixed_ref[rows] = y + skip * x
            if c == 0:
                start = (tot_ref[q : q + 1] * start.astype(F32) + loc0_ref[s]).astype(BF16)
                s1_ref[s] = start


def fwd_b(x, bc, dt, cum, cumt, s0, loc0, tot, skip, head_dim):
    tokens, inner = x.shape
    seqs, state, _ = s0.shape
    groups = inner // GROUP
    wide = pl.BlockSpec((tokens, GROUP), lambda i: (0, i))
    states = pl.BlockSpec((seqs, state, GROUP), lambda i: (0, 0, i))
    return pl.pallas_call(
        functools.partial(fwd_b_kernel, head_dim),
        grid=(groups,),
        in_specs=[
            wide, whole(bc.shape), whole(dt.shape), whole(cum.shape), whole(cumt.shape),
            states, states,
            pl.BlockSpec((8, GROUP), lambda i: (0, i)),
            pl.BlockSpec((1, GROUP), lambda i: (0, i)),
        ],
        out_specs=[wide, states],
        out_shape=[
            jax.ShapeDtypeStruct((tokens, inner), F32),
            jax.ShapeDtypeStruct((seqs, state, inner), BF16),
        ],
        scratch_shapes=[pltpu.VMEM((tokens // CHUNK, CHUNK, CHUNK), F32)],
        compiler_params=params(),
        name="scan_outputs",
    )(x, bc, dt, cum, cumt, s0, loc0, tot, skip)


def halves(v):
    high = v.astype(BF16)
    return high, (v - high.astype(F32)).astype(BF16)


def dot_pairs(a, b, dims=((1,), (0,))):
    (ah, al), (bh, bl) = halves(a), halves(b)
    return dot(ah, bh, dims) + (dot(al, bh, dims) + dot(ah, bl, dims))


def dot_pair(a, b, dims=((1,), (0,))):
    high, low = halves(a)
    return dot(high, b, dims) + dot(low, b, dims)


def nt_exact(a, b):
    return lax.dot_general(a, b, (((1,), (1,)), ((), ())), precision=HIGH, preferred_element_type=F32)


class Chain:
    def __init__(self, place, came, sent, send, recv, backward):
        self.came, self.sent, self.send, self.recv = came, sent, send, recv
        self.gets, self.gives = place.has_left, place.has_right
        self.to = place.left if backward else place.right
        if backward:
            self.gets, self.gives = self.gives, self.gets
        self.behind = place.depth - 1 - place.z if backward else place.z

    def copy(self, g):
        return remote(self.sent.at[g], self.came.at[g], self.send.at[g], self.recv.at[g], self.to)

    def step(self, g, total, own):
        pl.when(self.gets)(lambda: self.copy(g).wait_recv())

        @pl.when(jnp.logical_not(self.gets))
        def _():
            self.came[g] = jnp.zeros(self.came.shape[1:], self.came.dtype)

        self.sent[g] = (total * self.came[g].astype(F32) + own).astype(BF16)
        pl.when(self.gives)(lambda: self.copy(g).start())

    def finish(self):
        groups = self.came.shape[0]

        def one(g, carry):
            self.copy(g).wait_send()
            return carry

        @pl.when(self.gives)
        def _():
            lax.fori_loop(0, groups, one, 0)


def scan_forward_kernel(
    depth, head_dim, groups,
    pc_ref, w_ref, b_ref, raw_ref, sb_ref, dl_ref, skip_ref, normed_ref, cot_ref, wi_src, wo_src,
    bc_ref, dt_ref, cum_ref, cumt_ref, mixed_ref, s0_ref, s1_ref, s2_ref, tot_ref, z_out, dno_out, wg_out, wo_out,
    bt_ref, cb_ref, x_ring, loc_ring, seg_ring, tot_ring, came, sent,
    z_ref, dno_ref, wg_ref, wo_ref, chain_send, chain_recv, own_sem, keep_sem, out_sem, send, recv,
):
    step = pl.program_id(0)
    lag = depth - 1
    seqs = pc_ref.shape[0]
    seg = pc_ref.shape[1] - EDGE
    chunks = seg // CHUNK
    heads = GROUP // head_dim
    w, b = w_ref[...], b_ref[...]
    place = Place(depth)
    chain = Chain(place, came, sent, chain_send, chain_recv, False)
    wg_src = wi_src.at[:, pl.ds(0, z_ref.shape[1])]
    gate = Gather(place, wg_src, lambda y, x, c: wg_ref.at[y, x, c], "y", "x", send.at[0], recv.at[0])
    out = Gather(place, wo_src, lambda y, x, c: wo_ref.at[y, x, c], "x", "y", send.at[1], recv.at[1])
    mine = (place.own["y"], place.own["x"], place.own["c"], place.z)
    copies = [
        pltpu.make_async_copy(wg_src, wg_ref.at[mine], own_sem.at[0]),
        pltpu.make_async_copy(wo_src, wo_ref.at[mine], own_sem.at[1]),
    ]

    def waves(*steps):
        for lane, name, k in steps:
            getattr(lane, name)(k)

    def acts_of(s):
        pre = causal_conv(pc_ref[s], w, b, seg)
        return pre * sigmoid(pre)

    @pl.when(step == 0)
    def _():
        place.meet()
        waves((gate, "line", 0))
        for copy in copies:
            copy.start()
        row = lax.broadcasted_iota(jnp.int32, (CHUNK, CHUNK), 0)
        col = lax.broadcasted_iota(jnp.int32, (CHUNK, CHUNK), 1)
        tri = (col <= row).astype(F32)
        rate = -jnp.exp(dl_ref[...])
        for s in range(seqs):
            acts = acts_of(s)
            bc_ref[s * seg : (s + 1) * seg] = acts
            for c in range(chunks):
                q = s * chunks + c
                rows = slice(q * CHUNK, (q + 1) * CHUNK)
                b_proj = acts[c * CHUNK : (c + 1) * CHUNK, :LANES]
                c_proj = acts[c * CHUNK : (c + 1) * CHUNK, LANES:]
                bt_ref[q] = b_proj.T
                cb_ref[q] = nt_exact(c_proj, b_proj)
                dt = softplus(raw_ref[s, EDGE + c * CHUNK : EDGE + (c + 1) * CHUNK] + sb_ref[...])
                cum = LOG2E * jnp.dot(tri, dt * rate, precision=HIGH, preferred_element_type=F32)
                dt_ref[rows] = dt
                cum_ref[rows] = cum
                cumt_ref[:, rows] = cum.T

    @pl.when((step > 0) & (step <= groups))
    def _():
        g = step - 1
        at = lax.rem(g, lag + 1)
        first = g * heads
        cumg = lane_shift(cum_ref[...], first)
        dtg = lane_shift(dt_ref[...], first)
        for s in range(seqs):
            x = acts_of(s)
            x_ring[at, s * seg : (s + 1) * seg] = x
            state, total = None, None
            for c in range(chunks):
                q = s * chunks + c
                rows = slice(q * CHUNK, (q + 1) * CHUNK)
                ce = spread_all(cumg[rows], heads, head_dim)
                de = spread_all(dtg[rows], heads, head_dim)
                end = ce[CHUNK - 1 : CHUNK]
                uw = x[c * CHUNK : (c + 1) * CHUNK] * de * jnp.exp2(end - ce)
                loc = dot_pairs(bt_ref[q], uw)
                tot = jnp.exp2(end)
                tot_ring[at, q : q + 1] = tot
                if c == 0:
                    loc_ring[at, s] = loc
                    state, total = loc, tot
                else:
                    state, total = tot * state + loc, tot * total
            seg_ring[at, s] = state
            tot_ring[at, seqs * chunks + s : seqs * chunks + s + 1] = total

    handed = step - 1 - chain.behind

    @pl.when((handed >= 0) & (handed < groups))
    def _():
        at = lax.rem(handed, lag + 1)
        totals = tot_ring[at, seqs * chunks : seqs * chunks + seqs]
        chain.step(handed, totals[:, None, :], seg_ring[at])

    @pl.when(step > lag)
    def _():
        g = step - 1 - lag
        at = lax.rem(g, lag + 1)
        first = g * heads
        cumg = lane_shift(cum_ref[...], first)
        dtg = lane_shift(dt_ref[...], first)
        cumr = head_rows(cumt_ref, first)
        row = lax.broadcasted_iota(jnp.int32, (CHUNK, CHUNK), 0)
        col = lax.broadcasted_iota(jnp.int32, (CHUNK, CHUNK), 1)
        causal = col <= row
        skip = skip_ref[...]
        s0_ref[...] = came[g]
        s2_ref[...] = sent[g]
        tot_ref[...] = tot_ring[at]
        for s in range(seqs):
            start = came[g, s]
            for c in range(chunks):
                q = s * chunks + c
                rows = slice(q * CHUNK, (q + 1) * CHUNK)
                x = x_ring[at, rows]
                ce = spread_all(cumg[rows], heads, head_dim)
                de = spread_all(dtg[rows], heads, head_dim)
                ub = (x * de).astype(BF16)
                cb = cb_ref[q]
                parts = []
                for j in range(0, heads, 2):
                    mats = []
                    for h in (j, j + 1):
                        there = jnp.broadcast_to(cumg[rows, h : h + 1], (CHUNK, CHUNK))
                        here = cumr[h : h + 1, rows]
                        decay = jnp.exp2(jnp.where(causal, there - here, -jnp.inf))
                        mats.append((decay * cb).astype(BF16))
                    pair = ub[:, j * head_dim : (j + 2) * head_dim]
                    parts.append(dot(jnp.concatenate(mats, axis=1), block_diagonal(pair, head_dim)))
                y = jnp.concatenate(parts, axis=1)
                y = y + jnp.exp2(ce) * dot(bc_ref[rows, LANES:].astype(BF16), start)
                mixed_ref[rows] = y + skip * x
                if c == 0:
                    later = tot_ring[at, q : q + 1] * start.astype(F32) + loc_ring[at, s]
                    s1_ref[s] = later
                    start = later.astype(BF16)

    every = range(depth)
    by_group = ((), ("y",), ("x",), ("y", "x"))

    def both(lane, *waves_of):
        return [(lane, name, k) for k in waves_of for name in ("from_first", "from_second")]

    beside = {
        3: [(gate, "line", 1)],
        6: [(gate, "line", 2), (out, "line", 0)],
        9: [(gate, "line", 3), *both(gate, 0)],
        11: [(out, "line", 1), *both(gate, 1)],
        13: both(gate, 2),
    }
    for at, steps in beside.items():
        pl.when(step == at)(lambda: waves(*steps))

    @pl.when(step == 9)
    def _():
        for copy in copies:
            copy.wait()
        waves((gate, "core", 0))

    @pl.when(step == groups + lag)
    def _():
        rows = 2 * depth * wi_src.shape[0]
        tile = 4 * LANES
        size = dno_ref.shape[1] // 8

        def keep(lane, g):
            src, dst = (wg_ref, wg_out) if lane is gate else (wo_ref, wo_out)
            at = place.flipped(*by_group[g])
            return pltpu.make_async_copy(
                src.at[at["y"], at["x"]], dst.at[at["y"], at["x"]], keep_sem.at[int(lane is out), g]
            )

        def ready(lane, g):
            lane.whole(g if g in (0, 3) or lane is gate else 3 - g)
            keep(lane, g).start()

        def group_of(g):
            at = place.flipped(*by_group[g])
            return 2 * at["y"] + at["x"]

        def gate_product(g):
            at = place.flipped(*by_group[g])
            here = pl.ds(pl.multiple_of(group_of(g) * rows, LANES), rows)
            for start in range(0, z_ref.shape[1], tile):
                cols = slice(start, start + tile)
                block = jnp.concatenate(
                    [wg_ref[at["y"], at["x"], c, z, :, cols] for c in (0, 1) for z in every], axis=0
                )
                for s in range(seqs):
                    part = dot(normed_ref[s, EDGE:, here], block)
                    at_rows = slice(s * seg, (s + 1) * seg)
                    if g == 0:
                        z_ref[at_rows, cols] = part
                    else:
                        z_ref[at_rows, cols] += part

        def out_product(g):
            at = place.flipped(*by_group[g])
            for c in (0, 1):
                block = jnp.concatenate([wo_ref[at["y"], at["x"], c, z] for z in every], axis=0)
                cols = pl.ds(pl.multiple_of((2 * group_of(g) + c) * size, LANES), size)
                dno_ref[:, cols] = nt(cot_ref[...], block)
            dno_copy(g).start()

        def dno_copy(g):
            cols = pl.ds(pl.multiple_of(group_of(g) * 2 * size, LANES), 2 * size)
            return pltpu.make_async_copy(dno_ref.at[:, cols], dno_out.at[:, cols], out_sem.at[g])

        last = depth - 1
        waves((out, "line", 2), *both(gate, 3), (gate, "core", 1), (gate, "core", 2))
        waves((out, "from_first", 0))
        ready(gate, 0)
        gate_product(0)
        waves((out, "line", 3), (out, "core", 0), (out, "from_first", 1))
        ready(gate, 1)
        gate_product(1)
        waves((out, "from_first", 2), (out, "from_second", 0), (out, "from_second", 1), (gate, "from_both", 0))
        ready(gate, 2)
        gate_product(2)
        waves((out, "from_first", 3), (out, "from_second", 2), (out, "from_second", 3))
        waves((out, "core", 1), (out, "core", 2), (gate, "from_both", 1))
        ready(out, 0)
        out_product(0)
        waves((gate, "from_both", 2), (out, "from_both", 0), (out, "from_both", 1))
        ready(out, 1)
        out_product(1)
        waves((out, "from_both", 2))
        ready(out, 2)
        out_product(2)
        waves((gate, "from_both", last), (out, "from_both", last))
        ready(gate, 3)
        gate_product(3)
        z_copy = pltpu.make_async_copy(z_ref, z_out, out_sem.at[4])
        z_copy.start()
        ready(out, 3)
        out_product(3)
        for lane in (gate, out):
            lane.finish()
        chain.finish()
        for g in range(4):
            dno_copy(g).wait()
            keep(gate, g).wait()
            keep(out, g).wait()
        z_copy.wait()


def scan_forward(pc, w, b, sb, dl, skip, normed, cot, w_in, wo, inner, head_dim, depth):
    seqs, rows, cols = pc.shape
    tokens = seqs * (rows - EDGE)
    groups = inner // GROUP
    lag = depth - 1
    chunks = tokens // CHUNK
    shape, dma = jax.ShapeDtypeStruct, pltpu.SemaphoreType.DMA
    into = lambda i: jnp.where(i == 0, groups, jnp.minimum(i - 1, groups - 1))
    out = lambda i: jnp.maximum(i - 1 - lag, 0)
    states = pl.BlockSpec((seqs, LANES, GROUP), lambda i: (0, 0, out(i)))
    anywhere = pl.BlockSpec(memory_space=pl.ANY)
    sends, receives = Gather.sems(depth)
    slots = (2, 2, 2, depth)
    ring = lambda *dims: pltpu.VMEM((lag + 1,) + dims, F32)
    link = pltpu.VMEM((groups, seqs, LANES, GROUP), BF16)
    once = lambda v: pl.BlockSpec(v.shape, lambda i: (0,) * v.ndim, pipeline_mode=pl.Buffered(1))
    return pl.pallas_call(
        functools.partial(scan_forward_kernel, depth, head_dim, groups),
        grid=(groups + 1 + lag,),
        in_specs=[
            pl.BlockSpec((seqs, rows, GROUP), lambda i: (0, 0, into(i))),
            pl.BlockSpec((w.shape[0], GROUP), lambda i: (0, into(i))),
            pl.BlockSpec((1, GROUP), lambda i: (0, into(i))),
            pl.BlockSpec((seqs, rows, LANES), lambda i: (0, 0, cols // LANES - 1)),
            whole((1, LANES)),
            whole((1, LANES)),
            pl.BlockSpec((1, GROUP), lambda i: (0, out(i))),
            once(normed),
            once(cot),
            once(w_in),
            once(wo),
        ],
        out_specs=[
            whole((tokens, GROUP)),
            whole((tokens, LANES)),
            whole((tokens, LANES)),
            whole((LANES, tokens)),
            pl.BlockSpec((tokens, GROUP), lambda i: (0, out(i))),
            states, states, states,
            pl.BlockSpec((8, GROUP), lambda i: (0, out(i))),
            anywhere,
            anywhere,
            anywhere,
            anywhere,
        ],
        out_shape=[
            shape((tokens, GROUP), F32),
            shape((tokens, LANES), F32),
            shape((tokens, LANES), F32),
            shape((LANES, tokens), F32),
            shape((tokens, inner), F32),
            shape((seqs, LANES, inner), BF16),
            shape((seqs, LANES, inner), F32),
            shape((seqs, LANES, inner), BF16),
            shape((8, inner), F32),
            shape((tokens, inner), F32),
            shape((tokens, inner), F32),
            shape(slots + (w_in.shape[0], inner), BF16),
            shape(slots + wo.shape, BF16),
        ],
        scratch_shapes=[
            pltpu.VMEM((chunks, LANES, CHUNK), F32),
            pltpu.VMEM((chunks, CHUNK, CHUNK), F32),
            ring(tokens, GROUP), ring(seqs, LANES, GROUP), ring(seqs, LANES, GROUP), ring(8, GROUP),
            link, link,
            pltpu.VMEM((tokens, inner), F32), pltpu.VMEM((tokens, inner), F32),
            pltpu.VMEM(slots + (w_in.shape[0], inner), BF16), pltpu.VMEM(slots + wo.shape, BF16),
            dma((groups,)), dma((groups,)), dma((2,)), dma((2, 4)), dma((5,)), dma((2, sends)), dma((2, receives)),
        ],
        compiler_params=pltpu.CompilerParams(
            dimension_semantics=("arbitrary",), collective_id=3, has_side_effects=True,
            vmem_limit_bytes=VMEM_LIMIT,
        ),
        name="scan_forward",
    )(pc, w, b, pc, sb, dl, skip, normed, cot, w_in, wo)


def mid_kernel(
    z_ref, dno_ref, mixed_ref, wo_ref, gain_ref, in_ref, not_ref, out_ref, dm_ref, dz_ref, gg_ref, acc_ref,
):
    step = pl.program_id(0)
    inner = mixed_ref.shape[1]
    tiles, tile = not_ref.shape[0], not_ref.shape[1]

    @pl.when(step == 0)
    def _():
        gg_ref[...] = jnp.zeros_like(gg_ref)

    def lanes_of(i):
        return pl.ds(pl.multiple_of(i * tile, tile), tile)

    def fold(v):
        total = v[:, :LANES]
        for k in range(LANES, tile, LANES):
            total = total + v[:, k : k + LANES]
        return total

    def one(i, sums):
        sq, hg = sums
        at = lanes_of(i)
        z = z_ref[:, at]
        g = mixed_ref[:, at] * z * sigmoid(z)
        return sq + fold(g * g), hg + fold(dno_ref[:, at] * gain_ref[:, at] * g)

    zero = jnp.zeros((mixed_ref.shape[0], LANES), F32)
    sq, hg = lax.fori_loop(0, tiles, one, (zero, zero))
    scale = lax.rsqrt(jnp.sum(sq, axis=1, keepdims=True) / inner + EPS)
    pull = scale * scale * scale * (jnp.sum(hg, axis=1, keepdims=True) / inner)
    acc_ref[...] = in_ref[...].astype(F32)

    def two(i, carry):
        at = lanes_of(i)
        z, mixed, dno, gain = z_ref[:, at], mixed_ref[:, at], dno_ref[:, at], gain_ref[:, at]
        sig = sigmoid(z)
        act = z * sig
        g = mixed * act
        gs = g * scale
        no = gs * gain
        not_ref[i] = no.T.astype(BF16)
        acc_ref[...] += dot(no.astype(BF16), wo_ref[at, :])
        gg_ref[:, at] += jnp.sum(dno * gs, axis=0, keepdims=True)
        dg = scale * (dno * gain) - g * pull
        dm_ref[:, at] = dg * act
        dz_ref[:, at] = (dg * mixed * (sig * (1.0 + z * (1.0 - sig)))).astype(BF16)
        return carry

    lax.fori_loop(0, tiles, two, 0)
    out_ref[...] = acc_ref[...].astype(BF16)


def mid(z, dno, mixed, wo, gain, inputs, tiles):
    tokens, inner = mixed.shape
    width = inputs.shape[1]
    tile = inner // tiles
    narrow = pl.BlockSpec((CHUNK, width), lambda i: (i, 0))
    wide = pl.BlockSpec((CHUNK, inner), lambda i: (i, 0))
    once = lambda v: pl.BlockSpec(v.shape, lambda i: (0,) * v.ndim, pipeline_mode=pl.Buffered(1))
    return pl.pallas_call(
        mid_kernel,
        grid=(tokens // CHUNK,),
        in_specs=[wide, wide, wide, once(wo), whole((1, inner)), narrow],
        out_specs=[
            pl.BlockSpec((tiles, tile, CHUNK), lambda i: (0, 0, i)), narrow, wide, wide,
            whole((1, inner)),
        ],
        out_shape=[
            jax.ShapeDtypeStruct((tiles, tile, tokens), BF16),
            jax.ShapeDtypeStruct((tokens, width), BF16),
            jax.ShapeDtypeStruct((tokens, inner), F32),
            jax.ShapeDtypeStruct((tokens, inner), BF16),
            jax.ShapeDtypeStruct((1, inner), F32),
        ],
        scratch_shapes=[pltpu.VMEM((CHUNK, width), F32)],
        compiler_params=params(),
        name="gate_norm_project",
    )(z, dno, mixed, wo, gain, inputs)


def bwd_a_kernel(head_dim, seqs, dm_ref, bc_ref, cum_ref, tot_ref, seg_ref, ct_ref):
    step = pl.program_id(0)
    chunks = dm_ref.shape[0] // CHUNK // seqs
    heads = GROUP // head_dim

    @pl.when(step == 0)
    def _():
        for q in range(seqs * chunks):
            ct_ref[q] = bc_ref[q * CHUNK : (q + 1) * CHUNK, LANES:].T.astype(BF16)

    cumg = lane_shift(cum_ref[...], step * heads)
    for s in range(seqs):
        state = None
        for c in range(chunks - 1, -1, -1):
            q = s * chunks + c
            rows = slice(q * CHUNK, (q + 1) * CHUNK)
            ey = jnp.exp2(spread_all(cumg[rows], heads, head_dim)) * dm_ref[rows]
            loc = dot(ct_ref[q], ey.astype(BF16))
            state = loc if state is None else tot_ref[q : q + 1] * state + loc
        seg_ref[s] = state.astype(BF16)


def bwd_a(dm, bc, cum, tot, seqs, head_dim):
    tokens, inner = dm.shape
    return pl.pallas_call(
        functools.partial(bwd_a_kernel, head_dim, seqs),
        grid=(inner // GROUP,),
        in_specs=[
            pl.BlockSpec((tokens, GROUP), lambda i: (0, i)), whole(bc.shape), whole(cum.shape),
            pl.BlockSpec((8, GROUP), lambda i: (0, i)),
        ],
        out_specs=pl.BlockSpec((seqs, LANES, GROUP), lambda i: (0, 0, i)),
        out_shape=jax.ShapeDtypeStruct((seqs, LANES, inner), BF16),
        scratch_shapes=[pltpu.VMEM((tokens // CHUNK, LANES, CHUNK), BF16)],
        compiler_params=params(),
        name="adjoint_states",
    )(dm, bc, cum, tot)


def bwd_b_kernel(
    head_dim, groups, pc_ref, w_ref, b_ref, raw_ref, sb_ref, dl_ref, bc_ref, dt_ref, cum_ref, cumt_ref,
    dm_ref, mixed_ref, s0_ref, s1_ref, s2_ref, g_ref, tot_ref, skip_ref,
    dc_ref, tail_ref, edge_ref, gw_ref, gb_ref, gskip_ref, draw_ref, hsum_ref,
    cbt_ref, dcbt_ref, db_acc, dc_acc, r1_ref, r2_ref, dtot_ref,
):
    step = pl.program_id(0)
    seqs = pc_ref.shape[0]
    seg = pc_ref.shape[1] - EDGE
    chunks = seg // CHUNK
    heads = GROUP // head_dim
    w, b = w_ref[...], b_ref[...]
    taps = w.shape[0]

    @pl.when(step == 0)
    def _():
        for q in range(seqs * chunks):
            rows = slice(q * CHUNK, (q + 1) * CHUNK)
            cbt_ref[q] = nt(bc_ref[rows, :LANES].astype(BF16), bc_ref[rows, LANES:].astype(BF16))
        dcbt_ref[...] = jnp.zeros_like(dcbt_ref)
        db_acc[...] = jnp.zeros_like(db_acc)
        dc_acc[...] = jnp.zeros_like(dc_acc)
        r1_ref[...] = jnp.zeros_like(r1_ref)
        r2_ref[...] = jnp.zeros_like(r2_ref)
        dtot_ref[...] = jnp.zeros_like(dtot_ref)

    def conv_back(s, ext, pre, sig, d_act):
        d_pre = d_act * (sig * (1.0 + pre * (1.0 - sig)))
        zero = jnp.zeros((EDGE, d_pre.shape[1]), F32)
        padded = jnp.concatenate([zero, d_pre, zero], axis=0)
        total = None
        for k in range(taps):
            at = taps - 1 - k
            term = w[k : k + 1] * padded[at : at + seg + EDGE]
            total = term if total is None else total + term
        edge_ref[s] = total[:EDGE]
        dc_ref[s * seg : (s + 1) * seg] = total[EDGE:].astype(BF16)
        tail_ref[s] = total[seg:]
        for k in range(taps):
            at = EDGE - (taps - 1) + k
            grad = jnp.sum(ext[at : at + seg] * d_pre, axis=0, keepdims=True)
            gw_ref[k : k + 1] = grad if s == 0 else gw_ref[k : k + 1] + grad
        grad = jnp.sum(d_pre, axis=0, keepdims=True)
        gb_ref[...] = grad if s == 0 else gb_ref[...] + grad

    def by_head(value, pick):
        high = value.astype(BF16)
        return dot(high, pick) + dot((value - high.astype(F32)).astype(BF16), pick)

    @pl.when(step < groups)
    def _():
        first = step * heads
        cumg = lane_shift(cum_ref[...], first)
        dtg = lane_shift(dt_ref[...], first)
        cumr = head_rows(cumt_ref, first)
        row = lax.broadcasted_iota(jnp.int32, (CHUNK, CHUNK), 0)
        col = lax.broadcasted_iota(jnp.int32, (CHUNK, CHUNK), 1)
        causal = row <= col
        lane = lax.broadcasted_iota(jnp.int32, (GROUP, LANES), 0)
        head = lax.broadcasted_iota(jnp.int32, (GROUP, LANES), 1)
        pick = (head == first + lane // head_dim).astype(BF16)
        skip = skip_ref[...]
        grad_skip = None
        for s in range(seqs):
            ext = pc_ref[s]
            pre = causal_conv(ext, w, b, seg)
            sig = sigmoid(pre)
            acts = pre * sig
            adj = g_ref[s].astype(F32)
            d_acts = [None] * chunks
            for c in range(chunks - 1, -1, -1):
                q = s * chunks + c
                rows = slice(q * CHUNK, (q + 1) * CHUNK)
                x = acts[c * CHUNK : (c + 1) * CHUNK]
                dy = dm_ref[rows]
                ce = spread_all(cumg[rows], heads, head_dim)
                de = spread_all(dtg[rows], heads, head_dim)
                weight = jnp.exp2(ce[CHUNK - 1 : CHUNK] - ce)
                u = x * de
                ub = u.astype(BF16)
                dyb = dy.astype(BF16)
                cbt = cbt_ref[q]
                parts = []
                dcbt = dcbt_ref[q]
                for j in range(0, heads, 2):
                    lanes = slice(j * head_dim, (j + 2) * head_dim)
                    dy_block = block_diagonal(dyb[:, lanes], head_dim)
                    dm = nt(ub[:, lanes], dy_block)
                    mats = []
                    for k, h in enumerate((j, j + 1)):
                        here = jnp.broadcast_to(cumg[rows, h : h + 1], (CHUNK, CHUNK))
                        there = cumr[h : h + 1, rows]
                        decay = jnp.exp2(jnp.where(causal, there - here, -jnp.inf))
                        mats.append((decay * cbt).astype(BF16))
                        dcbt = dcbt + decay * dm[:, k * CHUNK : (k + 1) * CHUNK]
                    parts.append(dot(jnp.concatenate(mats, axis=1), dy_block))
                dcbt_ref[q] = dcbt
                start = s0_ref[s] if c == 0 else s1_ref[s]
                end = s2_ref[s] if c == chunks - 1 else s1_ref[s]
                adj_b = adj.astype(BF16)
                bb = bc_ref[rows, :LANES].astype(BF16)
                cb = bc_ref[rows, LANES:].astype(BF16)
                ey = (jnp.exp2(ce) * dy).astype(BF16)
                du = jnp.concatenate(parts, axis=1) + weight * dot(bb, adj_b)
                db_acc[rows] += nt((u * weight).astype(BF16), adj_b)
                dc_acc[rows] += nt(ey, start)
                r1_ref[rows] += by_head(dyb.astype(F32) * (mixed_ref[rows] - skip * x), pick)
                r2_ref[rows] += by_head(x * du, pick)
                dtot_ref[q : q + 1] += by_head(
                    jnp.sum(adj * end.astype(F32), axis=0, keepdims=True), pick
                )
                grad = jnp.sum(dy * x, axis=0, keepdims=True)
                grad_skip = grad if grad_skip is None else grad_skip + grad
                d_acts[c] = du * de + skip * dy
                if c > 0:
                    adj = tot_ref[q : q + 1] * adj + dot(cb, ey, ((0,), (0,)))
            conv_back(s, ext, pre, sig, jnp.concatenate(d_acts, axis=0))
        gskip_ref[...] = grad_skip

    @pl.when(step == groups)
    def _():
        row = lax.broadcasted_iota(jnp.int32, (CHUNK, CHUNK), 0)
        col = lax.broadcasted_iota(jnp.int32, (CHUNK, CHUNK), 1)
        later = (row <= col).astype(F32)
        rate = -jnp.exp(dl_ref[...])
        sum_raw = jnp.zeros((1, LANES), F32)
        sum_log = jnp.zeros((1, LANES), F32)
        for s in range(seqs):
            ext = pc_ref[s]
            pre = causal_conv(ext, w, b, seg)
            sig = sigmoid(pre)
            parts = []
            for c in range(chunks):
                q = s * chunks + c
                rows = slice(q * CHUNK, (q + 1) * CHUNK)
                dcbt = dcbt_ref[q]
                bb = bc_ref[rows, :LANES].astype(BF16)
                cb = bc_ref[rows, LANES:].astype(BF16)
                d_b = db_acc[rows] + dot(dcbt.astype(BF16), cb)
                d_c = dc_acc[rows] + dot(dcbt.T.astype(BF16), bb)
                parts.append(jnp.concatenate([d_b, d_c], axis=1))
                dt = dt_ref[rows]
                r2 = r2_ref[rows]
                d_log = jnp.dot(
                    later, r1_ref[rows] - dt * r2, precision=HIGH, preferred_element_type=F32
                )
                d_log = d_log + dtot_ref[q : q + 1]
                raw = raw_ref[s, EDGE + c * CHUNK : EDGE + (c + 1) * CHUNK] + sb_ref[...]
                d_raw = (r2 + rate * d_log) * sigmoid(raw)
                draw_ref[rows] = d_raw
                sum_raw = sum_raw + jnp.sum(d_raw, axis=0, keepdims=True)
                sum_log = sum_log + jnp.sum(d_log * dt, axis=0, keepdims=True) * rate
            conv_back(s, ext, pre, sig, jnp.concatenate(parts, axis=0))
        hsum_ref[0:1] = sum_raw
        hsum_ref[1:2] = sum_log


def bwd_b(pc, w, b, sb, dl, bc, dt, cum, cumt, dm, mixed, s0, s1, s2, g, tot, skip, head_dim):
    seqs, rows, cols = pc.shape
    tokens, inner = dm.shape
    groups = inner // GROUP
    taps, channels = w.shape
    wide = pl.BlockSpec((tokens, GROUP), lambda i: (0, jnp.minimum(i, groups - 1)))
    states = pl.BlockSpec((seqs, LANES, GROUP), lambda i: (0, 0, jnp.minimum(i, groups - 1)))
    line = lambda n: pl.BlockSpec((n, GROUP), lambda i: (0, jnp.minimum(i, groups - 1)))
    conv = lambda n: pl.BlockSpec((n, GROUP), lambda i: (0, i))
    ends = pl.BlockSpec((seqs, EDGE, GROUP), lambda i: (0, 0, i))
    chunks = tokens // CHUNK
    shape = jax.ShapeDtypeStruct
    return pl.pallas_call(
        functools.partial(bwd_b_kernel, head_dim, groups),
        grid=(groups + 1,),
        in_specs=[
            pl.BlockSpec((seqs, rows, GROUP), lambda i: (0, 0, i)),
            conv(taps),
            conv(1),
            pl.BlockSpec((seqs, rows, LANES), lambda i: (0, 0, cols // LANES - 1)),
            whole((1, LANES)), whole((1, LANES)),
            whole(bc.shape), whole(dt.shape), whole(cum.shape), whole(cumt.shape),
            wide, wide, states, states, states, states, line(8), line(1),
        ],
        out_specs=[
            conv(tokens), ends, ends, conv(taps), conv(1), line(1),
            whole((tokens, LANES)), whole((2, LANES)),
        ],
        out_shape=[
            shape((tokens, channels), BF16),
            shape((seqs, EDGE, channels), F32),
            shape((seqs, EDGE, channels), F32),
            shape((taps, channels), F32),
            shape((1, channels), F32),
            shape((1, inner), F32),
            shape((tokens, LANES), F32),
            shape((2, LANES), F32),
        ],
        scratch_shapes=[
            pltpu.VMEM((chunks, CHUNK, CHUNK), F32),
            pltpu.VMEM((chunks, CHUNK, CHUNK), F32),
            pltpu.VMEM((tokens, LANES), F32),
            pltpu.VMEM((tokens, LANES), F32),
            pltpu.VMEM((tokens, LANES), F32),
            pltpu.VMEM((tokens, LANES), F32),
            pltpu.VMEM((8, LANES), F32),
        ],
        compiler_params=params(),
        name="scan_backward",
    )(pc, w, b, pc, sb, dl, bc, dt, cum, cumt, dm, mixed, s0, s1, s2, g, tot, skip)


PIECES = (3, 2, 1)


def piece_of(columns, n):
    unit = columns // sum(PIECES)
    return sum(PIECES[:n]) * unit, sum(PIECES[: n + 1]) * unit


def pair_copies(place, lhs, rhs, send, recv):
    other = 1 - place.own["c"]
    parts = [(src.at[2 * g + other], dst.at[g]) for src, dst in lhs for g in range(4)] + list(rhs)
    return [
        remote(src, dst, send.at[n], recv.at[n], place.to["c"]) for n, (src, dst) in enumerate(parts)
    ]


def scan_backward_kernel(
    depth, head_dim, groups,
    pc_ref, w_ref, b_ref, raw_ref, sb_ref, dl_ref, bc_ref, dt_ref, cum_ref, cumt_ref,
    dma_ref, dm_ref, mixed_ref, s0_ref, s1_ref, s2_ref, tot_ref, skip_ref,
    nt_src, dz_src, no_src, cot_src,
    dc_out, gw_ref, gb_ref, hsum_ref, a_out, b_out, nt_out,
    cbt_ref, ct_ref, dcbt_ref, db_acc, dc_acc, r1_ref, r2_ref, dtot_ref, skip_acc,
    dc_ref, tail_ref, edge_ref, edge_came, seg_ring, tot_ring, came, sent,
    nt_pair, dz_pair, no_pair, cot_pair,
    chain_send, chain_recv, edge_send, edge_recv, pair_send, pair_recv, out_sem, send, recv, *bufs,
):
    step = pl.program_id(0)
    lag = depth - 1
    seqs = pc_ref.shape[0]
    seg = pc_ref.shape[1] - EDGE
    chunks = seg // CHUNK
    heads = GROUP // head_dim
    w, b = w_ref[...], b_ref[...]
    taps = w.shape[0]
    channels = tail_ref.shape[2]
    place = Place(depth)
    chain = Chain(place, came, sent, chain_send, chain_recv, True)
    cut = lambda ref, lo, hi: ref.at[:, pl.ds(lo, hi - lo)]
    rhs = []
    for n in range(2):
        for src, dst in ((dz_src, dz_pair), (cot_src, cot_pair)):
            lo, hi = piece_of(src.shape[1], n)
            hi = hi if n == 0 else src.shape[1]
            rhs.append((cut(src, lo, hi), cut(dst, lo, hi)))
    pairs = pair_copies(place, ((nt_src, nt_pair), (no_src, no_pair)), rhs, pair_send, pair_recv)
    def piece(ref, n):
        lo, hi = piece_of(ref.shape[1], n)
        return ref.at[:, pl.ds(lo, hi - lo)]

    lanes = []
    for n in range(len(PIECES)):
        lanes += [
            Scatter(place, nt_src, nt_pair, piece(dz_src, n), piece(dz_pair, n), "y", "x",
                    bufs[14 * n : 14 * n + 7], send.at[2 * n], recv.at[2 * n]),
            Scatter(place, no_src, no_pair, piece(cot_src, n), piece(cot_pair, n), "x", "y",
                    bufs[14 * n + 7 : 14 * n + 14], send.at[2 * n + 1], recv.at[2 * n + 1]),
        ]
    edges = [
        remote(edge_ref.at[:, :, cols], edge_came.at[:, :, cols], edge_send.at[n], edge_recv.at[n], place.left)
        for n, cols in enumerate((pl.ds(0, channels - GROUP), pl.ds(channels - GROUP, GROUP)))
    ]
    outs = [
        pltpu.make_async_copy(src, dst, out_sem.at[n])
        for n, (src, dst) in enumerate(((nt_pair, nt_out), (dc_ref, dc_out)))
    ]

    def run(first, name, *rest):
        for lane in lanes[2 * first : 2 * first + 2]:
            getattr(lane, name)(*rest)

    def at_step(n, *what):
        pl.when(step == n)(lambda: run(*what))

    @pl.when(step == 0)
    def _():
        place.meet()
        for copy in pairs:
            copy.start()
        for q in range(seqs * chunks):
            rows = slice(q * CHUNK, (q + 1) * CHUNK)
            b_proj, c_proj = bc_ref[rows, :LANES], bc_ref[rows, LANES:]
            cbt_ref[q] = nt_exact(b_proj, c_proj)
            ct_ref[q] = c_proj.T
        dcbt_ref[...] = jnp.zeros_like(dcbt_ref)
        db_acc[...] = jnp.zeros_like(db_acc)
        dc_acc[...] = jnp.zeros_like(dc_acc)
        r1_ref[...] = jnp.zeros_like(r1_ref)
        r2_ref[...] = jnp.zeros_like(r2_ref)
        skip_acc[...] = jnp.zeros_like(skip_acc)
        dtot_ref[...] = jnp.zeros_like(dtot_ref)

    @pl.when(step < groups)
    def _():
        at = lax.rem(step, lag + 1)
        cumg = lane_shift(cum_ref[...], step * heads)
        tot_ring[at] = tot_ref[...]
        for s in range(seqs):
            state = None
            for c in range(chunks - 1, -1, -1):
                q = s * chunks + c
                rows = slice(q * CHUNK, (q + 1) * CHUNK)
                ey = jnp.exp2(spread_all(cumg[rows], heads, head_dim)) * dma_ref[rows]
                loc = dot_pairs(ct_ref[q], ey)
                state = loc if state is None else tot_ref[q : q + 1] * state + loc
            seg_ring[at, s] = state

    handed = step - chain.behind

    @pl.when((handed >= 0) & (handed < groups))
    def _():
        at = lax.rem(handed, lag + 1)
        totals = tot_ring[at, seqs * chunks : seqs * chunks + seqs]
        chain.step(handed, totals[:, None, :], seg_ring[at])

    @pl.when(step == lag)
    def _():
        for copy in pairs[:10]:
            copy.wait_recv()
        outs[0].start()

    @pl.when(step == lag + 4)
    def _():
        for copy in pairs[10:]:
            copy.wait_recv()

    at_step(lag, 0, "send_second", 0)
    at_step(lag + 1, 0, "send_second", 1)
    at_step(lag + 3, 0, "send_first")
    at_step(lag + 4, 1, "send_second", 0)
    at_step(lag + 5, 1, "send_second", 1)
    at_step(lag + 6, 0, "hold")
    at_step(lag + 7, 2, "send_second", 0)
    at_step(lag + 8, 2, "send_second", 1)
    for n, k in enumerate(lanes[0].waves()):
        at_step(lag + 8 + n, 0, "step", k)
    at_step(lag + 10, 1, "send_first")

    def conv_back(s, ext, pre, sig, d_act, at):
        lanes_at = pl.ds(pl.multiple_of(at * GROUP, GROUP), GROUP)
        d_pre = d_act * (sig * (1.0 + pre * (1.0 - sig)))
        zero = jnp.zeros((EDGE, d_pre.shape[1]), F32)
        padded = jnp.concatenate([zero, d_pre, zero], axis=0)
        total = None
        for k in range(taps):
            start = taps - 1 - k
            term = w[k : k + 1] * padded[start : start + seg + EDGE]
            total = term if total is None else total + term
        edge_ref[s, :, lanes_at] = total[:EDGE].astype(BF16)
        dc_ref[s * seg : (s + 1) * seg, lanes_at] = total[EDGE:].astype(BF16)
        tail_ref[s, :, lanes_at] = total[seg:]
        for k in range(taps):
            start = EDGE - (taps - 1) + k
            grad = jnp.sum(ext[start : start + seg] * d_pre, axis=0, keepdims=True)
            gw_ref[k : k + 1] = grad if s == 0 else gw_ref[k : k + 1] + grad
        grad = jnp.sum(d_pre, axis=0, keepdims=True)
        gb_ref[...] = grad if s == 0 else gb_ref[...] + grad

    def by_head(value, pick):
        high = value.astype(BF16)
        return dot(high, pick) + dot((value - high.astype(F32)).astype(BF16), pick)

    @pl.when((step >= lag) & (step < lag + groups))
    def _():
        g = step - lag
        at = lax.rem(g, lag + 1)
        first = g * heads
        cumg = lane_shift(cum_ref[...], first)
        dtg = lane_shift(dt_ref[...], first)
        cumr = head_rows(cumt_ref, first)
        row = lax.broadcasted_iota(jnp.int32, (CHUNK, CHUNK), 0)
        col = lax.broadcasted_iota(jnp.int32, (CHUNK, CHUNK), 1)
        causal = row <= col
        lane = lax.broadcasted_iota(jnp.int32, (GROUP, LANES), 0)
        head = lax.broadcasted_iota(jnp.int32, (GROUP, LANES), 1)
        pick = (head == first + lane // head_dim).astype(BF16)
        skip = skip_ref[...]
        grad_skip = None
        for s in range(seqs):
            ext = pc_ref[s]
            pre = causal_conv(ext, w, b, seg)
            sig = sigmoid(pre)
            acts = pre * sig
            adj = came[g, s].astype(F32)
            d_acts = [None] * chunks
            for c in range(chunks - 1, -1, -1):
                q = s * chunks + c
                rows = slice(q * CHUNK, (q + 1) * CHUNK)
                x = acts[c * CHUNK : (c + 1) * CHUNK]
                dy = dm_ref[rows]
                ce = spread_all(cumg[rows], heads, head_dim)
                de = spread_all(dtg[rows], heads, head_dim)
                weight = jnp.exp2(ce[CHUNK - 1 : CHUNK] - ce)
                u = x * de
                ub = u.astype(BF16)
                dyb = dy.astype(BF16)
                cbt = cbt_ref[q]
                parts = []
                dcbt = dcbt_ref[q]
                for j in range(0, heads, 2):
                    two = slice(j * head_dim, (j + 2) * head_dim)
                    dy_block = block_diagonal(dyb[:, two], head_dim)
                    dm = nt(ub[:, two], dy_block)
                    mats = []
                    for k, h in enumerate((j, j + 1)):
                        here = jnp.broadcast_to(cumg[rows, h : h + 1], (CHUNK, CHUNK))
                        there = cumr[h : h + 1, rows]
                        decay = jnp.exp2(jnp.where(causal, there - here, -jnp.inf))
                        mats.append((decay * cbt).astype(BF16))
                        dcbt = dcbt + decay * dm[:, k * CHUNK : (k + 1) * CHUNK]
                    parts.append(dot(jnp.concatenate(mats, axis=1), dy_block))
                dcbt_ref[q] = dcbt
                start = s0_ref[s] if c == 0 else s1_ref[s]
                end = s2_ref[s] if c == chunks - 1 else s1_ref[s]
                adj_b = adj.astype(BF16)
                bb = bc_ref[rows, :LANES].astype(BF16)
                ey = jnp.exp2(ce) * dy
                du = jnp.concatenate(parts, axis=1) + weight * dot(bb, adj_b)
                uw = u * weight
                across = ((1,), (1,))
                db_acc[rows] += dot_pair(uw, adj_b, across) if c == chunks - 1 else dot_pairs(uw, adj, across)
                dc_acc[rows] += dot_pair(ey, start, across) if c == 0 else dot_pairs(ey, start, across)
                r1_ref[rows] += by_head(dyb.astype(F32) * (mixed_ref[rows] - skip * x), pick)
                r2_ref[rows] += by_head(x * du, pick)
                dtot_ref[q : q + 1] += by_head(
                    jnp.sum(adj * end.astype(F32), axis=0, keepdims=True), pick
                )
                grad = jnp.sum(dy * x, axis=0, keepdims=True)
                grad_skip = grad if grad_skip is None else grad_skip + grad
                d_acts[c] = du * de + skip * dy
                if c > 0:
                    adj = tot_ring[at, q : q + 1] * adj + dot_pairs(ct_ref[q], ey)
            conv_back(s, ext, pre, sig, jnp.concatenate(d_acts, axis=0), g)
        skip_acc[0:1] += by_head(grad_skip, pick)

    @pl.when(step == lag + groups)
    def _():
        pl.when(place.has_left)(edges[0].start)
        row = lax.broadcasted_iota(jnp.int32, (CHUNK, CHUNK), 0)
        col = lax.broadcasted_iota(jnp.int32, (CHUNK, CHUNK), 1)
        later = (row <= col).astype(F32)
        rate = -jnp.exp(dl_ref[...])
        sum_raw = jnp.zeros((1, LANES), F32)
        sum_log = jnp.zeros((1, LANES), F32)
        for s in range(seqs):
            ext = pc_ref[s]
            pre = causal_conv(ext, w, b, seg)
            sig = sigmoid(pre)
            parts = []
            for c in range(chunks):
                q = s * chunks + c
                rows = slice(q * CHUNK, (q + 1) * CHUNK)
                dcbt = dcbt_ref[q]
                d_b = db_acc[rows] + dot_pairs(dcbt, bc_ref[rows, LANES:])
                d_c = dc_acc[rows] + dot_pairs(dcbt.T, bc_ref[rows, :LANES])
                parts.append(jnp.concatenate([d_b, d_c], axis=1))
                dt = dt_ref[rows]
                r2 = r2_ref[rows]
                d_log = jnp.dot(
                    later, r1_ref[rows] - dt * r2, precision=HIGH, preferred_element_type=F32
                )
                d_log = d_log + dtot_ref[q : q + 1]
                raw = raw_ref[s, EDGE + c * CHUNK : EDGE + (c + 1) * CHUNK] + sb_ref[...]
                d_raw = (r2 + rate * d_log) * sigmoid(raw)
                dc_ref[rows, channels:] = d_raw.astype(BF16)
                sum_raw = sum_raw + jnp.sum(d_raw, axis=0, keepdims=True)
                sum_log = sum_log + jnp.sum(d_log * dt, axis=0, keepdims=True) * rate
            conv_back(s, ext, pre, sig, jnp.concatenate(parts, axis=0), groups)
        hsum_ref[0:1] = sum_raw
        hsum_ref[1:2] = sum_log
        hsum_ref[2:3] = skip_acc[0:1]
        pl.when(place.has_left)(edges[1].start)

        @pl.when(place.has_right)
        def _():
            for copy in edges:
                copy.wait_recv()
            for s in range(seqs):
                fixed = tail_ref[s] + edge_came[s].astype(F32)
                dc_ref[(s + 1) * seg - EDGE : (s + 1) * seg, :channels] = fixed.astype(BF16)

        outs[1].start()
        run(1, "hold")
        run(2, "send_first")
        for k in lanes[0].waves():
            run(1, "step", k)
        run(2, "hold")
        for k in lanes[0].waves():
            run(2, "step", k)
        for n, out in enumerate((a_out, b_out)):
            for i in range(len(PIECES)):
                lo, hi = piece_of(out.shape[1], i)
                out[:, lo:hi] = lanes[2 * i + n].keep[place.z]
        for lane in lanes:
            lane.finish()
        chain.finish()

        @pl.when(place.has_left)
        def _():
            for copy in edges:
                copy.wait_send()

        for copy in pairs:
            copy.wait_send()
        for copy in outs:
            copy.wait()


def scan_backward(
    pc, w, b, sb, dl, bc, dt, cum, cumt, dm, mixed, s0, s1, s2, tot, skip, normed_t, dz, turned, cot,
    head_dim, depth,
):
    seqs, rows, cols = pc.shape
    tokens, inner = dm.shape
    groups = inner // GROUP
    lag = depth - 1
    taps, channels = w.shape
    out = lambda i: jnp.maximum(i - lag, 0)
    inside = lambda i: jnp.minimum(out(i), groups - 1)
    wide = pl.BlockSpec((tokens, GROUP), lambda i: (0, inside(i)))
    states = pl.BlockSpec((seqs, LANES, GROUP), lambda i: (0, 0, inside(i)))
    line = lambda n: pl.BlockSpec((n, GROUP), lambda i: (0, inside(i)))
    conv = lambda n: pl.BlockSpec((n, GROUP), lambda i: (0, out(i)))
    ahead = lambda n: pl.BlockSpec((n, GROUP), lambda i: (0, jnp.minimum(i, groups - 1)))
    once = lambda v: pl.BlockSpec(v.shape, lambda i: (0,) * v.ndim, pipeline_mode=pl.Buffered(1))
    anywhere = pl.BlockSpec(memory_space=pl.ANY)
    chunks = tokens // CHUNK
    shape, dma = jax.ShapeDtypeStruct, pltpu.SemaphoreType.DMA
    a_rows, b_rows = normed_t.shape[1] // depth, turned.shape[1] // depth
    a_cols, b_cols = dz.shape[1], cot.shape[1]
    half = lambda v: (4,) + v.shape[1:]
    sends, receives = Scatter.sems(depth)
    buffers = []
    for n in range(len(PIECES)):
        for rows_of, cols_of in ((a_rows, a_cols), (b_rows, b_cols)):
            lo, hi = piece_of(cols_of, n)
            buffers += Scatter.scratch(depth, rows_of, hi - lo)
    ring = lambda *dims: pltpu.VMEM((lag + 1,) + dims, F32)
    link = pltpu.VMEM((groups, seqs, LANES, GROUP), BF16)
    square = pltpu.VMEM((chunks, CHUNK, CHUNK), F32)
    column = pltpu.VMEM((tokens, LANES), F32)
    return pl.pallas_call(
        functools.partial(scan_backward_kernel, depth, head_dim, groups),
        grid=(groups + 1 + lag,),
        in_specs=[
            pl.BlockSpec((seqs, rows, GROUP), lambda i: (0, 0, out(i))),
            conv(taps),
            conv(1),
            pl.BlockSpec((seqs, rows, LANES), lambda i: (0, 0, cols // LANES - 1)),
            whole((1, LANES)), whole((1, LANES)),
            whole(bc.shape), whole(dt.shape), whole(cum.shape), whole(cumt.shape),
            ahead(tokens), wide, wide, states, states, states, ahead(8), line(1),
            once(normed_t), once(dz), once(turned), once(cot),
        ],
        out_specs=[
            anywhere, conv(taps), conv(1), whole((3, LANES)),
            whole((a_rows, a_cols)), whole((b_rows, b_cols)), anywhere,
        ],
        out_shape=[
            shape((tokens, cols), BF16),
            shape((taps, channels), F32),
            shape((1, channels), F32),
            shape((3, LANES), F32),
            shape((a_rows, a_cols), F32),
            shape((b_rows, b_cols), F32),
            shape(half(normed_t), BF16),
        ],
        scratch_shapes=[
            square, pltpu.VMEM((chunks, LANES, CHUNK), F32), square, column, column, column, column,
            pltpu.VMEM((8, LANES), F32),
            pltpu.VMEM((8, LANES), F32),
            pltpu.VMEM((tokens, cols), BF16),
            pltpu.VMEM((seqs, EDGE, channels), F32),
            pltpu.VMEM((seqs, EDGE, channels), BF16),
            pltpu.VMEM((seqs, EDGE, channels), BF16),
            ring(seqs, LANES, GROUP), ring(8, GROUP), link, link,
            pltpu.VMEM(half(normed_t), BF16), pltpu.VMEM(dz.shape, BF16),
            pltpu.VMEM(half(turned), BF16), pltpu.VMEM(cot.shape, BF16),
            dma((groups,)), dma((groups,)), dma((2,)), dma((2,)), dma((12,)), dma((12,)), dma((2,)),
            dma((2 * len(PIECES), sends)), dma((2 * len(PIECES), receives)),
            *buffers,
        ],
        compiler_params=pltpu.CompilerParams(
            dimension_semantics=("arbitrary",), collective_id=1, has_side_effects=True,
            vmem_limit_bytes=VMEM_LIMIT,
        ),
        name="scan_backward_sums",
    )(
        pc, w, b, pc, sb, dl, bc, dt, cum, cumt, dm, dm, mixed, s0, s1, s2, tot, skip,
        normed_t, dz, turned, cot,
    )


def scatter_last_kernel(
    depth, splits, nt_ref, nt_pair, dc_ref, dz_ref, wg_src, wc_src, x_ref, cot_ref, gain_ref,
    ggain_ref, gb_ref, gw_ref, hsum_ref, c_out, gi_ref, small_out, *refs,
):
    place = Place(depth)
    place.meet()
    pieces = len(splits) - 1
    dc_pairs, refs = refs[:pieces], refs[pieces:]
    small_src, tiles_ref, tile_sem, pair_send, pair_recv, send, recv, small_send, small_recv = refs[:9]
    refs = refs[9:]
    cuts = [dc_ref.at[:, pl.ds(lo, hi - lo)] for lo, hi in zip(splits, splits[1:])]
    copies = pair_copies(place, (), tuple(zip(cuts, dc_pairs)), pair_send, pair_recv)
    for copy in copies:
        copy.start()
    lanes = [
        Scatter(place, nt_ref, nt_pair, cut, pair, *(("y", "x") if n % 2 == 0 else ("x", "y")),
                refs[7 * n : 7 * n + 7], send.at[n], recv.at[n])
        for n, (cut, pair) in enumerate(zip(cuts, dc_pairs))
    ]
    small = SmallScatter(place, small_src, *refs[7 * pieces :], small_send, small_recv)
    tile = tiles_ref.shape[2]
    tokens = x_ref.shape[0]

    def d_normed(src, grad_ref, first):
        count = src.shape[1] // tile

        def fetch(i, slot):
            cols = pl.ds(pl.multiple_of(i * tile, LANES), tile)
            return pltpu.make_async_copy(src.at[:, cols], tiles_ref.at[slot], tile_sem.at[slot])

        fetch(0, 0).start()

        def one(i, carry):
            slot = lax.rem(i, 2)
            pl.when(i + 1 < count)(lambda: fetch(i + 1, 1 - slot).start())
            fetch(i, slot).wait()
            cols = pl.ds(pl.multiple_of(i * tile, LANES), tile)
            for r in range(0, tokens, 2 * CHUNK):
                rows = slice(r, r + 2 * CHUNK)
                part = nt(grad_ref[rows, cols], tiles_ref[slot])
                if first:

                    @pl.when(i == 0)
                    def _():
                        gi_ref[rows] = part

                    @pl.when(i > 0)
                    def _():
                        gi_ref[rows] += part
                else:
                    gi_ref[rows] += part
            return carry

        lax.fori_loop(0, count, one, 0)

    def input_grad():
        gain = gain_ref[...]
        size = 64

        def one(i, total):
            rows = pl.ds(pl.multiple_of(i * size, size), size)
            d = gi_ref[rows, :]
            values = x_ref[rows, :].astype(F32)
            scale = lax.rsqrt(jnp.mean(values * values, axis=1, keepdims=True) + EPS)
            hat = values * scale
            weighted = d * gain
            pull = jnp.mean(weighted * hat, axis=1, keepdims=True)
            gi_ref[rows, :] = scale * (weighted - hat * pull) + cot_ref[rows, :].astype(F32)
            return total + jnp.sum(d * hat, axis=0, keepdims=True)

        grad_gain = lax.fori_loop(0, tokens // size, one, jnp.zeros(gain.shape, F32))
        small_src[...] = jnp.zeros_like(small_src)
        taps = gw_ref.shape[0]
        shares = ((0, grad_gain), (1, ggain_ref[...]), (2, gb_ref[...]), (3, gw_ref[...]))
        heads = hsum_ref[:, : LANES // 2]
        for n in range(8 * depth):
            at = (n // depth // 4, n // depth // 2 % 2, n // depth % 2, n % depth)
            for row, value in shares:
                own = value.shape[1] // (8 * depth)
                where = (*at, slice(row, row + value.shape[0]), slice(0, own))
                small_src[where] = value[:, n * own : (n + 1) * own]
            small_src[(*at, slice(0, 1), slice(LANES // 2, LANES))] = heads[0:1]
            small_src[(*at, slice(3 + taps, 4 + taps), slice(0, LANES // 2))] = heads[1:2]
            small_src[(*at, slice(3 + taps, 4 + taps), slice(LANES // 2, LANES))] = heads[2:3]

    def run(first, name, *rest):
        for lane in lanes[first : first + 2]:
            getattr(lane, name)(*rest)

    for copy in copies[:2]:
        copy.wait_recv()
    run(0, "send_second", 0)
    run(0, "send_second", 1)
    for copy in copies[2:]:
        copy.wait_recv()
    run(2, "send_second", 0)
    run(2, "send_second", 1)
    d_normed(wg_src, dz_ref, True)
    run(0, "send_first")
    run(4, "send_second", 0)
    run(4, "send_second", 1)
    d_normed(wc_src, dc_ref, False)
    run(0, "hold")
    run(2, "send_first")
    input_grad()
    small.stage(0)
    run(2, "hold")
    small.stage(1)
    for k in lanes[0].waves():
        run(0, "step", k)
    small.stage(2)
    run(4, "send_first")
    for n, k in enumerate(lanes[0].waves()):
        run(2, "step", k)
    small.stage(3)
    run(4, "hold")
    for k in lanes[0].waves():
        small.sums.step(k)
        run(4, "step", k)
    for lane, lo, hi in zip(lanes, splits, splits[1:]):
        c_out[:, lo:hi] = lane.keep[place.z]
    small_out[...] = small.keep[place.z]
    for lane in lanes:
        lane.finish()
    small.finish()
    for copy in copies:
        copy.wait_send()


def scatter_last(normed_t, nt_pair, dc, dz, wg, wc, x, cot, gain, ggain, gb, gw, hsum, depth):
    shape = jax.ShapeDtypeStruct
    vmem, dma = pl.BlockSpec(memory_space=pltpu.VMEM), pltpu.SemaphoreType.DMA
    anywhere = pl.BlockSpec(memory_space=pl.ANY)
    sends, receives = Scatter.sems(depth)
    rows = normed_t.shape[1] // depth
    tokens, width = dc.shape
    blocks = width // LANES
    parts = [share for share in PIECES for _ in (0, 1)]
    splits = tuple(LANES * (blocks * sum(parts[:n]) // sum(parts)) for n in range(len(parts) + 1))
    small_shape = (8, LANES)
    small_sends, small_receives = SmallScatter.sems(depth)
    sizes = [hi - lo for lo, hi in zip(splits, splits[1:])]
    scratch = []
    for size in sizes:
        scratch += Scatter.scratch(depth, rows, size)
    return pl.pallas_call(
        functools.partial(scatter_last_kernel, depth, splits),
        in_specs=[vmem, vmem, vmem, vmem, anywhere, anywhere] + [vmem] * 7,
        out_specs=[vmem] * 3,
        out_shape=[shape((rows, width), F32), shape((tokens, x.shape[1]), F32), shape(small_shape, F32)],
        scratch_shapes=[
            *(pltpu.VMEM((tokens, size), BF16) for size in sizes),
            pltpu.VMEM((2, 2, 2, depth) + small_shape, F32),
            pltpu.VMEM((2, wg.shape[0], 3 * LANES), BF16),
            dma((2,)), dma((6,)), dma((6,)), dma((6, sends)), dma((6, receives)),
            dma((small_sends,)), dma((small_receives,)),
            *scratch,
            *SmallScatter.scratch(depth, small_shape),
        ],
        compiler_params=pltpu.CompilerParams(
            collective_id=2, has_side_effects=True, vmem_limit_bytes=VMEM_LIMIT
        ),
        name="scatter_last",
    )(normed_t, nt_pair, dc, dz, wg, wc, x, cot, gain, ggain, gb, gw, hsum)


def passed_along(value, axis, steps):
    count = lax.axis_size(axis)
    initial, last = (max(0, -steps), min(count, count - steps))
    return lax.ppermute(value, axis, [(source, source + steps) for source in range(initial, last)])


def prefix(total, local, axis, backward):
    count, here = lax.axis_size(axis), lax.axis_index(axis)
    totals = lax.all_gather(total.astype(BF16), axis)
    locals_ = lax.all_gather(local, axis)
    state = jnp.zeros(local.shape, F32)
    order = range(count - 1, 0, -1) if backward else range(count - 1)
    for lap in order:
        new = totals[lap].astype(F32) * state + locals_[lap].astype(F32)
        reached = lap > here if backward else lap < here
        state = jnp.where(reached, new, state)
    leaves = total * state + local.astype(F32)
    return state.astype(BF16), leaves.astype(BF16)


AXES = ("dp", "ctx")


def body(
    inputs, gain_in, in_weight, conv_weight, conv_bias, step_bias, decay_log, skip_gain, gain_out,
    out_weight, cotangent,
):
    seqs, seg, width = inputs.shape
    tokens = seqs * seg
    count = lax.axis_size(AXES)
    dp, depth = lax.axis_size("dp"), lax.axis_size("ctx")
    own_links = dp == 8 and depth == 4
    inner = out_weight.shape[0] * count
    taps, channels = conv_weight.shape[0], conv_weight.shape[1] * count
    num_heads = step_bias.shape[0]
    head_dim = inner // num_heads
    a, b, c = gain_in.shape[0], gain_out.shape[0], conv_bias.shape[0]

    w_gate = in_weight[:, :inner]
    w_conv = in_weight[:, inner:]
    spare = -w_conv.shape[1] % LANES
    w_conv = jnp.pad(w_conv, ((0, 0), (0, spare)))
    rest = jnp.concatenate([gain_out, conv_bias, conv_weight.reshape(-1)])
    ends = taps - 1
    flat = inputs.reshape(tokens, width)
    cot = cotangent.reshape(tokens, width)

    if own_links:
        group = 2 * depth * a
        at = lax.rem(lax.axis_index("dp"), 2) * depth + lax.axis_index("ctx")
        head = lax.dynamic_update_slice(jnp.zeros((group,), F32), gain_in.astype(F32), (at * a,))
        small = jnp.concatenate([head, rest.astype(F32)])
        small = jnp.pad(small, (0, 8 * LANES - small.size)).reshape(8, LANES)
        pc, normed_ext, normed_t, small, w_conv = gather_project(inputs, small, w_conv, depth)
        w_conv = w_conv.reshape(width, -1)
        small = small.reshape(4, 2 * depth, 8 * LANES)
        g_in = small[:, :, :group].sum(axis=1).reshape(1, width)
        rest = small[:, :, group:].reshape(count, -1)
    else:
        before = passed_along(inputs[:, seg - EDGE :], "ctx", 1)
        ext = jnp.concatenate([before, inputs], axis=1).astype(F32)
        scale_ext = lax.rsqrt(jnp.mean(ext * ext, axis=-1, keepdims=True) + EPS)
        small = lax.all_gather(jnp.concatenate([gain_in, rest]), AXES).astype(F32)
        w_conv = lax.all_gather(w_conv, AXES, axis=0, tiled=True)
        w_gate = lax.all_gather(w_gate, AXES, axis=0, tiled=True)
        w_out = lax.all_gather(out_weight, AXES, axis=0, tiled=True)
        g_in, rest = small[:, :a].reshape(1, width), small[:, a:]
        normed_ext = (ext * scale_ext * g_in).astype(BF16)
        pc = dot(normed_ext.reshape(-1, width), w_conv).reshape(seqs, seg + EDGE, -1)
    g_out = rest[:, :b].reshape(1, inner)
    bias = rest[:, b : b + c].reshape(1, channels)
    kernel = rest[:, b + c : b + c + taps * c].reshape(count, taps, c).transpose(1, 0, 2)
    kernel = kernel.reshape(taps, channels)
    pad_head = lambda v: jnp.pad(v, (0, LANES - num_heads)).reshape(1, LANES)
    sb, dl = pad_head(step_bias), pad_head(decay_log)
    skip = jnp.repeat(skip_gain, head_dim).reshape(1, inner)

    if own_links:
        bc, dt, cum, cumt, mixed, s0, s1, s2, tot, z, dno, w_gate, w_out = scan_forward(
            pc, kernel, bias, sb, dl, skip, normed_ext, cot, in_weight, out_weight, inner, head_dim, depth
        )
        w_gate = w_gate.reshape(width, inner)
        w_out = w_out.reshape(inner, width)
        per_seq = tot[tokens // CHUNK : tokens // CHUNK + seqs][:, None, :]
    else:
        x, bc, dt, cum, cumt, loc0, local, tot = fwd_a(pc, kernel, bias, sb, dl, inner, head_dim)
        per_seq = tot[tokens // CHUNK : tokens // CHUNK + seqs][:, None, :]
        s0, s2 = prefix(per_seq, local, "ctx", False)
        mixed, s1 = fwd_b(x, bc, dt, cum, cumt, s0, loc0, tot, skip, head_dim)
        z = dot(normed_ext[:, EDGE:].reshape(tokens, width), w_gate)
        dno = nt(cot, w_out)

    turned, output, d_mixed, d_gate, grad_gain_out = mid(z, dno, mixed, w_out, g_out, flat, 8)
    if own_links:
        (
            d_conv, grad_kernel, grad_bias, head_sums, grad_gate_weight, grad_out_weight, nt_pair
        ) = scan_backward(
            pc, kernel, bias, sb, dl, bc, dt, cum, cumt, d_mixed, mixed, s0, s1, s2, tot, skip,
            normed_t, d_gate, turned, cot, head_dim, depth,
        )
    else:
        scatter = lambda v: lax.psum_scatter(v.astype(BF16), AXES, scatter_dimension=0, tiled=True).astype(F32)
        normed = normed_ext[:, EDGE:].reshape(tokens, width)
        grad_out_weight = scatter(dot(turned.reshape(inner, tokens), cot))
        grad_gate_weight = scatter(dot(normed, d_gate, ((0,), (0,))))
        adjoint = bwd_a(d_mixed, bc, cum, tot, seqs, head_dim)
        g, _ = prefix(per_seq, adjoint, "ctx", True)
        d_conv, tail, edge, grad_kernel, grad_bias, grad_skip, d_raw, head_sums = bwd_b(
            pc, kernel, bias, sb, dl, bc, dt, cum, cumt, d_mixed, mixed, s0, s1, s2, g, tot, skip, head_dim
        )
        after = passed_along(edge[:, EDGE - ends :].astype(BF16), "ctx", -1).astype(F32)
        tail = tail[:, EDGE - ends :] + after
        d_conv = d_conv.reshape(seqs, seg, channels).at[:, seg - ends :].set(tail.astype(BF16))
        d_conv = jnp.concatenate([d_conv.reshape(tokens, channels), d_raw.astype(BF16)], axis=1)

    real = d_conv.shape[1] - spare
    if own_links:
        grad_conv_cols, grad_input, mine = scatter_last(
            normed_t, nt_pair, d_conv, d_gate, w_gate, w_conv, flat, cot, g_in,
            grad_gain_out, grad_bias, grad_kernel, head_sums, depth,
        )
        grad_conv_cols = grad_conv_cols[:, :real]
        half = LANES // 2
        grad_gain_in, grad_step = mine[0, :a], mine[0, half : half + num_heads]
        grad_gain_out, grad_bias, grad_kernel = mine[1, :b], mine[2, :c], mine[3 : 3 + taps, :c]
        grad_decay = mine[3 + taps, :num_heads]
        grad_skip = mine[3 + taps, half : half + num_heads]
    else:
        d_normed = nt(d_gate, w_gate) + nt(d_conv, w_conv)
        values = flat.astype(F32)
        scale = lax.rsqrt(jnp.mean(values * values, axis=-1, keepdims=True) + EPS)
        hat = values * scale
        weighted = d_normed * g_in
        pull = jnp.mean(weighted * hat, axis=-1, keepdims=True)
        grad_input = scale * (weighted - hat * pull) + cot.astype(F32)
        grad_conv_cols = scatter(dot(normed, d_conv[:, :real], ((0,), (0,))))
        grad_skip = jnp.sum(grad_skip.reshape(num_heads, head_dim), axis=1)
        heads_sum = jnp.concatenate([head_sums[0, :num_heads], head_sums[1, :num_heads], grad_skip])
        by_owner = jnp.concatenate(
            [
                jnp.sum(d_normed * hat, axis=0).reshape(count, a),
                grad_gain_out.reshape(count, b),
                grad_bias.reshape(count, c),
                grad_kernel.reshape(taps, count, c).transpose(1, 0, 2).reshape(count, taps * c),
                jnp.broadcast_to(heads_sum, (count, 3 * num_heads)),
            ],
            axis=1,
        )
        mine = lax.dynamic_index_in_dim(lax.psum(by_owner, AXES), lax.axis_index(AXES), 0, False)
        cuts = [0, a, a + b, a + b + c, a + b + c + taps * c]
        cuts += [cuts[-1] + n * num_heads for n in (1, 2, 3)]
        parts = [mine[lo:hi] for lo, hi in zip(cuts, cuts[1:])]
        grad_gain_in, grad_gain_out, grad_bias, grad_kernel, grad_step, grad_decay, grad_skip = parts
    return (
        output.reshape(seqs, seg, width),
        grad_input.reshape(seqs, seg, width),
        grad_gain_in,
        jnp.concatenate([grad_gate_weight, grad_conv_cols], axis=1),
        grad_kernel.reshape(taps, c),
        grad_bias,
        grad_step,
        grad_decay,
        grad_skip,
        grad_gain_out,
        grad_out_weight,
    )


def solution(mesh):
    rows, cols, both = P("dp", "ctx", None), P(AXES, None), P(AXES)
    return jax.shard_map(
        body,
        mesh=mesh,
        in_specs=(rows, both, cols, P(None, AXES), both, P(), P(), P(), both, cols, rows),
        out_specs=(rows, rows, both, cols, P(None, AXES), both, P(), P(), P(), both, cols),
        check_vma=False,
    )
```

```python
import functools

import jax
import jax.numpy as jnp
from jax import lax
from jax.experimental import pallas as pl
from jax.experimental.pallas import tpu as pltpu
from jax.sharding import PartitionSpec as P

EPS = 1e-05
LOG2E = 1.4426950408889634
HIGH = lax.Precision.HIGHEST
F32 = jnp.float32
BF16 = jnp.bfloat16
CHUNK = 128
GROUP = 256
EDGE = 16
LANES = 128
VMEM_LIMIT = 60 * 1024 * 1024


def dot(a, b, dims=((1,), (0,))):
    return lax.dot_general(a, b, (dims, ((), ())), preferred_element_type=F32)


def nt(a, b):
    return dot(a, b, ((1,), (1,)))


def params():
    return pltpu.CompilerParams(
        dimension_semantics=("arbitrary",), vmem_limit_bytes=VMEM_LIMIT
    )


def whole(shape):
    return pl.BlockSpec(shape, lambda i: (0,) * len(shape))


def sigmoid(v):
    return 1.0 / (1.0 + jnp.exp(-v))


def softplus(v):
    return jnp.maximum(v, 0.0) + jnp.log1p(jnp.exp(-jnp.abs(v)))


def causal_conv(ext, w, b, seg):
    taps = w.shape[0]
    total = b
    for k in range(taps):
        at = EDGE - (taps - 1) + k
        total = total + w[k : k + 1] * ext[at : at + seg]
    return total


def lane_shift(value, lanes):
    return pltpu.roll(value, lax.rem(LANES - lanes, LANES), 1)


def head_rows(ref, first):
    base = pl.multiple_of(first // 8 * 8, 8)
    return pltpu.roll(ref[pl.ds(base, 8), :], lax.rem(8 - lax.rem(first, 8), 8), 0)


def spread(cols, at, head_dim):
    rows = cols.shape[0]
    lane = lax.broadcasted_iota(jnp.int32, (rows, LANES), 1)
    first = jnp.broadcast_to(cols[:, at : at + 1], (rows, LANES))
    second = jnp.broadcast_to(cols[:, at + 1 : at + 2], (rows, LANES))
    return jnp.where(lane < head_dim, first, second)


def spread_all(cols, heads, head_dim):
    return jnp.concatenate([spread(cols, j, head_dim) for j in range(0, heads, 2)], axis=1)


def block_diagonal(pair, head_dim):
    lane = lax.broadcasted_iota(jnp.int32, pair.shape, 1)
    zero = jnp.zeros_like(pair)
    return jnp.concatenate(
        [jnp.where(lane < head_dim, pair, zero), jnp.where(lane < head_dim, zero, pair)], axis=0
    )


MESH = pl.DeviceIdType.MESH


class Place:
    def __init__(self, depth):
        dp, z = lax.axis_index("dp"), lax.axis_index("ctx")
        self.depth, self.z = depth, z
        self.own = {"y": lax.div(dp, 4), "x": lax.rem(lax.div(dp, 2), 2), "c": lax.rem(dp, 2)}
        self.to = {
            name: {"dp": dp + step * (1 - 2 * self.own[name])}
            for name, step in (("y", 4), ("x", 2), ("c", 1))
        }
        self.has_left, self.has_right = z > 0, z < depth - 1
        self.left, self.right = {"ctx": z - 1}, {"ctx": z + 1}

    def flipped(self, *names):
        return {n: 1 - v if n in names else v for n, v in self.own.items()}

    def near(self, k):
        z, last = self.z, self.depth - 1
        reach = jnp.minimum(z, last - z)
        pair = jnp.where(k % 2 == 1, z - (k + 1) // 2, z + k // 2)
        alone = jnp.where(z > last - z, last - k, k)
        return z if k == 0 else jnp.where(k <= 2 * reach, pair, alone)

    def meet(self):
        barrier = pltpu.get_barrier_semaphore()
        signal = functools.partial(pl.semaphore_signal, barrier, inc=1, device_id_type=MESH)
        for name in ("y", "x", "c"):
            signal(device_id=self.to[name])
        pl.when(self.has_left)(lambda: signal(device_id=self.left))
        pl.when(self.has_right)(lambda: signal(device_id=self.right))
        ends = self.has_left.astype(jnp.int32) + self.has_right.astype(jnp.int32)
        pl.semaphore_wait(barrier, 3 + ends)


def remote(src, dst, send, recv, to):
    return pltpu.make_async_remote_copy(
        src_ref=src, dst_ref=dst, send_sem=send, recv_sem=recv, device_id=to, device_id_type=MESH
    )


class Gather:
    def __init__(self, place, src, line, first, second, send, recv, part=()):
        self.place, self.src, self.line_of, self.part = place, src, line, part
        self.first, self.second, self.send, self.recv = first, second, send, recv

    @staticmethod
    def sems(depth):
        return 6 * depth + 3, 5 * depth + 3

    def flips(self, g):
        return ((), (self.first,), (self.second,), (self.first, self.second))[g]

    def slot(self, k, *flips):
        return self.line_of(**self.place.flipped(*flips)).at[(self.place.near(k), *self.part)]

    def copy(self, k, where, to, send, recv):
        src = self.src if k == 0 and where == () else self.slot(k, *where)
        return remote(src, self.slot(k, *where), self.send.at[send], self.recv.at[recv], to)

    def along(self, k, right):
        p = self.place
        return self.copy(k, (), p.right if right else p.left, int(right) * p.depth + k, p.near(k))

    def goes(self, k, right):
        p, at = self.place, self.place.near(k)
        if right:
            return p.has_right if k == 0 else p.has_right & (at < p.z)
        return p.has_left if k == 0 else p.has_left & (at > p.z)

    def to_axis(self, k, stage, there=False):
        p, depth = self.place, self.place.depth
        f, s = self.first, self.second
        where = ((), (), (f,), (f, s))[stage]
        axis = (f, s, s, "c")[stage]
        if there:
            where = where + (axis,)
        return self.copy(k, where, p.to[axis], (2 + stage) * depth + k, (1 + stage) * depth + k)

    def to_core(self, g, there=False):
        depth = self.place.depth
        flips = self.flips(g) + (("c",) if there else ())
        line = self.line_of(**self.place.flipped(*flips)).at[(pl.ds(0, depth), *self.part)]
        return remote(line, line, self.send.at[6 * depth + g], self.recv.at[5 * depth + g], self.place.to["c"])

    def line(self, k):
        if k:
            self.along(k, True).wait_recv()
        for right in (True, False):
            pl.when(self.goes(k, right))(lambda: self.along(k, right).start())
        for stage in (0, 1):
            self.to_axis(k, stage).start()

    def from_first(self, k):
        self.to_axis(k, 0, True).wait_recv()
        self.to_axis(k, 2).start()

    def from_second(self, k):
        self.to_axis(k, 1, True).wait_recv()

    def from_both(self, k):
        self.to_axis(k, 2, True).wait_recv()
        self.to_axis(k, 3).start()

    def core(self, g):
        self.to_core(g).start()

    def whole(self, g):
        if g < 3:
            self.to_core(g, True).wait_recv()
        else:
            for k in range(self.place.depth):
                self.to_axis(k, 3, True).wait_recv()

    def finish(self):
        for k in range(self.place.depth):
            for right in (True, False):
                pl.when(self.goes(k, right))(lambda: self.along(k, right).wait_send())
            for stage in range(4):
                self.to_axis(k, stage).wait_send()
        for g in range(3):
            self.to_core(g).wait_send()


class Line:
    def __init__(self, place, keep, sent, came, send, recv):
        self.place, self.keep, self.sent, self.came = place, keep, sent, came
        self.send, self.recv = send, recv

    def copy(self, k, to, at):
        zk = self.place.near(k)
        return remote(self.sent.at[zk], self.came.at[at], self.send.at[k], self.recv.at[at], to)

    def take(self, at):
        self.copy(1, self.place.left, at).wait_recv()
        zk = jnp.where(at == self.place.depth, self.place.z, at)
        self.keep[zk] = self.keep[zk] + self.came[at].astype(F32)

    def moves(self, k):
        p, zk = self.place, self.place.near(k)
        return (
            (zk < p.z, p.left, zk),
            (zk > p.z, p.right, jnp.where(zk == p.z + 1, p.depth, zk)),
        )

    def step(self, k):
        p, zk = self.place, self.place.near(k)
        if k == 0:
            pl.when(p.has_right)(lambda: self.take(p.z))
            pl.when(p.has_left)(lambda: self.take(p.depth))
            return
        farther = ((zk < p.z) & p.has_right) | ((zk > p.z) & p.has_left)
        pl.when(farther)(lambda: self.take(zk))
        self.sent[zk] = self.keep[zk].astype(self.sent.dtype)
        for goes, to, at in self.moves(k):
            pl.when(goes)(lambda: self.copy(k, to, at).start())

    def finish(self):
        for k in range(1, self.place.depth):
            for goes, to, at in self.moves(k):
                pl.when(goes)(lambda: self.copy(k, to, at).wait_send())


class Scatter:
    def __init__(self, place, lhs, lhs_pair, rhs, rhs_pair, first, second, bufs, send, recv):
        self.place, self.lhs, self.lhs_pair, self.rhs, self.rhs_pair = place, lhs, lhs_pair, rhs, rhs_pair
        self.first, self.second, self.send, self.recv = first, second, send, recv
        self.s_sent, self.s_came, self.f_sent, self.f_came, self.keep, z_sent, z_came = bufs
        depth = place.depth
        self.sums = Line(place, self.keep, z_sent, z_came, send.at[pl.ds(2 + depth, depth)],
                         recv.at[pl.ds(2 + depth, depth + 1)])

    @staticmethod
    def sems(depth):
        return 2 + 2 * depth, 3 + 2 * depth

    @staticmethod
    def scratch(depth, rows, cols):
        block = lambda *lead: pltpu.VMEM(lead + (rows, cols), BF16)
        return [
            block(2, depth), block(2, depth), block(depth), block(depth),
            pltpu.VMEM((depth, rows, cols), F32), block(depth), block(depth + 1),
        ]

    def product(self, flips, store):
        at = self.place.flipped(*flips)
        pair = 2 * at["y"] + at["x"]
        one = 2 * pair + at["c"]
        rows, cols = self.keep.shape[1:]
        tile = 512

        def block(start, size):
            lanes = pl.ds(start, size)
            part = dot(self.lhs[one], self.rhs[:, lanes]) + dot(self.lhs_pair[pair], self.rhs_pair[:, lanes])
            for z in range(self.place.depth):
                store(z, lanes, part[z * rows : (z + 1) * rows])

        def loop(i, carry):
            block(pl.multiple_of(i * tile, tile), tile)
            return carry

        lax.fori_loop(0, cols // tile, loop, 0)
        if cols % tile:
            block(cols // tile * tile, cols % tile)

    def to_second(self, j):
        return remote(self.s_sent.at[j], self.s_came.at[j], self.send.at[j], self.recv.at[j],
                      self.place.to[self.second])

    def to_first(self, k):
        zk, n = self.place.near(k), 2 + k
        return remote(self.f_sent.at[zk], self.f_came.at[zk], self.send.at[n], self.recv.at[n],
                      self.place.to[self.first])

    def waves(self):
        return range(self.place.depth - 1, -1, -1)

    def send_second(self, j):
        def store(z, lanes, part):
            self.s_sent[j, z, :, lanes] = part.astype(BF16)

        self.product((self.second, self.first) if j == 0 else (self.second,), store)
        self.to_second(j).start()

    def send_first(self):
        self.to_second(0).wait_recv()

        def store(z, lanes, part):
            self.f_sent[z, :, lanes] = (part + self.s_came[0, z, :, lanes].astype(F32)).astype(BF16)

        self.product((self.first,), store)
        for k in self.waves():
            self.to_first(k).start()

    def hold(self):
        self.to_second(1).wait_recv()

        def store(z, lanes, part):
            self.keep[z, :, lanes] = part + self.s_came[1, z, :, lanes].astype(F32)

        self.product((), store)

    def step(self, k):
        self.to_first(k).wait_recv()
        zk = self.place.near(k)
        self.keep[zk] = self.keep[zk] + self.f_came[zk].astype(F32)
        self.sums.step(k)

    def finish(self):
        for j in (0, 1):
            self.to_second(j).wait_send()
        for k in self.waves():
            self.to_first(k).wait_send()
        self.sums.finish()


class SmallScatter:
    def __init__(self, place, src, c_came, half, x_came, keep, y_came, z_sent, z_came, send, recv):
        self.place, self.src, self.c_came, self.half = place, src, c_came, half
        self.x_came, self.keep, self.y_came = x_came, keep, y_came
        self.send, self.recv = send, recv
        depth = place.depth
        self.sums = Line(place, keep, z_sent, z_came, send.at[pl.ds(7, depth)],
                         recv.at[pl.ds(7, depth + 1)])

    @staticmethod
    def sems(depth):
        return 7 + depth, 8 + depth

    @staticmethod
    def scratch(depth, shape):
        block = lambda *lead: pltpu.VMEM(lead + shape, F32)
        return [
            block(2, 2, depth), block(2, 2, depth), block(2, depth), block(depth), block(depth),
            block(depth), block(depth + 1),
        ]

    def copy(self, n):
        p, own = self.place, self.place.own
        if n < 4:
            y, x = n // 2, n % 2
            src, dst, to = self.src.at[y, x, 1 - own["c"]], self.c_came.at[y, x], "c"
        elif n < 6:
            src, dst, to = self.half.at[n - 4, 1 - own["x"]], self.x_came.at[n - 4], "x"
        else:
            src, dst, to = self.half.at[1 - own["y"], own["x"]], self.y_came, "y"
        return remote(src, dst, self.send.at[n], self.recv.at[n], p.to[to])

    def stage(self, n):
        own = self.place.own
        if n == 0:
            for i in range(4):
                self.copy(i).start()
        elif n == 1:
            for i in range(4):
                self.copy(i).wait_recv()
            for y in (0, 1):
                for x in (0, 1):
                    self.half[y, x] = self.src[y, x, own["c"]] + self.c_came[y, x]
            for i in (4, 5):
                self.copy(i).start()
        elif n == 2:
            for i in (4, 5):
                self.copy(i).wait_recv()
            for y in (0, 1):
                self.half[y, own["x"]] = self.half[y, own["x"]] + self.x_came[y]
            self.copy(6).start()
        else:
            self.copy(6).wait_recv()
            self.keep[...] = self.half[own["y"], own["x"]] + self.y_came[...]

    def finish(self):
        for n in range(7):
            self.copy(n).wait_send()
        self.sums.finish()


def gather_kernel(
    depth, half, x_ref, small_src, wc_src, pc_ref, normed_ref, normt_ref, small_ref, wc_out,
    hat_ref, edge_ref, wc_ref, edge_sem, own_sem, out_sem, send, recv,
):
    place = Place(depth)
    place.meet()
    seqs, seg, features = x_ref.shape
    width = wc_src.shape[1]
    lo, hi = pl.ds(0, half), pl.ds(half, width - half)
    every = slice(None)
    weights = lambda y, x, c: wc_ref.at[y, x, c]
    lanes = [
        Gather(place, small_src, lambda y, x, c: small_ref.at[y, x, c], "y", "x", send.at[0], recv.at[0]),
        Gather(place, wc_src.at[:, lo], weights, "y", "x", send.at[1], recv.at[1], (every, lo)),
        Gather(place, wc_src.at[:, hi], weights, "x", "y", send.at[2], recv.at[2], (every, hi)),
    ]
    early, late = lanes[:2], lanes[2:]
    own = place.own
    mine = (own["y"], own["x"], own["c"], place.z)
    copies = [
        pltpu.make_async_copy(src, dst.at[mine], own_sem.at[n])
        for n, (src, dst) in enumerate(((small_src, small_ref), (wc_src, wc_ref)))
    ]
    edge = remote(x_ref.at[:, pl.ds(seg - EDGE, EDGE)], edge_ref, edge_sem.at[0], edge_sem.at[1], place.right)

    def each(group, *steps):
        for name, k in steps:
            for lane in group:
                getattr(lane, name)(k)

    def keep(n):
        at = place.flipped(*((), ("y",), ("x",), ("y", "x"))[n])
        return pltpu.make_async_copy(wc_ref.at[at["y"], at["x"]], wc_out.at[at["y"], at["x"]], out_sem.at[n])

    rows = wc_src.shape[0]
    count = 2 * depth * rows

    def norm(flips):
        at = place.flipped(*flips)
        group = 2 * at["y"] + at["x"]
        here = pl.ds(pl.multiple_of(group * count, LANES), count)
        gain = sum(
            small_ref[at["y"], at["x"], c, z, : count // LANES] for c in (0, 1) for z in range(depth)
        )
        gain = jnp.concatenate([gain[i : i + 1] for i in range(count // LANES)], axis=1)
        for s in range(seqs):
            normed = (hat_ref[s, :, here] * gain).astype(BF16)
            normed_ref[s, :, here] = normed
            turned = normed[EDGE:].astype(F32).T.astype(BF16)
            for c in (0, 1):
                normt_ref[2 * group + c, :, s * seg : (s + 1) * seg] = turned[c * depth * rows : (c + 1) * depth * rows]

    def multiply(flips, n):
        at = place.flipped(*flips)
        here = pl.ds(pl.multiple_of((2 * at["y"] + at["x"]) * count, LANES), count)
        first, last = ((0, half), (half, width))[n]
        tile = 4 * LANES
        for start in range(first, last, tile):
            cols = slice(start, min(start + tile, last))
            block = jnp.concatenate(
                [wc_ref[at["y"], at["x"], c, z, :, cols] for c in (0, 1) for z in range(depth)], axis=0
            )
            for s in range(seqs):
                part = dot(normed_ref[s, :, here], block)
                if flips == ():
                    pc_ref[s, :, cols] = part
                else:
                    pc_ref[s, :, cols] += part

    each(early, ("line", 0))
    pl.when(place.has_right)(edge.start)
    for copy in copies:
        copy.start()
    pl.when(place.has_left)(edge.wait_recv)

    @pl.when(jnp.logical_not(place.has_left))
    def _():
        edge_ref[...] = jnp.zeros_like(edge_ref)

    def scale_rows(s, start, rows_in, r, step):
        values = rows_in[s, r : r + step].astype(F32)
        mean = jnp.mean(values * values, axis=1, keepdims=True)
        hat_ref[s, start + r : start + r + step] = values * lax.rsqrt(mean + EPS)

    pieces = []
    for s in range(seqs):
        pieces.append((s, 0, edge_ref, 0, EDGE))
        pieces += [(s, EDGE, x_ref, r, 64) for r in range(0, seg, 64)]
    share = -(-len(pieces) // depth)
    for k in range(depth):
        for piece in pieces[k * share : (k + 1) * share]:
            scale_rows(*piece)
        if k + 1 < depth:
            each(early, ("line", k + 1))
        if k == depth - 2:
            each(late, ("line", 0))
    for copy in copies:
        copy.wait()
    each(early, ("core", 0))
    for k in range(1, depth):
        each(late, ("line", k))
    each(late, ("core", 0))
    for k in range(depth):
        each(early, ("from_first", k), ("from_second", k))
    each(early, ("core", 1), ("core", 2))
    each(late, ("from_first", 0), ("from_first", 1))
    each(early, ("whole", 0))
    norm(())
    multiply((), 0)
    for k in range(2, depth):
        each(late, ("from_first", k))
    each(early, ("whole", 1))
    norm(("y",))
    multiply(("y",), 0)
    for k in range(depth):
        each(late, ("from_second", k))
    each(late, ("core", 1), ("core", 2))
    each(early, ("whole", 2))
    norm(("x",))
    multiply(("x",), 0)
    each(late, ("whole", 0))
    keep(0).start()
    multiply((), 1)
    for k in range(depth - 1):
        each(lanes, ("from_both", k))
    each(late, ("whole", 1), ("whole", 2))
    keep(1).start()
    keep(2).start()
    multiply(("y",), 1)
    multiply(("x",), 1)
    each(lanes, ("from_both", depth - 1))
    each(early, ("whole", 3))
    norm(("y", "x"))
    multiply(("y", "x"), 0)
    each(late, ("whole", 3))
    keep(3).start()
    multiply(("y", "x"), 1)
    for lane in lanes:
        lane.finish()
    for n in range(4):
        keep(n).wait()
    pl.when(place.has_right)(edge.wait_send)


def gather_project(x, small, wc, depth):
    shape = jax.ShapeDtypeStruct
    seqs, seg, features = x.shape
    slots = (2, 2, 2, depth)
    sends, receives = Gather.sems(depth)
    width = wc.shape[1]
    half = width // 2 // LANES * LANES
    anywhere, vmem = pl.BlockSpec(memory_space=pl.ANY), pl.BlockSpec(memory_space=pltpu.VMEM)
    dma = pltpu.SemaphoreType.DMA
    return pl.pallas_call(
        functools.partial(gather_kernel, depth, half),
        in_specs=[vmem, vmem, vmem],
        out_specs=[vmem, vmem, vmem, vmem, anywhere],
        out_shape=[
            shape((seqs, seg + EDGE, width), F32),
            shape((seqs, seg + EDGE, features), BF16),
            shape((8, depth * wc.shape[0], seqs * seg), BF16),
            shape(slots + small.shape, F32),
            shape(slots + wc.shape, BF16),
        ],
        scratch_shapes=[
            pltpu.VMEM((seqs, seg + EDGE, features), F32),
            pltpu.VMEM((seqs, EDGE, features), BF16),
            pltpu.VMEM(slots + wc.shape, BF16),
            dma((2,)), dma((2,)), dma((4,)), dma((3, sends)), dma((3, receives)),
        ],
        compiler_params=pltpu.CompilerParams(
            collective_id=0, has_side_effects=True, vmem_limit_bytes=VMEM_LIMIT
        ),
        name="gather_project",
    )(x, small, wc)


def fwd_a_kernel(
    head_dim, pc_ref, w_ref, b_ref, raw_ref, sb_ref, dl_ref,
    x_ref, bc_ref, dt_ref, cum_ref, cumt_ref, loc0_ref, seg_ref, tot_ref, bt_ref,
):
    step = pl.program_id(0)
    seqs = pc_ref.shape[0]
    seg = pc_ref.shape[1] - EDGE
    chunks = seg // CHUNK
    w, b = w_ref[...], b_ref[...]

    def acts_of(s):
        pre = causal_conv(pc_ref[s], w, b, seg)
        return pre * sigmoid(pre)

    @pl.when(step == 0)
    def _():
        row = lax.broadcasted_iota(jnp.int32, (CHUNK, CHUNK), 0)
        col = lax.broadcasted_iota(jnp.int32, (CHUNK, CHUNK), 1)
        tri = (col <= row).astype(F32)
        rate = -jnp.exp(dl_ref[...])
        for s in range(seqs):
            acts = acts_of(s)
            bc_ref[s * seg : (s + 1) * seg] = acts
            for c in range(chunks):
                q = s * chunks + c
                rows = slice(q * CHUNK, (q + 1) * CHUNK)
                bt_ref[q] = acts[c * CHUNK : (c + 1) * CHUNK, :LANES].T.astype(BF16)
                dt = softplus(raw_ref[s, EDGE + c * CHUNK : EDGE + (c + 1) * CHUNK] + sb_ref[...])
                cum = LOG2E * jnp.dot(tri, dt * rate, precision=HIGH, preferred_element_type=F32)
                dt_ref[rows] = dt
                cum_ref[rows] = cum
                cumt_ref[:, rows] = cum.T

    @pl.when(step > 0)
    def _():
        heads = GROUP // head_dim
        first = (step - 1) * heads
        cumg = lane_shift(cum_ref[...], first)
        dtg = lane_shift(dt_ref[...], first)
        for s in range(seqs):
            x = acts_of(s)
            x_ref[s * seg : (s + 1) * seg] = x
            state, total = None, None
            for c in range(chunks):
                q = s * chunks + c
                rows = slice(q * CHUNK, (q + 1) * CHUNK)
                ce = spread_all(cumg[rows], heads, head_dim)
                de = spread_all(dtg[rows], heads, head_dim)
                end = ce[CHUNK - 1 : CHUNK]
                uw = x[c * CHUNK : (c + 1) * CHUNK] * de * jnp.exp2(end - ce)
                loc = dot(bt_ref[q], uw.astype(BF16))
                tot = jnp.exp2(end)
                tot_ref[q : q + 1] = tot
                if c == 0:
                    loc0_ref[s] = loc
                    state, total = loc, tot
                else:
                    state, total = tot * state + loc, tot * total
            seg_ref[s] = state.astype(BF16)
            tot_ref[seqs * chunks + s : seqs * chunks + s + 1] = total


def fwd_a(pc, w, b, sb, dl, inner, head_dim):
    seqs, rows, cols = pc.shape
    seg = rows - EDGE
    tokens = seqs * seg
    groups = inner // GROUP
    state = LANES
    chunks = tokens // CHUNK
    at = lambda i: (i + groups) % (groups + 1)
    back = lambda i: jnp.maximum(i - 1, 0)
    return pl.pallas_call(
        functools.partial(fwd_a_kernel, head_dim),
        grid=(groups + 1,),
        in_specs=[
            pl.BlockSpec((seqs, rows, GROUP), lambda i: (0, 0, at(i))),
            pl.BlockSpec((w.shape[0], GROUP), lambda i: (0, at(i))),
            pl.BlockSpec((1, GROUP), lambda i: (0, at(i))),
            pl.BlockSpec((seqs, rows, LANES), lambda i: (0, 0, cols // LANES - 1)),
            whole((1, LANES)),
            whole((1, LANES)),
        ],
        out_specs=[
            pl.BlockSpec((tokens, GROUP), lambda i: (0, back(i))),
            whole((tokens, GROUP)),
            whole((tokens, LANES)),
            whole((tokens, LANES)),
            whole((LANES, tokens)),
            pl.BlockSpec((seqs, state, GROUP), lambda i: (0, 0, back(i))),
            pl.BlockSpec((seqs, state, GROUP), lambda i: (0, 0, back(i))),
            pl.BlockSpec((8, GROUP), lambda i: (0, back(i))),
        ],
        out_shape=[
            jax.ShapeDtypeStruct((tokens, inner), F32),
            jax.ShapeDtypeStruct((tokens, GROUP), F32),
            jax.ShapeDtypeStruct((tokens, LANES), F32),
            jax.ShapeDtypeStruct((tokens, LANES), F32),
            jax.ShapeDtypeStruct((LANES, tokens), F32),
            jax.ShapeDtypeStruct((seqs, state, inner), F32),
            jax.ShapeDtypeStruct((seqs, state, inner), BF16),
            jax.ShapeDtypeStruct((8, inner), F32),
        ],
        scratch_shapes=[pltpu.VMEM((chunks, LANES, CHUNK), BF16)],
        compiler_params=params(),
        name="conv_states",
    )(pc, w, b, pc, sb, dl)


def fwd_b_kernel(
    head_dim, x_ref, bc_ref, dt_ref, cum_ref, cumt_ref, s0_ref, loc0_ref, tot_ref, skip_ref,
    mixed_ref, s1_ref, cb_ref,
):
    step = pl.program_id(0)
    seqs = s0_ref.shape[0]
    chunks = x_ref.shape[0] // CHUNK // seqs
    heads = GROUP // head_dim

    @pl.when(step == 0)
    def _():
        for q in range(seqs * chunks):
            rows = slice(q * CHUNK, (q + 1) * CHUNK)
            cb_ref[q] = nt(bc_ref[rows, LANES:].astype(BF16), bc_ref[rows, :LANES].astype(BF16))

    first = step * heads
    cumg = lane_shift(cum_ref[...], first)
    dtg = lane_shift(dt_ref[...], first)
    cumr = head_rows(cumt_ref, first)
    row = lax.broadcasted_iota(jnp.int32, (CHUNK, CHUNK), 0)
    col = lax.broadcasted_iota(jnp.int32, (CHUNK, CHUNK), 1)
    causal = col <= row
    skip = skip_ref[...]
    for s in range(seqs):
        start = s0_ref[s]
        for c in range(chunks):
            q = s * chunks + c
            rows = slice(q * CHUNK, (q + 1) * CHUNK)
            x = x_ref[rows]
            ce = spread_all(cumg[rows], heads, head_dim)
            de = spread_all(dtg[rows], heads, head_dim)
            ub = (x * de).astype(BF16)
            cb = cb_ref[q]
            parts = []
            for j in range(0, heads, 2):
                mats = []
                for h in (j, j + 1):
                    there = jnp.broadcast_to(cumg[rows, h : h + 1], (CHUNK, CHUNK))
                    here = cumr[h : h + 1, rows]
                    decay = jnp.exp2(jnp.where(causal, there - here, -jnp.inf))
                    mats.append((decay * cb).astype(BF16))
                pair = ub[:, j * head_dim : (j + 2) * head_dim]
                parts.append(dot(jnp.concatenate(mats, axis=1), block_diagonal(pair, head_dim)))
            y = jnp.concatenate(parts, axis=1)
            y = y + jnp.exp2(ce) * dot(bc_ref[rows, LANES:].astype(BF16), start)
            mixed_ref[rows] = y + skip * x
            if c == 0:
                start = (tot_ref[q : q + 1] * start.astype(F32) + loc0_ref[s]).astype(BF16)
                s1_ref[s] = start


def fwd_b(x, bc, dt, cum, cumt, s0, loc0, tot, skip, head_dim):
    tokens, inner = x.shape
    seqs, state, _ = s0.shape
    groups = inner // GROUP
    wide = pl.BlockSpec((tokens, GROUP), lambda i: (0, i))
    states = pl.BlockSpec((seqs, state, GROUP), lambda i: (0, 0, i))
    return pl.pallas_call(
        functools.partial(fwd_b_kernel, head_dim),
        grid=(groups,),
        in_specs=[
            wide, whole(bc.shape), whole(dt.shape), whole(cum.shape), whole(cumt.shape),
            states, states,
            pl.BlockSpec((8, GROUP), lambda i: (0, i)),
            pl.BlockSpec((1, GROUP), lambda i: (0, i)),
        ],
        out_specs=[wide, states],
        out_shape=[
            jax.ShapeDtypeStruct((tokens, inner), F32),
            jax.ShapeDtypeStruct((seqs, state, inner), BF16),
        ],
        scratch_shapes=[pltpu.VMEM((tokens // CHUNK, CHUNK, CHUNK), F32)],
        compiler_params=params(),
        name="scan_outputs",
    )(x, bc, dt, cum, cumt, s0, loc0, tot, skip)


def halves(v):
    high = v.astype(BF16)
    return high, (v - high.astype(F32)).astype(BF16)


def dot_pairs(a, b, dims=((1,), (0,))):
    (ah, al), (bh, bl) = halves(a), halves(b)
    return dot(ah, bh, dims) + (dot(al, bh, dims) + dot(ah, bl, dims))


def dot_pair(a, b, dims=((1,), (0,))):
    high, low = halves(a)
    return dot(high, b, dims) + dot(low, b, dims)


def nt_exact(a, b):
    return lax.dot_general(a, b, (((1,), (1,)), ((), ())), precision=HIGH, preferred_element_type=F32)


class Chain:
    def __init__(self, place, came, sent, send, recv, backward):
        self.came, self.sent, self.send, self.recv = came, sent, send, recv
        self.gets, self.gives = place.has_left, place.has_right
        self.to = place.left if backward else place.right
        if backward:
            self.gets, self.gives = self.gives, self.gets
        self.behind = place.depth - 1 - place.z if backward else place.z

    def copy(self, g):
        return remote(self.sent.at[g], self.came.at[g], self.send.at[g], self.recv.at[g], self.to)

    def step(self, g, total, own):
        pl.when(self.gets)(lambda: self.copy(g).wait_recv())

        @pl.when(jnp.logical_not(self.gets))
        def _():
            self.came[g] = jnp.zeros(self.came.shape[1:], self.came.dtype)

        self.sent[g] = (total * self.came[g].astype(F32) + own).astype(BF16)
        pl.when(self.gives)(lambda: self.copy(g).start())

    def finish(self):
        groups = self.came.shape[0]

        def one(g, carry):
            self.copy(g).wait_send()
            return carry

        @pl.when(self.gives)
        def _():
            lax.fori_loop(0, groups, one, 0)


def scan_forward_kernel(
    depth, head_dim, groups,
    pc_ref, w_ref, b_ref, raw_ref, sb_ref, dl_ref, skip_ref, normed_ref, cot_ref, wi_src, wo_src,
    bc_ref, dt_ref, cum_ref, cumt_ref, mixed_ref, s0_ref, s1_ref, s2_ref, tot_ref, z_out, dno_out, wg_out, wo_out,
    bt_ref, cb_ref, x_ring, loc_ring, seg_ring, tot_ring, came, sent,
    z_ref, dno_ref, wg_ref, wo_ref, chain_send, chain_recv, own_sem, keep_sem, out_sem, send, recv,
):
    step = pl.program_id(0)
    lag = depth - 1
    seqs = pc_ref.shape[0]
    seg = pc_ref.shape[1] - EDGE
    chunks = seg // CHUNK
    heads = GROUP // head_dim
    w, b = w_ref[...], b_ref[...]
    place = Place(depth)
    chain = Chain(place, came, sent, chain_send, chain_recv, False)
    wg_src = wi_src.at[:, pl.ds(0, z_ref.shape[1])]
    gate = Gather(place, wg_src, lambda y, x, c: wg_ref.at[y, x, c], "y", "x", send.at[0], recv.at[0])
    out = Gather(place, wo_src, lambda y, x, c: wo_ref.at[y, x, c], "x", "y", send.at[1], recv.at[1])
    mine = (place.own["y"], place.own["x"], place.own["c"], place.z)
    copies = [
        pltpu.make_async_copy(wg_src, wg_ref.at[mine], own_sem.at[0]),
        pltpu.make_async_copy(wo_src, wo_ref.at[mine], own_sem.at[1]),
    ]

    def waves(*steps):
        for lane, name, k in steps:
            getattr(lane, name)(k)

    def acts_of(s):
        pre = causal_conv(pc_ref[s], w, b, seg)
        return pre * sigmoid(pre)

    @pl.when(step == 0)
    def _():
        place.meet()
        waves((gate, "line", 0))
        for copy in copies:
            copy.start()
        row = lax.broadcasted_iota(jnp.int32, (CHUNK, CHUNK), 0)
        col = lax.broadcasted_iota(jnp.int32, (CHUNK, CHUNK), 1)
        tri = (col <= row).astype(F32)
        rate = -jnp.exp(dl_ref[...])
        for s in range(seqs):
            acts = acts_of(s)
            bc_ref[s * seg : (s + 1) * seg] = acts
            for c in range(chunks):
                q = s * chunks + c
                rows = slice(q * CHUNK, (q + 1) * CHUNK)
                b_proj = acts[c * CHUNK : (c + 1) * CHUNK, :LANES]
                c_proj = acts[c * CHUNK : (c + 1) * CHUNK, LANES:]
                bt_ref[q] = b_proj.T
                cb_ref[q] = nt_exact(c_proj, b_proj)
                dt = softplus(raw_ref[s, EDGE + c * CHUNK : EDGE + (c + 1) * CHUNK] + sb_ref[...])
                cum = LOG2E * jnp.dot(tri, dt * rate, precision=HIGH, preferred_element_type=F32)
                dt_ref[rows] = dt
                cum_ref[rows] = cum
                cumt_ref[:, rows] = cum.T

    @pl.when((step > 0) & (step <= groups))
    def _():
        g = step - 1
        at = lax.rem(g, lag + 1)
        first = g * heads
        cumg = lane_shift(cum_ref[...], first)
        dtg = lane_shift(dt_ref[...], first)
        for s in range(seqs):
            x = acts_of(s)
            x_ring[at, s * seg : (s + 1) * seg] = x
            state, total = None, None
            for c in range(chunks):
                q = s * chunks + c
                rows = slice(q * CHUNK, (q + 1) * CHUNK)
                ce = spread_all(cumg[rows], heads, head_dim)
                de = spread_all(dtg[rows], heads, head_dim)
                end = ce[CHUNK - 1 : CHUNK]
                uw = x[c * CHUNK : (c + 1) * CHUNK] * de * jnp.exp2(end - ce)
                loc = dot_pairs(bt_ref[q], uw)
                tot = jnp.exp2(end)
                tot_ring[at, q : q + 1] = tot
                if c == 0:
                    loc_ring[at, s] = loc
                    state, total = loc, tot
                else:
                    state, total = tot * state + loc, tot * total
            seg_ring[at, s] = state
            tot_ring[at, seqs * chunks + s : seqs * chunks + s + 1] = total

    handed = step - 1 - chain.behind

    @pl.when((handed >= 0) & (handed < groups))
    def _():
        at = lax.rem(handed, lag + 1)
        totals = tot_ring[at, seqs * chunks : seqs * chunks + seqs]
        chain.step(handed, totals[:, None, :], seg_ring[at])

    @pl.when(step > lag)
    def _():
        g = step - 1 - lag
        at = lax.rem(g, lag + 1)
        first = g * heads
        cumg = lane_shift(cum_ref[...], first)
        dtg = lane_shift(dt_ref[...], first)
        cumr = head_rows(cumt_ref, first)
        row = lax.broadcasted_iota(jnp.int32, (CHUNK, CHUNK), 0)
        col = lax.broadcasted_iota(jnp.int32, (CHUNK, CHUNK), 1)
        causal = col <= row
        skip = skip_ref[...]
        s0_ref[...] = came[g]
        s2_ref[...] = sent[g]
        tot_ref[...] = tot_ring[at]
        for s in range(seqs):
            start = came[g, s]
            for c in range(chunks):
                q = s * chunks + c
                rows = slice(q * CHUNK, (q + 1) * CHUNK)
                x = x_ring[at, rows]
                ce = spread_all(cumg[rows], heads, head_dim)
                de = spread_all(dtg[rows], heads, head_dim)
                ub = (x * de).astype(BF16)
                cb = cb_ref[q]
                parts = []
                for j in range(0, heads, 2):
                    mats = []
                    for h in (j, j + 1):
                        there = jnp.broadcast_to(cumg[rows, h : h + 1], (CHUNK, CHUNK))
                        here = cumr[h : h + 1, rows]
                        decay = jnp.exp2(jnp.where(causal, there - here, -jnp.inf))
                        mats.append((decay * cb).astype(BF16))
                    pair = ub[:, j * head_dim : (j + 2) * head_dim]
                    parts.append(dot(jnp.concatenate(mats, axis=1), block_diagonal(pair, head_dim)))
                y = jnp.concatenate(parts, axis=1)
                y = y + jnp.exp2(ce) * dot(bc_ref[rows, LANES:].astype(BF16), start)
                mixed_ref[rows] = y + skip * x
                if c == 0:
                    later = tot_ring[at, q : q + 1] * start.astype(F32) + loc_ring[at, s]
                    s1_ref[s] = later
                    start = later.astype(BF16)

    every = range(depth)
    by_group = ((), ("y",), ("x",), ("y", "x"))

    def both(lane, *waves_of):
        return [(lane, name, k) for k in waves_of for name in ("from_first", "from_second")]

    beside = {
        3: [(gate, "line", 1)],
        6: [(gate, "line", 2), (out, "line", 0)],
        9: [(gate, "line", 3)],
        11: [(out, "line", 1)],
    }
    for at, steps in beside.items():
        pl.when(step == at)(lambda: waves(*steps))

    @pl.when(step == 9)
    def _():
        for copy in copies:
            copy.wait()
        waves((gate, "core", 0))

    @pl.when(step == groups + lag)
    def _():
        rows = 2 * depth * wi_src.shape[0]
        tile = 4 * LANES
        size = dno_ref.shape[1] // 8

        def keep(lane, g):
            src, dst = (wg_ref, wg_out) if lane is gate else (wo_ref, wo_out)
            at = place.flipped(*by_group[g])
            return pltpu.make_async_copy(
                src.at[at["y"], at["x"]], dst.at[at["y"], at["x"]], keep_sem.at[int(lane is out), g]
            )

        def ready(lane, g):
            lane.whole(g if g in (0, 3) or lane is gate else 3 - g)
            keep(lane, g).start()

        def group_of(g):
            at = place.flipped(*by_group[g])
            return 2 * at["y"] + at["x"]

        def gate_product(g):
            at = place.flipped(*by_group[g])
            here = pl.ds(pl.multiple_of(group_of(g) * rows, LANES), rows)
            for start in range(0, z_ref.shape[1], tile):
                cols = slice(start, start + tile)
                block = jnp.concatenate(
                    [wg_ref[at["y"], at["x"], c, z, :, cols] for c in (0, 1) for z in every], axis=0
                )
                for s in range(seqs):
                    part = dot(normed_ref[s, EDGE:, here], block)
                    at_rows = slice(s * seg, (s + 1) * seg)
                    if g == 0:
                        z_ref[at_rows, cols] = part
                    else:
                        z_ref[at_rows, cols] += part

        def out_product(g):
            at = place.flipped(*by_group[g])
            for c in (0, 1):
                block = jnp.concatenate([wo_ref[at["y"], at["x"], c, z] for z in every], axis=0)
                cols = pl.ds(pl.multiple_of((2 * group_of(g) + c) * size, LANES), size)
                dno_ref[:, cols] = nt(cot_ref[...], block)
            dno_copy(g).start()

        def dno_copy(g):
            cols = pl.ds(pl.multiple_of(group_of(g) * 2 * size, LANES), 2 * size)
            return pltpu.make_async_copy(dno_ref.at[:, cols], dno_out.at[:, cols], out_sem.at[g])

        last = depth - 1
        waves((out, "line", 2))
        ready(gate, 0)
        gate_product(0)
        waves((out, "line", 3), (out, "core", 0))
        waves(*both(gate, *every), (gate, "core", 1), (gate, "core", 2))
        waves(*((out, "from_first", k) for k in range(last)))
        ready(gate, 1)
        gate_product(1)
        waves((out, "from_first", last), *((out, "from_second", k) for k in every))
        waves((out, "core", 1), (out, "core", 2))
        ready(gate, 2)
        gate_product(2)
        waves((gate, "from_both", 0), (out, "from_both", 0))
        ready(out, 0)
        out_product(0)
        waves((gate, "from_both", 1), (out, "from_both", 1))
        ready(out, 1)
        out_product(1)
        waves((gate, "from_both", 2), (out, "from_both", 2))
        ready(out, 2)
        out_product(2)
        waves((gate, "from_both", last), (out, "from_both", last))
        ready(gate, 3)
        gate_product(3)
        z_copy = pltpu.make_async_copy(z_ref, z_out, out_sem.at[4])
        z_copy.start()
        ready(out, 3)
        out_product(3)
        for lane in (gate, out):
            lane.finish()
        chain.finish()
        for g in range(4):
            dno_copy(g).wait()
            keep(gate, g).wait()
            keep(out, g).wait()
        z_copy.wait()


def scan_forward(pc, w, b, sb, dl, skip, normed, cot, w_in, wo, inner, head_dim, depth):
    seqs, rows, cols = pc.shape
    tokens = seqs * (rows - EDGE)
    groups = inner // GROUP
    lag = depth - 1
    chunks = tokens // CHUNK
    shape, dma = jax.ShapeDtypeStruct, pltpu.SemaphoreType.DMA
    into = lambda i: jnp.where(i == 0, groups, jnp.minimum(i - 1, groups - 1))
    out = lambda i: jnp.maximum(i - 1 - lag, 0)
    states = pl.BlockSpec((seqs, LANES, GROUP), lambda i: (0, 0, out(i)))
    anywhere = pl.BlockSpec(memory_space=pl.ANY)
    sends, receives = Gather.sems(depth)
    slots = (2, 2, 2, depth)
    ring = lambda *dims: pltpu.VMEM((lag + 1,) + dims, F32)
    link = pltpu.VMEM((groups, seqs, LANES, GROUP), BF16)
    once = lambda v: pl.BlockSpec(v.shape, lambda i: (0,) * v.ndim, pipeline_mode=pl.Buffered(1))
    return pl.pallas_call(
        functools.partial(scan_forward_kernel, depth, head_dim, groups),
        grid=(groups + 1 + lag,),
        in_specs=[
            pl.BlockSpec((seqs, rows, GROUP), lambda i: (0, 0, into(i))),
            pl.BlockSpec((w.shape[0], GROUP), lambda i: (0, into(i))),
            pl.BlockSpec((1, GROUP), lambda i: (0, into(i))),
            pl.BlockSpec((seqs, rows, LANES), lambda i: (0, 0, cols // LANES - 1)),
            whole((1, LANES)),
            whole((1, LANES)),
            pl.BlockSpec((1, GROUP), lambda i: (0, out(i))),
            once(normed),
            once(cot),
            once(w_in),
            once(wo),
        ],
        out_specs=[
            whole((tokens, GROUP)),
            whole((tokens, LANES)),
            whole((tokens, LANES)),
            whole((LANES, tokens)),
            pl.BlockSpec((tokens, GROUP), lambda i: (0, out(i))),
            states, states, states,
            pl.BlockSpec((8, GROUP), lambda i: (0, out(i))),
            anywhere,
            anywhere,
            anywhere,
            anywhere,
        ],
        out_shape=[
            shape((tokens, GROUP), F32),
            shape((tokens, LANES), F32),
            shape((tokens, LANES), F32),
            shape((LANES, tokens), F32),
            shape((tokens, inner), F32),
            shape((seqs, LANES, inner), BF16),
            shape((seqs, LANES, inner), F32),
            shape((seqs, LANES, inner), BF16),
            shape((8, inner), F32),
            shape((tokens, inner), F32),
            shape((tokens, inner), F32),
            shape(slots + (w_in.shape[0], inner), BF16),
            shape(slots + wo.shape, BF16),
        ],
        scratch_shapes=[
            pltpu.VMEM((chunks, LANES, CHUNK), F32),
            pltpu.VMEM((chunks, CHUNK, CHUNK), F32),
            ring(tokens, GROUP), ring(seqs, LANES, GROUP), ring(seqs, LANES, GROUP), ring(8, GROUP),
            link, link,
            pltpu.VMEM((tokens, inner), F32), pltpu.VMEM((tokens, inner), F32),
            pltpu.VMEM(slots + (w_in.shape[0], inner), BF16), pltpu.VMEM(slots + wo.shape, BF16),
            dma((groups,)), dma((groups,)), dma((2,)), dma((2, 4)), dma((5,)), dma((2, sends)), dma((2, receives)),
        ],
        compiler_params=pltpu.CompilerParams(
            dimension_semantics=("arbitrary",), collective_id=3, has_side_effects=True,
            vmem_limit_bytes=VMEM_LIMIT,
        ),
        name="scan_forward",
    )(pc, w, b, pc, sb, dl, skip, normed, cot, w_in, wo)


def mid_kernel(
    z_ref, dno_ref, mixed_ref, wo_ref, gain_ref, in_ref, not_ref, out_ref, dm_ref, dz_ref, gg_ref, acc_ref,
):
    step = pl.program_id(0)
    inner = mixed_ref.shape[1]
    tiles, tile = not_ref.shape[0], not_ref.shape[1]

    @pl.when(step == 0)
    def _():
        gg_ref[...] = jnp.zeros_like(gg_ref)

    def lanes_of(i):
        return pl.ds(pl.multiple_of(i * tile, tile), tile)

    def fold(v):
        total = v[:, :LANES]
        for k in range(LANES, tile, LANES):
            total = total + v[:, k : k + LANES]
        return total

    def one(i, sums):
        sq, hg = sums
        at = lanes_of(i)
        z = z_ref[:, at]
        g = mixed_ref[:, at] * z * sigmoid(z)
        return sq + fold(g * g), hg + fold(dno_ref[:, at] * gain_ref[:, at] * g)

    zero = jnp.zeros((mixed_ref.shape[0], LANES), F32)
    sq, hg = lax.fori_loop(0, tiles, one, (zero, zero))
    scale = lax.rsqrt(jnp.sum(sq, axis=1, keepdims=True) / inner + EPS)
    pull = scale * scale * scale * (jnp.sum(hg, axis=1, keepdims=True) / inner)
    acc_ref[...] = in_ref[...].astype(F32)

    def two(i, carry):
        at = lanes_of(i)
        z, mixed, dno, gain = z_ref[:, at], mixed_ref[:, at], dno_ref[:, at], gain_ref[:, at]
        sig = sigmoid(z)
        act = z * sig
        g = mixed * act
        gs = g * scale
        no = gs * gain
        not_ref[i] = no.T.astype(BF16)
        acc_ref[...] += dot(no.astype(BF16), wo_ref[at, :])
        gg_ref[:, at] += jnp.sum(dno * gs, axis=0, keepdims=True)
        dg = scale * (dno * gain) - g * pull
        dm_ref[:, at] = dg * act
        dz_ref[:, at] = (dg * mixed * (sig * (1.0 + z * (1.0 - sig)))).astype(BF16)
        return carry

    lax.fori_loop(0, tiles, two, 0)
    out_ref[...] = acc_ref[...].astype(BF16)


def mid(z, dno, mixed, wo, gain, inputs, tiles):
    tokens, inner = mixed.shape
    width = inputs.shape[1]
    tile = inner // tiles
    narrow = pl.BlockSpec((CHUNK, width), lambda i: (i, 0))
    wide = pl.BlockSpec((CHUNK, inner), lambda i: (i, 0))
    once = lambda v: pl.BlockSpec(v.shape, lambda i: (0,) * v.ndim, pipeline_mode=pl.Buffered(1))
    return pl.pallas_call(
        mid_kernel,
        grid=(tokens // CHUNK,),
        in_specs=[wide, wide, wide, once(wo), whole((1, inner)), narrow],
        out_specs=[
            pl.BlockSpec((tiles, tile, CHUNK), lambda i: (0, 0, i)), narrow, wide, wide,
            whole((1, inner)),
        ],
        out_shape=[
            jax.ShapeDtypeStruct((tiles, tile, tokens), BF16),
            jax.ShapeDtypeStruct((tokens, width), BF16),
            jax.ShapeDtypeStruct((tokens, inner), F32),
            jax.ShapeDtypeStruct((tokens, inner), BF16),
            jax.ShapeDtypeStruct((1, inner), F32),
        ],
        scratch_shapes=[pltpu.VMEM((CHUNK, width), F32)],
        compiler_params=params(),
        name="gate_norm_project",
    )(z, dno, mixed, wo, gain, inputs)


def bwd_a_kernel(head_dim, seqs, dm_ref, bc_ref, cum_ref, tot_ref, seg_ref, ct_ref):
    step = pl.program_id(0)
    chunks = dm_ref.shape[0] // CHUNK // seqs
    heads = GROUP // head_dim

    @pl.when(step == 0)
    def _():
        for q in range(seqs * chunks):
            ct_ref[q] = bc_ref[q * CHUNK : (q + 1) * CHUNK, LANES:].T.astype(BF16)

    cumg = lane_shift(cum_ref[...], step * heads)
    for s in range(seqs):
        state = None
        for c in range(chunks - 1, -1, -1):
            q = s * chunks + c
            rows = slice(q * CHUNK, (q + 1) * CHUNK)
            ey = jnp.exp2(spread_all(cumg[rows], heads, head_dim)) * dm_ref[rows]
            loc = dot(ct_ref[q], ey.astype(BF16))
            state = loc if state is None else tot_ref[q : q + 1] * state + loc
        seg_ref[s] = state.astype(BF16)


def bwd_a(dm, bc, cum, tot, seqs, head_dim):
    tokens, inner = dm.shape
    return pl.pallas_call(
        functools.partial(bwd_a_kernel, head_dim, seqs),
        grid=(inner // GROUP,),
        in_specs=[
            pl.BlockSpec((tokens, GROUP), lambda i: (0, i)), whole(bc.shape), whole(cum.shape),
            pl.BlockSpec((8, GROUP), lambda i: (0, i)),
        ],
        out_specs=pl.BlockSpec((seqs, LANES, GROUP), lambda i: (0, 0, i)),
        out_shape=jax.ShapeDtypeStruct((seqs, LANES, inner), BF16),
        scratch_shapes=[pltpu.VMEM((tokens // CHUNK, LANES, CHUNK), BF16)],
        compiler_params=params(),
        name="adjoint_states",
    )(dm, bc, cum, tot)


def bwd_b_kernel(
    head_dim, groups, pc_ref, w_ref, b_ref, raw_ref, sb_ref, dl_ref, bc_ref, dt_ref, cum_ref, cumt_ref,
    dm_ref, mixed_ref, s0_ref, s1_ref, s2_ref, g_ref, tot_ref, skip_ref,
    dc_ref, tail_ref, edge_ref, gw_ref, gb_ref, gskip_ref, draw_ref, hsum_ref,
    cbt_ref, dcbt_ref, db_acc, dc_acc, r1_ref, r2_ref, dtot_ref,
):
    step = pl.program_id(0)
    seqs = pc_ref.shape[0]
    seg = pc_ref.shape[1] - EDGE
    chunks = seg // CHUNK
    heads = GROUP // head_dim
    w, b = w_ref[...], b_ref[...]
    taps = w.shape[0]

    @pl.when(step == 0)
    def _():
        for q in range(seqs * chunks):
            rows = slice(q * CHUNK, (q + 1) * CHUNK)
            cbt_ref[q] = nt(bc_ref[rows, :LANES].astype(BF16), bc_ref[rows, LANES:].astype(BF16))
        dcbt_ref[...] = jnp.zeros_like(dcbt_ref)
        db_acc[...] = jnp.zeros_like(db_acc)
        dc_acc[...] = jnp.zeros_like(dc_acc)
        r1_ref[...] = jnp.zeros_like(r1_ref)
        r2_ref[...] = jnp.zeros_like(r2_ref)
        dtot_ref[...] = jnp.zeros_like(dtot_ref)

    def conv_back(s, ext, pre, sig, d_act):
        d_pre = d_act * (sig * (1.0 + pre * (1.0 - sig)))
        zero = jnp.zeros((EDGE, d_pre.shape[1]), F32)
        padded = jnp.concatenate([zero, d_pre, zero], axis=0)
        total = None
        for k in range(taps):
            at = taps - 1 - k
            term = w[k : k + 1] * padded[at : at + seg + EDGE]
            total = term if total is None else total + term
        edge_ref[s] = total[:EDGE]
        dc_ref[s * seg : (s + 1) * seg] = total[EDGE:].astype(BF16)
        tail_ref[s] = total[seg:]
        for k in range(taps):
            at = EDGE - (taps - 1) + k
            grad = jnp.sum(ext[at : at + seg] * d_pre, axis=0, keepdims=True)
            gw_ref[k : k + 1] = grad if s == 0 else gw_ref[k : k + 1] + grad
        grad = jnp.sum(d_pre, axis=0, keepdims=True)
        gb_ref[...] = grad if s == 0 else gb_ref[...] + grad

    def by_head(value, pick):
        high = value.astype(BF16)
        return dot(high, pick) + dot((value - high.astype(F32)).astype(BF16), pick)

    @pl.when(step < groups)
    def _():
        first = step * heads
        cumg = lane_shift(cum_ref[...], first)
        dtg = lane_shift(dt_ref[...], first)
        cumr = head_rows(cumt_ref, first)
        row = lax.broadcasted_iota(jnp.int32, (CHUNK, CHUNK), 0)
        col = lax.broadcasted_iota(jnp.int32, (CHUNK, CHUNK), 1)
        causal = row <= col
        lane = lax.broadcasted_iota(jnp.int32, (GROUP, LANES), 0)
        head = lax.broadcasted_iota(jnp.int32, (GROUP, LANES), 1)
        pick = (head == first + lane // head_dim).astype(BF16)
        skip = skip_ref[...]
        grad_skip = None
        for s in range(seqs):
            ext = pc_ref[s]
            pre = causal_conv(ext, w, b, seg)
            sig = sigmoid(pre)
            acts = pre * sig
            adj = g_ref[s].astype(F32)
            d_acts = [None] * chunks
            for c in range(chunks - 1, -1, -1):
                q = s * chunks + c
                rows = slice(q * CHUNK, (q + 1) * CHUNK)
                x = acts[c * CHUNK : (c + 1) * CHUNK]
                dy = dm_ref[rows]
                ce = spread_all(cumg[rows], heads, head_dim)
                de = spread_all(dtg[rows], heads, head_dim)
                weight = jnp.exp2(ce[CHUNK - 1 : CHUNK] - ce)
                u = x * de
                ub = u.astype(BF16)
                dyb = dy.astype(BF16)
                cbt = cbt_ref[q]
                parts = []
                dcbt = dcbt_ref[q]
                for j in range(0, heads, 2):
                    lanes = slice(j * head_dim, (j + 2) * head_dim)
                    dy_block = block_diagonal(dyb[:, lanes], head_dim)
                    dm = nt(ub[:, lanes], dy_block)
                    mats = []
                    for k, h in enumerate((j, j + 1)):
                        here = jnp.broadcast_to(cumg[rows, h : h + 1], (CHUNK, CHUNK))
                        there = cumr[h : h + 1, rows]
                        decay = jnp.exp2(jnp.where(causal, there - here, -jnp.inf))
                        mats.append((decay * cbt).astype(BF16))
                        dcbt = dcbt + decay * dm[:, k * CHUNK : (k + 1) * CHUNK]
                    parts.append(dot(jnp.concatenate(mats, axis=1), dy_block))
                dcbt_ref[q] = dcbt
                start = s0_ref[s] if c == 0 else s1_ref[s]
                end = s2_ref[s] if c == chunks - 1 else s1_ref[s]
                adj_b = adj.astype(BF16)
                bb = bc_ref[rows, :LANES].astype(BF16)
                cb = bc_ref[rows, LANES:].astype(BF16)
                ey = (jnp.exp2(ce) * dy).astype(BF16)
                du = jnp.concatenate(parts, axis=1) + weight * dot(bb, adj_b)
                db_acc[rows] += nt((u * weight).astype(BF16), adj_b)
                dc_acc[rows] += nt(ey, start)
                r1_ref[rows] += by_head(dyb.astype(F32) * (mixed_ref[rows] - skip * x), pick)
                r2_ref[rows] += by_head(x * du, pick)
                dtot_ref[q : q + 1] += by_head(
                    jnp.sum(adj * end.astype(F32), axis=0, keepdims=True), pick
                )
                grad = jnp.sum(dy * x, axis=0, keepdims=True)
                grad_skip = grad if grad_skip is None else grad_skip + grad
                d_acts[c] = du * de + skip * dy
                if c > 0:
                    adj = tot_ref[q : q + 1] * adj + dot(cb, ey, ((0,), (0,)))
            conv_back(s, ext, pre, sig, jnp.concatenate(d_acts, axis=0))
        gskip_ref[...] = grad_skip

    @pl.when(step == groups)
    def _():
        row = lax.broadcasted_iota(jnp.int32, (CHUNK, CHUNK), 0)
        col = lax.broadcasted_iota(jnp.int32, (CHUNK, CHUNK), 1)
        later = (row <= col).astype(F32)
        rate = -jnp.exp(dl_ref[...])
        sum_raw = jnp.zeros((1, LANES), F32)
        sum_log = jnp.zeros((1, LANES), F32)
        for s in range(seqs):
            ext = pc_ref[s]
            pre = causal_conv(ext, w, b, seg)
            sig = sigmoid(pre)
            parts = []
            for c in range(chunks):
                q = s * chunks + c
                rows = slice(q * CHUNK, (q + 1) * CHUNK)
                dcbt = dcbt_ref[q]
                bb = bc_ref[rows, :LANES].astype(BF16)
                cb = bc_ref[rows, LANES:].astype(BF16)
                d_b = db_acc[rows] + dot(dcbt.astype(BF16), cb)
                d_c = dc_acc[rows] + dot(dcbt.T.astype(BF16), bb)
                parts.append(jnp.concatenate([d_b, d_c], axis=1))
                dt = dt_ref[rows]
                r2 = r2_ref[rows]
                d_log = jnp.dot(
                    later, r1_ref[rows] - dt * r2, precision=HIGH, preferred_element_type=F32
                )
                d_log = d_log + dtot_ref[q : q + 1]
                raw = raw_ref[s, EDGE + c * CHUNK : EDGE + (c + 1) * CHUNK] + sb_ref[...]
                d_raw = (r2 + rate * d_log) * sigmoid(raw)
                draw_ref[rows] = d_raw
                sum_raw = sum_raw + jnp.sum(d_raw, axis=0, keepdims=True)
                sum_log = sum_log + jnp.sum(d_log * dt, axis=0, keepdims=True) * rate
            conv_back(s, ext, pre, sig, jnp.concatenate(parts, axis=0))
        hsum_ref[0:1] = sum_raw
        hsum_ref[1:2] = sum_log


def bwd_b(pc, w, b, sb, dl, bc, dt, cum, cumt, dm, mixed, s0, s1, s2, g, tot, skip, head_dim):
    seqs, rows, cols = pc.shape
    tokens, inner = dm.shape
    groups = inner // GROUP
    taps, channels = w.shape
    wide = pl.BlockSpec((tokens, GROUP), lambda i: (0, jnp.minimum(i, groups - 1)))
    states = pl.BlockSpec((seqs, LANES, GROUP), lambda i: (0, 0, jnp.minimum(i, groups - 1)))
    line = lambda n: pl.BlockSpec((n, GROUP), lambda i: (0, jnp.minimum(i, groups - 1)))
    conv = lambda n: pl.BlockSpec((n, GROUP), lambda i: (0, i))
    ends = pl.BlockSpec((seqs, EDGE, GROUP), lambda i: (0, 0, i))
    chunks = tokens // CHUNK
    shape = jax.ShapeDtypeStruct
    return pl.pallas_call(
        functools.partial(bwd_b_kernel, head_dim, groups),
        grid=(groups + 1,),
        in_specs=[
            pl.BlockSpec((seqs, rows, GROUP), lambda i: (0, 0, i)),
            conv(taps),
            conv(1),
            pl.BlockSpec((seqs, rows, LANES), lambda i: (0, 0, cols // LANES - 1)),
            whole((1, LANES)), whole((1, LANES)),
            whole(bc.shape), whole(dt.shape), whole(cum.shape), whole(cumt.shape),
            wide, wide, states, states, states, states, line(8), line(1),
        ],
        out_specs=[
            conv(tokens), ends, ends, conv(taps), conv(1), line(1),
            whole((tokens, LANES)), whole((2, LANES)),
        ],
        out_shape=[
            shape((tokens, channels), BF16),
            shape((seqs, EDGE, channels), F32),
            shape((seqs, EDGE, channels), F32),
            shape((taps, channels), F32),
            shape((1, channels), F32),
            shape((1, inner), F32),
            shape((tokens, LANES), F32),
            shape((2, LANES), F32),
        ],
        scratch_shapes=[
            pltpu.VMEM((chunks, CHUNK, CHUNK), F32),
            pltpu.VMEM((chunks, CHUNK, CHUNK), F32),
            pltpu.VMEM((tokens, LANES), F32),
            pltpu.VMEM((tokens, LANES), F32),
            pltpu.VMEM((tokens, LANES), F32),
            pltpu.VMEM((tokens, LANES), F32),
            pltpu.VMEM((8, LANES), F32),
        ],
        compiler_params=params(),
        name="scan_backward",
    )(pc, w, b, pc, sb, dl, bc, dt, cum, cumt, dm, mixed, s0, s1, s2, g, tot, skip)


PIECES = (3, 2, 1)


def piece_of(columns, n):
    unit = columns // sum(PIECES)
    return sum(PIECES[:n]) * unit, sum(PIECES[: n + 1]) * unit


def pair_copies(place, lhs, rhs, send, recv):
    other = 1 - place.own["c"]
    parts = [(src.at[2 * g + other], dst.at[g]) for src, dst in lhs for g in range(4)] + list(rhs)
    return [
        remote(src, dst, send.at[n], recv.at[n], place.to["c"]) for n, (src, dst) in enumerate(parts)
    ]


def scan_backward_kernel(
    depth, head_dim, groups,
    pc_ref, w_ref, b_ref, raw_ref, sb_ref, dl_ref, bc_ref, dt_ref, cum_ref, cumt_ref,
    dma_ref, dm_ref, mixed_ref, s0_ref, s1_ref, s2_ref, tot_ref, skip_ref,
    nt_src, dz_src, no_src, cot_src,
    dc_out, gw_ref, gb_ref, hsum_ref, a_out, b_out, nt_out,
    cbt_ref, ct_ref, dcbt_ref, db_acc, dc_acc, r1_ref, r2_ref, dtot_ref, skip_acc,
    dc_ref, tail_ref, edge_ref, edge_came, seg_ring, tot_ring, came, sent,
    nt_pair, dz_pair, no_pair, cot_pair,
    chain_send, chain_recv, edge_send, edge_recv, pair_send, pair_recv, out_sem, send, recv, *bufs,
):
    step = pl.program_id(0)
    lag = depth - 1
    seqs = pc_ref.shape[0]
    seg = pc_ref.shape[1] - EDGE
    chunks = seg // CHUNK
    heads = GROUP // head_dim
    w, b = w_ref[...], b_ref[...]
    taps = w.shape[0]
    channels = tail_ref.shape[2]
    place = Place(depth)
    chain = Chain(place, came, sent, chain_send, chain_recv, True)
    cut = lambda ref, lo, hi: ref.at[:, pl.ds(lo, hi - lo)]
    rhs = []
    for n in range(2):
        for src, dst in ((dz_src, dz_pair), (cot_src, cot_pair)):
            lo, hi = piece_of(src.shape[1], n)
            hi = hi if n == 0 else src.shape[1]
            rhs.append((cut(src, lo, hi), cut(dst, lo, hi)))
    pairs = pair_copies(place, ((nt_src, nt_pair), (no_src, no_pair)), rhs, pair_send, pair_recv)
    def piece(ref, n):
        lo, hi = piece_of(ref.shape[1], n)
        return ref.at[:, pl.ds(lo, hi - lo)]

    lanes = []
    for n in range(len(PIECES)):
        lanes += [
            Scatter(place, nt_src, nt_pair, piece(dz_src, n), piece(dz_pair, n), "y", "x",
                    bufs[14 * n : 14 * n + 7], send.at[2 * n], recv.at[2 * n]),
            Scatter(place, no_src, no_pair, piece(cot_src, n), piece(cot_pair, n), "x", "y",
                    bufs[14 * n + 7 : 14 * n + 14], send.at[2 * n + 1], recv.at[2 * n + 1]),
        ]
    edges = [
        remote(edge_ref.at[:, :, cols], edge_came.at[:, :, cols], edge_send.at[n], edge_recv.at[n], place.left)
        for n, cols in enumerate((pl.ds(0, channels - GROUP), pl.ds(channels - GROUP, GROUP)))
    ]
    outs = [
        pltpu.make_async_copy(src, dst, out_sem.at[n])
        for n, (src, dst) in enumerate(((nt_pair, nt_out), (dc_ref, dc_out)))
    ]

    def run(first, name, *rest):
        for lane in lanes[2 * first : 2 * first + 2]:
            getattr(lane, name)(*rest)

    def at_step(n, *what):
        pl.when(step == n)(lambda: run(*what))

    @pl.when(step == 0)
    def _():
        place.meet()
        for copy in pairs:
            copy.start()
        for q in range(seqs * chunks):
            rows = slice(q * CHUNK, (q + 1) * CHUNK)
            b_proj, c_proj = bc_ref[rows, :LANES], bc_ref[rows, LANES:]
            cbt_ref[q] = nt_exact(b_proj, c_proj)
            ct_ref[q] = c_proj.T
        dcbt_ref[...] = jnp.zeros_like(dcbt_ref)
        db_acc[...] = jnp.zeros_like(db_acc)
        dc_acc[...] = jnp.zeros_like(dc_acc)
        r1_ref[...] = jnp.zeros_like(r1_ref)
        r2_ref[...] = jnp.zeros_like(r2_ref)
        skip_acc[...] = jnp.zeros_like(skip_acc)
        dtot_ref[...] = jnp.zeros_like(dtot_ref)

    @pl.when(step < groups)
    def _():
        at = lax.rem(step, lag + 1)
        cumg = lane_shift(cum_ref[...], step * heads)
        tot_ring[at] = tot_ref[...]
        for s in range(seqs):
            state = None
            for c in range(chunks - 1, -1, -1):
                q = s * chunks + c
                rows = slice(q * CHUNK, (q + 1) * CHUNK)
                ey = jnp.exp2(spread_all(cumg[rows], heads, head_dim)) * dma_ref[rows]
                loc = dot_pairs(ct_ref[q], ey)
                state = loc if state is None else tot_ref[q : q + 1] * state + loc
            seg_ring[at, s] = state

    handed = step - chain.behind

    @pl.when((handed >= 0) & (handed < groups))
    def _():
        at = lax.rem(handed, lag + 1)
        totals = tot_ring[at, seqs * chunks : seqs * chunks + seqs]
        chain.step(handed, totals[:, None, :], seg_ring[at])

    @pl.when(step == lag)
    def _():
        for copy in pairs[:10]:
            copy.wait_recv()
        outs[0].start()

    @pl.when(step == lag + 4)
    def _():
        for copy in pairs[10:]:
            copy.wait_recv()

    at_step(lag, 0, "send_second", 0)
    at_step(lag + 1, 0, "send_second", 1)
    at_step(lag + 3, 0, "send_first")
    at_step(lag + 4, 1, "send_second", 0)
    at_step(lag + 4, 1, "send_second", 1)
    at_step(lag + 5, 0, "hold")
    at_step(lag + 6, 2, "send_second", 0)
    at_step(lag + 6, 2, "send_second", 1)
    for n, k in enumerate(lanes[0].waves()):
        at_step(lag + 7 + n, 0, "step", k)
    at_step(lag + 8, 1, "send_first")
    at_step(lag + 9, 1, "hold")
    at_step(lag + 10, 2, "send_first")
    at_step(lag + 11, 1, "step", depth - 1)
    at_step(lag + 12, 1, "step", depth - 2)
    at_step(lag + 12, 2, "hold")

    def conv_back(s, ext, pre, sig, d_act, at):
        lanes_at = pl.ds(pl.multiple_of(at * GROUP, GROUP), GROUP)
        d_pre = d_act * (sig * (1.0 + pre * (1.0 - sig)))
        zero = jnp.zeros((EDGE, d_pre.shape[1]), F32)
        padded = jnp.concatenate([zero, d_pre, zero], axis=0)
        total = None
        for k in range(taps):
            start = taps - 1 - k
            term = w[k : k + 1] * padded[start : start + seg + EDGE]
            total = term if total is None else total + term
        edge_ref[s, :, lanes_at] = total[:EDGE].astype(BF16)
        dc_ref[s * seg : (s + 1) * seg, lanes_at] = total[EDGE:].astype(BF16)
        tail_ref[s, :, lanes_at] = total[seg:]
        for k in range(taps):
            start = EDGE - (taps - 1) + k
            grad = jnp.sum(ext[start : start + seg] * d_pre, axis=0, keepdims=True)
            gw_ref[k : k + 1] = grad if s == 0 else gw_ref[k : k + 1] + grad
        grad = jnp.sum(d_pre, axis=0, keepdims=True)
        gb_ref[...] = grad if s == 0 else gb_ref[...] + grad

    def by_head(value, pick):
        high = value.astype(BF16)
        return dot(high, pick) + dot((value - high.astype(F32)).astype(BF16), pick)

    @pl.when((step >= lag) & (step < lag + groups))
    def _():
        g = step - lag
        at = lax.rem(g, lag + 1)
        first = g * heads
        cumg = lane_shift(cum_ref[...], first)
        dtg = lane_shift(dt_ref[...], first)
        cumr = head_rows(cumt_ref, first)
        row = lax.broadcasted_iota(jnp.int32, (CHUNK, CHUNK), 0)
        col = lax.broadcasted_iota(jnp.int32, (CHUNK, CHUNK), 1)
        causal = row <= col
        lane = lax.broadcasted_iota(jnp.int32, (GROUP, LANES), 0)
        head = lax.broadcasted_iota(jnp.int32, (GROUP, LANES), 1)
        pick = (head == first + lane // head_dim).astype(BF16)
        skip = skip_ref[...]
        grad_skip = None
        for s in range(seqs):
            ext = pc_ref[s]
            pre = causal_conv(ext, w, b, seg)
            sig = sigmoid(pre)
            acts = pre * sig
            adj = came[g, s].astype(F32)
            d_acts = [None] * chunks
            for c in range(chunks - 1, -1, -1):
                q = s * chunks + c
                rows = slice(q * CHUNK, (q + 1) * CHUNK)
                x = acts[c * CHUNK : (c + 1) * CHUNK]
                dy = dm_ref[rows]
                ce = spread_all(cumg[rows], heads, head_dim)
                de = spread_all(dtg[rows], heads, head_dim)
                weight = jnp.exp2(ce[CHUNK - 1 : CHUNK] - ce)
                u = x * de
                ub = u.astype(BF16)
                dyb = dy.astype(BF16)
                cbt = cbt_ref[q]
                parts = []
                dcbt = dcbt_ref[q]
                for j in range(0, heads, 2):
                    two = slice(j * head_dim, (j + 2) * head_dim)
                    dy_block = block_diagonal(dyb[:, two], head_dim)
                    dm = nt(ub[:, two], dy_block)
                    mats = []
                    for k, h in enumerate((j, j + 1)):
                        here = jnp.broadcast_to(cumg[rows, h : h + 1], (CHUNK, CHUNK))
                        there = cumr[h : h + 1, rows]
                        decay = jnp.exp2(jnp.where(causal, there - here, -jnp.inf))
                        mats.append((decay * cbt).astype(BF16))
                        dcbt = dcbt + decay * dm[:, k * CHUNK : (k + 1) * CHUNK]
                    parts.append(dot(jnp.concatenate(mats, axis=1), dy_block))
                dcbt_ref[q] = dcbt
                start = s0_ref[s] if c == 0 else s1_ref[s]
                end = s2_ref[s] if c == chunks - 1 else s1_ref[s]
                adj_b = adj.astype(BF16)
                bb = bc_ref[rows, :LANES].astype(BF16)
                ey = jnp.exp2(ce) * dy
                du = jnp.concatenate(parts, axis=1) + weight * dot(bb, adj_b)
                uw = u * weight
                across = ((1,), (1,))
                db_acc[rows] += dot_pair(uw, adj_b, across) if c == chunks - 1 else dot_pairs(uw, adj, across)
                dc_acc[rows] += dot_pair(ey, start, across) if c == 0 else dot_pairs(ey, start, across)
                r1_ref[rows] += by_head(dyb.astype(F32) * (mixed_ref[rows] - skip * x), pick)
                r2_ref[rows] += by_head(x * du, pick)
                dtot_ref[q : q + 1] += by_head(
                    jnp.sum(adj * end.astype(F32), axis=0, keepdims=True), pick
                )
                grad = jnp.sum(dy * x, axis=0, keepdims=True)
                grad_skip = grad if grad_skip is None else grad_skip + grad
                d_acts[c] = du * de + skip * dy
                if c > 0:
                    adj = tot_ring[at, q : q + 1] * adj + dot_pairs(ct_ref[q], ey)
            conv_back(s, ext, pre, sig, jnp.concatenate(d_acts, axis=0), g)
        skip_acc[0:1] += by_head(grad_skip, pick)

    @pl.when(step == lag + groups)
    def _():
        pl.when(place.has_left)(edges[0].start)
        row = lax.broadcasted_iota(jnp.int32, (CHUNK, CHUNK), 0)
        col = lax.broadcasted_iota(jnp.int32, (CHUNK, CHUNK), 1)
        later = (row <= col).astype(F32)
        rate = -jnp.exp(dl_ref[...])
        sum_raw = jnp.zeros((1, LANES), F32)
        sum_log = jnp.zeros((1, LANES), F32)
        for s in range(seqs):
            ext = pc_ref[s]
            pre = causal_conv(ext, w, b, seg)
            sig = sigmoid(pre)
            parts = []
            for c in range(chunks):
                q = s * chunks + c
                rows = slice(q * CHUNK, (q + 1) * CHUNK)
                dcbt = dcbt_ref[q]
                d_b = db_acc[rows] + dot_pairs(dcbt, bc_ref[rows, LANES:])
                d_c = dc_acc[rows] + dot_pairs(dcbt.T, bc_ref[rows, :LANES])
                parts.append(jnp.concatenate([d_b, d_c], axis=1))
                dt = dt_ref[rows]
                r2 = r2_ref[rows]
                d_log = jnp.dot(
                    later, r1_ref[rows] - dt * r2, precision=HIGH, preferred_element_type=F32
                )
                d_log = d_log + dtot_ref[q : q + 1]
                raw = raw_ref[s, EDGE + c * CHUNK : EDGE + (c + 1) * CHUNK] + sb_ref[...]
                d_raw = (r2 + rate * d_log) * sigmoid(raw)
                dc_ref[rows, channels:] = d_raw.astype(BF16)
                sum_raw = sum_raw + jnp.sum(d_raw, axis=0, keepdims=True)
                sum_log = sum_log + jnp.sum(d_log * dt, axis=0, keepdims=True) * rate
            conv_back(s, ext, pre, sig, jnp.concatenate(parts, axis=0), groups)
        hsum_ref[0:1] = sum_raw
        hsum_ref[1:2] = sum_log
        hsum_ref[2:3] = skip_acc[0:1]
        pl.when(place.has_left)(edges[1].start)

        @pl.when(place.has_right)
        def _():
            for copy in edges:
                copy.wait_recv()
            for s in range(seqs):
                fixed = tail_ref[s] + edge_came[s].astype(F32)
                dc_ref[(s + 1) * seg - EDGE : (s + 1) * seg, :channels] = fixed.astype(BF16)

        outs[1].start()
        run(2, "step", depth - 1)
        for k in range(depth - 3, -1, -1):
            run(1, "step", k)
            run(2, "step", k + 1)
        run(2, "step", 0)
        for n, out in enumerate((a_out, b_out)):
            for i in range(len(PIECES)):
                lo, hi = piece_of(out.shape[1], i)
                out[:, lo:hi] = lanes[2 * i + n].keep[place.z]
        for lane in lanes:
            lane.finish()
        chain.finish()

        @pl.when(place.has_left)
        def _():
            for copy in edges:
                copy.wait_send()

        for copy in pairs:
            copy.wait_send()
        for copy in outs:
            copy.wait()


def scan_backward(
    pc, w, b, sb, dl, bc, dt, cum, cumt, dm, mixed, s0, s1, s2, tot, skip, normed_t, dz, turned, cot,
    head_dim, depth,
):
    seqs, rows, cols = pc.shape
    tokens, inner = dm.shape
    groups = inner // GROUP
    lag = depth - 1
    taps, channels = w.shape
    out = lambda i: jnp.maximum(i - lag, 0)
    inside = lambda i: jnp.minimum(out(i), groups - 1)
    wide = pl.BlockSpec((tokens, GROUP), lambda i: (0, inside(i)))
    states = pl.BlockSpec((seqs, LANES, GROUP), lambda i: (0, 0, inside(i)))
    line = lambda n: pl.BlockSpec((n, GROUP), lambda i: (0, inside(i)))
    conv = lambda n: pl.BlockSpec((n, GROUP), lambda i: (0, out(i)))
    ahead = lambda n: pl.BlockSpec((n, GROUP), lambda i: (0, jnp.minimum(i, groups - 1)))
    once = lambda v: pl.BlockSpec(v.shape, lambda i: (0,) * v.ndim, pipeline_mode=pl.Buffered(1))
    anywhere = pl.BlockSpec(memory_space=pl.ANY)
    chunks = tokens // CHUNK
    shape, dma = jax.ShapeDtypeStruct, pltpu.SemaphoreType.DMA
    a_rows, b_rows = normed_t.shape[1] // depth, turned.shape[1] // depth
    a_cols, b_cols = dz.shape[1], cot.shape[1]
    half = lambda v: (4,) + v.shape[1:]
    sends, receives = Scatter.sems(depth)
    buffers = []
    for n in range(len(PIECES)):
        for rows_of, cols_of in ((a_rows, a_cols), (b_rows, b_cols)):
            lo, hi = piece_of(cols_of, n)
            buffers += Scatter.scratch(depth, rows_of, hi - lo)
    ring = lambda *dims: pltpu.VMEM((lag + 1,) + dims, F32)
    link = pltpu.VMEM((groups, seqs, LANES, GROUP), BF16)
    square = pltpu.VMEM((chunks, CHUNK, CHUNK), F32)
    column = pltpu.VMEM((tokens, LANES), F32)
    return pl.pallas_call(
        functools.partial(scan_backward_kernel, depth, head_dim, groups),
        grid=(groups + 1 + lag,),
        in_specs=[
            pl.BlockSpec((seqs, rows, GROUP), lambda i: (0, 0, out(i))),
            conv(taps),
            conv(1),
            pl.BlockSpec((seqs, rows, LANES), lambda i: (0, 0, cols // LANES - 1)),
            whole((1, LANES)), whole((1, LANES)),
            whole(bc.shape), whole(dt.shape), whole(cum.shape), whole(cumt.shape),
            ahead(tokens), wide, wide, states, states, states, ahead(8), line(1),
            once(normed_t), once(dz), once(turned), once(cot),
        ],
        out_specs=[
            anywhere, conv(taps), conv(1), whole((3, LANES)),
            whole((a_rows, a_cols)), whole((b_rows, b_cols)), anywhere,
        ],
        out_shape=[
            shape((tokens, cols), BF16),
            shape((taps, channels), F32),
            shape((1, channels), F32),
            shape((3, LANES), F32),
            shape((a_rows, a_cols), F32),
            shape((b_rows, b_cols), F32),
            shape(half(normed_t), BF16),
        ],
        scratch_shapes=[
            square, pltpu.VMEM((chunks, LANES, CHUNK), F32), square, column, column, column, column,
            pltpu.VMEM((8, LANES), F32),
            pltpu.VMEM((8, LANES), F32),
            pltpu.VMEM((tokens, cols), BF16),
            pltpu.VMEM((seqs, EDGE, channels), F32),
            pltpu.VMEM((seqs, EDGE, channels), BF16),
            pltpu.VMEM((seqs, EDGE, channels), BF16),
            ring(seqs, LANES, GROUP), ring(8, GROUP), link, link,
            pltpu.VMEM(half(normed_t), BF16), pltpu.VMEM(dz.shape, BF16),
            pltpu.VMEM(half(turned), BF16), pltpu.VMEM(cot.shape, BF16),
            dma((groups,)), dma((groups,)), dma((2,)), dma((2,)), dma((12,)), dma((12,)), dma((2,)),
            dma((2 * len(PIECES), sends)), dma((2 * len(PIECES), receives)),
            *buffers,
        ],
        compiler_params=pltpu.CompilerParams(
            dimension_semantics=("arbitrary",), collective_id=1, has_side_effects=True,
            vmem_limit_bytes=VMEM_LIMIT,
        ),
        name="scan_backward_sums",
    )(
        pc, w, b, pc, sb, dl, bc, dt, cum, cumt, dm, dm, mixed, s0, s1, s2, tot, skip,
        normed_t, dz, turned, cot,
    )


def scatter_last_kernel(
    depth, splits, nt_ref, nt_pair, dc_ref, dz_ref, wg_src, wc_src, x_ref, cot_ref, gain_ref,
    ggain_ref, gb_ref, gw_ref, hsum_ref, c_out, gi_ref, small_out, *refs,
):
    place = Place(depth)
    place.meet()
    pieces = len(splits) - 1
    dc_pairs, refs = refs[:pieces], refs[pieces:]
    small_src, tiles_ref, tile_sem, pair_send, pair_recv, send, recv, small_send, small_recv = refs[:9]
    refs = refs[9:]
    cuts = [dc_ref.at[:, pl.ds(lo, hi - lo)] for lo, hi in zip(splits, splits[1:])]
    copies = pair_copies(place, (), tuple(zip(cuts, dc_pairs)), pair_send, pair_recv)
    for copy in copies:
        copy.start()
    lanes = [
        Scatter(place, nt_ref, nt_pair, cut, pair, *(("y", "x") if n % 2 == 0 else ("x", "y")),
                refs[7 * n : 7 * n + 7], send.at[n], recv.at[n])
        for n, (cut, pair) in enumerate(zip(cuts, dc_pairs))
    ]
    small = SmallScatter(place, small_src, *refs[7 * pieces :], small_send, small_recv)
    tile = tiles_ref.shape[2]
    tokens = x_ref.shape[0]

    def d_normed(src, grad_ref, first, start=0, count=None):
        count = src.shape[1] // tile if count is None else count

        def fetch(i, slot):
            cols = pl.ds(pl.multiple_of(i * tile, LANES), tile)
            return pltpu.make_async_copy(src.at[:, cols], tiles_ref.at[slot], tile_sem.at[slot])

        fetch(start, start % 2).start()

        def one(i, carry):
            slot = lax.rem(i, 2)
            pl.when(i + 1 < count)(lambda: fetch(i + 1, 1 - slot).start())
            fetch(i, slot).wait()
            cols = pl.ds(pl.multiple_of(i * tile, LANES), tile)
            for r in range(0, tokens, 2 * CHUNK):
                rows = slice(r, r + 2 * CHUNK)
                part = nt(grad_ref[rows, cols], tiles_ref[slot])
                if first:

                    @pl.when(i == 0)
                    def _():
                        gi_ref[rows] = part

                    @pl.when(i > 0)
                    def _():
                        gi_ref[rows] += part
                else:
                    gi_ref[rows] += part
            return carry

        lax.fori_loop(start, count, one, 0)

    def input_grad():
        gain = gain_ref[...]
        size = 64

        def one(i, total):
            rows = pl.ds(pl.multiple_of(i * size, size), size)
            d = gi_ref[rows, :]
            values = x_ref[rows, :].astype(F32)
            scale = lax.rsqrt(jnp.mean(values * values, axis=1, keepdims=True) + EPS)
            hat = values * scale
            weighted = d * gain
            pull = jnp.mean(weighted * hat, axis=1, keepdims=True)
            gi_ref[rows, :] = scale * (weighted - hat * pull) + cot_ref[rows, :].astype(F32)
            return total + jnp.sum(d * hat, axis=0, keepdims=True)

        grad_gain = lax.fori_loop(0, tokens // size, one, jnp.zeros(gain.shape, F32))
        small_src[...] = jnp.zeros_like(small_src)
        taps = gw_ref.shape[0]
        shares = ((0, grad_gain), (1, ggain_ref[...]), (2, gb_ref[...]), (3, gw_ref[...]))
        heads = hsum_ref[:, : LANES // 2]
        for n in range(8 * depth):
            at = (n // depth // 4, n // depth // 2 % 2, n // depth % 2, n % depth)
            for row, value in shares:
                own = value.shape[1] // (8 * depth)
                where = (*at, slice(row, row + value.shape[0]), slice(0, own))
                small_src[where] = value[:, n * own : (n + 1) * own]
            small_src[(*at, slice(0, 1), slice(LANES // 2, LANES))] = heads[0:1]
            small_src[(*at, slice(3 + taps, 4 + taps), slice(0, LANES // 2))] = heads[1:2]
            small_src[(*at, slice(3 + taps, 4 + taps), slice(LANES // 2, LANES))] = heads[2:3]

    def run(first, name, *rest):
        for lane in lanes[first : first + 2]:
            getattr(lane, name)(*rest)

    for copy in copies[:2]:
        copy.wait_recv()
    run(0, "send_second", 0)
    run(0, "send_second", 1)
    for copy in copies[2:]:
        copy.wait_recv()
    run(2, "send_second", 0)
    run(2, "send_second", 1)
    d_normed(wg_src, dz_ref, True)
    run(0, "send_first")
    run(4, "send_second", 0)
    run(4, "send_second", 1)
    middle = wc_src.shape[1] // tile // 2
    d_normed(wc_src, dc_ref, False, 0, middle)
    run(0, "hold")
    run(2, "send_first")
    d_normed(wc_src, dc_ref, False, middle)
    run(2, "hold")
    run(0, "step", depth - 1)
    run(4, "send_first")
    input_grad()
    small.stage(0)
    run(0, "step", depth - 2)
    run(2, "step", depth - 1)
    run(4, "hold")
    small.stage(1)
    rounds = [[] for _ in range(depth + 3)]
    for n in range(depth):
        for first, start in ((0, -2), (2, -1), (4, 0)):
            if start + n >= 0:
                rounds[start + n].append((first, depth - 1 - n))
    for n, items in enumerate(rounds):
        for first, k in items:
            run(first, "step", k)
        if n < 2:
            small.stage(2 + n)
        elif n - 2 < depth:
            small.sums.step(depth - 1 - (n - 2))
    for lane, lo, hi in zip(lanes, splits, splits[1:]):
        c_out[:, lo:hi] = lane.keep[place.z]
    small_out[...] = small.keep[place.z]
    for lane in lanes:
        lane.finish()
    small.finish()
    for copy in copies:
        copy.wait_send()


def scatter_last(normed_t, nt_pair, dc, dz, wg, wc, x, cot, gain, ggain, gb, gw, hsum, depth):
    shape = jax.ShapeDtypeStruct
    vmem, dma = pl.BlockSpec(memory_space=pltpu.VMEM), pltpu.SemaphoreType.DMA
    anywhere = pl.BlockSpec(memory_space=pl.ANY)
    sends, receives = Scatter.sems(depth)
    rows = normed_t.shape[1] // depth
    tokens, width = dc.shape
    blocks = width // LANES
    parts = [share for share in PIECES for _ in (0, 1)]
    splits = tuple(LANES * (blocks * sum(parts[:n]) // sum(parts)) for n in range(len(parts) + 1))
    small_shape = (8, LANES)
    small_sends, small_receives = SmallScatter.sems(depth)
    sizes = [hi - lo for lo, hi in zip(splits, splits[1:])]
    scratch = []
    for size in sizes:
        scratch += Scatter.scratch(depth, rows, size)
    return pl.pallas_call(
        functools.partial(scatter_last_kernel, depth, splits),
        in_specs=[vmem, vmem, vmem, vmem, anywhere, anywhere] + [vmem] * 7,
        out_specs=[vmem] * 3,
        out_shape=[shape((rows, width), F32), shape((tokens, x.shape[1]), F32), shape(small_shape, F32)],
        scratch_shapes=[
            *(pltpu.VMEM((tokens, size), BF16) for size in sizes),
            pltpu.VMEM((2, 2, 2, depth) + small_shape, F32),
            pltpu.VMEM((2, wg.shape[0], 3 * LANES), BF16),
            dma((2,)), dma((6,)), dma((6,)), dma((6, sends)), dma((6, receives)),
            dma((small_sends,)), dma((small_receives,)),
            *scratch,
            *SmallScatter.scratch(depth, small_shape),
        ],
        compiler_params=pltpu.CompilerParams(
            collective_id=2, has_side_effects=True, vmem_limit_bytes=VMEM_LIMIT
        ),
        name="scatter_last",
    )(normed_t, nt_pair, dc, dz, wg, wc, x, cot, gain, ggain, gb, gw, hsum)


def passed_along(value, axis, steps):
    count = lax.axis_size(axis)
    initial, last = (max(0, -steps), min(count, count - steps))
    return lax.ppermute(value, axis, [(source, source + steps) for source in range(initial, last)])


def prefix(total, local, axis, backward):
    count, here = lax.axis_size(axis), lax.axis_index(axis)
    totals = lax.all_gather(total.astype(BF16), axis)
    locals_ = lax.all_gather(local, axis)
    state = jnp.zeros(local.shape, F32)
    order = range(count - 1, 0, -1) if backward else range(count - 1)
    for lap in order:
        new = totals[lap].astype(F32) * state + locals_[lap].astype(F32)
        reached = lap > here if backward else lap < here
        state = jnp.where(reached, new, state)
    leaves = total * state + local.astype(F32)
    return state.astype(BF16), leaves.astype(BF16)


AXES = ("dp", "ctx")


def body(
    inputs, gain_in, in_weight, conv_weight, conv_bias, step_bias, decay_log, skip_gain, gain_out,
    out_weight, cotangent,
):
    seqs, seg, width = inputs.shape
    tokens = seqs * seg
    count = lax.axis_size(AXES)
    dp, depth = lax.axis_size("dp"), lax.axis_size("ctx")
    own_links = dp == 8 and depth == 4
    inner = out_weight.shape[0] * count
    taps, channels = conv_weight.shape[0], conv_weight.shape[1] * count
    num_heads = step_bias.shape[0]
    head_dim = inner // num_heads
    a, b, c = gain_in.shape[0], gain_out.shape[0], conv_bias.shape[0]

    w_gate = in_weight[:, :inner]
    w_conv = in_weight[:, inner:]
    spare = -w_conv.shape[1] % LANES
    w_conv = jnp.pad(w_conv, ((0, 0), (0, spare)))
    rest = jnp.concatenate([gain_out, conv_bias, conv_weight.reshape(-1)])
    ends = taps - 1
    flat = inputs.reshape(tokens, width)
    cot = cotangent.reshape(tokens, width)

    if own_links:
        group = 2 * depth * a
        at = lax.rem(lax.axis_index("dp"), 2) * depth + lax.axis_index("ctx")
        head = lax.dynamic_update_slice(jnp.zeros((group,), F32), gain_in.astype(F32), (at * a,))
        small = jnp.concatenate([head, rest.astype(F32)])
        small = jnp.pad(small, (0, 8 * LANES - small.size)).reshape(8, LANES)
        pc, normed_ext, normed_t, small, w_conv = gather_project(inputs, small, w_conv, depth)
        w_conv = w_conv.reshape(width, -1)
        small = small.reshape(4, 2 * depth, 8 * LANES)
        g_in = small[:, :, :group].sum(axis=1).reshape(1, width)
        rest = small[:, :, group:].reshape(count, -1)
    else:
        before = passed_along(inputs[:, seg - EDGE :], "ctx", 1)
        ext = jnp.concatenate([before, inputs], axis=1).astype(F32)
        scale_ext = lax.rsqrt(jnp.mean(ext * ext, axis=-1, keepdims=True) + EPS)
        small = lax.all_gather(jnp.concatenate([gain_in, rest]), AXES).astype(F32)
        w_conv = lax.all_gather(w_conv, AXES, axis=0, tiled=True)
        w_gate = lax.all_gather(w_gate, AXES, axis=0, tiled=True)
        w_out = lax.all_gather(out_weight, AXES, axis=0, tiled=True)
        g_in, rest = small[:, :a].reshape(1, width), small[:, a:]
        normed_ext = (ext * scale_ext * g_in).astype(BF16)
        pc = dot(normed_ext.reshape(-1, width), w_conv).reshape(seqs, seg + EDGE, -1)
    g_out = rest[:, :b].reshape(1, inner)
    bias = rest[:, b : b + c].reshape(1, channels)
    kernel = rest[:, b + c : b + c + taps * c].reshape(count, taps, c).transpose(1, 0, 2)
    kernel = kernel.reshape(taps, channels)
    pad_head = lambda v: jnp.pad(v, (0, LANES - num_heads)).reshape(1, LANES)
    sb, dl = pad_head(step_bias), pad_head(decay_log)
    skip = jnp.repeat(skip_gain, head_dim).reshape(1, inner)

    if own_links:
        bc, dt, cum, cumt, mixed, s0, s1, s2, tot, z, dno, w_gate, w_out = scan_forward(
            pc, kernel, bias, sb, dl, skip, normed_ext, cot, in_weight, out_weight, inner, head_dim, depth
        )
        w_gate = w_gate.reshape(width, inner)
        w_out = w_out.reshape(inner, width)
        per_seq = tot[tokens // CHUNK : tokens // CHUNK + seqs][:, None, :]
    else:
        x, bc, dt, cum, cumt, loc0, local, tot = fwd_a(pc, kernel, bias, sb, dl, inner, head_dim)
        per_seq = tot[tokens // CHUNK : tokens // CHUNK + seqs][:, None, :]
        s0, s2 = prefix(per_seq, local, "ctx", False)
        mixed, s1 = fwd_b(x, bc, dt, cum, cumt, s0, loc0, tot, skip, head_dim)
        z = dot(normed_ext[:, EDGE:].reshape(tokens, width), w_gate)
        dno = nt(cot, w_out)

    turned, output, d_mixed, d_gate, grad_gain_out = mid(z, dno, mixed, w_out, g_out, flat, 8)
    if own_links:
        (
            d_conv, grad_kernel, grad_bias, head_sums, grad_gate_weight, grad_out_weight, nt_pair
        ) = scan_backward(
            pc, kernel, bias, sb, dl, bc, dt, cum, cumt, d_mixed, mixed, s0, s1, s2, tot, skip,
            normed_t, d_gate, turned, cot, head_dim, depth,
        )
    else:
        scatter = lambda v: lax.psum_scatter(v.astype(BF16), AXES, scatter_dimension=0, tiled=True).astype(F32)
        normed = normed_ext[:, EDGE:].reshape(tokens, width)
        grad_out_weight = scatter(dot(turned.reshape(inner, tokens), cot))
        grad_gate_weight = scatter(dot(normed, d_gate, ((0,), (0,))))
        adjoint = bwd_a(d_mixed, bc, cum, tot, seqs, head_dim)
        g, _ = prefix(per_seq, adjoint, "ctx", True)
        d_conv, tail, edge, grad_kernel, grad_bias, grad_skip, d_raw, head_sums = bwd_b(
            pc, kernel, bias, sb, dl, bc, dt, cum, cumt, d_mixed, mixed, s0, s1, s2, g, tot, skip, head_dim
        )
        after = passed_along(edge[:, EDGE - ends :].astype(BF16), "ctx", -1).astype(F32)
        tail = tail[:, EDGE - ends :] + after
        d_conv = d_conv.reshape(seqs, seg, channels).at[:, seg - ends :].set(tail.astype(BF16))
        d_conv = jnp.concatenate([d_conv.reshape(tokens, channels), d_raw.astype(BF16)], axis=1)

    real = d_conv.shape[1] - spare
    if own_links:
        grad_conv_cols, grad_input, mine = scatter_last(
            normed_t, nt_pair, d_conv, d_gate, w_gate, w_conv, flat, cot, g_in,
            grad_gain_out, grad_bias, grad_kernel, head_sums, depth,
        )
        grad_conv_cols = grad_conv_cols[:, :real]
        half = LANES // 2
        grad_gain_in, grad_step = mine[0, :a], mine[0, half : half + num_heads]
        grad_gain_out, grad_bias, grad_kernel = mine[1, :b], mine[2, :c], mine[3 : 3 + taps, :c]
        grad_decay = mine[3 + taps, :num_heads]
        grad_skip = mine[3 + taps, half : half + num_heads]
    else:
        d_normed = nt(d_gate, w_gate) + nt(d_conv, w_conv)
        values = flat.astype(F32)
        scale = lax.rsqrt(jnp.mean(values * values, axis=-1, keepdims=True) + EPS)
        hat = values * scale
        weighted = d_normed * g_in
        pull = jnp.mean(weighted * hat, axis=-1, keepdims=True)
        grad_input = scale * (weighted - hat * pull) + cot.astype(F32)
        grad_conv_cols = scatter(dot(normed, d_conv[:, :real], ((0,), (0,))))
        grad_skip = jnp.sum(grad_skip.reshape(num_heads, head_dim), axis=1)
        heads_sum = jnp.concatenate([head_sums[0, :num_heads], head_sums[1, :num_heads], grad_skip])
        by_owner = jnp.concatenate(
            [
                jnp.sum(d_normed * hat, axis=0).reshape(count, a),
                grad_gain_out.reshape(count, b),
                grad_bias.reshape(count, c),
                grad_kernel.reshape(taps, count, c).transpose(1, 0, 2).reshape(count, taps * c),
                jnp.broadcast_to(heads_sum, (count, 3 * num_heads)),
            ],
            axis=1,
        )
        mine = lax.dynamic_index_in_dim(lax.psum(by_owner, AXES), lax.axis_index(AXES), 0, False)
        cuts = [0, a, a + b, a + b + c, a + b + c + taps * c]
        cuts += [cuts[-1] + n * num_heads for n in (1, 2, 3)]
        parts = [mine[lo:hi] for lo, hi in zip(cuts, cuts[1:])]
        grad_gain_in, grad_gain_out, grad_bias, grad_kernel, grad_step, grad_decay, grad_skip = parts
    return (
        output.reshape(seqs, seg, width),
        grad_input.reshape(seqs, seg, width),
        grad_gain_in,
        jnp.concatenate([grad_gate_weight, grad_conv_cols], axis=1),
        grad_kernel.reshape(taps, c),
        grad_bias,
        grad_step,
        grad_decay,
        grad_skip,
        grad_gain_out,
        grad_out_weight,
    )


def solution(mesh):
    rows, cols, both = P("dp", "ctx", None), P(AXES, None), P(AXES)
    return jax.shard_map(
        body,
        mesh=mesh,
        in_specs=(rows, both, cols, P(None, AXES), both, P(), P(), P(), both, cols, rows),
        out_specs=(rows, rows, both, cols, P(None, AXES), both, P(), P(), P(), both, cols),
        check_vma=False,
    )
```

```python
import functools

import jax
import jax.numpy as jnp
from jax import lax
from jax.experimental import pallas as pl
from jax.experimental.pallas import tpu as pltpu
from jax.sharding import PartitionSpec as P

EPS = 1e-05
LOG2E = 1.4426950408889634
HIGH = lax.Precision.HIGHEST
F32 = jnp.float32
BF16 = jnp.bfloat16
CHUNK = 128
GROUP = 256
EDGE = 16
LANES = 128
VMEM_LIMIT = 62 * 1024 * 1024


def dot(a, b, dims=((1,), (0,))):
    return lax.dot_general(a, b, (dims, ((), ())), preferred_element_type=F32)


def nt(a, b):
    return dot(a, b, ((1,), (1,)))


def params():
    return pltpu.CompilerParams(
        dimension_semantics=("arbitrary",), vmem_limit_bytes=VMEM_LIMIT
    )


def whole(shape):
    return pl.BlockSpec(shape, lambda i: (0,) * len(shape))


def sigmoid(v):
    return 1.0 / (1.0 + jnp.exp(-v))


def softplus(v):
    return jnp.maximum(v, 0.0) + jnp.log1p(jnp.exp(-jnp.abs(v)))


def causal_conv(ext, w, b, seg):
    taps = w.shape[0]
    total = b
    for k in range(taps):
        at = EDGE - (taps - 1) + k
        total = total + w[k : k + 1] * ext[at : at + seg]
    return total


def lane_shift(value, lanes):
    return pltpu.roll(value, lax.rem(LANES - lanes, LANES), 1)


def head_rows(ref, first):
    base = pl.multiple_of(first // 8 * 8, 8)
    return pltpu.roll(ref[pl.ds(base, 8), :], lax.rem(8 - lax.rem(first, 8), 8), 0)


def spread(cols, at, head_dim):
    rows = cols.shape[0]
    lane = lax.broadcasted_iota(jnp.int32, (rows, LANES), 1)
    first = jnp.broadcast_to(cols[:, at : at + 1], (rows, LANES))
    second = jnp.broadcast_to(cols[:, at + 1 : at + 2], (rows, LANES))
    return jnp.where(lane < head_dim, first, second)


def spread_all(cols, heads, head_dim):
    return jnp.concatenate([spread(cols, j, head_dim) for j in range(0, heads, 2)], axis=1)


def block_diagonal(pair, head_dim):
    lane = lax.broadcasted_iota(jnp.int32, pair.shape, 1)
    zero = jnp.zeros_like(pair)
    return jnp.concatenate(
        [jnp.where(lane < head_dim, pair, zero), jnp.where(lane < head_dim, zero, pair)], axis=0
    )


MESH = pl.DeviceIdType.MESH


class Place:
    def __init__(self, depth):
        dp, z = lax.axis_index("dp"), lax.axis_index("ctx")
        self.depth, self.z = depth, z
        self.own = {"y": lax.div(dp, 4), "x": lax.rem(lax.div(dp, 2), 2), "c": lax.rem(dp, 2)}
        self.to = {
            name: {"dp": dp + step * (1 - 2 * self.own[name])}
            for name, step in (("y", 4), ("x", 2), ("c", 1))
        }
        self.has_left, self.has_right = z > 0, z < depth - 1
        self.left, self.right = {"ctx": z - 1}, {"ctx": z + 1}

    def flipped(self, *names):
        return {n: 1 - v if n in names else v for n, v in self.own.items()}

    def near(self, k):
        z, last = self.z, self.depth - 1
        reach = jnp.minimum(z, last - z)
        pair = jnp.where(k % 2 == 1, z - (k + 1) // 2, z + k // 2)
        alone = jnp.where(z > last - z, last - k, k)
        return z if k == 0 else jnp.where(k <= 2 * reach, pair, alone)

    def meet(self):
        barrier = pltpu.get_barrier_semaphore()
        signal = functools.partial(pl.semaphore_signal, barrier, inc=1, device_id_type=MESH)
        for name in ("y", "x", "c"):
            signal(device_id=self.to[name])
        pl.when(self.has_left)(lambda: signal(device_id=self.left))
        pl.when(self.has_right)(lambda: signal(device_id=self.right))
        ends = self.has_left.astype(jnp.int32) + self.has_right.astype(jnp.int32)
        pl.semaphore_wait(barrier, 3 + ends)


def remote(src, dst, send, recv, to):
    return pltpu.make_async_remote_copy(
        src_ref=src, dst_ref=dst, send_sem=send, recv_sem=recv, device_id=to, device_id_type=MESH
    )


class Gather:
    def __init__(self, place, src, line, first, second, send, recv, part=()):
        self.place, self.src, self.line_of, self.part = place, src, line, part
        self.first, self.second, self.send, self.recv = first, second, send, recv

    @staticmethod
    def sems(depth):
        return 6 * depth + 3, 5 * depth + 3

    def flips(self, g):
        return ((), (self.first,), (self.second,), (self.first, self.second))[g]

    def slot(self, k, *flips):
        return self.line_of(**self.place.flipped(*flips)).at[(self.place.near(k), *self.part)]

    def copy(self, k, where, to, send, recv):
        src = self.src if k == 0 and where == () else self.slot(k, *where)
        return remote(src, self.slot(k, *where), self.send.at[send], self.recv.at[recv], to)

    def along(self, k, right):
        p = self.place
        return self.copy(k, (), p.right if right else p.left, int(right) * p.depth + k, p.near(k))

    def goes(self, k, right):
        p, at = self.place, self.place.near(k)
        if right:
            return p.has_right if k == 0 else p.has_right & (at < p.z)
        return p.has_left if k == 0 else p.has_left & (at > p.z)

    def to_axis(self, k, stage, there=False):
        p, depth = self.place, self.place.depth
        f, s = self.first, self.second
        where = ((), (), (f,), (f, s))[stage]
        axis = (f, s, s, "c")[stage]
        if there:
            where = where + (axis,)
        return self.copy(k, where, p.to[axis], (2 + stage) * depth + k, (1 + stage) * depth + k)

    def to_core(self, g, there=False):
        depth = self.place.depth
        flips = self.flips(g) + (("c",) if there else ())
        line = self.line_of(**self.place.flipped(*flips)).at[(pl.ds(0, depth), *self.part)]
        return remote(line, line, self.send.at[6 * depth + g], self.recv.at[5 * depth + g], self.place.to["c"])

    def line(self, k):
        if k:
            self.along(k, True).wait_recv()
        for right in (True, False):
            pl.when(self.goes(k, right))(lambda: self.along(k, right).start())
        for stage in (0, 1):
            self.to_axis(k, stage).start()

    def from_first(self, k):
        self.to_axis(k, 0, True).wait_recv()
        self.to_axis(k, 2).start()

    def from_second(self, k):
        self.to_axis(k, 1, True).wait_recv()

    def from_both(self, k):
        self.to_axis(k, 2, True).wait_recv()
        self.to_axis(k, 3).start()

    def core(self, g):
        self.to_core(g).start()

    def whole(self, g):
        if g < 3:
            self.to_core(g, True).wait_recv()
        else:
            for k in range(self.place.depth):
                self.to_axis(k, 3, True).wait_recv()

    def finish(self):
        for k in range(self.place.depth):
            for right in (True, False):
                pl.when(self.goes(k, right))(lambda: self.along(k, right).wait_send())
            for stage in range(4):
                self.to_axis(k, stage).wait_send()
        for g in range(3):
            self.to_core(g).wait_send()


class LineGather(Gather):
    def copy(self, k, where, to, send, recv):
        src = self.src.at[self.place.near(k)] if where == () else self.slot(k, *where)
        return remote(src, self.slot(k, *where), self.send.at[send], self.recv.at[recv], to)

    def line(self, k):
        for stage in (0, 1):
            self.to_axis(k, stage).start()

    def finish(self):
        for k in range(self.place.depth):
            for stage in range(4):
                self.to_axis(k, stage).wait_send()
        for g in range(3):
            self.to_core(g).wait_send()


class OwnLine(Gather):
    def __init__(self, place, src, line, send, recv):
        super().__init__(place, src, lambda y, x, c: line, "y", "x", send, recv)

    def line(self, k):
        if k:
            self.along(k, True).wait_recv()
        for right in (True, False):
            pl.when(self.goes(k, right))(lambda: self.along(k, right).start())

    def finish(self):
        for k in range(self.place.depth):
            for right in (True, False):
                pl.when(self.goes(k, right))(lambda: self.along(k, right).wait_send())


class Line:
    def __init__(self, place, keep, sent, came, send, recv):
        self.place, self.keep, self.sent, self.came = place, keep, sent, came
        self.send, self.recv = send, recv

    def copy(self, k, to, at):
        zk = self.place.near(k)
        return remote(self.sent.at[zk], self.came.at[at], self.send.at[k], self.recv.at[at], to)

    def take(self, at):
        self.copy(1, self.place.left, at).wait_recv()
        zk = jnp.where(at == self.place.depth, self.place.z, at)
        self.keep[zk] = self.keep[zk] + self.came[at].astype(F32)

    def moves(self, k):
        p, zk = self.place, self.place.near(k)
        return (
            (zk < p.z, p.left, zk),
            (zk > p.z, p.right, jnp.where(zk == p.z + 1, p.depth, zk)),
        )

    def step(self, k):
        p, zk = self.place, self.place.near(k)
        if k == 0:
            pl.when(p.has_right)(lambda: self.take(p.z))
            pl.when(p.has_left)(lambda: self.take(p.depth))
            return
        farther = ((zk < p.z) & p.has_right) | ((zk > p.z) & p.has_left)
        pl.when(farther)(lambda: self.take(zk))
        self.sent[zk] = self.keep[zk].astype(self.sent.dtype)
        for goes, to, at in self.moves(k):
            pl.when(goes)(lambda: self.copy(k, to, at).start())

    def finish(self):
        for k in range(1, self.place.depth):
            for goes, to, at in self.moves(k):
                pl.when(goes)(lambda: self.copy(k, to, at).wait_send())


class Scatter:
    def __init__(self, place, lhs, lhs_pair, rhs, rhs_pair, first, second, bufs, send, recv):
        self.place, self.lhs, self.lhs_pair, self.rhs, self.rhs_pair = place, lhs, lhs_pair, rhs, rhs_pair
        self.first, self.second, self.send, self.recv = first, second, send, recv
        self.s_sent, self.s_came, self.f_sent, self.f_came, self.keep, z_sent, z_came = bufs
        depth = place.depth
        self.sums = Line(place, self.keep, z_sent, z_came, send.at[pl.ds(2 + depth, depth)],
                         recv.at[pl.ds(2 + depth, depth + 1)])

    @staticmethod
    def sems(depth):
        return 2 + 2 * depth, 3 + 2 * depth

    @staticmethod
    def scratch(depth, rows, cols):
        block = lambda *lead: pltpu.VMEM(lead + (rows, cols), BF16)
        return [
            block(2, depth), block(2, depth), block(depth), block(depth),
            pltpu.VMEM((depth, rows, cols), F32), block(depth), block(depth + 1),
        ]

    def product(self, flips, store):
        at = self.place.flipped(*flips)
        pair = 2 * at["y"] + at["x"]
        one = 2 * pair + at["c"]
        rows, cols = self.keep.shape[1:]
        tile = 512

        def block(start, size):
            lanes = pl.ds(start, size)
            part = dot(self.lhs[one], self.rhs[:, lanes]) + dot(self.lhs_pair[pair], self.rhs_pair[:, lanes])
            for z in range(self.place.depth):
                store(z, lanes, part[z * rows : (z + 1) * rows])

        def loop(i, carry):
            block(pl.multiple_of(i * tile, tile), tile)
            return carry

        lax.fori_loop(0, cols // tile, loop, 0)
        if cols % tile:
            block(cols // tile * tile, cols % tile)

    def to_second(self, j):
        return remote(self.s_sent.at[j], self.s_came.at[j], self.send.at[j], self.recv.at[j],
                      self.place.to[self.second])

    def to_first(self, k):
        zk, n = self.place.near(k), 2 + k
        return remote(self.f_sent.at[zk], self.f_came.at[zk], self.send.at[n], self.recv.at[n],
                      self.place.to[self.first])

    def waves(self):
        return range(self.place.depth - 1, -1, -1)

    def send_second(self, j):
        def store(z, lanes, part):
            self.s_sent[j, z, :, lanes] = part.astype(BF16)

        self.product((self.second, self.first) if j == 0 else (self.second,), store)
        self.to_second(j).start()

    def send_first(self):
        self.to_second(0).wait_recv()

        def store(z, lanes, part):
            self.f_sent[z, :, lanes] = (part + self.s_came[0, z, :, lanes].astype(F32)).astype(BF16)

        self.product((self.first,), store)
        for k in self.waves():
            self.to_first(k).start()

    def hold(self):
        self.to_second(1).wait_recv()

        def store(z, lanes, part):
            self.keep[z, :, lanes] = part + self.s_came[1, z, :, lanes].astype(F32)

        self.product((), store)

    def step(self, k):
        self.to_first(k).wait_recv()
        zk = self.place.near(k)
        self.keep[zk] = self.keep[zk] + self.f_came[zk].astype(F32)
        self.sums.step(k)

    def finish(self):
        for j in (0, 1):
            self.to_second(j).wait_send()
        for k in self.waves():
            self.to_first(k).wait_send()
        self.sums.finish()


class SmallScatter:
    def __init__(self, place, src, c_came, half, x_came, keep, y_came, z_sent, z_came, send, recv):
        self.place, self.src, self.c_came, self.half = place, src, c_came, half
        self.x_came, self.keep, self.y_came = x_came, keep, y_came
        self.send, self.recv = send, recv
        depth = place.depth
        self.sums = Line(place, keep, z_sent, z_came, send.at[pl.ds(7, depth)],
                         recv.at[pl.ds(7, depth + 1)])

    @staticmethod
    def sems(depth):
        return 7 + depth, 8 + depth

    @staticmethod
    def scratch(depth, shape):
        block = lambda *lead: pltpu.VMEM(lead + shape, F32)
        return [
            block(2, 2, depth), block(2, 2, depth), block(2, depth), block(depth), block(depth),
            block(depth), block(depth + 1),
        ]

    def copy(self, n):
        p, own = self.place, self.place.own
        if n < 4:
            y, x = n // 2, n % 2
            src, dst, to = self.src.at[y, x, 1 - own["c"]], self.c_came.at[y, x], "c"
        elif n < 6:
            src, dst, to = self.half.at[n - 4, 1 - own["x"]], self.x_came.at[n - 4], "x"
        else:
            src, dst, to = self.half.at[1 - own["y"], own["x"]], self.y_came, "y"
        return remote(src, dst, self.send.at[n], self.recv.at[n], p.to[to])

    def stage(self, n):
        own = self.place.own
        if n == 0:
            for i in range(4):
                self.copy(i).start()
        elif n == 1:
            for i in range(4):
                self.copy(i).wait_recv()
            for y in (0, 1):
                for x in (0, 1):
                    self.half[y, x] = self.src[y, x, own["c"]] + self.c_came[y, x]
            for i in (4, 5):
                self.copy(i).start()
        elif n == 2:
            for i in (4, 5):
                self.copy(i).wait_recv()
            for y in (0, 1):
                self.half[y, own["x"]] = self.half[y, own["x"]] + self.x_came[y]
            self.copy(6).start()
        else:
            self.copy(6).wait_recv()
            self.keep[...] = self.half[own["y"], own["x"]] + self.y_came[...]

    def finish(self):
        for n in range(7):
            self.copy(n).wait_send()
        self.sums.finish()


def gather_kernel(
    depth, half, x_ref, small_src, wc_src, wg_src, pc_ref, normed_ref, normt_ref, small_ref, wc_out, gate_ref,
    hat_ref, edge_ref, wc_ref, edge_sem, own_sem, out_sem, send, recv, gate_send, gate_recv,
):
    place = Place(depth)
    place.meet()
    seqs, seg, features = x_ref.shape
    width = wc_src.shape[1]
    lo, hi = pl.ds(0, half), pl.ds(half, width - half)
    every = slice(None)
    weights = lambda y, x, c: wc_ref.at[y, x, c]
    lanes = [
        Gather(place, small_src, lambda y, x, c: small_ref.at[y, x, c], "y", "x", send.at[0], recv.at[0]),
        Gather(place, wc_src.at[:, lo], weights, "y", "x", send.at[1], recv.at[1], (every, lo)),
        Gather(place, wc_src.at[:, hi], weights, "x", "y", send.at[2], recv.at[2], (every, hi)),
    ]
    early, late = lanes[:2], lanes[2:]
    gate = OwnLine(place, wg_src, gate_ref, gate_send, gate_recv)
    own = place.own
    mine = (own["y"], own["x"], own["c"], place.z)
    copies = [
        pltpu.make_async_copy(src, dst.at[mine], own_sem.at[n])
        for n, (src, dst) in enumerate(((small_src, small_ref), (wc_src, wc_ref)))
    ]
    copies.append(pltpu.make_async_copy(wg_src, gate_ref.at[place.z], own_sem.at[2]))
    edge = remote(x_ref.at[:, pl.ds(seg - EDGE, EDGE)], edge_ref, edge_sem.at[0], edge_sem.at[1], place.right)

    def each(group, *steps):
        for name, k in steps:
            for lane in group:
                getattr(lane, name)(k)

    def keep(n):
        at = place.flipped(*((), ("y",), ("x",), ("y", "x"))[n])
        return pltpu.make_async_copy(wc_ref.at[at["y"], at["x"]], wc_out.at[at["y"], at["x"]], out_sem.at[n])

    rows = wc_src.shape[0]
    count = 2 * depth * rows

    def norm(flips):
        at = place.flipped(*flips)
        group = 2 * at["y"] + at["x"]
        here = pl.ds(pl.multiple_of(group * count, LANES), count)
        gain = sum(
            small_ref[at["y"], at["x"], c, z, : count // LANES] for c in (0, 1) for z in range(depth)
        )
        gain = jnp.concatenate([gain[i : i + 1] for i in range(count // LANES)], axis=1)
        for s in range(seqs):
            normed = (hat_ref[s, :, here] * gain).astype(BF16)
            normed_ref[s, :, here] = normed
            turned = normed[EDGE:].astype(F32).T.astype(BF16)
            for c in (0, 1):
                normt_ref[2 * group + c, :, s * seg : (s + 1) * seg] = turned[c * depth * rows : (c + 1) * depth * rows]

    def multiply(flips, n):
        at = place.flipped(*flips)
        here = pl.ds(pl.multiple_of((2 * at["y"] + at["x"]) * count, LANES), count)
        first, last = ((0, half), (half, width))[n]
        tile = 4 * LANES
        for start in range(first, last, tile):
            cols = slice(start, min(start + tile, last))
            block = jnp.concatenate(
                [wc_ref[at["y"], at["x"], c, z, :, cols] for c in (0, 1) for z in range(depth)], axis=0
            )
            for s in range(seqs):
                part = dot(normed_ref[s, :, here], block)
                if flips == ():
                    pc_ref[s, :, cols] = part
                else:
                    pc_ref[s, :, cols] += part

    each(early, ("line", 0))
    pl.when(place.has_right)(edge.start)
    for copy in copies:
        copy.start()
    pl.when(place.has_left)(edge.wait_recv)

    @pl.when(jnp.logical_not(place.has_left))
    def _():
        edge_ref[...] = jnp.zeros_like(edge_ref)

    def scale_rows(s, start, rows_in, r, step):
        values = rows_in[s, r : r + step].astype(F32)
        mean = jnp.mean(values * values, axis=1, keepdims=True)
        hat_ref[s, start + r : start + r + step] = values * lax.rsqrt(mean + EPS)

    pieces = []
    for s in range(seqs):
        pieces.append((s, 0, edge_ref, 0, EDGE))
        pieces += [(s, EDGE, x_ref, r, 64) for r in range(0, seg, 64)]
    share = -(-len(pieces) // depth)
    for k in range(depth):
        for piece in pieces[k * share : (k + 1) * share]:
            scale_rows(*piece)
        if k + 1 < depth:
            each(early, ("line", k + 1))
        if k == depth - 2:
            each(late, ("line", 0))
    for copy in copies:
        copy.wait()
    each(early, ("core", 0))
    for k in range(1, depth):
        each(late, ("line", k))
    each(late, ("core", 0))
    gate.line(0)
    for k in range(depth):
        each(early, ("from_first", k), ("from_second", k))
    each(early, ("core", 1), ("core", 2))
    each(late, ("from_first", 0), ("from_first", 1))
    each(early, ("whole", 0))
    norm(())
    multiply((), 0)
    for k in range(2, depth):
        each(late, ("from_first", k))
    each(early, ("whole", 1))
    norm(("y",))
    multiply(("y",), 0)
    for k in range(depth):
        each(late, ("from_second", k))
    each(late, ("core", 1), ("core", 2))
    each(early, ("whole", 2))
    norm(("x",))
    multiply(("x",), 0)
    gate.line(1)
    each(late, ("whole", 0))
    keep(0).start()
    multiply((), 1)
    for k in range(depth - 1):
        each(lanes, ("from_both", k))
    each(late, ("whole", 1), ("whole", 2))
    keep(1).start()
    keep(2).start()
    multiply(("y",), 1)
    gate.line(2)
    multiply(("x",), 1)
    each(lanes, ("from_both", depth - 1))
    each(early, ("whole", 3))
    norm(("y", "x"))
    multiply(("y", "x"), 0)
    gate.line(3)
    each(late, ("whole", 3))
    keep(3).start()
    multiply(("y", "x"), 1)
    for lane in (*lanes, gate):
        lane.finish()
    for n in range(4):
        keep(n).wait()
    pl.when(place.has_right)(edge.wait_send)


def gather_project(x, small, wc, wg, depth):
    shape = jax.ShapeDtypeStruct
    seqs, seg, features = x.shape
    slots = (2, 2, 2, depth)
    sends, receives = Gather.sems(depth)
    width = wc.shape[1]
    half = width // 2 // LANES * LANES
    anywhere, vmem = pl.BlockSpec(memory_space=pl.ANY), pl.BlockSpec(memory_space=pltpu.VMEM)
    dma = pltpu.SemaphoreType.DMA
    return pl.pallas_call(
        functools.partial(gather_kernel, depth, half),
        in_specs=[vmem, vmem, vmem, vmem],
        out_specs=[vmem, vmem, vmem, vmem, anywhere, vmem],
        out_shape=[
            shape((seqs, seg + EDGE, width), F32),
            shape((seqs, seg + EDGE, features), BF16),
            shape((8, depth * wc.shape[0], seqs * seg), BF16),
            shape(slots + small.shape, F32),
            shape(slots + wc.shape, BF16),
            shape((depth,) + wg.shape, BF16),
        ],
        scratch_shapes=[
            pltpu.VMEM((seqs, seg + EDGE, features), F32),
            pltpu.VMEM((seqs, EDGE, features), BF16),
            pltpu.VMEM(slots + wc.shape, BF16),
            dma((2,)), dma((3,)), dma((4,)), dma((3, sends)), dma((3, receives)),
            dma((2 * depth,)), dma((depth,)),
        ],
        compiler_params=pltpu.CompilerParams(
            collective_id=0, has_side_effects=True, vmem_limit_bytes=VMEM_LIMIT
        ),
        name="gather_project",
    )(x, small, wc, wg)


def fwd_a_kernel(
    head_dim, pc_ref, w_ref, b_ref, raw_ref, sb_ref, dl_ref,
    x_ref, bc_ref, dt_ref, cum_ref, cumt_ref, loc0_ref, seg_ref, tot_ref, bt_ref,
):
    step = pl.program_id(0)
    seqs = pc_ref.shape[0]
    seg = pc_ref.shape[1] - EDGE
    chunks = seg // CHUNK
    w, b = w_ref[...], b_ref[...]

    def acts_of(s):
        pre = causal_conv(pc_ref[s], w, b, seg)
        return pre * sigmoid(pre)

    @pl.when(step == 0)
    def _():
        row = lax.broadcasted_iota(jnp.int32, (CHUNK, CHUNK), 0)
        col = lax.broadcasted_iota(jnp.int32, (CHUNK, CHUNK), 1)
        tri = (col <= row).astype(F32)
        rate = -jnp.exp(dl_ref[...])
        for s in range(seqs):
            acts = acts_of(s)
            bc_ref[s * seg : (s + 1) * seg] = acts
            for c in range(chunks):
                q = s * chunks + c
                rows = slice(q * CHUNK, (q + 1) * CHUNK)
                bt_ref[q] = acts[c * CHUNK : (c + 1) * CHUNK, :LANES].T.astype(BF16)
                dt = softplus(raw_ref[s, EDGE + c * CHUNK : EDGE + (c + 1) * CHUNK] + sb_ref[...])
                cum = LOG2E * jnp.dot(tri, dt * rate, precision=HIGH, preferred_element_type=F32)
                dt_ref[rows] = dt
                cum_ref[rows] = cum
                cumt_ref[:, rows] = cum.T

    @pl.when(step > 0)
    def _():
        heads = GROUP // head_dim
        first = (step - 1) * heads
        cumg = lane_shift(cum_ref[...], first)
        dtg = lane_shift(dt_ref[...], first)
        for s in range(seqs):
            x = acts_of(s)
            x_ref[s * seg : (s + 1) * seg] = x
            state, total = None, None
            for c in range(chunks):
                q = s * chunks + c
                rows = slice(q * CHUNK, (q + 1) * CHUNK)
                ce = spread_all(cumg[rows], heads, head_dim)
                de = spread_all(dtg[rows], heads, head_dim)
                end = ce[CHUNK - 1 : CHUNK]
                uw = x[c * CHUNK : (c + 1) * CHUNK] * de * jnp.exp2(end - ce)
                loc = dot(bt_ref[q], uw.astype(BF16))
                tot = jnp.exp2(end)
                tot_ref[q : q + 1] = tot
                if c == 0:
                    loc0_ref[s] = loc
                    state, total = loc, tot
                else:
                    state, total = tot * state + loc, tot * total
            seg_ref[s] = state.astype(BF16)
            tot_ref[seqs * chunks + s : seqs * chunks + s + 1] = total


def fwd_a(pc, w, b, sb, dl, inner, head_dim):
    seqs, rows, cols = pc.shape
    seg = rows - EDGE
    tokens = seqs * seg
    groups = inner // GROUP
    state = LANES
    chunks = tokens // CHUNK
    at = lambda i: (i + groups) % (groups + 1)
    back = lambda i: jnp.maximum(i - 1, 0)
    return pl.pallas_call(
        functools.partial(fwd_a_kernel, head_dim),
        grid=(groups + 1,),
        in_specs=[
            pl.BlockSpec((seqs, rows, GROUP), lambda i: (0, 0, at(i))),
            pl.BlockSpec((w.shape[0], GROUP), lambda i: (0, at(i))),
            pl.BlockSpec((1, GROUP), lambda i: (0, at(i))),
            pl.BlockSpec((seqs, rows, LANES), lambda i: (0, 0, cols // LANES - 1)),
            whole((1, LANES)),
            whole((1, LANES)),
        ],
        out_specs=[
            pl.BlockSpec((tokens, GROUP), lambda i: (0, back(i))),
            whole((tokens, GROUP)),
            whole((tokens, LANES)),
            whole((tokens, LANES)),
            whole((LANES, tokens)),
            pl.BlockSpec((seqs, state, GROUP), lambda i: (0, 0, back(i))),
            pl.BlockSpec((seqs, state, GROUP), lambda i: (0, 0, back(i))),
            pl.BlockSpec((8, GROUP), lambda i: (0, back(i))),
        ],
        out_shape=[
            jax.ShapeDtypeStruct((tokens, inner), F32),
            jax.ShapeDtypeStruct((tokens, GROUP), F32),
            jax.ShapeDtypeStruct((tokens, LANES), F32),
            jax.ShapeDtypeStruct((tokens, LANES), F32),
            jax.ShapeDtypeStruct((LANES, tokens), F32),
            jax.ShapeDtypeStruct((seqs, state, inner), F32),
            jax.ShapeDtypeStruct((seqs, state, inner), BF16),
            jax.ShapeDtypeStruct((8, inner), F32),
        ],
        scratch_shapes=[pltpu.VMEM((chunks, LANES, CHUNK), BF16)],
        compiler_params=params(),
        name="conv_states",
    )(pc, w, b, pc, sb, dl)


def fwd_b_kernel(
    head_dim, x_ref, bc_ref, dt_ref, cum_ref, cumt_ref, s0_ref, loc0_ref, tot_ref, skip_ref,
    mixed_ref, s1_ref, cb_ref,
):
    step = pl.program_id(0)
    seqs = s0_ref.shape[0]
    chunks = x_ref.shape[0] // CHUNK // seqs
    heads = GROUP // head_dim

    @pl.when(step == 0)
    def _():
        for q in range(seqs * chunks):
            rows = slice(q * CHUNK, (q + 1) * CHUNK)
            cb_ref[q] = nt(bc_ref[rows, LANES:].astype(BF16), bc_ref[rows, :LANES].astype(BF16))

    first = step * heads
    cumg = lane_shift(cum_ref[...], first)
    dtg = lane_shift(dt_ref[...], first)
    cumr = head_rows(cumt_ref, first)
    row = lax.broadcasted_iota(jnp.int32, (CHUNK, CHUNK), 0)
    col = lax.broadcasted_iota(jnp.int32, (CHUNK, CHUNK), 1)
    causal = col <= row
    skip = skip_ref[...]
    for s in range(seqs):
        start = s0_ref[s]
        for c in range(chunks):
            q = s * chunks + c
            rows = slice(q * CHUNK, (q + 1) * CHUNK)
            x = x_ref[rows]
            ce = spread_all(cumg[rows], heads, head_dim)
            de = spread_all(dtg[rows], heads, head_dim)
            ub = (x * de).astype(BF16)
            cb = cb_ref[q]
            parts = []
            for j in range(0, heads, 2):
                mats = []
                for h in (j, j + 1):
                    there = jnp.broadcast_to(cumg[rows, h : h + 1], (CHUNK, CHUNK))
                    here = cumr[h : h + 1, rows]
                    decay = jnp.exp2(jnp.where(causal, there - here, -jnp.inf))
                    mats.append((decay * cb).astype(BF16))
                pair = ub[:, j * head_dim : (j + 2) * head_dim]
                parts.append(dot(jnp.concatenate(mats, axis=1), block_diagonal(pair, head_dim)))
            y = jnp.concatenate(parts, axis=1)
            y = y + jnp.exp2(ce) * dot(bc_ref[rows, LANES:].astype(BF16), start)
            mixed_ref[rows] = y + skip * x
            if c == 0:
                start = (tot_ref[q : q + 1] * start.astype(F32) + loc0_ref[s]).astype(BF16)
                s1_ref[s] = start


def fwd_b(x, bc, dt, cum, cumt, s0, loc0, tot, skip, head_dim):
    tokens, inner = x.shape
    seqs, state, _ = s0.shape
    groups = inner // GROUP
    wide = pl.BlockSpec((tokens, GROUP), lambda i: (0, i))
    states = pl.BlockSpec((seqs, state, GROUP), lambda i: (0, 0, i))
    return pl.pallas_call(
        functools.partial(fwd_b_kernel, head_dim),
        grid=(groups,),
        in_specs=[
            wide, whole(bc.shape), whole(dt.shape), whole(cum.shape), whole(cumt.shape),
            states, states,
            pl.BlockSpec((8, GROUP), lambda i: (0, i)),
            pl.BlockSpec((1, GROUP), lambda i: (0, i)),
        ],
        out_specs=[wide, states],
        out_shape=[
            jax.ShapeDtypeStruct((tokens, inner), F32),
            jax.ShapeDtypeStruct((seqs, state, inner), BF16),
        ],
        scratch_shapes=[pltpu.VMEM((tokens // CHUNK, CHUNK, CHUNK), F32)],
        compiler_params=params(),
        name="scan_outputs",
    )(x, bc, dt, cum, cumt, s0, loc0, tot, skip)


def halves(v):
    high = v.astype(BF16)
    return high, (v - high.astype(F32)).astype(BF16)


def dot_pairs(a, b, dims=((1,), (0,))):
    (ah, al), (bh, bl) = halves(a), halves(b)
    return dot(ah, bh, dims) + (dot(al, bh, dims) + dot(ah, bl, dims))


def dot_pair(a, b, dims=((1,), (0,))):
    high, low = halves(a)
    return dot(high, b, dims) + dot(low, b, dims)


def nt_exact(a, b):
    return lax.dot_general(a, b, (((1,), (1,)), ((), ())), precision=HIGH, preferred_element_type=F32)


class Chain:
    def __init__(self, place, came, sent, send, recv, backward):
        self.came, self.sent, self.send, self.recv = came, sent, send, recv
        self.gets, self.gives = place.has_left, place.has_right
        self.to = place.left if backward else place.right
        if backward:
            self.gets, self.gives = self.gives, self.gets
        self.behind = place.depth - 1 - place.z if backward else place.z

    def copy(self, g):
        return remote(self.sent.at[g], self.came.at[g], self.send.at[g], self.recv.at[g], self.to)

    def step(self, g, total, own):
        pl.when(self.gets)(lambda: self.copy(g).wait_recv())

        @pl.when(jnp.logical_not(self.gets))
        def _():
            self.came[g] = jnp.zeros(self.came.shape[1:], self.came.dtype)

        self.sent[g] = (total * self.came[g].astype(F32) + own).astype(BF16)
        pl.when(self.gives)(lambda: self.copy(g).start())

    def finish(self):
        groups = self.came.shape[0]

        def one(g, carry):
            self.copy(g).wait_send()
            return carry

        @pl.when(self.gives)
        def _():
            lax.fori_loop(0, groups, one, 0)


def scan_forward_kernel(
    depth, head_dim, groups,
    pc_ref, w_ref, b_ref, pcb_ref, wb_ref, bb_ref, raw_ref, sb_ref, dl_ref, skip_ref, normed_ref, cot_ref,
    gate_src, wo_src,
    bc_ref, dt_ref, cum_ref, cumt_ref, mixed_ref, s0_ref, s1_ref, s2_ref, tot_ref, z_out, dno_out, wg_out, wo_out,
    bt_ref, cb_ref, x_all, loc_all, seg_ring, tot_all, came, sent,
    z_ref, dno_ref, wg_ref, wo_ref, chain_send, chain_recv, own_sem, keep_sem, out_sem, send, recv,
):
    step = pl.program_id(0)
    lag = depth - 1
    seqs = pc_ref.shape[0]
    seg = pc_ref.shape[1] - EDGE
    chunks = seg // CHUNK
    heads = GROUP // head_dim
    place = Place(depth)
    chain = Chain(place, came, sent, chain_send, chain_recv, False)
    gate = LineGather(place, gate_src, lambda y, x, c: wg_ref.at[y, x, c], "y", "x", send.at[0], recv.at[0])
    out = Gather(place, wo_src, lambda y, x, c: wo_ref.at[y, x, c], "x", "y", send.at[1], recv.at[1])
    mine = (place.own["y"], place.own["x"], place.own["c"], place.z)
    copies = [
        pltpu.make_async_copy(gate_src, wg_ref.at[mine[:3]], own_sem.at[0]),
        pltpu.make_async_copy(wo_src, wo_ref.at[mine], own_sem.at[1]),
    ]

    def waves(*steps):
        for lane, name, k in steps:
            getattr(lane, name)(k)

    def acts_of(s, refs, j=0):
        part, w, b = refs
        cols = slice(j * GROUP, (j + 1) * GROUP)
        pre = causal_conv(part[s, :, cols], w[:, cols], b[:, cols], seg)
        return pre * sigmoid(pre)

    @pl.when(step == 0)
    def _():
        place.meet()
        waves(*((gate, "line", k) for k in range(depth)))
        for copy in copies:
            copy.start()
        row = lax.broadcasted_iota(jnp.int32, (CHUNK, CHUNK), 0)
        col = lax.broadcasted_iota(jnp.int32, (CHUNK, CHUNK), 1)
        tri = (col <= row).astype(F32)
        rate = -jnp.exp(dl_ref[...])
        for s in range(seqs):
            acts = acts_of(s, (pcb_ref, wb_ref, bb_ref))
            bc_ref[s * seg : (s + 1) * seg] = acts
            for c in range(chunks):
                q = s * chunks + c
                rows = slice(q * CHUNK, (q + 1) * CHUNK)
                b_proj = acts[c * CHUNK : (c + 1) * CHUNK, :LANES]
                c_proj = acts[c * CHUNK : (c + 1) * CHUNK, LANES:]
                bt_ref[q] = b_proj.T
                cb_ref[q] = nt_exact(c_proj, b_proj)
                dt = softplus(raw_ref[s, EDGE + c * CHUNK : EDGE + (c + 1) * CHUNK] + sb_ref[...])
                cum = LOG2E * jnp.dot(tri, dt * rate, precision=HIGH, preferred_element_type=F32)
                dt_ref[rows] = dt
                cum_ref[rows] = cum
                cumt_ref[:, rows] = cum.T

    slots = seg_ring.shape[0]

    def local_states(g, j):
        first = g * heads
        cumg = lane_shift(cum_ref[...], first)
        dtg = lane_shift(dt_ref[...], first)
        for s in range(seqs):
            x = acts_of(s, (pc_ref, w_ref, b_ref), j)
            x_all[g, s * seg : (s + 1) * seg] = x
            state, total = None, None
            for c in range(chunks):
                q = s * chunks + c
                rows = slice(q * CHUNK, (q + 1) * CHUNK)
                ce = spread_all(cumg[rows], heads, head_dim)
                de = spread_all(dtg[rows], heads, head_dim)
                end = ce[CHUNK - 1 : CHUNK]
                uw = x[c * CHUNK : (c + 1) * CHUNK] * de * jnp.exp2(end - ce)
                loc = dot_pairs(bt_ref[q], uw)
                tot = jnp.exp2(end)
                tot_all[g, q : q + 1] = tot
                if c == 0:
                    loc_all[g, s] = loc
                    state, total = loc, tot
                else:
                    state, total = tot * state + loc, tot * total
            seg_ring[lax.rem(g, slots), s] = state
            tot_all[g, seqs * chunks + s : seqs * chunks + s + 1] = total

    @pl.when((step > 0) & (step <= groups // 2))
    def _():
        for j in (0, 1):
            local_states(2 * (step - 1) + j, j)

    handed = step - 1 - chain.behind

    @pl.when((handed >= 0) & (handed < groups // 2))
    def _():
        for j in (0, 1):
            g = 2 * handed + j
            totals = tot_all[g, seqs * chunks : seqs * chunks + seqs]
            chain.step(g, totals[:, None, :], seg_ring[lax.rem(g, slots)])

    @pl.when(step > lag)
    def _():
        g = step - 1 - lag
        first = g * heads
        cumg = lane_shift(cum_ref[...], first)
        dtg = lane_shift(dt_ref[...], first)
        cumr = head_rows(cumt_ref, first)
        row = lax.broadcasted_iota(jnp.int32, (CHUNK, CHUNK), 0)
        col = lax.broadcasted_iota(jnp.int32, (CHUNK, CHUNK), 1)
        causal = col <= row
        skip = skip_ref[...]
        s0_ref[...] = came[g]
        s2_ref[...] = sent[g]
        tot_ref[...] = tot_all[g]
        for s in range(seqs):
            start = came[g, s]
            for c in range(chunks):
                q = s * chunks + c
                rows = slice(q * CHUNK, (q + 1) * CHUNK)
                x = x_all[g, rows]
                ce = spread_all(cumg[rows], heads, head_dim)
                de = spread_all(dtg[rows], heads, head_dim)
                ub = (x * de).astype(BF16)
                cb = cb_ref[q]
                parts = []
                for j in range(0, heads, 2):
                    mats = []
                    for h in (j, j + 1):
                        there = jnp.broadcast_to(cumg[rows, h : h + 1], (CHUNK, CHUNK))
                        here = cumr[h : h + 1, rows]
                        decay = jnp.exp2(jnp.where(causal, there - here, -jnp.inf))
                        mats.append((decay * cb).astype(BF16))
                    pair = ub[:, j * head_dim : (j + 2) * head_dim]
                    parts.append(dot(jnp.concatenate(mats, axis=1), block_diagonal(pair, head_dim)))
                y = jnp.concatenate(parts, axis=1)
                y = y + jnp.exp2(ce) * dot(bc_ref[rows, LANES:].astype(BF16), start)
                mixed_ref[rows] = y + skip * x
                if c == 0:
                    later = tot_all[g, q : q + 1] * start.astype(F32) + loc_all[g, s]
                    s1_ref[s] = later
                    start = later.astype(BF16)

    every = range(depth)
    by_group = ((), ("y",), ("x",), ("y", "x"))

    def both(lane, *waves_of):
        return [(lane, name, k) for k in waves_of for name in ("from_first", "from_second")]

    beside = {
        4: [(out, "line", 0), *both(gate, 0)],
        7: [(out, "line", 1), *both(gate, 1)],
        10: [(out, "line", 2)],
        13: [(out, "line", 3), (out, "core", 0)],
        14: [*both(gate, 2, 3), (gate, "core", 1), (gate, "core", 2)],
    }
    for at, steps in beside.items():
        pl.when(step == at)(lambda: waves(*steps))

    @pl.when(step == 2)
    def _():
        for copy in copies:
            copy.wait()
        waves((gate, "core", 0))

    @pl.when(step == groups + lag)
    def _():
        rows = 2 * depth * gate_src.shape[1]
        tile = 4 * LANES
        size = dno_ref.shape[1] // 8

        def keep(lane, g):
            src, dst = (wg_ref, wg_out) if lane is gate else (wo_ref, wo_out)
            at = place.flipped(*by_group[g])
            return pltpu.make_async_copy(
                src.at[at["y"], at["x"]], dst.at[at["y"], at["x"]], keep_sem.at[int(lane is out), g]
            )

        def ready(lane, g):
            lane.whole(g if g in (0, 3) or lane is gate else 3 - g)
            keep(lane, g).start()

        def group_of(g):
            at = place.flipped(*by_group[g])
            return 2 * at["y"] + at["x"]

        def gate_product(g):
            at = place.flipped(*by_group[g])
            here = pl.ds(pl.multiple_of(group_of(g) * rows, LANES), rows)
            for start in range(0, z_ref.shape[1], tile):
                cols = slice(start, start + tile)
                block = jnp.concatenate(
                    [wg_ref[at["y"], at["x"], c, z, :, cols] for c in (0, 1) for z in every], axis=0
                )
                for s in range(seqs):
                    part = dot(normed_ref[s, EDGE:, here], block)
                    at_rows = slice(s * seg, (s + 1) * seg)
                    if g == 0:
                        z_ref[at_rows, cols] = part
                    else:
                        z_ref[at_rows, cols] += part

        def out_product(g):
            at = place.flipped(*by_group[g])
            for c in (0, 1):
                block = jnp.concatenate([wo_ref[at["y"], at["x"], c, z] for z in every], axis=0)
                cols = pl.ds(pl.multiple_of((2 * group_of(g) + c) * size, LANES), size)
                dno_ref[:, cols] = nt(cot_ref[...], block)
            dno_copy(g).start()

        def dno_copy(g):
            cols = pl.ds(pl.multiple_of(group_of(g) * 2 * size, LANES), 2 * size)
            return pltpu.make_async_copy(dno_ref.at[:, cols], dno_out.at[:, cols], out_sem.at[g])

        last = depth - 1
        waves((out, "from_first", 0), (out, "from_first", 1))
        ready(gate, 0)
        gate_product(0)
        waves(*((out, "from_first", k) for k in range(2, last)))
        ready(gate, 1)
        gate_product(1)
        waves((out, "from_first", last), *((out, "from_second", k) for k in every))
        waves((out, "core", 1), (out, "core", 2))
        ready(gate, 2)
        gate_product(2)
        waves((gate, "from_both", 0), (out, "from_both", 0))
        ready(out, 0)
        out_product(0)
        waves((gate, "from_both", 1), (out, "from_both", 1))
        ready(out, 1)
        out_product(1)
        waves((gate, "from_both", 2), (out, "from_both", 2))
        ready(out, 2)
        out_product(2)
        waves((gate, "from_both", last), (out, "from_both", last))
        ready(gate, 3)
        gate_product(3)
        z_copy = pltpu.make_async_copy(z_ref, z_out, out_sem.at[4])
        z_copy.start()
        ready(out, 3)
        out_product(3)
        for lane in (gate, out):
            lane.finish()
        chain.finish()
        for g in range(4):
            dno_copy(g).wait()
            keep(gate, g).wait()
            keep(out, g).wait()
        z_copy.wait()


def scan_forward(pc, w, b, sb, dl, skip, normed, cot, gate_line, wo, inner, head_dim, depth):
    seqs, rows, cols = pc.shape
    tokens = seqs * (rows - EDGE)
    groups = inner // GROUP
    lag = depth - 1
    chunks = tokens // CHUNK
    shape, dma = jax.ShapeDtypeStruct, pltpu.SemaphoreType.DMA
    into = lambda i: jnp.clip(i - 1, 0, groups // 2 - 1)
    out = lambda i: jnp.maximum(i - 1 - lag, 0)
    states = pl.BlockSpec((seqs, LANES, GROUP), lambda i: (0, 0, out(i)))
    anywhere = pl.BlockSpec(memory_space=pl.ANY)
    sends, receives = Gather.sems(depth)
    slots = (2, 2, 2, depth)
    link = pltpu.VMEM((groups, seqs, LANES, GROUP), BF16)
    once = lambda v: pl.BlockSpec(v.shape, lambda i: (0,) * v.ndim, pipeline_mode=pl.Buffered(1))
    return pl.pallas_call(
        functools.partial(scan_forward_kernel, depth, head_dim, groups),
        grid=(groups + 1 + lag,),
        in_specs=[
            pl.BlockSpec((seqs, rows, 2 * GROUP), lambda i: (0, 0, into(i))),
            pl.BlockSpec((w.shape[0], 2 * GROUP), lambda i: (0, into(i))),
            pl.BlockSpec((1, 2 * GROUP), lambda i: (0, into(i))),
            pl.BlockSpec((seqs, rows, GROUP), lambda i: (0, 0, groups), pipeline_mode=pl.Buffered(1)),
            pl.BlockSpec((w.shape[0], GROUP), lambda i: (0, groups)),
            pl.BlockSpec((1, GROUP), lambda i: (0, groups)),
            pl.BlockSpec((seqs, rows, LANES), lambda i: (0, 0, cols // LANES - 1)),
            whole((1, LANES)),
            whole((1, LANES)),
            pl.BlockSpec((1, GROUP), lambda i: (0, out(i))),
            once(normed),
            once(cot),
            once(gate_line),
            once(wo),
        ],
        out_specs=[
            whole((tokens, GROUP)),
            whole((tokens, LANES)),
            whole((tokens, LANES)),
            whole((LANES, tokens)),
            pl.BlockSpec((tokens, GROUP), lambda i: (0, out(i))),
            states, states, states,
            pl.BlockSpec((8, GROUP), lambda i: (0, out(i))),
            anywhere,
            anywhere,
            anywhere,
            anywhere,
        ],
        out_shape=[
            shape((tokens, GROUP), F32),
            shape((tokens, LANES), F32),
            shape((tokens, LANES), F32),
            shape((LANES, tokens), F32),
            shape((tokens, inner), F32),
            shape((seqs, LANES, inner), BF16),
            shape((seqs, LANES, inner), F32),
            shape((seqs, LANES, inner), BF16),
            shape((8, inner), F32),
            shape((tokens, inner), F32),
            shape((tokens, inner), F32),
            shape(slots + gate_line.shape[1:], BF16),
            shape(slots + wo.shape, BF16),
        ],
        scratch_shapes=[
            pltpu.VMEM((chunks, LANES, CHUNK), F32),
            pltpu.VMEM((chunks, CHUNK, CHUNK), F32),
            pltpu.VMEM((groups, tokens, GROUP), F32), pltpu.VMEM((groups, seqs, LANES, GROUP), F32),
            pltpu.VMEM((2 * lag + 2, seqs, LANES, GROUP), F32), pltpu.VMEM((groups, 8, GROUP), F32),
            link, link,
            pltpu.VMEM((tokens, inner), F32), pltpu.VMEM((tokens, inner), F32),
            pltpu.VMEM(slots + gate_line.shape[1:], BF16), pltpu.VMEM(slots + wo.shape, BF16),
            dma((groups,)), dma((groups,)), dma((2,)), dma((2, 4)), dma((5,)), dma((2, sends)), dma((2, receives)),
        ],
        compiler_params=pltpu.CompilerParams(
            dimension_semantics=("arbitrary",), collective_id=3, has_side_effects=True,
            vmem_limit_bytes=VMEM_LIMIT,
        ),
        name="scan_forward",
    )(pc, w, b, pc, w, b, pc, sb, dl, skip, normed, cot, gate_line, wo)


def mid_kernel(
    z_ref, dno_ref, mixed_ref, wo_ref, gain_ref, in_ref, not_ref, out_ref, dm_ref, dz_ref, gg_ref, acc_ref,
):
    step = pl.program_id(0)
    inner = mixed_ref.shape[1]
    tiles, tile = not_ref.shape[0], not_ref.shape[1]

    @pl.when(step == 0)
    def _():
        gg_ref[...] = jnp.zeros_like(gg_ref)

    def lanes_of(i):
        return pl.ds(pl.multiple_of(i * tile, tile), tile)

    def fold(v):
        total = v[:, :LANES]
        for k in range(LANES, tile, LANES):
            total = total + v[:, k : k + LANES]
        return total

    def one(i, sums):
        sq, hg = sums
        at = lanes_of(i)
        z = z_ref[:, at]
        g = mixed_ref[:, at] * z * sigmoid(z)
        return sq + fold(g * g), hg + fold(dno_ref[:, at] * gain_ref[:, at] * g)

    zero = jnp.zeros((mixed_ref.shape[0], LANES), F32)
    sq, hg = lax.fori_loop(0, tiles, one, (zero, zero))
    scale = lax.rsqrt(jnp.sum(sq, axis=1, keepdims=True) / inner + EPS)
    pull = scale * scale * scale * (jnp.sum(hg, axis=1, keepdims=True) / inner)
    acc_ref[...] = in_ref[...].astype(F32)

    def two(i, carry):
        at = lanes_of(i)
        z, mixed, dno, gain = z_ref[:, at], mixed_ref[:, at], dno_ref[:, at], gain_ref[:, at]
        sig = sigmoid(z)
        act = z * sig
        g = mixed * act
        gs = g * scale
        no = gs * gain
        not_ref[i] = no.T.astype(BF16)
        acc_ref[...] += dot(no.astype(BF16), wo_ref[at, :])
        gg_ref[:, at] += jnp.sum(dno * gs, axis=0, keepdims=True)
        dg = scale * (dno * gain) - g * pull
        dm_ref[:, at] = dg * act
        dz_ref[:, at] = (dg * mixed * (sig * (1.0 + z * (1.0 - sig)))).astype(BF16)
        return carry

    lax.fori_loop(0, tiles, two, 0)
    out_ref[...] = acc_ref[...].astype(BF16)


def mid(z, dno, mixed, wo, gain, inputs, tiles):
    tokens, inner = mixed.shape
    width = inputs.shape[1]
    tile = inner // tiles
    narrow = pl.BlockSpec((CHUNK, width), lambda i: (i, 0))
    wide = pl.BlockSpec((CHUNK, inner), lambda i: (i, 0))
    once = lambda v: pl.BlockSpec(v.shape, lambda i: (0,) * v.ndim, pipeline_mode=pl.Buffered(1))
    return pl.pallas_call(
        mid_kernel,
        grid=(tokens // CHUNK,),
        in_specs=[wide, wide, wide, once(wo), whole((1, inner)), narrow],
        out_specs=[
            pl.BlockSpec((tiles, tile, CHUNK), lambda i: (0, 0, i)), narrow, wide, wide,
            whole((1, inner)),
        ],
        out_shape=[
            jax.ShapeDtypeStruct((tiles, tile, tokens), BF16),
            jax.ShapeDtypeStruct((tokens, width), BF16),
            jax.ShapeDtypeStruct((tokens, inner), F32),
            jax.ShapeDtypeStruct((tokens, inner), BF16),
            jax.ShapeDtypeStruct((1, inner), F32),
        ],
        scratch_shapes=[pltpu.VMEM((CHUNK, width), F32)],
        compiler_params=params(),
        name="gate_norm_project",
    )(z, dno, mixed, wo, gain, inputs)


def bwd_a_kernel(head_dim, seqs, dm_ref, bc_ref, cum_ref, tot_ref, seg_ref, ct_ref):
    step = pl.program_id(0)
    chunks = dm_ref.shape[0] // CHUNK // seqs
    heads = GROUP // head_dim

    @pl.when(step == 0)
    def _():
        for q in range(seqs * chunks):
            ct_ref[q] = bc_ref[q * CHUNK : (q + 1) * CHUNK, LANES:].T.astype(BF16)

    cumg = lane_shift(cum_ref[...], step * heads)
    for s in range(seqs):
        state = None
        for c in range(chunks - 1, -1, -1):
            q = s * chunks + c
            rows = slice(q * CHUNK, (q + 1) * CHUNK)
            ey = jnp.exp2(spread_all(cumg[rows], heads, head_dim)) * dm_ref[rows]
            loc = dot(ct_ref[q], ey.astype(BF16))
            state = loc if state is None else tot_ref[q : q + 1] * state + loc
        seg_ref[s] = state.astype(BF16)


def bwd_a(dm, bc, cum, tot, seqs, head_dim):
    tokens, inner = dm.shape
    return pl.pallas_call(
        functools.partial(bwd_a_kernel, head_dim, seqs),
        grid=(inner // GROUP,),
        in_specs=[
            pl.BlockSpec((tokens, GROUP), lambda i: (0, i)), whole(bc.shape), whole(cum.shape),
            pl.BlockSpec((8, GROUP), lambda i: (0, i)),
        ],
        out_specs=pl.BlockSpec((seqs, LANES, GROUP), lambda i: (0, 0, i)),
        out_shape=jax.ShapeDtypeStruct((seqs, LANES, inner), BF16),
        scratch_shapes=[pltpu.VMEM((tokens // CHUNK, LANES, CHUNK), BF16)],
        compiler_params=params(),
        name="adjoint_states",
    )(dm, bc, cum, tot)


def bwd_b_kernel(
    head_dim, groups, pc_ref, w_ref, b_ref, raw_ref, sb_ref, dl_ref, bc_ref, dt_ref, cum_ref, cumt_ref,
    dm_ref, mixed_ref, s0_ref, s1_ref, s2_ref, g_ref, tot_ref, skip_ref,
    dc_ref, tail_ref, edge_ref, gw_ref, gb_ref, gskip_ref, draw_ref, hsum_ref,
    cbt_ref, dcbt_ref, db_acc, dc_acc, r1_ref, r2_ref, dtot_ref,
):
    step = pl.program_id(0)
    seqs = pc_ref.shape[0]
    seg = pc_ref.shape[1] - EDGE
    chunks = seg // CHUNK
    heads = GROUP // head_dim
    w, b = w_ref[...], b_ref[...]
    taps = w.shape[0]

    @pl.when(step == 0)
    def _():
        for q in range(seqs * chunks):
            rows = slice(q * CHUNK, (q + 1) * CHUNK)
            cbt_ref[q] = nt(bc_ref[rows, :LANES].astype(BF16), bc_ref[rows, LANES:].astype(BF16))
        dcbt_ref[...] = jnp.zeros_like(dcbt_ref)
        db_acc[...] = jnp.zeros_like(db_acc)
        dc_acc[...] = jnp.zeros_like(dc_acc)
        r1_ref[...] = jnp.zeros_like(r1_ref)
        r2_ref[...] = jnp.zeros_like(r2_ref)
        dtot_ref[...] = jnp.zeros_like(dtot_ref)

    def conv_back(s, ext, pre, sig, d_act):
        d_pre = d_act * (sig * (1.0 + pre * (1.0 - sig)))
        zero = jnp.zeros((EDGE, d_pre.shape[1]), F32)
        padded = jnp.concatenate([zero, d_pre, zero], axis=0)
        total = None
        for k in range(taps):
            at = taps - 1 - k
            term = w[k : k + 1] * padded[at : at + seg + EDGE]
            total = term if total is None else total + term
        edge_ref[s] = total[:EDGE]
        dc_ref[s * seg : (s + 1) * seg] = total[EDGE:].astype(BF16)
        tail_ref[s] = total[seg:]
        for k in range(taps):
            at = EDGE - (taps - 1) + k
            grad = jnp.sum(ext[at : at + seg] * d_pre, axis=0, keepdims=True)
            gw_ref[k : k + 1] = grad if s == 0 else gw_ref[k : k + 1] + grad
        grad = jnp.sum(d_pre, axis=0, keepdims=True)
        gb_ref[...] = grad if s == 0 else gb_ref[...] + grad

    def by_head(value, pick):
        high = value.astype(BF16)
        return dot(high, pick) + dot((value - high.astype(F32)).astype(BF16), pick)

    @pl.when(step < groups)
    def _():
        first = step * heads
        cumg = lane_shift(cum_ref[...], first)
        dtg = lane_shift(dt_ref[...], first)
        cumr = head_rows(cumt_ref, first)
        row = lax.broadcasted_iota(jnp.int32, (CHUNK, CHUNK), 0)
        col = lax.broadcasted_iota(jnp.int32, (CHUNK, CHUNK), 1)
        causal = row <= col
        lane = lax.broadcasted_iota(jnp.int32, (GROUP, LANES), 0)
        head = lax.broadcasted_iota(jnp.int32, (GROUP, LANES), 1)
        pick = (head == first + lane // head_dim).astype(BF16)
        skip = skip_ref[...]
        grad_skip = None
        for s in range(seqs):
            ext = pc_ref[s]
            pre = causal_conv(ext, w, b, seg)
            sig = sigmoid(pre)
            acts = pre * sig
            adj = g_ref[s].astype(F32)
            d_acts = [None] * chunks
            for c in range(chunks - 1, -1, -1):
                q = s * chunks + c
                rows = slice(q * CHUNK, (q + 1) * CHUNK)
                x = acts[c * CHUNK : (c + 1) * CHUNK]
                dy = dm_ref[rows]
                ce = spread_all(cumg[rows], heads, head_dim)
                de = spread_all(dtg[rows], heads, head_dim)
                weight = jnp.exp2(ce[CHUNK - 1 : CHUNK] - ce)
                u = x * de
                ub = u.astype(BF16)
                dyb = dy.astype(BF16)
                cbt = cbt_ref[q]
                parts = []
                dcbt = dcbt_ref[q]
                for j in range(0, heads, 2):
                    lanes = slice(j * head_dim, (j + 2) * head_dim)
                    dy_block = block_diagonal(dyb[:, lanes], head_dim)
                    dm = nt(ub[:, lanes], dy_block)
                    mats = []
                    for k, h in enumerate((j, j + 1)):
                        here = jnp.broadcast_to(cumg[rows, h : h + 1], (CHUNK, CHUNK))
                        there = cumr[h : h + 1, rows]
                        decay = jnp.exp2(jnp.where(causal, there - here, -jnp.inf))
                        mats.append((decay * cbt).astype(BF16))
                        dcbt = dcbt + decay * dm[:, k * CHUNK : (k + 1) * CHUNK]
                    parts.append(dot(jnp.concatenate(mats, axis=1), dy_block))
                dcbt_ref[q] = dcbt
                start = s0_ref[s] if c == 0 else s1_ref[s]
                end = s2_ref[s] if c == chunks - 1 else s1_ref[s]
                adj_b = adj.astype(BF16)
                bb = bc_ref[rows, :LANES].astype(BF16)
                cb = bc_ref[rows, LANES:].astype(BF16)
                ey = (jnp.exp2(ce) * dy).astype(BF16)
                du = jnp.concatenate(parts, axis=1) + weight * dot(bb, adj_b)
                db_acc[rows] += nt((u * weight).astype(BF16), adj_b)
                dc_acc[rows] += nt(ey, start)
                r1_ref[rows] += by_head(dyb.astype(F32) * (mixed_ref[rows] - skip * x), pick)
                r2_ref[rows] += by_head(x * du, pick)
                dtot_ref[q : q + 1] += by_head(
                    jnp.sum(adj * end.astype(F32), axis=0, keepdims=True), pick
                )
                grad = jnp.sum(dy * x, axis=0, keepdims=True)
                grad_skip = grad if grad_skip is None else grad_skip + grad
                d_acts[c] = du * de + skip * dy
                if c > 0:
                    adj = tot_ref[q : q + 1] * adj + dot(cb, ey, ((0,), (0,)))
            conv_back(s, ext, pre, sig, jnp.concatenate(d_acts, axis=0))
        gskip_ref[...] = grad_skip

    @pl.when(step == groups)
    def _():
        row = lax.broadcasted_iota(jnp.int32, (CHUNK, CHUNK), 0)
        col = lax.broadcasted_iota(jnp.int32, (CHUNK, CHUNK), 1)
        later = (row <= col).astype(F32)
        rate = -jnp.exp(dl_ref[...])
        sum_raw = jnp.zeros((1, LANES), F32)
        sum_log = jnp.zeros((1, LANES), F32)
        for s in range(seqs):
            ext = pc_ref[s]
            pre = causal_conv(ext, w, b, seg)
            sig = sigmoid(pre)
            parts = []
            for c in range(chunks):
                q = s * chunks + c
                rows = slice(q * CHUNK, (q + 1) * CHUNK)
                dcbt = dcbt_ref[q]
                bb = bc_ref[rows, :LANES].astype(BF16)
                cb = bc_ref[rows, LANES:].astype(BF16)
                d_b = db_acc[rows] + dot(dcbt.astype(BF16), cb)
                d_c = dc_acc[rows] + dot(dcbt.T.astype(BF16), bb)
                parts.append(jnp.concatenate([d_b, d_c], axis=1))
                dt = dt_ref[rows]
                r2 = r2_ref[rows]
                d_log = jnp.dot(
                    later, r1_ref[rows] - dt * r2, precision=HIGH, preferred_element_type=F32
                )
                d_log = d_log + dtot_ref[q : q + 1]
                raw = raw_ref[s, EDGE + c * CHUNK : EDGE + (c + 1) * CHUNK] + sb_ref[...]
                d_raw = (r2 + rate * d_log) * sigmoid(raw)
                draw_ref[rows] = d_raw
                sum_raw = sum_raw + jnp.sum(d_raw, axis=0, keepdims=True)
                sum_log = sum_log + jnp.sum(d_log * dt, axis=0, keepdims=True) * rate
            conv_back(s, ext, pre, sig, jnp.concatenate(parts, axis=0))
        hsum_ref[0:1] = sum_raw
        hsum_ref[1:2] = sum_log


def bwd_b(pc, w, b, sb, dl, bc, dt, cum, cumt, dm, mixed, s0, s1, s2, g, tot, skip, head_dim):
    seqs, rows, cols = pc.shape
    tokens, inner = dm.shape
    groups = inner // GROUP
    taps, channels = w.shape
    wide = pl.BlockSpec((tokens, GROUP), lambda i: (0, jnp.minimum(i, groups - 1)))
    states = pl.BlockSpec((seqs, LANES, GROUP), lambda i: (0, 0, jnp.minimum(i, groups - 1)))
    line = lambda n: pl.BlockSpec((n, GROUP), lambda i: (0, jnp.minimum(i, groups - 1)))
    conv = lambda n: pl.BlockSpec((n, GROUP), lambda i: (0, i))
    ends = pl.BlockSpec((seqs, EDGE, GROUP), lambda i: (0, 0, i))
    chunks = tokens // CHUNK
    shape = jax.ShapeDtypeStruct
    return pl.pallas_call(
        functools.partial(bwd_b_kernel, head_dim, groups),
        grid=(groups + 1,),
        in_specs=[
            pl.BlockSpec((seqs, rows, GROUP), lambda i: (0, 0, i)),
            conv(taps),
            conv(1),
            pl.BlockSpec((seqs, rows, LANES), lambda i: (0, 0, cols // LANES - 1)),
            whole((1, LANES)), whole((1, LANES)),
            whole(bc.shape), whole(dt.shape), whole(cum.shape), whole(cumt.shape),
            wide, wide, states, states, states, states, line(8), line(1),
        ],
        out_specs=[
            conv(tokens), ends, ends, conv(taps), conv(1), line(1),
            whole((tokens, LANES)), whole((2, LANES)),
        ],
        out_shape=[
            shape((tokens, channels), BF16),
            shape((seqs, EDGE, channels), F32),
            shape((seqs, EDGE, channels), F32),
            shape((taps, channels), F32),
            shape((1, channels), F32),
            shape((1, inner), F32),
            shape((tokens, LANES), F32),
            shape((2, LANES), F32),
        ],
        scratch_shapes=[
            pltpu.VMEM((chunks, CHUNK, CHUNK), F32),
            pltpu.VMEM((chunks, CHUNK, CHUNK), F32),
            pltpu.VMEM((tokens, LANES), F32),
            pltpu.VMEM((tokens, LANES), F32),
            pltpu.VMEM((tokens, LANES), F32),
            pltpu.VMEM((tokens, LANES), F32),
            pltpu.VMEM((8, LANES), F32),
        ],
        compiler_params=params(),
        name="scan_backward",
    )(pc, w, b, pc, sb, dl, bc, dt, cum, cumt, dm, mixed, s0, s1, s2, g, tot, skip)


PIECES = (3, 2, 1)


def piece_of(columns, n):
    unit = columns // sum(PIECES)
    return sum(PIECES[:n]) * unit, sum(PIECES[: n + 1]) * unit


def pair_copies(place, lhs, rhs, send, recv):
    other = 1 - place.own["c"]
    parts = [(src.at[2 * g + other], dst.at[g]) for src, dst in lhs for g in range(4)] + list(rhs)
    return [
        remote(src, dst, send.at[n], recv.at[n], place.to["c"]) for n, (src, dst) in enumerate(parts)
    ]


def scan_backward_kernel(
    depth, head_dim, groups,
    pc_ref, w_ref, b_ref, raw_ref, sb_ref, dl_ref, bc_ref, dt_ref, cum_ref, cumt_ref,
    dma_ref, dm_ref, mixed_ref, s0_ref, s1_ref, s2_ref, tot_ref, skip_ref,
    nt_src, dz_src, no_src, cot_src,
    dc_out, gw_ref, gb_ref, hsum_ref, a_out, b_out, nt_out,
    cbt_ref, ct_ref, dcbt_ref, db_acc, dc_acc, r1_ref, r2_ref, dtot_ref, skip_acc,
    dc_ref, tail_ref, edge_ref, edge_came, seg_ring, tot_all, came, sent,
    nt_pair, dz_pair, no_pair, cot_pair,
    chain_send, chain_recv, edge_send, edge_recv, pair_send, pair_recv, out_sem, send, recv, *bufs,
):
    step = pl.program_id(0)
    lag = depth - 1
    seqs = pc_ref.shape[0]
    seg = pc_ref.shape[1] - EDGE
    chunks = seg // CHUNK
    heads = GROUP // head_dim
    w, b = w_ref[...], b_ref[...]
    taps = w.shape[0]
    channels = tail_ref.shape[2]
    place = Place(depth)
    chain = Chain(place, came, sent, chain_send, chain_recv, True)
    cut = lambda ref, lo, hi: ref.at[:, pl.ds(lo, hi - lo)]
    rhs = []
    for n in range(2):
        for src, dst in ((dz_src, dz_pair), (cot_src, cot_pair)):
            lo, hi = piece_of(src.shape[1], n)
            hi = hi if n == 0 else src.shape[1]
            rhs.append((cut(src, lo, hi), cut(dst, lo, hi)))
    pairs = pair_copies(place, ((nt_src, nt_pair), (no_src, no_pair)), rhs, pair_send, pair_recv)
    def piece(ref, n):
        lo, hi = piece_of(ref.shape[1], n)
        return ref.at[:, pl.ds(lo, hi - lo)]

    lanes = []
    for n in range(len(PIECES)):
        lanes += [
            Scatter(place, nt_src, nt_pair, piece(dz_src, n), piece(dz_pair, n), "y", "x",
                    bufs[14 * n : 14 * n + 7], send.at[2 * n], recv.at[2 * n]),
            Scatter(place, no_src, no_pair, piece(cot_src, n), piece(cot_pair, n), "x", "y",
                    bufs[14 * n + 7 : 14 * n + 14], send.at[2 * n + 1], recv.at[2 * n + 1]),
        ]
    edges = [
        remote(edge_ref.at[:, :, cols], edge_came.at[:, :, cols], edge_send.at[n], edge_recv.at[n], place.left)
        for n, cols in enumerate((pl.ds(0, channels - GROUP), pl.ds(channels - GROUP, GROUP)))
    ]
    outs = [
        pltpu.make_async_copy(src, dst, out_sem.at[n])
        for n, (src, dst) in enumerate(((nt_pair, nt_out), (dc_ref, dc_out)))
    ]

    def run(first, name, *rest):
        for lane in lanes[2 * first : 2 * first + 2]:
            getattr(lane, name)(*rest)

    def at_step(n, *what):
        pl.when(step == n)(lambda: run(*what))

    @pl.when(step == 0)
    def _():
        place.meet()
        for copy in pairs:
            copy.start()
        for q in range(seqs * chunks):
            rows = slice(q * CHUNK, (q + 1) * CHUNK)
            b_proj, c_proj = bc_ref[rows, :LANES], bc_ref[rows, LANES:]
            cbt_ref[q] = nt_exact(b_proj, c_proj)
            ct_ref[q] = c_proj.T
        dcbt_ref[...] = jnp.zeros_like(dcbt_ref)
        db_acc[...] = jnp.zeros_like(db_acc)
        dc_acc[...] = jnp.zeros_like(dc_acc)
        r1_ref[...] = jnp.zeros_like(r1_ref)
        r2_ref[...] = jnp.zeros_like(r2_ref)
        skip_acc[...] = jnp.zeros_like(skip_acc)
        dtot_ref[...] = jnp.zeros_like(dtot_ref)

    slots = seg_ring.shape[0]

    @pl.when(step < groups // 2)
    def _():
        for j in (0, 1):
            g = 2 * step + j
            cols = slice(j * GROUP, (j + 1) * GROUP)
            cumg = lane_shift(cum_ref[...], g * heads)
            tot_all[g] = tot_ref[:, cols]
            for s in range(seqs):
                state = None
                for c in range(chunks - 1, -1, -1):
                    q = s * chunks + c
                    rows = slice(q * CHUNK, (q + 1) * CHUNK)
                    ey = jnp.exp2(spread_all(cumg[rows], heads, head_dim)) * dma_ref[rows, cols]
                    loc = dot_pairs(ct_ref[q], ey)
                    state = loc if state is None else tot_ref[q : q + 1, cols] * state + loc
                seg_ring[lax.rem(g, slots), s] = state

    handed = step - chain.behind

    @pl.when((handed >= 0) & (handed < groups // 2))
    def _():
        for j in (0, 1):
            g = 2 * handed + j
            totals = tot_all[g, seqs * chunks : seqs * chunks + seqs]
            chain.step(g, totals[:, None, :], seg_ring[lax.rem(g, slots)])

    @pl.when(step == lag)
    def _():
        for copy in pairs[:10]:
            copy.wait_recv()
        outs[0].start()

    @pl.when(step == lag + 4)
    def _():
        for copy in pairs[10:]:
            copy.wait_recv()

    at_step(lag, 0, "send_second", 0)
    at_step(lag + 1, 0, "send_second", 1)
    at_step(lag + 3, 0, "send_first")
    at_step(lag + 4, 1, "send_second", 0)
    at_step(lag + 4, 1, "send_second", 1)
    at_step(lag + 5, 0, "hold")
    at_step(lag + 6, 2, "send_second", 0)
    at_step(lag + 6, 2, "send_second", 1)
    for n, k in enumerate(lanes[0].waves()):
        at_step(lag + 7 + n, 0, "step", k)
    at_step(lag + 8, 1, "send_first")
    at_step(lag + 9, 1, "hold")
    at_step(lag + 10, 2, "send_first")
    at_step(lag + 11, 1, "step", depth - 1)
    at_step(lag + 12, 1, "step", depth - 2)
    at_step(lag + 12, 2, "hold")

    def conv_back(s, ext, pre, sig, d_act, at):
        lanes_at = pl.ds(pl.multiple_of(at * GROUP, GROUP), GROUP)
        d_pre = d_act * (sig * (1.0 + pre * (1.0 - sig)))
        zero = jnp.zeros((EDGE, d_pre.shape[1]), F32)
        padded = jnp.concatenate([zero, d_pre, zero], axis=0)
        total = None
        for k in range(taps):
            start = taps - 1 - k
            term = w[k : k + 1] * padded[start : start + seg + EDGE]
            total = term if total is None else total + term
        edge_ref[s, :, lanes_at] = total[:EDGE].astype(BF16)
        dc_ref[s * seg : (s + 1) * seg, lanes_at] = total[EDGE:].astype(BF16)
        tail_ref[s, :, lanes_at] = total[seg:]
        for k in range(taps):
            start = EDGE - (taps - 1) + k
            grad = jnp.sum(ext[start : start + seg] * d_pre, axis=0, keepdims=True)
            gw_ref[k : k + 1] = grad if s == 0 else gw_ref[k : k + 1] + grad
        grad = jnp.sum(d_pre, axis=0, keepdims=True)
        gb_ref[...] = grad if s == 0 else gb_ref[...] + grad

    def by_head(value, pick):
        high = value.astype(BF16)
        return dot(high, pick) + dot((value - high.astype(F32)).astype(BF16), pick)

    @pl.when((step >= lag) & (step < lag + groups))
    def _():
        g = step - lag
        first = g * heads
        cumg = lane_shift(cum_ref[...], first)
        dtg = lane_shift(dt_ref[...], first)
        cumr = head_rows(cumt_ref, first)
        row = lax.broadcasted_iota(jnp.int32, (CHUNK, CHUNK), 0)
        col = lax.broadcasted_iota(jnp.int32, (CHUNK, CHUNK), 1)
        causal = row <= col
        lane = lax.broadcasted_iota(jnp.int32, (GROUP, LANES), 0)
        head = lax.broadcasted_iota(jnp.int32, (GROUP, LANES), 1)
        pick = (head == first + lane // head_dim).astype(BF16)
        skip = skip_ref[...]
        grad_skip = None
        for s in range(seqs):
            ext = pc_ref[s]
            pre = causal_conv(ext, w, b, seg)
            sig = sigmoid(pre)
            acts = pre * sig
            adj = came[g, s].astype(F32)
            d_acts = [None] * chunks
            for c in range(chunks - 1, -1, -1):
                q = s * chunks + c
                rows = slice(q * CHUNK, (q + 1) * CHUNK)
                x = acts[c * CHUNK : (c + 1) * CHUNK]
                dy = dm_ref[rows]
                ce = spread_all(cumg[rows], heads, head_dim)
                de = spread_all(dtg[rows], heads, head_dim)
                weight = jnp.exp2(ce[CHUNK - 1 : CHUNK] - ce)
                u = x * de
                ub = u.astype(BF16)
                dyb = dy.astype(BF16)
                cbt = cbt_ref[q]
                parts = []
                dcbt = dcbt_ref[q]
                for j in range(0, heads, 2):
                    two = slice(j * head_dim, (j + 2) * head_dim)
                    dy_block = block_diagonal(dyb[:, two], head_dim)
                    dm = nt(ub[:, two], dy_block)
                    mats = []
                    for k, h in enumerate((j, j + 1)):
                        here = jnp.broadcast_to(cumg[rows, h : h + 1], (CHUNK, CHUNK))
                        there = cumr[h : h + 1, rows]
                        decay = jnp.exp2(jnp.where(causal, there - here, -jnp.inf))
                        mats.append((decay * cbt).astype(BF16))
                        dcbt = dcbt + decay * dm[:, k * CHUNK : (k + 1) * CHUNK]
                    parts.append(dot(jnp.concatenate(mats, axis=1), dy_block))
                dcbt_ref[q] = dcbt
                start = s0_ref[s] if c == 0 else s1_ref[s]
                end = s2_ref[s] if c == chunks - 1 else s1_ref[s]
                adj_b = adj.astype(BF16)
                bb = bc_ref[rows, :LANES].astype(BF16)
                ey = jnp.exp2(ce) * dy
                du = jnp.concatenate(parts, axis=1) + weight * dot(bb, adj_b)
                uw = u * weight
                across = ((1,), (1,))
                db_acc[rows] += dot_pair(uw, adj_b, across) if c == chunks - 1 else dot_pairs(uw, adj, across)
                dc_acc[rows] += dot_pair(ey, start, across) if c == 0 else dot_pairs(ey, start, across)
                r1_ref[rows] += by_head(dyb.astype(F32) * (mixed_ref[rows] - skip * x), pick)
                r2_ref[rows] += by_head(x * du, pick)
                dtot_ref[q : q + 1] += by_head(
                    jnp.sum(adj * end.astype(F32), axis=0, keepdims=True), pick
                )
                grad = jnp.sum(dy * x, axis=0, keepdims=True)
                grad_skip = grad if grad_skip is None else grad_skip + grad
                d_acts[c] = du * de + skip * dy
                if c > 0:
                    adj = tot_all[g, q : q + 1] * adj + dot_pairs(ct_ref[q], ey)
            conv_back(s, ext, pre, sig, jnp.concatenate(d_acts, axis=0), g)
        skip_acc[0:1] += by_head(grad_skip, pick)

    @pl.when(step == lag + groups)
    def _():
        pl.when(place.has_left)(edges[0].start)
        row = lax.broadcasted_iota(jnp.int32, (CHUNK, CHUNK), 0)
        col = lax.broadcasted_iota(jnp.int32, (CHUNK, CHUNK), 1)
        later = (row <= col).astype(F32)
        rate = -jnp.exp(dl_ref[...])
        sum_raw = jnp.zeros((1, LANES), F32)
        sum_log = jnp.zeros((1, LANES), F32)
        for s in range(seqs):
            ext = pc_ref[s]
            pre = causal_conv(ext, w, b, seg)
            sig = sigmoid(pre)
            parts = []
            for c in range(chunks):
                q = s * chunks + c
                rows = slice(q * CHUNK, (q + 1) * CHUNK)
                dcbt = dcbt_ref[q]
                d_b = db_acc[rows] + dot_pairs(dcbt, bc_ref[rows, LANES:])
                d_c = dc_acc[rows] + dot_pairs(dcbt.T, bc_ref[rows, :LANES])
                parts.append(jnp.concatenate([d_b, d_c], axis=1))
                dt = dt_ref[rows]
                r2 = r2_ref[rows]
                d_log = jnp.dot(
                    later, r1_ref[rows] - dt * r2, precision=HIGH, preferred_element_type=F32
                )
                d_log = d_log + dtot_ref[q : q + 1]
                raw = raw_ref[s, EDGE + c * CHUNK : EDGE + (c + 1) * CHUNK] + sb_ref[...]
                d_raw = (r2 + rate * d_log) * sigmoid(raw)
                dc_ref[rows, channels:] = d_raw.astype(BF16)
                sum_raw = sum_raw + jnp.sum(d_raw, axis=0, keepdims=True)
                sum_log = sum_log + jnp.sum(d_log * dt, axis=0, keepdims=True) * rate
            conv_back(s, ext, pre, sig, jnp.concatenate(parts, axis=0), groups)
        hsum_ref[0:1] = sum_raw
        hsum_ref[1:2] = sum_log
        hsum_ref[2:3] = skip_acc[0:1]
        pl.when(place.has_left)(edges[1].start)

        @pl.when(place.has_right)
        def _():
            for copy in edges:
                copy.wait_recv()
            for s in range(seqs):
                fixed = tail_ref[s] + edge_came[s].astype(F32)
                dc_ref[(s + 1) * seg - EDGE : (s + 1) * seg, :channels] = fixed.astype(BF16)

        outs[1].start()
        run(2, "step", depth - 1)
        for k in range(depth - 3, -1, -1):
            run(1, "step", k)
            run(2, "step", k + 1)
        run(2, "step", 0)
        for n, out in enumerate((a_out, b_out)):
            for i in range(len(PIECES)):
                lo, hi = piece_of(out.shape[1], i)
                out[:, lo:hi] = lanes[2 * i + n].keep[place.z]
        for lane in lanes:
            lane.finish()
        chain.finish()

        @pl.when(place.has_left)
        def _():
            for copy in edges:
                copy.wait_send()

        for copy in pairs:
            copy.wait_send()
        for copy in outs:
            copy.wait()


def scan_backward(
    pc, w, b, sb, dl, bc, dt, cum, cumt, dm, mixed, s0, s1, s2, tot, skip, normed_t, dz, turned, cot,
    head_dim, depth,
):
    seqs, rows, cols = pc.shape
    tokens, inner = dm.shape
    groups = inner // GROUP
    lag = depth - 1
    taps, channels = w.shape
    out = lambda i: jnp.maximum(i - lag, 0)
    inside = lambda i: jnp.minimum(out(i), groups - 1)
    wide = pl.BlockSpec((tokens, GROUP), lambda i: (0, inside(i)))
    states = pl.BlockSpec((seqs, LANES, GROUP), lambda i: (0, 0, inside(i)))
    line = lambda n: pl.BlockSpec((n, GROUP), lambda i: (0, inside(i)))
    conv = lambda n: pl.BlockSpec((n, GROUP), lambda i: (0, out(i)))
    ahead = lambda n: pl.BlockSpec((n, 2 * GROUP), lambda i: (0, jnp.minimum(i, groups // 2 - 1)))
    once = lambda v: pl.BlockSpec(v.shape, lambda i: (0,) * v.ndim, pipeline_mode=pl.Buffered(1))
    anywhere = pl.BlockSpec(memory_space=pl.ANY)
    chunks = tokens // CHUNK
    shape, dma = jax.ShapeDtypeStruct, pltpu.SemaphoreType.DMA
    a_rows, b_rows = normed_t.shape[1] // depth, turned.shape[1] // depth
    a_cols, b_cols = dz.shape[1], cot.shape[1]
    half = lambda v: (4,) + v.shape[1:]
    sends, receives = Scatter.sems(depth)
    buffers = []
    for n in range(len(PIECES)):
        for rows_of, cols_of in ((a_rows, a_cols), (b_rows, b_cols)):
            lo, hi = piece_of(cols_of, n)
            buffers += Scatter.scratch(depth, rows_of, hi - lo)
    link = pltpu.VMEM((groups, seqs, LANES, GROUP), BF16)
    square = pltpu.VMEM((chunks, CHUNK, CHUNK), F32)
    column = pltpu.VMEM((tokens, LANES), F32)
    return pl.pallas_call(
        functools.partial(scan_backward_kernel, depth, head_dim, groups),
        grid=(groups + 1 + lag,),
        in_specs=[
            pl.BlockSpec((seqs, rows, GROUP), lambda i: (0, 0, out(i))),
            conv(taps),
            conv(1),
            pl.BlockSpec(
                (seqs, rows, LANES), lambda i: (0, 0, cols // LANES - 1), pipeline_mode=pl.Buffered(1)
            ),
            whole((1, LANES)), whole((1, LANES)),
            once(bc), once(dt), once(cum), once(cumt),
            ahead(tokens), wide, wide, states, states, states, ahead(8), line(1),
            once(normed_t), once(dz), once(turned), once(cot),
        ],
        out_specs=[
            anywhere, conv(taps), conv(1), whole((3, LANES)),
            whole((a_rows, a_cols)), whole((b_rows, b_cols)), anywhere,
        ],
        out_shape=[
            shape((tokens, cols), BF16),
            shape((taps, channels), F32),
            shape((1, channels), F32),
            shape((3, LANES), F32),
            shape((a_rows, a_cols), F32),
            shape((b_rows, b_cols), F32),
            shape(half(normed_t), BF16),
        ],
        scratch_shapes=[
            square, pltpu.VMEM((chunks, LANES, CHUNK), F32), square, column, column, column, column,
            pltpu.VMEM((8, LANES), F32),
            pltpu.VMEM((8, LANES), F32),
            pltpu.VMEM((tokens, cols), BF16),
            pltpu.VMEM((seqs, EDGE, channels), F32),
            pltpu.VMEM((seqs, EDGE, channels), BF16),
            pltpu.VMEM((seqs, EDGE, channels), BF16),
            pltpu.VMEM((2 * lag + 2, seqs, LANES, GROUP), F32), pltpu.VMEM((groups, 8, GROUP), F32), link, link,
            pltpu.VMEM(half(normed_t), BF16), pltpu.VMEM(dz.shape, BF16),
            pltpu.VMEM(half(turned), BF16), pltpu.VMEM(cot.shape, BF16),
            dma((groups,)), dma((groups,)), dma((2,)), dma((2,)), dma((12,)), dma((12,)), dma((2,)),
            dma((2 * len(PIECES), sends)), dma((2 * len(PIECES), receives)),
            *buffers,
        ],
        compiler_params=pltpu.CompilerParams(
            dimension_semantics=("arbitrary",), collective_id=1, has_side_effects=True,
            vmem_limit_bytes=VMEM_LIMIT,
        ),
        name="scan_backward_sums",
    )(
        pc, w, b, pc, sb, dl, bc, dt, cum, cumt, dm, dm, mixed, s0, s1, s2, tot, skip,
        normed_t, dz, turned, cot,
    )


def scatter_last_kernel(
    depth, splits, nt_ref, nt_pair, dc_ref, dz_ref, wg_src, wc_src, x_ref, cot_ref, gain_ref,
    ggain_ref, gb_ref, gw_ref, hsum_ref, c_out, gi_ref, small_out, *refs,
):
    place = Place(depth)
    place.meet()
    pieces = len(splits) - 1
    dc_pairs, refs = refs[:pieces], refs[pieces:]
    small_src, tiles_ref, tile_sem, pair_send, pair_recv, send, recv, small_send, small_recv = refs[:9]
    refs = refs[9:]
    cuts = [dc_ref.at[:, pl.ds(lo, hi - lo)] for lo, hi in zip(splits, splits[1:])]
    copies = pair_copies(place, (), tuple(zip(cuts, dc_pairs)), pair_send, pair_recv)
    for copy in copies:
        copy.start()
    lanes = [
        Scatter(place, nt_ref, nt_pair, cut, pair, *(("y", "x") if n % 2 == 0 else ("x", "y")),
                refs[7 * n : 7 * n + 7], send.at[n], recv.at[n])
        for n, (cut, pair) in enumerate(zip(cuts, dc_pairs))
    ]
    small = SmallScatter(place, small_src, *refs[7 * pieces :], small_send, small_recv)
    tile = tiles_ref.shape[2]
    tokens = x_ref.shape[0]

    def d_normed(src, grad_ref, first, start=0, count=None):
        count = src.shape[1] // tile if count is None else count

        def fetch(i, slot):
            cols = pl.ds(pl.multiple_of(i * tile, LANES), tile)
            return pltpu.make_async_copy(src.at[:, cols], tiles_ref.at[slot], tile_sem.at[slot])

        fetch(start, start % 2).start()

        def one(i, carry):
            slot = lax.rem(i, 2)
            pl.when(i + 1 < count)(lambda: fetch(i + 1, 1 - slot).start())
            fetch(i, slot).wait()
            cols = pl.ds(pl.multiple_of(i * tile, LANES), tile)
            for r in range(0, tokens, 2 * CHUNK):
                rows = slice(r, r + 2 * CHUNK)
                part = nt(grad_ref[rows, cols], tiles_ref[slot])
                if first:

                    @pl.when(i == 0)
                    def _():
                        gi_ref[rows] = part

                    @pl.when(i > 0)
                    def _():
                        gi_ref[rows] += part
                else:
                    gi_ref[rows] += part
            return carry

        lax.fori_loop(start, count, one, 0)

    def input_grad():
        gain = gain_ref[...]
        size = 64

        def one(i, total):
            rows = pl.ds(pl.multiple_of(i * size, size), size)
            d = gi_ref[rows, :]
            values = x_ref[rows, :].astype(F32)
            scale = lax.rsqrt(jnp.mean(values * values, axis=1, keepdims=True) + EPS)
            hat = values * scale
            weighted = d * gain
            pull = jnp.mean(weighted * hat, axis=1, keepdims=True)
            gi_ref[rows, :] = scale * (weighted - hat * pull) + cot_ref[rows, :].astype(F32)
            return total + jnp.sum(d * hat, axis=0, keepdims=True)

        grad_gain = lax.fori_loop(0, tokens // size, one, jnp.zeros(gain.shape, F32))
        small_src[...] = jnp.zeros_like(small_src)
        taps = gw_ref.shape[0]
        shares = ((0, grad_gain), (1, ggain_ref[...]), (2, gb_ref[...]), (3, gw_ref[...]))
        heads = hsum_ref[:, : LANES // 2]
        for n in range(8 * depth):
            at = (n // depth // 4, n // depth // 2 % 2, n // depth % 2, n % depth)
            for row, value in shares:
                own = value.shape[1] // (8 * depth)
                where = (*at, slice(row, row + value.shape[0]), slice(0, own))
                small_src[where] = value[:, n * own : (n + 1) * own]
            small_src[(*at, slice(0, 1), slice(LANES // 2, LANES))] = heads[0:1]
            small_src[(*at, slice(3 + taps, 4 + taps), slice(0, LANES // 2))] = heads[1:2]
            small_src[(*at, slice(3 + taps, 4 + taps), slice(LANES // 2, LANES))] = heads[2:3]

    def run(first, name, *rest):
        for lane in lanes[first : first + 2]:
            getattr(lane, name)(*rest)

    for copy in copies[:2]:
        copy.wait_recv()
    run(0, "send_second", 0)
    run(0, "send_second", 1)
    for copy in copies[2:]:
        copy.wait_recv()
    run(2, "send_second", 0)
    run(2, "send_second", 1)
    d_normed(wg_src, dz_ref, True)
    run(0, "send_first")
    run(4, "send_second", 0)
    run(4, "send_second", 1)
    middle = wc_src.shape[1] // tile // 2
    d_normed(wc_src, dc_ref, False, 0, middle)
    run(0, "hold")
    run(2, "send_first")
    d_normed(wc_src, dc_ref, False, middle)
    run(2, "hold")
    run(0, "step", depth - 1)
    run(4, "send_first")
    input_grad()
    small.stage(0)
    run(0, "step", depth - 2)
    run(2, "step", depth - 1)
    run(4, "hold")
    small.stage(1)
    rounds = [[] for _ in range(depth + 3)]
    for n in range(depth):
        for first, start in ((0, -2), (2, -1), (4, 0)):
            if start + n >= 0:
                rounds[start + n].append((first, depth - 1 - n))
    for n, items in enumerate(rounds):
        for first, k in items:
            run(first, "step", k)
        if n < 2:
            small.stage(2 + n)
        elif n - 2 < depth:
            small.sums.step(depth - 1 - (n - 2))
    for lane, lo, hi in zip(lanes, splits, splits[1:]):
        c_out[:, lo:hi] = lane.keep[place.z]
    small_out[...] = small.keep[place.z]
    for lane in lanes:
        lane.finish()
    small.finish()
    for copy in copies:
        copy.wait_send()


def scatter_last(normed_t, nt_pair, dc, dz, wg, wc, x, cot, gain, ggain, gb, gw, hsum, depth):
    shape = jax.ShapeDtypeStruct
    vmem, dma = pl.BlockSpec(memory_space=pltpu.VMEM), pltpu.SemaphoreType.DMA
    anywhere = pl.BlockSpec(memory_space=pl.ANY)
    sends, receives = Scatter.sems(depth)
    rows = normed_t.shape[1] // depth
    tokens, width = dc.shape
    blocks = width // LANES
    parts = [share for share in PIECES for _ in (0, 1)]
    splits = tuple(LANES * (blocks * sum(parts[:n]) // sum(parts)) for n in range(len(parts) + 1))
    small_shape = (8, LANES)
    small_sends, small_receives = SmallScatter.sems(depth)
    sizes = [hi - lo for lo, hi in zip(splits, splits[1:])]
    scratch = []
    for size in sizes:
        scratch += Scatter.scratch(depth, rows, size)
    return pl.pallas_call(
        functools.partial(scatter_last_kernel, depth, splits),
        in_specs=[vmem, vmem, vmem, vmem, anywhere, anywhere] + [vmem] * 7,
        out_specs=[vmem] * 3,
        out_shape=[shape((rows, width), F32), shape((tokens, x.shape[1]), F32), shape(small_shape, F32)],
        scratch_shapes=[
            *(pltpu.VMEM((tokens, size), BF16) for size in sizes),
            pltpu.VMEM((2, 2, 2, depth) + small_shape, F32),
            pltpu.VMEM((2, wg.shape[0], 3 * LANES), BF16),
            dma((2,)), dma((6,)), dma((6,)), dma((6, sends)), dma((6, receives)),
            dma((small_sends,)), dma((small_receives,)),
            *scratch,
            *SmallScatter.scratch(depth, small_shape),
        ],
        compiler_params=pltpu.CompilerParams(
            collective_id=2, has_side_effects=True, vmem_limit_bytes=VMEM_LIMIT
        ),
        name="scatter_last",
    )(normed_t, nt_pair, dc, dz, wg, wc, x, cot, gain, ggain, gb, gw, hsum)


def passed_along(value, axis, steps):
    count = lax.axis_size(axis)
    initial, last = (max(0, -steps), min(count, count - steps))
    return lax.ppermute(value, axis, [(source, source + steps) for source in range(initial, last)])


def prefix(total, local, axis, backward):
    count, here = lax.axis_size(axis), lax.axis_index(axis)
    totals = lax.all_gather(total.astype(BF16), axis)
    locals_ = lax.all_gather(local, axis)
    state = jnp.zeros(local.shape, F32)
    order = range(count - 1, 0, -1) if backward else range(count - 1)
    for lap in order:
        new = totals[lap].astype(F32) * state + locals_[lap].astype(F32)
        reached = lap > here if backward else lap < here
        state = jnp.where(reached, new, state)
    leaves = total * state + local.astype(F32)
    return state.astype(BF16), leaves.astype(BF16)


AXES = ("dp", "ctx")


def body(
    inputs, gain_in, in_weight, conv_weight, conv_bias, step_bias, decay_log, skip_gain, gain_out,
    out_weight, cotangent,
):
    seqs, seg, width = inputs.shape
    tokens = seqs * seg
    count = lax.axis_size(AXES)
    dp, depth = lax.axis_size("dp"), lax.axis_size("ctx")
    own_links = dp == 8 and depth == 4
    inner = out_weight.shape[0] * count
    taps, channels = conv_weight.shape[0], conv_weight.shape[1] * count
    num_heads = step_bias.shape[0]
    head_dim = inner // num_heads
    a, b, c = gain_in.shape[0], gain_out.shape[0], conv_bias.shape[0]

    w_gate = in_weight[:, :inner]
    w_conv = in_weight[:, inner:]
    spare = -w_conv.shape[1] % LANES
    w_conv = jnp.pad(w_conv, ((0, 0), (0, spare)))
    rest = jnp.concatenate([gain_out, conv_bias, conv_weight.reshape(-1)])
    ends = taps - 1
    flat = inputs.reshape(tokens, width)
    cot = cotangent.reshape(tokens, width)

    if own_links:
        group = 2 * depth * a
        at = lax.rem(lax.axis_index("dp"), 2) * depth + lax.axis_index("ctx")
        head = lax.dynamic_update_slice(jnp.zeros((group,), F32), gain_in.astype(F32), (at * a,))
        small = jnp.concatenate([head, rest.astype(F32)])
        small = jnp.pad(small, (0, 8 * LANES - small.size)).reshape(8, LANES)
        pc, normed_ext, normed_t, small, w_conv, gate_line = gather_project(
            inputs, small, w_conv, w_gate, depth
        )
        w_conv = w_conv.reshape(width, -1)
        small = small.reshape(4, 2 * depth, 8 * LANES)
        g_in = small[:, :, :group].sum(axis=1).reshape(1, width)
        rest = small[:, :, group:].reshape(count, -1)
    else:
        before = passed_along(inputs[:, seg - EDGE :], "ctx", 1)
        ext = jnp.concatenate([before, inputs], axis=1).astype(F32)
        scale_ext = lax.rsqrt(jnp.mean(ext * ext, axis=-1, keepdims=True) + EPS)
        small = lax.all_gather(jnp.concatenate([gain_in, rest]), AXES).astype(F32)
        w_conv = lax.all_gather(w_conv, AXES, axis=0, tiled=True)
        w_gate = lax.all_gather(w_gate, AXES, axis=0, tiled=True)
        w_out = lax.all_gather(out_weight, AXES, axis=0, tiled=True)
        g_in, rest = small[:, :a].reshape(1, width), small[:, a:]
        normed_ext = (ext * scale_ext * g_in).astype(BF16)
        pc = dot(normed_ext.reshape(-1, width), w_conv).reshape(seqs, seg + EDGE, -1)
    g_out = rest[:, :b].reshape(1, inner)
    bias = rest[:, b : b + c].reshape(1, channels)
    kernel = rest[:, b + c : b + c + taps * c].reshape(count, taps, c).transpose(1, 0, 2)
    kernel = kernel.reshape(taps, channels)
    pad_head = lambda v: jnp.pad(v, (0, LANES - num_heads)).reshape(1, LANES)
    sb, dl = pad_head(step_bias), pad_head(decay_log)
    skip = jnp.repeat(skip_gain, head_dim).reshape(1, inner)

    if own_links:
        bc, dt, cum, cumt, mixed, s0, s1, s2, tot, z, dno, w_gate, w_out = scan_forward(
            pc, kernel, bias, sb, dl, skip, normed_ext, cot, gate_line, out_weight, inner, head_dim, depth
        )
        w_gate = w_gate.reshape(width, inner)
        w_out = w_out.reshape(inner, width)
        per_seq = tot[tokens // CHUNK : tokens // CHUNK + seqs][:, None, :]
    else:
        x, bc, dt, cum, cumt, loc0, local, tot = fwd_a(pc, kernel, bias, sb, dl, inner, head_dim)
        per_seq = tot[tokens // CHUNK : tokens // CHUNK + seqs][:, None, :]
        s0, s2 = prefix(per_seq, local, "ctx", False)
        mixed, s1 = fwd_b(x, bc, dt, cum, cumt, s0, loc0, tot, skip, head_dim)
        z = dot(normed_ext[:, EDGE:].reshape(tokens, width), w_gate)
        dno = nt(cot, w_out)

    turned, output, d_mixed, d_gate, grad_gain_out = mid(z, dno, mixed, w_out, g_out, flat, 8)
    if own_links:
        (
            d_conv, grad_kernel, grad_bias, head_sums, grad_gate_weight, grad_out_weight, nt_pair
        ) = scan_backward(
            pc, kernel, bias, sb, dl, bc, dt, cum, cumt, d_mixed, mixed, s0, s1, s2, tot, skip,
            normed_t, d_gate, turned, cot, head_dim, depth,
        )
    else:
        scatter = lambda v: lax.psum_scatter(v.astype(BF16), AXES, scatter_dimension=0, tiled=True).astype(F32)
        normed = normed_ext[:, EDGE:].reshape(tokens, width)
        grad_out_weight = scatter(dot(turned.reshape(inner, tokens), cot))
        grad_gate_weight = scatter(dot(normed, d_gate, ((0,), (0,))))
        adjoint = bwd_a(d_mixed, bc, cum, tot, seqs, head_dim)
        g, _ = prefix(per_seq, adjoint, "ctx", True)
        d_conv, tail, edge, grad_kernel, grad_bias, grad_skip, d_raw, head_sums = bwd_b(
            pc, kernel, bias, sb, dl, bc, dt, cum, cumt, d_mixed, mixed, s0, s1, s2, g, tot, skip, head_dim
        )
        after = passed_along(edge[:, EDGE - ends :].astype(BF16), "ctx", -1).astype(F32)
        tail = tail[:, EDGE - ends :] + after
        d_conv = d_conv.reshape(seqs, seg, channels).at[:, seg - ends :].set(tail.astype(BF16))
        d_conv = jnp.concatenate([d_conv.reshape(tokens, channels), d_raw.astype(BF16)], axis=1)

    real = d_conv.shape[1] - spare
    if own_links:
        grad_conv_cols, grad_input, mine = scatter_last(
            normed_t, nt_pair, d_conv, d_gate, w_gate, w_conv, flat, cot, g_in,
            grad_gain_out, grad_bias, grad_kernel, head_sums, depth,
        )
        grad_conv_cols = grad_conv_cols[:, :real]
        half = LANES // 2
        grad_gain_in, grad_step = mine[0, :a], mine[0, half : half + num_heads]
        grad_gain_out, grad_bias, grad_kernel = mine[1, :b], mine[2, :c], mine[3 : 3 + taps, :c]
        grad_decay = mine[3 + taps, :num_heads]
        grad_skip = mine[3 + taps, half : half + num_heads]
    else:
        d_normed = nt(d_gate, w_gate) + nt(d_conv, w_conv)
        values = flat.astype(F32)
        scale = lax.rsqrt(jnp.mean(values * values, axis=-1, keepdims=True) + EPS)
        hat = values * scale
        weighted = d_normed * g_in
        pull = jnp.mean(weighted * hat, axis=-1, keepdims=True)
        grad_input = scale * (weighted - hat * pull) + cot.astype(F32)
        grad_conv_cols = scatter(dot(normed, d_conv[:, :real], ((0,), (0,))))
        grad_skip = jnp.sum(grad_skip.reshape(num_heads, head_dim), axis=1)
        heads_sum = jnp.concatenate([head_sums[0, :num_heads], head_sums[1, :num_heads], grad_skip])
        by_owner = jnp.concatenate(
            [
                jnp.sum(d_normed * hat, axis=0).reshape(count, a),
                grad_gain_out.reshape(count, b),
                grad_bias.reshape(count, c),
                grad_kernel.reshape(taps, count, c).transpose(1, 0, 2).reshape(count, taps * c),
                jnp.broadcast_to(heads_sum, (count, 3 * num_heads)),
            ],
            axis=1,
        )
        mine = lax.dynamic_index_in_dim(lax.psum(by_owner, AXES), lax.axis_index(AXES), 0, False)
        cuts = [0, a, a + b, a + b + c, a + b + c + taps * c]
        cuts += [cuts[-1] + n * num_heads for n in (1, 2, 3)]
        parts = [mine[lo:hi] for lo, hi in zip(cuts, cuts[1:])]
        grad_gain_in, grad_gain_out, grad_bias, grad_kernel, grad_step, grad_decay, grad_skip = parts
    return (
        output.reshape(seqs, seg, width),
        grad_input.reshape(seqs, seg, width),
        grad_gain_in,
        jnp.concatenate([grad_gate_weight, grad_conv_cols], axis=1),
        grad_kernel.reshape(taps, c),
        grad_bias,
        grad_step,
        grad_decay,
        grad_skip,
        grad_gain_out,
        grad_out_weight,
    )


def solution(mesh):
    rows, cols, both = P("dp", "ctx", None), P(AXES, None), P(AXES)
    return jax.shard_map(
        body,
        mesh=mesh,
        in_specs=(rows, both, cols, P(None, AXES), both, P(), P(), P(), both, cols, rows),
        out_specs=(rows, rows, both, cols, P(None, AXES), both, P(), P(), P(), both, cols),
        check_vma=False,
    )
```

```python
import functools

import jax
import jax.numpy as jnp
from jax import lax
from jax.experimental import pallas as pl
from jax.experimental.pallas import tpu as pltpu
from jax.sharding import PartitionSpec as P

EPS = 1e-05
LOG2E = 1.4426950408889634
HIGH = lax.Precision.HIGHEST
F32 = jnp.float32
BF16 = jnp.bfloat16
CHUNK = 128
GROUP = 256
EDGE = 16
LANES = 128
VMEM_LIMIT = 62 * 1024 * 1024


def dot(a, b, dims=((1,), (0,))):
    return lax.dot_general(a, b, (dims, ((), ())), preferred_element_type=F32)


def nt(a, b):
    return dot(a, b, ((1,), (1,)))


def params():
    return pltpu.CompilerParams(
        dimension_semantics=("arbitrary",), vmem_limit_bytes=VMEM_LIMIT
    )


def whole(shape):
    return pl.BlockSpec(shape, lambda i: (0,) * len(shape))


def sigmoid(v):
    return 1.0 / (1.0 + jnp.exp(-v))


def softplus(v):
    return jnp.maximum(v, 0.0) + jnp.log1p(jnp.exp(-jnp.abs(v)))


def causal_conv(ext, w, b, seg):
    taps = w.shape[0]
    total = b
    for k in range(taps):
        at = EDGE - (taps - 1) + k
        total = total + w[k : k + 1] * ext[at : at + seg]
    return total


def lane_shift(value, lanes):
    return pltpu.roll(value, lax.rem(LANES - lanes, LANES), 1)


def head_rows(ref, first):
    base = pl.multiple_of(first // 8 * 8, 8)
    return pltpu.roll(ref[pl.ds(base, 8), :], lax.rem(8 - lax.rem(first, 8), 8), 0)


def spread(cols, at, head_dim):
    rows = cols.shape[0]
    lane = lax.broadcasted_iota(jnp.int32, (rows, LANES), 1)
    first = jnp.broadcast_to(cols[:, at : at + 1], (rows, LANES))
    second = jnp.broadcast_to(cols[:, at + 1 : at + 2], (rows, LANES))
    return jnp.where(lane < head_dim, first, second)


def spread_all(cols, heads, head_dim):
    return jnp.concatenate([spread(cols, j, head_dim) for j in range(0, heads, 2)], axis=1)


def skip_row(ref, first, heads, head_dim):
    value = lane_shift(jnp.broadcast_to(ref[...], (8, LANES)), first)
    return spread_all(value, heads, head_dim)[0:1]


def block_diagonal(pair, head_dim):
    lane = lax.broadcasted_iota(jnp.int32, pair.shape, 1)
    zero = jnp.zeros_like(pair)
    return jnp.concatenate(
        [jnp.where(lane < head_dim, pair, zero), jnp.where(lane < head_dim, zero, pair)], axis=0
    )


MESH = pl.DeviceIdType.MESH


class Place:
    def __init__(self, depth):
        dp, z = lax.axis_index("dp"), lax.axis_index("ctx")
        self.depth, self.z = depth, z
        self.own = {"y": lax.div(dp, 4), "x": lax.rem(lax.div(dp, 2), 2), "c": lax.rem(dp, 2)}
        self.to = {
            name: {"dp": dp + step * (1 - 2 * self.own[name])}
            for name, step in (("y", 4), ("x", 2), ("c", 1))
        }
        self.has_left, self.has_right = z > 0, z < depth - 1
        self.left, self.right = {"ctx": z - 1}, {"ctx": z + 1}

    def flipped(self, *names):
        return {n: 1 - v if n in names else v for n, v in self.own.items()}

    def near(self, k):
        z, last = self.z, self.depth - 1
        reach = jnp.minimum(z, last - z)
        pair = jnp.where(k % 2 == 1, z - (k + 1) // 2, z + k // 2)
        alone = jnp.where(z > last - z, last - k, k)
        return z if k == 0 else jnp.where(k <= 2 * reach, pair, alone)

    def meet(self):
        barrier = pltpu.get_barrier_semaphore()
        signal = functools.partial(pl.semaphore_signal, barrier, inc=1, device_id_type=MESH)
        for name in ("y", "x", "c"):
            signal(device_id=self.to[name])
        pl.when(self.has_left)(lambda: signal(device_id=self.left))
        pl.when(self.has_right)(lambda: signal(device_id=self.right))
        ends = self.has_left.astype(jnp.int32) + self.has_right.astype(jnp.int32)
        pl.semaphore_wait(barrier, 3 + ends)


def remote(src, dst, send, recv, to):
    return pltpu.make_async_remote_copy(
        src_ref=src, dst_ref=dst, send_sem=send, recv_sem=recv, device_id=to, device_id_type=MESH
    )


class Gather:
    def __init__(self, place, src, line, first, second, send, recv, part=()):
        self.place, self.src, self.line_of, self.part = place, src, line, part
        self.first, self.second, self.send, self.recv = first, second, send, recv

    @staticmethod
    def sems(depth):
        return 6 * depth + 3, 5 * depth + 3

    def flips(self, g):
        return ((), (self.first,), (self.second,), (self.first, self.second))[g]

    def slot(self, k, *flips):
        return self.line_of(**self.place.flipped(*flips)).at[(self.place.near(k), *self.part)]

    def copy(self, k, where, to, send, recv):
        src = self.src if k == 0 and where == () else self.slot(k, *where)
        return remote(src, self.slot(k, *where), self.send.at[send], self.recv.at[recv], to)

    def along(self, k, right):
        p = self.place
        return self.copy(k, (), p.right if right else p.left, int(right) * p.depth + k, p.near(k))

    def goes(self, k, right):
        p, at = self.place, self.place.near(k)
        if right:
            return p.has_right if k == 0 else p.has_right & (at < p.z)
        return p.has_left if k == 0 else p.has_left & (at > p.z)

    def to_axis(self, k, stage, there=False):
        p, depth = self.place, self.place.depth
        f, s = self.first, self.second
        where = ((), (), (f,), (f, s))[stage]
        axis = (f, s, s, "c")[stage]
        if there:
            where = where + (axis,)
        return self.copy(k, where, p.to[axis], (2 + stage) * depth + k, (1 + stage) * depth + k)

    def to_core(self, g, there=False):
        depth = self.place.depth
        flips = self.flips(g) + (("c",) if there else ())
        line = self.line_of(**self.place.flipped(*flips)).at[(pl.ds(0, depth), *self.part)]
        return remote(line, line, self.send.at[6 * depth + g], self.recv.at[5 * depth + g], self.place.to["c"])

    def line(self, k):
        if k:
            self.along(k, True).wait_recv()
        for right in (True, False):
            pl.when(self.goes(k, right))(lambda: self.along(k, right).start())
        for stage in (0, 1):
            self.to_axis(k, stage).start()

    def from_first(self, k):
        self.to_axis(k, 0, True).wait_recv()
        self.to_axis(k, 2).start()

    def from_second(self, k):
        self.to_axis(k, 1, True).wait_recv()

    def from_both(self, k):
        self.to_axis(k, 2, True).wait_recv()
        self.to_axis(k, 3).start()

    def core(self, g):
        self.to_core(g).start()

    def whole(self, g):
        if g < 3:
            self.to_core(g, True).wait_recv()
        else:
            for k in range(self.place.depth):
                self.to_axis(k, 3, True).wait_recv()

    def finish(self):
        for k in range(self.place.depth):
            for right in (True, False):
                pl.when(self.goes(k, right))(lambda: self.along(k, right).wait_send())
            for stage in range(4):
                self.to_axis(k, stage).wait_send()
        for g in range(3):
            self.to_core(g).wait_send()


class LineGather(Gather):
    def copy(self, k, where, to, send, recv):
        src = self.src.at[self.place.near(k)] if where == () else self.slot(k, *where)
        return remote(src, self.slot(k, *where), self.send.at[send], self.recv.at[recv], to)

    def line(self, k):
        for stage in (0, 1):
            self.to_axis(k, stage).start()

    def finish(self):
        for k in range(self.place.depth):
            for stage in range(4):
                self.to_axis(k, stage).wait_send()
        for g in range(3):
            self.to_core(g).wait_send()


class OwnLine(Gather):
    def __init__(self, place, src, line, send, recv):
        super().__init__(place, src, lambda y, x, c: line, "y", "x", send, recv)

    def line(self, k):
        if k:
            self.along(k, True).wait_recv()
        for right in (True, False):
            pl.when(self.goes(k, right))(lambda: self.along(k, right).start())

    def finish(self):
        for k in range(self.place.depth):
            for right in (True, False):
                pl.when(self.goes(k, right))(lambda: self.along(k, right).wait_send())


class Line:
    def __init__(self, place, keep, sent, came, send, recv):
        self.place, self.keep, self.sent, self.came = place, keep, sent, came
        self.send, self.recv = send, recv

    def copy(self, k, to, at):
        zk = self.place.near(k)
        return remote(self.sent.at[zk], self.came.at[at], self.send.at[k], self.recv.at[at], to)

    def take(self, at):
        self.copy(1, self.place.left, at).wait_recv()
        zk = jnp.where(at == self.place.depth, self.place.z, at)
        self.keep[zk] = self.keep[zk] + self.came[at].astype(F32)

    def moves(self, k):
        p, zk = self.place, self.place.near(k)
        return (
            (zk < p.z, p.left, zk),
            (zk > p.z, p.right, jnp.where(zk == p.z + 1, p.depth, zk)),
        )

    def step(self, k):
        p, zk = self.place, self.place.near(k)
        if k == 0:
            pl.when(p.has_right)(lambda: self.take(p.z))
            pl.when(p.has_left)(lambda: self.take(p.depth))
            return
        farther = ((zk < p.z) & p.has_right) | ((zk > p.z) & p.has_left)
        pl.when(farther)(lambda: self.take(zk))
        self.sent[zk] = self.keep[zk].astype(self.sent.dtype)
        for goes, to, at in self.moves(k):
            pl.when(goes)(lambda: self.copy(k, to, at).start())

    def finish(self):
        for k in range(1, self.place.depth):
            for goes, to, at in self.moves(k):
                pl.when(goes)(lambda: self.copy(k, to, at).wait_send())


class Scatter:
    def __init__(self, place, lhs, lhs_pair, rhs, rhs_pair, first, second, bufs, send, recv):
        self.place, self.lhs, self.lhs_pair, self.rhs, self.rhs_pair = place, lhs, lhs_pair, rhs, rhs_pair
        self.first, self.second, self.send, self.recv = first, second, send, recv
        self.s_sent, self.s_came, self.f_sent, self.f_came, self.keep, z_sent, z_came = bufs
        depth = place.depth
        self.sums = Line(place, self.keep, z_sent, z_came, send.at[pl.ds(2 + depth, depth)],
                         recv.at[pl.ds(2 + depth, depth + 1)])

    @staticmethod
    def sems(depth):
        return 2 + 2 * depth, 3 + 2 * depth

    @staticmethod
    def scratch(depth, rows, cols):
        block = lambda *lead: pltpu.VMEM(lead + (rows, cols), BF16)
        return [
            block(2, depth), block(2, depth), block(depth), block(depth),
            pltpu.VMEM((depth, rows, cols), F32), block(depth), block(depth + 1),
        ]

    def product(self, flips, store):
        at = self.place.flipped(*flips)
        pair = 2 * at["y"] + at["x"]
        one = 2 * pair + at["c"]
        rows, cols = self.keep.shape[1:]
        tile = 512

        def block(start, size):
            lanes = pl.ds(start, size)
            part = dot(self.lhs[one], self.rhs[:, lanes]) + dot(self.lhs_pair[pair], self.rhs_pair[:, lanes])
            for z in range(self.place.depth):
                store(z, lanes, part[z * rows : (z + 1) * rows])

        def loop(i, carry):
            block(pl.multiple_of(i * tile, tile), tile)
            return carry

        lax.fori_loop(0, cols // tile, loop, 0)
        if cols % tile:
            block(cols // tile * tile, cols % tile)

    def to_second(self, j):
        return remote(self.s_sent.at[j], self.s_came.at[j], self.send.at[j], self.recv.at[j],
                      self.place.to[self.second])

    def to_first(self, k):
        zk, n = self.place.near(k), 2 + k
        return remote(self.f_sent.at[zk], self.f_came.at[zk], self.send.at[n], self.recv.at[n],
                      self.place.to[self.first])

    def waves(self):
        return range(self.place.depth - 1, -1, -1)

    def send_second(self, j):
        def store(z, lanes, part):
            self.s_sent[j, z, :, lanes] = part.astype(BF16)

        self.product((self.second, self.first) if j == 0 else (self.second,), store)
        self.to_second(j).start()

    def send_first(self):
        self.to_second(0).wait_recv()

        def store(z, lanes, part):
            self.f_sent[z, :, lanes] = (part + self.s_came[0, z, :, lanes].astype(F32)).astype(BF16)

        self.product((self.first,), store)
        for k in self.waves():
            self.to_first(k).start()

    def hold(self):
        self.to_second(1).wait_recv()

        def store(z, lanes, part):
            self.keep[z, :, lanes] = part + self.s_came[1, z, :, lanes].astype(F32)

        self.product((), store)

    def step(self, k):
        self.to_first(k).wait_recv()
        zk = self.place.near(k)
        self.keep[zk] = self.keep[zk] + self.f_came[zk].astype(F32)
        self.sums.step(k)

    def finish(self):
        for j in (0, 1):
            self.to_second(j).wait_send()
        for k in self.waves():
            self.to_first(k).wait_send()
        self.sums.finish()


class SmallScatter:
    def __init__(self, place, src, c_came, half, x_came, keep, y_came, z_sent, z_came, send, recv):
        self.place, self.src, self.c_came, self.half = place, src, c_came, half
        self.x_came, self.keep, self.y_came = x_came, keep, y_came
        self.send, self.recv = send, recv
        depth = place.depth
        self.sums = Line(place, keep, z_sent, z_came, send.at[pl.ds(7, depth)],
                         recv.at[pl.ds(7, depth + 1)])

    @staticmethod
    def sems(depth):
        return 7 + depth, 8 + depth

    @staticmethod
    def scratch(depth, shape):
        block = lambda *lead: pltpu.VMEM(lead + shape, F32)
        return [
            block(2, 2, depth), block(2, 2, depth), block(2, depth), block(depth), block(depth),
            block(depth), block(depth + 1),
        ]

    def copy(self, n):
        p, own = self.place, self.place.own
        if n < 4:
            y, x = n // 2, n % 2
            src, dst, to = self.src.at[y, x, 1 - own["c"]], self.c_came.at[y, x], "c"
        elif n < 6:
            src, dst, to = self.half.at[n - 4, 1 - own["x"]], self.x_came.at[n - 4], "x"
        else:
            src, dst, to = self.half.at[1 - own["y"], own["x"]], self.y_came, "y"
        return remote(src, dst, self.send.at[n], self.recv.at[n], p.to[to])

    def stage(self, n):
        own = self.place.own
        if n == 0:
            for i in range(4):
                self.copy(i).start()
        elif n == 1:
            for i in range(4):
                self.copy(i).wait_recv()
            for y in (0, 1):
                for x in (0, 1):
                    self.half[y, x] = self.src[y, x, own["c"]] + self.c_came[y, x]
            for i in (4, 5):
                self.copy(i).start()
        elif n == 2:
            for i in (4, 5):
                self.copy(i).wait_recv()
            for y in (0, 1):
                self.half[y, own["x"]] = self.half[y, own["x"]] + self.x_came[y]
            self.copy(6).start()
        else:
            self.copy(6).wait_recv()
            self.keep[...] = self.half[own["y"], own["x"]] + self.y_came[...]

    def finish(self):
        for n in range(7):
            self.copy(n).wait_send()
        self.sums.finish()


def gather_kernel(
    depth, half, x_ref, small_src, wc_src, wg_src, pc_ref, normed_ref, normt_ref,
    gin_ref, gout_ref, bias_ref, taps_ref, wc_out, gate_ref,
    small_ref, gain_row, hat_ref, edge_ref, wc_ref, edge_sem, own_sem, out_sem, send, recv, gate_send, gate_recv,
):
    place = Place(depth)
    place.meet()
    seqs, seg, features = x_ref.shape
    width = wc_src.shape[1]
    lo, hi = pl.ds(0, half), pl.ds(half, width - half)
    every = slice(None)
    weights = lambda y, x, c: wc_ref.at[y, x, c]
    lanes = [
        Gather(place, small_src, lambda y, x, c: small_ref.at[y, x, c], "y", "x", send.at[0], recv.at[0]),
        Gather(place, wc_src.at[:, lo], weights, "y", "x", send.at[1], recv.at[1], (every, lo)),
        Gather(place, wc_src.at[:, hi], weights, "x", "y", send.at[2], recv.at[2], (every, hi)),
    ]
    early, late = lanes[:2], lanes[2:]
    gate = OwnLine(place, wg_src, gate_ref, gate_send, gate_recv)
    own = place.own
    mine = (own["y"], own["x"], own["c"], place.z)
    copies = [
        pltpu.make_async_copy(src, dst.at[mine], own_sem.at[n])
        for n, (src, dst) in enumerate(((small_src, small_ref), (wc_src, wc_ref)))
    ]
    copies.append(pltpu.make_async_copy(wg_src, gate_ref.at[place.z], own_sem.at[2]))
    edge = remote(x_ref.at[:, pl.ds(seg - EDGE, EDGE)], edge_ref, edge_sem.at[0], edge_sem.at[1], place.right)

    def each(group, *steps):
        for name, k in steps:
            for lane in group:
                getattr(lane, name)(k)

    def keep(n):
        at = place.flipped(*((), ("y",), ("x",), ("y", "x"))[n])
        return pltpu.make_async_copy(wc_ref.at[at["y"], at["x"]], wc_out.at[at["y"], at["x"]], out_sem.at[n])

    rows = wc_src.shape[0]
    count = 2 * depth * rows

    def norm(flips):
        at = place.flipped(*flips)
        group = 2 * at["y"] + at["x"]
        here = pl.ds(pl.multiple_of(group * count, LANES), count)
        for c in (0, 1):
            for z in range(depth):
                start = (c * depth + z) * rows
                gain_row[:, start : start + rows] = small_ref[at["y"], at["x"], c, z, 0:1, :rows]
        gain = gain_row[...]
        for s in range(seqs):
            normed = (hat_ref[s, :, here] * gain).astype(BF16)
            normed_ref[s, :, here] = normed
            turned = normed[EDGE:].astype(F32).T.astype(BF16)
            for c in (0, 1):
                normt_ref[2 * group + c, :, s * seg : (s + 1) * seg] = turned[c * depth * rows : (c + 1) * depth * rows]

    def multiply(flips, n):
        at = place.flipped(*flips)
        here = pl.ds(pl.multiple_of((2 * at["y"] + at["x"]) * count, LANES), count)
        first, last = ((0, half), (half, width))[n]
        tile = 4 * LANES
        for start in range(first, last, tile):
            cols = slice(start, min(start + tile, last))
            block = jnp.concatenate(
                [wc_ref[at["y"], at["x"], c, z, :, cols] for c in (0, 1) for z in range(depth)], axis=0
            )
            for s in range(seqs):
                part = dot(normed_ref[s, :, here], block)
                if flips == ():
                    pc_ref[s, :, cols] = part
                else:
                    pc_ref[s, :, cols] += part

    each(early, ("line", 0))
    pl.when(place.has_right)(edge.start)
    for copy in copies:
        copy.start()
    pl.when(place.has_left)(edge.wait_recv)

    @pl.when(jnp.logical_not(place.has_left))
    def _():
        edge_ref[...] = jnp.zeros_like(edge_ref)

    def scale_rows(s, start, rows_in, r, step):
        values = rows_in[s, r : r + step].astype(F32)
        mean = jnp.mean(values * values, axis=1, keepdims=True)
        hat_ref[s, start + r : start + r + step] = values * lax.rsqrt(mean + EPS)

    pieces = []
    for s in range(seqs):
        pieces.append((s, 0, edge_ref, 0, EDGE))
        pieces += [(s, EDGE, x_ref, r, 64) for r in range(0, seg, 64)]
    share = -(-len(pieces) // depth)
    for k in range(depth):
        for piece in pieces[k * share : (k + 1) * share]:
            scale_rows(*piece)
        if k + 1 < depth:
            each(early, ("line", k + 1))
        if k == depth - 2:
            each(late, ("line", 0))
    for copy in copies:
        copy.wait()
    each(early, ("core", 0))
    for k in range(1, depth):
        each(late, ("line", k))
        if k == depth - 2:
            gate.line(0)
    each(late, ("core", 0))
    for k in range(depth):
        each(early, ("from_first", k), ("from_second", k))
    each(early, ("core", 1), ("core", 2))
    each(late, ("from_first", 0), ("from_first", 1))
    each(early, ("whole", 0))
    norm(())
    multiply((), 0)
    for k in range(2, depth):
        each(late, ("from_first", k))
    gate.line(1)
    each(early, ("whole", 1))
    norm(("y",))
    multiply(("y",), 0)
    for k in range(depth):
        each(late, ("from_second", k))
    each(late, ("core", 1), ("core", 2))
    each(early, ("whole", 2))
    norm(("x",))
    multiply(("x",), 0)
    gate.line(2)
    each(late, ("whole", 0))
    keep(0).start()
    multiply((), 1)
    for k in range(depth - 1):
        each(lanes, ("from_both", k))
    each(late, ("whole", 1), ("whole", 2))
    keep(1).start()
    keep(2).start()
    multiply(("y",), 1)
    gate.line(3)
    multiply(("x",), 1)
    each(lanes, ("from_both", depth - 1))
    each(early, ("whole", 3))
    norm(("y", "x"))
    multiply(("y", "x"), 0)
    each(late, ("whole", 3))
    keep(3).start()
    multiply(("y", "x"), 1)
    parts = ((gin_ref, 0), (gout_ref, 1), (bias_ref, 2), (taps_ref, 3))
    for n in range(8 * depth):
        at = (n // depth // 4, n // depth // 2 % 2, n // depth % 2, n % depth)
        for out, row in parts:
            size = out.shape[1] // (8 * depth)
            out[:, n * size : (n + 1) * size] = small_ref[(*at, slice(row, row + out.shape[0]), slice(0, size))]
    for lane in (*lanes, gate):
        lane.finish()
    for n in range(4):
        keep(n).wait()
    pl.when(place.has_right)(edge.wait_send)


def gather_project(x, small, wc, wg, inner, channels, taps, depth):
    shape = jax.ShapeDtypeStruct
    seqs, seg, features = x.shape
    slots = (2, 2, 2, depth)
    sends, receives = Gather.sems(depth)
    width = wc.shape[1]
    half = width // 2 // LANES * LANES
    anywhere, vmem = pl.BlockSpec(memory_space=pl.ANY), pl.BlockSpec(memory_space=pltpu.VMEM)
    dma = pltpu.SemaphoreType.DMA
    return pl.pallas_call(
        functools.partial(gather_kernel, depth, half),
        in_specs=[vmem, vmem, vmem, vmem],
        out_specs=[vmem] * 7 + [anywhere, vmem],
        out_shape=[
            shape((seqs, seg + EDGE, width), F32),
            shape((seqs, seg + EDGE, features), BF16),
            shape((8, depth * wc.shape[0], seqs * seg), BF16),
            shape((1, features), F32),
            shape((1, inner), F32),
            shape((1, channels), F32),
            shape((taps, channels), F32),
            shape(slots + wc.shape, BF16),
            shape((depth,) + wg.shape, BF16),
        ],
        scratch_shapes=[
            pltpu.VMEM(slots + small.shape, F32),
            pltpu.VMEM((1, 2 * depth * wc.shape[0]), F32),
            pltpu.VMEM((seqs, seg + EDGE, features), F32),
            pltpu.VMEM((seqs, EDGE, features), BF16),
            pltpu.VMEM(slots + wc.shape, BF16),
            dma((2,)), dma((3,)), dma((4,)), dma((3, sends)), dma((3, receives)),
            dma((2 * depth,)), dma((depth,)),
        ],
        compiler_params=pltpu.CompilerParams(
            collective_id=0, has_side_effects=True, vmem_limit_bytes=VMEM_LIMIT
        ),
        name="gather_project",
    )(x, small, wc, wg)


def fwd_a_kernel(
    head_dim, pc_ref, w_ref, b_ref, raw_ref, sb_ref, dl_ref,
    x_ref, bc_ref, dt_ref, cum_ref, cumt_ref, loc0_ref, seg_ref, tot_ref, bt_ref,
):
    step = pl.program_id(0)
    seqs = pc_ref.shape[0]
    seg = pc_ref.shape[1] - EDGE
    chunks = seg // CHUNK
    w, b = w_ref[...], b_ref[...]

    def acts_of(s):
        pre = causal_conv(pc_ref[s], w, b, seg)
        return pre * sigmoid(pre)

    @pl.when(step == 0)
    def _():
        row = lax.broadcasted_iota(jnp.int32, (CHUNK, CHUNK), 0)
        col = lax.broadcasted_iota(jnp.int32, (CHUNK, CHUNK), 1)
        tri = (col <= row).astype(F32)
        rate = -jnp.exp(dl_ref[...])
        for s in range(seqs):
            acts = acts_of(s)
            bc_ref[s * seg : (s + 1) * seg] = acts
            for c in range(chunks):
                q = s * chunks + c
                rows = slice(q * CHUNK, (q + 1) * CHUNK)
                bt_ref[q] = acts[c * CHUNK : (c + 1) * CHUNK, :LANES].T.astype(BF16)
                dt = softplus(raw_ref[s, EDGE + c * CHUNK : EDGE + (c + 1) * CHUNK] + sb_ref[...])
                cum = LOG2E * jnp.dot(tri, dt * rate, precision=HIGH, preferred_element_type=F32)
                dt_ref[rows] = dt
                cum_ref[rows] = cum
                cumt_ref[:, rows] = cum.T

    @pl.when(step > 0)
    def _():
        heads = GROUP // head_dim
        first = (step - 1) * heads
        cumg = lane_shift(cum_ref[...], first)
        dtg = lane_shift(dt_ref[...], first)
        for s in range(seqs):
            x = acts_of(s)
            x_ref[s * seg : (s + 1) * seg] = x
            state, total = None, None
            for c in range(chunks):
                q = s * chunks + c
                rows = slice(q * CHUNK, (q + 1) * CHUNK)
                ce = spread_all(cumg[rows], heads, head_dim)
                de = spread_all(dtg[rows], heads, head_dim)
                end = ce[CHUNK - 1 : CHUNK]
                uw = x[c * CHUNK : (c + 1) * CHUNK] * de * jnp.exp2(end - ce)
                loc = dot(bt_ref[q], uw.astype(BF16))
                tot = jnp.exp2(end)
                tot_ref[q : q + 1] = tot
                if c == 0:
                    loc0_ref[s] = loc
                    state, total = loc, tot
                else:
                    state, total = tot * state + loc, tot * total
            seg_ref[s] = state.astype(BF16)
            tot_ref[seqs * chunks + s : seqs * chunks + s + 1] = total


def fwd_a(pc, w, b, sb, dl, inner, head_dim):
    seqs, rows, cols = pc.shape
    seg = rows - EDGE
    tokens = seqs * seg
    groups = inner // GROUP
    state = LANES
    chunks = tokens // CHUNK
    at = lambda i: (i + groups) % (groups + 1)
    back = lambda i: jnp.maximum(i - 1, 0)
    return pl.pallas_call(
        functools.partial(fwd_a_kernel, head_dim),
        grid=(groups + 1,),
        in_specs=[
            pl.BlockSpec((seqs, rows, GROUP), lambda i: (0, 0, at(i))),
            pl.BlockSpec((w.shape[0], GROUP), lambda i: (0, at(i))),
            pl.BlockSpec((1, GROUP), lambda i: (0, at(i))),
            pl.BlockSpec((seqs, rows, LANES), lambda i: (0, 0, cols // LANES - 1)),
            whole((1, LANES)),
            whole((1, LANES)),
        ],
        out_specs=[
            pl.BlockSpec((tokens, GROUP), lambda i: (0, back(i))),
            whole((tokens, GROUP)),
            whole((tokens, LANES)),
            whole((tokens, LANES)),
            whole((LANES, tokens)),
            pl.BlockSpec((seqs, state, GROUP), lambda i: (0, 0, back(i))),
            pl.BlockSpec((seqs, state, GROUP), lambda i: (0, 0, back(i))),
            pl.BlockSpec((8, GROUP), lambda i: (0, back(i))),
        ],
        out_shape=[
            jax.ShapeDtypeStruct((tokens, inner), F32),
            jax.ShapeDtypeStruct((tokens, GROUP), F32),
            jax.ShapeDtypeStruct((tokens, LANES), F32),
            jax.ShapeDtypeStruct((tokens, LANES), F32),
            jax.ShapeDtypeStruct((LANES, tokens), F32),
            jax.ShapeDtypeStruct((seqs, state, inner), F32),
            jax.ShapeDtypeStruct((seqs, state, inner), BF16),
            jax.ShapeDtypeStruct((8, inner), F32),
        ],
        scratch_shapes=[pltpu.VMEM((chunks, LANES, CHUNK), BF16)],
        compiler_params=params(),
        name="conv_states",
    )(pc, w, b, pc, sb, dl)


def fwd_b_kernel(
    head_dim, x_ref, bc_ref, dt_ref, cum_ref, cumt_ref, s0_ref, loc0_ref, tot_ref, skip_ref,
    mixed_ref, s1_ref, cb_ref,
):
    step = pl.program_id(0)
    seqs = s0_ref.shape[0]
    chunks = x_ref.shape[0] // CHUNK // seqs
    heads = GROUP // head_dim

    @pl.when(step == 0)
    def _():
        for q in range(seqs * chunks):
            rows = slice(q * CHUNK, (q + 1) * CHUNK)
            cb_ref[q] = nt(bc_ref[rows, LANES:].astype(BF16), bc_ref[rows, :LANES].astype(BF16))

    first = step * heads
    cumg = lane_shift(cum_ref[...], first)
    dtg = lane_shift(dt_ref[...], first)
    cumr = head_rows(cumt_ref, first)
    row = lax.broadcasted_iota(jnp.int32, (CHUNK, CHUNK), 0)
    col = lax.broadcasted_iota(jnp.int32, (CHUNK, CHUNK), 1)
    causal = col <= row
    skip = skip_ref[...]
    for s in range(seqs):
        start = s0_ref[s]
        for c in range(chunks):
            q = s * chunks + c
            rows = slice(q * CHUNK, (q + 1) * CHUNK)
            x = x_ref[rows]
            ce = spread_all(cumg[rows], heads, head_dim)
            de = spread_all(dtg[rows], heads, head_dim)
            ub = (x * de).astype(BF16)
            cb = cb_ref[q]
            parts = []
            for j in range(0, heads, 2):
                mats = []
                for h in (j, j + 1):
                    there = jnp.broadcast_to(cumg[rows, h : h + 1], (CHUNK, CHUNK))
                    here = cumr[h : h + 1, rows]
                    decay = jnp.exp2(jnp.where(causal, there - here, -jnp.inf))
                    mats.append((decay * cb).astype(BF16))
                pair = ub[:, j * head_dim : (j + 2) * head_dim]
                parts.append(dot(jnp.concatenate(mats, axis=1), block_diagonal(pair, head_dim)))
            y = jnp.concatenate(parts, axis=1)
            y = y + jnp.exp2(ce) * dot(bc_ref[rows, LANES:].astype(BF16), start)
            mixed_ref[rows] = y + skip * x
            if c == 0:
                start = (tot_ref[q : q + 1] * start.astype(F32) + loc0_ref[s]).astype(BF16)
                s1_ref[s] = start


def fwd_b(x, bc, dt, cum, cumt, s0, loc0, tot, skip, head_dim):
    tokens, inner = x.shape
    seqs, state, _ = s0.shape
    groups = inner // GROUP
    wide = pl.BlockSpec((tokens, GROUP), lambda i: (0, i))
    states = pl.BlockSpec((seqs, state, GROUP), lambda i: (0, 0, i))
    return pl.pallas_call(
        functools.partial(fwd_b_kernel, head_dim),
        grid=(groups,),
        in_specs=[
            wide, whole(bc.shape), whole(dt.shape), whole(cum.shape), whole(cumt.shape),
            states, states,
            pl.BlockSpec((8, GROUP), lambda i: (0, i)),
            pl.BlockSpec((1, GROUP), lambda i: (0, i)),
        ],
        out_specs=[wide, states],
        out_shape=[
            jax.ShapeDtypeStruct((tokens, inner), F32),
            jax.ShapeDtypeStruct((seqs, state, inner), BF16),
        ],
        scratch_shapes=[pltpu.VMEM((tokens // CHUNK, CHUNK, CHUNK), F32)],
        compiler_params=params(),
        name="scan_outputs",
    )(x, bc, dt, cum, cumt, s0, loc0, tot, skip)


def halves(v):
    high = v.astype(BF16)
    return high, (v - high.astype(F32)).astype(BF16)


def dot_pairs(a, b, dims=((1,), (0,))):
    (ah, al), (bh, bl) = halves(a), halves(b)
    return dot(ah, bh, dims) + (dot(al, bh, dims) + dot(ah, bl, dims))


def dot_pair(a, b, dims=((1,), (0,))):
    high, low = halves(a)
    return dot(high, b, dims) + dot(low, b, dims)


def nt_exact(a, b):
    return lax.dot_general(a, b, (((1,), (1,)), ((), ())), precision=HIGH, preferred_element_type=F32)


class Chain:
    def __init__(self, place, came, sent, send, recv, backward):
        self.came, self.sent, self.send, self.recv = came, sent, send, recv
        self.gets, self.gives = place.has_left, place.has_right
        self.to = place.left if backward else place.right
        if backward:
            self.gets, self.gives = self.gives, self.gets
        self.behind = place.depth - 1 - place.z if backward else place.z

    def copy(self, g):
        return remote(self.sent.at[g], self.came.at[g], self.send.at[g], self.recv.at[g], self.to)

    def step(self, g, total, own):
        pl.when(self.gets)(lambda: self.copy(g).wait_recv())

        @pl.when(jnp.logical_not(self.gets))
        def _():
            self.came[g] = jnp.zeros(self.came.shape[1:], self.came.dtype)

        self.sent[g] = (total * self.came[g].astype(F32) + own).astype(BF16)
        pl.when(self.gives)(lambda: self.copy(g).start())

    def finish(self):
        groups = self.came.shape[0]

        def one(g, carry):
            self.copy(g).wait_send()
            return carry

        @pl.when(self.gives)
        def _():
            lax.fori_loop(0, groups, one, 0)


def scan_forward_kernel(
    depth, head_dim, groups,
    pc_ref, w_ref, b_ref, pcb_ref, wb_ref, bb_ref, raw_ref, sb_ref, dl_ref, skip_ref, normed_ref, cot_ref,
    gate_src, wo_src,
    bc_ref, dt_ref, cum_ref, cumt_ref, mixed_ref, s0_ref, s1_ref, s2_ref, tot_ref, z_out, dno_out, wg_out, wo_out,
    bt_ref, cb_ref, x_all, loc_all, seg_ring, tot_all, came, sent,
    z_ref, dno_ref, wg_ref, wo_ref, chain_send, chain_recv, own_sem, keep_sem, out_sem, send, recv,
):
    step = pl.program_id(0)
    lag = depth - 1
    seqs = pc_ref.shape[0]
    seg = pc_ref.shape[1] - EDGE
    chunks = seg // CHUNK
    heads = GROUP // head_dim
    place = Place(depth)
    chain = Chain(place, came, sent, chain_send, chain_recv, False)
    gate = LineGather(place, gate_src, lambda y, x, c: wg_ref.at[y, x, c], "y", "x", send.at[0], recv.at[0])
    out = Gather(place, wo_src, lambda y, x, c: wo_ref.at[y, x, c], "x", "y", send.at[1], recv.at[1])
    mine = (place.own["y"], place.own["x"], place.own["c"], place.z)
    copies = [
        pltpu.make_async_copy(gate_src, wg_ref.at[mine[:3]], own_sem.at[0]),
        pltpu.make_async_copy(wo_src, wo_ref.at[mine], own_sem.at[1]),
    ]

    def waves(*steps):
        for lane, name, k in steps:
            getattr(lane, name)(k)

    def acts_of(s, refs, j=0):
        part, w, b = refs
        cols = slice(j * GROUP, (j + 1) * GROUP)
        pre = causal_conv(part[s, :, cols], w[:, cols], b[:, cols], seg)
        return pre * sigmoid(pre)

    @pl.when(step == 0)
    def _():
        place.meet()
        waves(*((gate, "line", k) for k in range(depth)))
        for copy in copies:
            copy.start()
        row = lax.broadcasted_iota(jnp.int32, (CHUNK, CHUNK), 0)
        col = lax.broadcasted_iota(jnp.int32, (CHUNK, CHUNK), 1)
        tri = (col <= row).astype(F32)
        rate = -jnp.exp(dl_ref[...])
        for s in range(seqs):
            acts = acts_of(s, (pcb_ref, wb_ref, bb_ref))
            bc_ref[s * seg : (s + 1) * seg] = acts
            for c in range(chunks):
                q = s * chunks + c
                rows = slice(q * CHUNK, (q + 1) * CHUNK)
                b_proj = acts[c * CHUNK : (c + 1) * CHUNK, :LANES]
                c_proj = acts[c * CHUNK : (c + 1) * CHUNK, LANES:]
                bt_ref[q] = b_proj.T
                cb_ref[q] = nt_exact(c_proj, b_proj)
                dt = softplus(raw_ref[s, EDGE + c * CHUNK : EDGE + (c + 1) * CHUNK] + sb_ref[...])
                cum = LOG2E * jnp.dot(tri, dt * rate, precision=HIGH, preferred_element_type=F32)
                dt_ref[rows] = dt
                cum_ref[rows] = cum
                cumt_ref[:, rows] = cum.T

    slots = seg_ring.shape[0]

    def local_states(g, j):
        first = g * heads
        cumg = lane_shift(cum_ref[...], first)
        dtg = lane_shift(dt_ref[...], first)
        for s in range(seqs):
            x = acts_of(s, (pc_ref, w_ref, b_ref), j)
            x_all[g, s * seg : (s + 1) * seg] = x
            state, total = None, None
            for c in range(chunks):
                q = s * chunks + c
                rows = slice(q * CHUNK, (q + 1) * CHUNK)
                ce = spread_all(cumg[rows], heads, head_dim)
                de = spread_all(dtg[rows], heads, head_dim)
                end = ce[CHUNK - 1 : CHUNK]
                uw = x[c * CHUNK : (c + 1) * CHUNK] * de * jnp.exp2(end - ce)
                loc = dot_pairs(bt_ref[q], uw)
                tot = jnp.exp2(end)
                tot_all[g, q : q + 1] = tot
                if c == 0:
                    loc_all[g, s] = loc
                    state, total = loc, tot
                else:
                    state, total = tot * state + loc, tot * total
            seg_ring[lax.rem(g, slots), s] = state
            tot_all[g, seqs * chunks + s : seqs * chunks + s + 1] = total

    @pl.when((step > 0) & (step <= groups // 2))
    def _():
        for j in (0, 1):
            local_states(2 * (step - 1) + j, j)

    handed = step - 1 - chain.behind

    @pl.when((handed >= 0) & (handed < groups // 2))
    def _():
        for j in (0, 1):
            g = 2 * handed + j
            totals = tot_all[g, seqs * chunks : seqs * chunks + seqs]
            chain.step(g, totals[:, None, :], seg_ring[lax.rem(g, slots)])

    @pl.when(step > lag)
    def _():
        g = step - 1 - lag
        first = g * heads
        cumg = lane_shift(cum_ref[...], first)
        dtg = lane_shift(dt_ref[...], first)
        cumr = head_rows(cumt_ref, first)
        row = lax.broadcasted_iota(jnp.int32, (CHUNK, CHUNK), 0)
        col = lax.broadcasted_iota(jnp.int32, (CHUNK, CHUNK), 1)
        causal = col <= row
        skip = skip_row(skip_ref, first, heads, head_dim)
        s0_ref[...] = came[g]
        s2_ref[...] = sent[g]
        tot_ref[...] = tot_all[g]
        for s in range(seqs):
            start = came[g, s]
            for c in range(chunks):
                q = s * chunks + c
                rows = slice(q * CHUNK, (q + 1) * CHUNK)
                x = x_all[g, rows]
                ce = spread_all(cumg[rows], heads, head_dim)
                de = spread_all(dtg[rows], heads, head_dim)
                ub = (x * de).astype(BF16)
                cb = cb_ref[q]
                parts = []
                for j in range(0, heads, 2):
                    mats = []
                    for h in (j, j + 1):
                        there = jnp.broadcast_to(cumg[rows, h : h + 1], (CHUNK, CHUNK))
                        here = cumr[h : h + 1, rows]
                        decay = jnp.exp2(jnp.where(causal, there - here, -jnp.inf))
                        mats.append((decay * cb).astype(BF16))
                    pair = ub[:, j * head_dim : (j + 2) * head_dim]
                    parts.append(dot(jnp.concatenate(mats, axis=1), block_diagonal(pair, head_dim)))
                y = jnp.concatenate(parts, axis=1)
                y = y + jnp.exp2(ce) * dot(bc_ref[rows, LANES:].astype(BF16), start)
                mixed_ref[rows] = y + skip * x
                if c == 0:
                    later = tot_all[g, q : q + 1] * start.astype(F32) + loc_all[g, s]
                    s1_ref[s] = later
                    start = later.astype(BF16)

    every = range(depth)
    by_group = ((), ("y",), ("x",), ("y", "x"))

    def both(lane, *waves_of):
        return [(lane, name, k) for k in waves_of for name in ("from_first", "from_second")]

    beside = {
        4: [(out, "line", 0), *both(gate, 0)],
        7: [(out, "line", 1), *both(gate, 1)],
        10: [(out, "line", 2)],
        13: [(out, "line", 3), (out, "core", 0)],
        14: [*both(gate, 2, 3), (gate, "core", 1), (gate, "core", 2)],
    }
    for at, steps in beside.items():
        pl.when(step == at)(lambda: waves(*steps))

    @pl.when(step == 2)
    def _():
        for copy in copies:
            copy.wait()
        waves((gate, "core", 0))

    @pl.when(step == groups + lag)
    def _():
        rows = 2 * depth * gate_src.shape[1]
        tile = 4 * LANES
        size = dno_ref.shape[1] // 8

        def keep(lane, g):
            src, dst = (wg_ref, wg_out) if lane is gate else (wo_ref, wo_out)
            at = place.flipped(*by_group[g])
            return pltpu.make_async_copy(
                src.at[at["y"], at["x"]], dst.at[at["y"], at["x"]], keep_sem.at[int(lane is out), g]
            )

        def ready(lane, g):
            lane.whole(g if g in (0, 3) or lane is gate else 3 - g)
            keep(lane, g).start()

        def group_of(g):
            at = place.flipped(*by_group[g])
            return 2 * at["y"] + at["x"]

        def gate_product(g):
            at = place.flipped(*by_group[g])
            here = pl.ds(pl.multiple_of(group_of(g) * rows, LANES), rows)
            for start in range(0, z_ref.shape[1], tile):
                cols = slice(start, start + tile)
                block = jnp.concatenate(
                    [wg_ref[at["y"], at["x"], c, z, :, cols] for c in (0, 1) for z in every], axis=0
                )
                for s in range(seqs):
                    part = dot(normed_ref[s, EDGE:, here], block)
                    at_rows = slice(s * seg, (s + 1) * seg)
                    if g == 0:
                        z_ref[at_rows, cols] = part
                    else:
                        z_ref[at_rows, cols] += part

        def out_product(g):
            at = place.flipped(*by_group[g])
            for c in (0, 1):
                block = jnp.concatenate([wo_ref[at["y"], at["x"], c, z] for z in every], axis=0)
                cols = pl.ds(pl.multiple_of((2 * group_of(g) + c) * size, LANES), size)
                dno_ref[:, cols] = nt(cot_ref[...], block)
            dno_copy(g).start()

        def dno_copy(g):
            cols = pl.ds(pl.multiple_of(group_of(g) * 2 * size, LANES), 2 * size)
            return pltpu.make_async_copy(dno_ref.at[:, cols], dno_out.at[:, cols], out_sem.at[g])

        last = depth - 1
        waves((out, "from_first", 0), (out, "from_first", 1))
        ready(gate, 0)
        gate_product(0)
        waves(*((out, "from_first", k) for k in range(2, last)))
        ready(gate, 1)
        gate_product(1)
        waves((out, "from_first", last), *((out, "from_second", k) for k in every))
        waves((out, "core", 1), (out, "core", 2))
        ready(gate, 2)
        gate_product(2)
        waves((gate, "from_both", 0), (out, "from_both", 0))
        ready(out, 0)
        out_product(0)
        waves((gate, "from_both", 1), (out, "from_both", 1))
        ready(out, 1)
        out_product(1)
        waves((gate, "from_both", 2), (out, "from_both", 2))
        ready(out, 2)
        out_product(2)
        waves((gate, "from_both", last), (out, "from_both", last))
        ready(gate, 3)
        gate_product(3)
        z_copy = pltpu.make_async_copy(z_ref, z_out, out_sem.at[4])
        z_copy.start()
        ready(out, 3)
        out_product(3)
        for lane in (gate, out):
            lane.finish()
        chain.finish()
        for g in range(4):
            dno_copy(g).wait()
            keep(gate, g).wait()
            keep(out, g).wait()
        z_copy.wait()


def scan_forward(pc, w, b, sb, dl, skip, normed, cot, gate_line, wo, inner, head_dim, depth):
    seqs, rows, cols = pc.shape
    tokens = seqs * (rows - EDGE)
    groups = inner // GROUP
    lag = depth - 1
    chunks = tokens // CHUNK
    shape, dma = jax.ShapeDtypeStruct, pltpu.SemaphoreType.DMA
    into = lambda i: jnp.clip(i - 1, 0, groups // 2 - 1)
    out = lambda i: jnp.maximum(i - 1 - lag, 0)
    states = pl.BlockSpec((seqs, LANES, GROUP), lambda i: (0, 0, out(i)))
    anywhere = pl.BlockSpec(memory_space=pl.ANY)
    sends, receives = Gather.sems(depth)
    slots = (2, 2, 2, depth)
    link = pltpu.VMEM((groups, seqs, LANES, GROUP), BF16)
    once = lambda v: pl.BlockSpec(v.shape, lambda i: (0,) * v.ndim, pipeline_mode=pl.Buffered(1))
    return pl.pallas_call(
        functools.partial(scan_forward_kernel, depth, head_dim, groups),
        grid=(groups + 1 + lag,),
        in_specs=[
            pl.BlockSpec((seqs, rows, 2 * GROUP), lambda i: (0, 0, into(i))),
            pl.BlockSpec((w.shape[0], 2 * GROUP), lambda i: (0, into(i))),
            pl.BlockSpec((1, 2 * GROUP), lambda i: (0, into(i))),
            pl.BlockSpec((seqs, rows, GROUP), lambda i: (0, 0, groups), pipeline_mode=pl.Buffered(1)),
            pl.BlockSpec((w.shape[0], GROUP), lambda i: (0, groups)),
            pl.BlockSpec((1, GROUP), lambda i: (0, groups)),
            pl.BlockSpec((seqs, rows, LANES), lambda i: (0, 0, cols // LANES - 1)),
            whole((1, LANES)),
            whole((1, LANES)),
            whole((1, LANES)),
            once(normed),
            once(cot),
            once(gate_line),
            once(wo),
        ],
        out_specs=[
            whole((tokens, GROUP)),
            whole((tokens, LANES)),
            whole((tokens, LANES)),
            whole((LANES, tokens)),
            pl.BlockSpec((tokens, GROUP), lambda i: (0, out(i))),
            states, states, states,
            pl.BlockSpec((8, GROUP), lambda i: (0, out(i))),
            anywhere,
            anywhere,
            anywhere,
            anywhere,
        ],
        out_shape=[
            shape((tokens, GROUP), F32),
            shape((tokens, LANES), F32),
            shape((tokens, LANES), F32),
            shape((LANES, tokens), F32),
            shape((tokens, inner), F32),
            shape((seqs, LANES, inner), BF16),
            shape((seqs, LANES, inner), F32),
            shape((seqs, LANES, inner), BF16),
            shape((8, inner), F32),
            shape((tokens, inner), F32),
            shape((tokens, inner), F32),
            shape(slots + gate_line.shape[1:], BF16),
            shape(slots + wo.shape, BF16),
        ],
        scratch_shapes=[
            pltpu.VMEM((chunks, LANES, CHUNK), F32),
            pltpu.VMEM((chunks, CHUNK, CHUNK), F32),
            pltpu.VMEM((groups, tokens, GROUP), F32), pltpu.VMEM((groups, seqs, LANES, GROUP), F32),
            pltpu.VMEM((2 * lag + 2, seqs, LANES, GROUP), F32), pltpu.VMEM((groups, 8, GROUP), F32),
            link, link,
            pltpu.VMEM((tokens, inner), F32), pltpu.VMEM((tokens, inner), F32),
            pltpu.VMEM(slots + gate_line.shape[1:], BF16), pltpu.VMEM(slots + wo.shape, BF16),
            dma((groups,)), dma((groups,)), dma((2,)), dma((2, 4)), dma((5,)), dma((2, sends)), dma((2, receives)),
        ],
        compiler_params=pltpu.CompilerParams(
            dimension_semantics=("arbitrary",), collective_id=3, has_side_effects=True,
            vmem_limit_bytes=VMEM_LIMIT,
        ),
        name="scan_forward",
    )(pc, w, b, pc, w, b, pc, sb, dl, skip, normed, cot, gate_line, wo)


def mid_kernel(
    z_ref, dno_ref, mixed_ref, wo_ref, gain_ref, in_ref, not_ref, out_ref, dm_ref, dz_ref, gg_ref, acc_ref,
):
    step = pl.program_id(0)
    inner = mixed_ref.shape[1]
    tiles, tile = not_ref.shape[0], not_ref.shape[1]

    @pl.when(step == 0)
    def _():
        gg_ref[...] = jnp.zeros_like(gg_ref)

    def lanes_of(i):
        return pl.ds(pl.multiple_of(i * tile, tile), tile)

    def fold(v):
        total = v[:, :LANES]
        for k in range(LANES, tile, LANES):
            total = total + v[:, k : k + LANES]
        return total

    def one(i, sums):
        sq, hg = sums
        at = lanes_of(i)
        z = z_ref[:, at]
        g = mixed_ref[:, at] * z * sigmoid(z)
        return sq + fold(g * g), hg + fold(dno_ref[:, at] * gain_ref[:, at] * g)

    zero = jnp.zeros((mixed_ref.shape[0], LANES), F32)
    sq, hg = lax.fori_loop(0, tiles, one, (zero, zero))
    scale = lax.rsqrt(jnp.sum(sq, axis=1, keepdims=True) / inner + EPS)
    pull = scale * scale * scale * (jnp.sum(hg, axis=1, keepdims=True) / inner)
    acc_ref[...] = in_ref[...].astype(F32)

    def two(i, carry):
        at = lanes_of(i)
        z, mixed, dno, gain = z_ref[:, at], mixed_ref[:, at], dno_ref[:, at], gain_ref[:, at]
        sig = sigmoid(z)
        act = z * sig
        g = mixed * act
        gs = g * scale
        no = gs * gain
        not_ref[i] = no.T.astype(BF16)
        acc_ref[...] += dot(no.astype(BF16), wo_ref[at, :])
        gg_ref[:, at] += jnp.sum(dno * gs, axis=0, keepdims=True)
        dg = scale * (dno * gain) - g * pull
        dm_ref[:, at] = dg * act
        dz_ref[:, at] = (dg * mixed * (sig * (1.0 + z * (1.0 - sig)))).astype(BF16)
        return carry

    lax.fori_loop(0, tiles, two, 0)
    out_ref[...] = acc_ref[...].astype(BF16)


def mid(z, dno, mixed, wo, gain, inputs, tiles):
    tokens, inner = mixed.shape
    width = inputs.shape[1]
    tile = inner // tiles
    narrow = pl.BlockSpec((CHUNK, width), lambda i: (i, 0))
    wide = pl.BlockSpec((CHUNK, inner), lambda i: (i, 0))
    once = lambda v: pl.BlockSpec(v.shape, lambda i: (0,) * v.ndim, pipeline_mode=pl.Buffered(1))
    return pl.pallas_call(
        mid_kernel,
        grid=(tokens // CHUNK,),
        in_specs=[wide, wide, wide, once(wo), whole((1, inner)), narrow],
        out_specs=[
            pl.BlockSpec((tiles, tile, CHUNK), lambda i: (0, 0, i)), narrow, wide, wide,
            whole((1, inner)),
        ],
        out_shape=[
            jax.ShapeDtypeStruct((tiles, tile, tokens), BF16),
            jax.ShapeDtypeStruct((tokens, width), BF16),
            jax.ShapeDtypeStruct((tokens, inner), F32),
            jax.ShapeDtypeStruct((tokens, inner), BF16),
            jax.ShapeDtypeStruct((1, inner), F32),
        ],
        scratch_shapes=[pltpu.VMEM((CHUNK, width), F32)],
        compiler_params=params(),
        name="gate_norm_project",
    )(z, dno, mixed, wo, gain, inputs)


def bwd_a_kernel(head_dim, seqs, dm_ref, bc_ref, cum_ref, tot_ref, seg_ref, ct_ref):
    step = pl.program_id(0)
    chunks = dm_ref.shape[0] // CHUNK // seqs
    heads = GROUP // head_dim

    @pl.when(step == 0)
    def _():
        for q in range(seqs * chunks):
            ct_ref[q] = bc_ref[q * CHUNK : (q + 1) * CHUNK, LANES:].T.astype(BF16)

    cumg = lane_shift(cum_ref[...], step * heads)
    for s in range(seqs):
        state = None
        for c in range(chunks - 1, -1, -1):
            q = s * chunks + c
            rows = slice(q * CHUNK, (q + 1) * CHUNK)
            ey = jnp.exp2(spread_all(cumg[rows], heads, head_dim)) * dm_ref[rows]
            loc = dot(ct_ref[q], ey.astype(BF16))
            state = loc if state is None else tot_ref[q : q + 1] * state + loc
        seg_ref[s] = state.astype(BF16)


def bwd_a(dm, bc, cum, tot, seqs, head_dim):
    tokens, inner = dm.shape
    return pl.pallas_call(
        functools.partial(bwd_a_kernel, head_dim, seqs),
        grid=(inner // GROUP,),
        in_specs=[
            pl.BlockSpec((tokens, GROUP), lambda i: (0, i)), whole(bc.shape), whole(cum.shape),
            pl.BlockSpec((8, GROUP), lambda i: (0, i)),
        ],
        out_specs=pl.BlockSpec((seqs, LANES, GROUP), lambda i: (0, 0, i)),
        out_shape=jax.ShapeDtypeStruct((seqs, LANES, inner), BF16),
        scratch_shapes=[pltpu.VMEM((tokens // CHUNK, LANES, CHUNK), BF16)],
        compiler_params=params(),
        name="adjoint_states",
    )(dm, bc, cum, tot)


def bwd_b_kernel(
    head_dim, groups, pc_ref, w_ref, b_ref, raw_ref, sb_ref, dl_ref, bc_ref, dt_ref, cum_ref, cumt_ref,
    dm_ref, mixed_ref, s0_ref, s1_ref, s2_ref, g_ref, tot_ref, skip_ref,
    dc_ref, tail_ref, edge_ref, gw_ref, gb_ref, gskip_ref, draw_ref, hsum_ref,
    cbt_ref, dcbt_ref, db_acc, dc_acc, r1_ref, r2_ref, dtot_ref,
):
    step = pl.program_id(0)
    seqs = pc_ref.shape[0]
    seg = pc_ref.shape[1] - EDGE
    chunks = seg // CHUNK
    heads = GROUP // head_dim
    w, b = w_ref[...], b_ref[...]
    taps = w.shape[0]

    @pl.when(step == 0)
    def _():
        for q in range(seqs * chunks):
            rows = slice(q * CHUNK, (q + 1) * CHUNK)
            cbt_ref[q] = nt(bc_ref[rows, :LANES].astype(BF16), bc_ref[rows, LANES:].astype(BF16))
        dcbt_ref[...] = jnp.zeros_like(dcbt_ref)
        db_acc[...] = jnp.zeros_like(db_acc)
        dc_acc[...] = jnp.zeros_like(dc_acc)
        r1_ref[...] = jnp.zeros_like(r1_ref)
        r2_ref[...] = jnp.zeros_like(r2_ref)
        dtot_ref[...] = jnp.zeros_like(dtot_ref)

    def conv_back(s, ext, pre, sig, d_act):
        d_pre = d_act * (sig * (1.0 + pre * (1.0 - sig)))
        zero = jnp.zeros((EDGE, d_pre.shape[1]), F32)
        padded = jnp.concatenate([zero, d_pre, zero], axis=0)
        total = None
        for k in range(taps):
            at = taps - 1 - k
            term = w[k : k + 1] * padded[at : at + seg + EDGE]
            total = term if total is None else total + term
        edge_ref[s] = total[:EDGE]
        dc_ref[s * seg : (s + 1) * seg] = total[EDGE:].astype(BF16)
        tail_ref[s] = total[seg:]
        for k in range(taps):
            at = EDGE - (taps - 1) + k
            grad = jnp.sum(ext[at : at + seg] * d_pre, axis=0, keepdims=True)
            gw_ref[k : k + 1] = grad if s == 0 else gw_ref[k : k + 1] + grad
        grad = jnp.sum(d_pre, axis=0, keepdims=True)
        gb_ref[...] = grad if s == 0 else gb_ref[...] + grad

    def by_head(value, pick):
        high = value.astype(BF16)
        return dot(high, pick) + dot((value - high.astype(F32)).astype(BF16), pick)

    @pl.when(step < groups)
    def _():
        first = step * heads
        cumg = lane_shift(cum_ref[...], first)
        dtg = lane_shift(dt_ref[...], first)
        cumr = head_rows(cumt_ref, first)
        row = lax.broadcasted_iota(jnp.int32, (CHUNK, CHUNK), 0)
        col = lax.broadcasted_iota(jnp.int32, (CHUNK, CHUNK), 1)
        causal = row <= col
        lane = lax.broadcasted_iota(jnp.int32, (GROUP, LANES), 0)
        head = lax.broadcasted_iota(jnp.int32, (GROUP, LANES), 1)
        pick = (head == first + lane // head_dim).astype(BF16)
        skip = skip_ref[...]
        grad_skip = None
        for s in range(seqs):
            ext = pc_ref[s]
            pre = causal_conv(ext, w, b, seg)
            sig = sigmoid(pre)
            acts = pre * sig
            adj = g_ref[s].astype(F32)
            d_acts = [None] * chunks
            for c in range(chunks - 1, -1, -1):
                q = s * chunks + c
                rows = slice(q * CHUNK, (q + 1) * CHUNK)
                x = acts[c * CHUNK : (c + 1) * CHUNK]
                dy = dm_ref[rows]
                ce = spread_all(cumg[rows], heads, head_dim)
                de = spread_all(dtg[rows], heads, head_dim)
                weight = jnp.exp2(ce[CHUNK - 1 : CHUNK] - ce)
                u = x * de
                ub = u.astype(BF16)
                dyb = dy.astype(BF16)
                cbt = cbt_ref[q]
                parts = []
                dcbt = dcbt_ref[q]
                for j in range(0, heads, 2):
                    lanes = slice(j * head_dim, (j + 2) * head_dim)
                    dy_block = block_diagonal(dyb[:, lanes], head_dim)
                    dm = nt(ub[:, lanes], dy_block)
                    mats = []
                    for k, h in enumerate((j, j + 1)):
                        here = jnp.broadcast_to(cumg[rows, h : h + 1], (CHUNK, CHUNK))
                        there = cumr[h : h + 1, rows]
                        decay = jnp.exp2(jnp.where(causal, there - here, -jnp.inf))
                        mats.append((decay * cbt).astype(BF16))
                        dcbt = dcbt + decay * dm[:, k * CHUNK : (k + 1) * CHUNK]
                    parts.append(dot(jnp.concatenate(mats, axis=1), dy_block))
                dcbt_ref[q] = dcbt
                start = s0_ref[s] if c == 0 else s1_ref[s]
                end = s2_ref[s] if c == chunks - 1 else s1_ref[s]
                adj_b = adj.astype(BF16)
                bb = bc_ref[rows, :LANES].astype(BF16)
                cb = bc_ref[rows, LANES:].astype(BF16)
                ey = (jnp.exp2(ce) * dy).astype(BF16)
                du = jnp.concatenate(parts, axis=1) + weight * dot(bb, adj_b)
                db_acc[rows] += nt((u * weight).astype(BF16), adj_b)
                dc_acc[rows] += nt(ey, start)
                r1_ref[rows] += by_head(dyb.astype(F32) * (mixed_ref[rows] - skip * x), pick)
                r2_ref[rows] += by_head(x * du, pick)
                dtot_ref[q : q + 1] += by_head(
                    jnp.sum(adj * end.astype(F32), axis=0, keepdims=True), pick
                )
                grad = jnp.sum(dy * x, axis=0, keepdims=True)
                grad_skip = grad if grad_skip is None else grad_skip + grad
                d_acts[c] = du * de + skip * dy
                if c > 0:
                    adj = tot_ref[q : q + 1] * adj + dot(cb, ey, ((0,), (0,)))
            conv_back(s, ext, pre, sig, jnp.concatenate(d_acts, axis=0))
        gskip_ref[...] = grad_skip

    @pl.when(step == groups)
    def _():
        row = lax.broadcasted_iota(jnp.int32, (CHUNK, CHUNK), 0)
        col = lax.broadcasted_iota(jnp.int32, (CHUNK, CHUNK), 1)
        later = (row <= col).astype(F32)
        rate = -jnp.exp(dl_ref[...])
        sum_raw = jnp.zeros((1, LANES), F32)
        sum_log = jnp.zeros((1, LANES), F32)
        for s in range(seqs):
            ext = pc_ref[s]
            pre = causal_conv(ext, w, b, seg)
            sig = sigmoid(pre)
            parts = []
            for c in range(chunks):
                q = s * chunks + c
                rows = slice(q * CHUNK, (q + 1) * CHUNK)
                dcbt = dcbt_ref[q]
                bb = bc_ref[rows, :LANES].astype(BF16)
                cb = bc_ref[rows, LANES:].astype(BF16)
                d_b = db_acc[rows] + dot(dcbt.astype(BF16), cb)
                d_c = dc_acc[rows] + dot(dcbt.T.astype(BF16), bb)
                parts.append(jnp.concatenate([d_b, d_c], axis=1))
                dt = dt_ref[rows]
                r2 = r2_ref[rows]
                d_log = jnp.dot(
                    later, r1_ref[rows] - dt * r2, precision=HIGH, preferred_element_type=F32
                )
                d_log = d_log + dtot_ref[q : q + 1]
                raw = raw_ref[s, EDGE + c * CHUNK : EDGE + (c + 1) * CHUNK] + sb_ref[...]
                d_raw = (r2 + rate * d_log) * sigmoid(raw)
                draw_ref[rows] = d_raw
                sum_raw = sum_raw + jnp.sum(d_raw, axis=0, keepdims=True)
                sum_log = sum_log + jnp.sum(d_log * dt, axis=0, keepdims=True) * rate
            conv_back(s, ext, pre, sig, jnp.concatenate(parts, axis=0))
        hsum_ref[0:1] = sum_raw
        hsum_ref[1:2] = sum_log


def bwd_b(pc, w, b, sb, dl, bc, dt, cum, cumt, dm, mixed, s0, s1, s2, g, tot, skip, head_dim):
    seqs, rows, cols = pc.shape
    tokens, inner = dm.shape
    groups = inner // GROUP
    taps, channels = w.shape
    wide = pl.BlockSpec((tokens, GROUP), lambda i: (0, jnp.minimum(i, groups - 1)))
    states = pl.BlockSpec((seqs, LANES, GROUP), lambda i: (0, 0, jnp.minimum(i, groups - 1)))
    line = lambda n: pl.BlockSpec((n, GROUP), lambda i: (0, jnp.minimum(i, groups - 1)))
    conv = lambda n: pl.BlockSpec((n, GROUP), lambda i: (0, i))
    ends = pl.BlockSpec((seqs, EDGE, GROUP), lambda i: (0, 0, i))
    chunks = tokens // CHUNK
    shape = jax.ShapeDtypeStruct
    return pl.pallas_call(
        functools.partial(bwd_b_kernel, head_dim, groups),
        grid=(groups + 1,),
        in_specs=[
            pl.BlockSpec((seqs, rows, GROUP), lambda i: (0, 0, i)),
            conv(taps),
            conv(1),
            pl.BlockSpec((seqs, rows, LANES), lambda i: (0, 0, cols // LANES - 1)),
            whole((1, LANES)), whole((1, LANES)),
            whole(bc.shape), whole(dt.shape), whole(cum.shape), whole(cumt.shape),
            wide, wide, states, states, states, states, line(8), line(1),
        ],
        out_specs=[
            conv(tokens), ends, ends, conv(taps), conv(1), line(1),
            whole((tokens, LANES)), whole((2, LANES)),
        ],
        out_shape=[
            shape((tokens, channels), BF16),
            shape((seqs, EDGE, channels), F32),
            shape((seqs, EDGE, channels), F32),
            shape((taps, channels), F32),
            shape((1, channels), F32),
            shape((1, inner), F32),
            shape((tokens, LANES), F32),
            shape((2, LANES), F32),
        ],
        scratch_shapes=[
            pltpu.VMEM((chunks, CHUNK, CHUNK), F32),
            pltpu.VMEM((chunks, CHUNK, CHUNK), F32),
            pltpu.VMEM((tokens, LANES), F32),
            pltpu.VMEM((tokens, LANES), F32),
            pltpu.VMEM((tokens, LANES), F32),
            pltpu.VMEM((tokens, LANES), F32),
            pltpu.VMEM((8, LANES), F32),
        ],
        compiler_params=params(),
        name="scan_backward",
    )(pc, w, b, pc, sb, dl, bc, dt, cum, cumt, dm, mixed, s0, s1, s2, g, tot, skip)


PIECES = (3, 2, 1)


def piece_of(columns, n):
    unit = columns // sum(PIECES)
    return sum(PIECES[:n]) * unit, sum(PIECES[: n + 1]) * unit


def pair_copies(place, lhs, rhs, send, recv):
    other = 1 - place.own["c"]
    parts = [(src.at[2 * g + other], dst.at[g]) for src, dst in lhs for g in range(4)] + list(rhs)
    return [
        remote(src, dst, send.at[n], recv.at[n], place.to["c"]) for n, (src, dst) in enumerate(parts)
    ]


def scan_backward_kernel(
    depth, head_dim, groups,
    pc_ref, w_ref, b_ref, raw_ref, sb_ref, dl_ref, bc_ref, dt_ref, cum_ref, cumt_ref,
    dma_ref, dm_ref, mixed_ref, s0_ref, s1_ref, s2_ref, tot_ref, skip_ref,
    nt_src, dz_src, no_src, cot_src,
    dc_out, gw_ref, gb_ref, hsum_ref, a_out, b_out, nt_out,
    cbt_ref, ct_ref, dcbt_ref, db_acc, dc_acc, r1_ref, r2_ref, dtot_ref, skip_acc,
    dc_ref, tail_ref, edge_ref, edge_came, seg_ring, tot_all, came, sent,
    nt_pair, dz_pair, no_pair, cot_pair,
    chain_send, chain_recv, edge_send, edge_recv, pair_send, pair_recv, out_sem, send, recv, *bufs,
):
    step = pl.program_id(0)
    lag = depth - 1
    seqs = pc_ref.shape[0]
    seg = pc_ref.shape[1] - EDGE
    chunks = seg // CHUNK
    heads = GROUP // head_dim
    w, b = w_ref[...], b_ref[...]
    taps = w.shape[0]
    channels = tail_ref.shape[2]
    place = Place(depth)
    chain = Chain(place, came, sent, chain_send, chain_recv, True)
    cut = lambda ref, lo, hi: ref.at[:, pl.ds(lo, hi - lo)]
    rhs = []
    for n in range(2):
        for src, dst in ((dz_src, dz_pair), (cot_src, cot_pair)):
            lo, hi = piece_of(src.shape[1], n)
            hi = hi if n == 0 else src.shape[1]
            rhs.append((cut(src, lo, hi), cut(dst, lo, hi)))
    pairs = pair_copies(place, ((nt_src, nt_pair), (no_src, no_pair)), rhs, pair_send, pair_recv)
    def piece(ref, n):
        lo, hi = piece_of(ref.shape[1], n)
        return ref.at[:, pl.ds(lo, hi - lo)]

    lanes = []
    for n in range(len(PIECES)):
        lanes += [
            Scatter(place, nt_src, nt_pair, piece(dz_src, n), piece(dz_pair, n), "y", "x",
                    bufs[14 * n : 14 * n + 7], send.at[2 * n], recv.at[2 * n]),
            Scatter(place, no_src, no_pair, piece(cot_src, n), piece(cot_pair, n), "x", "y",
                    bufs[14 * n + 7 : 14 * n + 14], send.at[2 * n + 1], recv.at[2 * n + 1]),
        ]
    edges = [
        remote(edge_ref.at[:, :, cols], edge_came.at[:, :, cols], edge_send.at[n], edge_recv.at[n], place.left)
        for n, cols in enumerate((pl.ds(0, channels - GROUP), pl.ds(channels - GROUP, GROUP)))
    ]
    outs = [
        pltpu.make_async_copy(src, dst, out_sem.at[n])
        for n, (src, dst) in enumerate(((nt_pair, nt_out), (dc_ref, dc_out)))
    ]

    def run(first, name, *rest):
        for lane in lanes[2 * first : 2 * first + 2]:
            getattr(lane, name)(*rest)

    def at_step(n, *what):
        pl.when(step == n)(lambda: run(*what))

    @pl.when(step == 0)
    def _():
        place.meet()
        for copy in pairs:
            copy.start()
        for q in range(seqs * chunks):
            rows = slice(q * CHUNK, (q + 1) * CHUNK)
            b_proj, c_proj = bc_ref[rows, :LANES], bc_ref[rows, LANES:]
            cbt_ref[q] = nt_exact(b_proj, c_proj)
            ct_ref[q] = c_proj.T
        dcbt_ref[...] = jnp.zeros_like(dcbt_ref)
        db_acc[...] = jnp.zeros_like(db_acc)
        dc_acc[...] = jnp.zeros_like(dc_acc)
        r1_ref[...] = jnp.zeros_like(r1_ref)
        r2_ref[...] = jnp.zeros_like(r2_ref)
        skip_acc[...] = jnp.zeros_like(skip_acc)
        dtot_ref[...] = jnp.zeros_like(dtot_ref)

    slots = seg_ring.shape[0]

    @pl.when(step < groups // 2)
    def _():
        for j in (0, 1):
            g = 2 * step + j
            cols = slice(j * GROUP, (j + 1) * GROUP)
            cumg = lane_shift(cum_ref[...], g * heads)
            tot_all[g] = tot_ref[:, cols]
            for s in range(seqs):
                state = None
                for c in range(chunks - 1, -1, -1):
                    q = s * chunks + c
                    rows = slice(q * CHUNK, (q + 1) * CHUNK)
                    ey = jnp.exp2(spread_all(cumg[rows], heads, head_dim)) * dma_ref[rows, cols]
                    loc = dot_pairs(ct_ref[q], ey)
                    state = loc if state is None else tot_ref[q : q + 1, cols] * state + loc
                seg_ring[lax.rem(g, slots), s] = state

    handed = step - chain.behind

    @pl.when((handed >= 0) & (handed < groups // 2))
    def _():
        for j in (0, 1):
            g = 2 * handed + j
            totals = tot_all[g, seqs * chunks : seqs * chunks + seqs]
            chain.step(g, totals[:, None, :], seg_ring[lax.rem(g, slots)])

    @pl.when(step == lag)
    def _():
        for copy in pairs[:10]:
            copy.wait_recv()
        outs[0].start()

    @pl.when(step == lag + 2)
    def _():
        for copy in pairs[10:]:
            copy.wait_recv()

    at_step(lag, 0, "send_second", 0)
    at_step(lag + 1, 0, "send_second", 1)
    at_step(lag + 2, 1, "send_second", 0)
    at_step(lag + 3, 0, "send_first")
    at_step(lag + 4, 1, "send_second", 1)
    at_step(lag + 5, 2, "send_second", 0)
    at_step(lag + 5, 2, "send_second", 1)
    at_step(lag + 6, 0, "hold")
    at_step(lag + 8, 1, "send_first")
    for n, k in enumerate(lanes[0].waves()):
        at_step(lag + 9 + n, 0, "step", k)
    at_step(lag + 11, 1, "hold")

    def conv_back(s, ext, pre, sig, d_act, at):
        lanes_at = pl.ds(pl.multiple_of(at * GROUP, GROUP), GROUP)
        d_pre = d_act * (sig * (1.0 + pre * (1.0 - sig)))
        zero = jnp.zeros((EDGE, d_pre.shape[1]), F32)
        padded = jnp.concatenate([zero, d_pre, zero], axis=0)
        total = None
        for k in range(taps):
            start = taps - 1 - k
            term = w[k : k + 1] * padded[start : start + seg + EDGE]
            total = term if total is None else total + term
        edge_ref[s, :, lanes_at] = total[:EDGE].astype(BF16)
        dc_ref[s * seg : (s + 1) * seg, lanes_at] = total[EDGE:].astype(BF16)
        tail_ref[s, :, lanes_at] = total[seg:]
        for k in range(taps):
            start = EDGE - (taps - 1) + k
            grad = jnp.sum(ext[start : start + seg] * d_pre, axis=0, keepdims=True)
            gw_ref[k : k + 1] = grad if s == 0 else gw_ref[k : k + 1] + grad
        grad = jnp.sum(d_pre, axis=0, keepdims=True)
        gb_ref[...] = grad if s == 0 else gb_ref[...] + grad

    def by_head(value, pick):
        high = value.astype(BF16)
        return dot(high, pick) + dot((value - high.astype(F32)).astype(BF16), pick)

    @pl.when((step >= lag) & (step < lag + groups))
    def _():
        g = step - lag
        first = g * heads
        cumg = lane_shift(cum_ref[...], first)
        dtg = lane_shift(dt_ref[...], first)
        cumr = head_rows(cumt_ref, first)
        row = lax.broadcasted_iota(jnp.int32, (CHUNK, CHUNK), 0)
        col = lax.broadcasted_iota(jnp.int32, (CHUNK, CHUNK), 1)
        causal = row <= col
        lane = lax.broadcasted_iota(jnp.int32, (GROUP, LANES), 0)
        head = lax.broadcasted_iota(jnp.int32, (GROUP, LANES), 1)
        pick = (head == first + lane // head_dim).astype(BF16)
        skip = skip_row(skip_ref, first, heads, head_dim)
        grad_skip = None
        for s in range(seqs):
            ext = pc_ref[s]
            pre = causal_conv(ext, w, b, seg)
            sig = sigmoid(pre)
            acts = pre * sig
            adj = came[g, s].astype(F32)
            d_acts = [None] * chunks
            for c in range(chunks - 1, -1, -1):
                q = s * chunks + c
                rows = slice(q * CHUNK, (q + 1) * CHUNK)
                x = acts[c * CHUNK : (c + 1) * CHUNK]
                dy = dm_ref[rows]
                ce = spread_all(cumg[rows], heads, head_dim)
                de = spread_all(dtg[rows], heads, head_dim)
                weight = jnp.exp2(ce[CHUNK - 1 : CHUNK] - ce)
                u = x * de
                ub = u.astype(BF16)
                dyb = dy.astype(BF16)
                cbt = cbt_ref[q]
                parts = []
                dcbt = dcbt_ref[q]
                for j in range(0, heads, 2):
                    two = slice(j * head_dim, (j + 2) * head_dim)
                    dy_block = block_diagonal(dyb[:, two], head_dim)
                    dm = nt(ub[:, two], dy_block)
                    mats = []
                    for k, h in enumerate((j, j + 1)):
                        here = jnp.broadcast_to(cumg[rows, h : h + 1], (CHUNK, CHUNK))
                        there = cumr[h : h + 1, rows]
                        decay = jnp.exp2(jnp.where(causal, there - here, -jnp.inf))
                        mats.append((decay * cbt).astype(BF16))
                        dcbt = dcbt + decay * dm[:, k * CHUNK : (k + 1) * CHUNK]
                    parts.append(dot(jnp.concatenate(mats, axis=1), dy_block))
                dcbt_ref[q] = dcbt
                start = s0_ref[s] if c == 0 else s1_ref[s]
                end = s2_ref[s] if c == chunks - 1 else s1_ref[s]
                adj_b = adj.astype(BF16)
                bb = bc_ref[rows, :LANES].astype(BF16)
                ey = jnp.exp2(ce) * dy
                du = jnp.concatenate(parts, axis=1) + weight * dot(bb, adj_b)
                uw = u * weight
                across = ((1,), (1,))
                db_acc[rows] += dot_pair(uw, adj_b, across) if c == chunks - 1 else dot_pairs(uw, adj, across)
                dc_acc[rows] += dot_pair(ey, start, across) if c == 0 else dot_pairs(ey, start, across)
                r1_ref[rows] += by_head(dyb.astype(F32) * (mixed_ref[rows] - skip * x), pick)
                r2_ref[rows] += by_head(x * du, pick)
                dtot_ref[q : q + 1] += by_head(
                    jnp.sum(adj * end.astype(F32), axis=0, keepdims=True), pick
                )
                grad = jnp.sum(dy * x, axis=0, keepdims=True)
                grad_skip = grad if grad_skip is None else grad_skip + grad
                d_acts[c] = du * de + skip * dy
                if c > 0:
                    adj = tot_all[g, q : q + 1] * adj + dot_pairs(ct_ref[q], ey)
            conv_back(s, ext, pre, sig, jnp.concatenate(d_acts, axis=0), g)
        skip_acc[0:1] += by_head(grad_skip, pick)

    @pl.when(step == lag + groups)
    def _():
        pl.when(place.has_left)(edges[0].start)
        row = lax.broadcasted_iota(jnp.int32, (CHUNK, CHUNK), 0)
        col = lax.broadcasted_iota(jnp.int32, (CHUNK, CHUNK), 1)
        later = (row <= col).astype(F32)
        rate = -jnp.exp(dl_ref[...])
        sum_raw = jnp.zeros((1, LANES), F32)
        sum_log = jnp.zeros((1, LANES), F32)
        for s in range(seqs):
            ext = pc_ref[s]
            pre = causal_conv(ext, w, b, seg)
            sig = sigmoid(pre)
            parts = []
            for c in range(chunks):
                q = s * chunks + c
                rows = slice(q * CHUNK, (q + 1) * CHUNK)
                dcbt = dcbt_ref[q]
                d_b = db_acc[rows] + dot_pairs(dcbt, bc_ref[rows, LANES:])
                d_c = dc_acc[rows] + dot_pairs(dcbt.T, bc_ref[rows, :LANES])
                parts.append(jnp.concatenate([d_b, d_c], axis=1))
                dt = dt_ref[rows]
                r2 = r2_ref[rows]
                d_log = jnp.dot(
                    later, r1_ref[rows] - dt * r2, precision=HIGH, preferred_element_type=F32
                )
                d_log = d_log + dtot_ref[q : q + 1]
                raw = raw_ref[s, EDGE + c * CHUNK : EDGE + (c + 1) * CHUNK] + sb_ref[...]
                d_raw = (r2 + rate * d_log) * sigmoid(raw)
                dc_ref[rows, channels:] = d_raw.astype(BF16)
                sum_raw = sum_raw + jnp.sum(d_raw, axis=0, keepdims=True)
                sum_log = sum_log + jnp.sum(d_log * dt, axis=0, keepdims=True) * rate
            conv_back(s, ext, pre, sig, jnp.concatenate(parts, axis=0), groups)
        hsum_ref[0:1] = sum_raw
        hsum_ref[1:2] = sum_log
        hsum_ref[2:3] = skip_acc[0:1]
        pl.when(place.has_left)(edges[1].start)

        @pl.when(place.has_right)
        def _():
            for copy in edges:
                copy.wait_recv()
            for s in range(seqs):
                fixed = tail_ref[s] + edge_came[s].astype(F32)
                dc_ref[(s + 1) * seg - EDGE : (s + 1) * seg, :channels] = fixed.astype(BF16)

        outs[1].start()
        run(2, "send_first")
        run(1, "step", depth - 1)
        run(2, "hold")
        for k in range(depth - 2, -1, -1):
            run(1, "step", k)
            run(2, "step", k + 1)
        run(2, "step", 0)
        for n, out in enumerate((a_out, b_out)):
            for i in range(len(PIECES)):
                lo, hi = piece_of(out.shape[1], i)
                out[:, lo:hi] = lanes[2 * i + n].keep[place.z]
        for lane in lanes:
            lane.finish()
        chain.finish()

        @pl.when(place.has_left)
        def _():
            for copy in edges:
                copy.wait_send()

        for copy in pairs:
            copy.wait_send()
        for copy in outs:
            copy.wait()


def scan_backward(
    pc, w, b, sb, dl, bc, dt, cum, cumt, dm, mixed, s0, s1, s2, tot, skip, normed_t, dz, turned, cot,
    head_dim, depth,
):
    seqs, rows, cols = pc.shape
    tokens, inner = dm.shape
    groups = inner // GROUP
    lag = depth - 1
    taps, channels = w.shape
    out = lambda i: jnp.maximum(i - lag, 0)
    inside = lambda i: jnp.minimum(out(i), groups - 1)
    wide = pl.BlockSpec((tokens, GROUP), lambda i: (0, inside(i)))
    states = pl.BlockSpec((seqs, LANES, GROUP), lambda i: (0, 0, inside(i)))
    conv = lambda n: pl.BlockSpec((n, GROUP), lambda i: (0, out(i)))
    ahead = lambda n: pl.BlockSpec((n, 2 * GROUP), lambda i: (0, jnp.minimum(i, groups // 2 - 1)))
    once = lambda v: pl.BlockSpec(v.shape, lambda i: (0,) * v.ndim, pipeline_mode=pl.Buffered(1))
    anywhere = pl.BlockSpec(memory_space=pl.ANY)
    chunks = tokens // CHUNK
    shape, dma = jax.ShapeDtypeStruct, pltpu.SemaphoreType.DMA
    a_rows, b_rows = normed_t.shape[1] // depth, turned.shape[1] // depth
    a_cols, b_cols = dz.shape[1], cot.shape[1]
    half = lambda v: (4,) + v.shape[1:]
    sends, receives = Scatter.sems(depth)
    buffers = []
    for n in range(len(PIECES)):
        for rows_of, cols_of in ((a_rows, a_cols), (b_rows, b_cols)):
            lo, hi = piece_of(cols_of, n)
            buffers += Scatter.scratch(depth, rows_of, hi - lo)
    link = pltpu.VMEM((groups, seqs, LANES, GROUP), BF16)
    square = pltpu.VMEM((chunks, CHUNK, CHUNK), F32)
    column = pltpu.VMEM((tokens, LANES), F32)
    return pl.pallas_call(
        functools.partial(scan_backward_kernel, depth, head_dim, groups),
        grid=(groups + 1 + lag,),
        in_specs=[
            pl.BlockSpec((seqs, rows, GROUP), lambda i: (0, 0, out(i))),
            conv(taps),
            conv(1),
            pl.BlockSpec(
                (seqs, rows, LANES), lambda i: (0, 0, cols // LANES - 1), pipeline_mode=pl.Buffered(1)
            ),
            whole((1, LANES)), whole((1, LANES)),
            once(bc), once(dt), once(cum), once(cumt),
            ahead(tokens), wide, wide, states, states, states, ahead(8), whole((1, LANES)),
            once(normed_t), once(dz), once(turned), once(cot),
        ],
        out_specs=[
            anywhere, conv(taps), conv(1), whole((3, LANES)),
            whole((a_rows, a_cols)), whole((b_rows, b_cols)), anywhere,
        ],
        out_shape=[
            shape((tokens, cols), BF16),
            shape((taps, channels), F32),
            shape((1, channels), F32),
            shape((3, LANES), F32),
            shape((a_rows, a_cols), F32),
            shape((b_rows, b_cols), F32),
            shape(half(normed_t), BF16),
        ],
        scratch_shapes=[
            square, pltpu.VMEM((chunks, LANES, CHUNK), F32), square, column, column, column, column,
            pltpu.VMEM((8, LANES), F32),
            pltpu.VMEM((8, LANES), F32),
            pltpu.VMEM((tokens, cols), BF16),
            pltpu.VMEM((seqs, EDGE, channels), F32),
            pltpu.VMEM((seqs, EDGE, channels), BF16),
            pltpu.VMEM((seqs, EDGE, channels), BF16),
            pltpu.VMEM((2 * lag + 2, seqs, LANES, GROUP), F32), pltpu.VMEM((groups, 8, GROUP), F32), link, link,
            pltpu.VMEM(half(normed_t), BF16), pltpu.VMEM(dz.shape, BF16),
            pltpu.VMEM(half(turned), BF16), pltpu.VMEM(cot.shape, BF16),
            dma((groups,)), dma((groups,)), dma((2,)), dma((2,)), dma((12,)), dma((12,)), dma((2,)),
            dma((2 * len(PIECES), sends)), dma((2 * len(PIECES), receives)),
            *buffers,
        ],
        compiler_params=pltpu.CompilerParams(
            dimension_semantics=("arbitrary",), collective_id=1, has_side_effects=True,
            vmem_limit_bytes=VMEM_LIMIT,
        ),
        name="scan_backward_sums",
    )(
        pc, w, b, pc, sb, dl, bc, dt, cum, cumt, dm, dm, mixed, s0, s1, s2, tot, skip,
        normed_t, dz, turned, cot,
    )


def scatter_last_kernel(
    depth, splits, nt_ref, nt_pair, dc_ref, dz_ref, wg_src, wc_src, x_ref, cot_ref, gain_ref,
    ggain_ref, gb_ref, gw_ref, hsum_ref, c_out, gi_ref, small_out, *refs,
):
    place = Place(depth)
    place.meet()
    pieces = len(splits) - 1
    dc_pairs, refs = refs[:pieces], refs[pieces:]
    small_src, tiles_ref, tile_sem, pair_send, pair_recv, send, recv, small_send, small_recv = refs[:9]
    refs = refs[9:]
    cuts = [dc_ref.at[:, pl.ds(lo, hi - lo)] for lo, hi in zip(splits, splits[1:])]
    copies = pair_copies(place, (), tuple(zip(cuts, dc_pairs)), pair_send, pair_recv)
    for copy in copies:
        copy.start()
    lanes = [
        Scatter(place, nt_ref, nt_pair, cut, pair, *(("y", "x") if n % 2 == 0 else ("x", "y")),
                refs[7 * n : 7 * n + 7], send.at[n], recv.at[n])
        for n, (cut, pair) in enumerate(zip(cuts, dc_pairs))
    ]
    small = SmallScatter(place, small_src, *refs[7 * pieces :], small_send, small_recv)
    tile = tiles_ref.shape[2]
    tokens = x_ref.shape[0]

    def d_normed(src, grad_ref, first, start=0, count=None):
        count = src.shape[1] // tile if count is None else count

        def fetch(i, slot):
            cols = pl.ds(pl.multiple_of(i * tile, LANES), tile)
            return pltpu.make_async_copy(src.at[:, cols], tiles_ref.at[slot], tile_sem.at[slot])

        fetch(start, start % 2).start()

        def one(i, carry):
            slot = lax.rem(i, 2)
            pl.when(i + 1 < count)(lambda: fetch(i + 1, 1 - slot).start())
            fetch(i, slot).wait()
            cols = pl.ds(pl.multiple_of(i * tile, LANES), tile)
            for r in range(0, tokens, 2 * CHUNK):
                rows = slice(r, r + 2 * CHUNK)
                part = nt(grad_ref[rows, cols], tiles_ref[slot])
                if first:

                    @pl.when(i == 0)
                    def _():
                        gi_ref[rows] = part

                    @pl.when(i > 0)
                    def _():
                        gi_ref[rows] += part
                else:
                    gi_ref[rows] += part
            return carry

        lax.fori_loop(start, count, one, 0)

    def input_grad():
        gain = gain_ref[...]
        size = 64

        def one(i, total):
            rows = pl.ds(pl.multiple_of(i * size, size), size)
            d = gi_ref[rows, :]
            values = x_ref[rows, :].astype(F32)
            scale = lax.rsqrt(jnp.mean(values * values, axis=1, keepdims=True) + EPS)
            hat = values * scale
            weighted = d * gain
            pull = jnp.mean(weighted * hat, axis=1, keepdims=True)
            gi_ref[rows, :] = scale * (weighted - hat * pull) + cot_ref[rows, :].astype(F32)
            return total + jnp.sum(d * hat, axis=0, keepdims=True)

        grad_gain = lax.fori_loop(0, tokens // size, one, jnp.zeros(gain.shape, F32))
        small_src[...] = jnp.zeros_like(small_src)
        taps = gw_ref.shape[0]
        shares = ((0, grad_gain), (1, ggain_ref[...]), (2, gb_ref[...]), (3, gw_ref[...]))
        heads = hsum_ref[:, : LANES // 2]
        for n in range(8 * depth):
            at = (n // depth // 4, n // depth // 2 % 2, n // depth % 2, n % depth)
            for row, value in shares:
                own = value.shape[1] // (8 * depth)
                where = (*at, slice(row, row + value.shape[0]), slice(0, own))
                small_src[where] = value[:, n * own : (n + 1) * own]
            small_src[(*at, slice(0, 1), slice(LANES // 2, LANES))] = heads[0:1]
            small_src[(*at, slice(3 + taps, 4 + taps), slice(0, LANES // 2))] = heads[1:2]
            small_src[(*at, slice(3 + taps, 4 + taps), slice(LANES // 2, LANES))] = heads[2:3]

    def run(first, name, *rest):
        for lane in lanes[first : first + 2]:
            getattr(lane, name)(*rest)

    for copy in copies[:2]:
        copy.wait_recv()
    run(0, "send_second", 0)
    run(0, "send_second", 1)
    for copy in copies[2:]:
        copy.wait_recv()
    run(2, "send_second", 0)
    run(2, "send_second", 1)
    d_normed(wg_src, dz_ref, True)
    run(0, "send_first")
    run(4, "send_second", 0)
    run(4, "send_second", 1)
    middle = wc_src.shape[1] // tile // 2
    d_normed(wc_src, dc_ref, False, 0, middle)
    run(0, "hold")
    run(2, "send_first")
    d_normed(wc_src, dc_ref, False, middle)
    run(2, "hold")
    run(0, "step", depth - 1)
    run(4, "send_first")
    input_grad()
    small.stage(0)
    run(0, "step", depth - 2)
    run(2, "step", depth - 1)
    run(4, "hold")
    small.stage(1)
    rounds = [[] for _ in range(depth + 3)]
    for n in range(depth):
        for first, start in ((0, -2), (2, -1), (4, 0)):
            if start + n >= 0:
                rounds[start + n].append((first, depth - 1 - n))
    for n, items in enumerate(rounds):
        for first, k in items:
            run(first, "step", k)
        if n < 2:
            small.stage(2 + n)
        elif n - 2 < depth:
            small.sums.step(depth - 1 - (n - 2))
    for lane, lo, hi in zip(lanes, splits, splits[1:]):
        c_out[:, lo:hi] = lane.keep[place.z]
    small_out[...] = small.keep[place.z]
    for lane in lanes:
        lane.finish()
    small.finish()
    for copy in copies:
        copy.wait_send()


def scatter_last(normed_t, nt_pair, dc, dz, wg, wc, x, cot, gain, ggain, gb, gw, hsum, depth):
    shape = jax.ShapeDtypeStruct
    vmem, dma = pl.BlockSpec(memory_space=pltpu.VMEM), pltpu.SemaphoreType.DMA
    anywhere = pl.BlockSpec(memory_space=pl.ANY)
    sends, receives = Scatter.sems(depth)
    rows = normed_t.shape[1] // depth
    tokens, width = dc.shape
    blocks = width // LANES
    parts = [share for share in PIECES for _ in (0, 1)]
    splits = tuple(LANES * (blocks * sum(parts[:n]) // sum(parts)) for n in range(len(parts) + 1))
    small_shape = (8, LANES)
    small_sends, small_receives = SmallScatter.sems(depth)
    sizes = [hi - lo for lo, hi in zip(splits, splits[1:])]
    scratch = []
    for size in sizes:
        scratch += Scatter.scratch(depth, rows, size)
    return pl.pallas_call(
        functools.partial(scatter_last_kernel, depth, splits),
        in_specs=[vmem, vmem, vmem, vmem, anywhere, anywhere] + [vmem] * 7,
        out_specs=[vmem] * 3,
        out_shape=[shape((rows, width), F32), shape((tokens, x.shape[1]), F32), shape(small_shape, F32)],
        scratch_shapes=[
            *(pltpu.VMEM((tokens, size), BF16) for size in sizes),
            pltpu.VMEM((2, 2, 2, depth) + small_shape, F32),
            pltpu.VMEM((2, wg.shape[0], 3 * LANES), BF16),
            dma((2,)), dma((6,)), dma((6,)), dma((6, sends)), dma((6, receives)),
            dma((small_sends,)), dma((small_receives,)),
            *scratch,
            *SmallScatter.scratch(depth, small_shape),
        ],
        compiler_params=pltpu.CompilerParams(
            collective_id=2, has_side_effects=True, vmem_limit_bytes=VMEM_LIMIT
        ),
        name="scatter_last",
    )(normed_t, nt_pair, dc, dz, wg, wc, x, cot, gain, ggain, gb, gw, hsum)


def passed_along(value, axis, steps):
    count = lax.axis_size(axis)
    initial, last = (max(0, -steps), min(count, count - steps))
    return lax.ppermute(value, axis, [(source, source + steps) for source in range(initial, last)])


def prefix(total, local, axis, backward):
    count, here = lax.axis_size(axis), lax.axis_index(axis)
    totals = lax.all_gather(total.astype(BF16), axis)
    locals_ = lax.all_gather(local, axis)
    state = jnp.zeros(local.shape, F32)
    order = range(count - 1, 0, -1) if backward else range(count - 1)
    for lap in order:
        new = totals[lap].astype(F32) * state + locals_[lap].astype(F32)
        reached = lap > here if backward else lap < here
        state = jnp.where(reached, new, state)
    leaves = total * state + local.astype(F32)
    return state.astype(BF16), leaves.astype(BF16)


AXES = ("dp", "ctx")


def body(
    inputs, gain_in, in_weight, conv_weight, conv_bias, step_bias, decay_log, skip_gain, gain_out,
    out_weight, cotangent,
):
    seqs, seg, width = inputs.shape
    tokens = seqs * seg
    count = lax.axis_size(AXES)
    dp, depth = lax.axis_size("dp"), lax.axis_size("ctx")
    own_links = dp == 8 and depth == 4
    inner = out_weight.shape[0] * count
    taps, channels = conv_weight.shape[0], conv_weight.shape[1] * count
    num_heads = step_bias.shape[0]
    head_dim = inner // num_heads
    a, b, c = gain_in.shape[0], gain_out.shape[0], conv_bias.shape[0]

    w_gate = in_weight[:, :inner]
    w_conv = in_weight[:, inner:]
    spare = -w_conv.shape[1] % LANES
    w_conv = jnp.pad(w_conv, ((0, 0), (0, spare)))
    rest = jnp.concatenate([gain_out, conv_bias, conv_weight.reshape(-1)])
    ends = taps - 1
    flat = inputs.reshape(tokens, width)
    cot = cotangent.reshape(tokens, width)

    if own_links:
        row = lambda v: jnp.pad(v, ((0, 0), (0, LANES - v.shape[1])))
        small = [row(v.reshape(-1, v.shape[-1])) for v in (gain_in, gain_out, conv_bias, conv_weight)]
        small = jnp.concatenate(small + [jnp.zeros((5 - taps, LANES), BF16)]).astype(F32)
        pc, normed_ext, normed_t, g_in, g_out, bias, kernel, w_conv, gate_line = gather_project(
            inputs, small, w_conv, w_gate, inner, channels, taps, depth
        )
        w_conv = w_conv.reshape(width, -1)
    else:
        before = passed_along(inputs[:, seg - EDGE :], "ctx", 1)
        ext = jnp.concatenate([before, inputs], axis=1).astype(F32)
        scale_ext = lax.rsqrt(jnp.mean(ext * ext, axis=-1, keepdims=True) + EPS)
        small = lax.all_gather(jnp.concatenate([gain_in, rest]), AXES).astype(F32)
        w_conv = lax.all_gather(w_conv, AXES, axis=0, tiled=True)
        w_gate = lax.all_gather(w_gate, AXES, axis=0, tiled=True)
        w_out = lax.all_gather(out_weight, AXES, axis=0, tiled=True)
        g_in, rest = small[:, :a].reshape(1, width), small[:, a:]
        normed_ext = (ext * scale_ext * g_in).astype(BF16)
        pc = dot(normed_ext.reshape(-1, width), w_conv).reshape(seqs, seg + EDGE, -1)
        g_out = rest[:, :b].reshape(1, inner)
        bias = rest[:, b : b + c].reshape(1, channels)
        kernel = rest[:, b + c : b + c + taps * c].reshape(count, taps, c).transpose(1, 0, 2)
        kernel = kernel.reshape(taps, channels)
    pad_head = lambda v: jnp.pad(v, (0, LANES - num_heads)).reshape(1, LANES)
    sb, dl = pad_head(step_bias), pad_head(decay_log)
    skip = jnp.repeat(skip_gain, head_dim).reshape(1, inner)

    if own_links:
        bc, dt, cum, cumt, mixed, s0, s1, s2, tot, z, dno, w_gate, w_out = scan_forward(
            pc, kernel, bias, sb, dl, pad_head(skip_gain), normed_ext, cot, gate_line, out_weight, inner, head_dim, depth
        )
        w_gate = w_gate.reshape(width, inner)
        w_out = w_out.reshape(inner, width)
        per_seq = tot[tokens // CHUNK : tokens // CHUNK + seqs][:, None, :]
    else:
        x, bc, dt, cum, cumt, loc0, local, tot = fwd_a(pc, kernel, bias, sb, dl, inner, head_dim)
        per_seq = tot[tokens // CHUNK : tokens // CHUNK + seqs][:, None, :]
        s0, s2 = prefix(per_seq, local, "ctx", False)
        mixed, s1 = fwd_b(x, bc, dt, cum, cumt, s0, loc0, tot, skip, head_dim)
        z = dot(normed_ext[:, EDGE:].reshape(tokens, width), w_gate)
        dno = nt(cot, w_out)

    turned, output, d_mixed, d_gate, grad_gain_out = mid(z, dno, mixed, w_out, g_out, flat, 8)
    if own_links:
        (
            d_conv, grad_kernel, grad_bias, head_sums, grad_gate_weight, grad_out_weight, nt_pair
        ) = scan_backward(
            pc, kernel, bias, sb, dl, bc, dt, cum, cumt, d_mixed, mixed, s0, s1, s2, tot,
            pad_head(skip_gain), normed_t, d_gate, turned, cot, head_dim, depth,
        )
    else:
        scatter = lambda v: lax.psum_scatter(v.astype(BF16), AXES, scatter_dimension=0, tiled=True).astype(F32)
        normed = normed_ext[:, EDGE:].reshape(tokens, width)
        grad_out_weight = scatter(dot(turned.reshape(inner, tokens), cot))
        grad_gate_weight = scatter(dot(normed, d_gate, ((0,), (0,))))
        adjoint = bwd_a(d_mixed, bc, cum, tot, seqs, head_dim)
        g, _ = prefix(per_seq, adjoint, "ctx", True)
        d_conv, tail, edge, grad_kernel, grad_bias, grad_skip, d_raw, head_sums = bwd_b(
            pc, kernel, bias, sb, dl, bc, dt, cum, cumt, d_mixed, mixed, s0, s1, s2, g, tot, skip, head_dim
        )
        after = passed_along(edge[:, EDGE - ends :].astype(BF16), "ctx", -1).astype(F32)
        tail = tail[:, EDGE - ends :] + after
        d_conv = d_conv.reshape(seqs, seg, channels).at[:, seg - ends :].set(tail.astype(BF16))
        d_conv = jnp.concatenate([d_conv.reshape(tokens, channels), d_raw.astype(BF16)], axis=1)

    real = d_conv.shape[1] - spare
    if own_links:
        grad_conv_cols, grad_input, mine = scatter_last(
            normed_t, nt_pair, d_conv, d_gate, w_gate, w_conv, flat, cot, g_in,
            grad_gain_out, grad_bias, grad_kernel, head_sums, depth,
        )
        grad_conv_cols = grad_conv_cols[:, :real]
        half = LANES // 2
        grad_gain_in, grad_step = mine[0, :a], mine[0, half : half + num_heads]
        grad_gain_out, grad_bias, grad_kernel = mine[1, :b], mine[2, :c], mine[3 : 3 + taps, :c]
        grad_decay = mine[3 + taps, :num_heads]
        grad_skip = mine[3 + taps, half : half + num_heads]
    else:
        d_normed = nt(d_gate, w_gate) + nt(d_conv, w_conv)
        values = flat.astype(F32)
        scale = lax.rsqrt(jnp.mean(values * values, axis=-1, keepdims=True) + EPS)
        hat = values * scale
        weighted = d_normed * g_in
        pull = jnp.mean(weighted * hat, axis=-1, keepdims=True)
        grad_input = scale * (weighted - hat * pull) + cot.astype(F32)
        grad_conv_cols = scatter(dot(normed, d_conv[:, :real], ((0,), (0,))))
        grad_skip = jnp.sum(grad_skip.reshape(num_heads, head_dim), axis=1)
        heads_sum = jnp.concatenate([head_sums[0, :num_heads], head_sums[1, :num_heads], grad_skip])
        by_owner = jnp.concatenate(
            [
                jnp.sum(d_normed * hat, axis=0).reshape(count, a),
                grad_gain_out.reshape(count, b),
                grad_bias.reshape(count, c),
                grad_kernel.reshape(taps, count, c).transpose(1, 0, 2).reshape(count, taps * c),
                jnp.broadcast_to(heads_sum, (count, 3 * num_heads)),
            ],
            axis=1,
        )
        mine = lax.dynamic_index_in_dim(lax.psum(by_owner, AXES), lax.axis_index(AXES), 0, False)
        cuts = [0, a, a + b, a + b + c, a + b + c + taps * c]
        cuts += [cuts[-1] + n * num_heads for n in (1, 2, 3)]
        parts = [mine[lo:hi] for lo, hi in zip(cuts, cuts[1:])]
        grad_gain_in, grad_gain_out, grad_bias, grad_kernel, grad_step, grad_decay, grad_skip = parts
    return (
        output.reshape(seqs, seg, width),
        grad_input.reshape(seqs, seg, width),
        grad_gain_in,
        jnp.concatenate([grad_gate_weight, grad_conv_cols], axis=1),
        grad_kernel.reshape(taps, c),
        grad_bias,
        grad_step,
        grad_decay,
        grad_skip,
        grad_gain_out,
        grad_out_weight,
    )


def solution(mesh):
    rows, cols, both = P("dp", "ctx", None), P(AXES, None), P(AXES)
    return jax.shard_map(
        body,
        mesh=mesh,
        in_specs=(rows, both, cols, P(None, AXES), both, P(), P(), P(), both, cols, rows),
        out_specs=(rows, rows, both, cols, P(None, AXES), both, P(), P(), P(), both, cols),
        check_vma=False,
    )
```

```python
import functools

import jax
import jax.numpy as jnp
from jax import lax
from jax.experimental import pallas as pl
from jax.experimental.pallas import tpu as pltpu
from jax.sharding import PartitionSpec as P

EPS = 1e-05
LOG2E = 1.4426950408889634
HIGH = lax.Precision.HIGHEST
F32 = jnp.float32
BF16 = jnp.bfloat16
CHUNK = 128
GROUP = 256
EDGE = 16
LANES = 128
VMEM_LIMIT = 62 * 1024 * 1024


def dot(a, b, dims=((1,), (0,))):
    return lax.dot_general(a, b, (dims, ((), ())), preferred_element_type=F32)


def nt(a, b):
    return dot(a, b, ((1,), (1,)))


def params():
    return pltpu.CompilerParams(
        dimension_semantics=("arbitrary",), vmem_limit_bytes=VMEM_LIMIT
    )


def whole(shape):
    return pl.BlockSpec(shape, lambda i: (0,) * len(shape))


def sigmoid(v):
    return 1.0 / (1.0 + jnp.exp(-v))


def softplus(v):
    return jnp.maximum(v, 0.0) + jnp.log1p(jnp.exp(-jnp.abs(v)))


def causal_conv(ext, w, b, seg):
    taps = w.shape[0]
    total = b
    for k in range(taps):
        at = EDGE - (taps - 1) + k
        total = total + w[k : k + 1] * ext[at : at + seg]
    return total


def lane_shift(value, lanes):
    return pltpu.roll(value, lax.rem(LANES - lanes, LANES), 1)


def head_rows(ref, first):
    base = pl.multiple_of(first // 8 * 8, 8)
    return pltpu.roll(ref[pl.ds(base, 8), :], lax.rem(8 - lax.rem(first, 8), 8), 0)


def spread(cols, at, head_dim):
    rows = cols.shape[0]
    lane = lax.broadcasted_iota(jnp.int32, (rows, LANES), 1)
    first = jnp.broadcast_to(cols[:, at : at + 1], (rows, LANES))
    second = jnp.broadcast_to(cols[:, at + 1 : at + 2], (rows, LANES))
    return jnp.where(lane < head_dim, first, second)


def spread_all(cols, heads, head_dim):
    return jnp.concatenate([spread(cols, j, head_dim) for j in range(0, heads, 2)], axis=1)


def skip_row(ref, first, heads, head_dim):
    value = lane_shift(jnp.broadcast_to(ref[...], (8, LANES)), first)
    return spread_all(value, heads, head_dim)[0:1]


def block_diagonal(pair, head_dim):
    lane = lax.broadcasted_iota(jnp.int32, pair.shape, 1)
    zero = jnp.zeros_like(pair)
    return jnp.concatenate(
        [jnp.where(lane < head_dim, pair, zero), jnp.where(lane < head_dim, zero, pair)], axis=0
    )


MESH = pl.DeviceIdType.MESH


class Place:
    def __init__(self, depth):
        dp, z = lax.axis_index("dp"), lax.axis_index("ctx")
        self.depth, self.z = depth, z
        self.own = {"y": lax.div(dp, 4), "x": lax.rem(lax.div(dp, 2), 2), "c": lax.rem(dp, 2)}
        self.to = {
            name: {"dp": dp + step * (1 - 2 * self.own[name])}
            for name, step in (("y", 4), ("x", 2), ("c", 1))
        }
        self.has_left, self.has_right = z > 0, z < depth - 1
        self.left, self.right = {"ctx": z - 1}, {"ctx": z + 1}

    def flipped(self, *names):
        return {n: 1 - v if n in names else v for n, v in self.own.items()}

    def near(self, k):
        z, last = self.z, self.depth - 1
        reach = jnp.minimum(z, last - z)
        pair = jnp.where(k % 2 == 1, z - (k + 1) // 2, z + k // 2)
        alone = jnp.where(z > last - z, last - k, k)
        return z if k == 0 else jnp.where(k <= 2 * reach, pair, alone)

    def meet(self, line=False):
        barrier = pltpu.get_barrier_semaphore()
        signal = functools.partial(pl.semaphore_signal, barrier, inc=1, device_id_type=MESH)
        for name in ("y", "x", "c"):
            signal(device_id=self.to[name])
        if line:
            for k in range(1, self.depth):
                signal(device_id={"ctx": self.near(k)})
            pl.semaphore_wait(barrier, 3 + self.depth - 1)
            return
        pl.when(self.has_left)(lambda: signal(device_id=self.left))
        pl.when(self.has_right)(lambda: signal(device_id=self.right))
        ends = self.has_left.astype(jnp.int32) + self.has_right.astype(jnp.int32)
        pl.semaphore_wait(barrier, 3 + ends)


def remote(src, dst, send, recv, to):
    return pltpu.make_async_remote_copy(
        src_ref=src, dst_ref=dst, send_sem=send, recv_sem=recv, device_id=to, device_id_type=MESH
    )


class Gather:
    def __init__(self, place, src, line, first, second, send, recv, part=()):
        self.place, self.src, self.line_of, self.part = place, src, line, part
        self.first, self.second, self.send, self.recv = first, second, send, recv

    @staticmethod
    def sems(depth):
        return 6 * depth + 3, 5 * depth + 3

    def flips(self, g):
        return ((), (self.first,), (self.second,), (self.first, self.second))[g]

    def slot(self, k, *flips):
        return self.line_of(**self.place.flipped(*flips)).at[(self.place.near(k), *self.part)]

    def copy(self, k, where, to, send, recv):
        src = self.src if k == 0 and where == () else self.slot(k, *where)
        return remote(src, self.slot(k, *where), self.send.at[send], self.recv.at[recv], to)

    def along(self, k, right):
        p = self.place
        return self.copy(k, (), p.right if right else p.left, int(right) * p.depth + k, p.near(k))

    def goes(self, k, right):
        p, at = self.place, self.place.near(k)
        if right:
            return p.has_right if k == 0 else p.has_right & (at < p.z)
        return p.has_left if k == 0 else p.has_left & (at > p.z)

    def to_axis(self, k, stage, there=False):
        p, depth = self.place, self.place.depth
        f, s = self.first, self.second
        where = ((), (), (f,), (f, s))[stage]
        axis = (f, s, s, "c")[stage]
        if there:
            where = where + (axis,)
        return self.copy(k, where, p.to[axis], (2 + stage) * depth + k, (1 + stage) * depth + k)

    def to_core(self, g, there=False):
        depth = self.place.depth
        flips = self.flips(g) + (("c",) if there else ())
        line = self.line_of(**self.place.flipped(*flips)).at[(pl.ds(0, depth), *self.part)]
        return remote(line, line, self.send.at[6 * depth + g], self.recv.at[5 * depth + g], self.place.to["c"])

    def line(self, k):
        if k:
            self.along(k, True).wait_recv()
        for right in (True, False):
            pl.when(self.goes(k, right))(lambda: self.along(k, right).start())
        for stage in (0, 1):
            self.to_axis(k, stage).start()

    def from_first(self, k):
        self.to_axis(k, 0, True).wait_recv()
        self.to_axis(k, 2).start()

    def from_second(self, k):
        self.to_axis(k, 1, True).wait_recv()

    def from_both(self, k):
        self.to_axis(k, 2, True).wait_recv()
        self.to_axis(k, 3).start()

    def core(self, g):
        self.to_core(g).start()

    def whole(self, g):
        if g < 3:
            self.to_core(g, True).wait_recv()
        else:
            for k in range(self.place.depth):
                self.to_axis(k, 3, True).wait_recv()

    def finish(self):
        for k in range(self.place.depth):
            for right in (True, False):
                pl.when(self.goes(k, right))(lambda: self.along(k, right).wait_send())
            for stage in range(4):
                self.to_axis(k, stage).wait_send()
        for g in range(3):
            self.to_core(g).wait_send()


class LineGather(Gather):
    def copy(self, k, where, to, send, recv):
        src = self.src.at[self.place.near(k)] if where == () else self.slot(k, *where)
        return remote(src, self.slot(k, *where), self.send.at[send], self.recv.at[recv], to)

    def line(self, k):
        for stage in (0, 1):
            self.to_axis(k, stage).start()

    def finish(self):
        for k in range(self.place.depth):
            for stage in range(4):
                self.to_axis(k, stage).wait_send()
        for g in range(3):
            self.to_core(g).wait_send()


class OwnLine(Gather):
    def __init__(self, place, src, line, send, recv):
        super().__init__(place, src, lambda y, x, c: line, "y", "x", send, recv)

    def line(self, k):
        if k:
            self.along(k, True).wait_recv()
        for right in (True, False):
            pl.when(self.goes(k, right))(lambda: self.along(k, right).start())

    def finish(self):
        for k in range(self.place.depth):
            for right in (True, False):
                pl.when(self.goes(k, right))(lambda: self.along(k, right).wait_send())


class Line:
    def __init__(self, place, keep, sent, came, send, recv):
        self.place, self.keep, self.sent, self.came = place, keep, sent, came
        self.send, self.recv = send, recv

    def copy(self, k):
        z, zk = self.place.z, self.place.near(k)
        return remote(self.sent.at[zk], self.came.at[z], self.send.at[k], self.recv.at[z], {"ctx": zk})

    def step(self, k):
        place, zk = self.place, self.place.near(k)
        if k:
            self.sent[zk] = self.keep[zk].astype(self.sent.dtype)
            self.copy(k).start()
            return
        for other in range(1, place.depth):
            at = place.near(other)
            remote(self.sent.at[at], self.came.at[at], self.send.at[other], self.recv.at[at], {"ctx": at}).wait_recv()
            self.keep[zk] = self.keep[zk] + self.came[at].astype(F32)

    def finish(self):
        for k in range(1, self.place.depth):
            self.copy(k).wait_send()


class Scatter:
    def __init__(self, place, lhs, lhs_pair, rhs, rhs_pair, first, second, bufs, send, recv):
        self.place, self.lhs, self.lhs_pair, self.rhs, self.rhs_pair = place, lhs, lhs_pair, rhs, rhs_pair
        self.first, self.second, self.send, self.recv = first, second, send, recv
        self.s_sent, self.s_came, self.f_sent, self.f_came, self.keep, z_sent, z_came = bufs
        depth = place.depth
        self.sums = Line(place, self.keep, z_sent, z_came, send.at[pl.ds(2 + depth, depth)],
                         recv.at[pl.ds(2 + depth, depth + 1)])

    @staticmethod
    def sems(depth):
        return 2 + 2 * depth, 3 + 2 * depth

    @staticmethod
    def scratch(depth, rows, cols):
        block = lambda *lead: pltpu.VMEM(lead + (rows, cols), BF16)
        return [
            block(2, depth), block(2, depth), block(depth), block(depth),
            pltpu.VMEM((depth, rows, cols), F32), block(depth), block(depth + 1),
        ]

    def product(self, groups, store):
        pairs = [2 * at["y"] + at["x"] for at in (self.place.flipped(*flips) for flips in groups)]
        core = self.place.own["c"]
        rows, cols = self.keep.shape[1:]
        depth = self.place.depth
        tile = 2 * LANES

        def block(start, size):
            lanes = pl.ds(start, size)
            here = jnp.concatenate([self.lhs[2 * pair + core] for pair in pairs], axis=0)
            there = jnp.concatenate([self.lhs_pair[pair] for pair in pairs], axis=0)
            part = dot(here, self.rhs[:, lanes]) + dot(there, self.rhs_pair[:, lanes])
            for n in range(len(groups)):
                for z in range(depth):
                    first = (n * depth + z) * rows
                    store(n, z, lanes, part[first : first + rows])

        def loop(i, carry):
            block(pl.multiple_of(i * tile, tile), tile)
            return carry

        lax.fori_loop(0, cols // tile, loop, 0)
        if cols % tile:
            block(cols // tile * tile, cols % tile)

    def to_second(self, j):
        return remote(self.s_sent.at[j], self.s_came.at[j], self.send.at[j], self.recv.at[j],
                      self.place.to[self.second])

    def to_first(self, k):
        zk, n = self.place.near(k), 2 + k
        return remote(self.f_sent.at[zk], self.f_came.at[zk], self.send.at[n], self.recv.at[n],
                      self.place.to[self.first])

    def waves(self):
        return range(self.place.depth - 1, -1, -1)

    def send_second(self):
        def store(n, z, lanes, part):
            self.s_sent[n, z, :, lanes] = part.astype(BF16)

        self.product(((self.second, self.first), (self.second,)), store)
        for j in (0, 1):
            self.to_second(j).start()

    def send_first(self):
        self.to_second(0).wait_recv()

        def store(n, z, lanes, part):
            if n == 0:
                self.f_sent[z, :, lanes] = (part + self.s_came[0, z, :, lanes].astype(F32)).astype(BF16)
            else:
                self.keep[z, :, lanes] = part

        self.product(((self.first,), ()), store)
        for k in self.waves():
            self.to_first(k).start()

    def hold(self):
        self.to_second(1).wait_recv()
        for z in range(self.place.depth):
            self.keep[z] = self.keep[z] + self.s_came[1, z].astype(F32)

    def step(self, k):
        self.to_first(k).wait_recv()
        zk = self.place.near(k)
        self.keep[zk] = self.keep[zk] + self.f_came[zk].astype(F32)
        self.sums.step(k)

    def finish(self):
        for j in (0, 1):
            self.to_second(j).wait_send()
        for k in self.waves():
            self.to_first(k).wait_send()
        self.sums.finish()


class SmallScatter:
    def __init__(self, place, src, c_came, half, x_came, keep, y_came, z_sent, z_came, send, recv):
        self.place, self.src, self.c_came, self.half = place, src, c_came, half
        self.x_came, self.keep, self.y_came = x_came, keep, y_came
        self.send, self.recv = send, recv
        depth = place.depth
        self.sums = Line(place, keep, z_sent, z_came, send.at[pl.ds(7, depth)],
                         recv.at[pl.ds(7, depth + 1)])

    @staticmethod
    def sems(depth):
        return 7 + depth, 8 + depth

    @staticmethod
    def scratch(depth, shape):
        block = lambda *lead: pltpu.VMEM(lead + shape, F32)
        return [
            block(2, 2, depth), block(2, 2, depth), block(2, depth), block(depth), block(depth),
            block(depth), block(depth + 1),
        ]

    def copy(self, n):
        p, own = self.place, self.place.own
        if n < 4:
            y, x = n // 2, n % 2
            src, dst, to = self.src.at[y, x, 1 - own["c"]], self.c_came.at[y, x], "c"
        elif n < 6:
            src, dst, to = self.half.at[n - 4, 1 - own["x"]], self.x_came.at[n - 4], "x"
        else:
            src, dst, to = self.half.at[1 - own["y"], own["x"]], self.y_came, "y"
        return remote(src, dst, self.send.at[n], self.recv.at[n], p.to[to])

    def stage(self, n):
        own = self.place.own
        if n == 0:
            for i in range(4):
                self.copy(i).start()
        elif n == 1:
            for i in range(4):
                self.copy(i).wait_recv()
            for y in (0, 1):
                for x in (0, 1):
                    self.half[y, x] = self.src[y, x, own["c"]] + self.c_came[y, x]
            for i in (4, 5):
                self.copy(i).start()
        elif n == 2:
            for i in (4, 5):
                self.copy(i).wait_recv()
            for y in (0, 1):
                self.half[y, own["x"]] = self.half[y, own["x"]] + self.x_came[y]
            self.copy(6).start()
        else:
            self.copy(6).wait_recv()
            self.keep[...] = self.half[own["y"], own["x"]] + self.y_came[...]

    def finish(self):
        for n in range(7):
            self.copy(n).wait_send()
        self.sums.finish()


def gather_kernel(
    depth, half, x_ref, small_src, wc_src, wg_src, pc_ref, normed_ref, normt_ref,
    gin_ref, gout_ref, bias_ref, taps_ref, wc_out, gate_ref,
    small_ref, gain_row, hat_ref, edge_ref, wc_ref, edge_sem, own_sem, out_sem, send, recv, gate_send, gate_recv,
):
    place = Place(depth)
    place.meet()
    seqs, seg, features = x_ref.shape
    width = wc_src.shape[1]
    lo, hi = pl.ds(0, half), pl.ds(half, width - half)
    every = slice(None)
    weights = lambda y, x, c: wc_ref.at[y, x, c]
    lanes = [
        Gather(place, small_src, lambda y, x, c: small_ref.at[y, x, c], "y", "x", send.at[0], recv.at[0]),
        Gather(place, wc_src.at[:, lo], weights, "y", "x", send.at[1], recv.at[1], (every, lo)),
        Gather(place, wc_src.at[:, hi], weights, "x", "y", send.at[2], recv.at[2], (every, hi)),
    ]
    early, late = lanes[:2], lanes[2:]
    gate = OwnLine(place, wg_src, gate_ref, gate_send, gate_recv)
    own = place.own
    mine = (own["y"], own["x"], own["c"], place.z)
    copies = [
        pltpu.make_async_copy(src, dst.at[mine], own_sem.at[n])
        for n, (src, dst) in enumerate(((small_src, small_ref), (wc_src, wc_ref)))
    ]
    copies.append(pltpu.make_async_copy(wg_src, gate_ref.at[place.z], own_sem.at[2]))
    edge = remote(x_ref.at[:, pl.ds(seg - EDGE, EDGE)], edge_ref, edge_sem.at[0], edge_sem.at[1], place.right)

    def each(group, *steps):
        for name, k in steps:
            for lane in group:
                getattr(lane, name)(k)

    def keep(n):
        at = place.flipped(*((), ("y",), ("x",), ("y", "x"))[n])
        return pltpu.make_async_copy(wc_ref.at[at["y"], at["x"]], wc_out.at[at["y"], at["x"]], out_sem.at[n])

    rows = wc_src.shape[0]
    count = 2 * depth * rows

    def norm(flips):
        at = place.flipped(*flips)
        group = 2 * at["y"] + at["x"]
        here = pl.ds(pl.multiple_of(group * count, LANES), count)
        for c in (0, 1):
            for z in range(depth):
                start = (c * depth + z) * rows
                gain_row[:, start : start + rows] = small_ref[at["y"], at["x"], c, z, 0:1, :rows]
        gain = gain_row[...]
        for s in range(seqs):
            normed = (hat_ref[s, :, here] * gain).astype(BF16)
            normed_ref[s, :, here] = normed
            turned = normed[EDGE:].astype(F32).T.astype(BF16)
            for c in (0, 1):
                normt_ref[2 * group + c, :, s * seg : (s + 1) * seg] = turned[c * depth * rows : (c + 1) * depth * rows]

    def multiply(flips, n):
        at = place.flipped(*flips)
        here = pl.ds(pl.multiple_of((2 * at["y"] + at["x"]) * count, LANES), count)
        first, last = ((0, half), (half, width))[n]
        tile = 4 * LANES
        for start in range(first, last, tile):
            cols = slice(start, min(start + tile, last))
            block = jnp.concatenate(
                [wc_ref[at["y"], at["x"], c, z, :, cols] for c in (0, 1) for z in range(depth)], axis=0
            )
            for s in range(seqs):
                part = dot(normed_ref[s, :, here], block)
                if flips == ():
                    pc_ref[s, :, cols] = part
                else:
                    pc_ref[s, :, cols] += part

    each(early, ("line", 0))
    pl.when(place.has_right)(edge.start)
    for copy in copies:
        copy.start()
    pl.when(place.has_left)(edge.wait_recv)

    @pl.when(jnp.logical_not(place.has_left))
    def _():
        edge_ref[...] = jnp.zeros_like(edge_ref)

    def scale_rows(s, start, rows_in, r, step):
        values = rows_in[s, r : r + step].astype(F32)
        mean = jnp.mean(values * values, axis=1, keepdims=True)
        hat_ref[s, start + r : start + r + step] = values * lax.rsqrt(mean + EPS)

    pieces = []
    for s in range(seqs):
        pieces.append((s, 0, edge_ref, 0, EDGE))
        pieces += [(s, EDGE, x_ref, r, 64) for r in range(0, seg, 64)]
    share = -(-len(pieces) // depth)
    for k in range(depth):
        for piece in pieces[k * share : (k + 1) * share]:
            scale_rows(*piece)
        if k + 1 < depth:
            each(early, ("line", k + 1))
        if k == depth - 2:
            each(late, ("line", 0))
    for copy in copies:
        copy.wait()
    each(early, ("core", 0))
    for k in range(1, depth):
        each(late, ("line", k))
        if k == depth - 2:
            gate.line(0)
    each(late, ("core", 0))
    for k in range(depth):
        each(early, ("from_first", k), ("from_second", k))
    each(early, ("core", 1), ("core", 2))
    each(late, ("from_first", 0), ("from_first", 1))
    each(early, ("whole", 0))
    norm(())
    multiply((), 0)
    for k in range(2, depth):
        each(late, ("from_first", k))
    gate.line(1)
    each(early, ("whole", 1))
    norm(("y",))
    multiply(("y",), 0)
    for k in range(depth):
        each(late, ("from_second", k))
    each(late, ("core", 1), ("core", 2))
    each(early, ("whole", 2))
    norm(("x",))
    multiply(("x",), 0)
    gate.line(2)
    each(late, ("whole", 0))
    keep(0).start()
    multiply((), 1)
    for k in range(depth - 1):
        each(lanes, ("from_both", k))
    each(late, ("whole", 1), ("whole", 2))
    keep(1).start()
    keep(2).start()
    multiply(("y",), 1)
    gate.line(3)
    multiply(("x",), 1)
    each(lanes, ("from_both", depth - 1))
    each(early, ("whole", 3))
    norm(("y", "x"))
    multiply(("y", "x"), 0)
    each(late, ("whole", 3))
    keep(3).start()
    multiply(("y", "x"), 1)
    parts = ((gin_ref, 0), (gout_ref, 1), (bias_ref, 2), (taps_ref, 3))
    for n in range(8 * depth):
        at = (n // depth // 4, n // depth // 2 % 2, n // depth % 2, n % depth)
        for out, row in parts:
            size = out.shape[1] // (8 * depth)
            out[:, n * size : (n + 1) * size] = small_ref[(*at, slice(row, row + out.shape[0]), slice(0, size))]
    for lane in (*lanes, gate):
        lane.finish()
    for n in range(4):
        keep(n).wait()
    pl.when(place.has_right)(edge.wait_send)


def gather_project(x, small, wc, wg, inner, channels, taps, depth):
    shape = jax.ShapeDtypeStruct
    seqs, seg, features = x.shape
    slots = (2, 2, 2, depth)
    sends, receives = Gather.sems(depth)
    width = wc.shape[1]
    half = width // 2 // LANES * LANES
    anywhere, vmem = pl.BlockSpec(memory_space=pl.ANY), pl.BlockSpec(memory_space=pltpu.VMEM)
    dma = pltpu.SemaphoreType.DMA
    return pl.pallas_call(
        functools.partial(gather_kernel, depth, half),
        in_specs=[vmem, vmem, vmem, vmem],
        out_specs=[vmem] * 7 + [anywhere, vmem],
        out_shape=[
            shape((seqs, seg + EDGE, width), F32),
            shape((seqs, seg + EDGE, features), BF16),
            shape((8, depth * wc.shape[0], seqs * seg), BF16),
            shape((1, features), F32),
            shape((1, inner), F32),
            shape((1, channels), F32),
            shape((taps, channels), F32),
            shape(slots + wc.shape, BF16),
            shape((depth,) + wg.shape, BF16),
        ],
        scratch_shapes=[
            pltpu.VMEM(slots + small.shape, F32),
            pltpu.VMEM((1, 2 * depth * wc.shape[0]), F32),
            pltpu.VMEM((seqs, seg + EDGE, features), F32),
            pltpu.VMEM((seqs, EDGE, features), BF16),
            pltpu.VMEM(slots + wc.shape, BF16),
            dma((2,)), dma((3,)), dma((4,)), dma((3, sends)), dma((3, receives)),
            dma((2 * depth,)), dma((depth,)),
        ],
        compiler_params=pltpu.CompilerParams(
            collective_id=0, has_side_effects=True, vmem_limit_bytes=VMEM_LIMIT
        ),
        name="gather_project",
    )(x, small, wc, wg)


def fwd_a_kernel(
    head_dim, pc_ref, w_ref, b_ref, raw_ref, sb_ref, dl_ref,
    x_ref, bc_ref, dt_ref, cum_ref, cumt_ref, loc0_ref, seg_ref, tot_ref, bt_ref,
):
    step = pl.program_id(0)
    seqs = pc_ref.shape[0]
    seg = pc_ref.shape[1] - EDGE
    chunks = seg // CHUNK
    w, b = w_ref[...], b_ref[...]

    def acts_of(s):
        pre = causal_conv(pc_ref[s], w, b, seg)
        return pre * sigmoid(pre)

    @pl.when(step == 0)
    def _():
        row = lax.broadcasted_iota(jnp.int32, (CHUNK, CHUNK), 0)
        col = lax.broadcasted_iota(jnp.int32, (CHUNK, CHUNK), 1)
        tri = (col <= row).astype(F32)
        rate = -jnp.exp(dl_ref[...])
        for s in range(seqs):
            acts = acts_of(s)
            bc_ref[s * seg : (s + 1) * seg] = acts
            for c in range(chunks):
                q = s * chunks + c
                rows = slice(q * CHUNK, (q + 1) * CHUNK)
                bt_ref[q] = acts[c * CHUNK : (c + 1) * CHUNK, :LANES].T.astype(BF16)
                dt = softplus(raw_ref[s, EDGE + c * CHUNK : EDGE + (c + 1) * CHUNK] + sb_ref[...])
                cum = LOG2E * jnp.dot(tri, dt * rate, precision=HIGH, preferred_element_type=F32)
                dt_ref[rows] = dt
                cum_ref[rows] = cum
                cumt_ref[:, rows] = cum.T

    @pl.when(step > 0)
    def _():
        heads = GROUP // head_dim
        first = (step - 1) * heads
        cumg = lane_shift(cum_ref[...], first)
        dtg = lane_shift(dt_ref[...], first)
        for s in range(seqs):
            x = acts_of(s)
            x_ref[s * seg : (s + 1) * seg] = x
            state, total = None, None
            for c in range(chunks):
                q = s * chunks + c
                rows = slice(q * CHUNK, (q + 1) * CHUNK)
                ce = spread_all(cumg[rows], heads, head_dim)
                de = spread_all(dtg[rows], heads, head_dim)
                end = ce[CHUNK - 1 : CHUNK]
                uw = x[c * CHUNK : (c + 1) * CHUNK] * de * jnp.exp2(end - ce)
                loc = dot(bt_ref[q], uw.astype(BF16))
                tot = jnp.exp2(end)
                tot_ref[q : q + 1] = tot
                if c == 0:
                    loc0_ref[s] = loc
                    state, total = loc, tot
                else:
                    state, total = tot * state + loc, tot * total
            seg_ref[s] = state.astype(BF16)
            tot_ref[seqs * chunks + s : seqs * chunks + s + 1] = total


def fwd_a(pc, w, b, sb, dl, inner, head_dim):
    seqs, rows, cols = pc.shape
    seg = rows - EDGE
    tokens = seqs * seg
    groups = inner // GROUP
    state = LANES
    chunks = tokens // CHUNK
    at = lambda i: (i + groups) % (groups + 1)
    back = lambda i: jnp.maximum(i - 1, 0)
    return pl.pallas_call(
        functools.partial(fwd_a_kernel, head_dim),
        grid=(groups + 1,),
        in_specs=[
            pl.BlockSpec((seqs, rows, GROUP), lambda i: (0, 0, at(i))),
            pl.BlockSpec((w.shape[0], GROUP), lambda i: (0, at(i))),
            pl.BlockSpec((1, GROUP), lambda i: (0, at(i))),
            pl.BlockSpec((seqs, rows, LANES), lambda i: (0, 0, cols // LANES - 1)),
            whole((1, LANES)),
            whole((1, LANES)),
        ],
        out_specs=[
            pl.BlockSpec((tokens, GROUP), lambda i: (0, back(i))),
            whole((tokens, GROUP)),
            whole((tokens, LANES)),
            whole((tokens, LANES)),
            whole((LANES, tokens)),
            pl.BlockSpec((seqs, state, GROUP), lambda i: (0, 0, back(i))),
            pl.BlockSpec((seqs, state, GROUP), lambda i: (0, 0, back(i))),
            pl.BlockSpec((8, GROUP), lambda i: (0, back(i))),
        ],
        out_shape=[
            jax.ShapeDtypeStruct((tokens, inner), F32),
            jax.ShapeDtypeStruct((tokens, GROUP), F32),
            jax.ShapeDtypeStruct((tokens, LANES), F32),
            jax.ShapeDtypeStruct((tokens, LANES), F32),
            jax.ShapeDtypeStruct((LANES, tokens), F32),
            jax.ShapeDtypeStruct((seqs, state, inner), F32),
            jax.ShapeDtypeStruct((seqs, state, inner), BF16),
            jax.ShapeDtypeStruct((8, inner), F32),
        ],
        scratch_shapes=[pltpu.VMEM((chunks, LANES, CHUNK), BF16)],
        compiler_params=params(),
        name="conv_states",
    )(pc, w, b, pc, sb, dl)


def fwd_b_kernel(
    head_dim, x_ref, bc_ref, dt_ref, cum_ref, cumt_ref, s0_ref, loc0_ref, tot_ref, skip_ref,
    mixed_ref, s1_ref, cb_ref,
):
    step = pl.program_id(0)
    seqs = s0_ref.shape[0]
    chunks = x_ref.shape[0] // CHUNK // seqs
    heads = GROUP // head_dim

    @pl.when(step == 0)
    def _():
        for q in range(seqs * chunks):
            rows = slice(q * CHUNK, (q + 1) * CHUNK)
            cb_ref[q] = nt(bc_ref[rows, LANES:].astype(BF16), bc_ref[rows, :LANES].astype(BF16))

    first = step * heads
    cumg = lane_shift(cum_ref[...], first)
    dtg = lane_shift(dt_ref[...], first)
    cumr = head_rows(cumt_ref, first)
    row = lax.broadcasted_iota(jnp.int32, (CHUNK, CHUNK), 0)
    col = lax.broadcasted_iota(jnp.int32, (CHUNK, CHUNK), 1)
    causal = col <= row
    skip = skip_ref[...]
    for s in range(seqs):
        start = s0_ref[s]
        for c in range(chunks):
            q = s * chunks + c
            rows = slice(q * CHUNK, (q + 1) * CHUNK)
            x = x_ref[rows]
            ce = spread_all(cumg[rows], heads, head_dim)
            de = spread_all(dtg[rows], heads, head_dim)
            ub = (x * de).astype(BF16)
            cb = cb_ref[q]
            parts = []
            for j in range(0, heads, 2):
                mats = []
                for h in (j, j + 1):
                    there = jnp.broadcast_to(cumg[rows, h : h + 1], (CHUNK, CHUNK))
                    here = cumr[h : h + 1, rows]
                    decay = jnp.exp2(jnp.where(causal, there - here, -jnp.inf))
                    mats.append((decay * cb).astype(BF16))
                pair = ub[:, j * head_dim : (j + 2) * head_dim]
                parts.append(dot(jnp.concatenate(mats, axis=1), block_diagonal(pair, head_dim)))
            y = jnp.concatenate(parts, axis=1)
            y = y + jnp.exp2(ce) * dot(bc_ref[rows, LANES:].astype(BF16), start)
            mixed_ref[rows] = y + skip * x
            if c == 0:
                start = (tot_ref[q : q + 1] * start.astype(F32) + loc0_ref[s]).astype(BF16)
                s1_ref[s] = start


def fwd_b(x, bc, dt, cum, cumt, s0, loc0, tot, skip, head_dim):
    tokens, inner = x.shape
    seqs, state, _ = s0.shape
    groups = inner // GROUP
    wide = pl.BlockSpec((tokens, GROUP), lambda i: (0, i))
    states = pl.BlockSpec((seqs, state, GROUP), lambda i: (0, 0, i))
    return pl.pallas_call(
        functools.partial(fwd_b_kernel, head_dim),
        grid=(groups,),
        in_specs=[
            wide, whole(bc.shape), whole(dt.shape), whole(cum.shape), whole(cumt.shape),
            states, states,
            pl.BlockSpec((8, GROUP), lambda i: (0, i)),
            pl.BlockSpec((1, GROUP), lambda i: (0, i)),
        ],
        out_specs=[wide, states],
        out_shape=[
            jax.ShapeDtypeStruct((tokens, inner), F32),
            jax.ShapeDtypeStruct((seqs, state, inner), BF16),
        ],
        scratch_shapes=[pltpu.VMEM((tokens // CHUNK, CHUNK, CHUNK), F32)],
        compiler_params=params(),
        name="scan_outputs",
    )(x, bc, dt, cum, cumt, s0, loc0, tot, skip)


def halves(v):
    high = v.astype(BF16)
    return high, (v - high.astype(F32)).astype(BF16)


def dot_pairs(a, b, dims=((1,), (0,))):
    (ah, al), (bh, bl) = halves(a), halves(b)
    return dot(ah, bh, dims) + (dot(al, bh, dims) + dot(ah, bl, dims))


def dot_pair(a, b, dims=((1,), (0,))):
    high, low = halves(a)
    return dot(high, b, dims) + dot(low, b, dims)


def nt_exact(a, b):
    return lax.dot_general(a, b, (((1,), (1,)), ((), ())), precision=HIGH, preferred_element_type=F32)


class Chain:
    def __init__(self, place, came, sent, send, recv, backward):
        self.came, self.sent, self.send, self.recv = came, sent, send, recv
        self.gets, self.gives = place.has_left, place.has_right
        self.to = place.left if backward else place.right
        if backward:
            self.gets, self.gives = self.gives, self.gets
        self.behind = place.depth - 1 - place.z if backward else place.z

    def copy(self, g):
        return remote(self.sent.at[g], self.came.at[g], self.send.at[g], self.recv.at[g], self.to)

    def step(self, g, total, own):
        pl.when(self.gets)(lambda: self.copy(g).wait_recv())

        @pl.when(jnp.logical_not(self.gets))
        def _():
            self.came[g] = jnp.zeros(self.came.shape[1:], self.came.dtype)

        self.sent[g] = (total * self.came[g].astype(F32) + own).astype(BF16)
        pl.when(self.gives)(lambda: self.copy(g).start())

    def finish(self):
        groups = self.came.shape[0]

        def one(g, carry):
            self.copy(g).wait_send()
            return carry

        @pl.when(self.gives)
        def _():
            lax.fori_loop(0, groups, one, 0)


def scan_forward_kernel(
    depth, head_dim, groups,
    pc_ref, w_ref, b_ref, pcb_ref, wb_ref, bb_ref, raw_ref, sb_ref, dl_ref, skip_ref, normed_ref, cot_ref,
    gate_src, wo_src,
    bc_ref, dt_ref, cum_ref, cumt_ref, mixed_ref, s0_ref, s1_ref, s2_ref, tot_ref, z_out, dno_out, wg_out, wo_out,
    bt_ref, cb_ref, x_all, loc_all, seg_ring, tot_all, came, sent,
    z_ref, dno_ref, wg_ref, wo_ref, chain_send, chain_recv, own_sem, keep_sem, out_sem, send, recv,
):
    step = pl.program_id(0)
    lag = depth - 1
    seqs = pc_ref.shape[0]
    seg = pc_ref.shape[1] - EDGE
    chunks = seg // CHUNK
    heads = GROUP // head_dim
    place = Place(depth)
    chain = Chain(place, came, sent, chain_send, chain_recv, False)
    gate = LineGather(place, gate_src, lambda y, x, c: wg_ref.at[y, x, c], "y", "x", send.at[0], recv.at[0])
    out = Gather(place, wo_src, lambda y, x, c: wo_ref.at[y, x, c], "x", "y", send.at[1], recv.at[1])
    mine = (place.own["y"], place.own["x"], place.own["c"], place.z)
    copies = [
        pltpu.make_async_copy(gate_src, wg_ref.at[mine[:3]], own_sem.at[0]),
        pltpu.make_async_copy(wo_src, wo_ref.at[mine], own_sem.at[1]),
    ]

    def waves(*steps):
        for lane, name, k in steps:
            getattr(lane, name)(k)

    def acts_of(s, refs, j=0):
        part, w, b = refs
        cols = slice(j * GROUP, (j + 1) * GROUP)
        pre = causal_conv(part[s, :, cols], w[:, cols], b[:, cols], seg)
        return pre * sigmoid(pre)

    @pl.when(step == 0)
    def _():
        place.meet()
        waves(*((gate, "line", k) for k in range(depth)))
        for copy in copies:
            copy.start()
        row = lax.broadcasted_iota(jnp.int32, (CHUNK, CHUNK), 0)
        col = lax.broadcasted_iota(jnp.int32, (CHUNK, CHUNK), 1)
        tri = (col <= row).astype(F32)
        rate = -jnp.exp(dl_ref[...])
        for s in range(seqs):
            acts = acts_of(s, (pcb_ref, wb_ref, bb_ref))
            bc_ref[s * seg : (s + 1) * seg] = acts
            for c in range(chunks):
                q = s * chunks + c
                rows = slice(q * CHUNK, (q + 1) * CHUNK)
                b_proj = acts[c * CHUNK : (c + 1) * CHUNK, :LANES]
                c_proj = acts[c * CHUNK : (c + 1) * CHUNK, LANES:]
                bt_ref[q] = b_proj.T
                cb_ref[q] = nt_exact(c_proj, b_proj)
                dt = softplus(raw_ref[s, EDGE + c * CHUNK : EDGE + (c + 1) * CHUNK] + sb_ref[...])
                cum = LOG2E * jnp.dot(tri, dt * rate, precision=HIGH, preferred_element_type=F32)
                dt_ref[rows] = dt
                cum_ref[rows] = cum
                cumt_ref[:, rows] = cum.T

    slots = seg_ring.shape[0]

    def local_states(g, j):
        first = g * heads
        cumg = lane_shift(cum_ref[...], first)
        dtg = lane_shift(dt_ref[...], first)
        for s in range(seqs):
            x = acts_of(s, (pc_ref, w_ref, b_ref), j)
            x_all[g, s * seg : (s + 1) * seg] = x
            state, total = None, None
            for c in range(chunks):
                q = s * chunks + c
                rows = slice(q * CHUNK, (q + 1) * CHUNK)
                ce = spread_all(cumg[rows], heads, head_dim)
                de = spread_all(dtg[rows], heads, head_dim)
                end = ce[CHUNK - 1 : CHUNK]
                uw = x[c * CHUNK : (c + 1) * CHUNK] * de * jnp.exp2(end - ce)
                loc = dot_pairs(bt_ref[q], uw)
                tot = jnp.exp2(end)
                tot_all[g, q : q + 1] = tot
                if c == 0:
                    loc_all[g, s] = loc
                    state, total = loc, tot
                else:
                    state, total = tot * state + loc, tot * total
            seg_ring[lax.rem(g, slots), s] = state
            tot_all[g, seqs * chunks + s : seqs * chunks + s + 1] = total

    @pl.when((step > 0) & (step <= groups // 2))
    def _():
        for j in (0, 1):
            local_states(2 * (step - 1) + j, j)

    handed = step - 1 - chain.behind

    @pl.when((handed >= 0) & (handed < groups // 2))
    def _():
        for j in (0, 1):
            g = 2 * handed + j
            totals = tot_all[g, seqs * chunks : seqs * chunks + seqs]
            chain.step(g, totals[:, None, :], seg_ring[lax.rem(g, slots)])

    @pl.when(step > lag)
    def _():
        g = step - 1 - lag
        first = g * heads
        cumg = lane_shift(cum_ref[...], first)
        dtg = lane_shift(dt_ref[...], first)
        cumr = head_rows(cumt_ref, first)
        row = lax.broadcasted_iota(jnp.int32, (CHUNK, CHUNK), 0)
        col = lax.broadcasted_iota(jnp.int32, (CHUNK, CHUNK), 1)
        causal = col <= row
        skip = skip_row(skip_ref, first, heads, head_dim)
        s0_ref[...] = came[g]
        s2_ref[...] = sent[g]
        tot_ref[...] = tot_all[g]
        for s in range(seqs):
            start = came[g, s]
            for c in range(chunks):
                q = s * chunks + c
                rows = slice(q * CHUNK, (q + 1) * CHUNK)
                x = x_all[g, rows]
                ce = spread_all(cumg[rows], heads, head_dim)
                de = spread_all(dtg[rows], heads, head_dim)
                ub = (x * de).astype(BF16)
                cb = cb_ref[q]
                parts = []
                for j in range(0, heads, 2):
                    mats = []
                    for h in (j, j + 1):
                        there = jnp.broadcast_to(cumg[rows, h : h + 1], (CHUNK, CHUNK))
                        here = cumr[h : h + 1, rows]
                        decay = jnp.exp2(jnp.where(causal, there - here, -jnp.inf))
                        mats.append((decay * cb).astype(BF16))
                    pair = ub[:, j * head_dim : (j + 2) * head_dim]
                    parts.append(dot(jnp.concatenate(mats, axis=1), block_diagonal(pair, head_dim)))
                y = jnp.concatenate(parts, axis=1)
                y = y + jnp.exp2(ce) * dot(bc_ref[rows, LANES:].astype(BF16), start)
                mixed_ref[rows] = y + skip * x
                if c == 0:
                    later = tot_all[g, q : q + 1] * start.astype(F32) + loc_all[g, s]
                    s1_ref[s] = later
                    start = later.astype(BF16)

    every = range(depth)
    by_group = ((), ("y",), ("x",), ("y", "x"))

    def both(lane, *waves_of):
        return [(lane, name, k) for k in waves_of for name in ("from_first", "from_second")]

    beside = {
        4: [(out, "line", 0), *both(gate, 0)],
        7: [(out, "line", 1), *both(gate, 1)],
        10: [(out, "line", 2)],
        13: [(out, "line", 3), (out, "core", 0)],
        14: [*both(gate, 2, 3), (gate, "core", 1), (gate, "core", 2)],
    }
    for at, steps in beside.items():
        pl.when(step == at)(lambda: waves(*steps))

    @pl.when(step == 2)
    def _():
        for copy in copies:
            copy.wait()
        waves((gate, "core", 0))

    @pl.when(step == groups + lag)
    def _():
        rows = 2 * depth * gate_src.shape[1]
        tile = 4 * LANES
        size = dno_ref.shape[1] // 8

        def keep(lane, g):
            src, dst = (wg_ref, wg_out) if lane is gate else (wo_ref, wo_out)
            at = place.flipped(*by_group[g])
            return pltpu.make_async_copy(
                src.at[at["y"], at["x"]], dst.at[at["y"], at["x"]], keep_sem.at[int(lane is out), g]
            )

        def ready(lane, g):
            lane.whole(g if g in (0, 3) or lane is gate else 3 - g)
            keep(lane, g).start()

        def group_of(g):
            at = place.flipped(*by_group[g])
            return 2 * at["y"] + at["x"]

        def gate_product(g):
            at = place.flipped(*by_group[g])
            here = pl.ds(pl.multiple_of(group_of(g) * rows, LANES), rows)
            for start in range(0, z_ref.shape[1], tile):
                cols = slice(start, start + tile)
                block = jnp.concatenate(
                    [wg_ref[at["y"], at["x"], c, z, :, cols] for c in (0, 1) for z in every], axis=0
                )
                for s in range(seqs):
                    part = dot(normed_ref[s, EDGE:, here], block)
                    at_rows = slice(s * seg, (s + 1) * seg)
                    if g == 0:
                        z_ref[at_rows, cols] = part
                    else:
                        z_ref[at_rows, cols] += part

        def out_product(g):
            at = place.flipped(*by_group[g])
            for c in (0, 1):
                block = jnp.concatenate([wo_ref[at["y"], at["x"], c, z] for z in every], axis=0)
                cols = pl.ds(pl.multiple_of((2 * group_of(g) + c) * size, LANES), size)
                dno_ref[:, cols] = nt(cot_ref[...], block)
            dno_copy(g).start()

        def dno_copy(g):
            cols = pl.ds(pl.multiple_of(group_of(g) * 2 * size, LANES), 2 * size)
            return pltpu.make_async_copy(dno_ref.at[:, cols], dno_out.at[:, cols], out_sem.at[g])

        last = depth - 1
        waves((out, "from_first", 0), (out, "from_first", 1))
        ready(gate, 0)
        gate_product(0)
        waves(*((out, "from_first", k) for k in range(2, last)))
        ready(gate, 1)
        gate_product(1)
        waves((out, "from_first", last), *((out, "from_second", k) for k in every))
        waves((out, "core", 1), (out, "core", 2))
        ready(gate, 2)
        gate_product(2)
        waves((gate, "from_both", 0), (out, "from_both", 0))
        ready(out, 0)
        out_product(0)
        waves((gate, "from_both", 1), (out, "from_both", 1))
        ready(out, 1)
        out_product(1)
        waves((gate, "from_both", 2), (out, "from_both", 2))
        ready(out, 2)
        out_product(2)
        waves((gate, "from_both", last), (out, "from_both", last))
        ready(gate, 3)
        gate_product(3)
        z_copy = pltpu.make_async_copy(z_ref, z_out, out_sem.at[4])
        z_copy.start()
        ready(out, 3)
        out_product(3)
        for lane in (gate, out):
            lane.finish()
        chain.finish()
        for g in range(4):
            dno_copy(g).wait()
            keep(gate, g).wait()
            keep(out, g).wait()
        z_copy.wait()


def scan_forward(pc, w, b, sb, dl, skip, normed, cot, gate_line, wo, inner, head_dim, depth):
    seqs, rows, cols = pc.shape
    tokens = seqs * (rows - EDGE)
    groups = inner // GROUP
    lag = depth - 1
    chunks = tokens // CHUNK
    shape, dma = jax.ShapeDtypeStruct, pltpu.SemaphoreType.DMA
    into = lambda i: jnp.clip(i - 1, 0, groups // 2 - 1)
    out = lambda i: jnp.maximum(i - 1 - lag, 0)
    states = pl.BlockSpec((seqs, LANES, GROUP), lambda i: (0, 0, out(i)))
    anywhere = pl.BlockSpec(memory_space=pl.ANY)
    sends, receives = Gather.sems(depth)
    slots = (2, 2, 2, depth)
    link = pltpu.VMEM((groups, seqs, LANES, GROUP), BF16)
    once = lambda v: pl.BlockSpec(v.shape, lambda i: (0,) * v.ndim, pipeline_mode=pl.Buffered(1))
    return pl.pallas_call(
        functools.partial(scan_forward_kernel, depth, head_dim, groups),
        grid=(groups + 1 + lag,),
        in_specs=[
            pl.BlockSpec((seqs, rows, 2 * GROUP), lambda i: (0, 0, into(i))),
            pl.BlockSpec((w.shape[0], 2 * GROUP), lambda i: (0, into(i))),
            pl.BlockSpec((1, 2 * GROUP), lambda i: (0, into(i))),
            pl.BlockSpec((seqs, rows, GROUP), lambda i: (0, 0, groups), pipeline_mode=pl.Buffered(1)),
            pl.BlockSpec((w.shape[0], GROUP), lambda i: (0, groups)),
            pl.BlockSpec((1, GROUP), lambda i: (0, groups)),
            pl.BlockSpec((seqs, rows, LANES), lambda i: (0, 0, cols // LANES - 1)),
            whole((1, LANES)),
            whole((1, LANES)),
            whole((1, LANES)),
            once(normed),
            once(cot),
            once(gate_line),
            once(wo),
        ],
        out_specs=[
            whole((tokens, GROUP)),
            whole((tokens, LANES)),
            whole((tokens, LANES)),
            whole((LANES, tokens)),
            pl.BlockSpec((tokens, GROUP), lambda i: (0, out(i))),
            states, states, states,
            pl.BlockSpec((8, GROUP), lambda i: (0, out(i))),
            anywhere,
            anywhere,
            anywhere,
            anywhere,
        ],
        out_shape=[
            shape((tokens, GROUP), F32),
            shape((tokens, LANES), F32),
            shape((tokens, LANES), F32),
            shape((LANES, tokens), F32),
            shape((tokens, inner), F32),
            shape((seqs, LANES, inner), BF16),
            shape((seqs, LANES, inner), F32),
            shape((seqs, LANES, inner), BF16),
            shape((8, inner), F32),
            shape((tokens, inner), F32),
            shape((tokens, inner), F32),
            shape(slots + gate_line.shape[1:], BF16),
            shape(slots + wo.shape, BF16),
        ],
        scratch_shapes=[
            pltpu.VMEM((chunks, LANES, CHUNK), F32),
            pltpu.VMEM((chunks, CHUNK, CHUNK), F32),
            pltpu.VMEM((groups, tokens, GROUP), F32), pltpu.VMEM((groups, seqs, LANES, GROUP), F32),
            pltpu.VMEM((2 * lag + 2, seqs, LANES, GROUP), F32), pltpu.VMEM((groups, 8, GROUP), F32),
            link, link,
            pltpu.VMEM((tokens, inner), F32), pltpu.VMEM((tokens, inner), F32),
            pltpu.VMEM(slots + gate_line.shape[1:], BF16), pltpu.VMEM(slots + wo.shape, BF16),
            dma((groups,)), dma((groups,)), dma((2,)), dma((2, 4)), dma((5,)), dma((2, sends)), dma((2, receives)),
        ],
        compiler_params=pltpu.CompilerParams(
            dimension_semantics=("arbitrary",), collective_id=3, has_side_effects=True,
            vmem_limit_bytes=VMEM_LIMIT,
        ),
        name="scan_forward",
    )(pc, w, b, pc, w, b, pc, sb, dl, skip, normed, cot, gate_line, wo)


def mid_kernel(
    z_ref, dno_ref, mixed_ref, wo_ref, gain_ref, in_ref, not_ref, out_ref, dm_ref, dz_ref, gg_ref, acc_ref,
):
    step = pl.program_id(0)
    inner = mixed_ref.shape[1]
    tiles, tile = not_ref.shape[0], not_ref.shape[1]

    @pl.when(step == 0)
    def _():
        gg_ref[...] = jnp.zeros_like(gg_ref)

    def lanes_of(i):
        return pl.ds(pl.multiple_of(i * tile, tile), tile)

    def fold(v):
        total = v[:, :LANES]
        for k in range(LANES, tile, LANES):
            total = total + v[:, k : k + LANES]
        return total

    def one(i, sums):
        sq, hg = sums
        at = lanes_of(i)
        z = z_ref[:, at]
        g = mixed_ref[:, at] * z * sigmoid(z)
        return sq + fold(g * g), hg + fold(dno_ref[:, at] * gain_ref[:, at] * g)

    zero = jnp.zeros((mixed_ref.shape[0], LANES), F32)
    sq, hg = lax.fori_loop(0, tiles, one, (zero, zero))
    scale = lax.rsqrt(jnp.sum(sq, axis=1, keepdims=True) / inner + EPS)
    pull = scale * scale * scale * (jnp.sum(hg, axis=1, keepdims=True) / inner)
    acc_ref[...] = in_ref[...].astype(F32)

    def two(i, carry):
        at = lanes_of(i)
        z, mixed, dno, gain = z_ref[:, at], mixed_ref[:, at], dno_ref[:, at], gain_ref[:, at]
        sig = sigmoid(z)
        act = z * sig
        g = mixed * act
        gs = g * scale
        no = gs * gain
        not_ref[i] = no.T.astype(BF16)
        acc_ref[...] += dot(no.astype(BF16), wo_ref[at, :])
        gg_ref[:, at] += jnp.sum(dno * gs, axis=0, keepdims=True)
        dg = scale * (dno * gain) - g * pull
        dm_ref[:, at] = dg * act
        dz_ref[:, at] = (dg * mixed * (sig * (1.0 + z * (1.0 - sig)))).astype(BF16)
        return carry

    lax.fori_loop(0, tiles, two, 0)
    out_ref[...] = acc_ref[...].astype(BF16)


def mid(z, dno, mixed, wo, gain, inputs, tiles):
    tokens, inner = mixed.shape
    width = inputs.shape[1]
    tile = inner // tiles
    narrow = pl.BlockSpec((CHUNK, width), lambda i: (i, 0))
    wide = pl.BlockSpec((CHUNK, inner), lambda i: (i, 0))
    once = lambda v: pl.BlockSpec(v.shape, lambda i: (0,) * v.ndim, pipeline_mode=pl.Buffered(1))
    return pl.pallas_call(
        mid_kernel,
        grid=(tokens // CHUNK,),
        in_specs=[wide, wide, wide, once(wo), whole((1, inner)), narrow],
        out_specs=[
            pl.BlockSpec((tiles, tile, CHUNK), lambda i: (0, 0, i)), narrow, wide, wide,
            whole((1, inner)),
        ],
        out_shape=[
            jax.ShapeDtypeStruct((tiles, tile, tokens), BF16),
            jax.ShapeDtypeStruct((tokens, width), BF16),
            jax.ShapeDtypeStruct((tokens, inner), F32),
            jax.ShapeDtypeStruct((tokens, inner), BF16),
            jax.ShapeDtypeStruct((1, inner), F32),
        ],
        scratch_shapes=[pltpu.VMEM((CHUNK, width), F32)],
        compiler_params=params(),
        name="gate_norm_project",
    )(z, dno, mixed, wo, gain, inputs)


def bwd_a_kernel(head_dim, seqs, dm_ref, bc_ref, cum_ref, tot_ref, seg_ref, ct_ref):
    step = pl.program_id(0)
    chunks = dm_ref.shape[0] // CHUNK // seqs
    heads = GROUP // head_dim

    @pl.when(step == 0)
    def _():
        for q in range(seqs * chunks):
            ct_ref[q] = bc_ref[q * CHUNK : (q + 1) * CHUNK, LANES:].T.astype(BF16)

    cumg = lane_shift(cum_ref[...], step * heads)
    for s in range(seqs):
        state = None
        for c in range(chunks - 1, -1, -1):
            q = s * chunks + c
            rows = slice(q * CHUNK, (q + 1) * CHUNK)
            ey = jnp.exp2(spread_all(cumg[rows], heads, head_dim)) * dm_ref[rows]
            loc = dot(ct_ref[q], ey.astype(BF16))
            state = loc if state is None else tot_ref[q : q + 1] * state + loc
        seg_ref[s] = state.astype(BF16)


def bwd_a(dm, bc, cum, tot, seqs, head_dim):
    tokens, inner = dm.shape
    return pl.pallas_call(
        functools.partial(bwd_a_kernel, head_dim, seqs),
        grid=(inner // GROUP,),
        in_specs=[
            pl.BlockSpec((tokens, GROUP), lambda i: (0, i)), whole(bc.shape), whole(cum.shape),
            pl.BlockSpec((8, GROUP), lambda i: (0, i)),
        ],
        out_specs=pl.BlockSpec((seqs, LANES, GROUP), lambda i: (0, 0, i)),
        out_shape=jax.ShapeDtypeStruct((seqs, LANES, inner), BF16),
        scratch_shapes=[pltpu.VMEM((tokens // CHUNK, LANES, CHUNK), BF16)],
        compiler_params=params(),
        name="adjoint_states",
    )(dm, bc, cum, tot)


def bwd_b_kernel(
    head_dim, groups, pc_ref, w_ref, b_ref, raw_ref, sb_ref, dl_ref, bc_ref, dt_ref, cum_ref, cumt_ref,
    dm_ref, mixed_ref, s0_ref, s1_ref, s2_ref, g_ref, tot_ref, skip_ref,
    dc_ref, tail_ref, edge_ref, gw_ref, gb_ref, gskip_ref, draw_ref, hsum_ref,
    cbt_ref, dcbt_ref, db_acc, dc_acc, r1_ref, r2_ref, dtot_ref,
):
    step = pl.program_id(0)
    seqs = pc_ref.shape[0]
    seg = pc_ref.shape[1] - EDGE
    chunks = seg // CHUNK
    heads = GROUP // head_dim
    w, b = w_ref[...], b_ref[...]
    taps = w.shape[0]

    @pl.when(step == 0)
    def _():
        for q in range(seqs * chunks):
            rows = slice(q * CHUNK, (q + 1) * CHUNK)
            cbt_ref[q] = nt(bc_ref[rows, :LANES].astype(BF16), bc_ref[rows, LANES:].astype(BF16))
        dcbt_ref[...] = jnp.zeros_like(dcbt_ref)
        db_acc[...] = jnp.zeros_like(db_acc)
        dc_acc[...] = jnp.zeros_like(dc_acc)
        r1_ref[...] = jnp.zeros_like(r1_ref)
        r2_ref[...] = jnp.zeros_like(r2_ref)
        dtot_ref[...] = jnp.zeros_like(dtot_ref)

    def conv_back(s, ext, pre, sig, d_act):
        d_pre = d_act * (sig * (1.0 + pre * (1.0 - sig)))
        zero = jnp.zeros((EDGE, d_pre.shape[1]), F32)
        padded = jnp.concatenate([zero, d_pre, zero], axis=0)
        total = None
        for k in range(taps):
            at = taps - 1 - k
            term = w[k : k + 1] * padded[at : at + seg + EDGE]
            total = term if total is None else total + term
        edge_ref[s] = total[:EDGE]
        dc_ref[s * seg : (s + 1) * seg] = total[EDGE:].astype(BF16)
        tail_ref[s] = total[seg:]
        for k in range(taps):
            at = EDGE - (taps - 1) + k
            grad = jnp.sum(ext[at : at + seg] * d_pre, axis=0, keepdims=True)
            gw_ref[k : k + 1] = grad if s == 0 else gw_ref[k : k + 1] + grad
        grad = jnp.sum(d_pre, axis=0, keepdims=True)
        gb_ref[...] = grad if s == 0 else gb_ref[...] + grad

    def by_head(value, pick):
        high = value.astype(BF16)
        return dot(high, pick) + dot((value - high.astype(F32)).astype(BF16), pick)

    @pl.when(step < groups)
    def _():
        first = step * heads
        cumg = lane_shift(cum_ref[...], first)
        dtg = lane_shift(dt_ref[...], first)
        cumr = head_rows(cumt_ref, first)
        row = lax.broadcasted_iota(jnp.int32, (CHUNK, CHUNK), 0)
        col = lax.broadcasted_iota(jnp.int32, (CHUNK, CHUNK), 1)
        causal = row <= col
        lane = lax.broadcasted_iota(jnp.int32, (GROUP, LANES), 0)
        head = lax.broadcasted_iota(jnp.int32, (GROUP, LANES), 1)
        pick = (head == first + lane // head_dim).astype(BF16)
        skip = skip_ref[...]
        grad_skip = None
        for s in range(seqs):
            ext = pc_ref[s]
            pre = causal_conv(ext, w, b, seg)
            sig = sigmoid(pre)
            acts = pre * sig
            adj = g_ref[s].astype(F32)
            d_acts = [None] * chunks
            for c in range(chunks - 1, -1, -1):
                q = s * chunks + c
                rows = slice(q * CHUNK, (q + 1) * CHUNK)
                x = acts[c * CHUNK : (c + 1) * CHUNK]
                dy = dm_ref[rows]
                ce = spread_all(cumg[rows], heads, head_dim)
                de = spread_all(dtg[rows], heads, head_dim)
                weight = jnp.exp2(ce[CHUNK - 1 : CHUNK] - ce)
                u = x * de
                ub = u.astype(BF16)
                dyb = dy.astype(BF16)
                cbt = cbt_ref[q]
                parts = []
                dcbt = dcbt_ref[q]
                for j in range(0, heads, 2):
                    lanes = slice(j * head_dim, (j + 2) * head_dim)
                    dy_block = block_diagonal(dyb[:, lanes], head_dim)
                    dm = nt(ub[:, lanes], dy_block)
                    mats = []
                    for k, h in enumerate((j, j + 1)):
                        here = jnp.broadcast_to(cumg[rows, h : h + 1], (CHUNK, CHUNK))
                        there = cumr[h : h + 1, rows]
                        decay = jnp.exp2(jnp.where(causal, there - here, -jnp.inf))
                        mats.append((decay * cbt).astype(BF16))
                        dcbt = dcbt + decay * dm[:, k * CHUNK : (k + 1) * CHUNK]
                    parts.append(dot(jnp.concatenate(mats, axis=1), dy_block))
                dcbt_ref[q] = dcbt
                start = s0_ref[s] if c == 0 else s1_ref[s]
                end = s2_ref[s] if c == chunks - 1 else s1_ref[s]
                adj_b = adj.astype(BF16)
                bb = bc_ref[rows, :LANES].astype(BF16)
                cb = bc_ref[rows, LANES:].astype(BF16)
                ey = (jnp.exp2(ce) * dy).astype(BF16)
                du = jnp.concatenate(parts, axis=1) + weight * dot(bb, adj_b)
                db_acc[rows] += nt((u * weight).astype(BF16), adj_b)
                dc_acc[rows] += nt(ey, start)
                r1_ref[rows] += by_head(dyb.astype(F32) * (mixed_ref[rows] - skip * x), pick)
                r2_ref[rows] += by_head(x * du, pick)
                dtot_ref[q : q + 1] += by_head(
                    jnp.sum(adj * end.astype(F32), axis=0, keepdims=True), pick
                )
                grad = jnp.sum(dy * x, axis=0, keepdims=True)
                grad_skip = grad if grad_skip is None else grad_skip + grad
                d_acts[c] = du * de + skip * dy
                if c > 0:
                    adj = tot_ref[q : q + 1] * adj + dot(cb, ey, ((0,), (0,)))
            conv_back(s, ext, pre, sig, jnp.concatenate(d_acts, axis=0))
        gskip_ref[...] = grad_skip

    @pl.when(step == groups)
    def _():
        row = lax.broadcasted_iota(jnp.int32, (CHUNK, CHUNK), 0)
        col = lax.broadcasted_iota(jnp.int32, (CHUNK, CHUNK), 1)
        later = (row <= col).astype(F32)
        rate = -jnp.exp(dl_ref[...])
        sum_raw = jnp.zeros((1, LANES), F32)
        sum_log = jnp.zeros((1, LANES), F32)
        for s in range(seqs):
            ext = pc_ref[s]
            pre = causal_conv(ext, w, b, seg)
            sig = sigmoid(pre)
            parts = []
            for c in range(chunks):
                q = s * chunks + c
                rows = slice(q * CHUNK, (q + 1) * CHUNK)
                dcbt = dcbt_ref[q]
                bb = bc_ref[rows, :LANES].astype(BF16)
                cb = bc_ref[rows, LANES:].astype(BF16)
                d_b = db_acc[rows] + dot(dcbt.astype(BF16), cb)
                d_c = dc_acc[rows] + dot(dcbt.T.astype(BF16), bb)
                parts.append(jnp.concatenate([d_b, d_c], axis=1))
                dt = dt_ref[rows]
                r2 = r2_ref[rows]
                d_log = jnp.dot(
                    later, r1_ref[rows] - dt * r2, precision=HIGH, preferred_element_type=F32
                )
                d_log = d_log + dtot_ref[q : q + 1]
                raw = raw_ref[s, EDGE + c * CHUNK : EDGE + (c + 1) * CHUNK] + sb_ref[...]
                d_raw = (r2 + rate * d_log) * sigmoid(raw)
                draw_ref[rows] = d_raw
                sum_raw = sum_raw + jnp.sum(d_raw, axis=0, keepdims=True)
                sum_log = sum_log + jnp.sum(d_log * dt, axis=0, keepdims=True) * rate
            conv_back(s, ext, pre, sig, jnp.concatenate(parts, axis=0))
        hsum_ref[0:1] = sum_raw
        hsum_ref[1:2] = sum_log


def bwd_b(pc, w, b, sb, dl, bc, dt, cum, cumt, dm, mixed, s0, s1, s2, g, tot, skip, head_dim):
    seqs, rows, cols = pc.shape
    tokens, inner = dm.shape
    groups = inner // GROUP
    taps, channels = w.shape
    wide = pl.BlockSpec((tokens, GROUP), lambda i: (0, jnp.minimum(i, groups - 1)))
    states = pl.BlockSpec((seqs, LANES, GROUP), lambda i: (0, 0, jnp.minimum(i, groups - 1)))
    line = lambda n: pl.BlockSpec((n, GROUP), lambda i: (0, jnp.minimum(i, groups - 1)))
    conv = lambda n: pl.BlockSpec((n, GROUP), lambda i: (0, i))
    ends = pl.BlockSpec((seqs, EDGE, GROUP), lambda i: (0, 0, i))
    chunks = tokens // CHUNK
    shape = jax.ShapeDtypeStruct
    return pl.pallas_call(
        functools.partial(bwd_b_kernel, head_dim, groups),
        grid=(groups + 1,),
        in_specs=[
            pl.BlockSpec((seqs, rows, GROUP), lambda i: (0, 0, i)),
            conv(taps),
            conv(1),
            pl.BlockSpec((seqs, rows, LANES), lambda i: (0, 0, cols // LANES - 1)),
            whole((1, LANES)), whole((1, LANES)),
            whole(bc.shape), whole(dt.shape), whole(cum.shape), whole(cumt.shape),
            wide, wide, states, states, states, states, line(8), line(1),
        ],
        out_specs=[
            conv(tokens), ends, ends, conv(taps), conv(1), line(1),
            whole((tokens, LANES)), whole((2, LANES)),
        ],
        out_shape=[
            shape((tokens, channels), BF16),
            shape((seqs, EDGE, channels), F32),
            shape((seqs, EDGE, channels), F32),
            shape((taps, channels), F32),
            shape((1, channels), F32),
            shape((1, inner), F32),
            shape((tokens, LANES), F32),
            shape((2, LANES), F32),
        ],
        scratch_shapes=[
            pltpu.VMEM((chunks, CHUNK, CHUNK), F32),
            pltpu.VMEM((chunks, CHUNK, CHUNK), F32),
            pltpu.VMEM((tokens, LANES), F32),
            pltpu.VMEM((tokens, LANES), F32),
            pltpu.VMEM((tokens, LANES), F32),
            pltpu.VMEM((tokens, LANES), F32),
            pltpu.VMEM((8, LANES), F32),
        ],
        compiler_params=params(),
        name="scan_backward",
    )(pc, w, b, pc, sb, dl, bc, dt, cum, cumt, dm, mixed, s0, s1, s2, g, tot, skip)


PIECES = (3, 2, 1)


def piece_of(columns, n):
    unit = columns // sum(PIECES)
    return sum(PIECES[:n]) * unit, sum(PIECES[: n + 1]) * unit


def pair_copies(place, lhs, rhs, send, recv):
    other = 1 - place.own["c"]
    parts = [(src.at[2 * g + other], dst.at[g]) for src, dst in lhs for g in range(4)] + list(rhs)
    return [
        remote(src, dst, send.at[n], recv.at[n], place.to["c"]) for n, (src, dst) in enumerate(parts)
    ]


def scan_backward_kernel(
    depth, head_dim, groups,
    pc_ref, w_ref, b_ref, raw_ref, sb_ref, dl_ref, bc_ref, dt_ref, cum_ref, cumt_ref,
    dma_ref, dm_ref, mixed_ref, s0_ref, s1_ref, s2_ref, tot_ref, skip_ref,
    nt_src, dz_src, no_src, cot_src,
    dc_out, gw_ref, gb_ref, hsum_ref, a_out, b_out, nt_out,
    cbt_ref, ct_ref, dcbt_ref, db_acc, dc_acc, r1_ref, r2_ref, dtot_ref, skip_acc,
    dc_ref, tail_ref, edge_ref, edge_came, seg_ring, tot_all, came, sent,
    nt_pair, dz_pair, no_pair, cot_pair,
    chain_send, chain_recv, edge_send, edge_recv, pair_send, pair_recv, out_sem, send, recv, *bufs,
):
    step = pl.program_id(0)
    lag = depth - 1
    seqs = pc_ref.shape[0]
    seg = pc_ref.shape[1] - EDGE
    chunks = seg // CHUNK
    heads = GROUP // head_dim
    w, b = w_ref[...], b_ref[...]
    taps = w.shape[0]
    channels = tail_ref.shape[2]
    place = Place(depth)
    chain = Chain(place, came, sent, chain_send, chain_recv, True)
    cut = lambda ref, lo, hi: ref.at[:, pl.ds(lo, hi - lo)]
    rhs = []
    for n in range(2):
        for src, dst in ((dz_src, dz_pair), (cot_src, cot_pair)):
            lo, hi = piece_of(src.shape[1], n)
            hi = hi if n == 0 else src.shape[1]
            rhs.append((cut(src, lo, hi), cut(dst, lo, hi)))
    pairs = pair_copies(place, ((nt_src, nt_pair), (no_src, no_pair)), rhs, pair_send, pair_recv)
    def piece(ref, n):
        lo, hi = piece_of(ref.shape[1], n)
        return ref.at[:, pl.ds(lo, hi - lo)]

    lanes = []
    for n in range(len(PIECES)):
        lanes += [
            Scatter(place, nt_src, nt_pair, piece(dz_src, n), piece(dz_pair, n), "y", "x",
                    bufs[14 * n : 14 * n + 7], send.at[2 * n], recv.at[2 * n]),
            Scatter(place, no_src, no_pair, piece(cot_src, n), piece(cot_pair, n), "x", "y",
                    bufs[14 * n + 7 : 14 * n + 14], send.at[2 * n + 1], recv.at[2 * n + 1]),
        ]
    edges = [
        remote(edge_ref.at[:, :, cols], edge_came.at[:, :, cols], edge_send.at[n], edge_recv.at[n], place.left)
        for n, cols in enumerate((pl.ds(0, channels - GROUP), pl.ds(channels - GROUP, GROUP)))
    ]
    outs = [
        pltpu.make_async_copy(src, dst, out_sem.at[n])
        for n, (src, dst) in enumerate(((nt_pair, nt_out), (dc_ref, dc_out)))
    ]

    def run(first, name, *rest):
        for lane in lanes[2 * first : 2 * first + 2]:
            getattr(lane, name)(*rest)

    def at_step(n, *what):
        pl.when(step == n)(lambda: run(*what))

    @pl.when(step == 0)
    def _():
        place.meet(line=True)
        for copy in pairs:
            copy.start()
        for q in range(seqs * chunks):
            rows = slice(q * CHUNK, (q + 1) * CHUNK)
            b_proj, c_proj = bc_ref[rows, :LANES], bc_ref[rows, LANES:]
            cbt_ref[q] = nt_exact(b_proj, c_proj)
            ct_ref[q] = c_proj.T
        dcbt_ref[...] = jnp.zeros_like(dcbt_ref)
        db_acc[...] = jnp.zeros_like(db_acc)
        dc_acc[...] = jnp.zeros_like(dc_acc)
        r1_ref[...] = jnp.zeros_like(r1_ref)
        r2_ref[...] = jnp.zeros_like(r2_ref)
        skip_acc[...] = jnp.zeros_like(skip_acc)
        dtot_ref[...] = jnp.zeros_like(dtot_ref)

    slots = seg_ring.shape[0]

    @pl.when(step < groups // 2)
    def _():
        for j in (0, 1):
            g = 2 * step + j
            cols = slice(j * GROUP, (j + 1) * GROUP)
            cumg = lane_shift(cum_ref[...], g * heads)
            tot_all[g] = tot_ref[:, cols]
            for s in range(seqs):
                state = None
                for c in range(chunks - 1, -1, -1):
                    q = s * chunks + c
                    rows = slice(q * CHUNK, (q + 1) * CHUNK)
                    ey = jnp.exp2(spread_all(cumg[rows], heads, head_dim)) * dma_ref[rows, cols]
                    loc = dot_pairs(ct_ref[q], ey)
                    state = loc if state is None else tot_ref[q : q + 1, cols] * state + loc
                seg_ring[lax.rem(g, slots), s] = state

    handed = step - chain.behind

    @pl.when((handed >= 0) & (handed < groups // 2))
    def _():
        for j in (0, 1):
            g = 2 * handed + j
            totals = tot_all[g, seqs * chunks : seqs * chunks + seqs]
            chain.step(g, totals[:, None, :], seg_ring[lax.rem(g, slots)])

    @pl.when(step == lag)
    def _():
        for copy in pairs[:10]:
            copy.wait_recv()
        outs[0].start()

    @pl.when(step == lag + 2)
    def _():
        for copy in pairs[10:]:
            copy.wait_recv()

    at_step(lag, 0, "send_second")
    at_step(lag + 2, 1, "send_second")
    at_step(lag + 3, 0, "send_first")
    at_step(lag + 5, 2, "send_second")
    at_step(lag + 6, 0, "hold")
    at_step(lag + 8, 1, "send_first")
    for k in range(depth - 1, 0, -1):
        at_step(lag + (9 if k > 1 else 10), 0, "step", k)
    at_step(lag + 11, 1, "hold")

    def conv_back(s, ext, pre, sig, d_act, at):
        lanes_at = pl.ds(pl.multiple_of(at * GROUP, GROUP), GROUP)
        d_pre = d_act * (sig * (1.0 + pre * (1.0 - sig)))
        zero = jnp.zeros((EDGE, d_pre.shape[1]), F32)
        padded = jnp.concatenate([zero, d_pre, zero], axis=0)
        total = None
        for k in range(taps):
            start = taps - 1 - k
            term = w[k : k + 1] * padded[start : start + seg + EDGE]
            total = term if total is None else total + term
        edge_ref[s, :, lanes_at] = total[:EDGE].astype(BF16)
        dc_ref[s * seg : (s + 1) * seg, lanes_at] = total[EDGE:].astype(BF16)
        tail_ref[s, :, lanes_at] = total[seg:]
        for k in range(taps):
            start = EDGE - (taps - 1) + k
            grad = jnp.sum(ext[start : start + seg] * d_pre, axis=0, keepdims=True)
            gw_ref[k : k + 1] = grad if s == 0 else gw_ref[k : k + 1] + grad
        grad = jnp.sum(d_pre, axis=0, keepdims=True)
        gb_ref[...] = grad if s == 0 else gb_ref[...] + grad

    def by_head(value, pick):
        high = value.astype(BF16)
        return dot(high, pick) + dot((value - high.astype(F32)).astype(BF16), pick)

    @pl.when((step >= lag) & (step < lag + groups))
    def _():
        g = step - lag
        first = g * heads
        cumg = lane_shift(cum_ref[...], first)
        dtg = lane_shift(dt_ref[...], first)
        cumr = head_rows(cumt_ref, first)
        row = lax.broadcasted_iota(jnp.int32, (CHUNK, CHUNK), 0)
        col = lax.broadcasted_iota(jnp.int32, (CHUNK, CHUNK), 1)
        causal = row <= col
        lane = lax.broadcasted_iota(jnp.int32, (GROUP, LANES), 0)
        head = lax.broadcasted_iota(jnp.int32, (GROUP, LANES), 1)
        pick = (head == first + lane // head_dim).astype(BF16)
        skip = skip_row(skip_ref, first, heads, head_dim)
        grad_skip = None
        for s in range(seqs):
            ext = pc_ref[s]
            pre = causal_conv(ext, w, b, seg)
            sig = sigmoid(pre)
            acts = pre * sig
            adj = came[g, s].astype(F32)
            d_acts = [None] * chunks
            for c in range(chunks - 1, -1, -1):
                q = s * chunks + c
                rows = slice(q * CHUNK, (q + 1) * CHUNK)
                x = acts[c * CHUNK : (c + 1) * CHUNK]
                dy = dm_ref[rows]
                ce = spread_all(cumg[rows], heads, head_dim)
                de = spread_all(dtg[rows], heads, head_dim)
                weight = jnp.exp2(ce[CHUNK - 1 : CHUNK] - ce)
                u = x * de
                ub = u.astype(BF16)
                dyb = dy.astype(BF16)
                cbt = cbt_ref[q]
                parts = []
                dcbt = dcbt_ref[q]
                for j in range(0, heads, 2):
                    two = slice(j * head_dim, (j + 2) * head_dim)
                    dy_block = block_diagonal(dyb[:, two], head_dim)
                    dm = nt(ub[:, two], dy_block)
                    mats = []
                    for k, h in enumerate((j, j + 1)):
                        here = jnp.broadcast_to(cumg[rows, h : h + 1], (CHUNK, CHUNK))
                        there = cumr[h : h + 1, rows]
                        decay = jnp.exp2(jnp.where(causal, there - here, -jnp.inf))
                        mats.append((decay * cbt).astype(BF16))
                        dcbt = dcbt + decay * dm[:, k * CHUNK : (k + 1) * CHUNK]
                    parts.append(dot(jnp.concatenate(mats, axis=1), dy_block))
                dcbt_ref[q] = dcbt
                start = s0_ref[s] if c == 0 else s1_ref[s]
                end = s2_ref[s] if c == chunks - 1 else s1_ref[s]
                adj_b = adj.astype(BF16)
                bb = bc_ref[rows, :LANES].astype(BF16)
                ey = jnp.exp2(ce) * dy
                du = jnp.concatenate(parts, axis=1) + weight * dot(bb, adj_b)
                uw = u * weight
                across = ((1,), (1,))
                db_acc[rows] += dot_pair(uw, adj_b, across) if c == chunks - 1 else dot_pairs(uw, adj, across)
                dc_acc[rows] += dot_pair(ey, start, across) if c == 0 else dot_pairs(ey, start, across)
                r1_ref[rows] += by_head(dyb.astype(F32) * (mixed_ref[rows] - skip * x), pick)
                r2_ref[rows] += by_head(x * du, pick)
                dtot_ref[q : q + 1] += by_head(
                    jnp.sum(adj * end.astype(F32), axis=0, keepdims=True), pick
                )
                grad = jnp.sum(dy * x, axis=0, keepdims=True)
                grad_skip = grad if grad_skip is None else grad_skip + grad
                d_acts[c] = du * de + skip * dy
                if c > 0:
                    adj = tot_all[g, q : q + 1] * adj + dot_pairs(ct_ref[q], ey)
            conv_back(s, ext, pre, sig, jnp.concatenate(d_acts, axis=0), g)
        skip_acc[0:1] += by_head(grad_skip, pick)

    @pl.when(step == lag + groups)
    def _():
        pl.when(place.has_left)(edges[0].start)
        row = lax.broadcasted_iota(jnp.int32, (CHUNK, CHUNK), 0)
        col = lax.broadcasted_iota(jnp.int32, (CHUNK, CHUNK), 1)
        later = (row <= col).astype(F32)
        rate = -jnp.exp(dl_ref[...])
        sum_raw = jnp.zeros((1, LANES), F32)
        sum_log = jnp.zeros((1, LANES), F32)
        for s in range(seqs):
            ext = pc_ref[s]
            pre = causal_conv(ext, w, b, seg)
            sig = sigmoid(pre)
            parts = []
            for c in range(chunks):
                q = s * chunks + c
                rows = slice(q * CHUNK, (q + 1) * CHUNK)
                dcbt = dcbt_ref[q]
                d_b = db_acc[rows] + dot_pairs(dcbt, bc_ref[rows, LANES:])
                d_c = dc_acc[rows] + dot_pairs(dcbt.T, bc_ref[rows, :LANES])
                parts.append(jnp.concatenate([d_b, d_c], axis=1))
                dt = dt_ref[rows]
                r2 = r2_ref[rows]
                d_log = jnp.dot(
                    later, r1_ref[rows] - dt * r2, precision=HIGH, preferred_element_type=F32
                )
                d_log = d_log + dtot_ref[q : q + 1]
                raw = raw_ref[s, EDGE + c * CHUNK : EDGE + (c + 1) * CHUNK] + sb_ref[...]
                d_raw = (r2 + rate * d_log) * sigmoid(raw)
                dc_ref[rows, channels:] = d_raw.astype(BF16)
                sum_raw = sum_raw + jnp.sum(d_raw, axis=0, keepdims=True)
                sum_log = sum_log + jnp.sum(d_log * dt, axis=0, keepdims=True) * rate
            conv_back(s, ext, pre, sig, jnp.concatenate(parts, axis=0), groups)
        hsum_ref[0:1] = sum_raw
        hsum_ref[1:2] = sum_log
        hsum_ref[2:3] = skip_acc[0:1]
        pl.when(place.has_left)(edges[1].start)

        @pl.when(place.has_right)
        def _():
            for copy in edges:
                copy.wait_recv()
            for s in range(seqs):
                fixed = tail_ref[s] + edge_came[s].astype(F32)
                dc_ref[(s + 1) * seg - EDGE : (s + 1) * seg, :channels] = fixed.astype(BF16)

        outs[1].start()
        run(2, "send_first")
        for k in range(depth - 1, 0, -1):
            run(1, "step", k)
        run(2, "hold")
        run(0, "step", 0)
        for k in range(depth - 1, 0, -1):
            run(2, "step", k)
        run(1, "step", 0)
        run(2, "step", 0)
        for n, out in enumerate((a_out, b_out)):
            for i in range(len(PIECES)):
                lo, hi = piece_of(out.shape[1], i)
                out[:, lo:hi] = lanes[2 * i + n].keep[place.z]
        for lane in lanes:
            lane.finish()
        chain.finish()

        @pl.when(place.has_left)
        def _():
            for copy in edges:
                copy.wait_send()

        for copy in pairs:
            copy.wait_send()
        for copy in outs:
            copy.wait()


def scan_backward(
    pc, w, b, sb, dl, bc, dt, cum, cumt, dm, mixed, s0, s1, s2, tot, skip, normed_t, dz, turned, cot,
    head_dim, depth,
):
    seqs, rows, cols = pc.shape
    tokens, inner = dm.shape
    groups = inner // GROUP
    lag = depth - 1
    taps, channels = w.shape
    out = lambda i: jnp.maximum(i - lag, 0)
    inside = lambda i: jnp.minimum(out(i), groups - 1)
    wide = pl.BlockSpec((tokens, GROUP), lambda i: (0, inside(i)))
    states = pl.BlockSpec((seqs, LANES, GROUP), lambda i: (0, 0, inside(i)))
    conv = lambda n: pl.BlockSpec((n, GROUP), lambda i: (0, out(i)))
    ahead = lambda n: pl.BlockSpec((n, 2 * GROUP), lambda i: (0, jnp.minimum(i, groups // 2 - 1)))
    once = lambda v: pl.BlockSpec(v.shape, lambda i: (0,) * v.ndim, pipeline_mode=pl.Buffered(1))
    anywhere = pl.BlockSpec(memory_space=pl.ANY)
    chunks = tokens // CHUNK
    shape, dma = jax.ShapeDtypeStruct, pltpu.SemaphoreType.DMA
    a_rows, b_rows = normed_t.shape[1] // depth, turned.shape[1] // depth
    a_cols, b_cols = dz.shape[1], cot.shape[1]
    half = lambda v: (4,) + v.shape[1:]
    sends, receives = Scatter.sems(depth)
    buffers = []
    for n in range(len(PIECES)):
        for rows_of, cols_of in ((a_rows, a_cols), (b_rows, b_cols)):
            lo, hi = piece_of(cols_of, n)
            buffers += Scatter.scratch(depth, rows_of, hi - lo)
    link = pltpu.VMEM((groups, seqs, LANES, GROUP), BF16)
    square = pltpu.VMEM((chunks, CHUNK, CHUNK), F32)
    column = pltpu.VMEM((tokens, LANES), F32)
    return pl.pallas_call(
        functools.partial(scan_backward_kernel, depth, head_dim, groups),
        grid=(groups + 1 + lag,),
        in_specs=[
            pl.BlockSpec((seqs, rows, GROUP), lambda i: (0, 0, out(i))),
            conv(taps),
            conv(1),
            pl.BlockSpec(
                (seqs, rows, LANES), lambda i: (0, 0, cols // LANES - 1), pipeline_mode=pl.Buffered(1)
            ),
            whole((1, LANES)), whole((1, LANES)),
            once(bc), once(dt), once(cum), once(cumt),
            ahead(tokens), wide, wide, states, states, states, ahead(8), whole((1, LANES)),
            once(normed_t), once(dz), once(turned), once(cot),
        ],
        out_specs=[
            anywhere, conv(taps), conv(1), whole((3, LANES)),
            whole((a_rows, a_cols)), whole((b_rows, b_cols)), anywhere,
        ],
        out_shape=[
            shape((tokens, cols), BF16),
            shape((taps, channels), F32),
            shape((1, channels), F32),
            shape((3, LANES), F32),
            shape((a_rows, a_cols), F32),
            shape((b_rows, b_cols), F32),
            shape(half(normed_t), BF16),
        ],
        scratch_shapes=[
            square, pltpu.VMEM((chunks, LANES, CHUNK), F32), square, column, column, column, column,
            pltpu.VMEM((8, LANES), F32),
            pltpu.VMEM((8, LANES), F32),
            pltpu.VMEM((tokens, cols), BF16),
            pltpu.VMEM((seqs, EDGE, channels), F32),
            pltpu.VMEM((seqs, EDGE, channels), BF16),
            pltpu.VMEM((seqs, EDGE, channels), BF16),
            pltpu.VMEM((2 * lag + 2, seqs, LANES, GROUP), F32), pltpu.VMEM((groups, 8, GROUP), F32), link, link,
            pltpu.VMEM(half(normed_t), BF16), pltpu.VMEM(dz.shape, BF16),
            pltpu.VMEM(half(turned), BF16), pltpu.VMEM(cot.shape, BF16),
            dma((groups,)), dma((groups,)), dma((2,)), dma((2,)), dma((12,)), dma((12,)), dma((2,)),
            dma((2 * len(PIECES), sends)), dma((2 * len(PIECES), receives)),
            *buffers,
        ],
        compiler_params=pltpu.CompilerParams(
            dimension_semantics=("arbitrary",), collective_id=1, has_side_effects=True,
            vmem_limit_bytes=VMEM_LIMIT,
        ),
        name="scan_backward_sums",
    )(
        pc, w, b, pc, sb, dl, bc, dt, cum, cumt, dm, dm, mixed, s0, s1, s2, tot, skip,
        normed_t, dz, turned, cot,
    )


def scatter_last_kernel(
    depth, splits, nt_ref, nt_pair, dc_ref, dz_ref, wg_src, wc_src, x_ref, cot_ref, gain_ref,
    ggain_ref, gb_ref, gw_ref, hsum_ref, c_out, gi_ref, small_out, *refs,
):
    place = Place(depth)
    place.meet(line=True)
    pieces = len(splits) - 1
    dc_pairs, refs = refs[:pieces], refs[pieces:]
    small_src, tiles_ref, tile_sem, pair_send, pair_recv, send, recv, small_send, small_recv = refs[:9]
    refs = refs[9:]
    cuts = [dc_ref.at[:, pl.ds(lo, hi - lo)] for lo, hi in zip(splits, splits[1:])]
    copies = pair_copies(place, (), tuple(zip(cuts, dc_pairs)), pair_send, pair_recv)
    for copy in copies:
        copy.start()
    lanes = [
        Scatter(place, nt_ref, nt_pair, cut, pair, *(("y", "x") if n % 2 == 0 else ("x", "y")),
                refs[7 * n : 7 * n + 7], send.at[n], recv.at[n])
        for n, (cut, pair) in enumerate(zip(cuts, dc_pairs))
    ]
    small = SmallScatter(place, small_src, *refs[7 * pieces :], small_send, small_recv)
    tile = tiles_ref.shape[2]
    tokens = x_ref.shape[0]

    def d_normed(src, grad_ref, first, start=0, count=None):
        count = src.shape[1] // tile if count is None else count

        def fetch(i, slot):
            cols = pl.ds(pl.multiple_of(i * tile, LANES), tile)
            return pltpu.make_async_copy(src.at[:, cols], tiles_ref.at[slot], tile_sem.at[slot])

        fetch(start, start % 2).start()

        def one(i, carry):
            slot = lax.rem(i, 2)
            pl.when(i + 1 < count)(lambda: fetch(i + 1, 1 - slot).start())
            fetch(i, slot).wait()
            cols = pl.ds(pl.multiple_of(i * tile, LANES), tile)
            for r in range(0, tokens, 2 * CHUNK):
                rows = slice(r, r + 2 * CHUNK)
                part = nt(grad_ref[rows, cols], tiles_ref[slot])
                if first:

                    @pl.when(i == 0)
                    def _():
                        gi_ref[rows] = part

                    @pl.when(i > 0)
                    def _():
                        gi_ref[rows] += part
                else:
                    gi_ref[rows] += part
            return carry

        lax.fori_loop(start, count, one, 0)

    def input_grad():
        gain = gain_ref[...]
        size = 64

        def one(i, total):
            rows = pl.ds(pl.multiple_of(i * size, size), size)
            d = gi_ref[rows, :]
            values = x_ref[rows, :].astype(F32)
            scale = lax.rsqrt(jnp.mean(values * values, axis=1, keepdims=True) + EPS)
            hat = values * scale
            weighted = d * gain
            pull = jnp.mean(weighted * hat, axis=1, keepdims=True)
            gi_ref[rows, :] = scale * (weighted - hat * pull) + cot_ref[rows, :].astype(F32)
            return total + jnp.sum(d * hat, axis=0, keepdims=True)

        grad_gain = lax.fori_loop(0, tokens // size, one, jnp.zeros(gain.shape, F32))
        small_src[...] = jnp.zeros_like(small_src)
        taps = gw_ref.shape[0]
        shares = ((0, grad_gain), (1, ggain_ref[...]), (2, gb_ref[...]), (3, gw_ref[...]))
        heads = hsum_ref[:, : LANES // 2]
        for n in range(8 * depth):
            at = (n // depth // 4, n // depth // 2 % 2, n // depth % 2, n % depth)
            for row, value in shares:
                own = value.shape[1] // (8 * depth)
                where = (*at, slice(row, row + value.shape[0]), slice(0, own))
                small_src[where] = value[:, n * own : (n + 1) * own]
            small_src[(*at, slice(0, 1), slice(LANES // 2, LANES))] = heads[0:1]
            small_src[(*at, slice(3 + taps, 4 + taps), slice(0, LANES // 2))] = heads[1:2]
            small_src[(*at, slice(3 + taps, 4 + taps), slice(LANES // 2, LANES))] = heads[2:3]

    def run(first, name, *rest):
        for lane in lanes[first : first + 2]:
            getattr(lane, name)(*rest)

    for copy in copies[:2]:
        copy.wait_recv()
    run(0, "send_second")
    for copy in copies[2:]:
        copy.wait_recv()
    run(2, "send_second")
    d_normed(wg_src, dz_ref, True)
    run(0, "send_first")
    run(4, "send_second")
    middle = wc_src.shape[1] // tile // 2
    d_normed(wc_src, dc_ref, False, 0, middle)
    run(0, "hold")
    run(2, "send_first")
    d_normed(wc_src, dc_ref, False, middle)
    run(2, "hold")
    run(4, "send_first")
    run(0, "step", depth - 1)
    input_grad()
    small.stage(0)
    for k in range(depth - 2, 0, -1):
        run(0, "step", k)
    run(4, "hold")
    small.stage(1)
    for k in range(depth - 1, 0, -1):
        run(2, "step", k)
    small.stage(2)
    for k in range(depth - 1, 0, -1):
        run(4, "step", k)
    small.stage(3)
    for k in range(depth - 1, -1, -1):
        small.sums.step(k)
    for first in (0, 2, 4):
        run(first, "step", 0)
    for lane, lo, hi in zip(lanes, splits, splits[1:]):
        c_out[:, lo:hi] = lane.keep[place.z]
    small_out[...] = small.keep[place.z]
    for lane in lanes:
        lane.finish()
    small.finish()
    for copy in copies:
        copy.wait_send()


def scatter_last(normed_t, nt_pair, dc, dz, wg, wc, x, cot, gain, ggain, gb, gw, hsum, depth):
    shape = jax.ShapeDtypeStruct
    vmem, dma = pl.BlockSpec(memory_space=pltpu.VMEM), pltpu.SemaphoreType.DMA
    anywhere = pl.BlockSpec(memory_space=pl.ANY)
    sends, receives = Scatter.sems(depth)
    rows = normed_t.shape[1] // depth
    tokens, width = dc.shape
    blocks = width // LANES
    parts = [share for share in PIECES for _ in (0, 1)]
    splits = tuple(LANES * (blocks * sum(parts[:n]) // sum(parts)) for n in range(len(parts) + 1))
    small_shape = (8, LANES)
    small_sends, small_receives = SmallScatter.sems(depth)
    sizes = [hi - lo for lo, hi in zip(splits, splits[1:])]
    scratch = []
    for size in sizes:
        scratch += Scatter.scratch(depth, rows, size)
    return pl.pallas_call(
        functools.partial(scatter_last_kernel, depth, splits),
        in_specs=[vmem, vmem, vmem, vmem, anywhere, anywhere] + [vmem] * 7,
        out_specs=[vmem] * 3,
        out_shape=[shape((rows, width), F32), shape((tokens, x.shape[1]), F32), shape(small_shape, F32)],
        scratch_shapes=[
            *(pltpu.VMEM((tokens, size), BF16) for size in sizes),
            pltpu.VMEM((2, 2, 2, depth) + small_shape, F32),
            pltpu.VMEM((2, wg.shape[0], 3 * LANES), BF16),
            dma((2,)), dma((6,)), dma((6,)), dma((6, sends)), dma((6, receives)),
            dma((small_sends,)), dma((small_receives,)),
            *scratch,
            *SmallScatter.scratch(depth, small_shape),
        ],
        compiler_params=pltpu.CompilerParams(
            collective_id=2, has_side_effects=True, vmem_limit_bytes=VMEM_LIMIT
        ),
        name="scatter_last",
    )(normed_t, nt_pair, dc, dz, wg, wc, x, cot, gain, ggain, gb, gw, hsum)


def passed_along(value, axis, steps):
    count = lax.axis_size(axis)
    initial, last = (max(0, -steps), min(count, count - steps))
    return lax.ppermute(value, axis, [(source, source + steps) for source in range(initial, last)])


def prefix(total, local, axis, backward):
    count, here = lax.axis_size(axis), lax.axis_index(axis)
    totals = lax.all_gather(total.astype(BF16), axis)
    locals_ = lax.all_gather(local, axis)
    state = jnp.zeros(local.shape, F32)
    order = range(count - 1, 0, -1) if backward else range(count - 1)
    for lap in order:
        new = totals[lap].astype(F32) * state + locals_[lap].astype(F32)
        reached = lap > here if backward else lap < here
        state = jnp.where(reached, new, state)
    leaves = total * state + local.astype(F32)
    return state.astype(BF16), leaves.astype(BF16)


AXES = ("dp", "ctx")


def body(
    inputs, gain_in, in_weight, conv_weight, conv_bias, step_bias, decay_log, skip_gain, gain_out,
    out_weight, cotangent,
):
    seqs, seg, width = inputs.shape
    tokens = seqs * seg
    count = lax.axis_size(AXES)
    dp, depth = lax.axis_size("dp"), lax.axis_size("ctx")
    own_links = dp == 8 and depth == 4
    inner = out_weight.shape[0] * count
    taps, channels = conv_weight.shape[0], conv_weight.shape[1] * count
    num_heads = step_bias.shape[0]
    head_dim = inner // num_heads
    a, b, c = gain_in.shape[0], gain_out.shape[0], conv_bias.shape[0]

    w_gate = in_weight[:, :inner]
    w_conv = in_weight[:, inner:]
    spare = -w_conv.shape[1] % LANES
    w_conv = jnp.pad(w_conv, ((0, 0), (0, spare)))
    rest = jnp.concatenate([gain_out, conv_bias, conv_weight.reshape(-1)])
    ends = taps - 1
    flat = inputs.reshape(tokens, width)
    cot = cotangent.reshape(tokens, width)

    if own_links:
        row = lambda v: jnp.pad(v, ((0, 0), (0, LANES - v.shape[1])))
        small = [row(v.reshape(-1, v.shape[-1])) for v in (gain_in, gain_out, conv_bias, conv_weight)]
        small = jnp.concatenate(small + [jnp.zeros((5 - taps, LANES), BF16)]).astype(F32)
        pc, normed_ext, normed_t, g_in, g_out, bias, kernel, w_conv, gate_line = gather_project(
            inputs, small, w_conv, w_gate, inner, channels, taps, depth
        )
        w_conv = w_conv.reshape(width, -1)
    else:
        before = passed_along(inputs[:, seg - EDGE :], "ctx", 1)
        ext = jnp.concatenate([before, inputs], axis=1).astype(F32)
        scale_ext = lax.rsqrt(jnp.mean(ext * ext, axis=-1, keepdims=True) + EPS)
        small = lax.all_gather(jnp.concatenate([gain_in, rest]), AXES).astype(F32)
        w_conv = lax.all_gather(w_conv, AXES, axis=0, tiled=True)
        w_gate = lax.all_gather(w_gate, AXES, axis=0, tiled=True)
        w_out = lax.all_gather(out_weight, AXES, axis=0, tiled=True)
        g_in, rest = small[:, :a].reshape(1, width), small[:, a:]
        normed_ext = (ext * scale_ext * g_in).astype(BF16)
        pc = dot(normed_ext.reshape(-1, width), w_conv).reshape(seqs, seg + EDGE, -1)
        g_out = rest[:, :b].reshape(1, inner)
        bias = rest[:, b : b + c].reshape(1, channels)
        kernel = rest[:, b + c : b + c + taps * c].reshape(count, taps, c).transpose(1, 0, 2)
        kernel = kernel.reshape(taps, channels)
    pad_head = lambda v: jnp.pad(v, (0, LANES - num_heads)).reshape(1, LANES)
    sb, dl = pad_head(step_bias), pad_head(decay_log)
    skip = jnp.repeat(skip_gain, head_dim).reshape(1, inner)

    if own_links:
        bc, dt, cum, cumt, mixed, s0, s1, s2, tot, z, dno, w_gate, w_out = scan_forward(
            pc, kernel, bias, sb, dl, pad_head(skip_gain), normed_ext, cot, gate_line, out_weight, inner, head_dim, depth
        )
        w_gate = w_gate.reshape(width, inner)
        w_out = w_out.reshape(inner, width)
        per_seq = tot[tokens // CHUNK : tokens // CHUNK + seqs][:, None, :]
    else:
        x, bc, dt, cum, cumt, loc0, local, tot = fwd_a(pc, kernel, bias, sb, dl, inner, head_dim)
        per_seq = tot[tokens // CHUNK : tokens // CHUNK + seqs][:, None, :]
        s0, s2 = prefix(per_seq, local, "ctx", False)
        mixed, s1 = fwd_b(x, bc, dt, cum, cumt, s0, loc0, tot, skip, head_dim)
        z = dot(normed_ext[:, EDGE:].reshape(tokens, width), w_gate)
        dno = nt(cot, w_out)

    turned, output, d_mixed, d_gate, grad_gain_out = mid(z, dno, mixed, w_out, g_out, flat, 8)
    if own_links:
        (
            d_conv, grad_kernel, grad_bias, head_sums, grad_gate_weight, grad_out_weight, nt_pair
        ) = scan_backward(
            pc, kernel, bias, sb, dl, bc, dt, cum, cumt, d_mixed, mixed, s0, s1, s2, tot,
            pad_head(skip_gain), normed_t, d_gate, turned, cot, head_dim, depth,
        )
    else:
        scatter = lambda v: lax.psum_scatter(v.astype(BF16), AXES, scatter_dimension=0, tiled=True).astype(F32)
        normed = normed_ext[:, EDGE:].reshape(tokens, width)
        grad_out_weight = scatter(dot(turned.reshape(inner, tokens), cot))
        grad_gate_weight = scatter(dot(normed, d_gate, ((0,), (0,))))
        adjoint = bwd_a(d_mixed, bc, cum, tot, seqs, head_dim)
        g, _ = prefix(per_seq, adjoint, "ctx", True)
        d_conv, tail, edge, grad_kernel, grad_bias, grad_skip, d_raw, head_sums = bwd_b(
            pc, kernel, bias, sb, dl, bc, dt, cum, cumt, d_mixed, mixed, s0, s1, s2, g, tot, skip, head_dim
        )
        after = passed_along(edge[:, EDGE - ends :].astype(BF16), "ctx", -1).astype(F32)
        tail = tail[:, EDGE - ends :] + after
        d_conv = d_conv.reshape(seqs, seg, channels).at[:, seg - ends :].set(tail.astype(BF16))
        d_conv = jnp.concatenate([d_conv.reshape(tokens, channels), d_raw.astype(BF16)], axis=1)

    real = d_conv.shape[1] - spare
    if own_links:
        grad_conv_cols, grad_input, mine = scatter_last(
            normed_t, nt_pair, d_conv, d_gate, w_gate, w_conv, flat, cot, g_in,
            grad_gain_out, grad_bias, grad_kernel, head_sums, depth,
        )
        grad_conv_cols = grad_conv_cols[:, :real]
        half = LANES // 2
        grad_gain_in, grad_step = mine[0, :a], mine[0, half : half + num_heads]
        grad_gain_out, grad_bias, grad_kernel = mine[1, :b], mine[2, :c], mine[3 : 3 + taps, :c]
        grad_decay = mine[3 + taps, :num_heads]
        grad_skip = mine[3 + taps, half : half + num_heads]
    else:
        d_normed = nt(d_gate, w_gate) + nt(d_conv, w_conv)
        values = flat.astype(F32)
        scale = lax.rsqrt(jnp.mean(values * values, axis=-1, keepdims=True) + EPS)
        hat = values * scale
        weighted = d_normed * g_in
        pull = jnp.mean(weighted * hat, axis=-1, keepdims=True)
        grad_input = scale * (weighted - hat * pull) + cot.astype(F32)
        grad_conv_cols = scatter(dot(normed, d_conv[:, :real], ((0,), (0,))))
        grad_skip = jnp.sum(grad_skip.reshape(num_heads, head_dim), axis=1)
        heads_sum = jnp.concatenate([head_sums[0, :num_heads], head_sums[1, :num_heads], grad_skip])
        by_owner = jnp.concatenate(
            [
                jnp.sum(d_normed * hat, axis=0).reshape(count, a),
                grad_gain_out.reshape(count, b),
                grad_bias.reshape(count, c),
                grad_kernel.reshape(taps, count, c).transpose(1, 0, 2).reshape(count, taps * c),
                jnp.broadcast_to(heads_sum, (count, 3 * num_heads)),
            ],
            axis=1,
        )
        mine = lax.dynamic_index_in_dim(lax.psum(by_owner, AXES), lax.axis_index(AXES), 0, False)
        cuts = [0, a, a + b, a + b + c, a + b + c + taps * c]
        cuts += [cuts[-1] + n * num_heads for n in (1, 2, 3)]
        parts = [mine[lo:hi] for lo, hi in zip(cuts, cuts[1:])]
        grad_gain_in, grad_gain_out, grad_bias, grad_kernel, grad_step, grad_decay, grad_skip = parts
    return (
        output.reshape(seqs, seg, width),
        grad_input.reshape(seqs, seg, width),
        grad_gain_in,
        jnp.concatenate([grad_gate_weight, grad_conv_cols], axis=1),
        grad_kernel.reshape(taps, c),
        grad_bias,
        grad_step,
        grad_decay,
        grad_skip,
        grad_gain_out,
        grad_out_weight,
    )


def solution(mesh):
    rows, cols, both = P("dp", "ctx", None), P(AXES, None), P(AXES)
    return jax.shard_map(
        body,
        mesh=mesh,
        in_specs=(rows, both, cols, P(None, AXES), both, P(), P(), P(), both, cols, rows),
        out_specs=(rows, rows, both, cols, P(None, AXES), both, P(), P(), P(), both, cols),
        check_vma=False,
    )
```
